32 devices in a mesh: dp: 8 (over z, y), tensor: 4 (over x, core).
Axes of the slice: x: 2, y: 2, z: 4, core: 2. Of those that a mesh axis runs over, the one named last changes fastest.
Arguments:
- tokens: bfloat16 [8192, 1536], P('dp'), may hold values from -6 to 6
- inproj: bfloat16 [2, 2, 1536, 3072], P(None, None, 'dp', 'tensor'), may hold values from -0.15625 to 0.15625
- stepproj: bfloat16 [2, 1536, 48], P(None, None, 'tensor'), may hold values from -0.15625 to 0.15625
- stateproj: bfloat16 [2, 1536, 256], replicated, may hold values from -0.15625 to 0.15625
- outproj: bfloat16 [2, 3072, 1536], P(None, 'tensor', 'dp'), may hold values from -0.109375 to 0.109375
- convinner: float32 [2, 4, 3072], P(None, None, 'tensor'), may hold values from -3 to 3
- biasinner: float32 [2, 3072], P(None, 'tensor'), may hold values from -0.5 to 0.5
- convstate: float32 [2, 4, 256], replicated, may hold values from -3 to 3
- biasstate: float32 [2, 256], replicated, may hold values from -0.5 to 0.5
- stepbias: float32 [2, 48], P(None, 'tensor'), may hold values from -6 to -3
- decaylog: float32 [2, 48], P(None, 'tensor'), may hold values from 0 to 2.77
- skipgain: float32 [2, 48], P(None, 'tensor'), may hold values from 0.5 to 1.5
- normgain: float32 [2, 3072], P(None, 'tensor'), may hold values from 0.5 to 1.5
- inputgain: float32 [2, 1536], replicated, may hold values from 0.5 to 1.5
- cotangent: bfloat16 [8192, 1536], P('dp'), may hold values from -6 to 6
Outputs:
- mixed: bfloat16 [8192, 1536], P('dp')
- grad_tokens: float32 [8192, 1536], P('dp')
- inproj_grad: float32 [2, 2, 1536, 3072], P(None, None, 'dp', 'tensor')
- stepproj_grad: float32 [2, 1536, 48], P(None, None, 'tensor')
- stateproj_grad: float32 [2, 1536, 256], replicated
- outproj_grad: float32 [2, 3072, 1536], P(None, 'tensor', 'dp')
- convinner_grad: float32 [2, 4, 3072], P(None, None, 'tensor')
- biasinner_grad: float32 [2, 3072], P(None, 'tensor')
- convstate_grad: float32 [2, 4, 256], replicated
- biasstate_grad: float32 [2, 256], replicated
- stepbias_grad: float32 [2, 48], P(None, 'tensor')
- decaylog_grad: float32 [2, 48], P(None, 'tensor')
- skipgain_grad: float32 [2, 48], P(None, 'tensor')
- normgain_grad: float32 [2, 3072], P(None, 'tensor')
- inputgain_grad: float32 [2, 1536], replicated
The draws below stay inside these ranges and needn't reach their ends.
All inputs are finite; a program needn't handle non-finite values.
Results may differ from the reference program's by a relative error of at most 0.02.
Values may be sent and summed in bfloat16 or wider, within the bound.
A program may use at most 256 MiB of HBM per device.

```python
import jax
import jax.numpy as jnp
from jax import lax

D = 1536
HEADS = 48
STATE = 128
KCONV = 4
BLOCK = 256
LEN = 1024
LAYERS = 2
INNER = 3072
TOKENS = 8192


def block_scale(rng, shape, cuts, low, high):
    def one(position, shards_of):
        draws = jax.random.uniform(jax.random.fold_in(jax.random.fold_in(rng, 6), position), (shards_of,), jnp.float32, low / len(cuts), high / len(cuts))
        return jnp.repeat(jnp.exp(draws), shape[position] // shards_of).reshape((-1,) + (1,) * (len(shape) - position - 1))

    loudness = one(*cuts[0])
    for cut in cuts[1:]:
        loudness = loudness * one(*cut)
    return loudness


def noise(stream_key, extent, spread, bound, pieces=(), dtype=jnp.bfloat16):
    loudness = block_scale(stream_key, extent, pieces, -0.22, 0.18) if pieces else 1.0
    values = jax.random.normal(stream_key, extent, jnp.float32) * spread * loudness
    return jnp.minimum(jnp.maximum(values, -bound), bound).astype(dtype)


def setup_inputs(seed: int = 0) -> dict:
    streams_of = jax.random.split(jax.random.key(seed), 16)
    tokens = noise(streams_of[0], (TOKENS, D), 1.0, 6.0, ((0, 8),))
    inproj = noise(streams_of[1], (LAYERS, 2, D, INNER), D ** -0.5, 0.15625, ((2, 8), (3, 4)))
    stepproj = noise(streams_of[2], (LAYERS, D, HEADS), D ** -0.5, 0.15625, ((2, 4),))
    stateproj = noise(streams_of[3], (LAYERS, D, 2 * STATE), D ** -0.5, 0.15625)
    outproj = noise(streams_of[4], (LAYERS, INNER, D), INNER ** -0.5, 0.109375, ((1, 4), (2, 8)))
    convinner = noise(streams_of[5], (LAYERS, KCONV, INNER), KCONV ** -0.5, 3.0, ((2, 4),), jnp.float32)
    biasinner = jnp.clip(jax.random.uniform(streams_of[6], (LAYERS, INNER), jnp.float32, -0.5, 0.5) * block_scale(streams_of[6], (LAYERS, INNER), ((1, 4),), -0.4, 0.0), -0.5, 0.5)
    convstate = noise(streams_of[7], (LAYERS, KCONV, 2 * STATE), KCONV ** -0.5, 3.0, (), jnp.float32)
    biasstate = jnp.clip(jax.random.uniform(streams_of[8], (LAYERS, 2 * STATE), jnp.float32, -0.5, 0.5), -0.5, 0.5)
    stepbias = jnp.clip(-6.0 + 3.0 * jax.random.uniform(streams_of[9], (LAYERS, HEADS), jnp.float32) ** block_scale(streams_of[9], (LAYERS, HEADS), ((1, 4),), -0.2, 0.2), -6.0, -3.0)
    decaylog = jnp.clip(2.77 * jax.random.uniform(streams_of[10], (LAYERS, HEADS), jnp.float32) ** block_scale(streams_of[10], (LAYERS, HEADS), ((1, 4),), -0.2, 0.2), 0.0, 2.77)
    skipgain = jnp.clip(0.5 + 1.0 * jax.random.uniform(streams_of[11], (LAYERS, HEADS), jnp.float32) ** block_scale(streams_of[11], (LAYERS, HEADS), ((1, 4),), -0.2, 0.2), 0.5, 1.5)
    normgain = jnp.clip(1.0 + 0.1 * jax.random.normal(streams_of[12], (LAYERS, INNER), jnp.float32), 0.5, 1.5)
    inputgain = jnp.clip(1.0 + 0.1 * jax.random.normal(streams_of[13], (LAYERS, D), jnp.float32), 0.5, 1.5)
    cotangent = noise(streams_of[14], (TOKENS, D), 1.0, 6.0, ((0, 8),))
    return dict(tokens=tokens, inproj=inproj, stepproj=stepproj, stateproj=stateproj, outproj=outproj, convinner=convinner, biasinner=biasinner, convstate=convstate, biasstate=biasstate, stepbias=stepbias, decaylog=decaylog, skipgain=skipgain, normgain=normgain, inputgain=inputgain, cotangent=cotangent)


EPS = 1e-05
HIGH = lax.Precision.HIGHEST

@jax.custom_vjp
def low(v):
    return lax.optimization_barrier(v.astype(jnp.bfloat16)).astype(jnp.float32)

@jax.custom_vjp
def low_back(v):
    return v

def low_keep(v):
    return (low(v), None)

def low_pass(kept, grad):
    return (grad,)

def back_keep(v):
    return (v, None)

def back_low(kept, grad):
    return (low(grad),)
low.defvjp(low_keep, low_pass)
low_back.defvjp(back_keep, back_low)

def prenorm(residual, gain_vec):
    scale_row = lax.rsqrt(lax.optimization_barrier(jnp.mean(residual * residual, axis=1, keepdims=True)) + EPS)
    return residual * scale_row * gain_vec

def conv_act(pre_conv, kernel, offset):
    tokens_n, channels = pre_conv.shape
    window = kernel.shape[0]
    shaped = pre_conv.reshape(tokens_n // LEN, LEN, channels)
    padded = jnp.pad(shaped, ((0, 0), (window - 1, 0), (0, 0)))
    summed_taps = offset + kernel[0] * padded[:, 0:LEN]
    for tap_at in range(1, window):
        summed_taps = summed_taps + kernel[tap_at] * padded[:, tap_at:tap_at + LEN]
    return jax.nn.silu(summed_taps).reshape(tokens_n, channels)

def ssd_seq(inner_seq, step_seq, decay_rates, key_seq, query_seq, skip_vec):
    head_count = step_seq.shape[1]
    blocks = LEN // BLOCK
    in_blocks = inner_seq.reshape(blocks, BLOCK, head_count, -1)
    step_blocks = step_seq.reshape(blocks, BLOCK, head_count)
    key_blocks = key_seq.reshape(blocks, BLOCK, -1)
    query_blocks = query_seq.reshape(blocks, BLOCK, -1)
    running_log = jnp.cumsum(step_blocks * decay_rates, axis=1)
    order_ids = jnp.arange(BLOCK)
    lower_mask = order_ids[:, None] >= order_ids[None, :]
    log_gap = running_log[:, :, None, :] - running_log[:, None, :, :]
    decay_mat = jnp.exp(jnp.where(lower_mask[None, :, :, None], log_gap, -jnp.inf))
    scores = jnp.einsum('cin,cjn->cij', query_blocks, key_blocks, precision=HIGH)
    mixing = scores[:, :, :, None] * decay_mat * step_blocks[:, None, :, :]
    local_out = jnp.einsum('cijh,cjhp->cihp', mixing, in_blocks, precision=HIGH)
    block_log = running_log[:, -1, :]
    tail_weight = jnp.exp(block_log[:, None, :] - running_log) * step_blocks
    block_states = jnp.einsum('cjn,cjh,cjhp->chnp', key_blocks, tail_weight, in_blocks, precision=HIGH)

    def advance(carried, scan_items):
        fresh_state, block_drop = scan_items
        return (jnp.exp(block_drop)[:, None, None] * carried + fresh_state, carried)
    start_state = jnp.zeros(block_states.shape[1:], jnp.float32)
    _, before = lax.scan(advance, start_state, (block_states, block_log))
    carried_out = jnp.einsum('cin,chnp->cihp', query_blocks, before, precision=HIGH) * jnp.exp(running_log)[:, :, :, None]
    result = local_out + carried_out + skip_vec[None, None, :, None] * in_blocks
    return result.reshape(LEN, -1)

def mixer(gate_pre, inner_raw, step_raw, state_raw, kernel_in, offset_in, kernel_state, offset_state, step_offset, decay_log, skip_vec):
    tokens_n = gate_pre.shape[0]
    head_count = step_raw.shape[1]
    inner_act = conv_act(inner_raw, kernel_in, offset_in)
    state_act = conv_act(state_raw, kernel_state, offset_state)
    step_sizes = jax.nn.softplus(step_raw + step_offset)
    decay_rates = -jnp.exp(decay_log)
    seq_count = tokens_n // LEN

    def one_seq(seq_items):
        inner_seq, step_seq, state_seq = seq_items
        return ssd_seq(inner_seq.reshape(LEN, head_count, -1), step_seq, decay_rates, state_seq[:, :STATE], state_seq[:, STATE:], skip_vec)
    outputs = lax.map(jax.checkpoint(one_seq), (inner_act.reshape(seq_count, LEN, -1), step_sizes.reshape(seq_count, LEN, head_count), state_act.reshape(seq_count, LEN, -1)))
    return outputs.reshape(tokens_n, -1) * jax.nn.silu(gate_pre)

def mat(left, right):
    return jnp.dot(left, right, precision=HIGH, preferred_element_type=jnp.float32)

def layer(residual, inproj, stepproj, stateproj, outproj, kernel_in, offset_in, kernel_state, offset_state, step_offset, decay_log, skip_vec, norm_vec, input_vec):
    normed = low(prenorm(residual, input_vec))
    gate_pre = low_back(mat(normed, inproj[0]))
    inner_raw = low_back(mat(normed, inproj[1]))
    step_raw = low_back(mat(normed, stepproj))
    state_raw = low_back(mat(normed, stateproj))
    gated_out = mixer(gate_pre, inner_raw, step_raw, state_raw, kernel_in, offset_in, kernel_state, offset_state, step_offset, decay_log, skip_vec)
    factor = lax.rsqrt(lax.optimization_barrier(jnp.mean(gated_out * gated_out, axis=1, keepdims=True)) + EPS)
    scaled = low(norm_vec * gated_out)
    summed = low_back(mat(scaled, outproj))
    return residual + factor * summed

def forward(residual, inproj, stepproj, stateproj, outproj, convinner, biasinner, convstate, biasstate, stepbias, decaylog, skipgain, normgain, inputgain):
    for layer_at in range(LAYERS):
        residual = layer(residual, inproj[layer_at], stepproj[layer_at], stateproj[layer_at], outproj[layer_at], convinner[layer_at], biasinner[layer_at], convstate[layer_at], biasstate[layer_at], stepbias[layer_at], decaylog[layer_at], skipgain[layer_at], normgain[layer_at], inputgain[layer_at])
    return residual

def reference(tokens, inproj, stepproj, stateproj, outproj, convinner, biasinner, convstate, biasstate, stepbias, decaylog, skipgain, normgain, inputgain, cotangent):
    floats = (tokens.astype(jnp.float32), inproj.astype(jnp.float32), stepproj.astype(jnp.float32), stateproj.astype(jnp.float32), outproj.astype(jnp.float32), convinner, biasinner, convstate, biasstate, stepbias, decaylog, skipgain, normgain, inputgain)
    result, pull = jax.vjp(forward, *floats)
    pulled = pull(cotangent.astype(jnp.float32))
    return (result.astype(jnp.bfloat16), pulled[0], pulled[1], pulled[2], pulled[3], pulled[4], pulled[5], pulled[6], pulled[7], pulled[8], pulled[9], pulled[10], pulled[11], pulled[12], pulled[13])
```

```python
import functools

import jax
import jax.numpy as jnp
from jax import lax
from jax.experimental import pallas as pl
from jax.experimental.pallas import tpu as pltpu
from jax.sharding import PartitionSpec as P

STATE = 128
LEN = 1024
INNER = 3072
HEAD = 64
CHUNK = 128
LANES = 128
EPS = 1e-05
LOG2E = 1.4426950408889634

HIGH = lax.Precision.HIGHEST
NN = (((1,), (0,)), ((), ()))
NT = (((1,), (1,)), ((), ()))
TN = (((0,), (0,)), ((), ()))
F32 = jnp.float32
BF16 = jnp.bfloat16


def mm(left, right, dims=NN, precision=None):
    return lax.dot_general(left, right, dims, precision=precision, preferred_element_type=F32)


def sigmoid(v):
    return 0.5 * jnp.tanh(0.5 * v) + 0.5


def softplus(v):
    return jnp.maximum(v, 0.0) + jnp.log1p(jnp.exp(-jnp.abs(v)))


def split16(v):
    top = v.astype(BF16)
    return top, (v - top.astype(F32)).astype(BF16)


def expand(v, ind):
    top, rest = split16(v)
    return mm(top, ind) + mm(rest, ind)


def headsum(v, ind):
    top, rest = split16(v)
    return mm(top, ind, NT) + mm(rest, ind, NT)


def iotas(n):
    return (
        lax.broadcasted_iota(jnp.int32, (n, n), 0),
        lax.broadcasted_iota(jnp.int32, (n, n), 1),
    )


def colsum(v):
    return jnp.sum(v, axis=0, keepdims=True)


def conv_pre(ext, par, n):
    total = par[4:5, :] + par[0:1, :] * ext[5 : 5 + n, :]
    for tap in range(1, 4):
        total = total + par[tap : tap + 1, :] * ext[5 + tap : 5 + tap + n, :]
    return total


def scan_prep(small, hp, ind, n):
    rows, cols = iotas(n)
    raw = small[:, 2 * STATE :] + hp[0:1, :]
    step = softplus(raw)
    rate = -jnp.exp(hp[1:2, :])
    lower = jnp.where(rows >= cols, 1.0, 0.0).astype(F32)
    cs = mm(lower, step * rate, precision=HIGH)
    tail = jnp.exp(cs[n - 1 : n, :] - cs)
    wide = expand(jnp.concatenate([step, jnp.exp(cs), tail], axis=0), ind)
    return raw, step, rate, cs, wide[0:n], wide[n : 2 * n], wide[2 * n : 3 * n]


def fwd_body(
    inner_ref, gate_ref, small_ref, cp_ref, sp_ref, hp_ref, ind_ref,
    ssd_ref, scaled_ref, sq_ref, st_ref,
    ext, exts, state,
    *, heads, per,
):
    n = CHUNK

    @pl.when(lax.rem(pl.program_id(0), per) == 0)
    def _():
        ext[0:8, :] = jnp.zeros((8, ext.shape[1]), F32)
        exts[0:8, :] = jnp.zeros((8, exts.shape[1]), F32)
        state[...] = jnp.zeros_like(state)

    rows, cols = iotas(n)
    ind = ind_ref[...]
    ext[8 : 8 + n, :] = inner_ref[...]
    pre = conv_pre(ext, cp_ref, n)
    x = pre * sigmoid(pre)
    ext[0:8, :] = ext[n : n + 8, :]
    exts[8 : 8 + n, :] = small_ref[:, : 2 * STATE]
    pres = conv_pre(exts, sp_ref, n)
    bc = (pres * sigmoid(pres)).astype(BF16)
    exts[0:8, :] = exts[n : n + 8, :]
    key, query = bc[:, :STATE], bc[:, STATE:]

    _, step, rate, cs, wide_step, wide_cs, wide_tail = scan_prep(small_ref, hp_ref, ind, n)
    cs2 = cs * LOG2E
    cs2t = cs2.T
    xs = x * wide_step
    half = lax.rem(lax.broadcasted_iota(jnp.int32, xs.shape, 1), 2 * HEAD) < HEAD
    xs0 = jnp.where(half, xs, 0.0)
    xs1 = (xs - xs0).astype(BF16)
    xs0 = xs0.astype(BF16)
    before = state[...]
    low = before.astype(BF16)
    st_ref[0] = low
    carried = mm(query, low) * wide_cs
    xw = (xs * wide_tail).astype(BF16)
    state[...] = before * wide_cs[n - 1 : n, :] + mm(key, xw, TN)
    scores = jnp.where(rows >= cols, mm(query, key, NT), 0.0)
    for pair in range(heads // 2):
        lanes = slice(pair * 2 * HEAD, (pair + 1) * 2 * HEAD)
        mats = []
        for h in (2 * pair, 2 * pair + 1):
            dec = jnp.exp2(jnp.minimum(cs2[:, h : h + 1] - cs2t[h : h + 1, :], 0.0))
            mats.append((scores * dec).astype(BF16))
        local = mm(
            jnp.concatenate(mats, axis=1),
            jnp.concatenate([xs0[:, lanes], xs1[:, lanes]], axis=0),
        )
        ssd_ref[:, lanes] = local + carried[:, lanes] + cp_ref[6:7, lanes] * x[:, lanes]
    gate = gate_ref[...]
    gated = ssd_ref[...] * (gate * sigmoid(gate))
    sq_ref[...] = jnp.sum(gated * gated, axis=1, keepdims=True)
    scaled_ref[...] = (gated * cp_ref[5:6, :]).astype(BF16)


def fwd_scan(inner_raw, gate_pre, small, cp, sp, hp, ind, heads):
    tokens_n, width = inner_raw.shape
    steps = tokens_n // CHUNK

    def row(w):
        return pl.BlockSpec((CHUNK, w), lambda c: (c, 0))

    def whole(a):
        return pl.BlockSpec(a.shape, lambda c: (0, 0))

    return pl.pallas_call(
        functools.partial(fwd_body, heads=heads, per=LEN // CHUNK),
        grid=(steps,),
        in_specs=[row(width), row(width), row(small.shape[1])] + [whole(a) for a in (cp, sp, hp, ind)],
        out_specs=[
            row(width),
            row(width),
            row(1),
            pl.BlockSpec((1, STATE, width), lambda c: (c, 0, 0)),
        ],
        out_shape=[
            jax.ShapeDtypeStruct((tokens_n, width), F32),
            jax.ShapeDtypeStruct((tokens_n, width), BF16),
            jax.ShapeDtypeStruct((tokens_n, 1), F32),
            jax.ShapeDtypeStruct((steps, STATE, width), BF16),
        ],
        scratch_shapes=[
            pltpu.VMEM((CHUNK + 8, width), F32),
            pltpu.VMEM((CHUNK + 8, 2 * STATE), F32),
            pltpu.VMEM((STATE, width), F32),
        ],
        compiler_params=pltpu.CompilerParams(vmem_limit_bytes=32 * 1024 * 1024),
        cost_estimate=pl.CostEstimate(flops=3 * 10**9, bytes_accessed=16 * 10**6, transcendentals=0),
        name="fwd_scan",
    )(inner_raw, gate_pre, small, cp, sp, hp, ind)


def bwd_body(
    sd_ref, ssd_ref, gate_ref, inner_ref, iprev_ref, small_ref, sprev_ref, coef_ref, st_ref,
    cp_ref, sp_ref, hp_ref, ind_ref,
    glow_ref, ilow_ref, sdel_ref, steplow_ref, dcp_ref, dsp_ref, dhp_ref,
    ext, exts, cde, cdes, dstate, rq,
    *, heads, per, steps,
):
    n = CHUNK
    at = pl.program_id(0)
    chunk = steps - 1 - at

    @pl.when(at == 0)
    def _():
        dcp_ref[...] = jnp.zeros_like(dcp_ref)
        dsp_ref[...] = jnp.zeros_like(dsp_ref)
        dhp_ref[...] = jnp.zeros_like(dhp_ref)
        rq[...] = jnp.zeros_like(rq)

    @pl.when(lax.rem(chunk, per) == per - 1)
    def _():
        cde[n : n + 8, :] = jnp.zeros((8, cde.shape[1]), F32)
        cdes[n : n + 8, :] = jnp.zeros((8, cdes.shape[1]), F32)
        dstate[...] = jnp.zeros_like(dstate)

    first = lax.rem(chunk, per) == 0
    keep = jnp.where(first, 0.0, 1.0).astype(F32)
    rows, cols = iotas(n)
    ind = ind_ref[...]
    ext[0:8, :] = iprev_ref[...] * keep
    ext[8 : 8 + n, :] = inner_ref[...]
    exts[0:8, :] = sprev_ref[:, : 2 * STATE] * keep
    exts[8 : 8 + n, :] = small_ref[:, : 2 * STATE]
    pre = conv_pre(ext, cp_ref, n)
    sig = sigmoid(pre)
    x = pre * sig
    slope = sig + x * (1.0 - sig)
    pres = conv_pre(exts, sp_ref, n)
    sigs = sigmoid(pres)
    acts = pres * sigs
    slopes = sigs + acts * (1.0 - sigs)
    bc = acts.astype(BF16)
    key, query = bc[:, :STATE], bc[:, STATE:]

    gate = gate_ref[...]
    gsig = sigmoid(gate)
    gact = gate * gsig
    ssd = ssd_ref[...]
    sd = sd_ref[...]
    gated = ssd * gact
    gd = cp_ref[5:6, :] * sd - coef_ref[...] * gated
    dcp_ref[5:6, :] += colsum(gated * sd)
    dy = gd * gact
    glow_ref[...] = (gd * ssd * (gsig + gact * (1.0 - gsig))).astype(BF16)

    raw, step, rate, cs, wide_step, wide_cs, wide_tail = scan_prep(small_ref, hp_ref, ind, n)
    cs2 = cs * LOG2E
    cs2t = cs2.T
    xs = x * wide_step
    xsb = xs.astype(BF16)
    half = lax.rem(lax.broadcasted_iota(jnp.int32, xs.shape, 1), 2 * HEAD) < HEAD
    dy0 = jnp.where(half, dy, 0.0)
    dy1 = (dy - dy0).astype(BF16)
    dy0 = dy0.astype(BF16)
    low = st_ref[0]
    dst = dstate[...]
    dlow = dst.astype(BF16)
    dye = dy * wide_cs
    dyeb = dye.astype(BF16)
    up = headsum(dye * mm(query, low), ind)
    dxs_state = wide_tail * mm(key, dlow)
    down = headsum(xs * dxs_state, ind)
    qdel = mm(dyeb, low, NT)
    kdel = mm((xs * wide_tail).astype(BF16), dlow, NT)
    through = headsum(jnp.broadcast_to(colsum(low.astype(F32) * dst), (8, dst.shape[1])), ind)[0:1, :]
    through = through * jnp.exp(cs[n - 1 : n, :])
    dstate[...] = dst * wide_cs[n - 1 : n, :] + mm(query, dyeb, TN)

    scores = jnp.where(rows <= cols, mm(key, query, NT), 0.0)
    dscores = jnp.zeros((n, n), F32)
    colq = jnp.zeros((n, LANES), F32)
    lane = lax.broadcasted_iota(jnp.int32, (n, LANES), 1)
    dxs = []
    for pair in range(heads // 2):
        lanes = slice(pair * 2 * HEAD, (pair + 1) * 2 * HEAD)
        stacked = jnp.concatenate([dy0[:, lanes], dy1[:, lanes]], axis=0)
        both = mm(xsb[:, lanes], stacked, NT)
        mats = []
        for which, h in enumerate((2 * pair, 2 * pair + 1)):
            dec = jnp.exp2(jnp.minimum(cs2t[h : h + 1, :] - cs2[:, h : h + 1], 0.0))
            mats.append((scores * dec).astype(BF16))
            term = dec * both[:, which * n : (which + 1) * n]
            dscores = dscores + term
            quad = scores * term
            rq[h : h + 1, :] = colsum(quad)
            colq = jnp.where(lane == h, jnp.sum(quad, axis=1, keepdims=True), colq)
        dxs.append(mm(jnp.concatenate(mats, axis=1), stacked))
    dxs = jnp.concatenate(dxs, axis=1) + dxs_state
    dscores = jnp.where(rows <= cols, dscores, 0.0).astype(BF16)
    kdel = kdel + mm(dscores, query)
    qdel = qdel + mm(dscores, key, TN)

    upper = jnp.where(rows <= cols, 1.0, 0.0).astype(F32)
    strict = jnp.where(rows > cols, 1.0, 0.0).astype(F32)
    da = mm(upper, rq[...].T - colq + up, precision=HIGH) + mm(strict, down, precision=HIGH) + through
    size = headsum(x * dxs, ind) + rate * da
    step_pre = size * sigmoid(raw)
    steplow_ref[...] = step_pre.astype(BF16)
    dhp_ref[0:1, :] += colsum(step_pre)
    dhp_ref[1:2, :] += rate * colsum(step * da)
    dcp_ref[6:7, :] += colsum(dy * x)

    cd = (dxs * wide_step + cp_ref[6:7, :] * dy) * slope
    cde[0:n, :] = cd
    total = cp_ref[3:4, :] * cd
    for tap in range(3):
        total = total + cp_ref[tap : tap + 1, :] * cde[3 - tap : 3 - tap + n, :]
    ilow_ref[...] = total.astype(BF16)
    for tap in range(4):
        dcp_ref[tap : tap + 1, :] += colsum(cd * ext[5 + tap : 5 + tap + n, :])
    dcp_ref[4:5, :] += colsum(cd)
    cde[n : n + 8, :] = cde[0:8, :]

    cds = jnp.concatenate([kdel, qdel], axis=1) * slopes
    cdes[0:n, :] = cds
    total = sp_ref[3:4, :] * cds
    for tap in range(3):
        total = total + sp_ref[tap : tap + 1, :] * cdes[3 - tap : 3 - tap + n, :]
    sdel_ref[...] = total.astype(BF16)
    for tap in range(4):
        dsp_ref[tap : tap + 1, :] += colsum(cds * exts[5 + tap : 5 + tap + n, :])
    dsp_ref[4:5, :] += colsum(cds)
    cdes[n : n + 8, :] = cdes[0:8, :]

    @pl.when(at == steps - 1)
    def _():
        dhp_ref[2:3, :] = headsum(jnp.broadcast_to(dcp_ref[6:7, :], (8, dcp_ref.shape[1])), ind)[0:1, :]


def bwd_scan(sd, ssd, gate_pre, inner_raw, small, coef, states, cp, sp, hp, ind, heads):
    tokens_n, width = inner_raw.shape
    steps = tokens_n // CHUNK
    wide_small = small.shape[1]

    def row(w):
        return pl.BlockSpec((CHUNK, w), lambda c: (steps - 1 - c, 0))

    def prev(w):
        return pl.BlockSpec((8, w), lambda c: (jnp.maximum((steps - 1 - c) * (CHUNK // 8) - 1, 0), 0))

    def whole(a):
        return pl.BlockSpec(a.shape, lambda c: (0, 0))

    def flat(r, w):
        return pl.BlockSpec((r, w), lambda c: (0, 0))

    return pl.pallas_call(
        functools.partial(bwd_body, heads=heads, per=LEN // CHUNK, steps=steps),
        grid=(steps,),
        in_specs=[
            row(width), row(width), row(width), row(width), prev(width),
            row(wide_small), prev(wide_small), row(1),
            pl.BlockSpec((1, STATE, width), lambda c: (steps - 1 - c, 0, 0)),
        ] + [whole(a) for a in (cp, sp, hp, ind)],
        out_specs=[
            row(width), row(width), row(2 * STATE), row(LANES),
            flat(8, width), flat(8, 2 * STATE), flat(8, LANES),
        ],
        out_shape=[
            jax.ShapeDtypeStruct((tokens_n, width), BF16),
            jax.ShapeDtypeStruct((tokens_n, width), BF16),
            jax.ShapeDtypeStruct((tokens_n, 2 * STATE), BF16),
            jax.ShapeDtypeStruct((tokens_n, LANES), BF16),
            jax.ShapeDtypeStruct((8, width), F32),
            jax.ShapeDtypeStruct((8, 2 * STATE), F32),
            jax.ShapeDtypeStruct((8, LANES), F32),
        ],
        scratch_shapes=[
            pltpu.VMEM((CHUNK + 8, width), F32),
            pltpu.VMEM((CHUNK + 8, 2 * STATE), F32),
            pltpu.VMEM((CHUNK + 8, width), F32),
            pltpu.VMEM((CHUNK + 8, 2 * STATE), F32),
            pltpu.VMEM((STATE, width), F32),
            pltpu.VMEM((LANES, CHUNK), F32),
        ],
        compiler_params=pltpu.CompilerParams(vmem_limit_bytes=40 * 1024 * 1024),
        cost_estimate=pl.CostEstimate(flops=8 * 10**9, bytes_accessed=24 * 10**6, transcendentals=0),
        name="bwd_scan",
    )(sd, ssd, gate_pre, inner_raw, inner_raw, small, small, coef, states, cp, sp, hp, ind)


def shards(
    tokens, inproj, stepproj, stateproj, outproj, convinner, biasinner, convstate, biasstate,
    stepbias, decaylog, skipgain, normgain, inputgain, cotangent,
):
    layers = inproj.shape[0]
    width = inproj.shape[3]
    heads = stepproj.shape[2]
    model = tokens.shape[1]
    pad = LANES - heads
    ind = (jnp.arange(LANES)[:, None] == (jnp.arange(width) // HEAD)[None, :]).astype(BF16)
    small_w = jnp.concatenate([stateproj, stepproj, jnp.zeros((layers, model, pad), BF16)], axis=2)
    zero_row = jnp.zeros((layers, 1, width), F32)
    cp = jnp.concatenate(
        [convinner, biasinner[:, None], normgain[:, None], jnp.repeat(skipgain, HEAD, axis=1)[:, None], zero_row],
        axis=1,
    )
    sp = jnp.concatenate([convstate, biasstate[:, None], jnp.zeros((layers, 3, 2 * STATE), F32)], axis=1)
    hp = jnp.concatenate(
        [jnp.pad(jnp.stack([stepbias, decaylog], axis=1), ((0, 0), (0, 0), (0, pad))), jnp.zeros((layers, 6, LANES), F32)],
        axis=1,
    )
    w_in = [lax.all_gather(inproj[at], "dp", axis=1, tiled=True) for at in range(layers)]
    w_out = [lax.all_gather(outproj[at].T, "dp", axis=0, tiled=True) for at in range(layers)]

    residual = tokens.astype(F32)
    kept = []
    for at in range(layers):
        rnorm = lax.rsqrt(jnp.mean(residual * residual, axis=1, keepdims=True) + EPS)
        normed = (residual * rnorm * inputgain[at]).astype(BF16)
        gate_pre = mm(normed, w_in[at][0])
        inner_raw = mm(normed, w_in[at][1])
        small = mm(normed, small_w[at])
        ssd, scaled, sq, states = fwd_scan(inner_raw, gate_pre, small, cp[at], sp[at], hp[at], ind, heads)
        partial = mm(scaled, w_out[at], NT)
        summed = lax.psum(partial.astype(BF16), "tensor").astype(F32)
        factor = lax.rsqrt(lax.psum(sq, "tensor") / INNER + EPS)
        kept.append((residual, rnorm, normed, gate_pre, inner_raw, small, ssd, scaled, states, summed, factor))
        residual = residual + factor * summed
    mixed = residual.astype(BF16)

    upstream = cotangent.astype(F32)
    big = [None] * layers
    little = [None] * layers
    for at in reversed(range(layers)):
        residual_in, rnorm, normed, gate_pre, inner_raw, small, ssd, scaled, states, summed, factor = kept[at]
        factor_delta = jnp.sum(upstream * summed, axis=1, keepdims=True)
        delta_out = (factor * upstream).astype(BF16)
        scaled_delta = mm(delta_out, w_out[at])
        coef = factor * factor * factor * factor_delta / INNER
        glow, ilow, sdel, steplow, dcp, dsp, dhp = bwd_scan(
            scaled_delta, ssd, gate_pre, inner_raw, small, coef, states, cp[at], sp[at], hp[at], ind, heads
        )
        part = mm(glow, w_in[at][0], NT) + mm(ilow, w_in[at][1], NT) + mm(steplow, small_w[at][:, 2 * STATE :], NT)
        back, sdel = lax.psum((part.astype(BF16), sdel), "tensor")
        back = back.astype(F32) + mm(sdel, small_w[at][:, : 2 * STATE], NT)
        term = jnp.concatenate([mm(normed, glow, TN), mm(normed, ilow, TN), mm(delta_out, scaled, TN)], axis=1)
        big[at] = lax.psum_scatter(term.astype(BF16), "dp", scatter_dimension=0, tiled=True).astype(F32)
        step_grad = mm(normed, steplow, TN)[:, :heads]
        state_grad = mm(normed, sdel, TN)
        plain = back * residual_in * rnorm
        gain_grad = jnp.sum(plain, axis=0)
        gained = back * inputgain[at]
        mean = jnp.mean(gained * residual_in, axis=1, keepdims=True)
        upstream = upstream + rnorm * gained - rnorm * rnorm * rnorm * residual_in * mean
        dsp = lax.psum(dsp, "tensor")
        little[at] = (step_grad, state_grad, dcp, dsp, dhp, gain_grad)
    big = jnp.stack(big)
    inproj_grad = jnp.stack([big[:, :, :width], big[:, :, width : 2 * width]], axis=1)
    outproj_grad = jnp.swapaxes(big[:, :, 2 * width :], 1, 2)
    stacked = [jnp.stack([little[at][m] for at in range(layers)]) for m in range(6)]
    step_grad, state_grad, dcp, dsp, dhp, gain_grad = [
        v.astype(F32)
        for v in lax.psum(
            (stacked[0].astype(BF16), stacked[1].astype(BF16), stacked[2], stacked[3], stacked[4], stacked[5]), "dp"
        )
    ]
    return (
        mixed,
        upstream,
        inproj_grad,
        step_grad,
        state_grad,
        outproj_grad,
        dcp[:, 0:4],
        dcp[:, 4],
        dsp[:, 0:4],
        dsp[:, 4],
        dhp[:, 0, :heads],
        dhp[:, 1, :heads],
        dhp[:, 2, :heads],
        dcp[:, 5],
        gain_grad,
    )


def solution(mesh):
    in_specs = (
        P("dp", None),
        P(None, None, "dp", "tensor"),
        P(None, None, "tensor"),
        P(),
        P(None, "tensor", "dp"),
        P(None, None, "tensor"),
        P(None, "tensor"),
        P(),
        P(),
        P(None, "tensor"),
        P(None, "tensor"),
        P(None, "tensor"),
        P(None, "tensor"),
        P(),
        P("dp", None),
    )
    out_specs = (
        P("dp", None),
        P("dp", None),
        P(None, None, "dp", "tensor"),
        P(None, None, "tensor"),
        P(),
        P(None, "tensor", "dp"),
        P(None, None, "tensor"),
        P(None, "tensor"),
        P(),
        P(),
        P(None, "tensor"),
        P(None, "tensor"),
        P(None, "tensor"),
        P(None, "tensor"),
        P(),
    )
    return jax.shard_map(shards, mesh=mesh, in_specs=in_specs, out_specs=out_specs, check_vma=False)
```

```python
import functools

import jax
import jax.numpy as jnp
from jax import lax
from jax.experimental import pallas as pl
from jax.experimental.pallas import tpu as pltpu
from jax.sharding import PartitionSpec as P

STATE = 128
LEN = 1024
INNER = 3072
HEAD = 64
CHUNK = 128
LANES = 128
EPS = 1e-05
LOG2E = 1.4426950408889634

HIGH = lax.Precision.HIGHEST
NN = (((1,), (0,)), ((), ()))
NT = (((1,), (1,)), ((), ()))
TN = (((0,), (0,)), ((), ()))
F32 = jnp.float32
BF16 = jnp.bfloat16


def mm(left, right, dims=NN, precision=None):
    return lax.dot_general(left, right, dims, precision=precision, preferred_element_type=F32)


def sigmoid(v):
    return 0.5 * jnp.tanh(0.5 * v) + 0.5


def softplus(v):
    return jnp.maximum(v, 0.0) + jnp.log1p(jnp.exp(-jnp.abs(v)))


def split16(v):
    top = v.astype(BF16)
    return top, (v - top.astype(F32)).astype(BF16)


def expand(v, ind):
    top, rest = split16(v)
    return mm(top, ind) + mm(rest, ind)


def headsum(v, ind):
    top, rest = split16(v)
    return mm(top, ind, NT) + mm(rest, ind, NT)


def iotas(n):
    return (
        lax.broadcasted_iota(jnp.int32, (n, n), 0),
        lax.broadcasted_iota(jnp.int32, (n, n), 1),
    )


def colsum(v):
    return jnp.sum(v, axis=0, keepdims=True)


def conv_pre(ext, par, n):
    total = par[4:5, :] + par[0:1, :] * ext[5 : 5 + n, :]
    for tap in range(1, 4):
        total = total + par[tap : tap + 1, :] * ext[5 + tap : 5 + tap + n, :]
    return total


def scan_prep(small, hp, ind, n):
    rows, cols = iotas(n)
    raw = small[:, 2 * STATE :] + hp[0:1, :]
    step = softplus(raw)
    rate = -jnp.exp(hp[1:2, :])
    lower = jnp.where(rows >= cols, 1.0, 0.0).astype(F32)
    cs = mm(lower, step * rate, precision=HIGH)
    tail = jnp.exp(cs[n - 1 : n, :] - cs)
    wide = expand(jnp.concatenate([step, jnp.exp(cs), tail], axis=0), ind)
    return raw, step, rate, cs, wide[0:n], wide[n : 2 * n], wide[2 * n : 3 * n]


def fwd_body(
    inner_ref, gate_ref, small_ref, cp_ref, sp_ref, hp_ref, ind_ref,
    ssd_ref, scaled_ref, sq_ref, st_ref,
    ext, exts, state,
    *, heads, per,
):
    n = CHUNK

    @pl.when(lax.rem(pl.program_id(0), per) == 0)
    def _():
        ext[0:8, :] = jnp.zeros((8, ext.shape[1]), F32)
        exts[0:8, :] = jnp.zeros((8, exts.shape[1]), F32)
        state[...] = jnp.zeros_like(state)

    rows, cols = iotas(n)
    ind = ind_ref[...]
    ext[8 : 8 + n, :] = inner_ref[...]
    pre = conv_pre(ext, cp_ref, n)
    x = pre * sigmoid(pre)
    ext[0:8, :] = ext[n : n + 8, :]
    exts[8 : 8 + n, :] = small_ref[:, : 2 * STATE]
    pres = conv_pre(exts, sp_ref, n)
    bc = (pres * sigmoid(pres)).astype(BF16)
    exts[0:8, :] = exts[n : n + 8, :]
    key, query = bc[:, :STATE], bc[:, STATE:]

    _, step, rate, cs, wide_step, wide_cs, wide_tail = scan_prep(small_ref, hp_ref, ind, n)
    cs2 = cs * LOG2E
    cs2t = cs2.T
    xs = x * wide_step
    half = lax.rem(lax.broadcasted_iota(jnp.int32, xs.shape, 1), 2 * HEAD) < HEAD
    xs0 = jnp.where(half, xs, 0.0)
    xs1 = (xs - xs0).astype(BF16)
    xs0 = xs0.astype(BF16)
    before = state[...]
    low = before.astype(BF16)
    st_ref[0] = low
    carried = mm(query, low) * wide_cs
    xw = (xs * wide_tail).astype(BF16)
    state[...] = before * wide_cs[n - 1 : n, :] + mm(key, xw, TN)
    scores = jnp.where(rows >= cols, mm(query, key, NT), 0.0)
    for pair in range(heads // 2):
        lanes = slice(pair * 2 * HEAD, (pair + 1) * 2 * HEAD)
        mats = []
        for h in (2 * pair, 2 * pair + 1):
            dec = jnp.exp2(jnp.minimum(cs2[:, h : h + 1] - cs2t[h : h + 1, :], 0.0))
            mats.append((scores * dec).astype(BF16))
        local = mm(
            jnp.concatenate(mats, axis=1),
            jnp.concatenate([xs0[:, lanes], xs1[:, lanes]], axis=0),
        )
        ssd_ref[:, lanes] = local + carried[:, lanes] + cp_ref[6:7, lanes] * x[:, lanes]
    gate = gate_ref[...]
    gated = ssd_ref[...] * (gate * sigmoid(gate))
    sq_ref[...] = jnp.sum(gated * gated, axis=1, keepdims=True)
    scaled_ref[...] = (gated * cp_ref[5:6, :]).astype(BF16)


def fwd_scan(inner_raw, gate_pre, small, cp, sp, hp, ind, heads):
    tokens_n, width = inner_raw.shape
    steps = tokens_n // CHUNK

    def row(w):
        return pl.BlockSpec((CHUNK, w), lambda c: (c, 0))

    def whole(a):
        return pl.BlockSpec(a.shape, lambda c: (0, 0))

    return pl.pallas_call(
        functools.partial(fwd_body, heads=heads, per=LEN // CHUNK),
        grid=(steps,),
        in_specs=[row(width), row(width), row(small.shape[1])] + [whole(a) for a in (cp, sp, hp, ind)],
        out_specs=[
            row(width),
            row(width),
            row(1),
            pl.BlockSpec((1, STATE, width), lambda c: (c, 0, 0)),
        ],
        out_shape=[
            jax.ShapeDtypeStruct((tokens_n, width), F32),
            jax.ShapeDtypeStruct((tokens_n, width), BF16),
            jax.ShapeDtypeStruct((tokens_n, 1), F32),
            jax.ShapeDtypeStruct((steps, STATE, width), BF16),
        ],
        scratch_shapes=[
            pltpu.VMEM((CHUNK + 8, width), F32),
            pltpu.VMEM((CHUNK + 8, 2 * STATE), F32),
            pltpu.VMEM((STATE, width), F32),
        ],
        compiler_params=pltpu.CompilerParams(vmem_limit_bytes=32 * 1024 * 1024),
        cost_estimate=pl.CostEstimate(flops=3 * 10**9, bytes_accessed=16 * 10**6, transcendentals=0),
        name="fwd_scan",
    )(inner_raw, gate_pre, small, cp, sp, hp, ind)


def bwd_body(
    sd_ref, ssd_ref, gate_ref, inner_ref, iprev_ref, small_ref, sprev_ref, coef_ref, st_ref,
    cp_ref, sp_ref, hp_ref, ind_ref,
    glow_ref, ilow_ref, sdel_ref, steplow_ref, dcp_ref, dsp_ref, dhp_ref,
    ext, exts, cde, cdes, dstate, rq,
    *, heads, per, steps,
):
    n = CHUNK
    at = pl.program_id(0)
    chunk = steps - 1 - at

    @pl.when(at == 0)
    def _():
        dcp_ref[...] = jnp.zeros_like(dcp_ref)
        dsp_ref[...] = jnp.zeros_like(dsp_ref)
        dhp_ref[...] = jnp.zeros_like(dhp_ref)
        rq[...] = jnp.zeros_like(rq)

    @pl.when(lax.rem(chunk, per) == per - 1)
    def _():
        cde[n : n + 8, :] = jnp.zeros((8, cde.shape[1]), F32)
        cdes[n : n + 8, :] = jnp.zeros((8, cdes.shape[1]), F32)
        dstate[...] = jnp.zeros_like(dstate)

    first = lax.rem(chunk, per) == 0
    keep = jnp.where(first, 0.0, 1.0).astype(F32)
    rows, cols = iotas(n)
    ind = ind_ref[...]
    ext[0:8, :] = iprev_ref[...] * keep
    ext[8 : 8 + n, :] = inner_ref[...]
    exts[0:8, :] = sprev_ref[:, : 2 * STATE] * keep
    exts[8 : 8 + n, :] = small_ref[:, : 2 * STATE]
    pre = conv_pre(ext, cp_ref, n)
    sig = sigmoid(pre)
    x = pre * sig
    slope = sig + x * (1.0 - sig)
    pres = conv_pre(exts, sp_ref, n)
    sigs = sigmoid(pres)
    acts = pres * sigs
    slopes = sigs + acts * (1.0 - sigs)
    bc = acts.astype(BF16)
    key, query = bc[:, :STATE], bc[:, STATE:]

    gate = gate_ref[...]
    gsig = sigmoid(gate)
    gact = gate * gsig
    ssd = ssd_ref[...]
    sd = sd_ref[...]
    gated = ssd * gact
    gd = cp_ref[5:6, :] * sd - coef_ref[...] * gated
    dcp_ref[5:6, :] += colsum(gated * sd)
    dy = gd * gact
    glow_ref[...] = (gd * ssd * (gsig + gact * (1.0 - gsig))).astype(BF16)

    raw, step, rate, cs, wide_step, wide_cs, wide_tail = scan_prep(small_ref, hp_ref, ind, n)
    cs2 = cs * LOG2E
    cs2t = cs2.T
    xs = x * wide_step
    xsb = xs.astype(BF16)
    half = lax.rem(lax.broadcasted_iota(jnp.int32, xs.shape, 1), 2 * HEAD) < HEAD
    dy0 = jnp.where(half, dy, 0.0)
    dy1 = (dy - dy0).astype(BF16)
    dy0 = dy0.astype(BF16)
    low = st_ref[0]
    dst = dstate[...]
    dlow = dst.astype(BF16)
    dye = dy * wide_cs
    dyeb = dye.astype(BF16)
    up = headsum(dye * mm(query, low), ind)
    dxs_state = wide_tail * mm(key, dlow)
    down = headsum(xs * dxs_state, ind)
    qdel = mm(dyeb, low, NT)
    kdel = mm((xs * wide_tail).astype(BF16), dlow, NT)
    through = headsum(jnp.broadcast_to(colsum(low.astype(F32) * dst), (8, dst.shape[1])), ind)[0:1, :]
    through = through * jnp.exp(cs[n - 1 : n, :])
    dstate[...] = dst * wide_cs[n - 1 : n, :] + mm(query, dyeb, TN)

    scores = jnp.where(rows <= cols, mm(key, query, NT), 0.0)
    dscores = jnp.zeros((n, n), F32)
    colq = jnp.zeros((n, LANES), F32)
    lane = lax.broadcasted_iota(jnp.int32, (n, LANES), 1)
    dxs = []
    for pair in range(heads // 2):
        lanes = slice(pair * 2 * HEAD, (pair + 1) * 2 * HEAD)
        stacked = jnp.concatenate([dy0[:, lanes], dy1[:, lanes]], axis=0)
        both = mm(xsb[:, lanes], stacked, NT)
        mats = []
        for which, h in enumerate((2 * pair, 2 * pair + 1)):
            dec = jnp.exp2(jnp.minimum(cs2t[h : h + 1, :] - cs2[:, h : h + 1], 0.0))
            mats.append((scores * dec).astype(BF16))
            term = dec * both[:, which * n : (which + 1) * n]
            dscores = dscores + term
            quad = scores * term
            rq[h : h + 1, :] = colsum(quad)
            colq = jnp.where(lane == h, jnp.sum(quad, axis=1, keepdims=True), colq)
        dxs.append(mm(jnp.concatenate(mats, axis=1), stacked))
    dxs = jnp.concatenate(dxs, axis=1) + dxs_state
    dscores = jnp.where(rows <= cols, dscores, 0.0).astype(BF16)
    kdel = kdel + mm(dscores, query)
    qdel = qdel + mm(dscores, key, TN)

    upper = jnp.where(rows <= cols, 1.0, 0.0).astype(F32)
    strict = jnp.where(rows > cols, 1.0, 0.0).astype(F32)
    da = mm(upper, rq[...].T - colq + up, precision=HIGH) + mm(strict, down, precision=HIGH) + through
    size = headsum(x * dxs, ind) + rate * da
    step_pre = size * sigmoid(raw)
    steplow_ref[...] = step_pre.astype(BF16)
    dhp_ref[0:1, :] += colsum(step_pre)
    dhp_ref[1:2, :] += rate * colsum(step * da)
    dcp_ref[6:7, :] += colsum(dy * x)

    cd = (dxs * wide_step + cp_ref[6:7, :] * dy) * slope
    cde[0:n, :] = cd
    total = cp_ref[3:4, :] * cd
    for tap in range(3):
        total = total + cp_ref[tap : tap + 1, :] * cde[3 - tap : 3 - tap + n, :]
    ilow_ref[...] = total.astype(BF16)
    for tap in range(4):
        dcp_ref[tap : tap + 1, :] += colsum(cd * ext[5 + tap : 5 + tap + n, :])
    dcp_ref[4:5, :] += colsum(cd)
    cde[n : n + 8, :] = cde[0:8, :]

    cds = jnp.concatenate([kdel, qdel], axis=1) * slopes
    cdes[0:n, :] = cds
    total = sp_ref[3:4, :] * cds
    for tap in range(3):
        total = total + sp_ref[tap : tap + 1, :] * cdes[3 - tap : 3 - tap + n, :]
    sdel_ref[...] = total.astype(BF16)
    for tap in range(4):
        dsp_ref[tap : tap + 1, :] += colsum(cds * exts[5 + tap : 5 + tap + n, :])
    dsp_ref[4:5, :] += colsum(cds)
    cdes[n : n + 8, :] = cdes[0:8, :]

    @pl.when(at == steps - 1)
    def _():
        dhp_ref[2:3, :] = headsum(jnp.broadcast_to(dcp_ref[6:7, :], (8, dcp_ref.shape[1])), ind)[0:1, :]


def bwd_scan(sd, ssd, gate_pre, inner_raw, small, coef, states, cp, sp, hp, ind, heads):
    tokens_n, width = inner_raw.shape
    steps = tokens_n // CHUNK
    wide_small = small.shape[1]

    def row(w):
        return pl.BlockSpec((CHUNK, w), lambda c: (steps - 1 - c, 0))

    def prev(w):
        return pl.BlockSpec((8, w), lambda c: (jnp.maximum((steps - 1 - c) * (CHUNK // 8) - 1, 0), 0))

    def whole(a):
        return pl.BlockSpec(a.shape, lambda c: (0, 0))

    def flat(r, w):
        return pl.BlockSpec((r, w), lambda c: (0, 0))

    return pl.pallas_call(
        functools.partial(bwd_body, heads=heads, per=LEN // CHUNK, steps=steps),
        grid=(steps,),
        in_specs=[
            row(width), row(width), row(width), row(width), prev(width),
            row(wide_small), prev(wide_small), row(1),
            pl.BlockSpec((1, STATE, width), lambda c: (steps - 1 - c, 0, 0)),
        ] + [whole(a) for a in (cp, sp, hp, ind)],
        out_specs=[
            row(width), row(width), row(2 * STATE), row(LANES),
            flat(8, width), flat(8, 2 * STATE), flat(8, LANES),
        ],
        out_shape=[
            jax.ShapeDtypeStruct((tokens_n, width), BF16),
            jax.ShapeDtypeStruct((tokens_n, width), BF16),
            jax.ShapeDtypeStruct((tokens_n, 2 * STATE), BF16),
            jax.ShapeDtypeStruct((tokens_n, LANES), BF16),
            jax.ShapeDtypeStruct((8, width), F32),
            jax.ShapeDtypeStruct((8, 2 * STATE), F32),
            jax.ShapeDtypeStruct((8, LANES), F32),
        ],
        scratch_shapes=[
            pltpu.VMEM((CHUNK + 8, width), F32),
            pltpu.VMEM((CHUNK + 8, 2 * STATE), F32),
            pltpu.VMEM((CHUNK + 8, width), F32),
            pltpu.VMEM((CHUNK + 8, 2 * STATE), F32),
            pltpu.VMEM((STATE, width), F32),
            pltpu.VMEM((LANES, CHUNK), F32),
        ],
        compiler_params=pltpu.CompilerParams(vmem_limit_bytes=40 * 1024 * 1024),
        cost_estimate=pl.CostEstimate(flops=8 * 10**9, bytes_accessed=24 * 10**6, transcendentals=0),
        name="bwd_scan",
    )(sd, ssd, gate_pre, inner_raw, inner_raw, small, small, coef, states, cp, sp, hp, ind)


MESH = pl.DeviceIdType.MESH


def remote(src, dst, send, recv, where):
    return pltpu.make_async_remote_copy(
        src_ref=src, dst_ref=dst, send_sem=send, recv_sem=recv, device_id=where, device_id_type=MESH
    )


class Line:
    def __init__(self, size):
        self.n = size // 2
        me = lax.axis_index("dp")
        self.me = me
        self.at = me // 2
        self.side = lax.rem(me, 2)
        self.pair = {"dp": me + 1 - 2 * self.side}
        self.right = {"dp": jnp.minimum(me + 2, size - 1)}
        self.left = {"dp": jnp.maximum(me - 2, 0)}
        self.has_left = self.at > 0
        self.has_right = self.at < self.n - 1

    def greet(self, barrier):
        pl.semaphore_signal(barrier, inc=1, device_id=self.pair, device_id_type=MESH)

        @pl.when(self.has_left)
        def _():
            pl.semaphore_signal(barrier, inc=1, device_id=self.left, device_id_type=MESH)

        @pl.when(self.has_right)
        def _():
            pl.semaphore_signal(barrier, inc=1, device_id=self.right, device_id_type=MESH)

        peers = 1 + self.has_left.astype(jnp.int32) + self.has_right.astype(jnp.int32)
        pl.semaphore_wait(barrier, peers)


class Gather:
    def __init__(self, line, own, full, keep, send, recv):
        self.line, self.own, self.full, self.keep, self.send, self.recv = line, own, full, keep, send, recv

    def copy(self, j, slab, way, src=None):
        where = (self.line.right, self.line.left, self.line.pair)[way]
        src = self.full.at[j, slab] if src is None else src
        return remote(src, self.full.at[j, slab], self.send.at[j, way, slab], self.recv.at[j, slab], where)

    def start(self, j):
        line = self.line
        pltpu.make_async_copy(self.own(j), self.full.at[j, line.me], self.keep.at[j]).start()

        @pl.when(line.has_right)
        def _():
            self.copy(j, line.me, 0, self.own(j)).start()

        @pl.when(line.has_left)
        def _():
            self.copy(j, line.me, 1, self.own(j)).start()

        self.copy(j, line.me, 2, self.own(j)).start()

    def relay(self, j, k):
        line = self.line

        @pl.when(line.at >= k)
        def _():
            slab = line.me - 2 * k
            self.copy(j, slab, 0).wait_recv()

            @pl.when(line.has_right)
            def _():
                self.copy(j, slab, 0).start()

            self.copy(j, slab, 2).start()

        @pl.when(line.at + k < line.n)
        def _():
            slab = line.me + 2 * k
            self.copy(j, slab, 1).wait_recv()

            @pl.when(line.has_left)
            def _():
                self.copy(j, slab, 1).start()

            self.copy(j, slab, 2).start()

    def arrive(self, j):
        line = self.line
        pltpu.make_async_copy(self.own(j), self.full.at[j, line.me], self.keep.at[j]).wait()
        for place in range(line.n):
            self.copy(j, 2 * place + 1 - line.side, 2).wait_recv()

    def drain(self, j):
        line = self.line
        for place in range(line.n):
            slab = 2 * place + line.side
            self.copy(j, slab, 2).wait_send()

            @pl.when(line.has_right & (place <= line.at))
            def _():
                self.copy(j, slab, 0).wait_send()

            @pl.when(line.has_left & (place >= line.at))
            def _():
                self.copy(j, slab, 1).wait_send()


def gather_body(in_ref, out_ref, full_ref, keep, send, recv, *, size, pieces):
    line = Line(size)
    line.greet(pltpu.get_barrier_semaphore())

    def own(j):
        layer, kind = j // 3, j % 3
        return out_ref.at[layer] if kind == 2 else in_ref.at[layer, 1 - kind]

    job = Gather(line, own, full_ref, keep, send, recv)
    for j in range(pieces):
        job.start(j)
        for k in range(1, line.n):
            job.relay(j, k)
    for j in range(pieces):
        job.arrive(j)
        job.drain(j)


def gather(inproj, outt, size):
    layers, _, rows, width = inproj.shape
    pieces = 3 * layers
    any_spec = pl.BlockSpec(memory_space=pl.ANY)
    return pl.pallas_call(
        functools.partial(gather_body, size=size, pieces=pieces),
        in_specs=[any_spec, any_spec],
        out_specs=any_spec,
        out_shape=jax.ShapeDtypeStruct((pieces, size, rows, width), BF16),
        scratch_shapes=[
            pltpu.SemaphoreType.DMA((pieces,)),
            pltpu.SemaphoreType.DMA((pieces, 3, size)),
            pltpu.SemaphoreType.DMA((pieces, size)),
        ],
        compiler_params=pltpu.CompilerParams(collective_id=0, has_side_effects=True),
        name="gather",
    )(inproj, outt)


class Square:
    def __init__(self):
        me = lax.axis_index("tensor")
        self.me = me
        self.half = lax.rem(me, 2)
        self.mate = {"tensor": me + 1 - 2 * self.half}
        self.across = {"tensor": lax.rem(me + 2, 4)}

    def greet(self, barrier):
        for who in (self.mate, self.across):
            pl.semaphore_signal(barrier, inc=1, device_id=who, device_id_type=MESH)
        pl.semaphore_wait(barrier, 2)


class Total:
    def __init__(self, square, part, total, got, mine, far, send, recv):
        self.square, self.part, self.total, self.got, self.mine, self.far = square, part, total, got, mine, far
        self.send, self.recv = send, recv

    def first(self, c):
        sq = self.square
        return remote(
            self.part.at[2 * c + 1 - sq.half], self.got.at[c], self.send.at[0, c], self.recv.at[0, c], sq.mate
        )

    def second(self, c):
        sq = self.square
        return remote(self.mine.at[c], self.far.at[c], self.send.at[1, c], self.recv.at[1, c], sq.across)

    def third(self, c):
        sq = self.square
        slot = 2 * c + sq.half
        return remote(self.total.at[slot], self.total.at[slot], self.send.at[2, c], self.recv.at[2, c], sq.mate)

    def step(self, kind, c):
        sq = self.square
        if kind == 0:
            self.first(c).start()
        elif kind == 1:
            self.first(c).wait_recv()
            both = self.part[2 * c + sq.half].astype(F32) + self.got[c].astype(F32)
            self.mine[c] = both.astype(BF16)
            self.second(c).start()
        elif kind == 2:
            self.second(c).wait_recv()
            both = self.mine[c].astype(F32) + self.far[c].astype(F32)
            self.total[2 * c + sq.half] = both.astype(BF16)
            self.third(c).start()
        else:
            self.third(c).wait_recv()
            for copy in (self.first(c), self.second(c), self.third(c)):
                copy.wait_send()


def total_body(part_ref, row_ref, total_ref, rows_ref, got, mine, far, rgot, send, recv, rsend, rrecv, *, chunks):
    square = Square()
    barrier = pltpu.get_barrier_semaphore()
    for who in (1, 2, 3):
        pl.semaphore_signal(barrier, inc=1, device_id={"tensor": lax.rem(square.me + who, 4)}, device_id_type=MESH)
    pl.semaphore_wait(barrier, 3)
    job = Total(square, part_ref, total_ref, got, mine, far, send, recv)
    copies = [
        remote(row_ref, rgot.at[square.me], rsend.at[who], rrecv.at[who], {"tensor": lax.rem(square.me + who, 4)})
        for who in (1, 2, 3)
    ]
    for copy in copies:
        copy.start()
    for c in range(chunks + 3):
        for kind in range(4):
            if 0 <= c - kind < chunks:
                job.step(kind, c - kind)
    rgot[square.me] = row_ref[...]
    for copy in copies:
        copy.wait()
    rows_ref[...] = (rgot[0] + rgot[1]) + (rgot[2] + rgot[3])


def total(part, row, chunks, cid):
    tokens_n, width = part.shape
    rows = tokens_n // chunks // 2
    vm = pl.BlockSpec(memory_space=pltpu.VMEM)
    out, sums = pl.pallas_call(
        functools.partial(total_body, chunks=chunks),
        in_specs=[vm, vm],
        out_specs=[vm, vm],
        out_shape=[
            jax.ShapeDtypeStruct((2 * chunks, rows, width), BF16),
            jax.ShapeDtypeStruct(row.shape, F32),
        ],
        scratch_shapes=[
            pltpu.VMEM((chunks, rows, width), BF16),
            pltpu.VMEM((chunks, rows, width), BF16),
            pltpu.VMEM((chunks, rows, width), BF16),
            pltpu.VMEM((4,) + row.shape, F32),
            pltpu.SemaphoreType.DMA((3, chunks)),
            pltpu.SemaphoreType.DMA((3, chunks)),
            pltpu.SemaphoreType.DMA((4,)),
            pltpu.SemaphoreType.DMA((4,)),
        ],
        compiler_params=pltpu.CompilerParams(
            collective_id=cid, has_side_effects=True, vmem_limit_bytes=40 * 1024 * 1024
        ),
        name="total",
    )(part.reshape(2 * chunks, rows, width), row)
    return out.reshape(tokens_n, width), sums


class Scatter:
    def __init__(self, line, part, out, near, fro, to, send, recv):
        self.line, self.part, self.out, self.near, self.fro, self.to = line, part, out, near, fro, to
        self.send, self.recv = send, recv

    def order(self):
        n = self.line.n
        seq = []
        for i in range((n + 1) // 2):
            seq.append(i)
            if n - 1 - i != i:
                seq.append(n - 1 - i)
        return seq

    def cross(self, j, i):
        line = self.line
        return remote(
            self.part.at[j, 2 * i + 1 - line.side], self.near.at[j, i], self.send.at[0, j, i], self.recv.at[0, j, i], line.pair
        )

    def leftward(self, j, i):
        return remote(
            self.part.at[j, 2 * i + self.line.side], self.fro.at[j, i], self.send.at[1, j, i], self.recv.at[1, j, i], self.line.left
        )

    def rightward(self, j, i):
        return remote(
            self.part.at[j, 2 * i + self.line.side], self.to.at[j, i], self.send.at[2, j, i], self.recv.at[2, j, i], self.line.right
        )

    def start(self, j):
        for i in self.order():
            self.cross(j, i).start()

    def fold(self, j, i):
        self.cross(j, i).wait_recv()
        slot = 2 * i + self.line.side
        self.part[j, slot] = (self.part[j, slot].astype(F32) + self.near[j, i].astype(F32)).astype(BF16)

    def pass_on(self, j, i):
        line = self.line
        slot = 2 * i + line.side

        @pl.when(i < line.at)
        def _():
            @pl.when(line.has_right)
            def _():
                self.leftward(j, i).wait_recv()
                self.part[j, slot] = (self.part[j, slot].astype(F32) + self.fro[j, i].astype(F32)).astype(BF16)

            self.leftward(j, i).start()

        @pl.when(i > line.at)
        def _():
            @pl.when(line.has_left)
            def _():
                self.rightward(j, i).wait_recv()
                self.part[j, slot] = (self.part[j, slot].astype(F32) + self.to[j, i].astype(F32)).astype(BF16)

            self.rightward(j, i).start()

    def finish(self, j):
        line = self.line
        for i in range(line.n):
            @pl.when(i == line.at)
            def _():
                slot = 2 * i + line.side
                self.out[j] = self.part[j, slot].astype(F32)

                @pl.when(line.has_right)
                def _():
                    self.leftward(j, i).wait_recv()
                    self.out[j] += self.fro[j, i].astype(F32)

                @pl.when(line.has_left)
                def _():
                    self.rightward(j, i).wait_recv()
                    self.out[j] += self.to[j, i].astype(F32)

    def drain(self, j):
        for i in range(self.line.n):
            self.cross(j, i).wait_send()

            @pl.when(i < self.line.at)
            def _():
                self.leftward(j, i).wait_send()

            @pl.when(i > self.line.at)
            def _():
                self.rightward(j, i).wait_send()


def scatter_body(part_ref, out_ref, part, near, fro, to, load, send, recv, *, size, pieces):
    line = Line(size)
    loads = [pltpu.make_async_copy(part_ref.at[j], part.at[j], load.at[j]) for j in range(pieces)]
    for copy in loads:
        copy.start()
    line.greet(pltpu.get_barrier_semaphore())
    job = Scatter(line, part, out_ref, near, fro, to, send, recv)
    for j in range(pieces):
        loads[j].wait()
        job.start(j)
    for j in range(pieces):
        for i in job.order():
            job.fold(j, i)
            job.pass_on(j, i)
    for j in range(pieces):
        job.finish(j)
        job.drain(j)


def scatter(part, size, cid):
    pieces, _, rows, width = part.shape
    n = size // 2
    return pl.pallas_call(
        functools.partial(scatter_body, size=size, pieces=pieces),
        in_specs=[pl.BlockSpec(memory_space=pl.ANY)],
        out_specs=pl.BlockSpec(memory_space=pltpu.VMEM),
        out_shape=jax.ShapeDtypeStruct((pieces, rows, width), F32),
        scratch_shapes=[
            pltpu.VMEM(part.shape, BF16),
            pltpu.VMEM((pieces, n, rows, width), BF16),
            pltpu.VMEM((pieces, n, rows, width), BF16),
            pltpu.VMEM((pieces, n, rows, width), BF16),
            pltpu.SemaphoreType.DMA((pieces,)),
            pltpu.SemaphoreType.DMA((3, pieces, n)),
            pltpu.SemaphoreType.DMA((3, pieces, n)),
        ],
        compiler_params=pltpu.CompilerParams(
            collective_id=cid, has_side_effects=True, vmem_limit_bytes=50 * 1024 * 1024
        ),
        name="scatter",
    )(part)


def shards(
    tokens, inproj, stepproj, stateproj, outproj, convinner, biasinner, convstate, biasstate,
    stepbias, decaylog, skipgain, normgain, inputgain, cotangent,
):
    layers = inproj.shape[0]
    width = inproj.shape[3]
    heads = stepproj.shape[2]
    model = tokens.shape[1]
    pad = LANES - heads
    ind = (jnp.arange(LANES)[:, None] == (jnp.arange(width) // HEAD)[None, :]).astype(BF16)
    small_w = jnp.concatenate([stateproj, stepproj, jnp.zeros((layers, model, pad), BF16)], axis=2)
    zero_row = jnp.zeros((layers, 1, width), F32)
    cp = jnp.concatenate(
        [convinner, biasinner[:, None], normgain[:, None], jnp.repeat(skipgain, HEAD, axis=1)[:, None], zero_row],
        axis=1,
    )
    sp = jnp.concatenate([convstate, biasstate[:, None], jnp.zeros((layers, 3, 2 * STATE), F32)], axis=1)
    hp = jnp.concatenate(
        [jnp.pad(jnp.stack([stepbias, decaylog], axis=1), ((0, 0), (0, 0), (0, pad))), jnp.zeros((layers, 6, LANES), F32)],
        axis=1,
    )
    size = lax.axis_size("dp")
    quarter = model // 4
    tensor_at = lax.axis_index("tensor")
    full = gather(inproj, jnp.swapaxes(outproj, 1, 2), size).reshape(3 * layers, model, width)
    w_in = [(full[3 * at + 1], full[3 * at]) for at in range(layers)]
    w_out = [full[3 * at + 2] for at in range(layers)]

    residual = tokens.astype(F32)
    kept = []
    for at in range(layers):
        rnorm = lax.rsqrt(jnp.mean(residual * residual, axis=1, keepdims=True) + EPS)
        normed = (residual * rnorm * inputgain[at]).astype(BF16)
        gate_pre = mm(normed, w_in[at][0])
        inner_raw = mm(normed, w_in[at][1])
        small = mm(normed, small_w[at])
        ssd, scaled, sq, states = fwd_scan(inner_raw, gate_pre, small, cp[at], sp[at], hp[at], ind, heads)
        partial = mm(scaled, w_out[at], NT)
        summed, sq = total(partial.astype(BF16), sq.reshape(8, -1), 8, 1)
        summed = summed.astype(F32)
        factor = lax.rsqrt(sq.reshape(-1, 1) / INNER + EPS)
        kept.append((residual, rnorm, normed, gate_pre, inner_raw, small, ssd, scaled, states, summed, factor))
        residual = residual + factor * summed
    mixed = residual.astype(BF16)

    upstream = cotangent.astype(F32)
    big = [None] * layers
    little = [None] * layers
    for at in reversed(range(layers)):
        residual_in, rnorm, normed, gate_pre, inner_raw, small, ssd, scaled, states, summed, factor = kept[at]
        factor_delta = jnp.sum(upstream * summed, axis=1, keepdims=True)
        delta_out = (factor * upstream).astype(BF16)
        scaled_delta = mm(delta_out, w_out[at])
        coef = factor * factor * factor * factor_delta / INNER
        glow, ilow, sdel, steplow, dcp, dsp, dhp = bwd_scan(
            scaled_delta, ssd, gate_pre, inner_raw, small, coef, states, cp[at], sp[at], hp[at], ind, heads
        )
        part = mm(glow, w_in[at][0], NT) + mm(ilow, w_in[at][1], NT) + mm(steplow, small_w[at][:, 2 * STATE :], NT)
        part = part + mm(sdel, small_w[at][:, : 2 * STATE], NT)
        part = jnp.concatenate([part.astype(BF16), sdel], axis=1)
        part, _ = total(part, jnp.zeros((8, LANES), F32), 8, 2)
        back, sdel = part[:, :model].astype(F32), part[:, model:]
        term = jnp.stack([mm(delta_out, scaled, TN), mm(normed, glow, TN), mm(normed, ilow, TN)])
        big[at] = scatter(term.astype(BF16).reshape(3, size, model // size, width), size, 3)
        step_grad = mm(normed, steplow, TN)[:, :heads]
        state_grad = mm(lax.dynamic_slice_in_dim(normed, tensor_at * quarter, quarter, axis=1), sdel, TN)
        plain = back * residual_in * rnorm
        gain_grad = jnp.sum(plain, axis=0)
        gained = back * inputgain[at]
        mean = jnp.mean(gained * residual_in, axis=1, keepdims=True)
        upstream = upstream + rnorm * gained - rnorm * rnorm * rnorm * residual_in * mean
        little[at] = (step_grad, state_grad, dcp, dsp, dhp, gain_grad)
    big = jnp.stack(big)
    inproj_grad = big[:, 1:]
    outproj_grad = jnp.swapaxes(big[:, 0], 1, 2)
    stacked = [jnp.stack([little[at][m] for at in range(layers)]) for m in range(6)]
    step_grad, state_grad, dcp, dsp, dhp, gain_grad = [
        v.astype(F32)
        for v in lax.psum(
            (stacked[0].astype(BF16), stacked[1].astype(BF16), stacked[2], stacked[3], stacked[4], stacked[5]), "dp"
        )
    ]
    state_grad, dsp = lax.all_gather(state_grad.astype(BF16), "tensor", axis=1, tiled=True), lax.psum(dsp, "tensor")
    state_grad = state_grad.astype(F32)
    return (
        mixed,
        upstream,
        inproj_grad,
        step_grad,
        state_grad,
        outproj_grad,
        dcp[:, 0:4],
        dcp[:, 4],
        dsp[:, 0:4],
        dsp[:, 4],
        dhp[:, 0, :heads],
        dhp[:, 1, :heads],
        dhp[:, 2, :heads],
        dcp[:, 5],
        gain_grad,
    )


def solution(mesh):
    in_specs = (
        P("dp", None),
        P(None, None, "dp", "tensor"),
        P(None, None, "tensor"),
        P(),
        P(None, "tensor", "dp"),
        P(None, None, "tensor"),
        P(None, "tensor"),
        P(),
        P(),
        P(None, "tensor"),
        P(None, "tensor"),
        P(None, "tensor"),
        P(None, "tensor"),
        P(),
        P("dp", None),
    )
    out_specs = (
        P("dp", None),
        P("dp", None),
        P(None, None, "dp", "tensor"),
        P(None, None, "tensor"),
        P(),
        P(None, "tensor", "dp"),
        P(None, None, "tensor"),
        P(None, "tensor"),
        P(),
        P(),
        P(None, "tensor"),
        P(None, "tensor"),
        P(None, "tensor"),
        P(None, "tensor"),
        P(),
    )
    return jax.shard_map(shards, mesh=mesh, in_specs=in_specs, out_specs=out_specs, check_vma=False)
```

```python
import functools

import jax
import jax.numpy as jnp
from jax import lax
from jax.experimental import pallas as pl
from jax.experimental.pallas import tpu as pltpu
from jax.sharding import PartitionSpec as P

STATE = 128
LEN = 1024
INNER = 3072
HEAD = 64
CHUNK = 128
LANES = 128
EPS = 1e-05
LOG2E = 1.4426950408889634

HIGH = lax.Precision.HIGHEST
NN = (((1,), (0,)), ((), ()))
NT = (((1,), (1,)), ((), ()))
TN = (((0,), (0,)), ((), ()))
F32 = jnp.float32
BF16 = jnp.bfloat16
MESH = pl.DeviceIdType.MESH


def remote(src, dst, send, recv, where):
    return pltpu.make_async_remote_copy(
        src_ref=src, dst_ref=dst, send_sem=send, recv_sem=recv, device_id=where, device_id_type=MESH
    )


class Line:
    def __init__(self, size):
        self.n = size // 2
        me = lax.axis_index("dp")
        self.me = me
        self.at = me // 2
        self.side = lax.rem(me, 2)
        self.pair = {"dp": me + 1 - 2 * self.side}
        self.right = {"dp": jnp.minimum(me + 2, size - 1)}
        self.left = {"dp": jnp.maximum(me - 2, 0)}
        self.has_left = self.at > 0
        self.has_right = self.at < self.n - 1

    def greet(self, barrier, more=()):
        for who in more:
            pl.semaphore_signal(barrier, inc=1, device_id=who, device_id_type=MESH)
        pl.semaphore_signal(barrier, inc=1, device_id=self.pair, device_id_type=MESH)

        @pl.when(self.has_left)
        def _():
            pl.semaphore_signal(barrier, inc=1, device_id=self.left, device_id_type=MESH)

        @pl.when(self.has_right)
        def _():
            pl.semaphore_signal(barrier, inc=1, device_id=self.right, device_id_type=MESH)

        peers = 1 + len(more) + self.has_left.astype(jnp.int32) + self.has_right.astype(jnp.int32)
        pl.semaphore_wait(barrier, peers)


class Gather:
    def __init__(self, line, own, full, keep, send, recv):
        self.line, self.own, self.full, self.keep, self.send, self.recv = line, own, full, keep, send, recv

    def copy(self, j, slab, way, src=None):
        where = (self.line.right, self.line.left, self.line.pair)[way]
        src = self.full.at[j, slab] if src is None else src
        return remote(src, self.full.at[j, slab], self.send.at[j, way, slab], self.recv.at[j, slab], where)

    def start(self, j):
        line = self.line
        pltpu.make_async_copy(self.own(j), self.full.at[j, line.me], self.keep.at[j]).start()

        @pl.when(line.has_right)
        def _():
            self.copy(j, line.me, 0, self.own(j)).start()

        @pl.when(line.has_left)
        def _():
            self.copy(j, line.me, 1, self.own(j)).start()

        self.copy(j, line.me, 2, self.own(j)).start()

    def relay(self, j, k):
        line = self.line

        @pl.when(line.at >= k)
        def _():
            slab = line.me - 2 * k
            self.copy(j, slab, 0).wait_recv()

            @pl.when(line.has_right)
            def _():
                self.copy(j, slab, 0).start()

            self.copy(j, slab, 2).start()

        @pl.when(line.at + k < line.n)
        def _():
            slab = line.me + 2 * k
            self.copy(j, slab, 1).wait_recv()

            @pl.when(line.has_left)
            def _():
                self.copy(j, slab, 1).start()

            self.copy(j, slab, 2).start()

    def arrive(self, j):
        line = self.line
        pltpu.make_async_copy(self.own(j), self.full.at[j, line.me], self.keep.at[j]).wait()
        for place in range(line.n):
            self.copy(j, 2 * place + 1 - line.side, 2).wait_recv()

    def drain(self, j):
        line = self.line
        for place in range(line.n):
            slab = 2 * place + line.side
            self.copy(j, slab, 2).wait_send()

            @pl.when(line.has_right & (place <= line.at))
            def _():
                self.copy(j, slab, 0).wait_send()

            @pl.when(line.has_left & (place >= line.at))
            def _():
                self.copy(j, slab, 1).wait_send()


class Square:
    def __init__(self):
        me = lax.axis_index("tensor")
        self.me = me
        self.half = lax.rem(me, 2)
        self.mate = {"tensor": me + 1 - 2 * self.half}
        self.across = {"tensor": lax.rem(me + 2, 4)}

    def others(self):
        return [{"tensor": lax.rem(self.me + k, 4)} for k in (1, 2, 3)]


class Total:
    def __init__(self, square, part, total, got, mine, far, send, recv):
        self.square, self.part, self.total, self.got, self.mine, self.far = square, part, total, got, mine, far
        self.send, self.recv = send, recv

    def first(self, c):
        sq = self.square
        return remote(
            self.part.at[2 * c + 1 - sq.half], self.got.at[c], self.send.at[0, c], self.recv.at[0, c], sq.mate
        )

    def second(self, c):
        sq = self.square
        return remote(self.mine.at[c], self.far.at[c], self.send.at[1, c], self.recv.at[1, c], sq.across)

    def third(self, c):
        sq = self.square
        slot = 2 * c + sq.half
        return remote(self.total.at[slot], self.total.at[slot], self.send.at[2, c], self.recv.at[2, c], sq.mate)

    def step(self, kind, c):
        sq = self.square
        if kind == 0:
            self.first(c).start()
        elif kind == 1:
            self.first(c).wait_recv()
            both = self.part[2 * c + sq.half].astype(F32) + self.got[c].astype(F32)
            self.mine[c] = both.astype(BF16)
            self.second(c).start()
        elif kind == 2:
            self.second(c).wait_recv()
            both = self.mine[c].astype(F32) + self.far[c].astype(F32)
            self.total[2 * c + sq.half] = both.astype(BF16)
            self.third(c).start()
        else:
            self.third(c).wait_recv()
            for copy in (self.first(c), self.second(c), self.third(c)):
                copy.wait_send()


class Scatter:
    def __init__(self, line, part, out, near, fro, to, send, recv):
        self.line, self.part, self.out, self.near, self.fro, self.to = line, part, out, near, fro, to
        self.send, self.recv = send, recv

    def order(self):
        n = self.line.n
        seq = []
        for i in range((n + 1) // 2):
            seq.append(i)
            if n - 1 - i != i:
                seq.append(n - 1 - i)
        return seq

    def cross(self, j, i):
        line = self.line
        return remote(
            self.part.at[j, 2 * i + 1 - line.side], self.near.at[j, i], self.send.at[0, j, i], self.recv.at[0, j, i], line.pair
        )

    def leftward(self, j, i):
        return remote(
            self.part.at[j, 2 * i + self.line.side], self.fro.at[j, i], self.send.at[1, j, i], self.recv.at[1, j, i], self.line.left
        )

    def rightward(self, j, i):
        return remote(
            self.part.at[j, 2 * i + self.line.side], self.to.at[j, i], self.send.at[2, j, i], self.recv.at[2, j, i], self.line.right
        )

    def start(self, j):
        for i in self.order():
            self.cross(j, i).start()

    def fold(self, j, i):
        self.cross(j, i).wait_recv()
        slot = 2 * i + self.line.side
        self.part[j, slot] = (self.part[j, slot].astype(F32) + self.near[j, i].astype(F32)).astype(BF16)

    def pass_on(self, j, i):
        line = self.line
        slot = 2 * i + line.side

        @pl.when(i < line.at)
        def _():
            @pl.when(line.has_right)
            def _():
                self.leftward(j, i).wait_recv()
                self.part[j, slot] = (self.part[j, slot].astype(F32) + self.fro[j, i].astype(F32)).astype(BF16)

            self.leftward(j, i).start()

        @pl.when(i > line.at)
        def _():
            @pl.when(line.has_left)
            def _():
                self.rightward(j, i).wait_recv()
                self.part[j, slot] = (self.part[j, slot].astype(F32) + self.to[j, i].astype(F32)).astype(BF16)

            self.rightward(j, i).start()

    def finish(self, j):
        line = self.line
        for i in range(line.n):
            @pl.when(i == line.at)
            def _():
                slot = 2 * i + line.side
                self.out[j] = self.part[j, slot].astype(F32)

                @pl.when(line.has_right)
                def _():
                    self.leftward(j, i).wait_recv()
                    self.out[j] += self.fro[j, i].astype(F32)

                @pl.when(line.has_left)
                def _():
                    self.rightward(j, i).wait_recv()
                    self.out[j] += self.to[j, i].astype(F32)

    def drain(self, j):
        for i in range(self.line.n):
            self.cross(j, i).wait_send()

            @pl.when(i < self.line.at)
            def _():
                self.leftward(j, i).wait_send()

            @pl.when(i > self.line.at)
            def _():
                self.rightward(j, i).wait_send()


def mm(left, right, dims=NN, precision=None):
    return lax.dot_general(left, right, dims, precision=precision, preferred_element_type=F32)


def sigmoid(v):
    return 0.5 * jnp.tanh(0.5 * v) + 0.5


def softplus(v):
    return jnp.maximum(v, 0.0) + jnp.log1p(jnp.exp(-jnp.abs(v)))


def split16(v):
    top = v.astype(BF16)
    return top, (v - top.astype(F32)).astype(BF16)


def expand(v, ind):
    top, rest = split16(v)
    return mm(top, ind) + mm(rest, ind)


def headsum(v, ind):
    top, rest = split16(v)
    return mm(top, ind, NT) + mm(rest, ind, NT)


def iotas(n):
    return (
        lax.broadcasted_iota(jnp.int32, (n, n), 0),
        lax.broadcasted_iota(jnp.int32, (n, n), 1),
    )


def colsum(v):
    return jnp.sum(v, axis=0, keepdims=True)


def conv_pre(ext, par, n):
    total = par[4:5, :] + par[0:1, :] * ext[5 : 5 + n, :]
    for tap in range(1, 4):
        total = total + par[tap : tap + 1, :] * ext[5 + tap : 5 + tap + n, :]
    return total


def scan_prep(small, hp, ind, n):
    rows, cols = iotas(n)
    raw = small[:, 2 * STATE :] + hp[0:1, :]
    step = softplus(raw)
    rate = -jnp.exp(hp[1:2, :])
    lower = jnp.where(rows >= cols, 1.0, 0.0).astype(F32)
    cs = mm(lower, step * rate, precision=HIGH)
    tail = jnp.exp(cs[n - 1 : n, :] - cs)
    wide = expand(jnp.concatenate([step, jnp.exp(cs), tail], axis=0), ind)
    return raw, step, rate, cs, wide[0:n], wide[n : 2 * n], wide[2 * n : 3 * n]


def fwd_body(
    inner_ref, gate_ref, small_ref, cp_ref, sp_ref, hp_ref, ind_ref, own_ref,
    ssd_ref, scaled_ref, sq_ref, st_ref, full_ref,
    ext, exts, state, slabs, keep, send, recv, out_sem,
    *, heads, per, size, steps,
):
    n = CHUNK
    at = pl.program_id(0)
    line = Line(size)
    job = Gather(line, lambda j: own_ref, slabs, keep, send, recv)

    @pl.when(at == 0)
    def _():
        line.greet(pltpu.get_barrier_semaphore())
        job.start(0)


    @pl.when(lax.rem(at, per) == 0)
    def _():
        ext[0:8, :] = jnp.zeros((8, ext.shape[1]), F32)
        exts[0:8, :] = jnp.zeros((8, exts.shape[1]), F32)
        state[...] = jnp.zeros_like(state)

    rows, cols = iotas(n)
    ind = ind_ref[...]
    ext[8 : 8 + n, :] = inner_ref[...]
    pre = conv_pre(ext, cp_ref, n)
    x = pre * sigmoid(pre)
    ext[0:8, :] = ext[n : n + 8, :]
    exts[8 : 8 + n, :] = small_ref[:, : 2 * STATE]
    pres = conv_pre(exts, sp_ref, n)
    bc = (pres * sigmoid(pres)).astype(BF16)
    exts[0:8, :] = exts[n : n + 8, :]
    key, query = bc[:, :STATE], bc[:, STATE:]

    _, step, rate, cs, wide_step, wide_cs, wide_tail = scan_prep(small_ref, hp_ref, ind, n)
    cs2 = cs * LOG2E
    cs2t = cs2.T
    xs = x * wide_step
    half = lax.rem(lax.broadcasted_iota(jnp.int32, xs.shape, 1), 2 * HEAD) < HEAD
    xs0 = jnp.where(half, xs, 0.0)
    xs1 = (xs - xs0).astype(BF16)
    xs0 = xs0.astype(BF16)
    before = state[...]
    low = before.astype(BF16)
    st_ref[0] = low
    carried = mm(query, low) * wide_cs
    xw = (xs * wide_tail).astype(BF16)
    state[...] = before * wide_cs[n - 1 : n, :] + mm(key, xw, TN)
    scores = jnp.where(rows >= cols, mm(query, key, NT), 0.0)
    for pair in range(heads // 2):
        lanes = slice(pair * 2 * HEAD, (pair + 1) * 2 * HEAD)
        mats = []
        for h in (2 * pair, 2 * pair + 1):
            dec = jnp.exp2(jnp.minimum(cs2[:, h : h + 1] - cs2t[h : h + 1, :], 0.0))
            mats.append((scores * dec).astype(BF16))
        local = mm(
            jnp.concatenate(mats, axis=1),
            jnp.concatenate([xs0[:, lanes], xs1[:, lanes]], axis=0),
        )
        ssd_ref[:, lanes] = local + carried[:, lanes] + cp_ref[6:7, lanes] * x[:, lanes]
    gate = gate_ref[...]
    gated = ssd_ref[...] * (gate * sigmoid(gate))
    ones = jnp.ones((8, gated.shape[1]), BF16)
    top, rest = split16(gated * gated)
    sq_ref[0] = (mm(ones, top, NT) + mm(ones, rest, NT))[0:1, :]
    scaled_ref[...] = (gated * cp_ref[5:6, :]).astype(BF16)

    for k in range(1, line.n):
        @pl.when(at == k * steps // line.n)
        def _(k=k):
            job.relay(0, k)

    @pl.when(at == steps - 1)
    def _():
        job.arrive(0)
        out = pltpu.make_async_copy(slabs.at[0], full_ref, out_sem)
        out.start()
        job.drain(0)
        out.wait()


def fwd_scan(inner_raw, gate_pre, small, cp, sp, hp, ind, own, heads, size):
    tokens_n, width = inner_raw.shape
    steps = tokens_n // CHUNK
    any_spec = pl.BlockSpec(memory_space=pl.ANY)

    def row(w):
        return pl.BlockSpec((CHUNK, w), lambda c: (c, 0))

    def whole(a):
        return pl.BlockSpec(a.shape, lambda c: (0, 0))

    return pl.pallas_call(
        functools.partial(fwd_body, heads=heads, per=LEN // CHUNK, size=size, steps=steps),
        grid=(steps,),
        in_specs=[row(width), row(width), row(small.shape[1])] + [whole(a) for a in (cp, sp, hp, ind)] + [any_spec],
        out_specs=[
            row(width),
            row(width),
            pl.BlockSpec((1, 1, CHUNK), lambda c: (c, 0, 0)),
            pl.BlockSpec((1, STATE, width), lambda c: (c, 0, 0)),
            any_spec,
        ],
        out_shape=[
            jax.ShapeDtypeStruct((tokens_n, width), F32),
            jax.ShapeDtypeStruct((tokens_n, width), BF16),
            jax.ShapeDtypeStruct((steps, 1, CHUNK), F32),
            jax.ShapeDtypeStruct((steps, STATE, width), BF16),
            jax.ShapeDtypeStruct((size,) + own.shape, BF16),
        ],
        scratch_shapes=[
            pltpu.VMEM((CHUNK + 8, width), F32),
            pltpu.VMEM((CHUNK + 8, 2 * STATE), F32),
            pltpu.VMEM((STATE, width), F32),
            pltpu.VMEM((1, size) + own.shape, BF16),
            pltpu.SemaphoreType.DMA((1,)),
            pltpu.SemaphoreType.DMA((1, 3, size)),
            pltpu.SemaphoreType.DMA((1, size)),
            pltpu.SemaphoreType.DMA,
        ],
        compiler_params=pltpu.CompilerParams(
            collective_id=1, has_side_effects=True, vmem_limit_bytes=32 * 1024 * 1024
        ),
        cost_estimate=pl.CostEstimate(flops=3 * 10**9, bytes_accessed=16 * 10**6, transcendentals=0),
        name="fwd_scan",
    )(inner_raw, gate_pre, small, cp, sp, hp, ind, own)


def bwd_body(
    sd_ref, ssd_ref, gate_ref, inner_ref, iprev_ref, small_ref, sprev_ref, coef_ref, st_ref,
    cp_ref, sp_ref, hp_ref, ind_ref, term_ref,
    glow_ref, ilow_ref, sdel_ref, steplow_ref, dcp_ref, dsp_ref, dhp_ref, grad_ref,
    ext, exts, cde, cdes, dstate, rq, part, near, fro, to, load, send, recv,
    *, heads, per, steps, size,
):
    n = CHUNK
    at = pl.program_id(0)
    chunk = steps - 1 - at
    line = Line(size)
    job = Scatter(line, part, grad_ref, near, fro, to, send, recv)

    @pl.when(at == 0)
    def _():
        copy = pltpu.make_async_copy(term_ref, part.at[0], load)
        copy.start()
        line.greet(pltpu.get_barrier_semaphore())
        copy.wait()
        job.start(0)

    @pl.when(at == 0)
    def _():
        dcp_ref[...] = jnp.zeros_like(dcp_ref)
        dsp_ref[...] = jnp.zeros_like(dsp_ref)
        dhp_ref[...] = jnp.zeros_like(dhp_ref)
        rq[...] = jnp.zeros_like(rq)

    @pl.when(lax.rem(chunk, per) == per - 1)
    def _():
        cde[n : n + 8, :] = jnp.zeros((8, cde.shape[1]), F32)
        cdes[n : n + 8, :] = jnp.zeros((8, cdes.shape[1]), F32)
        dstate[...] = jnp.zeros_like(dstate)

    first = lax.rem(chunk, per) == 0
    keep = jnp.where(first, 0.0, 1.0).astype(F32)
    rows, cols = iotas(n)
    ind = ind_ref[...]
    ext[0:8, :] = iprev_ref[...] * keep
    ext[8 : 8 + n, :] = inner_ref[...]
    exts[0:8, :] = sprev_ref[:, : 2 * STATE] * keep
    exts[8 : 8 + n, :] = small_ref[:, : 2 * STATE]
    pre = conv_pre(ext, cp_ref, n)
    sig = sigmoid(pre)
    x = pre * sig
    slope = sig + x * (1.0 - sig)
    pres = conv_pre(exts, sp_ref, n)
    sigs = sigmoid(pres)
    acts = pres * sigs
    slopes = sigs + acts * (1.0 - sigs)
    bc = acts.astype(BF16)
    key, query = bc[:, :STATE], bc[:, STATE:]

    gate = gate_ref[...]
    gsig = sigmoid(gate)
    gact = gate * gsig
    ssd = ssd_ref[...]
    sd = sd_ref[...]
    gated = ssd * gact
    gd = cp_ref[5:6, :] * sd - coef_ref[...] * gated
    dcp_ref[5:6, :] += colsum(gated * sd)
    dy = gd * gact
    glow_ref[...] = (gd * ssd * (gsig + gact * (1.0 - gsig))).astype(BF16)

    raw, step, rate, cs, wide_step, wide_cs, wide_tail = scan_prep(small_ref, hp_ref, ind, n)
    cs2 = cs * LOG2E
    cs2t = cs2.T
    xs = x * wide_step
    xsb = xs.astype(BF16)
    half = lax.rem(lax.broadcasted_iota(jnp.int32, xs.shape, 1), 2 * HEAD) < HEAD
    dy0 = jnp.where(half, dy, 0.0)
    dy1 = (dy - dy0).astype(BF16)
    dy0 = dy0.astype(BF16)
    low = st_ref[0]
    dst = dstate[...]
    dlow = dst.astype(BF16)
    dye = dy * wide_cs
    dyeb = dye.astype(BF16)
    up = headsum(dye * mm(query, low), ind)
    dxs_state = wide_tail * mm(key, dlow)
    down = headsum(xs * dxs_state, ind)
    qdel = mm(dyeb, low, NT)
    kdel = mm((xs * wide_tail).astype(BF16), dlow, NT)
    through = headsum(jnp.broadcast_to(colsum(low.astype(F32) * dst), (8, dst.shape[1])), ind)[0:1, :]
    through = through * jnp.exp(cs[n - 1 : n, :])
    dstate[...] = dst * wide_cs[n - 1 : n, :] + mm(query, dyeb, TN)

    scores = jnp.where(rows <= cols, mm(key, query, NT), 0.0)
    dscores = jnp.zeros((n, n), F32)
    colq = jnp.zeros((n, LANES), F32)
    lane = lax.broadcasted_iota(jnp.int32, (n, LANES), 1)
    dxs = []
    for pair in range(heads // 2):
        lanes = slice(pair * 2 * HEAD, (pair + 1) * 2 * HEAD)
        stacked = jnp.concatenate([dy0[:, lanes], dy1[:, lanes]], axis=0)
        both = mm(xsb[:, lanes], stacked, NT)
        mats = []
        for which, h in enumerate((2 * pair, 2 * pair + 1)):
            dec = jnp.exp2(jnp.minimum(cs2t[h : h + 1, :] - cs2[:, h : h + 1], 0.0))
            mats.append((scores * dec).astype(BF16))
            term = dec * both[:, which * n : (which + 1) * n]
            dscores = dscores + term
            quad = scores * term
            rq[h : h + 1, :] = colsum(quad)
            colq = jnp.where(lane == h, jnp.sum(quad, axis=1, keepdims=True), colq)
        dxs.append(mm(jnp.concatenate(mats, axis=1), stacked))
    dxs = jnp.concatenate(dxs, axis=1) + dxs_state
    dscores = jnp.where(rows <= cols, dscores, 0.0).astype(BF16)
    kdel = kdel + mm(dscores, query)
    qdel = qdel + mm(dscores, key, TN)

    upper = jnp.where(rows <= cols, 1.0, 0.0).astype(F32)
    strict = jnp.where(rows > cols, 1.0, 0.0).astype(F32)
    da = mm(upper, rq[...].T - colq + up, precision=HIGH) + mm(strict, down, precision=HIGH) + through
    size = headsum(x * dxs, ind) + rate * da
    step_pre = size * sigmoid(raw)
    steplow_ref[...] = step_pre.astype(BF16)
    dhp_ref[0:1, :] += colsum(step_pre)
    dhp_ref[1:2, :] += rate * colsum(step * da)
    dcp_ref[6:7, :] += colsum(dy * x)

    cd = (dxs * wide_step + cp_ref[6:7, :] * dy) * slope
    cde[0:n, :] = cd
    total = cp_ref[3:4, :] * cd
    for tap in range(3):
        total = total + cp_ref[tap : tap + 1, :] * cde[3 - tap : 3 - tap + n, :]
    ilow_ref[...] = total.astype(BF16)
    for tap in range(4):
        dcp_ref[tap : tap + 1, :] += colsum(cd * ext[5 + tap : 5 + tap + n, :])
    dcp_ref[4:5, :] += colsum(cd)
    cde[n : n + 8, :] = cde[0:8, :]

    cds = jnp.concatenate([kdel, qdel], axis=1) * slopes
    cdes[0:n, :] = cds
    total = sp_ref[3:4, :] * cds
    for tap in range(3):
        total = total + sp_ref[tap : tap + 1, :] * cdes[3 - tap : 3 - tap + n, :]
    sdel_ref[...] = total.astype(BF16)
    for tap in range(4):
        dsp_ref[tap : tap + 1, :] += colsum(cds * exts[5 + tap : 5 + tap + n, :])
    dsp_ref[4:5, :] += colsum(cds)
    cdes[n : n + 8, :] = cdes[0:8, :]

    for m, i in enumerate(job.order()):
        @pl.when(at == 1 + m * (steps - 1) // line.n)
        def _(i=i):
            job.fold(0, i)
            job.pass_on(0, i)

    @pl.when(at == steps - 1)
    def _():
        job.finish(0)
        job.drain(0)
        dhp_ref[2:3, :] = headsum(jnp.broadcast_to(dcp_ref[6:7, :], (8, dcp_ref.shape[1])), ind)[0:1, :]


def bwd_scan(sd, ssd, gate_pre, inner_raw, small, coef, states, cp, sp, hp, ind, term, heads):
    tokens_n, width = inner_raw.shape
    steps = tokens_n // CHUNK
    wide_small = small.shape[1]
    size, rows, _ = term.shape
    half = size // 2

    def row(w):
        return pl.BlockSpec((CHUNK, w), lambda c: (steps - 1 - c, 0))

    def prev(w):
        return pl.BlockSpec((8, w), lambda c: (jnp.maximum((steps - 1 - c) * (CHUNK // 8) - 1, 0), 0))

    def whole(a):
        return pl.BlockSpec(a.shape, lambda c: (0, 0))

    def flat(r, w):
        return pl.BlockSpec((r, w), lambda c: (0, 0))

    return pl.pallas_call(
        functools.partial(bwd_body, heads=heads, per=LEN // CHUNK, steps=steps, size=size),
        grid=(steps,),
        in_specs=[
            row(width), row(width), row(width), row(width), prev(width),
            row(wide_small), prev(wide_small), row(1),
            pl.BlockSpec((1, STATE, width), lambda c: (steps - 1 - c, 0, 0)),
        ] + [whole(a) for a in (cp, sp, hp, ind)] + [pl.BlockSpec(memory_space=pl.ANY)],
        out_specs=[
            row(width), row(width), row(2 * STATE), row(LANES),
            flat(8, width), flat(8, 2 * STATE), flat(8, LANES),
            pl.BlockSpec((1, rows, width), lambda c: (0, 0, 0)),
        ],
        out_shape=[
            jax.ShapeDtypeStruct((tokens_n, width), BF16),
            jax.ShapeDtypeStruct((tokens_n, width), BF16),
            jax.ShapeDtypeStruct((tokens_n, 2 * STATE), BF16),
            jax.ShapeDtypeStruct((tokens_n, LANES), BF16),
            jax.ShapeDtypeStruct((8, width), F32),
            jax.ShapeDtypeStruct((8, 2 * STATE), F32),
            jax.ShapeDtypeStruct((8, LANES), F32),
            jax.ShapeDtypeStruct((1, rows, width), F32),
        ],
        scratch_shapes=[
            pltpu.VMEM((CHUNK + 8, width), F32),
            pltpu.VMEM((CHUNK + 8, 2 * STATE), F32),
            pltpu.VMEM((CHUNK + 8, width), F32),
            pltpu.VMEM((CHUNK + 8, 2 * STATE), F32),
            pltpu.VMEM((STATE, width), F32),
            pltpu.VMEM((LANES, CHUNK), F32),
            pltpu.VMEM((1,) + term.shape, BF16),
            pltpu.VMEM((1, half, rows, width), BF16),
            pltpu.VMEM((1, half, rows, width), BF16),
            pltpu.VMEM((1, half, rows, width), BF16),
            pltpu.SemaphoreType.DMA,
            pltpu.SemaphoreType.DMA((3, 1, half)),
            pltpu.SemaphoreType.DMA((3, 1, half)),
        ],
        compiler_params=pltpu.CompilerParams(
            collective_id=4, has_side_effects=True, vmem_limit_bytes=48 * 1024 * 1024
        ),
        cost_estimate=pl.CostEstimate(flops=8 * 10**9, bytes_accessed=24 * 10**6, transcendentals=0),
        name="bwd_scan",
    )(sd, ssd, gate_pre, inner_raw, inner_raw, small, small, coef, states, cp, sp, hp, ind, term)


SLICE = 256
TILE = 256


def stage_body(*refs, size, out, into):
    refs = list(refs)

    def take(n):
        got = refs[:n]
        del refs[:n]
        return got

    (res_ref,) = take(1)
    if out:
        scaled_ref, wout_ref, sq_ref = take(3)
    if into:
        gain_ref, wsmall_ref, own_ref = take(3)
    if out:
        new_ref, summed_ref, sums_ref = take(3)
    if into:
        normed_ref, rnorm_ref, small_ref, inner_ref, gate_ref, full_ref = take(6)
    if out:
        part, tot, got, mine, far, rows_got, facs, fresh, sends, recvs, rsend, rrecv = take(12)
    if into:
        slabs, normed, inner, gate, keep, gsend, grecv = take(7)
    (sems,) = take(1)
    assert not refs

    tokens_n, model = res_ref.shape
    line = Line(size)
    square = Square()
    barrier = pltpu.get_barrier_semaphore()
    if into:
        line.greet(barrier, square.others() if out else ())
    else:
        for who in square.others():
            pl.semaphore_signal(barrier, inc=1, device_id=who, device_id_type=MESH)
        pl.semaphore_wait(barrier, 3)

    pending = []

    def flush(src, dst):
        copy = pltpu.make_async_copy(src, dst, sems.at[len(pending)])
        copy.start()
        pending.append(copy)

    ticks = []
    if into:
        job = Gather(line, lambda j: own_ref.at[1 - j], slabs, keep, gsend, grecv)
        job.start(0)
        ticks = [functools.partial(job.relay, 0, k) for k in range(1, line.n)]
        ticks.append(functools.partial(job.start, 1))
        ticks += [functools.partial(job.relay, 1, k) for k in range(1, line.n)]

    if out:
        chunks = model // SLICE
        half = tokens_n // 2
        sums = Total(square, part, tot, got, mine, far, sends, recvs)
        copies = [
            remote(sq_ref, rows_got.at[square.me], rsend.at[k], rrecv.at[k], who)
            for k, who in enumerate(square.others())
        ]
        for copy in copies:
            copy.start()
        for c in range(chunks):
            value = mm(scaled_ref[...], wout_ref[c * SLICE : (c + 1) * SLICE, :], NT).astype(BF16)
            part[2 * c] = value[:half]
            part[2 * c + 1] = value[half:]
            sums.step(0, c)
        for c in range(chunks):
            sums.step(1, c)
        rows_got[square.me] = sq_ref[...]
        for copy in copies:
            copy.wait()
        total = (rows_got[0] + rows_got[1]) + (rows_got[2] + rows_got[3])
        sums_ref[...] = total
        factor = lax.rsqrt(total / INNER + EPS)
        for i in range(tokens_n // LANES):
            facs[i * LANES : (i + 1) * LANES, :] = jnp.broadcast_to(factor[i], (LANES, LANES)).T

        def use(c):
            for h in range(2):
                where = slice(h * half, (h + 1) * half)
                for s in range(SLICE // LANES):
                    lanes = slice(c * SLICE + s * LANES, c * SLICE + (s + 1) * LANES)
                    value = tot[2 * c + h, :, s * LANES : (s + 1) * LANES].astype(F32)
                    new = res_ref[where, lanes].astype(F32) + facs[where, :] * value
                    fresh[where, lanes] = new.astype(fresh.dtype)
                flush(tot.at[2 * c + h], summed_ref.at[pl.ds(h * half, half), pl.ds(c * SLICE, SLICE)])
            flush(fresh.at[:, pl.ds(c * SLICE, SLICE)], new_ref.at[:, pl.ds(c * SLICE, SLICE)])

        spread = max(1, -(-len(ticks) // chunks))
        for c in range(chunks):
            for tick in ticks[:spread]:
                tick()
            ticks = ticks[spread:]
            sums.step(2, c)
            if c:
                sums.step(3, c - 1)
                use(c - 1)
        sums.step(3, chunks - 1)
        use(chunks - 1)
        res_ref = fresh

    if into:
        def norm(i, _):
            rows = pl.ds(i * TILE, TILE)
            value = res_ref[rows, :].astype(F32)
            scale = lax.rsqrt(jnp.sum(value * value, axis=1, keepdims=True) / model + EPS)
            low = (value * scale * gain_ref[...]).astype(BF16)
            rnorm_ref[rows, :] = scale
            normed[rows, :] = low
            small_ref[rows, :] = mm(low, wsmall_ref[...])
            return 0

        lax.fori_loop(0, tokens_n // TILE, norm, 0)
        flush(normed, normed_ref)
        for tick in ticks:
            tick()

        def project(j, dst):
            weight = slabs[j].reshape(model, slabs.shape[3])

            def tile(i, _):
                rows = pl.ds(i * TILE, TILE)
                dst[rows, :] = mm(normed[rows, :], weight)
                return 0

            lax.fori_loop(0, tokens_n // TILE, tile, 0)

        for j, dst, ref in ((0, inner, inner_ref), (1, gate, gate_ref)):
            job.arrive(j)
            flush(slabs.at[j], full_ref.at[j])
            project(j, dst)
            flush(dst, ref)
        job.drain(0)
        job.drain(1)
    for copy in pending:
        copy.wait()


def stage(res, size, cid, out=None, into=None, last=False):
    tokens_n, model = res.shape
    vm = pl.BlockSpec(memory_space=pltpu.VMEM)
    hbm = pl.BlockSpec(memory_space=pl.ANY)
    chunks = model // SLICE
    args, in_specs = [res], [vm]
    out_specs, out_shape, scratch = [], [], []
    flushes = 0
    kind = BF16 if last else F32
    if out is not None:
        scaled, wout, sq = out
        args += [scaled, wout, sq]
        in_specs += [vm, vm, vm]
        out_specs += [hbm, hbm, vm]
        out_shape += [
            jax.ShapeDtypeStruct(res.shape, kind),
            jax.ShapeDtypeStruct(res.shape, BF16),
            jax.ShapeDtypeStruct(sq.shape, F32),
        ]
        chunk = pltpu.VMEM((chunks, tokens_n // 2, SLICE), BF16)
        both = pltpu.VMEM((2 * chunks, tokens_n // 2, SLICE), BF16)
        scratch += [
            both, both, chunk, chunk, chunk,
            pltpu.VMEM((4,) + sq.shape, F32),
            pltpu.VMEM((tokens_n, LANES), F32),
            pltpu.VMEM(res.shape, kind),
            pltpu.SemaphoreType.DMA((3, chunks)),
            pltpu.SemaphoreType.DMA((3, chunks)),
            pltpu.SemaphoreType.DMA((3,)),
            pltpu.SemaphoreType.DMA((3,)),
        ]
        flushes += 3 * chunks
    if into is not None:
        gain, wsmall, own = into
        rows, width = own.shape[1:]
        args += [gain, wsmall, own]
        in_specs += [vm, vm, hbm]
        out_specs += [hbm, vm, vm, hbm, hbm, hbm]
        out_shape += [
            jax.ShapeDtypeStruct(res.shape, BF16),
            jax.ShapeDtypeStruct((tokens_n, 1), F32),
            jax.ShapeDtypeStruct((tokens_n, wsmall.shape[1]), F32),
            jax.ShapeDtypeStruct((tokens_n, width), F32),
            jax.ShapeDtypeStruct((tokens_n, width), F32),
            jax.ShapeDtypeStruct((2, size, rows, width), BF16),
        ]
        scratch += [
            pltpu.VMEM((2, size, rows, width), BF16),
            pltpu.VMEM(res.shape, BF16),
            pltpu.VMEM((tokens_n, width), F32),
            pltpu.VMEM((tokens_n, width), F32),
            pltpu.SemaphoreType.DMA((2,)),
            pltpu.SemaphoreType.DMA((2, 3, size)),
            pltpu.SemaphoreType.DMA((2, size)),
        ]
        flushes += 5
    scratch.append(pltpu.SemaphoreType.DMA((flushes,)))
    return pl.pallas_call(
        functools.partial(stage_body, size=size, out=out is not None, into=into is not None),
        in_specs=in_specs,
        out_specs=out_specs,
        out_shape=out_shape,
        scratch_shapes=scratch,
        compiler_params=pltpu.CompilerParams(
            collective_id=cid, has_side_effects=True, vmem_limit_bytes=60 * 1024 * 1024
        ),
        name="stage",
    )(*args)


def grads_body(
    normed_ref, glow_ref, ilow_ref, steplow_ref, sdel_ref, win_ref, wsmall_ref,
    grad_ref, back_ref, sdsum_ref,
    terms, near, fro, to, part, tot, got, mine, far,
    ssend, srecv, sends, recvs, sems, *, size,
):
    tokens_n, model = normed_ref.shape
    rows = terms.shape[2]
    half = tokens_n // 2
    line = Line(size)
    square = Square()
    line.greet(pltpu.get_barrier_semaphore(), (square.mate, square.across))
    job = Scatter(line, terms, grad_ref, near, fro, to, ssend, srecv)
    sums = Total(square, part, tot, got, mine, far, sends, recvs)
    chunks = model // SLICE
    for j, low in enumerate((glow_ref, ilow_ref)):
        block = model // 4
        for b in range(4):
            value = mm(normed_ref[:, b * block : (b + 1) * block], low[...], TN).astype(BF16)
            for s in range(block // rows):
                terms[j, b * (block // rows) + s] = value[s * rows : (s + 1) * rows]
        job.start(j)
    value = sdel_ref[...]
    for c in range(chunks + 1):
        if c:
            span = slice((c - 1) * SLICE, c * SLICE)
            value = (
                mm(glow_ref[...], win_ref[1, span, :], NT)
                + mm(ilow_ref[...], win_ref[0, span, :], NT)
                + mm(steplow_ref[...], wsmall_ref[span, 2 * STATE :], NT)
                + mm(sdel_ref[...], wsmall_ref[span, : 2 * STATE], NT)
            ).astype(BF16)
        part[2 * c] = value[:half]
        part[2 * c + 1] = value[half:]
        sums.step(0, c)
        if c:
            sums.step(1, c - 1)
    sums.step(1, chunks)
    pending = []

    def use(c):
        for h in range(2):
            where = pl.ds(h * half, half)
            dst = back_ref.at[where, pl.ds((c - 1) * SLICE, SLICE)] if c else sdsum_ref.at[where, :]
            copy = pltpu.make_async_copy(tot.at[2 * c + h], dst, sems.at[len(pending)])
            copy.start()
            pending.append(copy)

    items = [(j, i) for j in range(2) for i in job.order()]
    spread = -(-len(items) // (chunks + 1))
    for c in range(chunks + 1):
        for j, i in items[:spread]:
            job.fold(j, i)
            job.pass_on(j, i)
        items = items[spread:]
        sums.step(2, c)
        if c:
            sums.step(3, c - 1)
            use(c - 1)
    sums.step(3, chunks)
    use(chunks)
    for j in range(2):
        job.finish(j)
        job.drain(j)
    for copy in pending:
        copy.wait()


def grads(normed, glow, ilow, steplow, sdel, win, wsmall, size, cid):
    tokens_n, model = normed.shape
    width = glow.shape[1]
    rows = model // size
    n = size // 2
    chunks = model // SLICE + 1
    vm = pl.BlockSpec(memory_space=pltpu.VMEM)
    hbm = pl.BlockSpec(memory_space=pl.ANY)
    chunk = pltpu.VMEM((chunks, tokens_n // 2, SLICE), BF16)
    both = pltpu.VMEM((2 * chunks, tokens_n // 2, SLICE), BF16)
    lane = pltpu.VMEM((2, n, rows, width), BF16)
    return pl.pallas_call(
        functools.partial(grads_body, size=size),
        in_specs=[vm] * 7,
        out_specs=[vm, hbm, hbm],
        out_shape=[
            jax.ShapeDtypeStruct((2, rows, width), F32),
            jax.ShapeDtypeStruct((tokens_n, model), BF16),
            jax.ShapeDtypeStruct((tokens_n, 2 * STATE), BF16),
        ],
        scratch_shapes=[
            pltpu.VMEM((2, size, rows, width), BF16), lane, lane, lane,
            both, both, chunk, chunk, chunk,
            pltpu.SemaphoreType.DMA((3, 2, n)),
            pltpu.SemaphoreType.DMA((3, 2, n)),
            pltpu.SemaphoreType.DMA((3, chunks)),
            pltpu.SemaphoreType.DMA((3, chunks)),
            pltpu.SemaphoreType.DMA((2 * chunks,)),
        ],
        compiler_params=pltpu.CompilerParams(
            collective_id=cid, has_side_effects=True, vmem_limit_bytes=60 * 1024 * 1024
        ),
        name="grads",
    )(normed, glow, ilow, steplow, sdel, win, wsmall)


def shards(
    tokens, inproj, stepproj, stateproj, outproj, convinner, biasinner, convstate, biasstate,
    stepbias, decaylog, skipgain, normgain, inputgain, cotangent,
):
    layers = inproj.shape[0]
    width = inproj.shape[3]
    heads = stepproj.shape[2]
    model = tokens.shape[1]
    pad = LANES - heads
    size = lax.axis_size("dp")
    rows = model // size
    quarter = model // 4
    tensor_at = lax.axis_index("tensor")
    ind = (jnp.arange(LANES)[:, None] == (jnp.arange(width) // HEAD)[None, :]).astype(BF16)
    small_w = jnp.concatenate([stateproj, stepproj, jnp.zeros((layers, model, pad), BF16)], axis=2)
    zero_row = jnp.zeros((layers, 1, width), F32)
    cp = jnp.concatenate(
        [convinner, biasinner[:, None], normgain[:, None], jnp.repeat(skipgain, HEAD, axis=1)[:, None], zero_row],
        axis=1,
    )
    sp = jnp.concatenate([convstate, biasstate[:, None], jnp.zeros((layers, 3, 2 * STATE), F32)], axis=1)
    hp = jnp.concatenate(
        [jnp.pad(jnp.stack([stepbias, decaylog], axis=1), ((0, 0), (0, 0), (0, pad))), jnp.zeros((layers, 6, LANES), F32)],
        axis=1,
    )
    outt = jnp.swapaxes(outproj, 1, 2)

    def into(at):
        return (inputgain[at][None, :], small_w[at], inproj[at])

    residual = tokens
    projected = stage(residual, size, 0, into=into(0))
    kept = []
    for at in range(layers):
        normed, rnorm, small, inner_raw, gate_pre, w_in = projected
        ssd, scaled, sq, states, w_out = fwd_scan(
            inner_raw, gate_pre, small, cp[at], sp[at], hp[at], ind, outt[at], heads, size
        )
        w_out = w_out.reshape(model, width)
        w_in = w_in.reshape(2, model, width)
        before = residual
        if at < layers - 1:
            residual, summed, sq, *projected = stage(residual, size, 2, out=(scaled, w_out, sq), into=into(at + 1))
        else:
            mixed, summed, sq = stage(residual, size, 3, out=(scaled, w_out, sq), last=True)
        factor = lax.rsqrt(sq.reshape(-1, 1) / INNER + EPS)
        kept.append((before, rnorm, normed, gate_pre, inner_raw, small, ssd, scaled, states, summed, factor, w_in, w_out))

    upstream = cotangent.astype(F32)
    in_grads = [None] * layers
    out_grads = [None] * layers
    little = [None] * layers
    for at in reversed(range(layers)):
        before, rnorm, normed, gate_pre, inner_raw, small, ssd, scaled, states, summed, factor, w_in, w_out = kept[at]
        before = before.astype(F32)
        factor_delta = jnp.sum(upstream * summed.astype(F32), axis=1, keepdims=True)
        delta_out = (factor * upstream).astype(BF16)
        scaled_delta = mm(delta_out, w_out)
        coef = factor * factor * factor * factor_delta / INNER
        term = mm(delta_out, scaled, TN).astype(BF16).reshape(size, rows, width)
        glow, ilow, sdel, steplow, dcp, dsp, dhp, out_grads[at] = bwd_scan(
            scaled_delta, ssd, gate_pre, inner_raw, small, coef, states, cp[at], sp[at], hp[at], ind, term, heads
        )
        in_grads[at], back, sdel = grads(normed, glow, ilow, steplow, sdel, w_in, small_w[at], size, 5)
        back = back.astype(F32)
        step_grad = mm(normed, steplow, TN)[:, :heads]
        state_grad = mm(lax.dynamic_slice_in_dim(normed, tensor_at * quarter, quarter, axis=1), sdel, TN)
        plain = back * before * rnorm
        gain_grad = jnp.sum(plain, axis=0)
        gained = back * inputgain[at]
        mean = jnp.mean(gained * before, axis=1, keepdims=True)
        upstream = upstream + rnorm * gained - rnorm * rnorm * rnorm * before * mean
        little[at] = (step_grad, state_grad, dcp, dsp, dhp, gain_grad)
    inproj_grad = jnp.stack(in_grads)[:, :, :, :]
    outproj_grad = jnp.swapaxes(jnp.concatenate(out_grads), 1, 2)
    stacked = [jnp.stack([little[at][m] for at in range(layers)]) for m in range(6)]
    step_grad, state_grad, dcp, dsp, dhp, gain_grad = [
        v.astype(F32)
        for v in lax.psum(
            (stacked[0].astype(BF16), stacked[1].astype(BF16), stacked[2], stacked[3], stacked[4], stacked[5]), "dp"
        )
    ]
    state_grad, dsp = lax.all_gather(state_grad.astype(BF16), "tensor", axis=1, tiled=True), lax.psum(dsp, "tensor")
    state_grad = state_grad.astype(F32)
    return (
        mixed,
        upstream,
        inproj_grad,
        step_grad,
        state_grad,
        outproj_grad,
        dcp[:, 0:4],
        dcp[:, 4],
        dsp[:, 0:4],
        dsp[:, 4],
        dhp[:, 0, :heads],
        dhp[:, 1, :heads],
        dhp[:, 2, :heads],
        dcp[:, 5],
        gain_grad,
    )


def solution(mesh):
    in_specs = (
        P("dp", None),
        P(None, None, "dp", "tensor"),
        P(None, None, "tensor"),
        P(),
        P(None, "tensor", "dp"),
        P(None, None, "tensor"),
        P(None, "tensor"),
        P(),
        P(),
        P(None, "tensor"),
        P(None, "tensor"),
        P(None, "tensor"),
        P(None, "tensor"),
        P(),
        P("dp", None),
    )
    out_specs = (
        P("dp", None),
        P("dp", None),
        P(None, None, "dp", "tensor"),
        P(None, None, "tensor"),
        P(),
        P(None, "tensor", "dp"),
        P(None, None, "tensor"),
        P(None, "tensor"),
        P(),
        P(),
        P(None, "tensor"),
        P(None, "tensor"),
        P(None, "tensor"),
        P(None, "tensor"),
        P(),
    )
    return jax.shard_map(shards, mesh=mesh, in_specs=in_specs, out_specs=out_specs, check_vma=False)
```

```python
import functools

import jax
import jax.numpy as jnp
from jax import lax
from jax.experimental import pallas as pl
from jax.experimental.pallas import tpu as pltpu
from jax.sharding import PartitionSpec as P

STATE = 128
LEN = 1024
INNER = 3072
HEAD = 64
CHUNK = 128
LANES = 128
EPS = 1e-05
LOG2E = 1.4426950408889634

HIGH = lax.Precision.HIGHEST
NN = (((1,), (0,)), ((), ()))
NT = (((1,), (1,)), ((), ()))
TN = (((0,), (0,)), ((), ()))
F32 = jnp.float32
BF16 = jnp.bfloat16
MESH = pl.DeviceIdType.MESH


def remote(src, dst, send, recv, where):
    return pltpu.make_async_remote_copy(
        src_ref=src, dst_ref=dst, send_sem=send, recv_sem=recv, device_id=where, device_id_type=MESH
    )


class Line:
    def __init__(self, size):
        self.n = size // 2
        me = lax.axis_index("dp")
        self.me = me
        self.at = me // 2
        self.side = lax.rem(me, 2)
        self.pair = {"dp": me + 1 - 2 * self.side}
        self.right = {"dp": jnp.minimum(me + 2, size - 1)}
        self.left = {"dp": jnp.maximum(me - 2, 0)}
        self.has_left = self.at > 0
        self.has_right = self.at < self.n - 1

    def greet(self, barrier, more=()):
        for who in more:
            pl.semaphore_signal(barrier, inc=1, device_id=who, device_id_type=MESH)
        pl.semaphore_signal(barrier, inc=1, device_id=self.pair, device_id_type=MESH)

        @pl.when(self.has_left)
        def _():
            pl.semaphore_signal(barrier, inc=1, device_id=self.left, device_id_type=MESH)

        @pl.when(self.has_right)
        def _():
            pl.semaphore_signal(barrier, inc=1, device_id=self.right, device_id_type=MESH)

        peers = 1 + len(more) + self.has_left.astype(jnp.int32) + self.has_right.astype(jnp.int32)
        pl.semaphore_wait(barrier, peers)

    def greet_all(self, barrier, more=()):
        for who in list(more) + [self.pair]:
            pl.semaphore_signal(barrier, inc=1, device_id=who, device_id_type=MESH)
        for i in range(self.n):
            @pl.when(i != self.at)
            def _(i=i):
                pl.semaphore_signal(barrier, inc=1, device_id={"dp": 2 * i + self.side}, device_id_type=MESH)
        pl.semaphore_wait(barrier, self.n + len(more))


class Gather:
    def __init__(self, line, own, full, keep, send, recv):
        self.line, self.own, self.full, self.keep, self.send, self.recv = line, own, full, keep, send, recv

    def copy(self, j, slab, way, src=None):
        where = (self.line.right, self.line.left, self.line.pair)[way]
        src = self.full.at[j, slab] if src is None else src
        return remote(src, self.full.at[j, slab], self.send.at[j, way, slab], self.recv.at[j, slab], where)

    def start(self, j):
        line = self.line
        pltpu.make_async_copy(self.own(j), self.full.at[j, line.me], self.keep.at[j]).start()

        @pl.when(line.has_right)
        def _():
            self.copy(j, line.me, 0, self.own(j)).start()

        @pl.when(line.has_left)
        def _():
            self.copy(j, line.me, 1, self.own(j)).start()

        self.copy(j, line.me, 2, self.own(j)).start()

    def relay(self, j, k):
        line = self.line

        @pl.when(line.at >= k)
        def _():
            slab = line.me - 2 * k
            self.copy(j, slab, 0).wait_recv()

            @pl.when(line.has_right)
            def _():
                self.copy(j, slab, 0).start()

            self.copy(j, slab, 2).start()

        @pl.when(line.at + k < line.n)
        def _():
            slab = line.me + 2 * k
            self.copy(j, slab, 1).wait_recv()

            @pl.when(line.has_left)
            def _():
                self.copy(j, slab, 1).start()

            self.copy(j, slab, 2).start()

    def arrive(self, j):
        line = self.line
        pltpu.make_async_copy(self.own(j), self.full.at[j, line.me], self.keep.at[j]).wait()
        for place in range(line.n):
            self.copy(j, 2 * place + 1 - line.side, 2).wait_recv()

    def drain(self, j):
        line = self.line
        for place in range(line.n):
            slab = 2 * place + line.side
            self.copy(j, slab, 2).wait_send()

            @pl.when(line.has_right & (place <= line.at))
            def _():
                self.copy(j, slab, 0).wait_send()

            @pl.when(line.has_left & (place >= line.at))
            def _():
                self.copy(j, slab, 1).wait_send()


class Square:
    def __init__(self):
        me = lax.axis_index("tensor")
        self.me = me
        self.half = lax.rem(me, 2)
        self.mate = {"tensor": me + 1 - 2 * self.half}
        self.across = {"tensor": lax.rem(me + 2, 4)}

    def others(self):
        return [{"tensor": lax.rem(self.me + k, 4)} for k in (1, 2, 3)]


class Total:
    def __init__(self, square, part, total, got, mine, far, send, recv):
        self.square, self.part, self.total, self.got, self.mine, self.far = square, part, total, got, mine, far
        self.send, self.recv = send, recv

    def first(self, c):
        sq = self.square
        return remote(
            self.part.at[2 * c + 1 - sq.half], self.got.at[c], self.send.at[0, c], self.recv.at[0, c], sq.mate
        )

    def second(self, c):
        sq = self.square
        return remote(self.mine.at[c], self.far.at[c], self.send.at[1, c], self.recv.at[1, c], sq.across)

    def third(self, c):
        sq = self.square
        slot = 2 * c + sq.half
        return remote(self.total.at[slot], self.total.at[slot], self.send.at[2, c], self.recv.at[2, c], sq.mate)

    def step(self, kind, c):
        sq = self.square
        if kind == 0:
            self.first(c).start()
        elif kind == 1:
            self.first(c).wait_recv()
            both = self.part[2 * c + sq.half].astype(F32) + self.got[c].astype(F32)
            self.mine[c] = both.astype(BF16)
            self.second(c).start()
        elif kind == 2:
            self.second(c).wait_recv()
            both = self.mine[c].astype(F32) + self.far[c].astype(F32)
            self.total[2 * c + sq.half] = both.astype(BF16)
            self.third(c).start()
        else:
            self.third(c).wait_recv()
            for copy in (self.first(c), self.second(c), self.third(c)):
                copy.wait_send()


class Scatter:
    def __init__(self, line, part, out, near, far, send, recv):
        self.line, self.part, self.out, self.near, self.far = line, part, out, near, far
        self.send, self.recv = send, recv

    def order(self):
        n = self.line.n
        seq = []
        for i in range((n + 1) // 2):
            seq.append(i)
            if n - 1 - i != i:
                seq.append(n - 1 - i)
        return seq

    def cross(self, j, i):
        line = self.line
        return remote(
            self.part.at[j, 2 * i + 1 - line.side], self.near.at[j, i], self.send.at[0, j, i], self.recv.at[0, j, i], line.pair
        )

    def straight(self, j, i, source):
        line = self.line
        return remote(
            self.part.at[j, 2 * i + line.side], self.far.at[j, source], self.send.at[1, j, i], self.recv.at[1, j, source],
            {"dp": 2 * i + line.side},
        )

    def start(self, j):
        for i in self.order():
            self.cross(j, i).start()

    def fold(self, j, i):
        line = self.line
        self.cross(j, i).wait_recv()
        slot = 2 * i + line.side
        self.part[j, slot] = (self.part[j, slot].astype(F32) + self.near[j, i].astype(F32)).astype(BF16)

        @pl.when(i != line.at)
        def _():
            self.straight(j, i, line.at).start()

    def finish(self, j):
        line = self.line
        self.out[j] = self.part[j, line.me].astype(self.out.dtype)
        for i in range(line.n):
            @pl.when(i != line.at)
            def _(i=i):
                self.straight(j, i, i).wait_recv()
                self.out[j] += self.far[j, i].astype(self.out.dtype)

    def drain(self, j):
        for i in range(self.line.n):
            self.cross(j, i).wait_send()

            @pl.when(i != self.line.at)
            def _(i=i):
                self.straight(j, i, self.line.at).wait_send()


def mm(left, right, dims=NN, precision=None):
    return lax.dot_general(left, right, dims, precision=precision, preferred_element_type=F32)


def sigmoid(v):
    return 0.5 * jnp.tanh(0.5 * v) + 0.5


def softplus(v):
    return jnp.maximum(v, 0.0) + jnp.log1p(jnp.exp(-jnp.abs(v)))


def split16(v):
    top = v.astype(BF16)
    return top, (v - top.astype(F32)).astype(BF16)


def expand(v, ind):
    top, rest = split16(v)
    return mm(top, ind) + mm(rest, ind)


def headsum(v, ind):
    top, rest = split16(v)
    return mm(top, ind, NT) + mm(rest, ind, NT)


def iotas(n):
    return (
        lax.broadcasted_iota(jnp.int32, (n, n), 0),
        lax.broadcasted_iota(jnp.int32, (n, n), 1),
    )


def colsum(v):
    return jnp.sum(v, axis=0, keepdims=True)


def conv_pre(ext, par, n):
    total = par[4:5, :] + par[0:1, :] * ext[5 : 5 + n, :]
    for tap in range(1, 4):
        total = total + par[tap : tap + 1, :] * ext[5 + tap : 5 + tap + n, :]
    return total


def scan_prep(small, hp, ind, n):
    rows, cols = iotas(n)
    raw = small[:, 2 * STATE :] + hp[0:1, :]
    step = softplus(raw)
    rate = -jnp.exp(hp[1:2, :])
    lower = jnp.where(rows >= cols, 1.0, 0.0).astype(F32)
    cs = mm(lower, step * rate, precision=HIGH)
    tail = jnp.exp(cs[n - 1 : n, :] - cs)
    wide = expand(jnp.concatenate([step, jnp.exp(cs), tail], axis=0), ind)
    return raw, step, rate, cs, wide[0:n], wide[n : 2 * n], wide[2 * n : 3 * n]


def fwd_body(
    inner_ref, gate_ref, small_ref, cp_ref, sp_ref, hp_ref, ind_ref, own_ref,
    ssd_ref, scaled_ref, sq_ref, st_ref, full_ref,
    ext, exts, state, slabs, keep, send, recv, out_sem,
    *, heads, per, size, steps,
):
    n = CHUNK
    at = pl.program_id(0)
    line = Line(size)
    job = Gather(line, lambda j: own_ref, slabs, keep, send, recv)

    @pl.when(at == 0)
    def _():
        line.greet(pltpu.get_barrier_semaphore())
        job.start(0)


    @pl.when(lax.rem(at, per) == 0)
    def _():
        ext[0:8, :] = jnp.zeros((8, ext.shape[1]), F32)
        exts[0:8, :] = jnp.zeros((8, exts.shape[1]), F32)
        state[...] = jnp.zeros_like(state)

    rows, cols = iotas(n)
    ind = ind_ref[...]
    ext[8 : 8 + n, :] = inner_ref[...]
    pre = conv_pre(ext, cp_ref, n)
    x = pre * sigmoid(pre)
    ext[0:8, :] = ext[n : n + 8, :]
    exts[8 : 8 + n, :] = small_ref[:, : 2 * STATE]
    pres = conv_pre(exts, sp_ref, n)
    bc = (pres * sigmoid(pres)).astype(BF16)
    exts[0:8, :] = exts[n : n + 8, :]
    key, query = bc[:, :STATE], bc[:, STATE:]

    _, step, rate, cs, wide_step, wide_cs, wide_tail = scan_prep(small_ref, hp_ref, ind, n)
    cs2 = cs * LOG2E
    cs2t = cs2.T
    xs = x * wide_step
    half = lax.rem(lax.broadcasted_iota(jnp.int32, xs.shape, 1), 2 * HEAD) < HEAD
    xs0 = jnp.where(half, xs, 0.0)
    xs1 = (xs - xs0).astype(BF16)
    xs0 = xs0.astype(BF16)
    before = state[...]
    low = before.astype(BF16)
    st_ref[0] = low
    carried = mm(query, low) * wide_cs
    xw = (xs * wide_tail).astype(BF16)
    state[...] = before * wide_cs[n - 1 : n, :] + mm(key, xw, TN)
    scores = jnp.where(rows >= cols, mm(query, key, NT), 0.0)
    for pair in range(heads // 2):
        lanes = slice(pair * 2 * HEAD, (pair + 1) * 2 * HEAD)
        mats = []
        for h in (2 * pair, 2 * pair + 1):
            dec = jnp.exp2(jnp.minimum(cs2[:, h : h + 1] - cs2t[h : h + 1, :], 0.0))
            mats.append((scores * dec).astype(BF16))
        local = mm(
            jnp.concatenate(mats, axis=1),
            jnp.concatenate([xs0[:, lanes], xs1[:, lanes]], axis=0),
        )
        ssd_ref[:, lanes] = local + carried[:, lanes] + cp_ref[6:7, lanes] * x[:, lanes]
    gate = gate_ref[...]
    gated = ssd_ref[...] * (gate * sigmoid(gate))
    ones = jnp.ones((8, gated.shape[1]), BF16)
    top, rest = split16(gated * gated)
    sq_ref[0] = (mm(ones, top, NT) + mm(ones, rest, NT))[0:1, :]
    scaled_ref[...] = (gated * cp_ref[5:6, :]).astype(BF16)

    for k in range(1, line.n):
        @pl.when(at == k * steps // line.n)
        def _(k=k):
            job.relay(0, k)

    @pl.when(at == steps - 1)
    def _():
        job.arrive(0)
        out = pltpu.make_async_copy(slabs.at[0], full_ref, out_sem)
        out.start()
        job.drain(0)
        out.wait()


def fwd_scan(inner_raw, gate_pre, small, cp, sp, hp, ind, own, heads, size):
    tokens_n, width = inner_raw.shape
    steps = tokens_n // CHUNK
    any_spec = pl.BlockSpec(memory_space=pl.ANY)

    def row(w):
        return pl.BlockSpec((CHUNK, w), lambda c: (c, 0))

    def whole(a):
        return pl.BlockSpec(a.shape, lambda c: (0, 0))

    return pl.pallas_call(
        functools.partial(fwd_body, heads=heads, per=LEN // CHUNK, size=size, steps=steps),
        grid=(steps,),
        in_specs=[row(width), row(width), row(small.shape[1])] + [whole(a) for a in (cp, sp, hp, ind)] + [any_spec],
        out_specs=[
            row(width),
            row(width),
            pl.BlockSpec((1, 1, CHUNK), lambda c: (c, 0, 0)),
            pl.BlockSpec((1, STATE, width), lambda c: (c, 0, 0)),
            any_spec,
        ],
        out_shape=[
            jax.ShapeDtypeStruct((tokens_n, width), F32),
            jax.ShapeDtypeStruct((tokens_n, width), BF16),
            jax.ShapeDtypeStruct((steps, 1, CHUNK), F32),
            jax.ShapeDtypeStruct((steps, STATE, width), BF16),
            jax.ShapeDtypeStruct((size,) + own.shape, BF16),
        ],
        scratch_shapes=[
            pltpu.VMEM((CHUNK + 8, width), F32),
            pltpu.VMEM((CHUNK + 8, 2 * STATE), F32),
            pltpu.VMEM((STATE, width), F32),
            pltpu.VMEM((1, size) + own.shape, BF16),
            pltpu.SemaphoreType.DMA((1,)),
            pltpu.SemaphoreType.DMA((1, 3, size)),
            pltpu.SemaphoreType.DMA((1, size)),
            pltpu.SemaphoreType.DMA,
        ],
        compiler_params=pltpu.CompilerParams(
            collective_id=1, has_side_effects=True, vmem_limit_bytes=32 * 1024 * 1024
        ),
        cost_estimate=pl.CostEstimate(flops=3 * 10**9, bytes_accessed=16 * 10**6, transcendentals=0),
        name="fwd_scan",
    )(inner_raw, gate_pre, small, cp, sp, hp, ind, own)


def bwd_body(
    sd_ref, ssd_ref, gate_ref, inner_ref, iprev_ref, small_ref, sprev_ref, coef_ref, st_ref,
    cp_ref, sp_ref, hp_ref, ind_ref, term_ref,
    glow_ref, ilow_ref, sdel_ref, steplow_ref, dcp_ref, dsp_ref, dhp_ref, grad_ref,
    ext, exts, cde, cdes, dstate, rq, part, near, far, load, send, recv,
    *, heads, per, steps, size,
):
    n = CHUNK
    at = pl.program_id(0)
    chunk = steps - 1 - at
    line = Line(size)
    job = Scatter(line, part, grad_ref, near, far, send, recv)

    @pl.when(at == 0)
    def _():
        copy = pltpu.make_async_copy(term_ref, part.at[0], load)
        copy.start()
        line.greet_all(pltpu.get_barrier_semaphore())
        copy.wait()
        job.start(0)

    @pl.when(at == 0)
    def _():
        dcp_ref[...] = jnp.zeros_like(dcp_ref)
        dsp_ref[...] = jnp.zeros_like(dsp_ref)
        dhp_ref[...] = jnp.zeros_like(dhp_ref)
        rq[...] = jnp.zeros_like(rq)

    @pl.when(lax.rem(chunk, per) == per - 1)
    def _():
        cde[n : n + 8, :] = jnp.zeros((8, cde.shape[1]), F32)
        cdes[n : n + 8, :] = jnp.zeros((8, cdes.shape[1]), F32)
        dstate[...] = jnp.zeros_like(dstate)

    first = lax.rem(chunk, per) == 0
    keep = jnp.where(first, 0.0, 1.0).astype(F32)
    rows, cols = iotas(n)
    ind = ind_ref[...]
    ext[0:8, :] = iprev_ref[...] * keep
    ext[8 : 8 + n, :] = inner_ref[...]
    exts[0:8, :] = sprev_ref[:, : 2 * STATE] * keep
    exts[8 : 8 + n, :] = small_ref[:, : 2 * STATE]
    pre = conv_pre(ext, cp_ref, n)
    sig = sigmoid(pre)
    x = pre * sig
    slope = sig + x * (1.0 - sig)
    pres = conv_pre(exts, sp_ref, n)
    sigs = sigmoid(pres)
    acts = pres * sigs
    slopes = sigs + acts * (1.0 - sigs)
    bc = acts.astype(BF16)
    key, query = bc[:, :STATE], bc[:, STATE:]

    gate = gate_ref[...]
    gsig = sigmoid(gate)
    gact = gate * gsig
    ssd = ssd_ref[...]
    sd = sd_ref[...]
    gated = ssd * gact
    gd = cp_ref[5:6, :] * sd - coef_ref[...] * gated
    dcp_ref[5:6, :] += colsum(gated * sd)
    dy = gd * gact
    glow_ref[...] = (gd * ssd * (gsig + gact * (1.0 - gsig))).astype(BF16)

    raw, step, rate, cs, wide_step, wide_cs, wide_tail = scan_prep(small_ref, hp_ref, ind, n)
    cs2 = cs * LOG2E
    cs2t = cs2.T
    xs = x * wide_step
    xsb = xs.astype(BF16)
    half = lax.rem(lax.broadcasted_iota(jnp.int32, xs.shape, 1), 2 * HEAD) < HEAD
    dy0 = jnp.where(half, dy, 0.0)
    dy1 = (dy - dy0).astype(BF16)
    dy0 = dy0.astype(BF16)
    low = st_ref[0]
    dst = dstate[...]
    dlow = dst.astype(BF16)
    dye = dy * wide_cs
    dyeb = dye.astype(BF16)
    up = headsum(dye * mm(query, low), ind)
    dxs_state = wide_tail * mm(key, dlow)
    down = headsum(xs * dxs_state, ind)
    qdel = mm(dyeb, low, NT)
    kdel = mm((xs * wide_tail).astype(BF16), dlow, NT)
    through = headsum(jnp.broadcast_to(colsum(low.astype(F32) * dst), (8, dst.shape[1])), ind)[0:1, :]
    through = through * jnp.exp(cs[n - 1 : n, :])
    dstate[...] = dst * wide_cs[n - 1 : n, :] + mm(query, dyeb, TN)

    scores = jnp.where(rows <= cols, mm(key, query, NT), 0.0)
    dscores = jnp.zeros((n, n), F32)
    colq = jnp.zeros((n, LANES), F32)
    lane = lax.broadcasted_iota(jnp.int32, (n, LANES), 1)
    dxs = []
    for pair in range(heads // 2):
        lanes = slice(pair * 2 * HEAD, (pair + 1) * 2 * HEAD)
        stacked = jnp.concatenate([dy0[:, lanes], dy1[:, lanes]], axis=0)
        both = mm(xsb[:, lanes], stacked, NT)
        mats = []
        for which, h in enumerate((2 * pair, 2 * pair + 1)):
            dec = jnp.exp2(jnp.minimum(cs2t[h : h + 1, :] - cs2[:, h : h + 1], 0.0))
            mats.append((scores * dec).astype(BF16))
            term = dec * both[:, which * n : (which + 1) * n]
            dscores = dscores + term
            quad = scores * term
            rq[h : h + 1, :] = colsum(quad)
            colq = jnp.where(lane == h, jnp.sum(quad, axis=1, keepdims=True), colq)
        dxs.append(mm(jnp.concatenate(mats, axis=1), stacked))
    dxs = jnp.concatenate(dxs, axis=1) + dxs_state
    dscores = jnp.where(rows <= cols, dscores, 0.0).astype(BF16)
    kdel = kdel + mm(dscores, query)
    qdel = qdel + mm(dscores, key, TN)

    upper = jnp.where(rows <= cols, 1.0, 0.0).astype(F32)
    strict = jnp.where(rows > cols, 1.0, 0.0).astype(F32)
    da = mm(upper, rq[...].T - colq + up, precision=HIGH) + mm(strict, down, precision=HIGH) + through
    size = headsum(x * dxs, ind) + rate * da
    step_pre = size * sigmoid(raw)
    steplow_ref[...] = step_pre.astype(BF16)
    dhp_ref[0:1, :] += colsum(step_pre)
    dhp_ref[1:2, :] += rate * colsum(step * da)
    dcp_ref[6:7, :] += colsum(dy * x)

    cd = (dxs * wide_step + cp_ref[6:7, :] * dy) * slope
    cde[0:n, :] = cd
    total = cp_ref[3:4, :] * cd
    for tap in range(3):
        total = total + cp_ref[tap : tap + 1, :] * cde[3 - tap : 3 - tap + n, :]
    ilow_ref[...] = total.astype(BF16)
    for tap in range(4):
        dcp_ref[tap : tap + 1, :] += colsum(cd * ext[5 + tap : 5 + tap + n, :])
    dcp_ref[4:5, :] += colsum(cd)
    cde[n : n + 8, :] = cde[0:8, :]

    cds = jnp.concatenate([kdel, qdel], axis=1) * slopes
    cdes[0:n, :] = cds
    total = sp_ref[3:4, :] * cds
    for tap in range(3):
        total = total + sp_ref[tap : tap + 1, :] * cdes[3 - tap : 3 - tap + n, :]
    sdel_ref[...] = total.astype(BF16)
    for tap in range(4):
        dsp_ref[tap : tap + 1, :] += colsum(cds * exts[5 + tap : 5 + tap + n, :])
    dsp_ref[4:5, :] += colsum(cds)
    cdes[n : n + 8, :] = cdes[0:8, :]

    for m, i in enumerate(job.order()):
        @pl.when(at == 1 + m * (steps - 1) // line.n)
        def _(i=i):
            job.fold(0, i)

    @pl.when(at == steps - 1)
    def _():
        job.finish(0)
        job.drain(0)
        dhp_ref[2:3, :] = headsum(jnp.broadcast_to(dcp_ref[6:7, :], (8, dcp_ref.shape[1])), ind)[0:1, :]


def bwd_scan(sd, ssd, gate_pre, inner_raw, small, coef, states, cp, sp, hp, ind, term, heads):
    tokens_n, width = inner_raw.shape
    steps = tokens_n // CHUNK
    wide_small = small.shape[1]
    size, rows, _ = term.shape
    half = size // 2

    def row(w):
        return pl.BlockSpec((CHUNK, w), lambda c: (steps - 1 - c, 0))

    def prev(w):
        return pl.BlockSpec((8, w), lambda c: (jnp.maximum((steps - 1 - c) * (CHUNK // 8) - 1, 0), 0))

    def whole(a):
        return pl.BlockSpec(a.shape, lambda c: (0, 0))

    def flat(r, w):
        return pl.BlockSpec((r, w), lambda c: (0, 0))

    return pl.pallas_call(
        functools.partial(bwd_body, heads=heads, per=LEN // CHUNK, steps=steps, size=size),
        grid=(steps,),
        in_specs=[
            row(width), row(width), row(width), row(width), prev(width),
            row(wide_small), prev(wide_small), row(1),
            pl.BlockSpec((1, STATE, width), lambda c: (steps - 1 - c, 0, 0)),
        ] + [whole(a) for a in (cp, sp, hp, ind)] + [pl.BlockSpec(memory_space=pl.ANY)],
        out_specs=[
            row(width), row(width), row(2 * STATE), row(LANES),
            flat(8, width), flat(8, 2 * STATE), flat(8, LANES),
            pl.BlockSpec((1, rows, width), lambda c: (0, 0, 0)),
        ],
        out_shape=[
            jax.ShapeDtypeStruct((tokens_n, width), BF16),
            jax.ShapeDtypeStruct((tokens_n, width), BF16),
            jax.ShapeDtypeStruct((tokens_n, 2 * STATE), BF16),
            jax.ShapeDtypeStruct((tokens_n, LANES), BF16),
            jax.ShapeDtypeStruct((8, width), F32),
            jax.ShapeDtypeStruct((8, 2 * STATE), F32),
            jax.ShapeDtypeStruct((8, LANES), F32),
            jax.ShapeDtypeStruct((1, rows, width), F32),
        ],
        scratch_shapes=[
            pltpu.VMEM((CHUNK + 8, width), F32),
            pltpu.VMEM((CHUNK + 8, 2 * STATE), F32),
            pltpu.VMEM((CHUNK + 8, width), F32),
            pltpu.VMEM((CHUNK + 8, 2 * STATE), F32),
            pltpu.VMEM((STATE, width), F32),
            pltpu.VMEM((LANES, CHUNK), F32),
            pltpu.VMEM((1,) + term.shape, BF16),
            pltpu.VMEM((1, half, rows, width), BF16),
            pltpu.VMEM((1, half, rows, width), BF16),
            pltpu.SemaphoreType.DMA,
            pltpu.SemaphoreType.DMA((2, 1, half)),
            pltpu.SemaphoreType.DMA((2, 1, half)),
        ],
        compiler_params=pltpu.CompilerParams(
            collective_id=4, has_side_effects=True, vmem_limit_bytes=48 * 1024 * 1024
        ),
        cost_estimate=pl.CostEstimate(flops=8 * 10**9, bytes_accessed=24 * 10**6, transcendentals=0),
        name="bwd_scan",
    )(sd, ssd, gate_pre, inner_raw, inner_raw, small, small, coef, states, cp, sp, hp, ind, term)


SLICE = 256
TILE = 256


def stage_body(*refs, size, out, into):
    refs = list(refs)

    def take(n):
        got = refs[:n]
        del refs[:n]
        return got

    (res_ref,) = take(1)
    if out:
        scaled_ref, wout_ref, sq_ref = take(3)
    if into:
        gain_ref, wsmall_ref, own_ref = take(3)
    if out:
        new_ref, summed_ref, sums_ref = take(3)
    if into:
        normed_ref, rnorm_ref, small_ref, inner_ref, gate_ref, full_ref = take(6)
    if out:
        part, tot, got, mine, far, rows_got, facs, fresh, sends, recvs, rsend, rrecv = take(12)
    if into:
        slabs, normed, inner, gate, keep, gsend, grecv = take(7)
    (sems,) = take(1)
    assert not refs

    tokens_n, model = res_ref.shape
    line = Line(size)
    square = Square()
    barrier = pltpu.get_barrier_semaphore()
    if into:
        line.greet(barrier, square.others() if out else ())
    else:
        for who in square.others():
            pl.semaphore_signal(barrier, inc=1, device_id=who, device_id_type=MESH)
        pl.semaphore_wait(barrier, 3)

    pending = []

    def flush(src, dst):
        copy = pltpu.make_async_copy(src, dst, sems.at[len(pending)])
        copy.start()
        pending.append(copy)

    ticks = []
    if into:
        job = Gather(line, lambda j: own_ref.at[1 - j], slabs, keep, gsend, grecv)
        job.start(0)
        ticks = [functools.partial(job.relay, 0, k) for k in range(1, line.n)]
        ticks.append(functools.partial(job.start, 1))
        ticks += [functools.partial(job.relay, 1, k) for k in range(1, line.n)]

    if out:
        chunks = model // SLICE
        half = tokens_n // 2
        sums = Total(square, part, tot, got, mine, far, sends, recvs)
        copies = [
            remote(sq_ref, rows_got.at[square.me], rsend.at[k], rrecv.at[k], who)
            for k, who in enumerate(square.others())
        ]
        for copy in copies:
            copy.start()
        for c in range(chunks):
            value = mm(scaled_ref[...], wout_ref[c * SLICE : (c + 1) * SLICE, :], NT).astype(BF16)
            part[2 * c] = value[:half]
            part[2 * c + 1] = value[half:]
            sums.step(0, c)
        for c in range(chunks):
            sums.step(1, c)
        rows_got[square.me] = sq_ref[...]
        for copy in copies:
            copy.wait()
        total = (rows_got[0] + rows_got[1]) + (rows_got[2] + rows_got[3])
        sums_ref[...] = total
        factor = lax.rsqrt(total / INNER + EPS)
        for i in range(tokens_n // LANES):
            facs[i * LANES : (i + 1) * LANES, :] = jnp.broadcast_to(factor[i], (LANES, LANES)).T

        def use(c):
            for h in range(2):
                where = slice(h * half, (h + 1) * half)
                for s in range(SLICE // LANES):
                    lanes = slice(c * SLICE + s * LANES, c * SLICE + (s + 1) * LANES)
                    value = tot[2 * c + h, :, s * LANES : (s + 1) * LANES].astype(F32)
                    new = res_ref[where, lanes].astype(F32) + facs[where, :] * value
                    fresh[where, lanes] = new.astype(fresh.dtype)
                flush(tot.at[2 * c + h], summed_ref.at[pl.ds(h * half, half), pl.ds(c * SLICE, SLICE)])
            flush(fresh.at[:, pl.ds(c * SLICE, SLICE)], new_ref.at[:, pl.ds(c * SLICE, SLICE)])

        spread = max(1, -(-len(ticks) // chunks))
        for c in range(chunks):
            for tick in ticks[:spread]:
                tick()
            ticks = ticks[spread:]
            sums.step(2, c)
            if c:
                sums.step(3, c - 1)
                use(c - 1)
        sums.step(3, chunks - 1)
        use(chunks - 1)
        res_ref = fresh

    if into:
        def norm(i, _):
            rows = pl.ds(i * TILE, TILE)
            value = res_ref[rows, :].astype(F32)
            scale = lax.rsqrt(jnp.sum(value * value, axis=1, keepdims=True) / model + EPS)
            low = (value * scale * gain_ref[...]).astype(BF16)
            rnorm_ref[rows, :] = scale
            normed[rows, :] = low
            small_ref[rows, :] = mm(low, wsmall_ref[...])
            return 0

        lax.fori_loop(0, tokens_n // TILE, norm, 0)
        flush(normed, normed_ref)
        for tick in ticks:
            tick()

        def project(j, dst):
            weight = slabs[j].reshape(model, slabs.shape[3])

            def tile(i, _):
                rows = pl.ds(i * TILE, TILE)
                dst[rows, :] = mm(normed[rows, :], weight)
                return 0

            lax.fori_loop(0, tokens_n // TILE, tile, 0)

        for j, dst, ref in ((0, inner, inner_ref), (1, gate, gate_ref)):
            job.arrive(j)
            flush(slabs.at[j], full_ref.at[j])
            project(j, dst)
            flush(dst, ref)
        job.drain(0)
        job.drain(1)
    for copy in pending:
        copy.wait()


def stage(res, size, cid, out=None, into=None, last=False):
    tokens_n, model = res.shape
    vm = pl.BlockSpec(memory_space=pltpu.VMEM)
    hbm = pl.BlockSpec(memory_space=pl.ANY)
    chunks = model // SLICE
    args, in_specs = [res], [vm]
    out_specs, out_shape, scratch = [], [], []
    flushes = 0
    kind = BF16 if last else F32
    if out is not None:
        scaled, wout, sq = out
        args += [scaled, wout, sq]
        in_specs += [vm, vm, vm]
        out_specs += [hbm, hbm, vm]
        out_shape += [
            jax.ShapeDtypeStruct(res.shape, kind),
            jax.ShapeDtypeStruct(res.shape, BF16),
            jax.ShapeDtypeStruct(sq.shape, F32),
        ]
        chunk = pltpu.VMEM((chunks, tokens_n // 2, SLICE), BF16)
        both = pltpu.VMEM((2 * chunks, tokens_n // 2, SLICE), BF16)
        scratch += [
            both, both, chunk, chunk, chunk,
            pltpu.VMEM((4,) + sq.shape, F32),
            pltpu.VMEM((tokens_n, LANES), F32),
            pltpu.VMEM(res.shape, kind),
            pltpu.SemaphoreType.DMA((3, chunks)),
            pltpu.SemaphoreType.DMA((3, chunks)),
            pltpu.SemaphoreType.DMA((3,)),
            pltpu.SemaphoreType.DMA((3,)),
        ]
        flushes += 3 * chunks
    if into is not None:
        gain, wsmall, own = into
        rows, width = own.shape[1:]
        args += [gain, wsmall, own]
        in_specs += [vm, vm, hbm]
        out_specs += [hbm, vm, vm, hbm, hbm, hbm]
        out_shape += [
            jax.ShapeDtypeStruct(res.shape, BF16),
            jax.ShapeDtypeStruct((tokens_n, 1), F32),
            jax.ShapeDtypeStruct((tokens_n, wsmall.shape[1]), F32),
            jax.ShapeDtypeStruct((tokens_n, width), F32),
            jax.ShapeDtypeStruct((tokens_n, width), F32),
            jax.ShapeDtypeStruct((2, size, rows, width), BF16),
        ]
        scratch += [
            pltpu.VMEM((2, size, rows, width), BF16),
            pltpu.VMEM(res.shape, BF16),
            pltpu.VMEM((tokens_n, width), F32),
            pltpu.VMEM((tokens_n, width), F32),
            pltpu.SemaphoreType.DMA((2,)),
            pltpu.SemaphoreType.DMA((2, 3, size)),
            pltpu.SemaphoreType.DMA((2, size)),
        ]
        flushes += 5
    scratch.append(pltpu.SemaphoreType.DMA((flushes,)))
    return pl.pallas_call(
        functools.partial(stage_body, size=size, out=out is not None, into=into is not None),
        in_specs=in_specs,
        out_specs=out_specs,
        out_shape=out_shape,
        scratch_shapes=scratch,
        compiler_params=pltpu.CompilerParams(
            collective_id=cid, has_side_effects=True, vmem_limit_bytes=60 * 1024 * 1024
        ),
        name="stage",
    )(*args)


def grads_body(
    normed_ref, glow_ref, ilow_ref, steplow_ref, sdel_ref, win_ref, wsmall_ref,
    grad_ref, back_ref, sdsum_ref,
    terms, near, away, part, tot, got, mine, far,
    ssend, srecv, sends, recvs, sems, *, size,
):
    tokens_n, model = normed_ref.shape
    rows = terms.shape[2]
    half = tokens_n // 2
    line = Line(size)
    square = Square()
    line.greet_all(pltpu.get_barrier_semaphore(), (square.mate, square.across))
    job = Scatter(line, terms, grad_ref, near, away, ssend, srecv)
    sums = Total(square, part, tot, got, mine, far, sends, recvs)
    chunks = model // SLICE
    for j, low in enumerate((glow_ref, ilow_ref)):
        block = model // 4
        for b in range(4):
            value = mm(normed_ref[:, b * block : (b + 1) * block], low[...], TN).astype(BF16)
            for s in range(block // rows):
                terms[j, b * (block // rows) + s] = value[s * rows : (s + 1) * rows]
        job.start(j)
    value = sdel_ref[...]
    for c in range(chunks + 1):
        if c:
            span = slice((c - 1) * SLICE, c * SLICE)
            value = (
                mm(glow_ref[...], win_ref[1, span, :], NT)
                + mm(ilow_ref[...], win_ref[0, span, :], NT)
                + mm(steplow_ref[...], wsmall_ref[span, 2 * STATE :], NT)
                + mm(sdel_ref[...], wsmall_ref[span, : 2 * STATE], NT)
            ).astype(BF16)
        part[2 * c] = value[:half]
        part[2 * c + 1] = value[half:]
        sums.step(0, c)
        if c:
            sums.step(1, c - 1)
    sums.step(1, chunks)
    pending = []

    def use(c):
        for h in range(2):
            where = pl.ds(h * half, half)
            dst = back_ref.at[where, pl.ds((c - 1) * SLICE, SLICE)] if c else sdsum_ref.at[where, :]
            copy = pltpu.make_async_copy(tot.at[2 * c + h], dst, sems.at[len(pending)])
            copy.start()
            pending.append(copy)

    items = [(j, i) for j in range(2) for i in job.order()]
    spread = -(-len(items) // (chunks + 1))
    for c in range(chunks + 1):
        for j, i in items[:spread]:
            job.fold(j, i)
        items = items[spread:]
        sums.step(2, c)
        if c:
            sums.step(3, c - 1)
            use(c - 1)
    sums.step(3, chunks)
    use(chunks)
    for j in range(2):
        job.finish(j)
        job.drain(j)
    for copy in pending:
        copy.wait()


def grads(normed, glow, ilow, steplow, sdel, win, wsmall, size, cid):
    tokens_n, model = normed.shape
    width = glow.shape[1]
    rows = model // size
    n = size // 2
    chunks = model // SLICE + 1
    vm = pl.BlockSpec(memory_space=pltpu.VMEM)
    hbm = pl.BlockSpec(memory_space=pl.ANY)
    chunk = pltpu.VMEM((chunks, tokens_n // 2, SLICE), BF16)
    both = pltpu.VMEM((2 * chunks, tokens_n // 2, SLICE), BF16)
    lane = pltpu.VMEM((2, n, rows, width), BF16)
    return pl.pallas_call(
        functools.partial(grads_body, size=size),
        in_specs=[vm] * 7,
        out_specs=[vm, hbm, hbm],
        out_shape=[
            jax.ShapeDtypeStruct((2, rows, width), F32),
            jax.ShapeDtypeStruct((tokens_n, model), BF16),
            jax.ShapeDtypeStruct((tokens_n, 2 * STATE), BF16),
        ],
        scratch_shapes=[
            pltpu.VMEM((2, size, rows, width), BF16), lane, lane,
            both, both, chunk, chunk, chunk,
            pltpu.SemaphoreType.DMA((2, 2, n)),
            pltpu.SemaphoreType.DMA((2, 2, n)),
            pltpu.SemaphoreType.DMA((3, chunks)),
            pltpu.SemaphoreType.DMA((3, chunks)),
            pltpu.SemaphoreType.DMA((2 * chunks,)),
        ],
        compiler_params=pltpu.CompilerParams(
            collective_id=cid, has_side_effects=True, vmem_limit_bytes=60 * 1024 * 1024
        ),
        name="grads",
    )(normed, glow, ilow, steplow, sdel, win, wsmall)


def smalls_body(pack_ref, full_ref, wide_ref, part, near, far, own, load, ssend, srecv, keep, gsend, grecv, send, recv, *, size, span):
    line = Line(size)
    square = Square()
    copy = pltpu.make_async_copy(pack_ref, part.at[0], load)
    copy.start()
    line.greet_all(pltpu.get_barrier_semaphore(), (square.mate, square.across))
    copy.wait()
    job = Scatter(line, part, own, near, far, ssend, srecv)
    job.start(0)
    for i in job.order():
        job.fold(0, i)
    job.finish(0)
    spread = Gather(line, lambda j: own.at[0], full_ref, keep, gsend, grecv)
    spread.start(0)
    for k in range(1, line.n):
        spread.relay(0, k)
    spread.arrive(0)
    flat = full_ref[0].reshape(-1, full_ref.shape[3])
    wide_ref[square.me] = flat[:span]
    over = lax.rem(square.me + 2, 4)
    first = remote(wide_ref.at[square.me], wide_ref.at[square.me], send.at[0], recv.at[0], square.across)
    first.start()
    second = remote(wide_ref.at[square.me], wide_ref.at[square.me], send.at[1], recv.at[1], square.mate)
    second.start()
    first.wait()
    third = remote(wide_ref.at[over], wide_ref.at[over], send.at[2], recv.at[2], square.mate)
    third.start()
    second.wait()
    third.wait()
    job.drain(0)
    spread.drain(0)


def smalls(pack, span, cid):
    size, r, w = pack.shape
    n = size // 2
    vm = pl.BlockSpec(memory_space=pltpu.VMEM)
    return pl.pallas_call(
        functools.partial(smalls_body, size=size, span=span),
        in_specs=[pl.BlockSpec(memory_space=pl.ANY)],
        out_specs=[vm, vm],
        out_shape=[
            jax.ShapeDtypeStruct((1,) + pack.shape, BF16),
            jax.ShapeDtypeStruct((4, span, w), BF16),
        ],
        scratch_shapes=[
            pltpu.VMEM((1,) + pack.shape, BF16),
            pltpu.VMEM((1, n, r, w), BF16),
            pltpu.VMEM((1, n, r, w), BF16),
            pltpu.VMEM((1, r, w), BF16),
            pltpu.SemaphoreType.DMA,
            pltpu.SemaphoreType.DMA((2, 1, n)),
            pltpu.SemaphoreType.DMA((2, 1, n)),
            pltpu.SemaphoreType.DMA((1,)),
            pltpu.SemaphoreType.DMA((1, 3, size)),
            pltpu.SemaphoreType.DMA((1, size)),
            pltpu.SemaphoreType.DMA((3,)),
            pltpu.SemaphoreType.DMA((3,)),
        ],
        compiler_params=pltpu.CompilerParams(
            collective_id=cid, has_side_effects=True, vmem_limit_bytes=32 * 1024 * 1024
        ),
        name="smalls",
    )(pack)


def fold_columns(v, w):
    return jnp.concatenate([v[:, i * w : (i + 1) * w] for i in range(v.shape[1] // w)], axis=0)


def unfold_columns(v, r):
    return jnp.concatenate([v[i * r : (i + 1) * r] for i in range(v.shape[0] // r)], axis=1)


def shards(
    tokens, inproj, stepproj, stateproj, outproj, convinner, biasinner, convstate, biasstate,
    stepbias, decaylog, skipgain, normgain, inputgain, cotangent,
):
    layers = inproj.shape[0]
    width = inproj.shape[3]
    heads = stepproj.shape[2]
    model = tokens.shape[1]
    pad = LANES - heads
    size = lax.axis_size("dp")
    rows = model // size
    quarter = model // 4
    tensor_at = lax.axis_index("tensor")
    ind = (jnp.arange(LANES)[:, None] == (jnp.arange(width) // HEAD)[None, :]).astype(BF16)
    small_w = jnp.concatenate([stateproj, stepproj, jnp.zeros((layers, model, pad), BF16)], axis=2)
    zero_row = jnp.zeros((layers, 1, width), F32)
    cp = jnp.concatenate(
        [convinner, biasinner[:, None], normgain[:, None], jnp.repeat(skipgain, HEAD, axis=1)[:, None], zero_row],
        axis=1,
    )
    sp = jnp.concatenate([convstate, biasstate[:, None], jnp.zeros((layers, 3, 2 * STATE), F32)], axis=1)
    hp = jnp.concatenate(
        [jnp.pad(jnp.stack([stepbias, decaylog], axis=1), ((0, 0), (0, 0), (0, pad))), jnp.zeros((layers, 6, LANES), F32)],
        axis=1,
    )
    outt = jnp.swapaxes(outproj, 1, 2)

    def into(at):
        return (inputgain[at][None, :], small_w[at], inproj[at])

    residual = tokens
    projected = stage(residual, size, 0, into=into(0))
    kept = []
    for at in range(layers):
        normed, rnorm, small, inner_raw, gate_pre, w_in = projected
        ssd, scaled, sq, states, w_out = fwd_scan(
            inner_raw, gate_pre, small, cp[at], sp[at], hp[at], ind, outt[at], heads, size
        )
        w_out = w_out.reshape(model, width)
        w_in = w_in.reshape(2, model, width)
        before = residual
        if at < layers - 1:
            residual, summed, sq, *projected = stage(residual, size, 2, out=(scaled, w_out, sq), into=into(at + 1))
        else:
            mixed, summed, sq = stage(residual, size, 3, out=(scaled, w_out, sq), last=True)
        factor = lax.rsqrt(sq.reshape(-1, 1) / INNER + EPS)
        kept.append((before, rnorm, normed, gate_pre, inner_raw, small, ssd, scaled, states, summed, factor, w_in, w_out))

    upstream = cotangent.astype(F32)
    in_grads = [None] * layers
    out_grads = [None] * layers
    little = [None] * layers
    for at in reversed(range(layers)):
        before, rnorm, normed, gate_pre, inner_raw, small, ssd, scaled, states, summed, factor, w_in, w_out = kept[at]
        before = before.astype(F32)
        factor_delta = jnp.sum(upstream * summed.astype(F32), axis=1, keepdims=True)
        delta_out = (factor * upstream).astype(BF16)
        scaled_delta = mm(delta_out, w_out)
        coef = factor * factor * factor * factor_delta / INNER
        term = mm(delta_out, scaled, TN).astype(BF16).reshape(size, rows, width)
        glow, ilow, sdel, steplow, dcp, dsp, dhp, out_grads[at] = bwd_scan(
            scaled_delta, ssd, gate_pre, inner_raw, small, coef, states, cp[at], sp[at], hp[at], ind, term, heads
        )
        in_grads[at], back, sdel = grads(normed, glow, ilow, steplow, sdel, w_in, small_w[at], size, 5)
        back = back.astype(F32)
        step_grad = mm(steplow, normed, TN)[:16]
        state_grad = mm(lax.dynamic_slice_in_dim(normed, tensor_at * quarter, quarter, axis=1), sdel, TN)
        plain = back * before * rnorm
        gain_grad = jnp.sum(plain, axis=0)
        gained = back * inputgain[at]
        mean = jnp.mean(gained * before, axis=1, keepdims=True)
        upstream = upstream + rnorm * gained - rnorm * rnorm * rnorm * before * mean
        little[at] = (step_grad, state_grad, dcp, dsp, dhp, gain_grad)
    inproj_grad = jnp.stack(in_grads)[:, :, :, :]
    outproj_grad = jnp.swapaxes(jnp.concatenate(out_grads), 1, 2)
    w = 2 * STATE
    blocks = [little[at][1] for at in range(layers)] + [little[at][3] for at in range(layers)]
    span = sum(v.shape[0] for v in blocks)
    for at in range(layers):
        step_grad, _, dcp, _, dhp, gain_grad = little[at]
        blocks += [fold_columns(step_grad, w), fold_columns(dcp, w), fold_columns(dhp.reshape(4, w), w)]
        blocks += [fold_columns(gain_grad[None, :], w)]
    places = [v.shape[0] for v in blocks]
    lines = -(-sum(places) // (16 * size)) * 16 * size
    pack = jnp.concatenate([v.astype(BF16) for v in blocks] + [jnp.zeros((lines - sum(places), w), BF16)], axis=0)
    full, wide = smalls(pack.reshape(size, lines // size, w), span, 6)
    full = full.reshape(lines, w).astype(F32)
    wide = wide.astype(F32)
    spots = [sum(places[:i]) for i in range(len(places))]
    state_grad = jnp.stack(
        [jnp.concatenate([wide[t, spots[at] : spots[at] + quarter] for t in range(4)], axis=0) for at in range(layers)]
    )
    dsp = jnp.sum(wide[:, spots[layers] :].reshape(4, layers, 8, w), axis=0)
    found = [[], [], [], []]
    for at in range(layers):
        for m, r in enumerate((16, 8, 4, 1)):
            i = 2 * layers + 4 * at + m
            found[m].append(unfold_columns(full[spots[i] : spots[i] + places[i]], r))
    step_grad = jnp.stack([jnp.swapaxes(v, 0, 1)[:, :heads] for v in found[0]])
    dcp = jnp.stack(found[1])
    dhp = jnp.stack([v.reshape(8, LANES) for v in found[2]])
    gain_grad = jnp.stack([v[0] for v in found[3]])
    return (
        mixed,
        upstream,
        inproj_grad,
        step_grad,
        state_grad,
        outproj_grad,
        dcp[:, 0:4],
        dcp[:, 4],
        dsp[:, 0:4],
        dsp[:, 4],
        dhp[:, 0, :heads],
        dhp[:, 1, :heads],
        dhp[:, 2, :heads],
        dcp[:, 5],
        gain_grad,
    )


def solution(mesh):
    in_specs = (
        P("dp", None),
        P(None, None, "dp", "tensor"),
        P(None, None, "tensor"),
        P(),
        P(None, "tensor", "dp"),
        P(None, None, "tensor"),
        P(None, "tensor"),
        P(),
        P(),
        P(None, "tensor"),
        P(None, "tensor"),
        P(None, "tensor"),
        P(None, "tensor"),
        P(),
        P("dp", None),
    )
    out_specs = (
        P("dp", None),
        P("dp", None),
        P(None, None, "dp", "tensor"),
        P(None, None, "tensor"),
        P(),
        P(None, "tensor", "dp"),
        P(None, None, "tensor"),
        P(None, "tensor"),
        P(),
        P(),
        P(None, "tensor"),
        P(None, "tensor"),
        P(None, "tensor"),
        P(None, "tensor"),
        P(),
    )
    return jax.shard_map(shards, mesh=mesh, in_specs=in_specs, out_specs=out_specs, check_vma=False)
```

```python
import functools

import jax
import jax.numpy as jnp
from jax import lax
from jax.experimental import pallas as pl
from jax.experimental.pallas import tpu as pltpu
from jax.sharding import PartitionSpec as P

STATE = 128
LEN = 1024
INNER = 3072
HEAD = 64
CHUNK = 128
LANES = 128
EPS = 1e-05
LOG2E = 1.4426950408889634

HIGH = lax.Precision.HIGHEST
NN = (((1,), (0,)), ((), ()))
NT = (((1,), (1,)), ((), ()))
TN = (((0,), (0,)), ((), ()))
F32 = jnp.float32
BF16 = jnp.bfloat16
MESH = pl.DeviceIdType.MESH


def remote(src, dst, send, recv, where):
    return pltpu.make_async_remote_copy(
        src_ref=src, dst_ref=dst, send_sem=send, recv_sem=recv, device_id=where, device_id_type=MESH
    )


class Line:
    def __init__(self, size):
        self.n = size // 2
        me = lax.axis_index("dp")
        self.me = me
        self.at = me // 2
        self.side = lax.rem(me, 2)
        self.pair = {"dp": me + 1 - 2 * self.side}
        self.right = {"dp": jnp.minimum(me + 2, size - 1)}
        self.left = {"dp": jnp.maximum(me - 2, 0)}
        self.has_left = self.at > 0
        self.has_right = self.at < self.n - 1

    def greet(self, barrier, more=()):
        for who in more:
            pl.semaphore_signal(barrier, inc=1, device_id=who, device_id_type=MESH)
        pl.semaphore_signal(barrier, inc=1, device_id=self.pair, device_id_type=MESH)

        @pl.when(self.has_left)
        def _():
            pl.semaphore_signal(barrier, inc=1, device_id=self.left, device_id_type=MESH)

        @pl.when(self.has_right)
        def _():
            pl.semaphore_signal(barrier, inc=1, device_id=self.right, device_id_type=MESH)

        peers = 1 + len(more) + self.has_left.astype(jnp.int32) + self.has_right.astype(jnp.int32)
        pl.semaphore_wait(barrier, peers)

    def greet_all(self, barrier, more=()):
        for who in list(more) + [self.pair]:
            pl.semaphore_signal(barrier, inc=1, device_id=who, device_id_type=MESH)
        for i in range(self.n):
            @pl.when(i != self.at)
            def _(i=i):
                pl.semaphore_signal(barrier, inc=1, device_id={"dp": 2 * i + self.side}, device_id_type=MESH)
        pl.semaphore_wait(barrier, self.n + len(more))


class Gather:
    def __init__(self, line, own, full, keep, send, recv):
        self.line, self.own, self.full, self.keep, self.send, self.recv = line, own, full, keep, send, recv

    def copy(self, j, slab, way, src=None):
        where = (self.line.right, self.line.left, self.line.pair)[way]
        src = self.full.at[j, slab] if src is None else src
        return remote(src, self.full.at[j, slab], self.send.at[j, way, slab], self.recv.at[j, slab], where)

    def start(self, j):
        line = self.line
        pltpu.make_async_copy(self.own(j), self.full.at[j, line.me], self.keep.at[j]).start()

        @pl.when(line.has_right)
        def _():
            self.copy(j, line.me, 0, self.own(j)).start()

        @pl.when(line.has_left)
        def _():
            self.copy(j, line.me, 1, self.own(j)).start()

        self.copy(j, line.me, 2, self.own(j)).start()

    def relay(self, j, k):
        line = self.line

        @pl.when(line.at >= k)
        def _():
            slab = line.me - 2 * k
            self.copy(j, slab, 0).wait_recv()

            @pl.when(line.has_right)
            def _():
                self.copy(j, slab, 0).start()

            self.copy(j, slab, 2).start()

        @pl.when(line.at + k < line.n)
        def _():
            slab = line.me + 2 * k
            self.copy(j, slab, 1).wait_recv()

            @pl.when(line.has_left)
            def _():
                self.copy(j, slab, 1).start()

            self.copy(j, slab, 2).start()

    def arrive(self, j):
        line = self.line
        pltpu.make_async_copy(self.own(j), self.full.at[j, line.me], self.keep.at[j]).wait()
        for place in range(line.n):
            self.copy(j, 2 * place + 1 - line.side, 2).wait_recv()

    def drain(self, j):
        line = self.line
        for place in range(line.n):
            slab = 2 * place + line.side
            self.copy(j, slab, 2).wait_send()

            @pl.when(line.has_right & (place <= line.at))
            def _():
                self.copy(j, slab, 0).wait_send()

            @pl.when(line.has_left & (place >= line.at))
            def _():
                self.copy(j, slab, 1).wait_send()


class Square:
    def __init__(self):
        me = lax.axis_index("tensor")
        self.me = me
        self.half = lax.rem(me, 2)
        self.mate = {"tensor": me + 1 - 2 * self.half}
        self.across = {"tensor": lax.rem(me + 2, 4)}

    def others(self):
        return [{"tensor": lax.rem(self.me + k, 4)} for k in (1, 2, 3)]


class Total:
    def __init__(self, square, part, total, got, mine, far, send, recv):
        self.square, self.part, self.total, self.got, self.mine, self.far = square, part, total, got, mine, far
        self.send, self.recv = send, recv

    def first(self, c):
        sq = self.square
        return remote(
            self.part.at[2 * c + 1 - sq.half], self.got.at[c], self.send.at[0, c], self.recv.at[0, c], sq.mate
        )

    def second(self, c):
        sq = self.square
        return remote(self.mine.at[c], self.far.at[c], self.send.at[1, c], self.recv.at[1, c], sq.across)

    def third(self, c):
        sq = self.square
        slot = 2 * c + sq.half
        return remote(self.total.at[slot], self.total.at[slot], self.send.at[2, c], self.recv.at[2, c], sq.mate)

    def step(self, kind, c):
        sq = self.square
        if kind == 0:
            self.first(c).start()
        elif kind == 1:
            self.first(c).wait_recv()
            both = self.part[2 * c + sq.half].astype(F32) + self.got[c].astype(F32)
            self.mine[c] = both.astype(BF16)
            self.second(c).start()
        elif kind == 2:
            self.second(c).wait_recv()
            both = self.mine[c].astype(F32) + self.far[c].astype(F32)
            self.total[2 * c + sq.half] = both.astype(BF16)
            self.third(c).start()
        else:
            self.third(c).wait_recv()
            for copy in (self.first(c), self.second(c), self.third(c)):
                copy.wait_send()


class Scatter:
    def __init__(self, line, part, out, near, far, send, recv):
        self.line, self.part, self.out, self.near, self.far = line, part, out, near, far
        self.send, self.recv = send, recv

    def order(self):
        n = self.line.n
        seq = []
        for i in range((n + 1) // 2):
            seq.append(i)
            if n - 1 - i != i:
                seq.append(n - 1 - i)
        return seq

    def cross(self, j, i):
        line = self.line
        return remote(
            self.part.at[j, 2 * i + 1 - line.side], self.near.at[j, i], self.send.at[0, j, i], self.recv.at[0, j, i], line.pair
        )

    def straight(self, j, i, source):
        line = self.line
        return remote(
            self.part.at[j, 2 * i + line.side], self.far.at[j, source], self.send.at[1, j, i], self.recv.at[1, j, source],
            {"dp": 2 * i + line.side},
        )

    def start(self, j):
        for i in self.order():
            self.cross(j, i).start()

    def emit(self, j, turned, right):
        rows = self.part.shape[2]
        for i in self.order():
            value = mm(turned[2 * i * rows : 2 * (i + 1) * rows, :], right[...]).astype(BF16)
            self.part[j, 2 * i] = value[:rows]
            self.part[j, 2 * i + 1] = value[rows:]
            self.cross(j, i).start()

    def fold(self, j, i):
        line = self.line
        self.cross(j, i).wait_recv()
        slot = 2 * i + line.side
        self.part[j, slot] = (self.part[j, slot].astype(F32) + self.near[j, i].astype(F32)).astype(BF16)

        @pl.when(i != line.at)
        def _():
            self.straight(j, i, line.at).start()

    def finish(self, j):
        line = self.line
        self.out[j] = self.part[j, line.me].astype(self.out.dtype)
        for i in range(line.n):
            @pl.when(i != line.at)
            def _(i=i):
                self.straight(j, i, i).wait_recv()
                self.out[j] += self.far[j, i].astype(self.out.dtype)

    def drain(self, j):
        for i in range(self.line.n):
            self.cross(j, i).wait_send()

            @pl.when(i != self.line.at)
            def _(i=i):
                self.straight(j, i, self.line.at).wait_send()


def mm(left, right, dims=NN, precision=None):
    return lax.dot_general(left, right, dims, precision=precision, preferred_element_type=F32)


def sigmoid(v):
    return 0.5 * jnp.tanh(0.5 * v) + 0.5


def softplus(v):
    return jnp.maximum(v, 0.0) + jnp.log1p(jnp.exp(-jnp.abs(v)))


def split16(v):
    top = v.astype(BF16)
    return top, (v - top.astype(F32)).astype(BF16)


def expand(v, ind):
    top, rest = split16(v)
    return mm(top, ind) + mm(rest, ind)


def headsum(v, ind):
    top, rest = split16(v)
    return mm(top, ind, NT) + mm(rest, ind, NT)


def iotas(n):
    return (
        lax.broadcasted_iota(jnp.int32, (n, n), 0),
        lax.broadcasted_iota(jnp.int32, (n, n), 1),
    )


def colsum(v):
    return jnp.sum(v, axis=0, keepdims=True)


def conv_pre(ext, par, n):
    total = par[4:5, :] + par[0:1, :] * ext[5 : 5 + n, :]
    for tap in range(1, 4):
        total = total + par[tap : tap + 1, :] * ext[5 + tap : 5 + tap + n, :]
    return total


def scan_prep(small, hp, ind, n):
    rows, cols = iotas(n)
    raw = small[:, 2 * STATE :] + hp[0:1, :]
    step = softplus(raw)
    rate = -jnp.exp(hp[1:2, :])
    lower = jnp.where(rows >= cols, 1.0, 0.0).astype(F32)
    cs = mm(lower, step * rate, precision=HIGH)
    tail = jnp.exp(cs[n - 1 : n, :] - cs)
    wide = expand(jnp.concatenate([step, jnp.exp(cs), tail], axis=0), ind)
    return raw, step, rate, cs, wide[0:n], wide[n : 2 * n], wide[2 * n : 3 * n]


def fwd_body(
    inner_ref, gate_ref, small_ref, cp_ref, sp_ref, hp_ref, ind_ref, own_ref,
    ssd_ref, scaled_ref, sq_ref, st_ref, full_ref,
    ext, exts, state, slabs, keep, send, recv, out_sem,
    *, heads, per, size, steps,
):
    n = CHUNK
    at = pl.program_id(0)
    line = Line(size)
    job = Gather(line, lambda j: own_ref, slabs, keep, send, recv)

    @pl.when(at == 0)
    def _():
        line.greet(pltpu.get_barrier_semaphore())
        job.start(0)


    @pl.when(lax.rem(at, per) == 0)
    def _():
        ext[0:8, :] = jnp.zeros((8, ext.shape[1]), F32)
        exts[0:8, :] = jnp.zeros((8, exts.shape[1]), F32)
        state[...] = jnp.zeros_like(state)

    rows, cols = iotas(n)
    ind = ind_ref[...]
    ext[8 : 8 + n, :] = inner_ref[...]
    pre = conv_pre(ext, cp_ref, n)
    x = pre * sigmoid(pre)
    ext[0:8, :] = ext[n : n + 8, :]
    exts[8 : 8 + n, :] = small_ref[:, : 2 * STATE]
    pres = conv_pre(exts, sp_ref, n)
    bc = (pres * sigmoid(pres)).astype(BF16)
    exts[0:8, :] = exts[n : n + 8, :]
    key, query = bc[:, :STATE], bc[:, STATE:]

    _, step, rate, cs, wide_step, wide_cs, wide_tail = scan_prep(small_ref, hp_ref, ind, n)
    cs2 = cs * LOG2E
    cs2t = cs2.T
    xs = x * wide_step
    half = lax.rem(lax.broadcasted_iota(jnp.int32, xs.shape, 1), 2 * HEAD) < HEAD
    xs0 = jnp.where(half, xs, 0.0)
    xs1 = (xs - xs0).astype(BF16)
    xs0 = xs0.astype(BF16)
    before = state[...]
    low = before.astype(BF16)
    st_ref[0] = low
    carried = mm(query, low) * wide_cs
    xw = (xs * wide_tail).astype(BF16)
    state[...] = before * wide_cs[n - 1 : n, :] + mm(key, xw, TN)
    scores = jnp.where(rows >= cols, mm(query, key, NT), 0.0)
    for pair in range(heads // 2):
        lanes = slice(pair * 2 * HEAD, (pair + 1) * 2 * HEAD)
        mats = []
        for h in (2 * pair, 2 * pair + 1):
            dec = jnp.exp2(jnp.minimum(cs2[:, h : h + 1] - cs2t[h : h + 1, :], 0.0))
            mats.append((scores * dec).astype(BF16))
        local = mm(
            jnp.concatenate(mats, axis=1),
            jnp.concatenate([xs0[:, lanes], xs1[:, lanes]], axis=0),
        )
        ssd_ref[:, lanes] = local + carried[:, lanes] + cp_ref[6:7, lanes] * x[:, lanes]
    gate = gate_ref[...]
    gated = ssd_ref[...] * (gate * sigmoid(gate))
    ones = jnp.ones((8, gated.shape[1]), BF16)
    top, rest = split16(gated * gated)
    sq_ref[0] = (mm(ones, top, NT) + mm(ones, rest, NT))[0:1, :]
    scaled_ref[...] = (gated * cp_ref[5:6, :]).astype(BF16)

    for k in range(1, line.n):
        @pl.when(at == k * steps // line.n)
        def _(k=k):
            job.relay(0, k)

    @pl.when(at == steps - 1)
    def _():
        job.arrive(0)
        out = pltpu.make_async_copy(slabs.at[0], full_ref, out_sem)
        out.start()
        job.drain(0)
        out.wait()


def fwd_scan(inner_raw, gate_pre, small, cp, sp, hp, ind, own, heads, size):
    tokens_n, width = inner_raw.shape
    steps = tokens_n // CHUNK
    any_spec = pl.BlockSpec(memory_space=pl.ANY)

    def row(w):
        return pl.BlockSpec((CHUNK, w), lambda c: (c, 0))

    def whole(a):
        return pl.BlockSpec(a.shape, lambda c: (0, 0))

    return pl.pallas_call(
        functools.partial(fwd_body, heads=heads, per=LEN // CHUNK, size=size, steps=steps),
        grid=(steps,),
        in_specs=[row(width), row(width), row(small.shape[1])] + [whole(a) for a in (cp, sp, hp, ind)] + [any_spec],
        out_specs=[
            row(width),
            row(width),
            pl.BlockSpec((1, 1, CHUNK), lambda c: (c, 0, 0)),
            pl.BlockSpec((1, STATE, width), lambda c: (c, 0, 0)),
            any_spec,
        ],
        out_shape=[
            jax.ShapeDtypeStruct((tokens_n, width), F32),
            jax.ShapeDtypeStruct((tokens_n, width), BF16),
            jax.ShapeDtypeStruct((steps, 1, CHUNK), F32),
            jax.ShapeDtypeStruct((steps, STATE, width), BF16),
            jax.ShapeDtypeStruct((size,) + own.shape, BF16),
        ],
        scratch_shapes=[
            pltpu.VMEM((CHUNK + 8, width), F32),
            pltpu.VMEM((CHUNK + 8, 2 * STATE), F32),
            pltpu.VMEM((STATE, width), F32),
            pltpu.VMEM((1, size) + own.shape, BF16),
            pltpu.SemaphoreType.DMA((1,)),
            pltpu.SemaphoreType.DMA((1, 3, size)),
            pltpu.SemaphoreType.DMA((1, size)),
            pltpu.SemaphoreType.DMA,
        ],
        compiler_params=pltpu.CompilerParams(
            collective_id=1, has_side_effects=True, vmem_limit_bytes=32 * 1024 * 1024
        ),
        cost_estimate=pl.CostEstimate(flops=3 * 10**9, bytes_accessed=16 * 10**6, transcendentals=0),
        name="fwd_scan",
    )(inner_raw, gate_pre, small, cp, sp, hp, ind, own)


def back_body(
    up_ref, fac_ref, fac2_ref, gate_ref, ssd_ref, inner_ref, iprev_ref, small_ref, sprev_ref, st_ref,
    res_ref, rn_ref, cp_ref, sp_ref, hp_ref, ind_ref, gain_ref,
    wout_hbm, scaled_hbm, win_hbm, wsmall_hbm, normed_hbm,
    new_ref, sdsum_ref, steplow_ref, dcp_ref, dsp_ref, dhp_ref, dgain_ref, grad_ref,
    ext, exts, cde, cdes, dstate, rq,
    wout, scaled, win, wsmall, turned, dy, glow, ilow, srow, sgot,
    part, near, away, tpart, tot, got, mine, far,
    load, rsend, rrecv, ssend, srecv, sends, recvs,
    *, heads, per, size, steps,
):
    n = CHUNK
    wide = 2 * n
    model = up_ref.shape[1]
    i = pl.program_id(0)
    begin_gate = steps
    begin_scan = begin_gate + steps // 2
    begin_norm = begin_scan + steps
    last = begin_norm + steps - 1
    line = Line(size)
    square = Square()
    job = Scatter(line, part, grad_ref, near, away, ssend, srecv)
    sums = Total(square, tpart, tot, got, mine, far, sends, recvs)
    loads = [
        pltpu.make_async_copy(src, dst, load.at[k])
        for k, (src, dst) in enumerate(
            ((wout_hbm, wout), (scaled_hbm, scaled), (win_hbm, win), (wsmall_hbm, wsmall), (normed_hbm, turned))
        )
    ]
    copies = [
        remote(srow, sgot.at[square.me], rsend.at[k], rrecv.at[k], who) for k, who in enumerate(square.others())
    ]
    order = job.order()
    early = [(j, p) for j in range(2) for p in order]
    ind = ind_ref[...]

    @pl.when(i == 0)
    def _():
        for copy in loads[:4]:
            copy.start()
        dcp_ref[...] = jnp.zeros_like(dcp_ref)
        dsp_ref[...] = jnp.zeros_like(dsp_ref)
        dhp_ref[...] = jnp.zeros_like(dhp_ref)
        dgain_ref[...] = jnp.zeros_like(dgain_ref)
        rq[...] = jnp.zeros_like(rq)
        line.greet_all(pltpu.get_barrier_semaphore(), square.others())
        loads[0].wait()
        loads[1].wait()

    @pl.when(i < begin_gate)
    def _():
        rows = pl.ds(pl.multiple_of(i * n, n), n)
        low = (fac_ref[...] * up_ref[...]).astype(BF16)
        turned[:, rows] = low.T
        sd = mm(low, wout[...])
        dy[rows, :] = sd
        top, rest = split16(scaled[rows, :].astype(F32) * sd)
        ones = jnp.ones((8, sd.shape[1]), BF16)
        srow[i] = (mm(ones, top, NT) + mm(ones, rest, NT))[0:1, :]

    @pl.when(i == begin_gate - 1)
    def _():
        for copy in copies:
            copy.start()
        job.emit(0, turned, scaled)
        loads[4].start()
        sgot[square.me] = srow[...]
        for copy in copies:
            copy.wait()
        srow[...] = (sgot[0] + sgot[1]) + (sgot[2] + sgot[3])

    @pl.when((i >= begin_gate) & (i < begin_scan))
    def _():
        c = i - begin_gate
        rows = pl.ds(pl.multiple_of(c * wide, wide), wide)
        fac = fac2_ref[...]
        both = [jnp.broadcast_to(srow[2 * c + h], (n, n)).T[:, 0:1] for h in range(2)]
        coef = fac * fac * jnp.concatenate(both, axis=0) / INNER
        gate = gate_ref[...]
        gsig = sigmoid(gate)
        gact = gate * gsig
        ssd = ssd_ref[...]
        sd = dy[rows, :]
        gated = ssd * gact
        gd = cp_ref[5:6, :] * sd - coef * gated
        dcp_ref[5:6, :] += colsum(gated * sd)
        dy[rows, :] = gd * gact
        glow[rows, :] = (gd * ssd * (gsig + gact * (1.0 - gsig))).astype(BF16)

    @pl.when(i == begin_scan - 1)
    def _():
        loads[4].wait()
        job.emit(1, turned, glow)
        loads[2].wait()
        loads[3].wait()

    @pl.when((i >= begin_scan) & (i < begin_norm))
    def _():
        q = i - begin_scan
        chunk = steps - 1 - q
        where = pl.ds(pl.multiple_of(chunk * n, n), n)

        @pl.when(lax.rem(chunk, per) == per - 1)
        def _():
            cde[n : n + 8, :] = jnp.zeros((8, cde.shape[1]), F32)
            cdes[n : n + 8, :] = jnp.zeros((8, cdes.shape[1]), F32)
            dstate[...] = jnp.zeros_like(dstate)

        keep = jnp.where(lax.rem(chunk, per) == 0, 0.0, 1.0).astype(F32)
        rows, cols = iotas(n)
        ext[0:8, :] = iprev_ref[...] * keep
        ext[8 : 8 + n, :] = inner_ref[...]
        exts[0:8, :] = sprev_ref[:, : 2 * STATE] * keep
        exts[8 : 8 + n, :] = small_ref[:, : 2 * STATE]
        pre = conv_pre(ext, cp_ref, n)
        sig = sigmoid(pre)
        x = pre * sig
        slope = sig + x * (1.0 - sig)
        pres = conv_pre(exts, sp_ref, n)
        sigs = sigmoid(pres)
        acts = pres * sigs
        slopes = sigs + acts * (1.0 - sigs)
        bc = acts.astype(BF16)
        key, query = bc[:, :STATE], bc[:, STATE:]
        dyc = dy[where, :]

        raw, step, rate, cs, wide_step, wide_cs, wide_tail = scan_prep(small_ref, hp_ref, ind, n)
        cs2 = cs * LOG2E
        cs2t = cs2.T
        xs = x * wide_step
        xsb = xs.astype(BF16)
        half = lax.rem(lax.broadcasted_iota(jnp.int32, xs.shape, 1), 2 * HEAD) < HEAD
        dy0 = jnp.where(half, dyc, 0.0)
        dy1 = (dyc - dy0).astype(BF16)
        dy0 = dy0.astype(BF16)
        low = st_ref[0]
        dst = dstate[...]
        dlow = dst.astype(BF16)
        dye = dyc * wide_cs
        dyeb = dye.astype(BF16)
        up = headsum(dye * mm(query, low), ind)
        dxs_state = wide_tail * mm(key, dlow)
        down = headsum(xs * dxs_state, ind)
        qdel = mm(dyeb, low, NT)
        kdel = mm((xs * wide_tail).astype(BF16), dlow, NT)
        through = headsum(jnp.broadcast_to(colsum(low.astype(F32) * dst), (8, dst.shape[1])), ind)[0:1, :]
        through = through * jnp.exp(cs[n - 1 : n, :])
        dstate[...] = dst * wide_cs[n - 1 : n, :] + mm(query, dyeb, TN)

        scores = jnp.where(rows <= cols, mm(key, query, NT), 0.0)
        dscores = jnp.zeros((n, n), F32)
        colq = jnp.zeros((n, LANES), F32)
        lane = lax.broadcasted_iota(jnp.int32, (n, LANES), 1)
        dxs = []
        for pair in range(heads // 2):
            lanes = slice(pair * 2 * HEAD, (pair + 1) * 2 * HEAD)
            stacked = jnp.concatenate([dy0[:, lanes], dy1[:, lanes]], axis=0)
            both = mm(xsb[:, lanes], stacked, NT)
            mats = []
            for which, h in enumerate((2 * pair, 2 * pair + 1)):
                dec = jnp.exp2(jnp.minimum(cs2t[h : h + 1, :] - cs2[:, h : h + 1], 0.0))
                mats.append((scores * dec).astype(BF16))
                term = dec * both[:, which * n : (which + 1) * n]
                dscores = dscores + term
                quad = scores * term
                rq[h : h + 1, :] = colsum(quad)
                colq = jnp.where(lane == h, jnp.sum(quad, axis=1, keepdims=True), colq)
            dxs.append(mm(jnp.concatenate(mats, axis=1), stacked))
        dxs = jnp.concatenate(dxs, axis=1) + dxs_state
        dscores = jnp.where(rows <= cols, dscores, 0.0).astype(BF16)
        kdel = kdel + mm(dscores, query)
        qdel = qdel + mm(dscores, key, TN)

        upper = jnp.where(rows <= cols, 1.0, 0.0).astype(F32)
        strict = jnp.where(rows > cols, 1.0, 0.0).astype(F32)
        da = mm(upper, rq[...].T - colq + up, precision=HIGH) + mm(strict, down, precision=HIGH) + through
        grown = headsum(x * dxs, ind) + rate * da
        step_pre = grown * sigmoid(raw)
        steplow = step_pre.astype(BF16)
        steplow_ref[...] = steplow
        dhp_ref[0:1, :] += colsum(step_pre)
        dhp_ref[1:2, :] += rate * colsum(step * da)
        dcp_ref[6:7, :] += colsum(dyc * x)

        cd = (dxs * wide_step + cp_ref[6:7, :] * dyc) * slope
        cde[0:n, :] = cd
        total = cp_ref[3:4, :] * cd
        for tap in range(3):
            total = total + cp_ref[tap : tap + 1, :] * cde[3 - tap : 3 - tap + n, :]
        inner_low = total.astype(BF16)
        ilow[where, :] = inner_low
        for tap in range(4):
            dcp_ref[tap : tap + 1, :] += colsum(cd * ext[5 + tap : 5 + tap + n, :])
        dcp_ref[4:5, :] += colsum(cd)
        cde[n : n + 8, :] = cde[0:8, :]

        cds = jnp.concatenate([kdel, qdel], axis=1) * slopes
        cdes[0:n, :] = cds
        total = sp_ref[3:4, :] * cds
        for tap in range(3):
            total = total + sp_ref[tap : tap + 1, :] * cdes[3 - tap : 3 - tap + n, :]
        sdel = total.astype(BF16)
        for tap in range(4):
            dsp_ref[tap : tap + 1, :] += colsum(cds * exts[5 + tap : 5 + tap + n, :])
        dsp_ref[4:5, :] += colsum(cds)
        cdes[n : n + 8, :] = cdes[0:8, :]

        value = (
            mm(glow[where, :], win[1], NT)
            + mm(inner_low, win[0], NT)
            + mm(jnp.concatenate([sdel, steplow], axis=1), wsmall[...], NT)
        ).astype(BF16)
        tpart[2 * q, :, :model] = value[: n // 2]
        tpart[2 * q + 1, :, :model] = value[n // 2 :]
        tpart[2 * q, :, model:] = sdel[: n // 2]
        tpart[2 * q + 1, :, model:] = sdel[n // 2 :]
        sums.step(0, q)

    @pl.when((i > begin_scan) & (i <= begin_norm))
    def _():
        sums.step(1, i - begin_scan - 1)

    for e, (j, p) in enumerate(early):
        @pl.when(i == begin_scan + 1 + e * steps // len(early))
        def _(j=j, p=p):
            job.fold(j, p)

    @pl.when((i >= begin_scan + 3) & (i < begin_norm + 3))
    def _():
        sums.step(2, i - begin_scan - 3)

    @pl.when((i >= begin_scan + 4) & (i < begin_norm + 4))
    def _():
        sums.step(3, i - begin_scan - 4)

    @pl.when(i == begin_norm - 1)
    def _():
        dhp_ref[2:3, :] = headsum(jnp.broadcast_to(dcp_ref[6:7, :], (8, dcp_ref.shape[1])), ind)[0:1, :]
        job.emit(2, turned, ilow)

    @pl.when(i >= begin_norm)
    def _():
        r = i - begin_norm
        for h in range(2):
            rows = slice(h * (n // 2), (h + 1) * (n // 2))
            back = tot[2 * r + h, :, :model].astype(F32)
            sdsum_ref[rows, :] = tot[2 * r + h, :, model:]
            res = res_ref[rows, :]
            rn = rn_ref[rows, :]
            dgain_ref[...] += colsum(back * res * rn)
            gained = back * gain_ref[...]
            mean = jnp.sum(gained * res, axis=1, keepdims=True) / model
            new_ref[rows, :] = up_ref[rows, :] + rn * gained - (rn * rn * rn * mean) * res

    @pl.when(i == last)
    def _():
        for p in order:
            job.fold(2, p)
        for j in range(3):
            job.finish(j)
            job.drain(j)


def back(up, factor, gate_pre, ssd, inner_raw, small, states, res, rnorm, cp, sp, hp, ind, gain,
         wout, scaled, win, wsmall, normed, heads, size, cid):
    tokens_n, width = inner_raw.shape
    model = up.shape[1]
    steps = tokens_n // CHUNK
    begin_scan = steps + steps // 2
    begin_norm = begin_scan + steps
    rows = model // size
    n = size // 2
    hbm = pl.BlockSpec(memory_space=pl.ANY)
    top = steps - 1

    def norm_at(i):
        return jnp.where(i < begin_norm, top, top - (i - begin_norm))

    def scan_at(i):
        return jnp.clip(top - (i - begin_scan), 0, top)

    def first(w):
        return pl.BlockSpec((CHUNK, w), lambda i: (jnp.where(i < steps, i, norm_at(i)), 0))

    def second(w):
        return pl.BlockSpec((2 * CHUNK, w), lambda i: (jnp.clip(i - steps, 0, steps // 2 - 1), 0))

    def scan(w):
        return pl.BlockSpec((CHUNK, w), lambda i: (scan_at(i), 0))

    def prev(w):
        return pl.BlockSpec((8, w), lambda i: (jnp.maximum(scan_at(i) * (CHUNK // 8) - 1, 0), 0))

    def norm(w):
        return pl.BlockSpec((CHUNK, w), lambda i: (norm_at(i), 0))

    def flat(r, w):
        return pl.BlockSpec((r, w), lambda i: (0, 0))

    def whole(a):
        return flat(*a.shape)

    extra = model + 2 * STATE
    quarter = pltpu.VMEM((steps, CHUNK // 2, extra), BF16)
    pieces = pltpu.VMEM((3, n, rows, width), BF16)
    return pl.pallas_call(
        functools.partial(back_body, heads=heads, per=LEN // CHUNK, size=size, steps=steps),
        grid=(begin_norm + steps,),
        in_specs=[
            first(model), pl.BlockSpec((CHUNK, 1), lambda i: (jnp.minimum(i, top), 0)), second(1),
            second(width), second(width),
            scan(width), prev(width), scan(small.shape[1]), prev(small.shape[1]),
            pl.BlockSpec((1, STATE, width), lambda i: (scan_at(i), 0, 0)),
            norm(model), norm(1),
        ] + [whole(a) for a in (cp, sp, hp, ind, gain)] + [hbm] * 5,
        out_specs=[
            norm(model), norm(2 * STATE), scan(LANES),
            flat(8, width), flat(8, 2 * STATE), flat(8, LANES), flat(1, model),
            pl.BlockSpec((3, rows, width), lambda i: (0, 0, 0)),
        ],
        out_shape=[
            jax.ShapeDtypeStruct((tokens_n, model), F32),
            jax.ShapeDtypeStruct((tokens_n, 2 * STATE), BF16),
            jax.ShapeDtypeStruct((tokens_n, LANES), BF16),
            jax.ShapeDtypeStruct((8, width), F32),
            jax.ShapeDtypeStruct((8, 2 * STATE), F32),
            jax.ShapeDtypeStruct((8, LANES), F32),
            jax.ShapeDtypeStruct((1, model), F32),
            jax.ShapeDtypeStruct((3, rows, width), F32),
        ],
        scratch_shapes=[
            pltpu.VMEM((CHUNK + 8, width), F32),
            pltpu.VMEM((CHUNK + 8, 2 * STATE), F32),
            pltpu.VMEM((CHUNK + 8, width), F32),
            pltpu.VMEM((CHUNK + 8, 2 * STATE), F32),
            pltpu.VMEM((STATE, width), F32),
            pltpu.VMEM((LANES, CHUNK), F32),
            pltpu.VMEM(wout.shape, BF16),
            pltpu.VMEM(scaled.shape, BF16),
            pltpu.VMEM(win.shape, BF16),
            pltpu.VMEM(wsmall.shape, BF16),
            pltpu.VMEM(normed.shape, BF16),
            pltpu.VMEM((tokens_n, width), F32),
            pltpu.VMEM((tokens_n, width), BF16),
            pltpu.VMEM((tokens_n, width), BF16),
            pltpu.VMEM((steps, 1, CHUNK), F32),
            pltpu.VMEM((4, steps, 1, CHUNK), F32),
            pltpu.VMEM((3, size, rows, width), BF16), pieces, pieces,
            pltpu.VMEM((2 * steps, CHUNK // 2, extra), BF16),
            pltpu.VMEM((2 * steps, CHUNK // 2, extra), BF16),
            quarter, quarter, quarter,
            pltpu.SemaphoreType.DMA((5,)),
            pltpu.SemaphoreType.DMA((3,)),
            pltpu.SemaphoreType.DMA((3,)),
            pltpu.SemaphoreType.DMA((2, 3, n)),
            pltpu.SemaphoreType.DMA((2, 3, n)),
            pltpu.SemaphoreType.DMA((3, steps)),
            pltpu.SemaphoreType.DMA((3, steps)),
        ],
        compiler_params=pltpu.CompilerParams(
            collective_id=cid, has_side_effects=True, vmem_limit_bytes=63 * 1024 * 1024
        ),
        name="back",
    )(up, factor, factor, gate_pre, ssd, inner_raw, inner_raw, small, small, states, res, rnorm,
      cp, sp, hp, ind, gain, wout, scaled, win, wsmall, normed)


SLICE = 256
TILE = 256


def stage_body(*refs, size, out, into):
    refs = list(refs)

    def take(n):
        got = refs[:n]
        del refs[:n]
        return got

    (res_ref,) = take(1)
    if out:
        scaled_ref, wout_ref, sq_ref = take(3)
    if into:
        gain_ref, wsmall_ref, own_ref = take(3)
    if out:
        new_ref, sums_ref = take(2)
    if into:
        normed_ref, rnorm_ref, small_ref, inner_ref, gate_ref, full_ref = take(6)
    if out:
        part, tot, got, mine, far, rows_got, facs, fresh, sends, recvs, rsend, rrecv = take(12)
    if into:
        slabs, normed, turned, inner, gate, keep, gsend, grecv = take(8)
    (sems,) = take(1)
    assert not refs

    tokens_n, model = res_ref.shape
    line = Line(size)
    square = Square()
    barrier = pltpu.get_barrier_semaphore()
    if into:
        line.greet(barrier, square.others() if out else ())
    else:
        for who in square.others():
            pl.semaphore_signal(barrier, inc=1, device_id=who, device_id_type=MESH)
        pl.semaphore_wait(barrier, 3)

    pending = []

    def flush(src, dst):
        copy = pltpu.make_async_copy(src, dst, sems.at[len(pending)])
        copy.start()
        pending.append(copy)

    ticks = []
    if into:
        job = Gather(line, lambda j: own_ref.at[1 - j], slabs, keep, gsend, grecv)
        job.start(0)
        ticks = [functools.partial(job.relay, 0, k) for k in range(1, line.n)]
        ticks.append(functools.partial(job.start, 1))
        ticks += [functools.partial(job.relay, 1, k) for k in range(1, line.n)]

    if out:
        chunks = model // SLICE
        half = tokens_n // 2
        sums = Total(square, part, tot, got, mine, far, sends, recvs)
        copies = [
            remote(sq_ref, rows_got.at[square.me], rsend.at[k], rrecv.at[k], who)
            for k, who in enumerate(square.others())
        ]
        for copy in copies:
            copy.start()
        for c in range(chunks):
            value = mm(scaled_ref[...], wout_ref[c * SLICE : (c + 1) * SLICE, :], NT).astype(BF16)
            part[2 * c] = value[:half]
            part[2 * c + 1] = value[half:]
            sums.step(0, c)
        for c in range(chunks):
            sums.step(1, c)
        rows_got[square.me] = sq_ref[...]
        for copy in copies:
            copy.wait()
        total = (rows_got[0] + rows_got[1]) + (rows_got[2] + rows_got[3])
        sums_ref[...] = total
        factor = lax.rsqrt(total / INNER + EPS)
        for i in range(tokens_n // LANES):
            facs[i * LANES : (i + 1) * LANES, :] = jnp.broadcast_to(factor[i], (LANES, LANES)).T

        def use(c):
            for h in range(2):
                where = slice(h * half, (h + 1) * half)
                for s in range(SLICE // LANES):
                    lanes = slice(c * SLICE + s * LANES, c * SLICE + (s + 1) * LANES)
                    value = tot[2 * c + h, :, s * LANES : (s + 1) * LANES].astype(F32)
                    new = res_ref[where, lanes].astype(F32) + facs[where, :] * value
                    fresh[where, lanes] = new.astype(fresh.dtype)
            flush(fresh.at[:, pl.ds(c * SLICE, SLICE)], new_ref.at[:, pl.ds(c * SLICE, SLICE)])

        spread = max(1, -(-len(ticks) // chunks))
        for c in range(chunks):
            for tick in ticks[:spread]:
                tick()
            ticks = ticks[spread:]
            sums.step(2, c)
            if c:
                sums.step(3, c - 1)
                use(c - 1)
        sums.step(3, chunks - 1)
        use(chunks - 1)
        res_ref = fresh

    if into:
        def norm(i, _):
            rows = pl.ds(pl.multiple_of(i * TILE, TILE), TILE)
            value = res_ref[rows, :].astype(F32)
            scale = lax.rsqrt(jnp.sum(value * value, axis=1, keepdims=True) / model + EPS)
            low = (value * scale * gain_ref[...]).astype(BF16)
            rnorm_ref[rows, :] = scale
            normed[rows, :] = low
            turned[:, rows] = low.T
            small_ref[rows, :] = mm(low, wsmall_ref[...])
            return 0

        lax.fori_loop(0, tokens_n // TILE, norm, 0)
        flush(turned, normed_ref)
        for tick in ticks:
            tick()

        def project(j, dst):
            weight = slabs[j].reshape(model, slabs.shape[3])

            def tile(i, _):
                rows = pl.ds(i * TILE, TILE)
                dst[rows, :] = mm(normed[rows, :], weight)
                return 0

            lax.fori_loop(0, tokens_n // TILE, tile, 0)

        for j, dst, ref in ((0, inner, inner_ref), (1, gate, gate_ref)):
            job.arrive(j)
            flush(slabs.at[j], full_ref.at[j])
            project(j, dst)
            flush(dst, ref)
        job.drain(0)
        job.drain(1)
    for copy in pending:
        copy.wait()


def stage(res, size, cid, out=None, into=None, last=False):
    tokens_n, model = res.shape
    vm = pl.BlockSpec(memory_space=pltpu.VMEM)
    hbm = pl.BlockSpec(memory_space=pl.ANY)
    chunks = model // SLICE
    args, in_specs = [res], [vm]
    out_specs, out_shape, scratch = [], [], []
    flushes = 0
    kind = BF16 if last else F32
    if out is not None:
        scaled, wout, sq = out
        args += [scaled, wout, sq]
        in_specs += [vm, vm, vm]
        out_specs += [hbm, vm]
        out_shape += [
            jax.ShapeDtypeStruct(res.shape, kind),
            jax.ShapeDtypeStruct(sq.shape, F32),
        ]
        chunk = pltpu.VMEM((chunks, tokens_n // 2, SLICE), BF16)
        both = pltpu.VMEM((2 * chunks, tokens_n // 2, SLICE), BF16)
        scratch += [
            both, both, chunk, chunk, chunk,
            pltpu.VMEM((4,) + sq.shape, F32),
            pltpu.VMEM((tokens_n, LANES), F32),
            pltpu.VMEM(res.shape, kind),
            pltpu.SemaphoreType.DMA((3, chunks)),
            pltpu.SemaphoreType.DMA((3, chunks)),
            pltpu.SemaphoreType.DMA((3,)),
            pltpu.SemaphoreType.DMA((3,)),
        ]
        flushes += chunks
    if into is not None:
        gain, wsmall, own = into
        rows, width = own.shape[1:]
        args += [gain, wsmall, own]
        in_specs += [vm, vm, hbm]
        out_specs += [hbm, vm, vm, hbm, hbm, hbm]
        out_shape += [
            jax.ShapeDtypeStruct((model, tokens_n), BF16),
            jax.ShapeDtypeStruct((tokens_n, 1), F32),
            jax.ShapeDtypeStruct((tokens_n, wsmall.shape[1]), F32),
            jax.ShapeDtypeStruct((tokens_n, width), F32),
            jax.ShapeDtypeStruct((tokens_n, width), F32),
            jax.ShapeDtypeStruct((2, size, rows, width), BF16),
        ]
        scratch += [
            pltpu.VMEM((2, size, rows, width), BF16),
            pltpu.VMEM(res.shape, BF16),
            pltpu.VMEM((model, tokens_n), BF16),
            pltpu.VMEM((tokens_n, width), F32),
            pltpu.VMEM((tokens_n, width), F32),
            pltpu.SemaphoreType.DMA((2,)),
            pltpu.SemaphoreType.DMA((2, 3, size)),
            pltpu.SemaphoreType.DMA((2, size)),
        ]
        flushes += 5
    scratch.append(pltpu.SemaphoreType.DMA((flushes,)))
    return pl.pallas_call(
        functools.partial(stage_body, size=size, out=out is not None, into=into is not None),
        in_specs=in_specs,
        out_specs=out_specs,
        out_shape=out_shape,
        scratch_shapes=scratch,
        compiler_params=pltpu.CompilerParams(
            collective_id=cid, has_side_effects=True, vmem_limit_bytes=60 * 1024 * 1024
        ),
        name="stage",
    )(*args)


def smalls_body(pack_ref, full_ref, wide_ref, part, near, far, own, load, ssend, srecv, keep, gsend, grecv, send, recv, *, size, span):
    line = Line(size)
    square = Square()
    copy = pltpu.make_async_copy(pack_ref, part.at[0], load)
    copy.start()
    line.greet_all(pltpu.get_barrier_semaphore(), (square.mate, square.across))
    copy.wait()
    job = Scatter(line, part, own, near, far, ssend, srecv)
    job.start(0)
    for i in job.order():
        job.fold(0, i)
    job.finish(0)
    spread = Gather(line, lambda j: own.at[0], full_ref, keep, gsend, grecv)
    spread.start(0)
    for k in range(1, line.n):
        spread.relay(0, k)
    spread.arrive(0)
    flat = full_ref[0].reshape(-1, full_ref.shape[3])
    wide_ref[square.me] = flat[:span]
    over = lax.rem(square.me + 2, 4)
    first = remote(wide_ref.at[square.me], wide_ref.at[square.me], send.at[0], recv.at[0], square.across)
    first.start()
    second = remote(wide_ref.at[square.me], wide_ref.at[square.me], send.at[1], recv.at[1], square.mate)
    second.start()
    first.wait()
    third = remote(wide_ref.at[over], wide_ref.at[over], send.at[2], recv.at[2], square.mate)
    third.start()
    second.wait()
    third.wait()
    job.drain(0)
    spread.drain(0)


def smalls(pack, span, cid):
    size, r, w = pack.shape
    n = size // 2
    vm = pl.BlockSpec(memory_space=pltpu.VMEM)
    return pl.pallas_call(
        functools.partial(smalls_body, size=size, span=span),
        in_specs=[pl.BlockSpec(memory_space=pl.ANY)],
        out_specs=[vm, vm],
        out_shape=[
            jax.ShapeDtypeStruct((1,) + pack.shape, BF16),
            jax.ShapeDtypeStruct((4, span, w), BF16),
        ],
        scratch_shapes=[
            pltpu.VMEM((1,) + pack.shape, BF16),
            pltpu.VMEM((1, n, r, w), BF16),
            pltpu.VMEM((1, n, r, w), BF16),
            pltpu.VMEM((1, r, w), BF16),
            pltpu.SemaphoreType.DMA,
            pltpu.SemaphoreType.DMA((2, 1, n)),
            pltpu.SemaphoreType.DMA((2, 1, n)),
            pltpu.SemaphoreType.DMA((1,)),
            pltpu.SemaphoreType.DMA((1, 3, size)),
            pltpu.SemaphoreType.DMA((1, size)),
            pltpu.SemaphoreType.DMA((3,)),
            pltpu.SemaphoreType.DMA((3,)),
        ],
        compiler_params=pltpu.CompilerParams(
            collective_id=cid, has_side_effects=True, vmem_limit_bytes=32 * 1024 * 1024
        ),
        name="smalls",
    )(pack)


def fold_columns(v, w):
    return jnp.concatenate([v[:, i * w : (i + 1) * w] for i in range(v.shape[1] // w)], axis=0)


def unfold_columns(v, r):
    return jnp.concatenate([v[i * r : (i + 1) * r] for i in range(v.shape[0] // r)], axis=1)


def shards(
    tokens, inproj, stepproj, stateproj, outproj, convinner, biasinner, convstate, biasstate,
    stepbias, decaylog, skipgain, normgain, inputgain, cotangent,
):
    layers = inproj.shape[0]
    width = inproj.shape[3]
    heads = stepproj.shape[2]
    model = tokens.shape[1]
    pad = LANES - heads
    size = lax.axis_size("dp")
    rows = model // size
    quarter = model // 4
    tensor_at = lax.axis_index("tensor")
    ind = (jnp.arange(LANES)[:, None] == (jnp.arange(width) // HEAD)[None, :]).astype(BF16)
    small_w = jnp.concatenate([stateproj, stepproj, jnp.zeros((layers, model, pad), BF16)], axis=2)
    zero_row = jnp.zeros((layers, 1, width), F32)
    cp = jnp.concatenate(
        [convinner, biasinner[:, None], normgain[:, None], jnp.repeat(skipgain, HEAD, axis=1)[:, None], zero_row],
        axis=1,
    )
    sp = jnp.concatenate([convstate, biasstate[:, None], jnp.zeros((layers, 3, 2 * STATE), F32)], axis=1)
    hp = jnp.concatenate(
        [jnp.pad(jnp.stack([stepbias, decaylog], axis=1), ((0, 0), (0, 0), (0, pad))), jnp.zeros((layers, 6, LANES), F32)],
        axis=1,
    )
    outt = jnp.swapaxes(outproj, 1, 2)

    def into(at):
        return (inputgain[at][None, :], small_w[at], inproj[at])

    residual = tokens
    projected = stage(residual, size, 0, into=into(0))
    kept = []
    for at in range(layers):
        normed, rnorm, small, inner_raw, gate_pre, w_in = projected
        ssd, scaled, sq, states, w_out = fwd_scan(
            inner_raw, gate_pre, small, cp[at], sp[at], hp[at], ind, outt[at], heads, size
        )
        w_out = w_out.reshape(model, width)
        w_in = w_in.reshape(2, model, width)
        before = residual
        if at < layers - 1:
            residual, sq, *projected = stage(residual, size, 2, out=(scaled, w_out, sq), into=into(at + 1))
        else:
            mixed, sq = stage(residual, size, 3, out=(scaled, w_out, sq), last=True)
        factor = lax.rsqrt(sq.reshape(-1, 1) / INNER + EPS)
        kept.append((before, rnorm, normed, gate_pre, inner_raw, small, ssd, scaled, states, factor, w_in, w_out))

    upstream = cotangent.astype(F32)
    big = [None] * layers
    little = [None] * layers
    for at in reversed(range(layers)):
        before, rnorm, normed, gate_pre, inner_raw, small, ssd, scaled, states, factor, w_in, w_out = kept[at]
        upstream, sdel, steplow, dcp, dsp, dhp, gain_grad, big[at] = back(
            upstream, factor, gate_pre, ssd, inner_raw, small, states, before.astype(F32), rnorm,
            cp[at], sp[at], hp[at], ind, inputgain[at][None, :], w_out, scaled, w_in, small_w[at], normed, heads, size, 4
        )
        step_grad = mm(steplow, normed, (((0,), (1,)), ((), ())))[:16]
        state_grad = mm(lax.dynamic_slice_in_dim(normed, tensor_at * quarter, quarter, axis=0), sdel)
        little[at] = (step_grad, state_grad, dcp, dsp, dhp, gain_grad)
    big = jnp.stack(big)
    inproj_grad = big[:, 1:]
    outproj_grad = jnp.swapaxes(big[:, 0], 1, 2)
    w = 2 * STATE
    blocks = [little[at][1] for at in range(layers)] + [little[at][3] for at in range(layers)]
    span = sum(v.shape[0] for v in blocks)
    for at in range(layers):
        step_grad, _, dcp, _, dhp, gain_grad = little[at]
        blocks += [fold_columns(step_grad, w), fold_columns(dcp, w), fold_columns(dhp.reshape(4, w), w)]
        blocks += [fold_columns(gain_grad, w)]
    places = [v.shape[0] for v in blocks]
    lines = -(-sum(places) // (16 * size)) * 16 * size
    pack = jnp.concatenate([v.astype(BF16) for v in blocks] + [jnp.zeros((lines - sum(places), w), BF16)], axis=0)
    full, wide = smalls(pack.reshape(size, lines // size, w), span, 6)
    full = full.reshape(lines, w).astype(F32)
    wide = wide.astype(F32)
    spots = [sum(places[:i]) for i in range(len(places))]
    state_grad = jnp.stack(
        [jnp.concatenate([wide[t, spots[at] : spots[at] + quarter] for t in range(4)], axis=0) for at in range(layers)]
    )
    dsp = jnp.sum(wide[:, spots[layers] :].reshape(4, layers, 8, w), axis=0)
    found = [[], [], [], []]
    for at in range(layers):
        for m, r in enumerate((16, 8, 4, 1)):
            i = 2 * layers + 4 * at + m
            found[m].append(unfold_columns(full[spots[i] : spots[i] + places[i]], r))
    step_grad = jnp.stack([jnp.swapaxes(v, 0, 1)[:, :heads] for v in found[0]])
    dcp = jnp.stack(found[1])
    dhp = jnp.stack([v.reshape(8, LANES) for v in found[2]])
    gain_grad = jnp.stack([v[0] for v in found[3]])
    return (
        mixed,
        upstream,
        inproj_grad,
        step_grad,
        state_grad,
        outproj_grad,
        dcp[:, 0:4],
        dcp[:, 4],
        dsp[:, 0:4],
        dsp[:, 4],
        dhp[:, 0, :heads],
        dhp[:, 1, :heads],
        dhp[:, 2, :heads],
        dcp[:, 5],
        gain_grad,
    )


def solution(mesh):
    in_specs = (
        P("dp", None),
        P(None, None, "dp", "tensor"),
        P(None, None, "tensor"),
        P(),
        P(None, "tensor", "dp"),
        P(None, None, "tensor"),
        P(None, "tensor"),
        P(),
        P(),
        P(None, "tensor"),
        P(None, "tensor"),
        P(None, "tensor"),
        P(None, "tensor"),
        P(),
        P("dp", None),
    )
    out_specs = (
        P("dp", None),
        P("dp", None),
        P(None, None, "dp", "tensor"),
        P(None, None, "tensor"),
        P(),
        P(None, "tensor", "dp"),
        P(None, None, "tensor"),
        P(None, "tensor"),
        P(),
        P(),
        P(None, "tensor"),
        P(None, "tensor"),
        P(None, "tensor"),
        P(None, "tensor"),
        P(),
    )
    return jax.shard_map(shards, mesh=mesh, in_specs=in_specs, out_specs=out_specs, check_vma=False)
```

```python
import functools
import math

import jax
import jax.numpy as jnp
from jax import lax
from jax.experimental import pallas as pl
from jax.experimental.pallas import tpu as pltpu
from jax.sharding import PartitionSpec as P

STATE = 128
LEN = 1024
INNER = 3072
HEAD = 64
CHUNK = 128
SLICE = 256
TILE = 256
PACK = 544
SPAN = 400
VMEM_LIMIT = 65000 * 1024
LANES = 128
EPS = 1e-05
LOG2E = 1.4426950408889634

HIGH = lax.Precision.HIGHEST
NN = (((1,), (0,)), ((), ()))
NT = (((1,), (1,)), ((), ()))
TN = (((0,), (0,)), ((), ()))
F32 = jnp.float32
BF16 = jnp.bfloat16
MESH = pl.DeviceIdType.MESH


def remote(src, dst, send, recv, where):
    return pltpu.make_async_remote_copy(
        src_ref=src, dst_ref=dst, send_sem=send, recv_sem=recv, device_id=where, device_id_type=MESH
    )


class Line:
    def __init__(self, size):
        self.n = size // 2
        me = lax.axis_index("dp")
        self.me = me
        self.at = me // 2
        self.side = lax.rem(me, 2)
        self.pair = {"dp": me + 1 - 2 * self.side}
        self.right = {"dp": jnp.minimum(me + 2, size - 1)}
        self.left = {"dp": jnp.maximum(me - 2, 0)}
        self.has_left = self.at > 0
        self.has_right = self.at < self.n - 1

    def greet(self, barrier, more=()):
        for who in more:
            pl.semaphore_signal(barrier, inc=1, device_id=who, device_id_type=MESH)
        pl.semaphore_signal(barrier, inc=1, device_id=self.pair, device_id_type=MESH)

        @pl.when(self.has_left)
        def _():
            pl.semaphore_signal(barrier, inc=1, device_id=self.left, device_id_type=MESH)

        @pl.when(self.has_right)
        def _():
            pl.semaphore_signal(barrier, inc=1, device_id=self.right, device_id_type=MESH)

        peers = 1 + len(more) + self.has_left.astype(jnp.int32) + self.has_right.astype(jnp.int32)
        pl.semaphore_wait(barrier, peers)

    def greet_all(self, barrier, more=()):
        for who in list(more) + [self.pair]:
            pl.semaphore_signal(barrier, inc=1, device_id=who, device_id_type=MESH)
        for i in range(self.n):
            @pl.when(i != self.at)
            def _(i=i):
                pl.semaphore_signal(barrier, inc=1, device_id={"dp": 2 * i + self.side}, device_id_type=MESH)
        pl.semaphore_wait(barrier, self.n + len(more))


class Gather:
    def __init__(self, line, own, full, keep, send, recv):
        self.line, self.own, self.full, self.keep, self.send, self.recv = line, own, full, keep, send, recv

    def copy(self, j, slab, way, src=None):
        where = (self.line.right, self.line.left, self.line.pair)[way]
        src = self.full.at[j, slab] if src is None else src
        return remote(src, self.full.at[j, slab], self.send.at[j, way, slab], self.recv.at[j, slab], where)

    def start(self, j):
        line = self.line
        pltpu.make_async_copy(self.own(j), self.full.at[j, line.me], self.keep.at[j]).start()

        @pl.when(line.has_right)
        def _():
            self.copy(j, line.me, 0, self.own(j)).start()

        @pl.when(line.has_left)
        def _():
            self.copy(j, line.me, 1, self.own(j)).start()

        self.copy(j, line.me, 2, self.own(j)).start()

    def relay(self, j, k):
        line = self.line

        @pl.when(line.at >= k)
        def _():
            slab = line.me - 2 * k
            self.copy(j, slab, 0).wait_recv()

            @pl.when(line.has_right)
            def _():
                self.copy(j, slab, 0).start()

            self.copy(j, slab, 2).start()

        @pl.when(line.at + k < line.n)
        def _():
            slab = line.me + 2 * k
            self.copy(j, slab, 1).wait_recv()

            @pl.when(line.has_left)
            def _():
                self.copy(j, slab, 1).start()

            self.copy(j, slab, 2).start()

    def arrive(self, j):
        line = self.line
        pltpu.make_async_copy(self.own(j), self.full.at[j, line.me], self.keep.at[j]).wait()
        for place in range(line.n):
            self.copy(j, 2 * place + 1 - line.side, 2).wait_recv()

    def drain(self, j):
        line = self.line
        for place in range(line.n):
            slab = 2 * place + line.side
            self.copy(j, slab, 2).wait_send()

            @pl.when(line.has_right & (place <= line.at))
            def _():
                self.copy(j, slab, 0).wait_send()

            @pl.when(line.has_left & (place >= line.at))
            def _():
                self.copy(j, slab, 1).wait_send()


class Square:
    def __init__(self):
        me = lax.axis_index("tensor")
        self.me = me
        self.half = lax.rem(me, 2)
        self.mate = {"tensor": me + 1 - 2 * self.half}
        self.across = {"tensor": lax.rem(me + 2, 4)}

    def others(self):
        return [{"tensor": lax.rem(self.me + k, 4)} for k in (1, 2, 3)]


class Total:
    def __init__(self, square, part, got, far, other, send, recv):
        self.square, self.part, self.got, self.far, self.other = square, part, got, far, other
        self.send, self.recv = send, recv

    def first(self, c):
        sq = self.square
        return remote(
            self.part.at[2 * c + 1 - sq.half], self.got.at[c], self.send.at[0, c], self.recv.at[0, c], sq.mate
        )

    def second(self, c):
        sq = self.square
        return remote(self.part.at[2 * c + sq.half], self.far.at[c], self.send.at[1, c], self.recv.at[1, c], sq.across)

    def third(self, c):
        sq = self.square
        return remote(self.part.at[2 * c + sq.half], self.other.at[c], self.send.at[2, c], self.recv.at[2, c], sq.mate)

    def step(self, kind, c):
        slot = 2 * c + self.square.half
        if kind == 0:
            self.first(c).start()
        elif kind == 1:
            self.first(c).wait_recv()
            self.part[slot] = (self.part[slot].astype(F32) + self.got[c].astype(F32)).astype(BF16)
            self.second(c).start()
        elif kind == 2:
            self.second(c).wait()
            self.part[slot] = (self.part[slot].astype(F32) + self.far[c].astype(F32)).astype(BF16)
            self.third(c).start()
        else:
            self.third(c).wait_recv()
            self.first(c).wait_send()
            self.third(c).wait_send()
            self.part[2 * c + 1 - self.square.half] = self.other[c]


class Scatter:
    def __init__(self, line, part, out, near, far, send, recv):
        self.line, self.part, self.out, self.near, self.far = line, part, out, near, far
        self.send, self.recv = send, recv

    def order(self):
        n = self.line.n
        seq = []
        for i in range((n + 1) // 2):
            seq.append(i)
            if n - 1 - i != i:
                seq.append(n - 1 - i)
        return seq

    def cross(self, j, i):
        line = self.line
        return remote(
            self.part.at[j, 2 * i + 1 - line.side], self.near.at[j, i], self.send.at[0, j, i], self.recv.at[0, j, i], line.pair
        )

    def straight(self, j, i, source):
        line = self.line
        return remote(
            self.part.at[j, 2 * i + line.side], self.far.at[j, source], self.send.at[1, j, i], self.recv.at[1, j, source],
            {"dp": 2 * i + line.side},
        )

    def start(self, j):
        for i in self.order():
            self.cross(j, i).start()

    def emit(self, j, turned, right):
        rows = self.part.shape[2]
        for i in self.order():
            value = mm(turned[2 * i * rows : 2 * (i + 1) * rows, :], right[...]).astype(BF16)
            self.part[j, 2 * i] = value[:rows]
            self.part[j, 2 * i + 1] = value[rows:]
            self.cross(j, i).start()

    def fold(self, j, i):
        line = self.line
        self.cross(j, i).wait_recv()
        slot = 2 * i + line.side
        self.part[j, slot] = (self.part[j, slot].astype(F32) + self.near[j, i].astype(F32)).astype(BF16)

        @pl.when(i != line.at)
        def _():
            self.straight(j, i, line.at).start()

    def finish(self, j):
        line = self.line
        out = self.out(j)
        out[...] = self.part[j, line.me].astype(out.dtype)
        for i in range(line.n):
            @pl.when(i != line.at)
            def _(i=i):
                self.straight(j, i, i).wait_recv()
                out[...] += self.far[j, i].astype(out.dtype)

    def drain(self, j):
        for i in range(self.line.n):
            self.cross(j, i).wait_send()

            @pl.when(i != self.line.at)
            def _(i=i):
                self.straight(j, i, self.line.at).wait_send()


def mm(left, right, dims=NN, precision=None):
    return lax.dot_general(left, right, dims, precision=precision, preferred_element_type=F32)


def sigmoid(v):
    return 0.5 * jnp.tanh(0.5 * v) + 0.5


def softplus(v):
    return jnp.maximum(v, 0.0) + jnp.log1p(jnp.exp(-jnp.abs(v)))


def split16(v):
    top = v.astype(BF16)
    return top, (v - top.astype(F32)).astype(BF16)


def expand(v, ind):
    top, rest = split16(v)
    return mm(top, ind) + mm(rest, ind)


def headsum(v, ind):
    top, rest = split16(v)
    return mm(top, ind, NT) + mm(rest, ind, NT)


def iotas(n):
    return (
        lax.broadcasted_iota(jnp.int32, (n, n), 0),
        lax.broadcasted_iota(jnp.int32, (n, n), 1),
    )


def colsum(v):
    return jnp.sum(v, axis=0, keepdims=True)


def conv_pre(ext, par, n):
    total = par[4:5, :] + par[0:1, :] * ext[5 : 5 + n, :]
    for tap in range(1, 4):
        total = total + par[tap : tap + 1, :] * ext[5 + tap : 5 + tap + n, :]
    return total


def scan_prep(small, hp, ind, n):
    rows, cols = iotas(n)
    raw = small[:, 2 * STATE :] + hp[0:1, :]
    step = softplus(raw)
    rate = -jnp.exp(hp[1:2, :])
    lower = jnp.where(rows >= cols, 1.0, 0.0).astype(F32)
    cs = mm(lower, step * rate, precision=HIGH)
    tail = jnp.exp(cs[n - 1 : n, :] - cs)
    wide = expand(jnp.concatenate([step, jnp.exp(cs), tail], axis=0), ind)
    return raw, step, rate, cs, wide[0:n], wide[n : 2 * n], wide[2 * n : 3 * n]


def block_of(slabs, at, rows):
    step = math.gcd(LANES, rows)
    pieces = []
    for k in range(LANES // step):
        row = at * LANES + k * step
        slab = row // rows
        pieces.append(slabs[slab, pl.ds(pl.multiple_of(row - slab * rows, step), step), :])
    return pieces[0] if len(pieces) == 1 else jnp.concatenate(pieces, axis=0)


def put_params(cp, sp, hp, ind, layer, params):
    conv, bias, norm, convs, biass, head = params
    width = cp.shape[1]
    row = lax.broadcasted_iota(jnp.int32, (LANES, width), 0)
    lane = lax.broadcasted_iota(jnp.int32, (LANES, width), 1)
    ind[...] = jnp.where(lane // HEAD == row, 1.0, 0.0).astype(BF16)
    hp[...] = head[layer]
    cp[0:4, :] = conv[layer]
    cp[4:5, :] = bias[layer : layer + 1, :]
    cp[5:6, :] = norm[layer : layer + 1, :]
    cp[6:8, :] = expand(hp[...], ind[...])[2:4, :]
    sp[0:4, :] = convs[layer]
    sp[4:5, :] = biass[layer : layer + 1, :]


def place_rows(dst, at, value):
    r = dst.shape[1]
    for g in range(0, value.shape[0], 16):
        dst[(at + g) // r, (at + g) % r : (at + g) % r + 16, :] = value[g : g + 16].astype(dst.dtype)


def pack_rows(size):
    return -(-PACK // (16 * size)) * 16


def put_pack(dst, me, turned, steps_low, sdel, dcp, dsp, dhp, dgain):
    model = turned.shape[0]
    quarter = model // 4
    w = sdel.shape[1]

    def empty(n):
        return jnp.zeros((n, w), F32)

    place_rows(dst, 0, mm(turned[pl.ds(pl.multiple_of(me * quarter, quarter), quarter), :], sdel[...]))
    place_rows(dst, quarter, jnp.concatenate([dsp, empty(8)], axis=0))
    grown = mm(turned[...], steps_low[...]).T[:16]
    at = quarter + 16
    for b in range(model // w):
        place_rows(dst, at, grown[:, b * w : (b + 1) * w])
        at += 16
    place_rows(dst, at, jnp.concatenate([dcp[:, :w], dcp[:, w : 2 * w]], axis=0))
    place_rows(dst, at + 16, jnp.concatenate([dcp[:, 2 * w :], jnp.concatenate([dhp, dhp], axis=1)], axis=0))
    rows = [dgain[:, b * w : (b + 1) * w] for b in range(model // w)]
    place_rows(dst, at + 32, jnp.concatenate(rows + [empty(16 - len(rows))], axis=0))
    assert at + 48 == PACK


class Smalls:
    def __init__(self, line, square, pack, near, away, own, full, wide, sems):
        send, recv, keep, gsend, grecv, self.xsend, self.xrecv = sems
        self.square, self.full, self.wide = square, full, wide
        self.sum = Scatter(line, pack, lambda j: own.at[j], near, away, send, recv)
        self.spread = Gather(line, lambda j: own.at[0], full, keep, gsend, grecv)

    def swap(self, k):
        sq = self.square
        slot = (sq.me, sq.me, lax.rem(sq.me + 2, 4))[k]
        who = (sq.across, sq.mate, sq.mate)[k]
        return remote(self.wide.at[slot], self.wide.at[slot], self.xsend.at[k], self.xrecv.at[k], who)

    def turn(self):
        self.sum.finish(0)
        self.spread.start(0)

    def cross(self):
        self.spread.arrive(0)
        flat = self.full[0].reshape(-1, self.full.shape[3])
        self.wide[self.square.me] = flat[: self.wide.shape[1]]
        self.swap(0).start()
        self.swap(1).start()

    def cross_on(self):
        self.swap(0).wait_recv()
        self.swap(2).start()

    def end(self):
        self.swap(1).wait_recv()
        self.swap(2).wait_recv()
        for k in range(3):
            self.swap(k).wait_send()
        self.sum.drain(0)
        self.spread.drain(0)


def smalls_scratch(size, w):
    r, n = pack_rows(size), size // 2
    buffers = [
        pltpu.VMEM((1, size, r, w), BF16),
        pltpu.VMEM((1, n, r, w), BF16),
        pltpu.VMEM((1, n, r, w), BF16),
        pltpu.VMEM((1, r, w), BF16),
        pltpu.VMEM((1, size, r, w), BF16),
        pltpu.VMEM((4, SPAN, w), BF16),
    ]
    sems = [
        pltpu.SemaphoreType.DMA((2, 1, n)),
        pltpu.SemaphoreType.DMA((2, 1, n)),
        pltpu.SemaphoreType.DMA((1,)),
        pltpu.SemaphoreType.DMA((1, 3, size)),
        pltpu.SemaphoreType.DMA((1, size)),
        pltpu.SemaphoreType.DMA((3,)),
        pltpu.SemaphoreType.DMA((3,)),
    ]
    return buffers + sems


def forward_body(*refs, size, heads, per, steps, layer):
    refs = list(refs)

    def take(n):
        got = refs[:n]
        del refs[:n]
        return got

    mid = layer > 0
    (res_hbm,) = take(1)
    if mid:
        scaled_hbm, wout_hbm, sq_ref = take(3)
    state_hbm, step_hbm, in_hbm, out_hbm, gain_ref = take(5)
    params = take(6)
    if mid:
        new_hbm, sums_ref = take(2)
    normed_hbm, rnorm_ref, small_hbm, inner_hbm, gate_hbm, wt_hbm, full_hbm, ssd_ref, scaled_ref, sqs_ref, st_ref = take(11)
    if mid:
        scaled_in, wout, part, got, far, other, rows_got, facs, fresh, sends, recvs, rsend, rrecv = take(13)
    res, wstate, wt, slabs, normed, turned, small, inner, gate, ext, exts, state = take(12)
    cp_ref, sp_ref, hp_ref, ind_ref, keep, gsend, grecv, load, sems = take(9)
    assert not refs

    n = CHUNK
    tokens_n, model = res.shape
    width = inner.shape[1]
    top = 2 * width + 2 * STATE
    i = pl.program_id(0)
    line = Line(size)
    square = Square()
    job = Gather(line, lambda j: out_hbm.at[layer] if j == 2 else in_hbm.at[layer, 1 - j], slabs, keep, gsend, grecv)
    outgoing = [(turned, normed_hbm), (small, small_hbm), (inner, inner_hbm), (gate, gate_hbm)]
    outgoing += [(wt, wt_hbm), (slabs.at[2], full_hbm)]
    if mid:
        outgoing.append((fresh, new_hbm))

    def flush(k):
        return pltpu.make_async_copy(*outgoing[k], sems.at[k])


    @pl.when(i == 0)
    def _():
        pairs = [(res_hbm, res), (state_hbm.at[layer], wstate), (step_hbm.at[layer], wt.at[pl.ds(top, LANES), :])]
        if mid:
            pairs = [(scaled_hbm, scaled_in), (wout_hbm, wout)] + pairs
        loads = [pltpu.make_async_copy(src, dst, load.at[k]) for k, (src, dst) in enumerate(pairs)]
        for copy in loads:
            copy.start()
        line.greet(pltpu.get_barrier_semaphore(), square.others() if mid else ())
        job.start(0)
        put_params(cp_ref, sp_ref, hp_ref, ind_ref, layer, params)
        ticks = [functools.partial(job.relay, 0, k) for k in range(1, line.n)]
        ticks.append(functools.partial(job.start, 1))
        ticks += [functools.partial(job.relay, 1, k) for k in range(1, line.n)]
        ticks.append(functools.partial(job.start, 2))

        if mid:
            chunks = model // SLICE
            half = tokens_n // 2
            sums = Total(square, part, got, far, other, sends, recvs)
            copies = [
                remote(sq_ref, rows_got.at[square.me], rsend.at[k], rrecv.at[k], who)
                for k, who in enumerate(square.others())
            ]
            for copy in copies:
                copy.start()
            loads[0].wait()
            loads[1].wait()
            for c in range(chunks):
                value = mm(scaled_in[...], wout[c * SLICE : (c + 1) * SLICE, :], NT).astype(BF16)
                part[2 * c] = value[:half]
                part[2 * c + 1] = value[half:]
                sums.step(0, c)
                if c:
                    sums.step(1, c - 1)
            sums.step(1, chunks - 1)
            rows_got[square.me] = sq_ref[...]
            for copy in copies:
                copy.wait()
            total = (rows_got[0] + rows_got[1]) + (rows_got[2] + rows_got[3])
            sums_ref[...] = total
            factor = lax.rsqrt(total / INNER + EPS)
            for t in range(tokens_n // LANES):
                facs[t * LANES : (t + 1) * LANES, :] = jnp.broadcast_to(factor[t], (LANES, LANES)).T
            loads[2].wait()

            def use(c):
                for h in range(2):
                    where = slice(h * half, (h + 1) * half)
                    for s in range(SLICE // LANES):
                        lanes = slice(c * SLICE + s * LANES, c * SLICE + (s + 1) * LANES)
                        value = part[2 * c + h, :, s * LANES : (s + 1) * LANES].astype(F32)
                        fresh[where, lanes] = res[where, lanes].astype(F32) + facs[where, :] * value

            spread = max(1, -(-len(ticks) // chunks))
            for c in range(chunks):
                for tick in ticks[:spread]:
                    tick()
                ticks = ticks[spread:]
                sums.step(2, c)
                if c:
                    sums.step(3, c - 1)
                    use(c - 1)
            sums.step(3, chunks - 1)
            use(chunks - 1)
            flush(6).start()
        else:
            loads[0].wait()
        loads[-2].wait()
        loads[-1].wait()
        for b in range(2 * STATE // LANES):
            rows = slice(2 * width + b * LANES, 2 * width + (b + 1) * LANES)
            wt[rows, :] = wstate[:, b * LANES : (b + 1) * LANES].T

        def norm(t, _):
            rows = pl.ds(pl.multiple_of(t * TILE, TILE), TILE)
            value = (fresh if mid else res)[rows, :].astype(F32)
            scale = lax.rsqrt(jnp.sum(value * value, axis=1, keepdims=True) / model + EPS)
            low = (value * scale * gain_ref[layer : layer + 1, :]).astype(BF16)
            rnorm_ref[rows, :] = scale
            normed[rows, :] = low
            turned[:, rows] = low.T
            small[rows, : 2 * STATE] = mm(low, wstate[...])
            small[rows, 2 * STATE :] = mm(low, wt[top:, :], NT)
            return 0

        lax.fori_loop(0, tokens_n // TILE, norm, 0)
        flush(0).start()
        flush(1).start()
        for tick in ticks:
            tick()

        def project(j, dst):
            weight = slabs[j].reshape(model, width)

            def tile(t, _):
                rows = pl.ds(pl.multiple_of(t * TILE, TILE), TILE)
                dst[rows, :] = mm(normed[rows, :], weight)
                return 0

            lax.fori_loop(0, tokens_n // TILE, tile, 0)

        for j, dst in ((0, inner), (1, gate)):
            job.arrive(j)
            project(j, dst)
            flush(2 + j).start()

    for k in range(1, line.n):
        @pl.when(i == 1 + (k - 1) * steps // line.n)
        def _(k=k):
            job.relay(2, k)

    @pl.when(i > 0)
    def _():
        at = i - 1
        where = pl.ds(pl.multiple_of(at * n, n), n)

        @pl.when(lax.rem(at, per) == 0)
        def _():
            ext[0:8, :] = jnp.zeros((8, width), F32)
            exts[0:8, :] = jnp.zeros((8, 2 * STATE), F32)
            state[...] = jnp.zeros_like(state)

        rows, cols = iotas(n)
        ind = ind_ref[...]
        ext[8 : 8 + n, :] = inner[where, :]
        pre = conv_pre(ext, cp_ref, n)
        x = pre * sigmoid(pre)
        ext[0:8, :] = ext[n : n + 8, :]
        mini = small[where, :]
        exts[8 : 8 + n, :] = mini[:, : 2 * STATE]
        pres = conv_pre(exts, sp_ref, n)
        bc = (pres * sigmoid(pres)).astype(BF16)
        exts[0:8, :] = exts[n : n + 8, :]
        key, query = bc[:, :STATE], bc[:, STATE:]

        _, step, rate, cs, wide_step, wide_cs, wide_tail = scan_prep(mini, hp_ref, ind, n)
        cs2 = cs * LOG2E
        cs2t = cs2.T
        xs = x * wide_step
        half = lax.rem(lax.broadcasted_iota(jnp.int32, xs.shape, 1), 2 * HEAD) < HEAD
        xs0 = jnp.where(half, xs, 0.0)
        xs1 = (xs - xs0).astype(BF16)
        xs0 = xs0.astype(BF16)
        before = state[...]
        low = before.astype(BF16)
        st_ref[0] = low
        carried = mm(query, low) * wide_cs
        xw = (xs * wide_tail).astype(BF16)
        state[...] = before * wide_cs[n - 1 : n, :] + mm(key, xw, TN)
        scores = jnp.where(rows >= cols, mm(query, key, NT), 0.0)
        for pair in range(heads // 2):
            lanes = slice(pair * 2 * HEAD, (pair + 1) * 2 * HEAD)
            mats = []
            for h in (2 * pair, 2 * pair + 1):
                dec = jnp.exp2(jnp.minimum(cs2[:, h : h + 1] - cs2t[h : h + 1, :], 0.0))
                mats.append((scores * dec).astype(BF16))
            local = mm(
                jnp.concatenate(mats, axis=1),
                jnp.concatenate([xs0[:, lanes], xs1[:, lanes]], axis=0),
            )
            ssd_ref[:, lanes] = local + carried[:, lanes] + cp_ref[6:7, lanes] * x[:, lanes]
        gates = gate[where, :]
        gated = ssd_ref[...] * (gates * sigmoid(gates))
        ones = jnp.ones((8, width), BF16)
        top, rest = split16(gated * gated)
        sqs_ref[0] = (mm(ones, top, NT) + mm(ones, rest, NT))[0:1, :]
        scaled_ref[...] = (gated * cp_ref[5:6, :]).astype(BF16)

        span = model // LANES
        share = -(-2 * span // steps)
        for k in range(share):
            b = at * share + k

            @pl.when(b < 2 * span)
            def _(b=b):
                j, col = b // span, lax.rem(b, span)
                slab_rows = slabs.shape[2]
                weight = slabs.at[j]
                piece = block_of(weight, col, slab_rows)
                wt[pl.ds(pl.multiple_of(j * width, width), width), pl.ds(pl.multiple_of(col * LANES, LANES), LANES)] = piece.T

    @pl.when(i == steps)
    def _():
        flush(4).start()
        job.arrive(2)
        flush(5).start()
        for j in range(3):
            job.drain(j)
        for k in range(len(outgoing)):
            flush(k).wait()


def forward(res, stateproj, steps_w, inproj, outt, gain, params, heads, size, layer, out=None):
    tokens_n, model = res.shape
    _, _, rows, width = inproj.shape
    top = 2 * width + 2 * STATE + LANES
    steps = tokens_n // CHUNK
    mid = out is not None
    hbm = pl.BlockSpec(memory_space=pl.ANY)
    chunks = model // SLICE

    def whole(a):
        return pl.BlockSpec(a.shape, lambda i: (0,) * len(a.shape))

    def row(w):
        return pl.BlockSpec((CHUNK, w), lambda i: (jnp.maximum(i - 1, 0), 0))

    args, in_specs, out_specs, out_shape, scratch = [res], [hbm], [], [], []
    if mid:
        args += list(out)
        in_specs += [hbm, hbm, whole(out[2])]
        out_specs += [hbm, whole(out[2])]
        out_shape += [jax.ShapeDtypeStruct(res.shape, F32), jax.ShapeDtypeStruct(out[2].shape, F32)]
        chunk = pltpu.VMEM((chunks, tokens_n // 2, SLICE), BF16)
        scratch += [
            pltpu.VMEM(out[0].shape, BF16),
            pltpu.VMEM(out[1].shape, BF16),
            pltpu.VMEM((2 * chunks, tokens_n // 2, SLICE), BF16),
            chunk, chunk, chunk,
            pltpu.VMEM((4,) + out[2].shape, F32),
            pltpu.VMEM((tokens_n, LANES), F32),
            pltpu.VMEM(res.shape, F32),
            pltpu.SemaphoreType.DMA((3, chunks)),
            pltpu.SemaphoreType.DMA((3, chunks)),
            pltpu.SemaphoreType.DMA((3,)),
            pltpu.SemaphoreType.DMA((3,)),
        ]
    args += [stateproj, steps_w, inproj, outt, gain, *params]
    in_specs += [hbm, hbm, hbm, hbm, whole(gain)] + [whole(v) for v in params]
    out_specs += [
        hbm, pl.BlockSpec((tokens_n, 1), lambda i: (0, 0)), hbm, hbm, hbm, hbm, hbm,
        row(width), row(width),
        pl.BlockSpec((1, 1, CHUNK), lambda i: (jnp.maximum(i - 1, 0), 0, 0)),
        pl.BlockSpec((1, STATE, width), lambda i: (jnp.maximum(i - 1, 0), 0, 0)),
    ]
    out_shape += [
        jax.ShapeDtypeStruct((model, tokens_n), BF16),
        jax.ShapeDtypeStruct((tokens_n, 1), F32),
        jax.ShapeDtypeStruct((tokens_n, 2 * STATE + LANES), F32),
        jax.ShapeDtypeStruct((tokens_n, width), F32),
        jax.ShapeDtypeStruct((tokens_n, width), F32),
        jax.ShapeDtypeStruct((top, model), BF16),
        jax.ShapeDtypeStruct((size, rows, width), BF16),
        jax.ShapeDtypeStruct((tokens_n, width), F32),
        jax.ShapeDtypeStruct((tokens_n, width), BF16),
        jax.ShapeDtypeStruct((steps, 1, CHUNK), F32),
        jax.ShapeDtypeStruct((steps, STATE, width), BF16),
    ]
    scratch += [
        pltpu.VMEM(res.shape, res.dtype),
        pltpu.VMEM((model, 2 * STATE), BF16),
        pltpu.VMEM((top, model), BF16),
        pltpu.VMEM((3, size, rows, width), BF16),
        pltpu.VMEM((tokens_n, model), BF16),
        pltpu.VMEM((model, tokens_n), BF16),
        pltpu.VMEM((tokens_n, 2 * STATE + LANES), F32),
        pltpu.VMEM((tokens_n, width), F32),
        pltpu.VMEM((tokens_n, width), F32),
        pltpu.VMEM((CHUNK + 8, width), F32),
        pltpu.VMEM((CHUNK + 8, 2 * STATE), F32),
        pltpu.VMEM((STATE, width), F32),
        pltpu.VMEM((8, width), F32),
        pltpu.VMEM((8, 2 * STATE), F32),
        pltpu.VMEM((8, LANES), F32),
        pltpu.VMEM((LANES, width), BF16),
        pltpu.SemaphoreType.DMA((3,)),
        pltpu.SemaphoreType.DMA((3, 3, size)),
        pltpu.SemaphoreType.DMA((3, size)),
        pltpu.SemaphoreType.DMA((5,)),
        pltpu.SemaphoreType.DMA((7,)),
    ]
    return pl.pallas_call(
        functools.partial(forward_body, size=size, heads=heads, per=LEN // CHUNK, steps=steps, layer=layer),
        grid=(steps + 1,),
        in_specs=in_specs,
        out_specs=out_specs,
        out_shape=out_shape,
        scratch_shapes=scratch,
        compiler_params=pltpu.CompilerParams(
            collective_id=min(layer, 1), has_side_effects=True, vmem_limit_bytes=VMEM_LIMIT
        ),
        name="forward",
    )(*args)


def back_body(*refs, heads, per, size, steps, layer, last):
    refs = list(refs)

    def take(n):
        got = refs[:n]
        del refs[:n]
        return got

    up_ref, sq_ref, gate_ref, ssd_ref, inner_ref, iprev_ref, small_ref, sprev_ref, st_ref, res_ref, rn_ref = take(11)
    gain_ref = take(1)[0]
    params = take(6)
    wout_hbm, scaled_hbm, wt_hbm, normed_hbm = take(4)
    if not last:
        next_normed, next_steps, next_sdel, next_dcp, next_dsp, next_dhp, next_dgain = take(7)
    new_ref, grad_hbm = take(2)
    if last:
        sdsum_ref, steplow_ref, dcp_ref, dsp_ref, dhp_ref, dgain_ref, mixed_ref = take(7)
    else:
        pack_ref, full_hbm, wide_hbm = take(3)
    ext, exts, cde, cdes, dstate, rq, cp_ref, sp_ref, hp_ref, ind_ref = take(10)
    wout, scaled, wt, turned, dy, glow, ilow, frow, srow, sgot = take(10)
    part, near, away, tpart, got, far, other = take(7)
    load, rsend, rrecv, ssend, srecv, sends, recvs, gsem = take(8)
    if last:
        fgot, opart, ogot, ofar, oother, fsend, frecv, osends, orecvs = take(9)
    else:
        dcp_ref, dsp_ref, dhp_ref, dgain_ref, step_all, sd_all = take(6)
        buffers = take(6)
        sems = take(7)
    assert not refs

    n = CHUNK
    model = up_ref.shape[1]
    i = pl.program_id(0)
    begin_gate = steps
    begin_scan = begin_gate + steps
    begin_norm = begin_scan + steps
    end = begin_norm + steps - 1
    line = Line(size)
    square = Square()
    rows_own = part.shape[2]
    count = part.shape[0]
    job = Scatter(line, part, lambda j: dy.at[pl.ds(j * rows_own, rows_own), :], near, away, ssend, srecv)
    sums = Total(square, tpart, got, far, other, sends, recvs)
    if last:
        outs = Total(square, opart, ogot, ofar, oother, osends, orecvs)
        half = steps * n // 2
        slices = model // SLICE
    else:
        minis = Smalls(line, square, *buffers, sems)
    moves = [(wout_hbm, wout), (scaled_hbm, scaled), (wt_hbm, wt), (normed_hbm, turned)]
    if not last:
        moves += [(next_normed, turned), (next_steps, step_all), (next_sdel, sd_all)]

    def move(k):
        return pltpu.make_async_copy(*moves[k], load.at[k])

    order = job.order()
    places = len(order)

    def spaced(begin, stop, m):
        return begin + m * (stop - begin) // places

    middle = begin_scan + steps // 2
    folds = [(spaced(begin_scan - steps // 2, middle, m), 0, p) for m, p in enumerate(order)]
    folds += [(spaced(middle, begin_norm, m), 1, p) for m, p in enumerate(order)]

    def column(row):
        return jnp.broadcast_to(row, (n, n)).T[:, 0:1]

    @pl.when(i == 0)
    def _():
        for k in range(len(moves)):
            if k != 3:
                move(k).start()
        put_params(cp_ref, sp_ref, hp_ref, ind_ref, layer, params)
        rq[...] = jnp.zeros_like(rq)
        line.greet_all(pltpu.get_barrier_semaphore(), square.others())
        if last:
            rows = [
                remote(sq_ref, fgot.at[square.me], fsend.at[k], frecv.at[k], who)
                for k, who in enumerate(square.others())
            ]
            for copy in rows:
                copy.start()
            fgot[square.me] = sq_ref[...]
            move(0).wait()
            move(1).wait()
            for c in range(slices):
                value = mm(scaled[...], wout[c * SLICE : (c + 1) * SLICE, :], NT).astype(BF16)
                opart[2 * c] = value[:half]
                opart[2 * c + 1] = value[half:]
                outs.step(0, c)
                if c:
                    outs.step(1, c - 1)
            outs.step(1, slices - 1)
            for copy in rows:
                copy.wait()
            total = (fgot[0] + fgot[1]) + (fgot[2] + fgot[3])
        else:
            total = sq_ref[...]
            move(4).wait()
            move(5).wait()
            move(6).wait()
            put_pack(
                buffers[0].at[0], square.me, turned, step_all, sd_all,
                next_dcp[...], next_dsp[...], next_dhp[...], next_dgain[...],
            )
            minis.sum.start(0)
            move(0).wait()
            move(1).wait()
        dcp_ref[...] = jnp.zeros_like(dcp_ref)
        dsp_ref[...] = jnp.zeros_like(dsp_ref)
        dhp_ref[...] = jnp.zeros_like(dhp_ref)
        dgain_ref[...] = jnp.zeros_like(dgain_ref)
        frow[...] = lax.rsqrt(total / INNER + EPS)

    ind = ind_ref[...]
    for at, j, p in folds:
        @pl.when(i == at)
        def _(j=j, p=p):
            job.fold(j, p)

    if not last:
        for m, p in enumerate(order):
            @pl.when(i == spaced(steps // 4, steps - 2, m))
            def _(p=p):
                minis.sum.fold(0, p)

        @pl.when(i == steps - 2)
        def _():
            minis.turn()

        for k in range(1, line.n):
            @pl.when(i == begin_gate + (k - 1) * (steps // 2) // max(1, line.n - 1))
            def _(k=k):
                minis.spread.relay(0, k)

        @pl.when(i == begin_gate + steps // 2)
        def _():
            minis.cross()

        @pl.when(i == begin_gate + 3 * steps // 4)
        def _():
            minis.cross_on()

    @pl.when(i < begin_gate)
    def _():
        rows = pl.ds(pl.multiple_of(i * n, n), n)
        low = (column(frow[i]) * up_ref[...].astype(F32)).astype(BF16)
        turned[:, rows] = low.T
        sd = mm(low, wout[...])
        dy[rows, :] = sd
        piece = scaled[rows, :]
        top, rest = split16(piece.astype(F32) * sd)
        ones = jnp.ones((8, sd.shape[1]), BF16)
        srow[i] = (mm(ones, top, NT) + mm(ones, rest, NT))[0:1, :]

    @pl.when(i == begin_gate - 1)
    def _():
        copies = [
            remote(srow, sgot.at[square.me], rsend.at[k], rrecv.at[k], who) for k, who in enumerate(square.others())
        ]
        for copy in copies:
            copy.start()
        job.emit(0, turned, scaled)
        move(3).start()
        sgot[square.me] = srow[...]
        for copy in copies:
            copy.wait()
        srow[...] = (sgot[0] + sgot[1]) + (sgot[2] + sgot[3])

    @pl.when((i >= begin_gate) & (i < begin_scan))
    def _():
        c = i - begin_gate
        rows = pl.ds(pl.multiple_of(c * n, n), n)
        coef = column(frow[c] * frow[c] * srow[c]) / INNER
        gate = gate_ref[...]
        gsig = sigmoid(gate)
        gact = gate * gsig
        ssd = ssd_ref[...]
        sd = dy[rows, :]
        gated = ssd * gact
        gd = cp_ref[5:6, :] * sd - coef * gated
        dcp_ref[5:6, :] += colsum(gated * sd)
        dy[rows, :] = gd * gact
        glow[rows, :] = (gd * ssd * (gsig + gact * (1.0 - gsig))).astype(BF16)

    @pl.when(i == begin_scan - 1)
    def _():
        move(3).wait()
        job.emit(1, turned, glow)
        move(2).wait()

    @pl.when((i >= begin_scan) & (i < begin_norm))
    def _():
        q = i - begin_scan
        chunk = steps - 1 - q
        where = pl.ds(pl.multiple_of(chunk * n, n), n)

        @pl.when(lax.rem(chunk, per) == per - 1)
        def _():
            cde[n : n + 8, :] = jnp.zeros((8, cde.shape[1]), F32)
            cdes[n : n + 8, :] = jnp.zeros((8, cdes.shape[1]), F32)
            dstate[...] = jnp.zeros_like(dstate)

        keep = jnp.where(lax.rem(chunk, per) == 0, 0.0, 1.0).astype(F32)
        rows, cols = iotas(n)
        ext[0:8, :] = iprev_ref[...] * keep
        ext[8 : 8 + n, :] = inner_ref[...]
        exts[0:8, :] = sprev_ref[:, : 2 * STATE] * keep
        exts[8 : 8 + n, :] = small_ref[:, : 2 * STATE]
        pre = conv_pre(ext, cp_ref, n)
        sig = sigmoid(pre)
        x = pre * sig
        slope = sig + x * (1.0 - sig)
        pres = conv_pre(exts, sp_ref, n)
        sigs = sigmoid(pres)
        acts = pres * sigs
        slopes = sigs + acts * (1.0 - sigs)
        bc = acts.astype(BF16)
        key, query = bc[:, :STATE], bc[:, STATE:]
        dyc = dy[where, :]

        raw, step, rate, cs, wide_step, wide_cs, wide_tail = scan_prep(small_ref, hp_ref, ind, n)
        cs2 = cs * LOG2E
        cs2t = cs2.T
        xs = x * wide_step
        xsb = xs.astype(BF16)
        half = lax.rem(lax.broadcasted_iota(jnp.int32, xs.shape, 1), 2 * HEAD) < HEAD
        dy0 = jnp.where(half, dyc, 0.0)
        dy1 = (dyc - dy0).astype(BF16)
        dy0 = dy0.astype(BF16)
        low = st_ref[0]
        dst = dstate[...]
        dlow = dst.astype(BF16)
        dye = dyc * wide_cs
        dyeb = dye.astype(BF16)
        up = headsum(dye * mm(query, low), ind)
        dxs_state = wide_tail * mm(key, dlow)
        down = headsum(xs * dxs_state, ind)
        qdel = mm(dyeb, low, NT)
        kdel = mm((xs * wide_tail).astype(BF16), dlow, NT)
        through = headsum(jnp.broadcast_to(colsum(low.astype(F32) * dst), (8, dst.shape[1])), ind)[0:1, :]
        through = through * jnp.exp(cs[n - 1 : n, :])
        dstate[...] = dst * wide_cs[n - 1 : n, :] + mm(query, dyeb, TN)

        scores = jnp.where(rows <= cols, mm(key, query, NT), 0.0)
        dscores = jnp.zeros((n, n), F32)
        colq = jnp.zeros((n, LANES), F32)
        lane = lax.broadcasted_iota(jnp.int32, (n, LANES), 1)
        dxs = []
        for pair in range(heads // 2):
            lanes = slice(pair * 2 * HEAD, (pair + 1) * 2 * HEAD)
            stacked = jnp.concatenate([dy0[:, lanes], dy1[:, lanes]], axis=0)
            both = mm(xsb[:, lanes], stacked, NT)
            mats = []
            for which, h in enumerate((2 * pair, 2 * pair + 1)):
                dec = jnp.exp2(jnp.minimum(cs2t[h : h + 1, :] - cs2[:, h : h + 1], 0.0))
                mats.append((scores * dec).astype(BF16))
                term = dec * both[:, which * n : (which + 1) * n]
                dscores = dscores + term
                quad = scores * term
                rq[h : h + 1, :] = colsum(quad)
                colq = jnp.where(lane == h, jnp.sum(quad, axis=1, keepdims=True), colq)
            dxs.append(mm(jnp.concatenate(mats, axis=1), stacked))
        dxs = jnp.concatenate(dxs, axis=1) + dxs_state
        dscores = jnp.where(rows <= cols, dscores, 0.0).astype(BF16)
        kdel = kdel + mm(dscores, query)
        qdel = qdel + mm(dscores, key, TN)

        upper = jnp.where(rows <= cols, 1.0, 0.0).astype(F32)
        strict = jnp.where(rows > cols, 1.0, 0.0).astype(F32)
        da = mm(upper, rq[...].T - colq + up, precision=HIGH) + mm(strict, down, precision=HIGH) + through
        grown = headsum(x * dxs, ind) + rate * da
        step_pre = grown * sigmoid(raw)
        steplow = step_pre.astype(BF16)
        if last:
            steplow_ref[...] = steplow
        else:
            step_all[where, :] = steplow
        dhp_ref[0:1, :] += colsum(step_pre)
        dhp_ref[1:2, :] += rate * colsum(step * da)
        dcp_ref[6:7, :] += colsum(dyc * x)

        cd = (dxs * wide_step + cp_ref[6:7, :] * dyc) * slope
        cde[0:n, :] = cd
        total = cp_ref[3:4, :] * cd
        for tap in range(3):
            total = total + cp_ref[tap : tap + 1, :] * cde[3 - tap : 3 - tap + n, :]
        inner_low = total.astype(BF16)
        ilow[where, :] = inner_low
        for tap in range(4):
            dcp_ref[tap : tap + 1, :] += colsum(cd * ext[5 + tap : 5 + tap + n, :])
        dcp_ref[4:5, :] += colsum(cd)
        cde[n : n + 8, :] = cde[0:8, :]

        cds = jnp.concatenate([kdel, qdel], axis=1) * slopes
        cdes[0:n, :] = cds
        total = sp_ref[3:4, :] * cds
        for tap in range(3):
            total = total + sp_ref[tap : tap + 1, :] * cdes[3 - tap : 3 - tap + n, :]
        sdel = total.astype(BF16)
        for tap in range(4):
            dsp_ref[tap : tap + 1, :] += colsum(cds * exts[5 + tap : 5 + tap + n, :])
        dsp_ref[4:5, :] += colsum(cds)
        cdes[n : n + 8, :] = cdes[0:8, :]

        lows = jnp.concatenate([inner_low, glow[where, :], sdel, steplow], axis=1)
        value = mm(lows, wt[...]).astype(BF16)
        tpart[2 * q, :, :model] = value[: n // 2]
        tpart[2 * q + 1, :, :model] = value[n // 2 :]
        tpart[2 * q, :, model:] = sdel[: n // 2]
        tpart[2 * q + 1, :, model:] = sdel[n // 2 :]
        sums.step(0, q)

    @pl.when((i > begin_scan) & (i <= begin_norm))
    def _():
        sums.step(1, i - begin_scan - 1)

    @pl.when((i >= begin_scan + 3) & (i < begin_norm + 3))
    def _():
        sums.step(2, i - begin_scan - 3)

    @pl.when((i >= begin_scan + 4) & (i < begin_norm + 4))
    def _():
        sums.step(3, i - begin_scan - 4)

    if last:
        @pl.when((i >= begin_scan) & (i < begin_scan + slices))
        def _():
            outs.step(2, i - begin_scan)

        @pl.when((i > begin_scan) & (i <= begin_scan + slices))
        def _():
            outs.step(3, i - begin_scan - 1)

    @pl.when(i == begin_norm - 1)
    def _():
        dhp_ref[2:3, :] = headsum(jnp.broadcast_to(dcp_ref[6:7, :], (8, dcp_ref.shape[1])), ind)[0:1, :]
        job.emit(2, turned, ilow)

    @pl.when(i >= begin_norm)
    def _():
        r = i - begin_norm
        chunk = steps - 1 - r
        if last:
            fac = column(frow[chunk])
            side = chunk // (steps // 2)
            base = (chunk - side * (steps // 2)) * n
        for h in range(2):
            rows = slice(h * (n // 2), (h + 1) * (n // 2))
            back = tpart[2 * r + h, :, :model].astype(F32)
            sdel = tpart[2 * r + h, :, model:]
            if last:
                sdsum_ref[rows, :] = sdel
            else:
                sd_all[pl.ds(pl.multiple_of(chunk * n + h * (n // 2), n // 2), n // 2), :] = sdel
            res = res_ref[rows, :].astype(F32)
            rn = rn_ref[rows, :]
            dgain_ref[...] += colsum(back * res * rn)
            gained = back * gain_ref[layer : layer + 1, :]
            mean = jnp.sum(gained * res, axis=1, keepdims=True) / model
            new_ref[rows, :] = up_ref[rows, :].astype(F32) + rn * gained - (rn * rn * rn * mean) * res
            if last:
                where = pl.ds(pl.multiple_of(base + h * (n // 2), n // 2), n // 2)
                for c in range(slices):
                    span = slice(c * SLICE, (c + 1) * SLICE)
                    summed = opart[2 * c + side, where, :].astype(F32)
                    mixed_ref[rows, span] = (res[:, span] + fac[rows, :] * summed).astype(BF16)

    @pl.when(i == end)
    def _():
        if not last:
            put_pack(
                pack_ref, square.me, turned, step_all, sd_all, dcp_ref[...], dsp_ref[...], dhp_ref[...], dgain_ref[...]
            )
            minis.end()
            tails = [
                pltpu.make_async_copy(src, dst, load.at[k])
                for k, (src, dst) in enumerate(((minis.full, full_hbm), (minis.wide, wide_hbm)))
            ]
            for copy in tails:
                copy.start()
        for p in order:
            job.fold(2, p)
        for j in range(count):
            job.finish(j)
            pltpu.make_async_copy(dy.at[pl.ds(j * rows_own, rows_own), :], grad_hbm.at[j], gsem.at[j]).start()
        for j in range(count):
            job.drain(j)
            pltpu.make_async_copy(dy.at[pl.ds(j * rows_own, rows_own), :], grad_hbm.at[j], gsem.at[j]).wait()
        if not last:
            for copy in tails:
                copy.wait()


def back(up, sq, gate_pre, ssd, inner_raw, small, states, res, rnorm, gain, params,
         wout, scaled, wt, normed, heads, size, layer, after=None):
    tokens_n, width = inner_raw.shape
    model = up.shape[1]
    last = after is None
    steps = tokens_n // CHUNK
    begin_scan = 2 * steps
    begin_norm = begin_scan + steps
    rows = model // size
    n = size // 2
    hbm = pl.BlockSpec(memory_space=pl.ANY)
    top = steps - 1

    def norm_at(i):
        return jnp.where(i < begin_norm, top, top - (i - begin_norm))

    def scan_at(i):
        return jnp.clip(top - (i - begin_scan), 0, top)

    def first(w):
        return pl.BlockSpec((CHUNK, w), lambda i: (jnp.where(i < steps, i, norm_at(i)), 0))

    def second(w):
        return pl.BlockSpec((CHUNK, w), lambda i: (jnp.clip(i - steps, 0, top), 0))

    def scan(w):
        return pl.BlockSpec((CHUNK, w), lambda i: (scan_at(i), 0))

    def prev(w):
        return pl.BlockSpec((8, w), lambda i: (jnp.maximum(scan_at(i) * (CHUNK // 8) - 1, 0), 0))

    def norm(w):
        return pl.BlockSpec((CHUNK, w), lambda i: (norm_at(i), 0))

    def whole(a):
        return pl.BlockSpec(a.shape, lambda i: (0,) * len(a.shape))

    extra = model + 2 * STATE
    quarter = pltpu.VMEM((steps, CHUNK // 2, extra), BF16)
    pieces = pltpu.VMEM((3, n, rows, width), BF16)
    args = [up, sq, gate_pre, ssd, inner_raw, inner_raw, small, small, states, res, rnorm, gain, *params,
            wout, scaled, wt, normed]
    in_specs = [
        first(model), whole(sq), second(width), second(width),
        scan(width), prev(width), scan(small.shape[1]), prev(small.shape[1]),
        pl.BlockSpec((1, STATE, width), lambda i: (scan_at(i), 0, 0)),
        norm(model), norm(1), whole(gain),
    ] + [whole(a) for a in params] + [hbm] * 4
    out_specs = [norm(model), hbm]
    out_shape = [jax.ShapeDtypeStruct((tokens_n, model), F32), jax.ShapeDtypeStruct((3, rows, width), F32)]
    totals = [(8, width), (8, 2 * STATE), (8, LANES), (1, model)]
    scratch = [
        pltpu.VMEM((CHUNK + 8, width), F32),
        pltpu.VMEM((CHUNK + 8, 2 * STATE), F32),
        pltpu.VMEM((CHUNK + 8, width), F32),
        pltpu.VMEM((CHUNK + 8, 2 * STATE), F32),
        pltpu.VMEM((STATE, width), F32),
        pltpu.VMEM((LANES, CHUNK), F32),
        pltpu.VMEM((8, width), F32),
        pltpu.VMEM((8, 2 * STATE), F32),
        pltpu.VMEM((8, LANES), F32),
        pltpu.VMEM((LANES, width), BF16),
        pltpu.VMEM(wout.shape, BF16),
        pltpu.VMEM(scaled.shape, BF16),
        pltpu.VMEM(wt.shape, BF16),
        pltpu.VMEM(normed.shape, BF16),
        pltpu.VMEM((tokens_n, width), F32),
        pltpu.VMEM((tokens_n, width), BF16),
        pltpu.VMEM((tokens_n, width), BF16),
        pltpu.VMEM((steps, 1, CHUNK), F32),
        pltpu.VMEM((steps, 1, CHUNK), F32),
        pltpu.VMEM((4, steps, 1, CHUNK), F32),
        pltpu.VMEM((3, size, rows, width), BF16), pieces, pieces,
        pltpu.VMEM((2 * steps, CHUNK // 2, extra), BF16), quarter, quarter, quarter,
        pltpu.SemaphoreType.DMA((7,)),
        pltpu.SemaphoreType.DMA((3,)),
        pltpu.SemaphoreType.DMA((3,)),
        pltpu.SemaphoreType.DMA((2, 3, n)),
        pltpu.SemaphoreType.DMA((2, 3, n)),
        pltpu.SemaphoreType.DMA((3, steps)),
        pltpu.SemaphoreType.DMA((3, steps)),
        pltpu.SemaphoreType.DMA((3,)),
    ]
    if last:
        out_specs += [norm(2 * STATE), scan(LANES)]
        out_specs += [pl.BlockSpec(v, lambda i: (0, 0)) for v in totals] + [norm(model)]
        out_shape += [
            jax.ShapeDtypeStruct((tokens_n, 2 * STATE), BF16),
            jax.ShapeDtypeStruct((tokens_n, LANES), BF16),
        ]
        out_shape += [jax.ShapeDtypeStruct(v, F32) for v in totals]
        out_shape.append(jax.ShapeDtypeStruct((tokens_n, model), BF16))
        slices = model // SLICE
        chunk = pltpu.VMEM((slices, tokens_n // 2, SLICE), BF16)
        scratch += [
            pltpu.VMEM((4, steps, 1, CHUNK), F32),
            pltpu.VMEM((2 * slices, tokens_n // 2, SLICE), BF16), chunk, chunk, chunk,
            pltpu.SemaphoreType.DMA((3,)),
            pltpu.SemaphoreType.DMA((3,)),
            pltpu.SemaphoreType.DMA((3, slices)),
            pltpu.SemaphoreType.DMA((3, slices)),
        ]
    else:
        w = 2 * STATE
        r = pack_rows(size)
        args += list(after)
        in_specs += [hbm] * 3 + [whole(v) for v in after[3:]]
        out_specs += [pl.BlockSpec((size, r, w), lambda i: (0, 0, 0)), hbm, hbm]
        out_shape += [
            jax.ShapeDtypeStruct((size, r, w), BF16),
            jax.ShapeDtypeStruct((1, size, r, w), BF16),
            jax.ShapeDtypeStruct((4, SPAN, w), BF16),
        ]
        scratch += [pltpu.VMEM(v, F32) for v in totals]
        scratch += [pltpu.VMEM((tokens_n, LANES), BF16), pltpu.VMEM((tokens_n, w), BF16)]
        scratch += smalls_scratch(size, w)
    return pl.pallas_call(
        functools.partial(
            back_body, heads=heads, per=LEN // CHUNK, size=size, steps=steps, layer=layer, last=last
        ),
        grid=(begin_norm + steps,),
        in_specs=in_specs,
        out_specs=out_specs,
        out_shape=out_shape,
        scratch_shapes=scratch,
        compiler_params=pltpu.CompilerParams(
            collective_id=2 if last else 3, has_side_effects=True, vmem_limit_bytes=VMEM_LIMIT
        ),
        name="back",
    )(*args)


def final_body(*refs, size, layers, heads):
    refs = list(refs)

    def take(n):
        got = refs[:n]
        del refs[:n]
        return got

    (pack_hbm,) = take(1)
    earlier = [take(2) for _ in range(layers - 1)]
    pieces = take(layers)
    pair_hbm, out_hbm, step_ref, state_ref, conv_ref, bias_ref, convs_ref, biass_ref = take(8)
    stepbias_ref, decay_ref, skip_ref, norm_ref, gain_ref = take(5)
    buffers = take(6)
    sems = take(7)
    load, moved = take(2)
    assert not refs
    line = Line(size)
    square = Square()
    minis = Smalls(line, square, *buffers, sems)
    copy = pltpu.make_async_copy(pack_hbm, buffers[0].at[0], load)
    copy.start()
    moves = []
    for layer in range(layers):
        for src, dst in (
            (pieces[layer].at[pl.ds(1, 2)], pair_hbm.at[layer]), (pieces[layer].at[0], out_hbm.at[layer])
        ):
            moves.append(pltpu.make_async_copy(src, dst, moved.at[len(moves)]))
            moves[-1].start()
    line.greet_all(pltpu.get_barrier_semaphore(), (square.mate, square.across))
    copy.wait()
    minis.sum.start(0)
    model = state_ref.shape[1]
    quarter = model // 4
    w = state_ref.shape[2]
    width = conv_ref.shape[2]

    def unpack(layer, full, wide):
        for t in range(4):
            state_ref[layer, t * quarter : (t + 1) * quarter, :] = wide[t, :quarter, :].astype(F32)
        taps = [wide[t, quarter : quarter + 16, :].astype(F32) for t in range(4)]
        taps = (taps[0] + taps[1]) + (taps[2] + taps[3])
        convs_ref[layer] = taps[0:4]
        biass_ref[layer : layer + 1, :] = taps[4:5]
        flat = full[...].reshape(-1, w)[:PACK].astype(F32)
        at = quarter + 16
        for b in range(model // w):
            step_ref[layer, :, b * w : (b + 1) * w] = flat[at : at + 16]
            at += 16
        for b in range(width // w):
            lanes = slice(b * w, (b + 1) * w)
            rows = flat[at + 8 * b : at + 8 * b + 8]
            conv_ref[layer, :, lanes] = rows[0:4]
            bias_ref[layer : layer + 1, lanes] = rows[4:5]
            norm_ref[layer : layer + 1, lanes] = rows[5:6]
        at += 8 * (width // w)
        for k, ref in enumerate((stepbias_ref, decay_ref, skip_ref)):
            ref[layer : layer + 1, :] = flat[at + k : at + k + 1, :heads]
        at += 8
        for b in range(model // w):
            gain_ref[layer : layer + 1, b * w : (b + 1) * w] = flat[at + b : at + b + 1]

    for layer, (full, wide) in enumerate(earlier):
        unpack(layer + 1, full.at[0], wide)
    for p in minis.sum.order():
        minis.sum.fold(0, p)
    minis.turn()
    for k in range(1, line.n):
        minis.spread.relay(0, k)
    minis.cross()
    minis.cross_on()
    minis.end()
    unpack(0, minis.full.at[0], minis.wide)
    for copy in moves:
        copy.wait()


def final(pack, earlier, pieces, heads):
    size, r, w = pack.shape
    layers = len(pieces)
    _, rows, width = pieces[0].shape
    model = rows * size
    vm = pl.BlockSpec(memory_space=pltpu.VMEM)
    hbm = pl.BlockSpec(memory_space=pl.ANY)
    shapes = [
        (layers, 2, rows, width), (layers, rows, width), (layers, 16, model), (layers, model, w), (layers, 4, width),
        (layers, width), (layers, 4, w), (layers, w), (layers, heads), (layers, heads), (layers, heads),
        (layers, width), (layers, model),
    ]
    flat = [v for both in earlier for v in both]
    return pl.pallas_call(
        functools.partial(final_body, size=size, layers=layers, heads=heads),
        in_specs=[hbm] + [vm] * len(flat) + [hbm] * layers,
        out_specs=[hbm, hbm] + [vm] * (len(shapes) - 2),
        out_shape=[jax.ShapeDtypeStruct(v, F32) for v in shapes],
        scratch_shapes=smalls_scratch(size, w) + [
            pltpu.SemaphoreType.DMA,
            pltpu.SemaphoreType.DMA((2 * layers,)),
        ],
        compiler_params=pltpu.CompilerParams(
            collective_id=4, has_side_effects=True, vmem_limit_bytes=VMEM_LIMIT
        ),
        name="final",
    )(pack, *flat, *pieces)


def shards(
    tokens, inproj, stepproj, stateproj, outproj, convinner, biasinner, convstate, biasstate,
    stepbias, decaylog, skipgain, normgain, inputgain, cotangent,
):
    layers = inproj.shape[0]
    width = inproj.shape[3]
    heads = stepproj.shape[2]
    model = tokens.shape[1]
    pad = LANES - heads
    size = lax.axis_size("dp")
    steps_w = jnp.pad(jnp.swapaxes(stepproj, 1, 2), ((0, 0), (0, pad), (0, 0)))
    head = jnp.pad(jnp.stack([stepbias, decaylog, skipgain], axis=1), ((0, 0), (0, 5), (0, pad)))
    outt = jnp.swapaxes(outproj, 1, 2)
    params = (convinner, biasinner, normgain, convstate, biasstate, head)

    residual = tokens
    kept = []
    out = None
    for at in range(layers):
        results = forward(residual, stateproj, steps_w, inproj, outt, inputgain, params, heads, size, at, out=out)
        if at:
            residual, kept[-1][-1] = results[:2]
            results = results[2:]
        normed, rnorm, small, inner_raw, gate_pre, wt, w_out, ssd, scaled, sq, states = results
        w_out = w_out.reshape(model, width)
        kept.append([residual, normed, rnorm, small, inner_raw, gate_pre, wt, w_out, ssd, scaled, states, sq])
        out = (scaled, w_out, sq)

    upstream = cotangent
    after = None
    pieces = [None] * layers
    earlier = []
    for at in reversed(range(layers)):
        before, normed, rnorm, small, inner_raw, gate_pre, wt, w_out, ssd, scaled, states, sq = kept[at]
        upstream, pieces[at], *rest = back(
            upstream, sq, gate_pre, ssd, inner_raw, small, states, before, rnorm, inputgain, params,
            w_out, scaled, wt, normed, heads, size, at, after=after,
        )
        if after is None:
            sdel, steplow, *totals, mixed = rest
            after = (normed, steplow, sdel, *totals)
        else:
            pack, *found = rest
            earlier.append(found)
    (
        inproj_grad, out_grad, step_grad, state_grad, conv_grad, bias_grad, convs_grad, biass_grad,
        stepbias_grad, decay_grad, skip_grad, norm_grad, gain_grad,
    ) = final(pack, earlier, pieces, heads)
    return (
        mixed,
        upstream,
        inproj_grad,
        jnp.swapaxes(step_grad[:, :heads], 1, 2),
        state_grad,
        jnp.swapaxes(out_grad, 1, 2),
        conv_grad,
        bias_grad,
        convs_grad,
        biass_grad,
        stepbias_grad,
        decay_grad,
        skip_grad,
        norm_grad,
        gain_grad,
    )


def solution(mesh):
    in_specs = (
        P("dp", None),
        P(None, None, "dp", "tensor"),
        P(None, None, "tensor"),
        P(),
        P(None, "tensor", "dp"),
        P(None, None, "tensor"),
        P(None, "tensor"),
        P(),
        P(),
        P(None, "tensor"),
        P(None, "tensor"),
        P(None, "tensor"),
        P(None, "tensor"),
        P(),
        P("dp", None),
    )
    out_specs = (
        P("dp", None),
        P("dp", None),
        P(None, None, "dp", "tensor"),
        P(None, None, "tensor"),
        P(),
        P(None, "tensor", "dp"),
        P(None, None, "tensor"),
        P(None, "tensor"),
        P(),
        P(),
        P(None, "tensor"),
        P(None, "tensor"),
        P(None, "tensor"),
        P(None, "tensor"),
        P(),
    )
    return jax.shard_map(shards, mesh=mesh, in_specs=in_specs, out_specs=out_specs, check_vma=False)
```

```python
import functools
import math

import jax
import jax.numpy as jnp
from jax import lax
from jax.experimental import pallas as pl
from jax.experimental.pallas import tpu as pltpu
from jax.sharding import PartitionSpec as P

STATE = 128
LEN = 1024
INNER = 3072
HEAD = 64
CHUNK = 128
SLICE = 256
TILE = 256
PACK = 544
SPAN = 400
VMEM_LIMIT = 65000 * 1024
LANES = 128
EPS = 1e-05
LOG2E = 1.4426950408889634

HIGH = lax.Precision.HIGHEST
NN = (((1,), (0,)), ((), ()))
NT = (((1,), (1,)), ((), ()))
TN = (((0,), (0,)), ((), ()))
F32 = jnp.float32
BF16 = jnp.bfloat16
MESH = pl.DeviceIdType.MESH


def remote(src, dst, send, recv, where):
    return pltpu.make_async_remote_copy(
        src_ref=src, dst_ref=dst, send_sem=send, recv_sem=recv, device_id=where, device_id_type=MESH
    )


class Line:
    def __init__(self, size):
        self.n = size // 2
        me = lax.axis_index("dp")
        self.me = me
        self.at = me // 2
        self.side = lax.rem(me, 2)
        self.pair = {"dp": me + 1 - 2 * self.side}
        self.right = {"dp": jnp.minimum(me + 2, size - 1)}
        self.left = {"dp": jnp.maximum(me - 2, 0)}
        self.has_left = self.at > 0
        self.has_right = self.at < self.n - 1

    def greet(self, barrier, more=()):
        for who in more:
            pl.semaphore_signal(barrier, inc=1, device_id=who, device_id_type=MESH)
        pl.semaphore_signal(barrier, inc=1, device_id=self.pair, device_id_type=MESH)

        @pl.when(self.has_left)
        def _():
            pl.semaphore_signal(barrier, inc=1, device_id=self.left, device_id_type=MESH)

        @pl.when(self.has_right)
        def _():
            pl.semaphore_signal(barrier, inc=1, device_id=self.right, device_id_type=MESH)

        peers = 1 + len(more) + self.has_left.astype(jnp.int32) + self.has_right.astype(jnp.int32)
        pl.semaphore_wait(barrier, peers)

    def greet_all(self, barrier, more=()):
        for who in list(more) + [self.pair]:
            pl.semaphore_signal(barrier, inc=1, device_id=who, device_id_type=MESH)
        for i in range(self.n):
            @pl.when(i != self.at)
            def _(i=i):
                pl.semaphore_signal(barrier, inc=1, device_id={"dp": 2 * i + self.side}, device_id_type=MESH)
        pl.semaphore_wait(barrier, self.n + len(more))


class Gather:
    def __init__(self, line, own, full, keep, send, recv):
        self.line, self.own, self.full, self.keep, self.send, self.recv = line, own, full, keep, send, recv

    def copy(self, j, slab, way, src=None):
        where = (self.line.right, self.line.left, self.line.pair)[way]
        src = self.full.at[j, slab] if src is None else src
        return remote(src, self.full.at[j, slab], self.send.at[j, way, slab], self.recv.at[j, slab], where)

    def start(self, j):
        line = self.line
        pltpu.make_async_copy(self.own(j), self.full.at[j, line.me], self.keep.at[j]).start()

        @pl.when(line.has_right)
        def _():
            self.copy(j, line.me, 0, self.own(j)).start()

        @pl.when(line.has_left)
        def _():
            self.copy(j, line.me, 1, self.own(j)).start()

        self.copy(j, line.me, 2, self.own(j)).start()

    def relay(self, j, k):
        line = self.line

        @pl.when(line.at >= k)
        def _():
            slab = line.me - 2 * k
            self.copy(j, slab, 0).wait_recv()

            @pl.when(line.has_right)
            def _():
                self.copy(j, slab, 0).start()

            self.copy(j, slab, 2).start()

        @pl.when(line.at + k < line.n)
        def _():
            slab = line.me + 2 * k
            self.copy(j, slab, 1).wait_recv()

            @pl.when(line.has_left)
            def _():
                self.copy(j, slab, 1).start()

            self.copy(j, slab, 2).start()

    def arrive(self, j):
        line = self.line
        pltpu.make_async_copy(self.own(j), self.full.at[j, line.me], self.keep.at[j]).wait()
        for place in range(line.n):
            self.copy(j, 2 * place + 1 - line.side, 2).wait_recv()

    def drain(self, j):
        line = self.line
        for place in range(line.n):
            slab = 2 * place + line.side
            self.copy(j, slab, 2).wait_send()

            @pl.when(line.has_right & (place <= line.at))
            def _():
                self.copy(j, slab, 0).wait_send()

            @pl.when(line.has_left & (place >= line.at))
            def _():
                self.copy(j, slab, 1).wait_send()


class Square:
    def __init__(self):
        me = lax.axis_index("tensor")
        self.me = me
        self.half = lax.rem(me, 2)
        self.mate = {"tensor": me + 1 - 2 * self.half}
        self.across = {"tensor": lax.rem(me + 2, 4)}

    def others(self):
        return [{"tensor": lax.rem(self.me + k, 4)} for k in (1, 2, 3)]


class Total:
    def __init__(self, square, part, got, far, other, send, recv):
        self.square, self.part, self.got, self.far, self.other = square, part, got, far, other
        self.send, self.recv = send, recv

    def first(self, c):
        sq = self.square
        return remote(
            self.part.at[2 * c + 1 - sq.half], self.got.at[c], self.send.at[0, c], self.recv.at[0, c], sq.mate
        )

    def second(self, c):
        sq = self.square
        return remote(self.part.at[2 * c + sq.half], self.far.at[c], self.send.at[1, c], self.recv.at[1, c], sq.across)

    def third(self, c):
        sq = self.square
        return remote(self.part.at[2 * c + sq.half], self.other.at[c], self.send.at[2, c], self.recv.at[2, c], sq.mate)

    def step(self, kind, c):
        slot = 2 * c + self.square.half
        if kind == 0:
            self.first(c).start()
        elif kind == 1:
            self.first(c).wait_recv()
            self.part[slot] = (self.part[slot].astype(F32) + self.got[c].astype(F32)).astype(BF16)
            self.second(c).start()
        elif kind == 2:
            self.second(c).wait()
            self.part[slot] = (self.part[slot].astype(F32) + self.far[c].astype(F32)).astype(BF16)
            self.third(c).start()
        else:
            self.third(c).wait_recv()
            self.first(c).wait_send()
            self.third(c).wait_send()
            self.part[2 * c + 1 - self.square.half] = self.other[c]


class Scatter:
    def __init__(self, line, part, out, near, far, send, recv):
        self.line, self.part, self.out, self.near, self.far = line, part, out, near, far
        self.send, self.recv = send, recv

    def order(self):
        n = self.line.n
        seq = []
        for i in range((n + 1) // 2):
            seq.append(i)
            if n - 1 - i != i:
                seq.append(n - 1 - i)
        return seq

    def cross(self, j, i):
        line = self.line
        return remote(
            self.part.at[j, 2 * i + 1 - line.side], self.near.at[j, i], self.send.at[0, j, i], self.recv.at[0, j, i], line.pair
        )

    def straight(self, j, i, source):
        line = self.line
        return remote(
            self.part.at[j, 2 * i + line.side], self.far.at[j, source], self.send.at[1, j, i], self.recv.at[1, j, source],
            {"dp": 2 * i + line.side},
        )

    def start(self, j):
        for i in self.order():
            self.cross(j, i).start()

    def emit(self, j, turned, right):
        rows = self.part.shape[2]
        for i in self.order():
            value = mm(turned[2 * i * rows : 2 * (i + 1) * rows, :], right[...]).astype(BF16)
            self.part[j, 2 * i] = value[:rows]
            self.part[j, 2 * i + 1] = value[rows:]
            self.cross(j, i).start()

    def fold(self, j, i):
        line = self.line
        self.cross(j, i).wait_recv()
        slot = 2 * i + line.side
        self.part[j, slot] = (self.part[j, slot].astype(F32) + self.near[j, i].astype(F32)).astype(BF16)

        @pl.when(i != line.at)
        def _():
            self.straight(j, i, line.at).start()

    def finish(self, j):
        line = self.line
        out = self.out(j)
        out[...] = self.part[j, line.me].astype(out.dtype)
        for i in range(line.n):
            @pl.when(i != line.at)
            def _(i=i):
                self.straight(j, i, i).wait_recv()
                out[...] += self.far[j, i].astype(out.dtype)

    def drain(self, j):
        for i in range(self.line.n):
            self.cross(j, i).wait_send()

            @pl.when(i != self.line.at)
            def _(i=i):
                self.straight(j, i, self.line.at).wait_send()


def mm(left, right, dims=NN, precision=None):
    return lax.dot_general(left, right, dims, precision=precision, preferred_element_type=F32)


def sigmoid(v):
    return 0.5 * jnp.tanh(0.5 * v) + 0.5


def softplus(v):
    return jnp.maximum(v, 0.0) + jnp.log1p(jnp.exp(-jnp.abs(v)))


def split16(v):
    top = v.astype(BF16)
    return top, (v - top.astype(F32)).astype(BF16)


def expand(v, ind):
    top, rest = split16(v)
    return mm(top, ind) + mm(rest, ind)


def headsum(v, ind):
    top, rest = split16(v)
    return mm(top, ind, NT) + mm(rest, ind, NT)


def iotas(n):
    return (
        lax.broadcasted_iota(jnp.int32, (n, n), 0),
        lax.broadcasted_iota(jnp.int32, (n, n), 1),
    )


def colsum(v):
    return jnp.sum(v, axis=0, keepdims=True)


def conv_pre(ext, par, n):
    total = par[4:5, :] + par[0:1, :] * ext[5 : 5 + n, :]
    for tap in range(1, 4):
        total = total + par[tap : tap + 1, :] * ext[5 + tap : 5 + tap + n, :]
    return total


def scan_prep(small, hp, ind, n):
    rows, cols = iotas(n)
    raw = small[:, 2 * STATE :] + hp[0:1, :]
    step = softplus(raw)
    rate = -jnp.exp(hp[1:2, :])
    lower = jnp.where(rows >= cols, 1.0, 0.0).astype(F32)
    cs = mm(lower, step * rate, precision=HIGH)
    tail = jnp.exp(cs[n - 1 : n, :] - cs)
    wide = expand(jnp.concatenate([step, jnp.exp(cs), tail], axis=0), ind)
    return raw, step, rate, cs, wide[0:n], wide[n : 2 * n], wide[2 * n : 3 * n]


def block_of(slabs, at, rows):
    step = math.gcd(LANES, rows)
    pieces = []
    for k in range(LANES // step):
        row = at * LANES + k * step
        slab = row // rows
        pieces.append(slabs[slab, pl.ds(pl.multiple_of(row - slab * rows, step), step), :])
    return pieces[0] if len(pieces) == 1 else jnp.concatenate(pieces, axis=0)


def put_params(cp, sp, hp, ind, layer, params):
    conv, bias, norm, convs, biass, head = params
    width = cp.shape[1]
    row = lax.broadcasted_iota(jnp.int32, (LANES, width), 0)
    lane = lax.broadcasted_iota(jnp.int32, (LANES, width), 1)
    ind[...] = jnp.where(lane // HEAD == row, 1.0, 0.0).astype(BF16)
    hp[...] = head[layer]
    cp[0:4, :] = conv[layer]
    cp[4:5, :] = bias[layer : layer + 1, :]
    cp[5:6, :] = norm[layer : layer + 1, :]
    cp[6:8, :] = expand(hp[...], ind[...])[2:4, :]
    sp[0:4, :] = convs[layer]
    sp[4:5, :] = biass[layer : layer + 1, :]


def place_rows(dst, at, value):
    r = dst.shape[1]
    for g in range(0, value.shape[0], 16):
        dst[(at + g) // r, (at + g) % r : (at + g) % r + 16, :] = value[g : g + 16].astype(dst.dtype)


def pack_rows(size):
    return -(-PACK // (16 * size)) * 16


def put_pack(dst, me, turned, steps_low, sdel, dcp, dsp, dhp, dgain):
    model = turned.shape[0]
    quarter = model // 4
    w = sdel.shape[1]

    def empty(n):
        return jnp.zeros((n, w), F32)

    place_rows(dst, 0, mm(turned[pl.ds(pl.multiple_of(me * quarter, quarter), quarter), :], sdel[...]))
    place_rows(dst, quarter, jnp.concatenate([dsp, empty(8)], axis=0))
    grown = mm(turned[...], steps_low[...]).T[:16]
    at = quarter + 16
    for b in range(model // w):
        place_rows(dst, at, grown[:, b * w : (b + 1) * w])
        at += 16
    place_rows(dst, at, jnp.concatenate([dcp[:, :w], dcp[:, w : 2 * w]], axis=0))
    place_rows(dst, at + 16, jnp.concatenate([dcp[:, 2 * w :], jnp.concatenate([dhp, dhp], axis=1)], axis=0))
    rows = [dgain[:, b * w : (b + 1) * w] for b in range(model // w)]
    place_rows(dst, at + 32, jnp.concatenate(rows + [empty(16 - len(rows))], axis=0))
    assert at + 48 == PACK


class Smalls:
    def __init__(self, line, square, pack, near, away, own, full, wide, sems):
        send, recv, keep, gsend, grecv, self.xsend, self.xrecv = sems
        self.square, self.full, self.wide = square, full, wide
        self.sum = Scatter(line, pack, lambda j: own.at[j], near, away, send, recv)
        self.spread = Gather(line, lambda j: own.at[0], full, keep, gsend, grecv)

    def swap(self, k):
        sq = self.square
        slot = (sq.me, sq.me, lax.rem(sq.me + 2, 4))[k]
        who = (sq.across, sq.mate, sq.mate)[k]
        return remote(self.wide.at[slot], self.wide.at[slot], self.xsend.at[k], self.xrecv.at[k], who)

    def turn(self):
        self.sum.finish(0)
        self.spread.start(0)

    def cross(self):
        self.spread.arrive(0)
        flat = self.full[0].reshape(-1, self.full.shape[3])
        self.wide[self.square.me] = flat[: self.wide.shape[1]]
        self.swap(0).start()
        self.swap(1).start()

    def cross_on(self):
        self.swap(0).wait_recv()
        self.swap(2).start()

    def end(self):
        self.swap(1).wait_recv()
        self.swap(2).wait_recv()
        for k in range(3):
            self.swap(k).wait_send()
        self.sum.drain(0)
        self.spread.drain(0)


def smalls_scratch(size, w):
    r, n = pack_rows(size), size // 2
    buffers = [
        pltpu.VMEM((1, size, r, w), BF16),
        pltpu.VMEM((1, n, r, w), BF16),
        pltpu.VMEM((1, n, r, w), BF16),
        pltpu.VMEM((1, r, w), BF16),
        pltpu.VMEM((1, size, r, w), BF16),
        pltpu.VMEM((4, SPAN, w), BF16),
    ]
    sems = [
        pltpu.SemaphoreType.DMA((2, 1, n)),
        pltpu.SemaphoreType.DMA((2, 1, n)),
        pltpu.SemaphoreType.DMA((1,)),
        pltpu.SemaphoreType.DMA((1, 3, size)),
        pltpu.SemaphoreType.DMA((1, size)),
        pltpu.SemaphoreType.DMA((3,)),
        pltpu.SemaphoreType.DMA((3,)),
    ]
    return buffers + sems


def forward_body(*refs, size, heads, per, steps, layer):
    refs = list(refs)

    def take(n):
        got = refs[:n]
        del refs[:n]
        return got

    mid = layer > 0
    (res_hbm,) = take(1)
    if mid:
        scaled_hbm, wout_hbm, sq_ref = take(3)
    state_hbm, step_hbm, in_hbm, out_hbm, gain_ref = take(5)
    params = take(6)
    if mid:
        new_hbm, sums_ref = take(2)
    normed_hbm, rnorm_ref, small_hbm, inner_hbm, gate_hbm, wt_hbm, full_hbm, ssd_ref, scaled_ref, sqs_ref, st_ref = take(11)
    if mid:
        scaled_in, wout, part, got, far, other, rows_got, facs, fresh, sends, recvs, rsend, rrecv = take(13)
    res, wstate, wt, slabs, normed, turned, small, inner, gate, ext, exts, state = take(12)
    cp_ref, sp_ref, hp_ref, ind_ref, keep, gsend, grecv, load, sems = take(9)
    assert not refs

    n = CHUNK
    tokens_n, model = res.shape
    width = inner.shape[1]
    top = 2 * width + 2 * STATE
    i = pl.program_id(0)
    line = Line(size)
    square = Square()
    job = Gather(line, lambda j: out_hbm.at[layer] if j == 2 else in_hbm.at[layer, 1 - j], slabs, keep, gsend, grecv)
    outgoing = [(turned, normed_hbm), (small, small_hbm), (inner, inner_hbm), (gate, gate_hbm)]
    outgoing += [(wt, wt_hbm), (slabs.at[2], full_hbm)]
    if mid:
        outgoing.append((fresh, new_hbm))

    def flush(k):
        return pltpu.make_async_copy(*outgoing[k], sems.at[k])


    @pl.when(i == 0)
    def _():
        pairs = [(res_hbm, res), (state_hbm.at[layer], wstate), (step_hbm.at[layer], wt.at[pl.ds(top, LANES), :])]
        if mid:
            pairs = [(scaled_hbm, scaled_in), (wout_hbm, wout)] + pairs
        loads = [pltpu.make_async_copy(src, dst, load.at[k]) for k, (src, dst) in enumerate(pairs)]
        for copy in loads:
            copy.start()
        line.greet(pltpu.get_barrier_semaphore(), square.others() if mid else ())
        job.start(0)
        put_params(cp_ref, sp_ref, hp_ref, ind_ref, layer, params)
        ticks = [functools.partial(job.relay, 0, k) for k in range(1, line.n)]
        ticks.append(functools.partial(job.start, 1))
        ticks += [functools.partial(job.relay, 1, k) for k in range(1, line.n)]
        ticks.append(functools.partial(job.start, 2))

        if mid:
            chunks = model // SLICE
            half = tokens_n // 2
            sums = Total(square, part, got, far, other, sends, recvs)
            copies = [
                remote(sq_ref, rows_got.at[square.me], rsend.at[k], rrecv.at[k], who)
                for k, who in enumerate(square.others())
            ]
            for copy in copies:
                copy.start()
            loads[0].wait()
            loads[1].wait()
            for c in range(chunks):
                value = mm(scaled_in[...], wout[c * SLICE : (c + 1) * SLICE, :], NT).astype(BF16)
                part[2 * c] = value[:half]
                part[2 * c + 1] = value[half:]
                sums.step(0, c)
                if c:
                    sums.step(1, c - 1)
            sums.step(1, chunks - 1)
            rows_got[square.me] = sq_ref[...]
            for copy in copies:
                copy.wait()
            total = (rows_got[0] + rows_got[1]) + (rows_got[2] + rows_got[3])
            sums_ref[...] = total
            factor = lax.rsqrt(total / INNER + EPS)
            for t in range(tokens_n // LANES):
                facs[t * LANES : (t + 1) * LANES, :] = jnp.broadcast_to(factor[t], (LANES, LANES)).T
            loads[2].wait()

            def use(c):
                for h in range(2):
                    where = slice(h * half, (h + 1) * half)
                    for s in range(SLICE // LANES):
                        lanes = slice(c * SLICE + s * LANES, c * SLICE + (s + 1) * LANES)
                        value = part[2 * c + h, :, s * LANES : (s + 1) * LANES].astype(F32)
                        fresh[where, lanes] = res[where, lanes].astype(F32) + facs[where, :] * value

            spread = max(1, -(-len(ticks) // chunks))
            for c in range(chunks):
                for tick in ticks[:spread]:
                    tick()
                ticks = ticks[spread:]
                sums.step(2, c)
                if c:
                    sums.step(3, c - 1)
                    use(c - 1)
            sums.step(3, chunks - 1)
            use(chunks - 1)
            flush(6).start()
        else:
            loads[0].wait()
        loads[-2].wait()
        loads[-1].wait()
        for b in range(2 * STATE // LANES):
            rows = slice(2 * width + b * LANES, 2 * width + (b + 1) * LANES)
            wt[rows, :] = wstate[:, b * LANES : (b + 1) * LANES].T

        def norm(t, _):
            rows = pl.ds(pl.multiple_of(t * TILE, TILE), TILE)
            value = (fresh if mid else res)[rows, :].astype(F32)
            scale = lax.rsqrt(jnp.sum(value * value, axis=1, keepdims=True) / model + EPS)
            low = (value * scale * gain_ref[layer : layer + 1, :]).astype(BF16)
            rnorm_ref[rows, :] = scale
            normed[rows, :] = low
            turned[:, rows] = low.T
            small[rows, : 2 * STATE] = mm(low, wstate[...])
            small[rows, 2 * STATE :] = mm(low, wt[top:, :], NT)
            return 0

        lax.fori_loop(0, tokens_n // TILE, norm, 0)
        flush(0).start()
        flush(1).start()
        for tick in ticks:
            tick()

        def project(j, dst):
            weight = slabs[j].reshape(model, width)

            def tile(t, _):
                rows = pl.ds(pl.multiple_of(t * TILE, TILE), TILE)
                dst[rows, :] = mm(normed[rows, :], weight)
                return 0

            lax.fori_loop(0, tokens_n // TILE, tile, 0)

        for j, dst in ((0, inner), (1, gate)):
            job.arrive(j)
            project(j, dst)
            flush(2 + j).start()

    for k in range(1, line.n):
        @pl.when(i == 1 + (k - 1) * steps // line.n)
        def _(k=k):
            job.relay(2, k)

    @pl.when(i > 0)
    def _():
        at = i - 1
        where = pl.ds(pl.multiple_of(at * n, n), n)

        @pl.when(lax.rem(at, per) == 0)
        def _():
            ext[0:8, :] = jnp.zeros((8, width), F32)
            exts[0:8, :] = jnp.zeros((8, 2 * STATE), F32)
            state[...] = jnp.zeros_like(state)

        rows, cols = iotas(n)
        ind = ind_ref[...]
        ext[8 : 8 + n, :] = inner[where, :]
        pre = conv_pre(ext, cp_ref, n)
        x = pre * sigmoid(pre)
        ext[0:8, :] = ext[n : n + 8, :]
        mini = small[where, :]
        exts[8 : 8 + n, :] = mini[:, : 2 * STATE]
        pres = conv_pre(exts, sp_ref, n)
        bc = (pres * sigmoid(pres)).astype(BF16)
        exts[0:8, :] = exts[n : n + 8, :]
        key, query = bc[:, :STATE], bc[:, STATE:]

        _, step, rate, cs, wide_step, wide_cs, wide_tail = scan_prep(mini, hp_ref, ind, n)
        cs2 = cs * LOG2E
        cs2t = cs2.T
        xs = x * wide_step
        half = lax.rem(lax.broadcasted_iota(jnp.int32, xs.shape, 1), 2 * HEAD) < HEAD
        xs0 = jnp.where(half, xs, 0.0)
        xs1 = (xs - xs0).astype(BF16)
        xs0 = xs0.astype(BF16)
        before = state[...]
        low = before.astype(BF16)
        st_ref[0] = low
        carried = mm(query, low) * wide_cs
        xw = (xs * wide_tail).astype(BF16)
        state[...] = before * wide_cs[n - 1 : n, :] + mm(key, xw, TN)
        scores = jnp.where(rows >= cols, mm(query, key, NT), 0.0)
        for pair in range(heads // 2):
            lanes = slice(pair * 2 * HEAD, (pair + 1) * 2 * HEAD)
            mats = []
            for h in (2 * pair, 2 * pair + 1):
                dec = jnp.exp2(jnp.minimum(cs2[:, h : h + 1] - cs2t[h : h + 1, :], 0.0))
                mats.append((scores * dec).astype(BF16))
            local = mm(
                jnp.concatenate(mats, axis=1),
                jnp.concatenate([xs0[:, lanes], xs1[:, lanes]], axis=0),
            )
            ssd_ref[:, lanes] = local + carried[:, lanes] + cp_ref[6:7, lanes] * x[:, lanes]
        gates = gate[where, :]
        gated = ssd_ref[...] * (gates * sigmoid(gates))
        ones = jnp.ones((8, width), BF16)
        top, rest = split16(gated * gated)
        sqs_ref[0] = (mm(ones, top, NT) + mm(ones, rest, NT))[0:1, :]
        scaled_ref[...] = (gated * cp_ref[5:6, :]).astype(BF16)

        span = model // LANES
        share = -(-2 * span // steps)
        for k in range(share):
            b = at * share + k

            @pl.when(b < 2 * span)
            def _(b=b):
                j, col = b // span, lax.rem(b, span)
                slab_rows = slabs.shape[2]
                weight = slabs.at[j]
                piece = block_of(weight, col, slab_rows)
                wt[pl.ds(pl.multiple_of(j * width, width), width), pl.ds(pl.multiple_of(col * LANES, LANES), LANES)] = piece.T

    @pl.when(i == steps)
    def _():
        flush(4).start()
        job.arrive(2)
        flush(5).start()
        for j in range(3):
            job.drain(j)
        for k in range(len(outgoing)):
            flush(k).wait()


def forward(res, stateproj, steps_w, inproj, outt, gain, params, heads, size, layer, out=None):
    tokens_n, model = res.shape
    _, _, rows, width = inproj.shape
    top = 2 * width + 2 * STATE + LANES
    steps = tokens_n // CHUNK
    mid = out is not None
    hbm = pl.BlockSpec(memory_space=pl.ANY)
    chunks = model // SLICE

    def whole(a):
        return pl.BlockSpec(a.shape, lambda i: (0,) * len(a.shape))

    def row(w):
        return pl.BlockSpec((CHUNK, w), lambda i: (jnp.maximum(i - 1, 0), 0))

    args, in_specs, out_specs, out_shape, scratch = [res], [hbm], [], [], []
    if mid:
        args += list(out)
        in_specs += [hbm, hbm, whole(out[2])]
        out_specs += [hbm, whole(out[2])]
        out_shape += [jax.ShapeDtypeStruct(res.shape, F32), jax.ShapeDtypeStruct(out[2].shape, F32)]
        chunk = pltpu.VMEM((chunks, tokens_n // 2, SLICE), BF16)
        scratch += [
            pltpu.VMEM(out[0].shape, BF16),
            pltpu.VMEM(out[1].shape, BF16),
            pltpu.VMEM((2 * chunks, tokens_n // 2, SLICE), BF16),
            chunk, chunk, chunk,
            pltpu.VMEM((4,) + out[2].shape, F32),
            pltpu.VMEM((tokens_n, LANES), F32),
            pltpu.VMEM(res.shape, F32),
            pltpu.SemaphoreType.DMA((3, chunks)),
            pltpu.SemaphoreType.DMA((3, chunks)),
            pltpu.SemaphoreType.DMA((3,)),
            pltpu.SemaphoreType.DMA((3,)),
        ]
    args += [stateproj, steps_w, inproj, outt, gain, *params]
    in_specs += [hbm, hbm, hbm, hbm, whole(gain)] + [whole(v) for v in params]
    out_specs += [
        hbm, pl.BlockSpec((tokens_n, 1), lambda i: (0, 0)), hbm, hbm, hbm, hbm, hbm,
        row(width), row(width),
        pl.BlockSpec((1, 1, CHUNK), lambda i: (jnp.maximum(i - 1, 0), 0, 0)),
        pl.BlockSpec((1, STATE, width), lambda i: (jnp.maximum(i - 1, 0), 0, 0)),
    ]
    out_shape += [
        jax.ShapeDtypeStruct((model, tokens_n), BF16),
        jax.ShapeDtypeStruct((tokens_n, 1), F32),
        jax.ShapeDtypeStruct((tokens_n, 2 * STATE + LANES), F32),
        jax.ShapeDtypeStruct((tokens_n, width), F32),
        jax.ShapeDtypeStruct((tokens_n, width), F32),
        jax.ShapeDtypeStruct((top, model), BF16),
        jax.ShapeDtypeStruct((size, rows, width), BF16),
        jax.ShapeDtypeStruct((tokens_n, width), F32),
        jax.ShapeDtypeStruct((tokens_n, width), BF16),
        jax.ShapeDtypeStruct((steps, 1, CHUNK), F32),
        jax.ShapeDtypeStruct((steps, STATE, width), BF16),
    ]
    scratch += [
        pltpu.VMEM(res.shape, res.dtype),
        pltpu.VMEM((model, 2 * STATE), BF16),
        pltpu.VMEM((top, model), BF16),
        pltpu.VMEM((3, size, rows, width), BF16),
        pltpu.VMEM((tokens_n, model), BF16),
        pltpu.VMEM((model, tokens_n), BF16),
        pltpu.VMEM((tokens_n, 2 * STATE + LANES), F32),
        pltpu.VMEM((tokens_n, width), F32),
        pltpu.VMEM((tokens_n, width), F32),
        pltpu.VMEM((CHUNK + 8, width), F32),
        pltpu.VMEM((CHUNK + 8, 2 * STATE), F32),
        pltpu.VMEM((STATE, width), F32),
        pltpu.VMEM((8, width), F32),
        pltpu.VMEM((8, 2 * STATE), F32),
        pltpu.VMEM((8, LANES), F32),
        pltpu.VMEM((LANES, width), BF16),
        pltpu.SemaphoreType.DMA((3,)),
        pltpu.SemaphoreType.DMA((3, 3, size)),
        pltpu.SemaphoreType.DMA((3, size)),
        pltpu.SemaphoreType.DMA((5,)),
        pltpu.SemaphoreType.DMA((7,)),
    ]
    return pl.pallas_call(
        functools.partial(forward_body, size=size, heads=heads, per=LEN // CHUNK, steps=steps, layer=layer),
        grid=(steps + 1,),
        in_specs=in_specs,
        out_specs=out_specs,
        out_shape=out_shape,
        scratch_shapes=scratch,
        compiler_params=pltpu.CompilerParams(
            collective_id=min(layer, 1), has_side_effects=True, vmem_limit_bytes=VMEM_LIMIT
        ),
        name="forward",
    )(*args)


def back_body(*refs, heads, per, size, steps, layer, last):
    refs = list(refs)

    def take(n):
        got = refs[:n]
        del refs[:n]
        return got

    up_ref, sq_ref, gate_ref, ssd_ref, inner_ref, iprev_ref, small_ref, sprev_ref, st_ref, res_ref, rn_ref = take(11)
    gain_ref = take(1)[0]
    params = take(6)
    wout_hbm, scaled_hbm, wt_hbm, normed_hbm = take(4)
    if not last:
        next_normed, next_steps, next_sdel, next_dcp, next_dsp, next_dhp, next_dgain = take(7)
    new_ref, grad_hbm = take(2)
    if last:
        sdsum_ref, steplow_ref, dcp_ref, dsp_ref, dhp_ref, dgain_ref, mixed_ref = take(7)
    else:
        pack_ref, full_hbm, wide_hbm = take(3)
    ext, exts, cde, cdes, dstate, rq, cp_ref, sp_ref, hp_ref, ind_ref = take(10)
    wout, scaled, wt, turned, dy, glow, ilow, frow, srow, sgot = take(10)
    part, near, away, tpart, got, far, other = take(7)
    load, rsend, rrecv, ssend, srecv, sends, recvs, gsem = take(8)
    if last:
        fgot, opart, ogot, ofar, oother, fsend, frecv, osends, orecvs = take(9)
    else:
        dcp_ref, dsp_ref, dhp_ref, dgain_ref, step_all, sd_all = take(6)
        buffers = take(6)
        sems = take(7)
    assert not refs

    n = CHUNK
    model = up_ref.shape[1]
    i = pl.program_id(0)
    begin_gate = steps
    begin_scan = begin_gate + steps
    begin_norm = begin_scan + steps
    end = begin_norm + steps - 1
    line = Line(size)
    square = Square()
    rows_own = part.shape[2]
    count = part.shape[0]
    job = Scatter(line, part, lambda j: dy.at[pl.ds(j * rows_own, rows_own), :], near, away, ssend, srecv)
    sums = Total(square, tpart, got, far, other, sends, recvs)
    if last:
        outs = Total(square, opart, ogot, ofar, oother, osends, orecvs)
        half = steps * n // 2
        slices = model // SLICE
    else:
        minis = Smalls(line, square, *buffers, sems)
    moves = [(wout_hbm, wout), (scaled_hbm, scaled), (wt_hbm, wt), (normed_hbm, turned)]
    if not last:
        moves += [(next_normed, turned), (next_steps, step_all), (next_sdel, sd_all)]

    def move(k):
        return pltpu.make_async_copy(*moves[k], load.at[k])

    order = job.order()
    places = len(order)

    def spaced(begin, stop, m):
        return begin + m * (stop - begin) // places

    middle = begin_scan + steps // 2
    folds = [(spaced(begin_scan - steps // 2, middle, m), 0, p) for m, p in enumerate(order)]
    folds += [(spaced(middle, begin_norm, m), 1, p) for m, p in enumerate(order)]

    def column(row):
        return jnp.broadcast_to(row, (n, n)).T[:, 0:1]

    @pl.when(i == 0)
    def _():
        for k in range(len(moves)):
            if k != 3:
                move(k).start()
        put_params(cp_ref, sp_ref, hp_ref, ind_ref, layer, params)
        rq[...] = jnp.zeros_like(rq)
        line.greet_all(pltpu.get_barrier_semaphore(), square.others())
        if last:
            rows = [
                remote(sq_ref, fgot.at[square.me], fsend.at[k], frecv.at[k], who)
                for k, who in enumerate(square.others())
            ]
            for copy in rows:
                copy.start()
            fgot[square.me] = sq_ref[...]
            move(0).wait()
            move(1).wait()
            for c in range(slices):
                value = mm(scaled[...], wout[c * SLICE : (c + 1) * SLICE, :], NT).astype(BF16)
                opart[2 * c] = value[:half]
                opart[2 * c + 1] = value[half:]
                outs.step(0, c)
            outs.step(1, 0)
            for copy in rows:
                copy.wait()
            total = (fgot[0] + fgot[1]) + (fgot[2] + fgot[3])
        else:
            total = sq_ref[...]
            move(4).wait()
            move(5).wait()
            move(6).wait()
            put_pack(
                buffers[0].at[0], square.me, turned, step_all, sd_all,
                next_dcp[...], next_dsp[...], next_dhp[...], next_dgain[...],
            )
            minis.sum.start(0)
            move(0).wait()
            move(1).wait()
        dcp_ref[...] = jnp.zeros_like(dcp_ref)
        dsp_ref[...] = jnp.zeros_like(dsp_ref)
        dhp_ref[...] = jnp.zeros_like(dhp_ref)
        dgain_ref[...] = jnp.zeros_like(dgain_ref)
        frow[...] = lax.rsqrt(total / INNER + EPS)

    ind = ind_ref[...]
    for at, j, p in folds:
        @pl.when(i == at)
        def _(j=j, p=p):
            job.fold(j, p)

    if not last:
        @pl.when(i == 1)
        def _():
            for p in order:
                minis.sum.fold(0, p)
            minis.turn()

        for k in range(1, line.n):
            @pl.when(i == 2 + k * (steps - 4) // line.n)
            def _(k=k):
                minis.spread.relay(0, k)

        @pl.when(i == steps - 2)
        def _():
            minis.cross()

        @pl.when(i == begin_gate)
        def _():
            minis.cross_on()

    @pl.when(i < begin_gate)
    def _():
        rows = pl.ds(pl.multiple_of(i * n, n), n)
        low = (column(frow[i]) * up_ref[...].astype(F32)).astype(BF16)
        turned[:, rows] = low.T
        sd = mm(low, wout[...])
        dy[rows, :] = sd
        piece = scaled[rows, :]
        top, rest = split16(piece.astype(F32) * sd)
        ones = jnp.ones((8, sd.shape[1]), BF16)
        srow[i] = (mm(ones, top, NT) + mm(ones, rest, NT))[0:1, :]

    @pl.when(i == begin_gate - 1)
    def _():
        copies = [
            remote(srow, sgot.at[square.me], rsend.at[k], rrecv.at[k], who) for k, who in enumerate(square.others())
        ]
        for copy in copies:
            copy.start()
        job.emit(0, turned, scaled)
        move(3).start()
        sgot[square.me] = srow[...]
        for copy in copies:
            copy.wait()
        srow[...] = (sgot[0] + sgot[1]) + (sgot[2] + sgot[3])

    if last:
        @pl.when(i == steps // 2)
        def _():
            outs.step(1, 1)

        @pl.when((i >= begin_gate) & (i < begin_gate + slices - 2))
        def _():
            outs.step(1, i - begin_gate + 2)

    @pl.when((i >= begin_gate) & (i < begin_scan))
    def _():
        c = i - begin_gate
        rows = pl.ds(pl.multiple_of(c * n, n), n)
        coef = column(frow[c] * frow[c] * srow[c]) / INNER
        gate = gate_ref[...]
        gsig = sigmoid(gate)
        gact = gate * gsig
        ssd = ssd_ref[...]
        sd = dy[rows, :]
        gated = ssd * gact
        gd = cp_ref[5:6, :] * sd - coef * gated
        dcp_ref[5:6, :] += colsum(gated * sd)
        dy[rows, :] = gd * gact
        glow[rows, :] = (gd * ssd * (gsig + gact * (1.0 - gsig))).astype(BF16)

    @pl.when(i == begin_scan - 1)
    def _():
        move(3).wait()
        job.emit(1, turned, glow)
        move(2).wait()

    @pl.when((i >= begin_scan) & (i < begin_norm))
    def _():
        q = i - begin_scan
        chunk = steps - 1 - q
        where = pl.ds(pl.multiple_of(chunk * n, n), n)

        @pl.when(lax.rem(chunk, per) == per - 1)
        def _():
            cde[n : n + 8, :] = jnp.zeros((8, cde.shape[1]), F32)
            cdes[n : n + 8, :] = jnp.zeros((8, cdes.shape[1]), F32)
            dstate[...] = jnp.zeros_like(dstate)

        keep = jnp.where(lax.rem(chunk, per) == 0, 0.0, 1.0).astype(F32)
        rows, cols = iotas(n)
        ext[0:8, :] = iprev_ref[...] * keep
        ext[8 : 8 + n, :] = inner_ref[...]
        exts[0:8, :] = sprev_ref[:, : 2 * STATE] * keep
        exts[8 : 8 + n, :] = small_ref[:, : 2 * STATE]
        pre = conv_pre(ext, cp_ref, n)
        sig = sigmoid(pre)
        x = pre * sig
        slope = sig + x * (1.0 - sig)
        pres = conv_pre(exts, sp_ref, n)
        sigs = sigmoid(pres)
        acts = pres * sigs
        slopes = sigs + acts * (1.0 - sigs)
        bc = acts.astype(BF16)
        key, query = bc[:, :STATE], bc[:, STATE:]
        dyc = dy[where, :]

        raw, step, rate, cs, wide_step, wide_cs, wide_tail = scan_prep(small_ref, hp_ref, ind, n)
        cs2 = cs * LOG2E
        cs2t = cs2.T
        xs = x * wide_step
        xsb = xs.astype(BF16)
        half = lax.rem(lax.broadcasted_iota(jnp.int32, xs.shape, 1), 2 * HEAD) < HEAD
        dy0 = jnp.where(half, dyc, 0.0)
        dy1 = (dyc - dy0).astype(BF16)
        dy0 = dy0.astype(BF16)
        low = st_ref[0]
        dst = dstate[...]
        dlow = dst.astype(BF16)
        dye = dyc * wide_cs
        dyeb = dye.astype(BF16)
        up = headsum(dye * mm(query, low), ind)
        dxs_state = wide_tail * mm(key, dlow)
        down = headsum(xs * dxs_state, ind)
        qdel = mm(dyeb, low, NT)
        kdel = mm((xs * wide_tail).astype(BF16), dlow, NT)
        through = headsum(jnp.broadcast_to(colsum(low.astype(F32) * dst), (8, dst.shape[1])), ind)[0:1, :]
        through = through * jnp.exp(cs[n - 1 : n, :])
        dstate[...] = dst * wide_cs[n - 1 : n, :] + mm(query, dyeb, TN)

        scores = jnp.where(rows <= cols, mm(key, query, NT), 0.0)
        dscores = jnp.zeros((n, n), F32)
        colq = jnp.zeros((n, LANES), F32)
        lane = lax.broadcasted_iota(jnp.int32, (n, LANES), 1)
        dxs = []
        for pair in range(heads // 2):
            lanes = slice(pair * 2 * HEAD, (pair + 1) * 2 * HEAD)
            stacked = jnp.concatenate([dy0[:, lanes], dy1[:, lanes]], axis=0)
            both = mm(xsb[:, lanes], stacked, NT)
            mats = []
            for which, h in enumerate((2 * pair, 2 * pair + 1)):
                dec = jnp.exp2(jnp.minimum(cs2t[h : h + 1, :] - cs2[:, h : h + 1], 0.0))
                mats.append((scores * dec).astype(BF16))
                term = dec * both[:, which * n : (which + 1) * n]
                dscores = dscores + term
                quad = scores * term
                rq[h : h + 1, :] = colsum(quad)
                colq = jnp.where(lane == h, jnp.sum(quad, axis=1, keepdims=True), colq)
            dxs.append(mm(jnp.concatenate(mats, axis=1), stacked))
        dxs = jnp.concatenate(dxs, axis=1) + dxs_state
        dscores = jnp.where(rows <= cols, dscores, 0.0).astype(BF16)
        kdel = kdel + mm(dscores, query)
        qdel = qdel + mm(dscores, key, TN)

        upper = jnp.where(rows <= cols, 1.0, 0.0).astype(F32)
        strict = jnp.where(rows > cols, 1.0, 0.0).astype(F32)
        da = mm(upper, rq[...].T - colq + up, precision=HIGH) + mm(strict, down, precision=HIGH) + through
        grown = headsum(x * dxs, ind) + rate * da
        step_pre = grown * sigmoid(raw)
        steplow = step_pre.astype(BF16)
        if last:
            steplow_ref[...] = steplow
        else:
            step_all[where, :] = steplow
        dhp_ref[0:1, :] += colsum(step_pre)
        dhp_ref[1:2, :] += rate * colsum(step * da)
        dcp_ref[6:7, :] += colsum(dyc * x)

        cd = (dxs * wide_step + cp_ref[6:7, :] * dyc) * slope
        cde[0:n, :] = cd
        total = cp_ref[3:4, :] * cd
        for tap in range(3):
            total = total + cp_ref[tap : tap + 1, :] * cde[3 - tap : 3 - tap + n, :]
        inner_low = total.astype(BF16)
        ilow[where, :] = inner_low
        for tap in range(4):
            dcp_ref[tap : tap + 1, :] += colsum(cd * ext[5 + tap : 5 + tap + n, :])
        dcp_ref[4:5, :] += colsum(cd)
        cde[n : n + 8, :] = cde[0:8, :]

        cds = jnp.concatenate([kdel, qdel], axis=1) * slopes
        cdes[0:n, :] = cds
        total = sp_ref[3:4, :] * cds
        for tap in range(3):
            total = total + sp_ref[tap : tap + 1, :] * cdes[3 - tap : 3 - tap + n, :]
        sdel = total.astype(BF16)
        for tap in range(4):
            dsp_ref[tap : tap + 1, :] += colsum(cds * exts[5 + tap : 5 + tap + n, :])
        dsp_ref[4:5, :] += colsum(cds)
        cdes[n : n + 8, :] = cdes[0:8, :]

        lows = jnp.concatenate([inner_low, glow[where, :], sdel, steplow], axis=1)
        value = mm(lows, wt[...]).astype(BF16)
        tpart[2 * q, :, :model] = value[: n // 2]
        tpart[2 * q + 1, :, :model] = value[n // 2 :]
        tpart[2 * q, :, model:] = sdel[: n // 2]
        tpart[2 * q + 1, :, model:] = sdel[n // 2 :]
        sums.step(0, q)

    @pl.when((i > begin_scan) & (i <= begin_norm))
    def _():
        sums.step(1, i - begin_scan - 1)

    @pl.when((i >= begin_scan + 3) & (i < begin_norm + 3))
    def _():
        sums.step(2, i - begin_scan - 3)

    @pl.when((i >= begin_scan + 4) & (i < begin_norm + 4))
    def _():
        sums.step(3, i - begin_scan - 4)

    if last:
        @pl.when((i > begin_scan) & (i <= begin_scan + slices))
        def _():
            outs.step(2, i - begin_scan - 1)

        @pl.when((i > begin_scan + 1) & (i <= begin_scan + slices + 1))
        def _():
            outs.step(3, i - begin_scan - 2)

    @pl.when(i == begin_norm - 1)
    def _():
        dhp_ref[2:3, :] = headsum(jnp.broadcast_to(dcp_ref[6:7, :], (8, dcp_ref.shape[1])), ind)[0:1, :]
        job.emit(2, turned, ilow)

    @pl.when(i >= begin_norm)
    def _():
        r = i - begin_norm
        chunk = steps - 1 - r
        if last:
            fac = column(frow[chunk])
            side = chunk // (steps // 2)
            base = (chunk - side * (steps // 2)) * n
        for h in range(2):
            rows = slice(h * (n // 2), (h + 1) * (n // 2))
            back = tpart[2 * r + h, :, :model].astype(F32)
            sdel = tpart[2 * r + h, :, model:]
            if last:
                sdsum_ref[rows, :] = sdel
            else:
                sd_all[pl.ds(pl.multiple_of(chunk * n + h * (n // 2), n // 2), n // 2), :] = sdel
            res = res_ref[rows, :].astype(F32)
            rn = rn_ref[rows, :]
            dgain_ref[...] += colsum(back * res * rn)
            gained = back * gain_ref[layer : layer + 1, :]
            mean = jnp.sum(gained * res, axis=1, keepdims=True) / model
            new_ref[rows, :] = up_ref[rows, :].astype(F32) + rn * gained - (rn * rn * rn * mean) * res
            if last:
                where = pl.ds(pl.multiple_of(base + h * (n // 2), n // 2), n // 2)
                for c in range(slices):
                    span = slice(c * SLICE, (c + 1) * SLICE)
                    summed = opart[2 * c + side, where, :].astype(F32)
                    mixed_ref[rows, span] = (res[:, span] + fac[rows, :] * summed).astype(BF16)

    @pl.when(i == end)
    def _():
        if not last:
            put_pack(
                pack_ref, square.me, turned, step_all, sd_all, dcp_ref[...], dsp_ref[...], dhp_ref[...], dgain_ref[...]
            )
            minis.end()
            tails = [
                pltpu.make_async_copy(src, dst, load.at[k])
                for k, (src, dst) in enumerate(((minis.full, full_hbm), (minis.wide, wide_hbm)))
            ]
            for copy in tails:
                copy.start()
        for p in order:
            job.fold(2, p)
        for j in range(count):
            job.finish(j)
            pltpu.make_async_copy(dy.at[pl.ds(j * rows_own, rows_own), :], grad_hbm.at[j], gsem.at[j]).start()
        for j in range(count):
            job.drain(j)
            pltpu.make_async_copy(dy.at[pl.ds(j * rows_own, rows_own), :], grad_hbm.at[j], gsem.at[j]).wait()
        if not last:
            for copy in tails:
                copy.wait()


def back(up, sq, gate_pre, ssd, inner_raw, small, states, res, rnorm, gain, params,
         wout, scaled, wt, normed, heads, size, layer, after=None):
    tokens_n, width = inner_raw.shape
    model = up.shape[1]
    last = after is None
    steps = tokens_n // CHUNK
    begin_scan = 2 * steps
    begin_norm = begin_scan + steps
    rows = model // size
    n = size // 2
    hbm = pl.BlockSpec(memory_space=pl.ANY)
    top = steps - 1

    def norm_at(i):
        return jnp.where(i < begin_norm, top, top - (i - begin_norm))

    def scan_at(i):
        return jnp.clip(top - (i - begin_scan), 0, top)

    def first(w):
        return pl.BlockSpec((CHUNK, w), lambda i: (jnp.where(i < steps, i, norm_at(i)), 0))

    def second(w):
        return pl.BlockSpec((CHUNK, w), lambda i: (jnp.clip(i - steps, 0, top), 0))

    def scan(w):
        return pl.BlockSpec((CHUNK, w), lambda i: (scan_at(i), 0))

    def prev(w):
        return pl.BlockSpec((8, w), lambda i: (jnp.maximum(scan_at(i) * (CHUNK // 8) - 1, 0), 0))

    def norm(w):
        return pl.BlockSpec((CHUNK, w), lambda i: (norm_at(i), 0))

    def whole(a):
        return pl.BlockSpec(a.shape, lambda i: (0,) * len(a.shape))

    extra = model + 2 * STATE
    quarter = pltpu.VMEM((steps, CHUNK // 2, extra), BF16)
    pieces = pltpu.VMEM((3, n, rows, width), BF16)
    args = [up, sq, gate_pre, ssd, inner_raw, inner_raw, small, small, states, res, rnorm, gain, *params,
            wout, scaled, wt, normed]
    in_specs = [
        first(model), whole(sq), second(width), second(width),
        scan(width), prev(width), scan(small.shape[1]), prev(small.shape[1]),
        pl.BlockSpec((1, STATE, width), lambda i: (scan_at(i), 0, 0)),
        norm(model), norm(1), whole(gain),
    ] + [whole(a) for a in params] + [hbm] * 4
    out_specs = [norm(model), hbm]
    out_shape = [jax.ShapeDtypeStruct((tokens_n, model), F32), jax.ShapeDtypeStruct((3, rows, width), F32)]
    totals = [(8, width), (8, 2 * STATE), (8, LANES), (1, model)]
    scratch = [
        pltpu.VMEM((CHUNK + 8, width), F32),
        pltpu.VMEM((CHUNK + 8, 2 * STATE), F32),
        pltpu.VMEM((CHUNK + 8, width), F32),
        pltpu.VMEM((CHUNK + 8, 2 * STATE), F32),
        pltpu.VMEM((STATE, width), F32),
        pltpu.VMEM((LANES, CHUNK), F32),
        pltpu.VMEM((8, width), F32),
        pltpu.VMEM((8, 2 * STATE), F32),
        pltpu.VMEM((8, LANES), F32),
        pltpu.VMEM((LANES, width), BF16),
        pltpu.VMEM(wout.shape, BF16),
        pltpu.VMEM(scaled.shape, BF16),
        pltpu.VMEM(wt.shape, BF16),
        pltpu.VMEM(normed.shape, BF16),
        pltpu.VMEM((tokens_n, width), F32),
        pltpu.VMEM((tokens_n, width), BF16),
        pltpu.VMEM((tokens_n, width), BF16),
        pltpu.VMEM((steps, 1, CHUNK), F32),
        pltpu.VMEM((steps, 1, CHUNK), F32),
        pltpu.VMEM((4, steps, 1, CHUNK), F32),
        pltpu.VMEM((3, size, rows, width), BF16), pieces, pieces,
        pltpu.VMEM((2 * steps, CHUNK // 2, extra), BF16), quarter, quarter, quarter,
        pltpu.SemaphoreType.DMA((7,)),
        pltpu.SemaphoreType.DMA((3,)),
        pltpu.SemaphoreType.DMA((3,)),
        pltpu.SemaphoreType.DMA((2, 3, n)),
        pltpu.SemaphoreType.DMA((2, 3, n)),
        pltpu.SemaphoreType.DMA((3, steps)),
        pltpu.SemaphoreType.DMA((3, steps)),
        pltpu.SemaphoreType.DMA((3,)),
    ]
    if last:
        out_specs += [norm(2 * STATE), scan(LANES)]
        out_specs += [pl.BlockSpec(v, lambda i: (0, 0)) for v in totals] + [norm(model)]
        out_shape += [
            jax.ShapeDtypeStruct((tokens_n, 2 * STATE), BF16),
            jax.ShapeDtypeStruct((tokens_n, LANES), BF16),
        ]
        out_shape += [jax.ShapeDtypeStruct(v, F32) for v in totals]
        out_shape.append(jax.ShapeDtypeStruct((tokens_n, model), BF16))
        slices = model // SLICE
        chunk = pltpu.VMEM((slices, tokens_n // 2, SLICE), BF16)
        scratch += [
            pltpu.VMEM((4, steps, 1, CHUNK), F32),
            pltpu.VMEM((2 * slices, tokens_n // 2, SLICE), BF16), chunk, chunk, chunk,
            pltpu.SemaphoreType.DMA((3,)),
            pltpu.SemaphoreType.DMA((3,)),
            pltpu.SemaphoreType.DMA((3, slices)),
            pltpu.SemaphoreType.DMA((3, slices)),
        ]
    else:
        w = 2 * STATE
        r = pack_rows(size)
        args += list(after)
        in_specs += [hbm] * 3 + [whole(v) for v in after[3:]]
        out_specs += [pl.BlockSpec((size, r, w), lambda i: (0, 0, 0)), hbm, hbm]
        out_shape += [
            jax.ShapeDtypeStruct((size, r, w), BF16),
            jax.ShapeDtypeStruct((1, size, r, w), BF16),
            jax.ShapeDtypeStruct((4, SPAN, w), BF16),
        ]
        scratch += [pltpu.VMEM(v, F32) for v in totals]
        scratch += [pltpu.VMEM((tokens_n, LANES), BF16), pltpu.VMEM((tokens_n, w), BF16)]
        scratch += smalls_scratch(size, w)
    return pl.pallas_call(
        functools.partial(
            back_body, heads=heads, per=LEN // CHUNK, size=size, steps=steps, layer=layer, last=last
        ),
        grid=(begin_norm + steps,),
        in_specs=in_specs,
        out_specs=out_specs,
        out_shape=out_shape,
        scratch_shapes=scratch,
        compiler_params=pltpu.CompilerParams(
            collective_id=2 if last else 3, has_side_effects=True, vmem_limit_bytes=VMEM_LIMIT
        ),
        name="back",
    )(*args)


def final_body(*refs, size, layers, heads):
    refs = list(refs)

    def take(n):
        got = refs[:n]
        del refs[:n]
        return got

    (pack_hbm,) = take(1)
    earlier = [take(2) for _ in range(layers - 1)]
    step_ref, state_ref, conv_ref, bias_ref, convs_ref, biass_ref = take(6)
    stepbias_ref, decay_ref, skip_ref, norm_ref, gain_ref = take(5)
    buffers = take(6)
    sems = take(7)
    (load,) = take(1)
    assert not refs
    line = Line(size)
    square = Square()
    minis = Smalls(line, square, *buffers, sems)
    copy = pltpu.make_async_copy(pack_hbm, buffers[0].at[0], load)
    copy.start()
    line.greet_all(pltpu.get_barrier_semaphore(), (square.mate, square.across))
    copy.wait()
    minis.sum.start(0)
    model = state_ref.shape[1]
    quarter = model // 4
    w = state_ref.shape[2]
    width = conv_ref.shape[2]

    def unpack(layer, full, wide):
        for t in range(4):
            state_ref[layer, t * quarter : (t + 1) * quarter, :] = wide[t, :quarter, :].astype(F32)
        taps = [wide[t, quarter : quarter + 16, :].astype(F32) for t in range(4)]
        taps = (taps[0] + taps[1]) + (taps[2] + taps[3])
        convs_ref[layer] = taps[0:4]
        biass_ref[layer : layer + 1, :] = taps[4:5]
        flat = full[...].reshape(-1, w)[:PACK].astype(F32)
        at = quarter + 16
        for b in range(model // w):
            step_ref[layer, :, b * w : (b + 1) * w] = flat[at : at + 16]
            at += 16
        for b in range(width // w):
            lanes = slice(b * w, (b + 1) * w)
            rows = flat[at + 8 * b : at + 8 * b + 8]
            conv_ref[layer, :, lanes] = rows[0:4]
            bias_ref[layer : layer + 1, lanes] = rows[4:5]
            norm_ref[layer : layer + 1, lanes] = rows[5:6]
        at += 8 * (width // w)
        for k, ref in enumerate((stepbias_ref, decay_ref, skip_ref)):
            ref[layer : layer + 1, :] = flat[at + k : at + k + 1, :heads]
        at += 8
        for b in range(model // w):
            gain_ref[layer : layer + 1, b * w : (b + 1) * w] = flat[at + b : at + b + 1]

    for layer, (full, wide) in enumerate(earlier):
        unpack(layer + 1, full.at[0], wide)
    for p in minis.sum.order():
        minis.sum.fold(0, p)
    minis.turn()
    for k in range(1, line.n):
        minis.spread.relay(0, k)
    minis.cross()
    minis.cross_on()
    minis.end()
    unpack(0, minis.full.at[0], minis.wide)


def final(pack, earlier, width, heads):
    size, r, w = pack.shape
    layers = len(earlier) + 1
    model = (SPAN - 16) * 4
    vm = pl.BlockSpec(memory_space=pltpu.VMEM)
    hbm = pl.BlockSpec(memory_space=pl.ANY)
    shapes = [
        (layers, 16, model), (layers, model, w), (layers, 4, width),
        (layers, width), (layers, 4, w), (layers, w), (layers, heads), (layers, heads), (layers, heads),
        (layers, width), (layers, model),
    ]
    flat = [v for both in earlier for v in both]
    return pl.pallas_call(
        functools.partial(final_body, size=size, layers=layers, heads=heads),
        in_specs=[hbm] + [vm] * len(flat),
        out_specs=[vm] * len(shapes),
        out_shape=[jax.ShapeDtypeStruct(v, F32) for v in shapes],
        scratch_shapes=smalls_scratch(size, w) + [pltpu.SemaphoreType.DMA],
        compiler_params=pltpu.CompilerParams(
            collective_id=4, has_side_effects=True, vmem_limit_bytes=VMEM_LIMIT
        ),
        name="final",
    )(pack, *flat)


def shards(
    tokens, inproj, stepproj, stateproj, outproj, convinner, biasinner, convstate, biasstate,
    stepbias, decaylog, skipgain, normgain, inputgain, cotangent,
):
    layers = inproj.shape[0]
    width = inproj.shape[3]
    heads = stepproj.shape[2]
    model = tokens.shape[1]
    pad = LANES - heads
    size = lax.axis_size("dp")
    steps_w = jnp.pad(jnp.swapaxes(stepproj, 1, 2), ((0, 0), (0, pad), (0, 0)))
    head = jnp.pad(jnp.stack([stepbias, decaylog, skipgain], axis=1), ((0, 0), (0, 5), (0, pad)))
    outt = jnp.swapaxes(outproj, 1, 2)
    params = (convinner, biasinner, normgain, convstate, biasstate, head)

    residual = tokens
    kept = []
    out = None
    for at in range(layers):
        results = forward(residual, stateproj, steps_w, inproj, outt, inputgain, params, heads, size, at, out=out)
        if at:
            residual, kept[-1][-1] = results[:2]
            results = results[2:]
        normed, rnorm, small, inner_raw, gate_pre, wt, w_out, ssd, scaled, sq, states = results
        w_out = w_out.reshape(model, width)
        kept.append([residual, normed, rnorm, small, inner_raw, gate_pre, wt, w_out, ssd, scaled, states, sq])
        out = (scaled, w_out, sq)

    upstream = cotangent
    after = None
    pieces = [None] * layers
    earlier = []
    for at in reversed(range(layers)):
        before, normed, rnorm, small, inner_raw, gate_pre, wt, w_out, ssd, scaled, states, sq = kept[at]
        upstream, pieces[at], *rest = back(
            upstream, sq, gate_pre, ssd, inner_raw, small, states, before, rnorm, inputgain, params,
            w_out, scaled, wt, normed, heads, size, at, after=after,
        )
        if after is None:
            sdel, steplow, *totals, mixed = rest
            after = (normed, steplow, sdel, *totals)
        else:
            pack, *found = rest
            earlier.append(found)
    (
        step_grad, state_grad, conv_grad, bias_grad, convs_grad, biass_grad,
        stepbias_grad, decay_grad, skip_grad, norm_grad, gain_grad,
    ) = final(pack, earlier, width, heads)
    return (
        mixed,
        upstream,
        jnp.stack([v[1:] for v in pieces]),
        jnp.swapaxes(step_grad[:, :heads], 1, 2),
        state_grad,
        jnp.swapaxes(jnp.stack([v[0] for v in pieces]), 1, 2),
        conv_grad,
        bias_grad,
        convs_grad,
        biass_grad,
        stepbias_grad,
        decay_grad,
        skip_grad,
        norm_grad,
        gain_grad,
    )


def solution(mesh):
    in_specs = (
        P("dp", None),
        P(None, None, "dp", "tensor"),
        P(None, None, "tensor"),
        P(),
        P(None, "tensor", "dp"),
        P(None, None, "tensor"),
        P(None, "tensor"),
        P(),
        P(),
        P(None, "tensor"),
        P(None, "tensor"),
        P(None, "tensor"),
        P(None, "tensor"),
        P(),
        P("dp", None),
    )
    out_specs = (
        P("dp", None),
        P("dp", None),
        P(None, None, "dp", "tensor"),
        P(None, None, "tensor"),
        P(),
        P(None, "tensor", "dp"),
        P(None, None, "tensor"),
        P(None, "tensor"),
        P(),
        P(),
        P(None, "tensor"),
        P(None, "tensor"),
        P(None, "tensor"),
        P(None, "tensor"),
        P(),
    )
    return jax.shard_map(shards, mesh=mesh, in_specs=in_specs, out_specs=out_specs, check_vma=False)
```

```python
import functools
import math

import jax
import jax.numpy as jnp
from jax import lax
from jax.experimental import pallas as pl
from jax.experimental.pallas import tpu as pltpu
from jax.sharding import PartitionSpec as P

STATE = 128
LEN = 1024
INNER = 3072
HEAD = 64
CHUNK = 128
SLICE = 256
TILE = 256
PACK = 544
SPAN = 400
VMEM_LIMIT = 65000 * 1024
LANES = 128
EPS = 1e-05
LOG2E = 1.4426950408889634

HIGH = lax.Precision.HIGHEST
NN = (((1,), (0,)), ((), ()))
NT = (((1,), (1,)), ((), ()))
TN = (((0,), (0,)), ((), ()))
F32 = jnp.float32
BF16 = jnp.bfloat16
MESH = pl.DeviceIdType.MESH


def remote(src, dst, send, recv, where):
    return pltpu.make_async_remote_copy(
        src_ref=src, dst_ref=dst, send_sem=send, recv_sem=recv, device_id=where, device_id_type=MESH
    )


class Line:
    def __init__(self, size):
        self.n = size // 2
        me = lax.axis_index("dp")
        self.me = me
        self.at = me // 2
        self.side = lax.rem(me, 2)
        self.pair = {"dp": me + 1 - 2 * self.side}
        self.right = {"dp": jnp.minimum(me + 2, size - 1)}
        self.left = {"dp": jnp.maximum(me - 2, 0)}
        self.has_left = self.at > 0
        self.has_right = self.at < self.n - 1

    def greet(self, barrier, more=()):
        for who in more:
            pl.semaphore_signal(barrier, inc=1, device_id=who, device_id_type=MESH)
        pl.semaphore_signal(barrier, inc=1, device_id=self.pair, device_id_type=MESH)

        @pl.when(self.has_left)
        def _():
            pl.semaphore_signal(barrier, inc=1, device_id=self.left, device_id_type=MESH)

        @pl.when(self.has_right)
        def _():
            pl.semaphore_signal(barrier, inc=1, device_id=self.right, device_id_type=MESH)

        peers = 1 + len(more) + self.has_left.astype(jnp.int32) + self.has_right.astype(jnp.int32)
        pl.semaphore_wait(barrier, peers)

    def greet_all(self, barrier, more=()):
        for who in list(more) + [self.pair]:
            pl.semaphore_signal(barrier, inc=1, device_id=who, device_id_type=MESH)
        for i in range(self.n):
            @pl.when(i != self.at)
            def _(i=i):
                pl.semaphore_signal(barrier, inc=1, device_id={"dp": 2 * i + self.side}, device_id_type=MESH)
        pl.semaphore_wait(barrier, self.n + len(more))


class Gather:
    def __init__(self, line, own, full, keep, send, recv):
        self.line, self.own, self.full, self.keep, self.send, self.recv = line, own, full, keep, send, recv

    def copy(self, j, slab, way, src=None):
        where = (self.line.right, self.line.left, self.line.pair)[way]
        src = self.full.at[j, slab] if src is None else src
        return remote(src, self.full.at[j, slab], self.send.at[j, way, slab], self.recv.at[j, slab], where)

    def start(self, j):
        line = self.line
        pltpu.make_async_copy(self.own(j), self.full.at[j, line.me], self.keep.at[j]).start()

        @pl.when(line.has_right)
        def _():
            self.copy(j, line.me, 0, self.own(j)).start()

        @pl.when(line.has_left)
        def _():
            self.copy(j, line.me, 1, self.own(j)).start()

        self.copy(j, line.me, 2, self.own(j)).start()

    def relay(self, j, k):
        line = self.line

        @pl.when(line.at >= k)
        def _():
            slab = line.me - 2 * k
            self.copy(j, slab, 0).wait_recv()

            @pl.when(line.has_right)
            def _():
                self.copy(j, slab, 0).start()

            self.copy(j, slab, 2).start()

        @pl.when(line.at + k < line.n)
        def _():
            slab = line.me + 2 * k
            self.copy(j, slab, 1).wait_recv()

            @pl.when(line.has_left)
            def _():
                self.copy(j, slab, 1).start()

            self.copy(j, slab, 2).start()

    def arrive(self, j):
        line = self.line
        pltpu.make_async_copy(self.own(j), self.full.at[j, line.me], self.keep.at[j]).wait()
        for place in range(line.n):
            self.copy(j, 2 * place + 1 - line.side, 2).wait_recv()

    def drain(self, j):
        line = self.line
        for place in range(line.n):
            slab = 2 * place + line.side
            self.copy(j, slab, 2).wait_send()

            @pl.when(line.has_right & (place <= line.at))
            def _():
                self.copy(j, slab, 0).wait_send()

            @pl.when(line.has_left & (place >= line.at))
            def _():
                self.copy(j, slab, 1).wait_send()


class Square:
    def __init__(self):
        me = lax.axis_index("tensor")
        self.me = me
        self.half = lax.rem(me, 2)
        self.mate = {"tensor": me + 1 - 2 * self.half}
        self.across = {"tensor": lax.rem(me + 2, 4)}

    def others(self):
        return [{"tensor": lax.rem(self.me + k, 4)} for k in (1, 2, 3)]


class Total:
    def __init__(self, square, part, got, far, other, send, recv):
        self.square, self.part, self.got, self.far, self.other = square, part, got, far, other
        self.send, self.recv = send, recv

    def first(self, c):
        sq = self.square
        return remote(
            self.part.at[2 * c + 1 - sq.half], self.got.at[c], self.send.at[0, c], self.recv.at[0, c], sq.mate
        )

    def second(self, c):
        sq = self.square
        return remote(self.part.at[2 * c + sq.half], self.far.at[c], self.send.at[1, c], self.recv.at[1, c], sq.across)

    def third(self, c):
        sq = self.square
        return remote(self.part.at[2 * c + sq.half], self.other.at[c], self.send.at[2, c], self.recv.at[2, c], sq.mate)

    def step(self, kind, c):
        slot = 2 * c + self.square.half
        if kind == 0:
            self.first(c).start()
        elif kind == 1:
            self.first(c).wait_recv()
            self.part[slot] = (self.part[slot].astype(F32) + self.got[c].astype(F32)).astype(BF16)
            self.second(c).start()
        elif kind == 2:
            self.second(c).wait()
            self.part[slot] = (self.part[slot].astype(F32) + self.far[c].astype(F32)).astype(BF16)
            self.third(c).start()
        else:
            self.third(c).wait_recv()
            self.first(c).wait_send()
            self.third(c).wait_send()
            self.part[2 * c + 1 - self.square.half] = self.other[c]


class Scatter:
    def __init__(self, line, part, out, near, far, send, recv):
        self.line, self.part, self.out, self.near, self.far = line, part, out, near, far
        self.send, self.recv = send, recv

    def order(self):
        n = self.line.n
        seq = []
        for i in range((n + 1) // 2):
            seq.append(i)
            if n - 1 - i != i:
                seq.append(n - 1 - i)
        return seq

    def cross(self, j, i):
        line = self.line
        return remote(
            self.part.at[j, 2 * i + 1 - line.side], self.near.at[j, i], self.send.at[0, j, i], self.recv.at[0, j, i], line.pair
        )

    def straight(self, j, i, source):
        line = self.line
        return remote(
            self.part.at[j, 2 * i + line.side], self.far.at[j, source], self.send.at[1, j, i], self.recv.at[1, j, source],
            {"dp": 2 * i + line.side},
        )

    def start(self, j):
        for i in self.order():
            self.cross(j, i).start()

    def emit(self, j, turned, right, now=None):
        rows = self.part.shape[2]
        for m, i in enumerate(self.order()):
            value = mm(turned[2 * i * rows : 2 * (i + 1) * rows, :], right[...]).astype(BF16)
            self.part[j, 2 * i] = value[:rows]
            self.part[j, 2 * i + 1] = value[rows:]
            if now is None or m < now:
                self.cross(j, i).start()

    def fold(self, j, i):
        line = self.line
        self.cross(j, i).wait_recv()
        slot = 2 * i + line.side
        self.part[j, slot] = (self.part[j, slot].astype(F32) + self.near[j, i].astype(F32)).astype(BF16)

        @pl.when(i != line.at)
        def _():
            self.straight(j, i, line.at).start()

    def finish(self, j):
        line = self.line
        out = self.out(j)
        out[...] = self.part[j, line.me].astype(out.dtype)
        for i in range(line.n):
            @pl.when(i != line.at)
            def _(i=i):
                self.straight(j, i, i).wait_recv()
                out[...] += self.far[j, i].astype(out.dtype)

    def drain(self, j):
        for i in range(self.line.n):
            self.cross(j, i).wait_send()

            @pl.when(i != self.line.at)
            def _(i=i):
                self.straight(j, i, self.line.at).wait_send()


def mm(left, right, dims=NN, precision=None):
    return lax.dot_general(left, right, dims, precision=precision, preferred_element_type=F32)


def sigmoid(v):
    return 0.5 * jnp.tanh(0.5 * v) + 0.5


def softplus(v):
    return jnp.maximum(v, 0.0) + jnp.log1p(jnp.exp(-jnp.abs(v)))


def split16(v):
    top = v.astype(BF16)
    return top, (v - top.astype(F32)).astype(BF16)


def expand(v, ind):
    top, rest = split16(v)
    return mm(top, ind) + mm(rest, ind)


def headsum(v, ind):
    top, rest = split16(v)
    return mm(top, ind, NT) + mm(rest, ind, NT)


def iotas(n):
    return (
        lax.broadcasted_iota(jnp.int32, (n, n), 0),
        lax.broadcasted_iota(jnp.int32, (n, n), 1),
    )


def colsum(v):
    return jnp.sum(v, axis=0, keepdims=True)


def conv_pre(ext, par, n):
    total = par[4:5, :] + par[0:1, :] * ext[5 : 5 + n, :]
    for tap in range(1, 4):
        total = total + par[tap : tap + 1, :] * ext[5 + tap : 5 + tap + n, :]
    return total


def scan_prep(small, hp, ind, n):
    rows, cols = iotas(n)
    raw = small[:, 2 * STATE :] + hp[0:1, :]
    step = softplus(raw)
    rate = -jnp.exp(hp[1:2, :])
    lower = jnp.where(rows >= cols, 1.0, 0.0).astype(F32)
    cs = mm(lower, step * rate, precision=HIGH)
    tail = jnp.exp(cs[n - 1 : n, :] - cs)
    wide = expand(jnp.concatenate([step, jnp.exp(cs), tail], axis=0), ind)
    return raw, step, rate, cs, wide[0:n], wide[n : 2 * n], wide[2 * n : 3 * n]


def block_of(slabs, at, rows):
    step = math.gcd(LANES, rows)
    pieces = []
    for k in range(LANES // step):
        row = at * LANES + k * step
        slab = row // rows
        pieces.append(slabs[slab, pl.ds(pl.multiple_of(row - slab * rows, step), step), :])
    return pieces[0] if len(pieces) == 1 else jnp.concatenate(pieces, axis=0)


def put_params(cp, sp, hp, ind, layer, params):
    conv, bias, norm, convs, biass, head = params
    width = cp.shape[1]
    row = lax.broadcasted_iota(jnp.int32, (LANES, width), 0)
    lane = lax.broadcasted_iota(jnp.int32, (LANES, width), 1)
    ind[...] = jnp.where(lane // HEAD == row, 1.0, 0.0).astype(BF16)
    hp[...] = head[layer]
    cp[0:4, :] = conv[layer]
    cp[4:5, :] = bias[layer : layer + 1, :]
    cp[5:6, :] = norm[layer : layer + 1, :]
    cp[6:8, :] = expand(hp[...], ind[...])[2:4, :]
    sp[0:4, :] = convs[layer]
    sp[4:5, :] = biass[layer : layer + 1, :]


def place_rows(dst, at, value):
    r = dst.shape[1]
    for g in range(0, value.shape[0], 16):
        dst[(at + g) // r, (at + g) % r : (at + g) % r + 16, :] = value[g : g + 16].astype(dst.dtype)


def pack_rows(size):
    return -(-PACK // (16 * size)) * 16


def put_pack(dst, me, turned, steps_low, sdel, dcp, dsp, dhp, dgain):
    model = turned.shape[0]
    quarter = model // 4
    w = sdel.shape[1]

    def empty(n):
        return jnp.zeros((n, w), F32)

    place_rows(dst, 0, mm(turned[pl.ds(pl.multiple_of(me * quarter, quarter), quarter), :], sdel[...]))
    place_rows(dst, quarter, jnp.concatenate([dsp, empty(8)], axis=0))
    grown = mm(turned[...], steps_low[...]).T[:16]
    at = quarter + 16
    for b in range(model // w):
        place_rows(dst, at, grown[:, b * w : (b + 1) * w])
        at += 16
    place_rows(dst, at, jnp.concatenate([dcp[:, :w], dcp[:, w : 2 * w]], axis=0))
    place_rows(dst, at + 16, jnp.concatenate([dcp[:, 2 * w :], jnp.concatenate([dhp, dhp], axis=1)], axis=0))
    rows = [dgain[:, b * w : (b + 1) * w] for b in range(model // w)]
    place_rows(dst, at + 32, jnp.concatenate(rows + [empty(16 - len(rows))], axis=0))
    assert at + 48 == PACK


class Smalls:
    def __init__(self, line, square, pack, near, away, own, full, wide, sems):
        send, recv, keep, gsend, grecv, self.xsend, self.xrecv = sems
        self.square, self.full, self.wide = square, full, wide
        self.layers = range(pack.shape[0])
        self.sum = Scatter(line, pack, lambda j: own.at[j], near, away, send, recv)
        self.spread = Gather(line, lambda j: own.at[j], full, keep, gsend, grecv)

    def swap(self, k):
        sq = self.square
        slot = (sq.me, sq.me, lax.rem(sq.me + 2, 4))[k]
        who = (sq.across, sq.mate, sq.mate)[k]
        return remote(self.wide.at[slot], self.wide.at[slot], self.xsend.at[k], self.xrecv.at[k], who)

    def start(self):
        for j in self.layers:
            self.sum.start(j)

    def fold(self):
        for j in self.layers:
            for p in self.sum.order():
                self.sum.fold(j, p)

    def turn(self):
        for j in self.layers:
            self.sum.finish(j)
            self.spread.start(j)

    def relay(self, k):
        for j in self.layers:
            self.spread.relay(j, k)

    def cross(self):
        for j in self.layers:
            self.spread.arrive(j)
            flat = self.full[j].reshape(-1, self.full.shape[3])
            self.wide[self.square.me, j] = flat[: self.wide.shape[2]]
        self.swap(0).start()
        self.swap(1).start()

    def cross_on(self):
        self.swap(0).wait_recv()
        self.swap(2).start()

    def end(self):
        self.swap(1).wait_recv()
        self.swap(2).wait_recv()
        for k in range(3):
            self.swap(k).wait_send()
        for j in self.layers:
            self.sum.drain(j)
            self.spread.drain(j)


def smalls_scratch(size, w, layers):
    r, n = pack_rows(size), size // 2
    buffers = [
        pltpu.VMEM((layers, size, r, w), BF16),
        pltpu.VMEM((layers, n, r, w), BF16),
        pltpu.VMEM((layers, n, r, w), BF16),
        pltpu.VMEM((layers, r, w), BF16),
        pltpu.VMEM((layers, size, r, w), BF16),
        pltpu.VMEM((4, layers, SPAN, w), BF16),
    ]
    sems = [
        pltpu.SemaphoreType.DMA((2, layers, n)),
        pltpu.SemaphoreType.DMA((2, layers, n)),
        pltpu.SemaphoreType.DMA((layers,)),
        pltpu.SemaphoreType.DMA((layers, 3, size)),
        pltpu.SemaphoreType.DMA((layers, size)),
        pltpu.SemaphoreType.DMA((3,)),
        pltpu.SemaphoreType.DMA((3,)),
    ]
    return buffers + sems


def forward_body(*refs, size, heads, per, steps, layer):
    refs = list(refs)

    def take(n):
        got = refs[:n]
        del refs[:n]
        return got

    mid = layer > 0
    (res_hbm,) = take(1)
    if mid:
        scaled_hbm, wout_hbm, sq_ref = take(3)
    state_hbm, step_hbm, in_hbm, out_hbm, gain_ref = take(5)
    params = take(6)
    if mid:
        new_hbm, sums_ref = take(2)
    normed_hbm, rnorm_ref, small_hbm, inner_hbm, gate_hbm, wt_hbm, full_hbm, ssd_ref, scaled_ref, sqs_ref, st_ref = take(11)
    if mid:
        scaled_in, wout, part, got, far, other, rows_got, facs, fresh, sends, recvs, rsend, rrecv = take(13)
    res, wstate, wt, slabs, normed, turned, small, inner, gate, ext, exts, state = take(12)
    cp_ref, sp_ref, hp_ref, ind_ref, keep, gsend, grecv, load, sems = take(9)
    assert not refs

    n = CHUNK
    tokens_n, model = res.shape
    width = inner.shape[1]
    top = 2 * width + 2 * STATE
    i = pl.program_id(0)
    line = Line(size)
    square = Square()
    job = Gather(line, lambda j: out_hbm.at[layer] if j == 2 else in_hbm.at[layer, 1 - j], slabs, keep, gsend, grecv)
    outgoing = [(turned, normed_hbm), (small, small_hbm), (inner, inner_hbm), (gate, gate_hbm)]
    outgoing += [(wt, wt_hbm), (slabs.at[2], full_hbm)]
    if mid:
        outgoing.append((fresh, new_hbm))

    def flush(k):
        return pltpu.make_async_copy(*outgoing[k], sems.at[k])


    @pl.when(i == 0)
    def _():
        pairs = [(res_hbm, res), (state_hbm.at[layer], wstate), (step_hbm.at[layer], wt.at[pl.ds(top, LANES), :])]
        if mid:
            pairs = [(scaled_hbm, scaled_in), (wout_hbm, wout)] + pairs
        loads = [pltpu.make_async_copy(src, dst, load.at[k]) for k, (src, dst) in enumerate(pairs)]
        for copy in loads:
            copy.start()
        line.greet(pltpu.get_barrier_semaphore(), square.others() if mid else ())
        job.start(0)
        put_params(cp_ref, sp_ref, hp_ref, ind_ref, layer, params)
        ticks = [functools.partial(job.relay, 0, k) for k in range(1, line.n)]
        ticks.append(functools.partial(job.start, 1))
        ticks += [functools.partial(job.relay, 1, k) for k in range(1, line.n)]
        ticks.append(functools.partial(job.start, 2))

        if mid:
            chunks = model // SLICE
            half = tokens_n // 2
            sums = Total(square, part, got, far, other, sends, recvs)
            copies = [
                remote(sq_ref, rows_got.at[square.me], rsend.at[k], rrecv.at[k], who)
                for k, who in enumerate(square.others())
            ]
            for copy in copies:
                copy.start()
            loads[0].wait()
            loads[1].wait()
            for c in range(chunks):
                value = mm(scaled_in[...], wout[c * SLICE : (c + 1) * SLICE, :], NT).astype(BF16)
                part[2 * c] = value[:half]
                part[2 * c + 1] = value[half:]
                sums.step(0, c)
                if c:
                    sums.step(1, c - 1)
            sums.step(1, chunks - 1)
            rows_got[square.me] = sq_ref[...]
            for copy in copies:
                copy.wait()
            total = (rows_got[0] + rows_got[1]) + (rows_got[2] + rows_got[3])
            sums_ref[...] = total
            factor = lax.rsqrt(total / INNER + EPS)
            for t in range(tokens_n // LANES):
                facs[t * LANES : (t + 1) * LANES, :] = jnp.broadcast_to(factor[t], (LANES, LANES)).T
            loads[2].wait()

            def use(c):
                for h in range(2):
                    where = slice(h * half, (h + 1) * half)
                    for s in range(SLICE // LANES):
                        lanes = slice(c * SLICE + s * LANES, c * SLICE + (s + 1) * LANES)
                        value = part[2 * c + h, :, s * LANES : (s + 1) * LANES].astype(F32)
                        fresh[where, lanes] = res[where, lanes].astype(F32) + facs[where, :] * value

            spread = max(1, -(-len(ticks) // chunks))
            for c in range(chunks):
                for tick in ticks[:spread]:
                    tick()
                ticks = ticks[spread:]
                sums.step(2, c)
                if c:
                    sums.step(3, c - 1)
                    use(c - 1)
            sums.step(3, chunks - 1)
            use(chunks - 1)
            flush(6).start()
        else:
            loads[0].wait()
        loads[-2].wait()
        loads[-1].wait()
        for b in range(2 * STATE // LANES):
            rows = slice(2 * width + b * LANES, 2 * width + (b + 1) * LANES)
            wt[rows, :] = wstate[:, b * LANES : (b + 1) * LANES].T

        def norm(t, _):
            rows = pl.ds(pl.multiple_of(t * TILE, TILE), TILE)
            value = (fresh if mid else res)[rows, :].astype(F32)
            scale = lax.rsqrt(jnp.sum(value * value, axis=1, keepdims=True) / model + EPS)
            low = (value * scale * gain_ref[layer : layer + 1, :]).astype(BF16)
            rnorm_ref[rows, :] = scale
            normed[rows, :] = low
            turned[:, rows] = low.T
            small[rows, : 2 * STATE] = mm(low, wstate[...])
            small[rows, 2 * STATE :] = mm(low, wt[top:, :], NT)
            return 0

        lax.fori_loop(0, tokens_n // TILE, norm, 0)
        flush(0).start()
        flush(1).start()
        for tick in ticks:
            tick()

        def project(j, dst):
            weight = slabs[j].reshape(model, width)

            def tile(t, _):
                rows = pl.ds(pl.multiple_of(t * TILE, TILE), TILE)
                dst[rows, :] = mm(normed[rows, :], weight)
                return 0

            lax.fori_loop(0, tokens_n // TILE, tile, 0)

        for j, dst in ((0, inner), (1, gate)):
            job.arrive(j)
            project(j, dst)
            flush(2 + j).start()

    for k in range(1, line.n):
        @pl.when(i == 1 + (k - 1) * steps // line.n)
        def _(k=k):
            job.relay(2, k)

    @pl.when(i > 0)
    def _():
        at = i - 1
        where = pl.ds(pl.multiple_of(at * n, n), n)

        @pl.when(lax.rem(at, per) == 0)
        def _():
            ext[0:8, :] = jnp.zeros((8, width), F32)
            exts[0:8, :] = jnp.zeros((8, 2 * STATE), F32)
            state[...] = jnp.zeros_like(state)

        rows, cols = iotas(n)
        ind = ind_ref[...]
        ext[8 : 8 + n, :] = inner[where, :]
        pre = conv_pre(ext, cp_ref, n)
        x = pre * sigmoid(pre)
        ext[0:8, :] = ext[n : n + 8, :]
        mini = small[where, :]
        exts[8 : 8 + n, :] = mini[:, : 2 * STATE]
        pres = conv_pre(exts, sp_ref, n)
        bc = (pres * sigmoid(pres)).astype(BF16)
        exts[0:8, :] = exts[n : n + 8, :]
        key, query = bc[:, :STATE], bc[:, STATE:]

        _, step, rate, cs, wide_step, wide_cs, wide_tail = scan_prep(mini, hp_ref, ind, n)
        cs2 = cs * LOG2E
        cs2t = cs2.T
        xs = x * wide_step
        half = lax.rem(lax.broadcasted_iota(jnp.int32, xs.shape, 1), 2 * HEAD) < HEAD
        xs0 = jnp.where(half, xs, 0.0)
        xs1 = (xs - xs0).astype(BF16)
        xs0 = xs0.astype(BF16)
        before = state[...]
        low = before.astype(BF16)
        st_ref[0] = low
        carried = mm(query, low) * wide_cs
        xw = (xs * wide_tail).astype(BF16)
        state[...] = before * wide_cs[n - 1 : n, :] + mm(key, xw, TN)
        scores = jnp.where(rows >= cols, mm(query, key, NT), 0.0)
        for pair in range(heads // 2):
            lanes = slice(pair * 2 * HEAD, (pair + 1) * 2 * HEAD)
            mats = []
            for h in (2 * pair, 2 * pair + 1):
                dec = jnp.exp2(jnp.minimum(cs2[:, h : h + 1] - cs2t[h : h + 1, :], 0.0))
                mats.append((scores * dec).astype(BF16))
            local = mm(
                jnp.concatenate(mats, axis=1),
                jnp.concatenate([xs0[:, lanes], xs1[:, lanes]], axis=0),
            )
            ssd_ref[:, lanes] = local + carried[:, lanes] + cp_ref[6:7, lanes] * x[:, lanes]
        gates = gate[where, :]
        gated = ssd_ref[...] * (gates * sigmoid(gates))
        ones = jnp.ones((8, width), BF16)
        top, rest = split16(gated * gated)
        sqs_ref[0] = (mm(ones, top, NT) + mm(ones, rest, NT))[0:1, :]
        scaled_ref[...] = (gated * cp_ref[5:6, :]).astype(BF16)

        span = model // LANES
        share = -(-2 * span // steps)
        for k in range(share):
            b = at * share + k

            @pl.when(b < 2 * span)
            def _(b=b):
                j, col = b // span, lax.rem(b, span)
                slab_rows = slabs.shape[2]
                weight = slabs.at[j]
                piece = block_of(weight, col, slab_rows)
                wt[pl.ds(pl.multiple_of(j * width, width), width), pl.ds(pl.multiple_of(col * LANES, LANES), LANES)] = piece.T

    @pl.when(i == steps)
    def _():
        flush(4).start()
        job.arrive(2)
        flush(5).start()
        for j in range(3):
            job.drain(j)
        for k in range(len(outgoing)):
            flush(k).wait()


def forward(res, stateproj, steps_w, inproj, outt, gain, params, heads, size, layer, out=None):
    tokens_n, model = res.shape
    _, _, rows, width = inproj.shape
    top = 2 * width + 2 * STATE + LANES
    steps = tokens_n // CHUNK
    mid = out is not None
    hbm = pl.BlockSpec(memory_space=pl.ANY)
    chunks = model // SLICE

    def whole(a):
        return pl.BlockSpec(a.shape, lambda i: (0,) * len(a.shape))

    def row(w):
        return pl.BlockSpec((CHUNK, w), lambda i: (jnp.maximum(i - 1, 0), 0))

    args, in_specs, out_specs, out_shape, scratch = [res], [hbm], [], [], []
    if mid:
        args += list(out)
        in_specs += [hbm, hbm, whole(out[2])]
        out_specs += [hbm, whole(out[2])]
        out_shape += [jax.ShapeDtypeStruct(res.shape, F32), jax.ShapeDtypeStruct(out[2].shape, F32)]
        chunk = pltpu.VMEM((chunks, tokens_n // 2, SLICE), BF16)
        scratch += [
            pltpu.VMEM(out[0].shape, BF16),
            pltpu.VMEM(out[1].shape, BF16),
            pltpu.VMEM((2 * chunks, tokens_n // 2, SLICE), BF16),
            chunk, chunk, chunk,
            pltpu.VMEM((4,) + out[2].shape, F32),
            pltpu.VMEM((tokens_n, LANES), F32),
            pltpu.VMEM(res.shape, F32),
            pltpu.SemaphoreType.DMA((3, chunks)),
            pltpu.SemaphoreType.DMA((3, chunks)),
            pltpu.SemaphoreType.DMA((3,)),
            pltpu.SemaphoreType.DMA((3,)),
        ]
    args += [stateproj, steps_w, inproj, outt, gain, *params]
    in_specs += [hbm, hbm, hbm, hbm, whole(gain)] + [whole(v) for v in params]
    out_specs += [
        hbm, pl.BlockSpec((tokens_n, 1), lambda i: (0, 0)), hbm, hbm, hbm, hbm, hbm,
        row(width), row(width),
        pl.BlockSpec((1, 1, CHUNK), lambda i: (jnp.maximum(i - 1, 0), 0, 0)),
        pl.BlockSpec((1, STATE, width), lambda i: (jnp.maximum(i - 1, 0), 0, 0)),
    ]
    out_shape += [
        jax.ShapeDtypeStruct((model, tokens_n), BF16),
        jax.ShapeDtypeStruct((tokens_n, 1), F32),
        jax.ShapeDtypeStruct((tokens_n, 2 * STATE + LANES), F32),
        jax.ShapeDtypeStruct((tokens_n, width), F32),
        jax.ShapeDtypeStruct((tokens_n, width), F32),
        jax.ShapeDtypeStruct((top, model), BF16),
        jax.ShapeDtypeStruct((size, rows, width), BF16),
        jax.ShapeDtypeStruct((tokens_n, width), F32),
        jax.ShapeDtypeStruct((tokens_n, width), BF16),
        jax.ShapeDtypeStruct((steps, 1, CHUNK), F32),
        jax.ShapeDtypeStruct((steps, STATE, width), BF16),
    ]
    scratch += [
        pltpu.VMEM(res.shape, res.dtype),
        pltpu.VMEM((model, 2 * STATE), BF16),
        pltpu.VMEM((top, model), BF16),
        pltpu.VMEM((3, size, rows, width), BF16),
        pltpu.VMEM((tokens_n, model), BF16),
        pltpu.VMEM((model, tokens_n), BF16),
        pltpu.VMEM((tokens_n, 2 * STATE + LANES), F32),
        pltpu.VMEM((tokens_n, width), F32),
        pltpu.VMEM((tokens_n, width), F32),
        pltpu.VMEM((CHUNK + 8, width), F32),
        pltpu.VMEM((CHUNK + 8, 2 * STATE), F32),
        pltpu.VMEM((STATE, width), F32),
        pltpu.VMEM((8, width), F32),
        pltpu.VMEM((8, 2 * STATE), F32),
        pltpu.VMEM((8, LANES), F32),
        pltpu.VMEM((LANES, width), BF16),
        pltpu.SemaphoreType.DMA((3,)),
        pltpu.SemaphoreType.DMA((3, 3, size)),
        pltpu.SemaphoreType.DMA((3, size)),
        pltpu.SemaphoreType.DMA((5,)),
        pltpu.SemaphoreType.DMA((7,)),
    ]
    return pl.pallas_call(
        functools.partial(forward_body, size=size, heads=heads, per=LEN // CHUNK, steps=steps, layer=layer),
        grid=(steps + 1,),
        in_specs=in_specs,
        out_specs=out_specs,
        out_shape=out_shape,
        scratch_shapes=scratch,
        compiler_params=pltpu.CompilerParams(
            collective_id=min(layer, 1), has_side_effects=True, vmem_limit_bytes=VMEM_LIMIT
        ),
        name="forward",
    )(*args)


def back_body(*refs, heads, per, size, steps, layer, last):
    refs = list(refs)

    def take(n):
        got = refs[:n]
        del refs[:n]
        return got

    up_ref, sq_ref, gate_ref, ssd_ref, inner_ref, iprev_ref, small_ref, sprev_ref, st_ref, res_ref, rn_ref = take(11)
    gain_ref = take(1)[0]
    params = take(6)
    wout_hbm, scaled_hbm, wt_hbm, normed_hbm = take(4)
    if not last:
        next_normed, next_steps, next_sdel, next_dcp, next_dsp, next_dhp, next_dgain = take(7)
    new_ref, grad_hbm = take(2)
    if last:
        sdsum_ref, steplow_ref, dcp_ref, dsp_ref, dhp_ref, dgain_ref, mixed_ref = take(7)
    else:
        full_hbm, wide_hbm = take(2)
    ext, exts, cde, cdes, dstate, rq, cp_ref, sp_ref, hp_ref, ind_ref = take(10)
    wout, scaled, wt, turned, dy, glow, ilow, frow, srow, sgot = take(10)
    part, near, away, tpart, got, far, other = take(7)
    load, rsend, rrecv, ssend, srecv, sends, recvs, gsem = take(8)
    if last:
        fgot, opart, ogot, ofar, oother, fsend, frecv, osends, orecvs = take(9)
    else:
        dcp_ref, dsp_ref, dhp_ref, dgain_ref, step_all, sd_all = take(6)
        buffers = take(6)
        sems = take(7)
    assert not refs

    n = CHUNK
    model = up_ref.shape[1]
    i = pl.program_id(0)
    begin_gate = steps
    begin_scan = begin_gate + steps
    begin_norm = begin_scan + steps
    end = begin_norm + steps - 1
    line = Line(size)
    square = Square()
    rows_own = part.shape[2]
    count = part.shape[0]
    job = Scatter(line, part, lambda j: dy.at[pl.ds(j * rows_own, rows_own), :], near, away, ssend, srecv)
    sums = Total(square, tpart, got, far, other, sends, recvs)
    if last:
        outs = Total(square, opart, ogot, ofar, oother, osends, orecvs)
        half = steps * n // 2
        slices = model // SLICE
    else:
        minis = Smalls(line, square, *buffers, sems)
    moves = [(wout_hbm, wout), (scaled_hbm, scaled), (wt_hbm, wt), (normed_hbm, turned)]
    if not last:
        tokens_n = steps * n
        spots = (wt.at[pl.ds(0, model), pl.ds(0, tokens_n)],)
        spots += tuple(
            wt.at[pl.ds(0, tokens_n), pl.ds(tokens_n + at, w)] for at, w in ((0, LANES), (LANES, 2 * STATE))
        )
        moves += [(next_normed, spots[0]), (next_steps, spots[1]), (next_sdel, spots[2])]

    def move(k):
        return pltpu.make_async_copy(*moves[k], load.at[k])

    order = job.order()
    places = len(order)

    def spaced(begin, stop, m):
        return begin + m * (stop - begin) // places

    middle = begin_scan + steps // 2
    folds = [(spaced(begin_scan - steps // 2, middle, m), 0, p) for m, p in enumerate(order)]
    folds += [(spaced(middle, begin_norm, m), 1, p) for m, p in enumerate(order)]

    def column(row):
        return jnp.broadcast_to(row, (n, n)).T[:, 0:1]

    @pl.when(i == 0)
    def _():
        for k in range(3):
            move(k).start()
        put_params(cp_ref, sp_ref, hp_ref, ind_ref, layer, params)
        rq[...] = jnp.zeros_like(rq)
        line.greet_all(pltpu.get_barrier_semaphore(), square.others())
        if last:
            rows = [
                remote(sq_ref, fgot.at[square.me], fsend.at[k], frecv.at[k], who)
                for k, who in enumerate(square.others())
            ]
            for copy in rows:
                copy.start()
            fgot[square.me] = sq_ref[...]
            move(0).wait()
            move(1).wait()
            for c in range(slices):
                value = mm(scaled[...], wout[c * SLICE : (c + 1) * SLICE, :], NT).astype(BF16)
                opart[2 * c] = value[:half]
                opart[2 * c + 1] = value[half:]
                outs.step(0, c)
            outs.step(1, 0)
            for copy in rows:
                copy.wait()
            total = (fgot[0] + fgot[1]) + (fgot[2] + fgot[3])
        else:
            total = sq_ref[...]
            move(0).wait()
            move(1).wait()
        dcp_ref[...] = jnp.zeros_like(dcp_ref)
        dsp_ref[...] = jnp.zeros_like(dsp_ref)
        dhp_ref[...] = jnp.zeros_like(dhp_ref)
        dgain_ref[...] = jnp.zeros_like(dgain_ref)
        frow[...] = lax.rsqrt(total / INNER + EPS)

    ind = ind_ref[...]
    for at, j, p in folds:
        @pl.when(i == at)
        def _(j=j, p=p):
            job.fold(j, p)

    @pl.when(i < begin_gate)
    def _():
        rows = pl.ds(pl.multiple_of(i * n, n), n)
        low = (column(frow[i]) * up_ref[...].astype(F32)).astype(BF16)
        turned[:, rows] = low.T
        sd = mm(low, wout[...])
        dy[rows, :] = sd
        piece = scaled[rows, :]
        top, rest = split16(piece.astype(F32) * sd)
        ones = jnp.ones((8, sd.shape[1]), BF16)
        srow[i] = (mm(ones, top, NT) + mm(ones, rest, NT))[0:1, :]

    @pl.when(i == begin_gate - 1)
    def _():
        copies = [
            remote(srow, sgot.at[square.me], rsend.at[k], rrecv.at[k], who) for k, who in enumerate(square.others())
        ]
        for copy in copies:
            copy.start()
        job.emit(0, turned, scaled)
        move(3).start()
        sgot[square.me] = srow[...]
        for copy in copies:
            copy.wait()
        srow[...] = (sgot[0] + sgot[1]) + (sgot[2] + sgot[3])

    if last:
        @pl.when(i == steps // 2)
        def _():
            outs.step(1, 1)

        @pl.when((i >= begin_gate) & (i < begin_gate + slices - 2))
        def _():
            outs.step(1, i - begin_gate + 2)

    @pl.when((i >= begin_gate) & (i < begin_scan))
    def _():
        c = i - begin_gate
        rows = pl.ds(pl.multiple_of(c * n, n), n)
        coef = column(frow[c] * frow[c] * srow[c]) / INNER
        gate = gate_ref[...]
        gsig = sigmoid(gate)
        gact = gate * gsig
        ssd = ssd_ref[...]
        sd = dy[rows, :]
        gated = ssd * gact
        gd = cp_ref[5:6, :] * sd - coef * gated
        dcp_ref[5:6, :] += colsum(gated * sd)
        dy[rows, :] = gd * gact
        glow[rows, :] = (gd * ssd * (gsig + gact * (1.0 - gsig))).astype(BF16)

    @pl.when(i == begin_scan - 1)
    def _():
        move(3).wait()
        job.emit(1, turned, glow)
        move(2).wait()

    @pl.when((i >= begin_scan) & (i < begin_norm))
    def _():
        q = i - begin_scan
        chunk = steps - 1 - q
        where = pl.ds(pl.multiple_of(chunk * n, n), n)

        @pl.when(lax.rem(chunk, per) == per - 1)
        def _():
            cde[n : n + 8, :] = jnp.zeros((8, cde.shape[1]), F32)
            cdes[n : n + 8, :] = jnp.zeros((8, cdes.shape[1]), F32)
            dstate[...] = jnp.zeros_like(dstate)

        keep = jnp.where(lax.rem(chunk, per) == 0, 0.0, 1.0).astype(F32)
        rows, cols = iotas(n)
        ext[0:8, :] = iprev_ref[...] * keep
        ext[8 : 8 + n, :] = inner_ref[...]
        exts[0:8, :] = sprev_ref[:, : 2 * STATE] * keep
        exts[8 : 8 + n, :] = small_ref[:, : 2 * STATE]
        pre = conv_pre(ext, cp_ref, n)
        sig = sigmoid(pre)
        x = pre * sig
        slope = sig + x * (1.0 - sig)
        pres = conv_pre(exts, sp_ref, n)
        sigs = sigmoid(pres)
        acts = pres * sigs
        slopes = sigs + acts * (1.0 - sigs)
        bc = acts.astype(BF16)
        key, query = bc[:, :STATE], bc[:, STATE:]
        dyc = dy[where, :]

        raw, step, rate, cs, wide_step, wide_cs, wide_tail = scan_prep(small_ref, hp_ref, ind, n)
        cs2 = cs * LOG2E
        cs2t = cs2.T
        xs = x * wide_step
        xsb = xs.astype(BF16)
        half = lax.rem(lax.broadcasted_iota(jnp.int32, xs.shape, 1), 2 * HEAD) < HEAD
        dy0 = jnp.where(half, dyc, 0.0)
        dy1 = (dyc - dy0).astype(BF16)
        dy0 = dy0.astype(BF16)
        low = st_ref[0]
        dst = dstate[...]
        dlow = dst.astype(BF16)
        dye = dyc * wide_cs
        dyeb = dye.astype(BF16)
        up = headsum(dye * mm(query, low), ind)
        dxs_state = wide_tail * mm(key, dlow)
        down = headsum(xs * dxs_state, ind)
        qdel = mm(dyeb, low, NT)
        kdel = mm((xs * wide_tail).astype(BF16), dlow, NT)
        through = headsum(jnp.broadcast_to(colsum(low.astype(F32) * dst), (8, dst.shape[1])), ind)[0:1, :]
        through = through * jnp.exp(cs[n - 1 : n, :])
        dstate[...] = dst * wide_cs[n - 1 : n, :] + mm(query, dyeb, TN)

        scores = jnp.where(rows <= cols, mm(key, query, NT), 0.0)
        dscores = jnp.zeros((n, n), F32)
        quads = []
        dxs = []
        for pair in range(heads // 2):
            lanes = slice(pair * 2 * HEAD, (pair + 1) * 2 * HEAD)
            stacked = jnp.concatenate([dy0[:, lanes], dy1[:, lanes]], axis=0)
            both = mm(xsb[:, lanes], stacked, NT)
            mats = []
            for which, h in enumerate((2 * pair, 2 * pair + 1)):
                dec = jnp.exp2(jnp.minimum(cs2t[h : h + 1, :] - cs2[:, h : h + 1], 0.0))
                mats.append((scores * dec).astype(BF16))
                term = dec * both[:, which * n : (which + 1) * n]
                dscores = dscores + term
                quads.append((scores * term).astype(BF16))
                rq[h : h + 1, :] = colsum(quads[-1].astype(F32))
            dxs.append(mm(jnp.concatenate(mats, axis=1), stacked))
        dxs = jnp.concatenate(dxs, axis=1) + dxs_state
        head_row = lax.broadcasted_iota(jnp.int32, (heads * n, LANES), 0) // n
        head_lane = lax.broadcasted_iota(jnp.int32, (heads * n, LANES), 1)
        colq = mm(jnp.concatenate(quads, axis=1), jnp.where(head_row == head_lane, 1.0, 0.0).astype(BF16))
        dscores = jnp.where(rows <= cols, dscores, 0.0).astype(BF16)
        kdel = kdel + mm(dscores, query)
        qdel = qdel + mm(dscores, key, TN)

        upper = jnp.where(rows <= cols, 1.0, 0.0).astype(F32)
        strict = jnp.where(rows > cols, 1.0, 0.0).astype(F32)
        da = mm(upper, rq[...].T - colq + up, precision=HIGH) + mm(strict, down, precision=HIGH) + through
        grown = headsum(x * dxs, ind) + rate * da
        step_pre = grown * sigmoid(raw)
        steplow = step_pre.astype(BF16)
        if last:
            steplow_ref[...] = steplow
        else:
            step_all[where, :] = steplow
        dhp_ref[0:1, :] += colsum(step_pre)
        dhp_ref[1:2, :] += rate * colsum(step * da)
        dcp_ref[6:7, :] += colsum(dyc * x)

        cd = (dxs * wide_step + cp_ref[6:7, :] * dyc) * slope
        cde[0:n, :] = cd
        total = cp_ref[3:4, :] * cd
        for tap in range(3):
            total = total + cp_ref[tap : tap + 1, :] * cde[3 - tap : 3 - tap + n, :]
        inner_low = total.astype(BF16)
        ilow[where, :] = inner_low
        for tap in range(4):
            dcp_ref[tap : tap + 1, :] += colsum(cd * ext[5 + tap : 5 + tap + n, :])
        dcp_ref[4:5, :] += colsum(cd)
        cde[n : n + 8, :] = cde[0:8, :]

        cds = jnp.concatenate([kdel, qdel], axis=1) * slopes
        cdes[0:n, :] = cds
        total = sp_ref[3:4, :] * cds
        for tap in range(3):
            total = total + sp_ref[tap : tap + 1, :] * cdes[3 - tap : 3 - tap + n, :]
        sdel = total.astype(BF16)
        for tap in range(4):
            dsp_ref[tap : tap + 1, :] += colsum(cds * exts[5 + tap : 5 + tap + n, :])
        dsp_ref[4:5, :] += colsum(cds)
        cdes[n : n + 8, :] = cdes[0:8, :]

        lows = jnp.concatenate([inner_low, glow[where, :], sdel, steplow], axis=1)
        value = mm(lows, wt[...]).astype(BF16)
        tpart[2 * q, :, :model] = value[: n // 2]
        tpart[2 * q + 1, :, :model] = value[n // 2 :]
        tpart[2 * q, :, model:] = sdel[: n // 2]
        tpart[2 * q + 1, :, model:] = sdel[n // 2 :]
        sums.step(0, q)

    @pl.when((i > begin_scan) & (i <= begin_norm))
    def _():
        sums.step(1, i - begin_scan - 1)

    @pl.when((i >= begin_scan + 3) & (i < begin_norm + 3))
    def _():
        sums.step(2, i - begin_scan - 3)

    @pl.when((i >= begin_scan + 4) & (i < begin_norm + 4))
    def _():
        sums.step(3, i - begin_scan - 4)

    if last:
        @pl.when((i > begin_scan) & (i <= begin_scan + slices))
        def _():
            outs.step(2, i - begin_scan - 1)

        @pl.when((i > begin_scan + 1) & (i <= begin_scan + slices + 1))
        def _():
            outs.step(3, i - begin_scan - 2)

    @pl.when(i == begin_norm - 1)
    def _():
        dhp_ref[2:3, :] = headsum(jnp.broadcast_to(dcp_ref[6:7, :], (8, dcp_ref.shape[1])), ind)[0:1, :]
        job.emit(2, turned, ilow, None if last else places // 2)
        if not last:
            for k in (4, 5, 6):
                move(k).start()

    if not last:
        @pl.when(i == begin_norm + 1)
        def _():
            for k in (4, 5, 6):
                move(k).wait()
            put_pack(
                buffers[0].at[1], square.me, *spots, next_dcp[...], next_dsp[...], next_dhp[...], next_dgain[...]
            )
            minis.sum.start(1)

    @pl.when(i >= begin_norm)
    def _():
        r = i - begin_norm
        chunk = steps - 1 - r
        if last:
            fac = column(frow[chunk])
            side = chunk // (steps // 2)
            base = (chunk - side * (steps // 2)) * n
        for h in range(2):
            rows = slice(h * (n // 2), (h + 1) * (n // 2))
            back = tpart[2 * r + h, :, :model].astype(F32)
            sdel = tpart[2 * r + h, :, model:]
            if last:
                sdsum_ref[rows, :] = sdel
            else:
                sd_all[pl.ds(pl.multiple_of(chunk * n + h * (n // 2), n // 2), n // 2), :] = sdel
            res = res_ref[rows, :].astype(F32)
            rn = rn_ref[rows, :]
            dgain_ref[...] += colsum(back * res * rn)
            gained = back * gain_ref[layer : layer + 1, :]
            mean = jnp.sum(gained * res, axis=1, keepdims=True) / model
            new_ref[rows, :] = up_ref[rows, :].astype(F32) + rn * gained - (rn * rn * rn * mean) * res
            if last:
                where = pl.ds(pl.multiple_of(base + h * (n // 2), n // 2), n // 2)
                for c in range(slices):
                    span = slice(c * SLICE, (c + 1) * SLICE)
                    summed = opart[2 * c + side, where, :].astype(F32)
                    mixed_ref[rows, span] = (res[:, span] + fac[rows, :] * summed).astype(BF16)

    @pl.when(i == end)
    def _():
        def finish(j):
            job.finish(j)
            pltpu.make_async_copy(dy.at[pl.ds(j * rows_own, rows_own), :], grad_hbm.at[j], gsem.at[j]).start()

        early = order if last else order[: places // 2]
        if not last:
            put_pack(
                buffers[0].at[0], square.me, turned, step_all, sd_all, dcp_ref[...], dsp_ref[...], dhp_ref[...], dgain_ref[...]
            )
            minis.sum.start(0)
            for p in order[places // 2 :]:
                job.cross(2, p).start()
        for p in early:
            job.fold(2, p)
        finish(0)
        finish(1)
        if not last:
            minis.fold()
            minis.turn()
            for k in range(1, line.n):
                minis.relay(k)
            for p in order[places // 2 :]:
                job.fold(2, p)
            minis.cross()
        finish(2)
        if not last:
            minis.cross_on()
            minis.end()
            tails = [
                pltpu.make_async_copy(src, dst, load.at[k])
                for k, (src, dst) in enumerate(((minis.full, full_hbm), (minis.wide, wide_hbm)))
            ]
            for copy in tails:
                copy.start()
        for j in range(count):
            job.drain(j)
            pltpu.make_async_copy(dy.at[pl.ds(j * rows_own, rows_own), :], grad_hbm.at[j], gsem.at[j]).wait()
        if not last:
            for copy in tails:
                copy.wait()


def back(up, sq, gate_pre, ssd, inner_raw, small, states, res, rnorm, gain, params,
         wout, scaled, wt, normed, heads, size, layer, after=None):
    tokens_n, width = inner_raw.shape
    model = up.shape[1]
    last = after is None
    steps = tokens_n // CHUNK
    begin_scan = 2 * steps
    begin_norm = begin_scan + steps
    rows = model // size
    n = size // 2
    hbm = pl.BlockSpec(memory_space=pl.ANY)
    top = steps - 1

    def norm_at(i):
        return jnp.where(i < begin_norm, top, top - (i - begin_norm))

    def scan_at(i):
        return jnp.clip(top - (i - begin_scan), 0, top)

    def first(w):
        return pl.BlockSpec((CHUNK, w), lambda i: (jnp.where(i < steps, i, norm_at(i)), 0))

    def second(w):
        return pl.BlockSpec((CHUNK, w), lambda i: (jnp.clip(i - steps, 0, top), 0))

    def scan(w):
        return pl.BlockSpec((CHUNK, w), lambda i: (scan_at(i), 0))

    def prev(w):
        return pl.BlockSpec((8, w), lambda i: (jnp.maximum(scan_at(i) * (CHUNK // 8) - 1, 0), 0))

    def norm(w):
        return pl.BlockSpec((CHUNK, w), lambda i: (norm_at(i), 0))

    def whole(a):
        return pl.BlockSpec(a.shape, lambda i: (0,) * len(a.shape))

    extra = model + 2 * STATE
    quarter = pltpu.VMEM((steps, CHUNK // 2, extra), BF16)
    pieces = pltpu.VMEM((3, n, rows, width), BF16)
    args = [up, sq, gate_pre, ssd, inner_raw, inner_raw, small, small, states, res, rnorm, gain, *params,
            wout, scaled, wt, normed]
    in_specs = [
        first(model), whole(sq), second(width), second(width),
        scan(width), prev(width), scan(small.shape[1]), prev(small.shape[1]),
        pl.BlockSpec((1, STATE, width), lambda i: (scan_at(i), 0, 0)),
        norm(model), norm(1), whole(gain),
    ] + [whole(a) for a in params] + [hbm] * 4
    out_specs = [norm(model), hbm]
    out_shape = [jax.ShapeDtypeStruct((tokens_n, model), F32), jax.ShapeDtypeStruct((3, rows, width), F32)]
    totals = [(8, width), (8, 2 * STATE), (8, LANES), (1, model)]
    scratch = [
        pltpu.VMEM((CHUNK + 8, width), F32),
        pltpu.VMEM((CHUNK + 8, 2 * STATE), F32),
        pltpu.VMEM((CHUNK + 8, width), F32),
        pltpu.VMEM((CHUNK + 8, 2 * STATE), F32),
        pltpu.VMEM((STATE, width), F32),
        pltpu.VMEM((LANES, CHUNK), F32),
        pltpu.VMEM((8, width), F32),
        pltpu.VMEM((8, 2 * STATE), F32),
        pltpu.VMEM((8, LANES), F32),
        pltpu.VMEM((LANES, width), BF16),
        pltpu.VMEM(wout.shape, BF16),
        pltpu.VMEM(scaled.shape, BF16),
        pltpu.VMEM(wt.shape, BF16),
        pltpu.VMEM(normed.shape, BF16),
        pltpu.VMEM((tokens_n, width), F32),
        pltpu.VMEM((tokens_n, width), BF16),
        pltpu.VMEM((tokens_n, width), BF16),
        pltpu.VMEM((steps, 1, CHUNK), F32),
        pltpu.VMEM((steps, 1, CHUNK), F32),
        pltpu.VMEM((4, steps, 1, CHUNK), F32),
        pltpu.VMEM((3, size, rows, width), BF16), pieces, pieces,
        pltpu.VMEM((2 * steps, CHUNK // 2, extra), BF16), quarter, quarter, quarter,
        pltpu.SemaphoreType.DMA((7,)),
        pltpu.SemaphoreType.DMA((3,)),
        pltpu.SemaphoreType.DMA((3,)),
        pltpu.SemaphoreType.DMA((2, 3, n)),
        pltpu.SemaphoreType.DMA((2, 3, n)),
        pltpu.SemaphoreType.DMA((3, steps)),
        pltpu.SemaphoreType.DMA((3, steps)),
        pltpu.SemaphoreType.DMA((3,)),
    ]
    if last:
        out_specs += [norm(2 * STATE), scan(LANES)]
        out_specs += [pl.BlockSpec(v, lambda i: (0, 0)) for v in totals] + [norm(model)]
        out_shape += [
            jax.ShapeDtypeStruct((tokens_n, 2 * STATE), BF16),
            jax.ShapeDtypeStruct((tokens_n, LANES), BF16),
        ]
        out_shape += [jax.ShapeDtypeStruct(v, F32) for v in totals]
        out_shape.append(jax.ShapeDtypeStruct((tokens_n, model), BF16))
        slices = model // SLICE
        chunk = pltpu.VMEM((slices, tokens_n // 2, SLICE), BF16)
        scratch += [
            pltpu.VMEM((4, steps, 1, CHUNK), F32),
            pltpu.VMEM((2 * slices, tokens_n // 2, SLICE), BF16), chunk, chunk, chunk,
            pltpu.SemaphoreType.DMA((3,)),
            pltpu.SemaphoreType.DMA((3,)),
            pltpu.SemaphoreType.DMA((3, slices)),
            pltpu.SemaphoreType.DMA((3, slices)),
        ]
    else:
        w = 2 * STATE
        r = pack_rows(size)
        args += list(after)
        in_specs += [hbm] * 3 + [whole(v) for v in after[3:]]
        out_specs += [hbm, hbm]
        out_shape += [
            jax.ShapeDtypeStruct((2, size, r, w), BF16),
            jax.ShapeDtypeStruct((4, 2, SPAN, w), BF16),
        ]
        scratch += [pltpu.VMEM(v, F32) for v in totals]
        scratch += [pltpu.VMEM((tokens_n, LANES), BF16), pltpu.VMEM((tokens_n, w), BF16)]
        scratch += smalls_scratch(size, w, 2)
    return pl.pallas_call(
        functools.partial(
            back_body, heads=heads, per=LEN // CHUNK, size=size, steps=steps, layer=layer, last=last
        ),
        grid=(begin_norm + steps,),
        in_specs=in_specs,
        out_specs=out_specs,
        out_shape=out_shape,
        scratch_shapes=scratch,
        compiler_params=pltpu.CompilerParams(
            collective_id=2 if last else 3, has_side_effects=True, vmem_limit_bytes=VMEM_LIMIT
        ),
        name="back",
    )(*args)


def unpack_body(full_ref, wide_ref, *refs, layers, heads):
    step_ref, state_ref, conv_ref, bias_ref, convs_ref, biass_ref = refs[:6]
    stepbias_ref, decay_ref, skip_ref, norm_ref, gain_ref = refs[6:]
    model = state_ref.shape[1]
    quarter = model // 4
    w = state_ref.shape[2]
    width = conv_ref.shape[2]
    for layer in range(layers):
        for t in range(4):
            state_ref[layer, t * quarter : (t + 1) * quarter, :] = wide_ref[t, layer, :quarter, :].astype(F32)
        taps = [wide_ref[t, layer, quarter : quarter + 16, :].astype(F32) for t in range(4)]
        taps = (taps[0] + taps[1]) + (taps[2] + taps[3])
        convs_ref[layer] = taps[0:4]
        biass_ref[layer : layer + 1, :] = taps[4:5]
        flat = full_ref[layer].reshape(-1, w)[:PACK].astype(F32)
        at = quarter + 16
        for b in range(model // w):
            step_ref[layer, :, b * w : (b + 1) * w] = flat[at : at + 16]
            at += 16
        for b in range(width // w):
            lanes = slice(b * w, (b + 1) * w)
            rows = flat[at + 8 * b : at + 8 * b + 8]
            conv_ref[layer, :, lanes] = rows[0:4]
            bias_ref[layer : layer + 1, lanes] = rows[4:5]
            norm_ref[layer : layer + 1, lanes] = rows[5:6]
        at += 8 * (width // w)
        for k, ref in enumerate((stepbias_ref, decay_ref, skip_ref)):
            ref[layer : layer + 1, :] = flat[at + k : at + k + 1, :heads]
        at += 8
        for b in range(model // w):
            gain_ref[layer : layer + 1, b * w : (b + 1) * w] = flat[at + b : at + b + 1]


def unpack(full, wide, model, width, heads):
    layers, w = full.shape[0], full.shape[3]
    vm = pl.BlockSpec(memory_space=pltpu.VMEM)
    shapes = [
        (layers, 16, model), (layers, model, w), (layers, 4, width), (layers, width), (layers, 4, w), (layers, w),
        (layers, heads), (layers, heads), (layers, heads), (layers, width), (layers, model),
    ]
    return pl.pallas_call(
        functools.partial(unpack_body, layers=layers, heads=heads),
        in_specs=[vm, vm],
        out_specs=[vm] * len(shapes),
        out_shape=[jax.ShapeDtypeStruct(v, F32) for v in shapes],
        compiler_params=pltpu.CompilerParams(vmem_limit_bytes=VMEM_LIMIT),
        name="unpack",
    )(full, wide)


def shards(
    tokens, inproj, stepproj, stateproj, outproj, convinner, biasinner, convstate, biasstate,
    stepbias, decaylog, skipgain, normgain, inputgain, cotangent,
):
    layers = inproj.shape[0]
    width = inproj.shape[3]
    heads = stepproj.shape[2]
    model = tokens.shape[1]
    pad = LANES - heads
    size = lax.axis_size("dp")
    steps_w = jnp.pad(jnp.swapaxes(stepproj, 1, 2), ((0, 0), (0, pad), (0, 0)))
    head = jnp.pad(jnp.stack([stepbias, decaylog, skipgain], axis=1), ((0, 0), (0, 5), (0, pad)))
    outt = jnp.swapaxes(outproj, 1, 2)
    params = (convinner, biasinner, normgain, convstate, biasstate, head)

    residual = tokens
    kept = []
    out = None
    for at in range(layers):
        results = forward(residual, stateproj, steps_w, inproj, outt, inputgain, params, heads, size, at, out=out)
        if at:
            residual, kept[-1][-1] = results[:2]
            results = results[2:]
        normed, rnorm, small, inner_raw, gate_pre, wt, w_out, ssd, scaled, sq, states = results
        w_out = w_out.reshape(model, width)
        kept.append([residual, normed, rnorm, small, inner_raw, gate_pre, wt, w_out, ssd, scaled, states, sq])
        out = (scaled, w_out, sq)

    assert layers == 2
    before, normed, rnorm, small, inner_raw, gate_pre, wt, w_out, ssd, scaled, states, sq = kept[1]
    upstream, second, sdel, steplow, *totals, mixed = back(
        cotangent, sq, gate_pre, ssd, inner_raw, small, states, before, rnorm, inputgain, params,
        w_out, scaled, wt, normed, heads, size, 1,
    )
    after = (normed, steplow, sdel, *totals)
    before, normed, rnorm, small, inner_raw, gate_pre, wt, w_out, ssd, scaled, states, sq = kept[0]
    upstream, first, full, wide = back(
        upstream, sq, gate_pre, ssd, inner_raw, small, states, before, rnorm, inputgain, params,
        w_out, scaled, wt, normed, heads, size, 0, after=after,
    )
    pieces = [first, second]
    (
        step_grad, state_grad, conv_grad, bias_grad, convs_grad, biass_grad,
        stepbias_grad, decay_grad, skip_grad, norm_grad, gain_grad,
    ) = unpack(full, wide, model, width, heads)
    return (
        mixed,
        upstream,
        jnp.stack([v[1:] for v in pieces]),
        jnp.swapaxes(step_grad[:, :heads], 1, 2),
        state_grad,
        jnp.swapaxes(jnp.stack([v[0] for v in pieces]), 1, 2),
        conv_grad,
        bias_grad,
        convs_grad,
        biass_grad,
        stepbias_grad,
        decay_grad,
        skip_grad,
        norm_grad,
        gain_grad,
    )


def solution(mesh):
    in_specs = (
        P("dp", None),
        P(None, None, "dp", "tensor"),
        P(None, None, "tensor"),
        P(),
        P(None, "tensor", "dp"),
        P(None, None, "tensor"),
        P(None, "tensor"),
        P(),
        P(),
        P(None, "tensor"),
        P(None, "tensor"),
        P(None, "tensor"),
        P(None, "tensor"),
        P(),
        P("dp", None),
    )
    out_specs = (
        P("dp", None),
        P("dp", None),
        P(None, None, "dp", "tensor"),
        P(None, None, "tensor"),
        P(),
        P(None, "tensor", "dp"),
        P(None, None, "tensor"),
        P(None, "tensor"),
        P(),
        P(),
        P(None, "tensor"),
        P(None, "tensor"),
        P(None, "tensor"),
        P(None, "tensor"),
        P(),
    )
    return jax.shard_map(shards, mesh=mesh, in_specs=in_specs, out_specs=out_specs, check_vma=False)
```

```python
import functools
import math

import jax
import jax.numpy as jnp
from jax import lax
from jax.experimental import pallas as pl
from jax.experimental.pallas import tpu as pltpu
from jax.sharding import PartitionSpec as P

STATE = 128
LEN = 1024
INNER = 3072
HEAD = 64
CHUNK = 128
SLICE = 256
TILE = 256
PACK = 544
SPAN = 400
VMEM_LIMIT = 65000 * 1024
LANES = 128
EPS = 1e-05
LOG2E = 1.4426950408889634

HIGH = lax.Precision.HIGHEST
NN = (((1,), (0,)), ((), ()))
NT = (((1,), (1,)), ((), ()))
TN = (((0,), (0,)), ((), ()))
F32 = jnp.float32
BF16 = jnp.bfloat16
MESH = pl.DeviceIdType.MESH


def remote(src, dst, send, recv, where):
    return pltpu.make_async_remote_copy(
        src_ref=src, dst_ref=dst, send_sem=send, recv_sem=recv, device_id=where, device_id_type=MESH
    )


class Line:
    def __init__(self, size):
        self.n = size // 2
        me = lax.axis_index("dp")
        self.me = me
        self.at = me // 2
        self.side = lax.rem(me, 2)
        self.pair = {"dp": me + 1 - 2 * self.side}
        self.right = {"dp": jnp.minimum(me + 2, size - 1)}
        self.left = {"dp": jnp.maximum(me - 2, 0)}
        odd = lax.rem(self.at, 2)
        self.odd = odd == 1
        self.near = {"dp": me + 2 - 4 * odd}
        self.has_left = self.at > 0
        self.has_right = self.at < self.n - 1

    def greet(self, barrier, more=()):
        for who in more:
            pl.semaphore_signal(barrier, inc=1, device_id=who, device_id_type=MESH)
        pl.semaphore_signal(barrier, inc=1, device_id=self.pair, device_id_type=MESH)

        @pl.when(self.has_left)
        def _():
            pl.semaphore_signal(barrier, inc=1, device_id=self.left, device_id_type=MESH)

        @pl.when(self.has_right)
        def _():
            pl.semaphore_signal(barrier, inc=1, device_id=self.right, device_id_type=MESH)

        peers = 1 + len(more) + self.has_left.astype(jnp.int32) + self.has_right.astype(jnp.int32)
        pl.semaphore_wait(barrier, peers)

    def greet_all(self, barrier, more=()):
        for who in list(more) + [self.pair]:
            pl.semaphore_signal(barrier, inc=1, device_id=who, device_id_type=MESH)
        for i in range(self.n):
            @pl.when(i != self.at)
            def _(i=i):
                pl.semaphore_signal(barrier, inc=1, device_id={"dp": 2 * i + self.side}, device_id_type=MESH)
        pl.semaphore_wait(barrier, self.n + len(more))


def upper(rows):
    return max(16, rows // 32 * 16)


class Gather:
    def __init__(self, line, own, full, keep, send, recv):
        self.line, self.own, self.full, self.keep, self.send, self.recv = line, own, full, keep, send, recv
        self.rows = full.shape[2]
        self.cut = upper(self.rows)

    def copy(self, j, slab, way, src=None, rest=False):
        where = (self.line.right, self.line.left, self.line.pair)[way]
        dst = self.full.at[j, slab]
        if rest:
            dst = self.full.at[j, slab, pl.ds(self.cut, self.rows - self.cut)]
        return remote(dst if src is None else src, dst, self.send.at[j, way, slab], self.recv.at[j, slab], where)

    def shared(self, j, slab, owner):
        part = self.full.at[j, slab, pl.ds(0, self.cut)]
        return remote(part, part, self.send.at[j, 0, slab], self.recv.at[j, owner], self.line.near)

    def start(self, j):
        line = self.line
        pltpu.make_async_copy(self.own(j), self.full.at[j, line.me], self.keep.at[j]).start()

        @pl.when(line.has_right)
        def _():
            self.copy(j, line.me, 0, self.own(j)).start()

        @pl.when(line.has_left)
        def _():
            self.copy(j, line.me, 1, self.own(j)).start()

        self.copy(j, line.me, 2, self.own(j)).start()

    def relay(self, j, k):
        line = self.line

        def forward(slab, way, go_on, near):
            self.copy(j, slab, way).wait_recv()

            @pl.when(go_on)
            def _():
                self.copy(j, slab, way).start()

            if k > 1:
                self.copy(j, slab, 2).start()
            else:
                @pl.when(near)
                def _():
                    self.copy(j, slab, 2, rest=True).start()

                @pl.when(jnp.logical_not(near))
                def _():
                    self.copy(j, slab, 2).start()

        @pl.when(line.at >= k)
        def _():
            forward(line.me - 2 * k, 0, line.has_right, line.odd)

        @pl.when(line.at + k < line.n)
        def _():
            forward(line.me + 2 * k, 1, line.has_left, jnp.logical_not(line.odd))

        if k == 1:
            slab = line.me + 1 - 2 * line.side
            self.copy(j, slab, 2).wait_recv()
            self.shared(j, slab, line.near["dp"]).start()

    def near_slab(self):
        line = self.line
        return line.near["dp"] + 1 - 2 * line.side

    def arrive(self, j):
        line = self.line
        pltpu.make_async_copy(self.own(j), self.full.at[j, line.me], self.keep.at[j]).wait()
        self.copy(j, self.near_slab(), 2, rest=True).wait_recv()
        self.shared(j, self.near_slab(), line.me).wait_recv()
        for place in range(line.n):
            slab = 2 * place + 1 - line.side

            @pl.when((slab != self.near_slab()) & (place != line.at))
            def _(slab=slab):
                self.copy(j, slab, 2).wait_recv()

    def drain(self, j):
        line = self.line
        self.shared(j, line.me + 1 - 2 * line.side, line.near["dp"]).wait_send()
        for place in range(line.n):
            slab = 2 * place + line.side
            near = slab == line.near["dp"]

            @pl.when(near)
            def _(slab=slab):
                self.copy(j, slab, 2, rest=True).wait_send()

            @pl.when(jnp.logical_not(near))
            def _(slab=slab):
                self.copy(j, slab, 2).wait_send()

            @pl.when(line.has_right & (place <= line.at))
            def _(slab=slab):
                self.copy(j, slab, 0).wait_send()

            @pl.when(line.has_left & (place >= line.at))
            def _(slab=slab):
                self.copy(j, slab, 1).wait_send()


class Square:
    def __init__(self):
        me = lax.axis_index("tensor")
        self.me = me
        self.half = lax.rem(me, 2)
        self.mate = {"tensor": me + 1 - 2 * self.half}
        self.across = {"tensor": lax.rem(me + 2, 4)}

    def others(self):
        return [{"tensor": lax.rem(self.me + k, 4)} for k in (1, 2, 3)]


class Total:
    def __init__(self, square, part, got, far, other, send, recv):
        self.square, self.part, self.got, self.far, self.other = square, part, got, far, other
        self.send, self.recv = send, recv

    def first(self, c):
        sq = self.square
        return remote(
            self.part.at[2 * c + 1 - sq.half], self.got.at[c], self.send.at[0, c], self.recv.at[0, c], sq.mate
        )

    def second(self, c):
        sq = self.square
        return remote(self.part.at[2 * c + sq.half], self.far.at[c], self.send.at[1, c], self.recv.at[1, c], sq.across)

    def third(self, c):
        sq = self.square
        return remote(self.part.at[2 * c + sq.half], self.other.at[c], self.send.at[2, c], self.recv.at[2, c], sq.mate)

    def step(self, kind, c):
        slot = 2 * c + self.square.half
        if kind == 0:
            self.first(c).start()
        elif kind == 1:
            self.first(c).wait_recv()
            self.part[slot] = (self.part[slot].astype(F32) + self.got[c].astype(F32)).astype(BF16)
            self.second(c).start()
        elif kind == 2:
            self.second(c).wait()
            self.part[slot] = (self.part[slot].astype(F32) + self.far[c].astype(F32)).astype(BF16)
            self.third(c).start()
        else:
            self.third(c).wait_recv()
            self.first(c).wait_send()
            self.third(c).wait_send()
            self.part[2 * c + 1 - self.square.half] = self.other[c]


class Scatter:
    def __init__(self, line, part, out, near, far, send, recv):
        self.line, self.part, self.out, self.near, self.far = line, part, out, near, far
        self.send, self.recv = send, recv
        self.rows = part.shape[2]
        self.cut = upper(self.rows)
        n = line.n
        self.masks = [1] + list(range(n - 1, 1, -1)) + [0]
        self.an_end = (line.at == 0) | (line.at == n - 1)
        self.by_end = (line.at == 1) | (line.at == n - 2)

    def place(self, mask):
        at = self.line.at
        bit, result = 1, at
        while bit <= mask:
            if mask & bit:
                result = result + bit - 2 * bit * lax.rem(at // bit, 2)
            bit *= 2
        return result

    def cross(self, j, m):
        line = self.line
        slab = 2 * self.place(self.masks[m]) + 1 - line.side
        src, dst = self.part.at[j, slab], self.near.at[j, m]
        if self.masks[m] == 1:
            rest = pl.ds(self.cut, self.rows - self.cut)
            src, dst = self.part.at[j, slab, rest], self.near.at[j, m, rest]
        return remote(src, dst, self.send.at[0, j, m], self.recv.at[0, j, m], line.pair)

    def shared(self, j):
        line = self.line
        slab = line.near["dp"] + 1 - 2 * line.side
        some = pl.ds(0, self.cut)
        return remote(
            self.part.at[j, slab, some], self.near.at[j, 0, some], self.send.at[2, j, 0], self.recv.at[2, j, 0], line.near
        )

    def straight(self, j, mask):
        line = self.line
        slab = 2 * self.place(mask) + line.side
        return remote(
            self.part.at[j, slab], self.far.at[j, mask - 1], self.send.at[1, j, mask - 1], self.recv.at[1, j, mask - 1],
            {"dp": slab},
        )

    def through(self, j):
        line = self.line
        n = line.n
        slab = 2 * self.place(n - 1) + line.side
        return remote(
            self.part.at[j, slab], self.far.at[j, n - 1], self.send.at[1, j, n - 2], self.recv.at[1, j, n - 1], line.near
        )

    def lead(self, j, m):
        line = self.line
        if self.masks[m] == 1:
            self.shared(j).start()
        if self.masks[m] == 0:
            self.shared(j).wait_recv()
            slab = line.me + 1 - 2 * line.side
            both = self.part[j, slab, : self.cut].astype(F32) + self.near[j, 0, : self.cut].astype(F32)
            self.part[j, slab, : self.cut] = both.astype(BF16)
        self.cross(j, m).start()

    def start(self, j):
        for m in range(self.line.n):
            self.lead(j, m)

    def emit(self, j, turned, right, now=None):
        rows = self.rows
        for m, mask in enumerate(self.masks):
            i = self.place(mask)
            left = turned[pl.ds(pl.multiple_of(2 * i * rows, 2 * rows), 2 * rows), :]
            value = mm(left, right[...]).astype(BF16)
            self.part[j, 2 * i] = value[:rows]
            self.part[j, 2 * i + 1] = value[rows:]
            if now is None or m < now:
                self.lead(j, m)

    def fold(self, j, m):
        line = self.line
        n = line.n
        mask = self.masks[m]
        self.cross(j, m).wait_recv()
        slot = 2 * self.place(mask) + line.side
        if mask == 1:
            both = self.part[j, slot, self.cut :].astype(F32) + self.near[j, m, self.cut :].astype(F32)
            self.part[j, slot, self.cut :] = both.astype(BF16)
        else:
            self.part[j, slot] = (self.part[j, slot].astype(F32) + self.near[j, m].astype(F32)).astype(BF16)
        if mask == n - 1:
            @pl.when(self.an_end)
            def _():
                self.through(j).start()

            @pl.when(jnp.logical_not(self.an_end))
            def _():
                self.straight(j, mask).start()
        elif mask:
            if mask == n - 2:
                @pl.when(self.by_end)
                def _():
                    self.through(j).wait_recv()
                    self.part[j, slot] = (self.part[j, slot].astype(F32) + self.far[j, n - 1].astype(F32)).astype(BF16)

            self.straight(j, mask).start()

    def finish(self, j):
        line = self.line
        n = line.n
        out = self.out(j)
        value = self.part[j, line.me].astype(out.dtype)
        for mask in range(1, n - 1):
            self.straight(j, mask).wait_recv()
            value = value + self.far[j, mask - 1].astype(out.dtype)
        out[...] = value

        @pl.when(jnp.logical_not(self.an_end))
        def _():
            self.straight(j, n - 1).wait_recv()
            out[...] += self.far[j, n - 2].astype(out.dtype)

    def drain(self, j):
        n = self.line.n
        self.shared(j).wait_send()
        for m in range(n):
            self.cross(j, m).wait_send()
        for mask in range(1, n):
            self.straight(j, mask).wait_send()


def mm(left, right, dims=NN, precision=None):
    return lax.dot_general(left, right, dims, precision=precision, preferred_element_type=F32)


def sigmoid(v):
    return 0.5 * jnp.tanh(0.5 * v) + 0.5


def softplus(v):
    return jnp.maximum(v, 0.0) + jnp.log1p(jnp.exp(-jnp.abs(v)))


def split16(v):
    top = v.astype(BF16)
    return top, (v - top.astype(F32)).astype(BF16)


def expand(v, ind):
    top, rest = split16(v)
    return mm(top, ind) + mm(rest, ind)


def headsum(v, ind):
    return mm(v.astype(BF16), ind, NT)


def rowsum(v):
    return mm(jnp.ones((8, v.shape[1]), BF16), v.astype(BF16), NT)[0:1, :]


def iotas(n):
    return (
        lax.broadcasted_iota(jnp.int32, (n, n), 0),
        lax.broadcasted_iota(jnp.int32, (n, n), 1),
    )


def colsum(v):
    return jnp.sum(v, axis=0, keepdims=True)


def conv_pre(ext, par, n):
    total = par[4:5, :] + par[0:1, :] * ext[5 : 5 + n, :]
    for tap in range(1, 4):
        total = total + par[tap : tap + 1, :] * ext[5 + tap : 5 + tap + n, :]
    return total


def scan_prep(small, hp, ind, n):
    rows, cols = iotas(n)
    raw = small[:, 2 * STATE :] + hp[0:1, :]
    step = softplus(raw)
    rate = -jnp.exp(hp[1:2, :])
    lower = jnp.where(rows >= cols, 1.0, 0.0).astype(F32)
    cs = mm(lower, step * rate, precision=HIGH)
    tail = jnp.exp(cs[n - 1 : n, :] - cs)
    wide = mm(jnp.concatenate([step, jnp.exp(cs), tail], axis=0).astype(BF16), ind)
    return raw, step, rate, cs, wide[0:n], wide[n : 2 * n], wide[2 * n : 3 * n]


def block_of(slabs, at, rows):
    step = math.gcd(LANES, rows)
    pieces = []
    for k in range(LANES // step):
        row = at * LANES + k * step
        slab = row // rows
        pieces.append(slabs[slab, pl.ds(pl.multiple_of(row - slab * rows, step), step), :])
    return pieces[0] if len(pieces) == 1 else jnp.concatenate(pieces, axis=0)


def put_params(cp, sp, hp, ind, layer, params):
    conv, bias, norm, convs, biass, head = params
    width = cp.shape[1]
    row = lax.broadcasted_iota(jnp.int32, (LANES, width), 0)
    lane = lax.broadcasted_iota(jnp.int32, (LANES, width), 1)
    ind[...] = jnp.where(lane // HEAD == row, 1.0, 0.0).astype(BF16)
    hp[...] = head[layer]
    cp[0:4, :] = conv[layer]
    cp[4:5, :] = bias[layer : layer + 1, :]
    cp[5:6, :] = norm[layer : layer + 1, :]
    cp[6:8, :] = expand(hp[...], ind[...])[2:4, :]
    sp[0:4, :] = convs[layer]
    sp[4:5, :] = biass[layer : layer + 1, :]


def place_rows(dst, at, value):
    r = dst.shape[1]
    for g in range(0, value.shape[0], 16):
        dst[(at + g) // r, (at + g) % r : (at + g) % r + 16, :] = value[g : g + 16].astype(dst.dtype)


def pack_rows(size):
    return -(-PACK // (16 * size)) * 16


def put_pack(dst, me, turned, steps_low, sdel, dcp, dsp, dhp, dgain):
    model = turned.shape[0]
    quarter = model // 4
    w = sdel.shape[1]

    def empty(n):
        return jnp.zeros((n, w), F32)

    place_rows(dst, 0, mm(turned[pl.ds(pl.multiple_of(me * quarter, quarter), quarter), :], sdel[...]))
    place_rows(dst, quarter, jnp.concatenate([dsp, empty(8)], axis=0))
    grown = mm(turned[...], steps_low[...]).T[:16]
    at = quarter + 16
    for b in range(model // w):
        place_rows(dst, at, grown[:, b * w : (b + 1) * w])
        at += 16
    place_rows(dst, at, jnp.concatenate([dcp[:, :w], dcp[:, w : 2 * w]], axis=0))
    place_rows(dst, at + 16, jnp.concatenate([dcp[:, 2 * w :], jnp.concatenate([dhp, dhp], axis=1)], axis=0))
    rows = [dgain[:, b * w : (b + 1) * w] for b in range(model // w)]
    place_rows(dst, at + 32, jnp.concatenate(rows + [empty(16 - len(rows))], axis=0))
    assert at + 48 == PACK


class Smalls:
    def __init__(self, line, square, pack, near, away, own, full, wide, sems):
        send, recv, keep, gsend, grecv, self.xsend, self.xrecv = sems
        self.square, self.full, self.wide = square, full, wide
        self.layers = range(pack.shape[0])
        self.sum = Scatter(line, pack, lambda j: own.at[j], near, away, send, recv)
        self.spread = Gather(line, lambda j: own.at[j], full, keep, gsend, grecv)

    def swap(self, k):
        sq = self.square
        slot = (sq.me, sq.me, lax.rem(sq.me + 2, 4))[k]
        who = (sq.across, sq.mate, sq.mate)[k]
        return remote(self.wide.at[slot], self.wide.at[slot], self.xsend.at[k], self.xrecv.at[k], who)

    def start(self):
        for j in self.layers:
            self.sum.start(j)

    def fold(self):
        for j in self.layers:
            for m in range(self.sum.line.n):
                self.sum.fold(j, m)

    def turn(self):
        for j in self.layers:
            self.sum.finish(j)
            self.spread.start(j)

    def relay(self, k):
        for j in self.layers:
            self.spread.relay(j, k)

    def cross(self):
        for j in self.layers:
            self.spread.arrive(j)
            flat = self.full[j].reshape(-1, self.full.shape[3])
            self.wide[self.square.me, j] = flat[: self.wide.shape[2]]
        self.swap(0).start()
        self.swap(1).start()

    def cross_on(self):
        self.swap(0).wait_recv()
        self.swap(2).start()

    def end(self):
        self.swap(1).wait_recv()
        self.swap(2).wait_recv()
        for k in range(3):
            self.swap(k).wait_send()
        for j in self.layers:
            self.sum.drain(j)
            self.spread.drain(j)


def smalls_scratch(size, w, layers):
    r, n = pack_rows(size), size // 2
    buffers = [
        pltpu.VMEM((layers, size, r, w), BF16),
        pltpu.VMEM((layers, n, r, w), BF16),
        pltpu.VMEM((layers, n, r, w), BF16),
        pltpu.VMEM((layers, r, w), BF16),
        pltpu.VMEM((layers, size, r, w), BF16),
        pltpu.VMEM((4, layers, SPAN, w), BF16),
    ]
    sems = [
        pltpu.SemaphoreType.DMA((3, layers, n)),
        pltpu.SemaphoreType.DMA((3, layers, n)),
        pltpu.SemaphoreType.DMA((layers,)),
        pltpu.SemaphoreType.DMA((layers, 3, size)),
        pltpu.SemaphoreType.DMA((layers, size)),
        pltpu.SemaphoreType.DMA((3,)),
        pltpu.SemaphoreType.DMA((3,)),
    ]
    return buffers + sems


def forward_body(*refs, size, heads, per, steps, layer):
    refs = list(refs)

    def take(n):
        got = refs[:n]
        del refs[:n]
        return got

    mid = layer > 0
    (res_hbm,) = take(1)
    if mid:
        scaled_hbm, wout_hbm, sq_ref = take(3)
    state_hbm, step_hbm, in_hbm, out_hbm, gain_ref = take(5)
    params = take(6)
    if mid:
        new_hbm, sums_ref = take(2)
    normed_hbm, rnorm_ref, small_hbm, inner_hbm, gate_hbm, wt_hbm, full_hbm, ssd_ref, scaled_ref, sqs_ref, st_ref = take(11)
    if mid:
        scaled_in, wout, part, got, far, other, rows_got, facs, fresh, sends, recvs, rsend, rrecv = take(13)
    res, wstate, wt, slabs, normed, turned, small, inner, gate, ext, exts, state = take(12)
    cp_ref, sp_ref, hp_ref, ind_ref, keep, gsend, grecv, load, sems = take(9)
    assert not refs

    n = CHUNK
    tokens_n, model = res.shape
    width = inner.shape[1]
    top = 2 * width + 2 * STATE
    i = pl.program_id(0)
    line = Line(size)
    square = Square()
    job = Gather(line, lambda j: out_hbm.at[layer] if j == 2 else in_hbm.at[layer, 1 - j], slabs, keep, gsend, grecv)
    outgoing = [(turned, normed_hbm), (small, small_hbm), (inner, inner_hbm), (gate, gate_hbm)]
    outgoing += [(wt, wt_hbm), (slabs.at[2], full_hbm)]
    if mid:
        outgoing.append((fresh, new_hbm))

    def flush(k):
        return pltpu.make_async_copy(*outgoing[k], sems.at[k])


    @pl.when(i == 0)
    def _():
        pairs = [(res_hbm, res), (state_hbm.at[layer], wstate), (step_hbm.at[layer], wt.at[pl.ds(top, LANES), :])]
        if mid:
            pairs = [(scaled_hbm, scaled_in), (wout_hbm, wout)] + pairs
        loads = [pltpu.make_async_copy(src, dst, load.at[k]) for k, (src, dst) in enumerate(pairs)]
        for copy in loads:
            copy.start()
        line.greet(pltpu.get_barrier_semaphore(), square.others() if mid else ())
        job.start(0)
        put_params(cp_ref, sp_ref, hp_ref, ind_ref, layer, params)
        ticks = [functools.partial(job.relay, 0, k) for k in range(1, line.n)]
        ticks.append(functools.partial(job.start, 1))
        ticks += [functools.partial(job.relay, 1, k) for k in range(1, line.n)]
        ticks.append(functools.partial(job.start, 2))

        if mid:
            chunks = model // SLICE
            half = tokens_n // 2
            sums = Total(square, part, got, far, other, sends, recvs)
            copies = [
                remote(sq_ref, rows_got.at[square.me], rsend.at[k], rrecv.at[k], who)
                for k, who in enumerate(square.others())
            ]
            for copy in copies:
                copy.start()
            loads[0].wait()
            loads[1].wait()
            for c in range(chunks):
                value = mm(scaled_in[...], wout[c * SLICE : (c + 1) * SLICE, :], NT).astype(BF16)
                part[2 * c] = value[:half]
                part[2 * c + 1] = value[half:]
                sums.step(0, c)
                if c:
                    sums.step(1, c - 1)
            sums.step(1, chunks - 1)
            rows_got[square.me] = sq_ref[...]
            for copy in copies:
                copy.wait()
            total = (rows_got[0] + rows_got[1]) + (rows_got[2] + rows_got[3])
            sums_ref[...] = total
            factor = lax.rsqrt(total / INNER + EPS)
            for t in range(tokens_n // LANES):
                facs[t * LANES : (t + 1) * LANES, :] = jnp.broadcast_to(factor[t], (LANES, LANES)).T
            loads[2].wait()

            def use(c):
                for h in range(2):
                    where = slice(h * half, (h + 1) * half)
                    for s in range(SLICE // LANES):
                        lanes = slice(c * SLICE + s * LANES, c * SLICE + (s + 1) * LANES)
                        value = part[2 * c + h, :, s * LANES : (s + 1) * LANES].astype(F32)
                        fresh[where, lanes] = res[where, lanes].astype(F32) + facs[where, :] * value

            spread = max(1, -(-len(ticks) // chunks))
            for c in range(chunks):
                for tick in ticks[:spread]:
                    tick()
                ticks = ticks[spread:]
                sums.step(2, c)
                if c:
                    sums.step(3, c - 1)
                    use(c - 1)
            sums.step(3, chunks - 1)
            use(chunks - 1)
            flush(6).start()
        else:
            loads[0].wait()
        loads[-2].wait()
        loads[-1].wait()
        for b in range(2 * STATE // LANES):
            rows = slice(2 * width + b * LANES, 2 * width + (b + 1) * LANES)
            wt[rows, :] = wstate[:, b * LANES : (b + 1) * LANES].T

        def norm(t, _):
            rows = pl.ds(pl.multiple_of(t * TILE, TILE), TILE)
            value = (fresh if mid else res)[rows, :].astype(F32)
            scale = lax.rsqrt(jnp.sum(value * value, axis=1, keepdims=True) / model + EPS)
            low = (value * scale * gain_ref[layer : layer + 1, :]).astype(BF16)
            rnorm_ref[rows, :] = scale
            normed[rows, :] = low
            turned[:, rows] = low.T
            small[rows, : 2 * STATE] = mm(low, wstate[...])
            small[rows, 2 * STATE :] = mm(low, wt[top:, :], NT)
            return 0

        lax.fori_loop(0, tokens_n // TILE, norm, 0)
        flush(0).start()
        flush(1).start()
        for tick in ticks:
            tick()

        def project(j, dst):
            weight = slabs[j].reshape(model, width)

            def tile(t, _):
                rows = pl.ds(pl.multiple_of(t * TILE, TILE), TILE)
                dst[rows, :] = mm(normed[rows, :], weight)
                return 0

            lax.fori_loop(0, tokens_n // TILE, tile, 0)

        for j, dst in ((0, inner), (1, gate)):
            job.arrive(j)
            project(j, dst)
            flush(2 + j).start()

    for k in range(1, line.n):
        @pl.when(i == 1 + (k - 1) * steps // line.n)
        def _(k=k):
            job.relay(2, k)

    @pl.when(i > 0)
    def _():
        at = i - 1
        where = pl.ds(pl.multiple_of(at * n, n), n)

        @pl.when(lax.rem(at, per) == 0)
        def _():
            ext[0:8, :] = jnp.zeros((8, width), F32)
            exts[0:8, :] = jnp.zeros((8, 2 * STATE), F32)
            state[...] = jnp.zeros_like(state)

        rows, cols = iotas(n)
        ind = ind_ref[...]
        ext[8 : 8 + n, :] = inner[where, :]
        pre = conv_pre(ext, cp_ref, n)
        x = pre * sigmoid(pre)
        ext[0:8, :] = ext[n : n + 8, :]
        mini = small[where, :]
        exts[8 : 8 + n, :] = mini[:, : 2 * STATE]
        pres = conv_pre(exts, sp_ref, n)
        bc = (pres * sigmoid(pres)).astype(BF16)
        exts[0:8, :] = exts[n : n + 8, :]
        key, query = bc[:, :STATE], bc[:, STATE:]

        _, step, rate, cs, wide_step, wide_cs, wide_tail = scan_prep(mini, hp_ref, ind, n)
        cs2 = cs * LOG2E
        cs2t = cs2.T
        xs = x * wide_step
        lane = lax.broadcasted_iota(jnp.int32, (1, width), 1)
        half = jnp.where(lax.rem(lane, 2 * HEAD) < HEAD, 1.0, 0.0).astype(BF16)
        xsb = xs.astype(BF16)
        xs0 = xsb * half
        xs1 = xsb - xs0
        before = state[...]
        low = before.astype(BF16)
        st_ref[0] = low
        carried = mm(query, low) * wide_cs
        xw = (xs * wide_tail).astype(BF16)
        state[...] = before * wide_cs[n - 1 : n, :] + mm(key, xw, TN)
        scores = jnp.where(rows >= cols, mm(query, key, NT), 0.0)
        for pair in range(heads // 2):
            lanes = slice(pair * 2 * HEAD, (pair + 1) * 2 * HEAD)
            mats = []
            for h in (2 * pair, 2 * pair + 1):
                dec = jnp.exp2(jnp.minimum(cs2[:, h : h + 1] - cs2t[h : h + 1, :], 0.0))
                mats.append((scores * dec).astype(BF16))
            local = mm(
                jnp.concatenate(mats, axis=1),
                jnp.concatenate([xs0[:, lanes], xs1[:, lanes]], axis=0),
            )
            ssd_ref[:, lanes] = local + carried[:, lanes] + cp_ref[6:7, lanes] * x[:, lanes]
        gates = gate[where, :]
        gated = ssd_ref[...] * (gates * sigmoid(gates))
        sqs_ref[0] = rowsum(gated * gated)
        scaled_ref[...] = (gated * cp_ref[5:6, :]).astype(BF16)

        span = model // LANES
        share = -(-2 * span // steps)
        for k in range(share):
            b = at * share + k

            @pl.when(b < 2 * span)
            def _(b=b):
                j, col = b // span, lax.rem(b, span)
                slab_rows = slabs.shape[2]
                weight = slabs.at[j]
                piece = block_of(weight, col, slab_rows)
                wt[pl.ds(pl.multiple_of(j * width, width), width), pl.ds(pl.multiple_of(col * LANES, LANES), LANES)] = piece.T

    @pl.when(i == steps)
    def _():
        flush(4).start()
        job.arrive(2)
        flush(5).start()
        for j in range(3):
            job.drain(j)
        for k in range(len(outgoing)):
            flush(k).wait()


def forward(res, stateproj, steps_w, inproj, outt, gain, params, heads, size, layer, out=None):
    tokens_n, model = res.shape
    _, _, rows, width = inproj.shape
    top = 2 * width + 2 * STATE + LANES
    steps = tokens_n // CHUNK
    mid = out is not None
    hbm = pl.BlockSpec(memory_space=pl.ANY)
    chunks = model // SLICE

    def whole(a):
        return pl.BlockSpec(a.shape, lambda i: (0,) * len(a.shape))

    def row(w):
        return pl.BlockSpec((CHUNK, w), lambda i: (jnp.maximum(i - 1, 0), 0))

    args, in_specs, out_specs, out_shape, scratch = [res], [hbm], [], [], []
    if mid:
        args += list(out)
        in_specs += [hbm, hbm, whole(out[2])]
        out_specs += [hbm, whole(out[2])]
        out_shape += [jax.ShapeDtypeStruct(res.shape, F32), jax.ShapeDtypeStruct(out[2].shape, F32)]
        chunk = pltpu.VMEM((chunks, tokens_n // 2, SLICE), BF16)
        scratch += [
            pltpu.VMEM(out[0].shape, BF16),
            pltpu.VMEM(out[1].shape, BF16),
            pltpu.VMEM((2 * chunks, tokens_n // 2, SLICE), BF16),
            chunk, chunk, chunk,
            pltpu.VMEM((4,) + out[2].shape, F32),
            pltpu.VMEM((tokens_n, LANES), F32),
            pltpu.VMEM(res.shape, F32),
            pltpu.SemaphoreType.DMA((3, chunks)),
            pltpu.SemaphoreType.DMA((3, chunks)),
            pltpu.SemaphoreType.DMA((3,)),
            pltpu.SemaphoreType.DMA((3,)),
        ]
    args += [stateproj, steps_w, inproj, outt, gain, *params]
    in_specs += [hbm, hbm, hbm, hbm, whole(gain)] + [whole(v) for v in params]
    out_specs += [
        hbm, pl.BlockSpec((tokens_n, 1), lambda i: (0, 0)), hbm, hbm, hbm, hbm, hbm,
        row(width), row(width),
        pl.BlockSpec((1, 1, CHUNK), lambda i: (jnp.maximum(i - 1, 0), 0, 0)),
        pl.BlockSpec((1, STATE, width), lambda i: (jnp.maximum(i - 1, 0), 0, 0)),
    ]
    out_shape += [
        jax.ShapeDtypeStruct((model, tokens_n), BF16),
        jax.ShapeDtypeStruct((tokens_n, 1), F32),
        jax.ShapeDtypeStruct((tokens_n, 2 * STATE + LANES), F32),
        jax.ShapeDtypeStruct((tokens_n, width), F32),
        jax.ShapeDtypeStruct((tokens_n, width), F32),
        jax.ShapeDtypeStruct((top, model), BF16),
        jax.ShapeDtypeStruct((size, rows, width), BF16),
        jax.ShapeDtypeStruct((tokens_n, width), F32),
        jax.ShapeDtypeStruct((tokens_n, width), BF16),
        jax.ShapeDtypeStruct((steps, 1, CHUNK), F32),
        jax.ShapeDtypeStruct((steps, STATE, width), BF16),
    ]
    scratch += [
        pltpu.VMEM(res.shape, res.dtype),
        pltpu.VMEM((model, 2 * STATE), BF16),
        pltpu.VMEM((top, model), BF16),
        pltpu.VMEM((3, size, rows, width), BF16),
        pltpu.VMEM((tokens_n, model), BF16),
        pltpu.VMEM((model, tokens_n), BF16),
        pltpu.VMEM((tokens_n, 2 * STATE + LANES), F32),
        pltpu.VMEM((tokens_n, width), F32),
        pltpu.VMEM((tokens_n, width), F32),
        pltpu.VMEM((CHUNK + 8, width), F32),
        pltpu.VMEM((CHUNK + 8, 2 * STATE), F32),
        pltpu.VMEM((STATE, width), F32),
        pltpu.VMEM((8, width), F32),
        pltpu.VMEM((8, 2 * STATE), F32),
        pltpu.VMEM((8, LANES), F32),
        pltpu.VMEM((LANES, width), BF16),
        pltpu.SemaphoreType.DMA((3,)),
        pltpu.SemaphoreType.DMA((3, 3, size)),
        pltpu.SemaphoreType.DMA((3, size)),
        pltpu.SemaphoreType.DMA((5,)),
        pltpu.SemaphoreType.DMA((7,)),
    ]
    return pl.pallas_call(
        functools.partial(forward_body, size=size, heads=heads, per=LEN // CHUNK, steps=steps, layer=layer),
        grid=(steps + 1,),
        in_specs=in_specs,
        out_specs=out_specs,
        out_shape=out_shape,
        scratch_shapes=scratch,
        compiler_params=pltpu.CompilerParams(
            collective_id=min(layer, 1), has_side_effects=True, vmem_limit_bytes=VMEM_LIMIT
        ),
        name="forward",
    )(*args)


def back_body(*refs, heads, per, size, steps, layer, last):
    refs = list(refs)

    def take(n):
        got = refs[:n]
        del refs[:n]
        return got

    up_ref, sq_ref, gate_ref, ssd_ref, inner_ref, iprev_ref, small_ref, sprev_ref, st_ref, res_ref, rn_ref = take(11)
    gain_ref = take(1)[0]
    params = take(6)
    wout_hbm, scaled_hbm, wt_hbm, normed_hbm = take(4)
    if not last:
        next_normed, next_steps, next_sdel, next_dcp, next_dsp, next_dhp, next_dgain = take(7)
    new_ref, grad_hbm = take(2)
    if last:
        sdsum_ref, steplow_ref, dcp_ref, dsp_ref, dhp_ref, dgain_ref, mixed_ref = take(7)
    else:
        full_hbm, wide_hbm = take(2)
    ext, exts, cde, cdes, dstate, rq, cp_ref, sp_ref, hp_ref, ind_ref = take(10)
    wout, scaled, wt, turned, dy, glow, ilow, frow, srow, sgot = take(10)
    part, near, away, tpart, got, far, other = take(7)
    load, rsend, rrecv, ssend, srecv, sends, recvs, gsem = take(8)
    if last:
        fgot, opart, ogot, ofar, oother, fsend, frecv, osends, orecvs = take(9)
    else:
        dcp_ref, dsp_ref, dhp_ref, dgain_ref, step_all, sd_all = take(6)
        buffers = take(6)
        sems = take(7)
    assert not refs

    n = CHUNK
    model = up_ref.shape[1]
    i = pl.program_id(0)
    begin_gate = steps
    begin_scan = begin_gate + steps
    begin_norm = begin_scan + steps
    end = begin_norm + steps - 1
    line = Line(size)
    square = Square()
    rows_own = part.shape[2]
    count = part.shape[0]
    job = Scatter(line, part, lambda j: dy.at[pl.ds(j * rows_own, rows_own), :], near, away, ssend, srecv)
    sums = Total(square, tpart, got, far, other, sends, recvs)
    if last:
        outs = Total(square, opart, ogot, ofar, oother, osends, orecvs)
        half = steps * n // 2
        slices = model // SLICE
    else:
        minis = Smalls(line, square, *buffers, sems)
    moves = [(wout_hbm, wout), (scaled_hbm, scaled), (wt_hbm, wt), (normed_hbm, turned)]
    if not last:
        tokens_n = steps * n
        spots = (wt.at[pl.ds(0, model), pl.ds(0, tokens_n)],)
        spots += tuple(
            wt.at[pl.ds(0, tokens_n), pl.ds(tokens_n + at, w)] for at, w in ((0, LANES), (LANES, 2 * STATE))
        )
        moves += [(next_normed, spots[0]), (next_steps, spots[1]), (next_sdel, spots[2])]

    def move(k):
        return pltpu.make_async_copy(*moves[k], load.at[k])

    places = line.n

    def spaced(begin, stop, m):
        return begin + m * (stop - begin) // places

    middle = begin_scan + steps // 2
    folds = [(spaced(begin_scan - steps // 2, middle, m), 0, m) for m in range(places)]
    folds += [(spaced(middle, begin_norm, m), 1, m) for m in range(places)]

    def column(row):
        return jnp.broadcast_to(row, (n, n)).T[:, 0:1]

    @pl.when(i == 0)
    def _():
        for k in range(3):
            move(k).start()
        put_params(cp_ref, sp_ref, hp_ref, ind_ref, layer, params)
        rq[...] = jnp.zeros_like(rq)
        line.greet_all(pltpu.get_barrier_semaphore(), square.others())
        if last:
            rows = [
                remote(sq_ref, fgot.at[square.me], fsend.at[k], frecv.at[k], who)
                for k, who in enumerate(square.others())
            ]
            for copy in rows:
                copy.start()
            fgot[square.me] = sq_ref[...]
            move(0).wait()
            move(1).wait()
            for c in range(slices):
                value = mm(scaled[...], wout[c * SLICE : (c + 1) * SLICE, :], NT).astype(BF16)
                opart[2 * c] = value[:half]
                opart[2 * c + 1] = value[half:]
                outs.step(0, c)
            outs.step(1, 0)
            for copy in rows:
                copy.wait()
            total = (fgot[0] + fgot[1]) + (fgot[2] + fgot[3])
        else:
            total = sq_ref[...]
            move(0).wait()
            move(1).wait()
        dcp_ref[...] = jnp.zeros_like(dcp_ref)
        dsp_ref[...] = jnp.zeros_like(dsp_ref)
        dhp_ref[...] = jnp.zeros_like(dhp_ref)
        dgain_ref[...] = jnp.zeros_like(dgain_ref)
        frow[...] = lax.rsqrt(total / INNER + EPS)

    ind = ind_ref[...]
    for at, j, m in folds:
        @pl.when(i == at)
        def _(j=j, m=m):
            job.fold(j, m)

    @pl.when(i < begin_gate)
    def _():
        rows = pl.ds(pl.multiple_of(i * n, n), n)
        low = (column(frow[i]) * up_ref[...].astype(F32)).astype(BF16)
        turned[:, rows] = low.T
        sd = mm(low, wout[...])
        dy[rows, :] = sd
        piece = scaled[rows, :]
        srow[i] = rowsum(piece.astype(F32) * sd)

    @pl.when(i == begin_gate - 1)
    def _():
        copies = [
            remote(srow, sgot.at[square.me], rsend.at[k], rrecv.at[k], who) for k, who in enumerate(square.others())
        ]
        for copy in copies:
            copy.start()
        job.emit(0, turned, scaled)
        move(3).start()
        sgot[square.me] = srow[...]
        for copy in copies:
            copy.wait()
        srow[...] = (sgot[0] + sgot[1]) + (sgot[2] + sgot[3])

    if last:
        @pl.when(i == steps // 2)
        def _():
            outs.step(1, 1)

        @pl.when((i >= begin_gate) & (i < begin_gate + slices - 2))
        def _():
            outs.step(1, i - begin_gate + 2)

    @pl.when((i >= begin_gate) & (i < begin_scan))
    def _():
        c = i - begin_gate
        rows = pl.ds(pl.multiple_of(c * n, n), n)
        coef = column(frow[c] * frow[c] * srow[c]) / INNER
        gate = gate_ref[...]
        gsig = sigmoid(gate)
        gact = gate * gsig
        ssd = ssd_ref[...]
        sd = dy[rows, :]
        gated = ssd * gact
        gd = cp_ref[5:6, :] * sd - coef * gated
        dcp_ref[5:6, :] += colsum(gated * sd)
        dy[rows, :] = gd * gact
        glow[rows, :] = (gd * ssd * (gsig + gact * (1.0 - gsig))).astype(BF16)

    @pl.when(i == begin_scan - 1)
    def _():
        move(3).wait()
        job.emit(1, turned, glow)
        move(2).wait()

    @pl.when((i >= begin_scan) & (i < begin_norm))
    def _():
        q = i - begin_scan
        chunk = steps - 1 - q
        where = pl.ds(pl.multiple_of(chunk * n, n), n)

        @pl.when(lax.rem(chunk, per) == per - 1)
        def _():
            cde[n : n + 8, :] = jnp.zeros((8, cde.shape[1]), F32)
            cdes[n : n + 8, :] = jnp.zeros((8, cdes.shape[1]), F32)
            dstate[...] = jnp.zeros_like(dstate)

        keep = jnp.where(lax.rem(chunk, per) == 0, 0.0, 1.0).astype(F32)
        rows, cols = iotas(n)
        ext[0:8, :] = iprev_ref[...] * keep
        ext[8 : 8 + n, :] = inner_ref[...]
        exts[0:8, :] = sprev_ref[:, : 2 * STATE] * keep
        exts[8 : 8 + n, :] = small_ref[:, : 2 * STATE]
        pre = conv_pre(ext, cp_ref, n)
        sig = sigmoid(pre)
        x = pre * sig
        slope = sig + x * (1.0 - sig)
        pres = conv_pre(exts, sp_ref, n)
        sigs = sigmoid(pres)
        acts = pres * sigs
        slopes = sigs + acts * (1.0 - sigs)
        bc = acts.astype(BF16)
        key, query = bc[:, :STATE], bc[:, STATE:]
        dyc = dy[where, :]

        raw, step, rate, cs, wide_step, wide_cs, wide_tail = scan_prep(small_ref, hp_ref, ind, n)
        cs2 = cs * LOG2E
        cs2t = cs2.T
        xs = x * wide_step
        xsb = xs.astype(BF16)
        dyb = dyc.astype(BF16)
        lane = lax.broadcasted_iota(jnp.int32, (1, xs.shape[1]), 1)
        half = jnp.where(lax.rem(lane, 2 * HEAD) < HEAD, 1.0, 0.0).astype(BF16)
        dy0 = dyb * half
        dy1 = dyb - dy0
        low = st_ref[0]
        dst = dstate[...]
        dlow = dst.astype(BF16)
        dye = dyc * wide_cs
        dyeb = dye.astype(BF16)
        up = headsum(dye * mm(query, low), ind)
        dxs_state = wide_tail * mm(key, dlow)
        down = headsum(xs * dxs_state, ind)
        qdel = mm(dyeb, low, NT)
        kdel = mm((xs * wide_tail).astype(BF16), dlow, NT)
        through = headsum(jnp.broadcast_to(colsum(low.astype(F32) * dst), (8, dst.shape[1])), ind)[0:1, :]
        through = through * jnp.exp(cs[n - 1 : n, :])
        dstate[...] = dst * wide_cs[n - 1 : n, :] + mm(query, dyeb, TN)

        scores = jnp.where(rows <= cols, mm(key, query, NT), 0.0)
        dscores = jnp.zeros((n, n), F32)
        colq = jnp.zeros((n, LANES), F32)
        lane = lax.broadcasted_iota(jnp.int32, (n, LANES), 1)
        dxs = []
        for pair in range(heads // 2):
            lanes = slice(pair * 2 * HEAD, (pair + 1) * 2 * HEAD)
            stacked = jnp.concatenate([dy0[:, lanes], dy1[:, lanes]], axis=0)
            both = mm(xsb[:, lanes], stacked, NT)
            mats = []
            for which, h in enumerate((2 * pair, 2 * pair + 1)):
                dec = jnp.exp2(jnp.minimum(cs2t[h : h + 1, :] - cs2[:, h : h + 1], 0.0))
                mats.append((scores * dec).astype(BF16))
                term = dec * both[:, which * n : (which + 1) * n]
                dscores = dscores + term
                quad = scores * term
                rq[h : h + 1, :] = colsum(quad)
                colq = jnp.where(lane == h, jnp.sum(quad, axis=1, keepdims=True), colq)
            dxs.append(mm(jnp.concatenate(mats, axis=1), stacked))
        dxs = jnp.concatenate(dxs, axis=1) + dxs_state
        dscores = jnp.where(rows <= cols, dscores, 0.0).astype(BF16)
        kdel = kdel + mm(dscores, query)
        qdel = qdel + mm(dscores, key, TN)

        upper = jnp.where(rows <= cols, 1.0, 0.0).astype(F32)
        strict = jnp.where(rows > cols, 1.0, 0.0).astype(F32)
        da = mm(upper, rq[...].T - colq + up, precision=HIGH) + mm(strict, down, precision=HIGH) + through
        grown = headsum(x * dxs, ind) + rate * da
        step_pre = grown * sigmoid(raw)
        steplow = step_pre.astype(BF16)
        if last:
            steplow_ref[...] = steplow
        else:
            step_all[where, :] = steplow
        dhp_ref[0:1, :] += colsum(step_pre)
        dhp_ref[1:2, :] += rate * colsum(step * da)
        dcp_ref[6:7, :] += colsum(dyc * x)

        cd = (dxs * wide_step + cp_ref[6:7, :] * dyc) * slope
        cde[0:n, :] = cd
        center = ext[8 : 8 + n, :]
        total = cp_ref[3:4, :] * cd
        dcp_ref[3:4, :] += colsum(cd * center)
        for tap in range(3):
            shifted = cde[3 - tap : 3 - tap + n, :]
            total = total + cp_ref[tap : tap + 1, :] * shifted
            dcp_ref[tap : tap + 1, :] += colsum(shifted * center)
        inner_low = total.astype(BF16)
        ilow[where, :] = inner_low
        dcp_ref[4:5, :] += colsum(cd)
        cde[n : n + 8, :] = cde[0:8, :]

        cds = jnp.concatenate([kdel, qdel], axis=1) * slopes
        cdes[0:n, :] = cds
        center = exts[8 : 8 + n, :]
        total = sp_ref[3:4, :] * cds
        dsp_ref[3:4, :] += colsum(cds * center)
        for tap in range(3):
            shifted = cdes[3 - tap : 3 - tap + n, :]
            total = total + sp_ref[tap : tap + 1, :] * shifted
            dsp_ref[tap : tap + 1, :] += colsum(shifted * center)
        sdel = total.astype(BF16)
        dsp_ref[4:5, :] += colsum(cds)
        cdes[n : n + 8, :] = cdes[0:8, :]

        lows = jnp.concatenate([inner_low, glow[where, :], sdel, steplow], axis=1)
        value = mm(lows, wt[...]).astype(BF16)
        tpart[2 * q, :, :model] = value[: n // 2]
        tpart[2 * q + 1, :, :model] = value[n // 2 :]
        tpart[2 * q, :, model:] = sdel[: n // 2]
        tpart[2 * q + 1, :, model:] = sdel[n // 2 :]
        sums.step(0, q)

    @pl.when((i > begin_scan) & (i <= begin_norm))
    def _():
        sums.step(1, i - begin_scan - 1)

    @pl.when((i >= begin_scan + 3) & (i < begin_norm + 3))
    def _():
        sums.step(2, i - begin_scan - 3)

    @pl.when((i >= begin_scan + 4) & (i < begin_norm + 4))
    def _():
        sums.step(3, i - begin_scan - 4)

    if last:
        @pl.when((i > begin_scan) & (i <= begin_scan + slices))
        def _():
            outs.step(2, i - begin_scan - 1)

        @pl.when((i > begin_scan + 1) & (i <= begin_scan + slices + 1))
        def _():
            outs.step(3, i - begin_scan - 2)

    @pl.when(i == begin_norm - 1)
    def _():
        dhp_ref[2:3, :] = headsum(jnp.broadcast_to(dcp_ref[6:7, :], (8, dcp_ref.shape[1])), ind)[0:1, :]
        job.emit(2, turned, ilow, None if last else places // 2)
        if not last:
            for k in (4, 5, 6):
                move(k).start()

    if not last:
        @pl.when(i == begin_norm + 1)
        def _():
            for k in (4, 5, 6):
                move(k).wait()
            put_pack(
                buffers[0].at[1], square.me, *spots, next_dcp[...], next_dsp[...], next_dhp[...], next_dgain[...]
            )
            minis.sum.start(1)

    @pl.when(i >= begin_norm)
    def _():
        r = i - begin_norm
        chunk = steps - 1 - r
        if last:
            fac = column(frow[chunk])
            side = chunk // (steps // 2)
            base = (chunk - side * (steps // 2)) * n
        for h in range(2):
            rows = slice(h * (n // 2), (h + 1) * (n // 2))
            back = tpart[2 * r + h, :, :model].astype(F32)
            sdel = tpart[2 * r + h, :, model:]
            if last:
                sdsum_ref[rows, :] = sdel
            else:
                sd_all[pl.ds(pl.multiple_of(chunk * n + h * (n // 2), n // 2), n // 2), :] = sdel
            res = res_ref[rows, :].astype(F32)
            rn = rn_ref[rows, :]
            dgain_ref[...] += colsum(back * res * rn)
            gained = back * gain_ref[layer : layer + 1, :]
            mean = jnp.sum(gained * res, axis=1, keepdims=True) / model
            new_ref[rows, :] = up_ref[rows, :].astype(F32) + rn * gained - (rn * rn * rn * mean) * res
            if last:
                where = pl.ds(pl.multiple_of(base + h * (n // 2), n // 2), n // 2)
                for c in range(slices):
                    span = slice(c * SLICE, (c + 1) * SLICE)
                    summed = opart[2 * c + side, where, :].astype(F32)
                    mixed_ref[rows, span] = (res[:, span] + fac[rows, :] * summed).astype(BF16)

    @pl.when(i == end)
    def _():
        def finish(j):
            job.finish(j)
            pltpu.make_async_copy(dy.at[pl.ds(j * rows_own, rows_own), :], grad_hbm.at[j], gsem.at[j]).start()

        early = places if last else places // 2
        if not last:
            put_pack(
                buffers[0].at[0], square.me, turned, step_all, sd_all, dcp_ref[...], dsp_ref[...], dhp_ref[...], dgain_ref[...]
            )
            minis.sum.start(0)
            for m in range(places // 2, places):
                job.lead(2, m)
        for m in range(early):
            job.fold(2, m)
        finish(0)
        finish(1)
        if not last:
            minis.fold()
            minis.turn()
            for k in range(1, line.n):
                minis.relay(k)
            for m in range(places // 2, places):
                job.fold(2, m)
            minis.cross()
        finish(2)
        if not last:
            minis.cross_on()
            minis.end()
            tails = [
                pltpu.make_async_copy(src, dst, load.at[k])
                for k, (src, dst) in enumerate(((minis.full, full_hbm), (minis.wide, wide_hbm)))
            ]
            for copy in tails:
                copy.start()
        for j in range(count):
            job.drain(j)
            pltpu.make_async_copy(dy.at[pl.ds(j * rows_own, rows_own), :], grad_hbm.at[j], gsem.at[j]).wait()
        if not last:
            for copy in tails:
                copy.wait()


def back(up, sq, gate_pre, ssd, inner_raw, small, states, res, rnorm, gain, params,
         wout, scaled, wt, normed, heads, size, layer, after=None):
    tokens_n, width = inner_raw.shape
    model = up.shape[1]
    last = after is None
    steps = tokens_n // CHUNK
    begin_scan = 2 * steps
    begin_norm = begin_scan + steps
    rows = model // size
    n = size // 2
    hbm = pl.BlockSpec(memory_space=pl.ANY)
    top = steps - 1

    def norm_at(i):
        return jnp.where(i < begin_norm, top, top - (i - begin_norm))

    def scan_at(i):
        return jnp.clip(top - (i - begin_scan), 0, top)

    def first(w):
        return pl.BlockSpec((CHUNK, w), lambda i: (jnp.where(i < steps, i, norm_at(i)), 0))

    def second(w):
        return pl.BlockSpec((CHUNK, w), lambda i: (jnp.clip(i - steps, 0, top), 0))

    def scan(w):
        return pl.BlockSpec((CHUNK, w), lambda i: (scan_at(i), 0))

    def prev(w):
        return pl.BlockSpec((8, w), lambda i: (jnp.maximum(scan_at(i) * (CHUNK // 8) - 1, 0), 0))

    def norm(w):
        return pl.BlockSpec((CHUNK, w), lambda i: (norm_at(i), 0))

    def whole(a):
        return pl.BlockSpec(a.shape, lambda i: (0,) * len(a.shape))

    extra = model + 2 * STATE
    quarter = pltpu.VMEM((steps, CHUNK // 2, extra), BF16)
    pieces = pltpu.VMEM((3, n, rows, width), BF16)
    args = [up, sq, gate_pre, ssd, inner_raw, inner_raw, small, small, states, res, rnorm, gain, *params,
            wout, scaled, wt, normed]
    in_specs = [
        first(model), whole(sq), second(width), second(width),
        scan(width), prev(width), scan(small.shape[1]), prev(small.shape[1]),
        pl.BlockSpec((1, STATE, width), lambda i: (scan_at(i), 0, 0)),
        norm(model), norm(1), whole(gain),
    ] + [whole(a) for a in params] + [hbm] * 4
    out_specs = [norm(model), hbm]
    out_shape = [jax.ShapeDtypeStruct((tokens_n, model), F32), jax.ShapeDtypeStruct((3, rows, width), F32)]
    totals = [(8, width), (8, 2 * STATE), (8, LANES), (1, model)]
    scratch = [
        pltpu.VMEM((CHUNK + 8, width), F32),
        pltpu.VMEM((CHUNK + 8, 2 * STATE), F32),
        pltpu.VMEM((CHUNK + 8, width), F32),
        pltpu.VMEM((CHUNK + 8, 2 * STATE), F32),
        pltpu.VMEM((STATE, width), F32),
        pltpu.VMEM((LANES, CHUNK), F32),
        pltpu.VMEM((8, width), F32),
        pltpu.VMEM((8, 2 * STATE), F32),
        pltpu.VMEM((8, LANES), F32),
        pltpu.VMEM((LANES, width), BF16),
        pltpu.VMEM(wout.shape, BF16),
        pltpu.VMEM(scaled.shape, BF16),
        pltpu.VMEM(wt.shape, BF16),
        pltpu.VMEM(normed.shape, BF16),
        pltpu.VMEM((tokens_n, width), F32),
        pltpu.VMEM((tokens_n, width), BF16),
        pltpu.VMEM((tokens_n, width), BF16),
        pltpu.VMEM((steps, 1, CHUNK), F32),
        pltpu.VMEM((steps, 1, CHUNK), F32),
        pltpu.VMEM((4, steps, 1, CHUNK), F32),
        pltpu.VMEM((3, size, rows, width), BF16), pieces, pieces,
        pltpu.VMEM((2 * steps, CHUNK // 2, extra), BF16), quarter, quarter, quarter,
        pltpu.SemaphoreType.DMA((7,)),
        pltpu.SemaphoreType.DMA((3,)),
        pltpu.SemaphoreType.DMA((3,)),
        pltpu.SemaphoreType.DMA((3, 3, n)),
        pltpu.SemaphoreType.DMA((3, 3, n)),
        pltpu.SemaphoreType.DMA((3, steps)),
        pltpu.SemaphoreType.DMA((3, steps)),
        pltpu.SemaphoreType.DMA((3,)),
    ]
    if last:
        out_specs += [norm(2 * STATE), scan(LANES)]
        out_specs += [pl.BlockSpec(v, lambda i: (0, 0)) for v in totals] + [norm(model)]
        out_shape += [
            jax.ShapeDtypeStruct((tokens_n, 2 * STATE), BF16),
            jax.ShapeDtypeStruct((tokens_n, LANES), BF16),
        ]
        out_shape += [jax.ShapeDtypeStruct(v, F32) for v in totals]
        out_shape.append(jax.ShapeDtypeStruct((tokens_n, model), BF16))
        slices = model // SLICE
        chunk = pltpu.VMEM((slices, tokens_n // 2, SLICE), BF16)
        scratch += [
            pltpu.VMEM((4, steps, 1, CHUNK), F32),
            pltpu.VMEM((2 * slices, tokens_n // 2, SLICE), BF16), chunk, chunk, chunk,
            pltpu.SemaphoreType.DMA((3,)),
            pltpu.SemaphoreType.DMA((3,)),
            pltpu.SemaphoreType.DMA((3, slices)),
            pltpu.SemaphoreType.DMA((3, slices)),
        ]
    else:
        w = 2 * STATE
        r = pack_rows(size)
        args += list(after)
        in_specs += [hbm] * 3 + [whole(v) for v in after[3:]]
        out_specs += [hbm, hbm]
        out_shape += [
            jax.ShapeDtypeStruct((2, size, r, w), BF16),
            jax.ShapeDtypeStruct((4, 2, SPAN, w), BF16),
        ]
        scratch += [pltpu.VMEM(v, F32) for v in totals]
        scratch += [pltpu.VMEM((tokens_n, LANES), BF16), pltpu.VMEM((tokens_n, w), BF16)]
        scratch += smalls_scratch(size, w, 2)
    return pl.pallas_call(
        functools.partial(
            back_body, heads=heads, per=LEN // CHUNK, size=size, steps=steps, layer=layer, last=last
        ),
        grid=(begin_norm + steps,),
        in_specs=in_specs,
        out_specs=out_specs,
        out_shape=out_shape,
        scratch_shapes=scratch,
        compiler_params=pltpu.CompilerParams(
            collective_id=2 if last else 3, has_side_effects=True, vmem_limit_bytes=VMEM_LIMIT
        ),
        name="back",
    )(*args)


def unpack_body(full_ref, wide_ref, *refs, layers, heads):
    step_ref, state_ref, conv_ref, bias_ref, convs_ref, biass_ref = refs[:6]
    stepbias_ref, decay_ref, skip_ref, norm_ref, gain_ref = refs[6:]
    model = state_ref.shape[1]
    quarter = model // 4
    w = state_ref.shape[2]
    width = conv_ref.shape[2]
    for layer in range(layers):
        for t in range(4):
            state_ref[layer, t * quarter : (t + 1) * quarter, :] = wide_ref[t, layer, :quarter, :].astype(F32)
        taps = [wide_ref[t, layer, quarter : quarter + 16, :].astype(F32) for t in range(4)]
        taps = (taps[0] + taps[1]) + (taps[2] + taps[3])
        convs_ref[layer] = taps[0:4]
        biass_ref[layer : layer + 1, :] = taps[4:5]
        flat = full_ref[layer].reshape(-1, w)[:PACK].astype(F32)
        at = quarter + 16
        for b in range(model // w):
            step_ref[layer, :, b * w : (b + 1) * w] = flat[at : at + 16]
            at += 16
        for b in range(width // w):
            lanes = slice(b * w, (b + 1) * w)
            rows = flat[at + 8 * b : at + 8 * b + 8]
            conv_ref[layer, :, lanes] = rows[0:4]
            bias_ref[layer : layer + 1, lanes] = rows[4:5]
            norm_ref[layer : layer + 1, lanes] = rows[5:6]
        at += 8 * (width // w)
        for k, ref in enumerate((stepbias_ref, decay_ref, skip_ref)):
            ref[layer : layer + 1, :] = flat[at + k : at + k + 1, :heads]
        at += 8
        for b in range(model // w):
            gain_ref[layer : layer + 1, b * w : (b + 1) * w] = flat[at + b : at + b + 1]


def unpack(full, wide, model, width, heads):
    layers, w = full.shape[0], full.shape[3]
    vm = pl.BlockSpec(memory_space=pltpu.VMEM)
    shapes = [
        (layers, 16, model), (layers, model, w), (layers, 4, width), (layers, width), (layers, 4, w), (layers, w),
        (layers, heads), (layers, heads), (layers, heads), (layers, width), (layers, model),
    ]
    return pl.pallas_call(
        functools.partial(unpack_body, layers=layers, heads=heads),
        in_specs=[vm, vm],
        out_specs=[vm] * len(shapes),
        out_shape=[jax.ShapeDtypeStruct(v, F32) for v in shapes],
        compiler_params=pltpu.CompilerParams(vmem_limit_bytes=VMEM_LIMIT),
        name="unpack",
    )(full, wide)


def shards(
    tokens, inproj, stepproj, stateproj, outproj, convinner, biasinner, convstate, biasstate,
    stepbias, decaylog, skipgain, normgain, inputgain, cotangent,
):
    layers = inproj.shape[0]
    width = inproj.shape[3]
    heads = stepproj.shape[2]
    model = tokens.shape[1]
    pad = LANES - heads
    size = lax.axis_size("dp")
    steps_w = jnp.pad(jnp.swapaxes(stepproj, 1, 2), ((0, 0), (0, pad), (0, 0)))
    head = jnp.pad(jnp.stack([stepbias, decaylog, skipgain], axis=1), ((0, 0), (0, 5), (0, pad)))
    outt = jnp.swapaxes(outproj, 1, 2)
    params = (convinner, biasinner, normgain, convstate, biasstate, head)

    residual = tokens
    kept = []
    out = None
    for at in range(layers):
        results = forward(residual, stateproj, steps_w, inproj, outt, inputgain, params, heads, size, at, out=out)
        if at:
            residual, kept[-1][-1] = results[:2]
            results = results[2:]
        normed, rnorm, small, inner_raw, gate_pre, wt, w_out, ssd, scaled, sq, states = results
        w_out = w_out.reshape(model, width)
        kept.append([residual, normed, rnorm, small, inner_raw, gate_pre, wt, w_out, ssd, scaled, states, sq])
        out = (scaled, w_out, sq)

    assert layers == 2
    before, normed, rnorm, small, inner_raw, gate_pre, wt, w_out, ssd, scaled, states, sq = kept[1]
    upstream, second, sdel, steplow, *totals, mixed = back(
        cotangent, sq, gate_pre, ssd, inner_raw, small, states, before, rnorm, inputgain, params,
        w_out, scaled, wt, normed, heads, size, 1,
    )
    after = (normed, steplow, sdel, *totals)
    before, normed, rnorm, small, inner_raw, gate_pre, wt, w_out, ssd, scaled, states, sq = kept[0]
    upstream, first, full, wide = back(
        upstream, sq, gate_pre, ssd, inner_raw, small, states, before, rnorm, inputgain, params,
        w_out, scaled, wt, normed, heads, size, 0, after=after,
    )
    pieces = [first, second]
    (
        step_grad, state_grad, conv_grad, bias_grad, convs_grad, biass_grad,
        stepbias_grad, decay_grad, skip_grad, norm_grad, gain_grad,
    ) = unpack(full, wide, model, width, heads)
    return (
        mixed,
        upstream,
        jnp.stack([v[1:] for v in pieces]),
        jnp.swapaxes(step_grad[:, :heads], 1, 2),
        state_grad,
        jnp.swapaxes(jnp.stack([v[0] for v in pieces]), 1, 2),
        conv_grad,
        bias_grad,
        convs_grad,
        biass_grad,
        stepbias_grad,
        decay_grad,
        skip_grad,
        norm_grad,
        gain_grad,
    )


def solution(mesh):
    in_specs = (
        P("dp", None),
        P(None, None, "dp", "tensor"),
        P(None, None, "tensor"),
        P(),
        P(None, "tensor", "dp"),
        P(None, None, "tensor"),
        P(None, "tensor"),
        P(),
        P(),
        P(None, "tensor"),
        P(None, "tensor"),
        P(None, "tensor"),
        P(None, "tensor"),
        P(),
        P("dp", None),
    )
    out_specs = (
        P("dp", None),
        P("dp", None),
        P(None, None, "dp", "tensor"),
        P(None, None, "tensor"),
        P(),
        P(None, "tensor", "dp"),
        P(None, None, "tensor"),
        P(None, "tensor"),
        P(),
        P(),
        P(None, "tensor"),
        P(None, "tensor"),
        P(None, "tensor"),
        P(None, "tensor"),
        P(),
    )
    return jax.shard_map(shards, mesh=mesh, in_specs=in_specs, out_specs=out_specs, check_vma=False)
```

```python
import functools
import math

import jax
import jax.numpy as jnp
from jax import lax
from jax.experimental import pallas as pl
from jax.experimental.pallas import tpu as pltpu
from jax.sharding import PartitionSpec as P

STATE = 128
LEN = 1024
INNER = 3072
HEAD = 64
CHUNK = 128
SLICE = 256
TILE = 256
PACK = 544
SPAN = 400
VMEM_LIMIT = 65000 * 1024
LANES = 128
EPS = 1e-05
LOG2E = 1.4426950408889634

HIGH = lax.Precision.HIGHEST
NN = (((1,), (0,)), ((), ()))
NT = (((1,), (1,)), ((), ()))
TN = (((0,), (0,)), ((), ()))
F32 = jnp.float32
BF16 = jnp.bfloat16
MESH = pl.DeviceIdType.MESH


def remote(src, dst, send, recv, where):
    return pltpu.make_async_remote_copy(
        src_ref=src, dst_ref=dst, send_sem=send, recv_sem=recv, device_id=where, device_id_type=MESH
    )


class Line:
    def __init__(self, size):
        self.n = size // 2
        me = lax.axis_index("dp")
        self.me = me
        self.at = me // 2
        self.side = lax.rem(me, 2)
        self.pair = {"dp": me + 1 - 2 * self.side}
        self.right = {"dp": jnp.minimum(me + 2, size - 1)}
        self.left = {"dp": jnp.maximum(me - 2, 0)}
        odd = lax.rem(self.at, 2)
        self.odd = odd == 1
        self.near = {"dp": me + 2 - 4 * odd}
        self.has_left = self.at > 0
        self.has_right = self.at < self.n - 1

    def greet(self, barrier, more=()):
        for who in more:
            pl.semaphore_signal(barrier, inc=1, device_id=who, device_id_type=MESH)
        pl.semaphore_signal(barrier, inc=1, device_id=self.pair, device_id_type=MESH)

        @pl.when(self.has_left)
        def _():
            pl.semaphore_signal(barrier, inc=1, device_id=self.left, device_id_type=MESH)

        @pl.when(self.has_right)
        def _():
            pl.semaphore_signal(barrier, inc=1, device_id=self.right, device_id_type=MESH)

        peers = 1 + len(more) + self.has_left.astype(jnp.int32) + self.has_right.astype(jnp.int32)
        pl.semaphore_wait(barrier, peers)

    def greet_all(self, barrier, more=()):
        for who in list(more) + [self.pair]:
            pl.semaphore_signal(barrier, inc=1, device_id=who, device_id_type=MESH)
        for i in range(self.n):
            @pl.when(i != self.at)
            def _(i=i):
                pl.semaphore_signal(barrier, inc=1, device_id={"dp": 2 * i + self.side}, device_id_type=MESH)
        pl.semaphore_wait(barrier, self.n + len(more))


def upper(rows):
    return max(16, rows // 32 * 16)


class Gather:
    def __init__(self, line, own, full, keep, send, recv):
        self.line, self.own, self.full, self.keep, self.send, self.recv = line, own, full, keep, send, recv
        self.rows = full.shape[2]
        self.cut = upper(self.rows)

    def copy(self, j, slab, way, src=None, rest=False):
        where = (self.line.right, self.line.left, self.line.pair)[way]
        dst = self.full.at[j, slab]
        if rest:
            dst = self.full.at[j, slab, pl.ds(self.cut, self.rows - self.cut)]
        return remote(dst if src is None else src, dst, self.send.at[j, way, slab], self.recv.at[j, slab], where)

    def shared(self, j, slab, owner):
        part = self.full.at[j, slab, pl.ds(0, self.cut)]
        return remote(part, part, self.send.at[j, 0, slab], self.recv.at[j, owner], self.line.near)

    def start(self, j):
        line = self.line
        pltpu.make_async_copy(self.own(j), self.full.at[j, line.me], self.keep.at[j]).start()

        @pl.when(line.has_right)
        def _():
            self.copy(j, line.me, 0, self.own(j)).start()

        @pl.when(line.has_left)
        def _():
            self.copy(j, line.me, 1, self.own(j)).start()

        self.copy(j, line.me, 2, self.own(j)).start()

    def relay(self, j, k):
        line = self.line

        def forward(slab, way, go_on, near):
            self.copy(j, slab, way).wait_recv()

            @pl.when(go_on)
            def _():
                self.copy(j, slab, way).start()

            if k > 1:
                self.copy(j, slab, 2).start()
            else:
                @pl.when(near)
                def _():
                    self.copy(j, slab, 2, rest=True).start()

                @pl.when(jnp.logical_not(near))
                def _():
                    self.copy(j, slab, 2).start()

        @pl.when(line.at >= k)
        def _():
            forward(line.me - 2 * k, 0, line.has_right, line.odd)

        @pl.when(line.at + k < line.n)
        def _():
            forward(line.me + 2 * k, 1, line.has_left, jnp.logical_not(line.odd))

        if k == 1:
            slab = line.me + 1 - 2 * line.side
            self.copy(j, slab, 2).wait_recv()
            self.shared(j, slab, line.near["dp"]).start()

    def near_slab(self):
        line = self.line
        return line.near["dp"] + 1 - 2 * line.side

    def arrive(self, j):
        line = self.line
        pltpu.make_async_copy(self.own(j), self.full.at[j, line.me], self.keep.at[j]).wait()
        self.copy(j, self.near_slab(), 2, rest=True).wait_recv()
        self.shared(j, self.near_slab(), line.me).wait_recv()
        for place in range(line.n):
            slab = 2 * place + 1 - line.side

            @pl.when((slab != self.near_slab()) & (place != line.at))
            def _(slab=slab):
                self.copy(j, slab, 2).wait_recv()

    def drain(self, j):
        line = self.line
        self.shared(j, line.me + 1 - 2 * line.side, line.near["dp"]).wait_send()
        for place in range(line.n):
            slab = 2 * place + line.side
            near = slab == line.near["dp"]

            @pl.when(near)
            def _(slab=slab):
                self.copy(j, slab, 2, rest=True).wait_send()

            @pl.when(jnp.logical_not(near))
            def _(slab=slab):
                self.copy(j, slab, 2).wait_send()

            @pl.when(line.has_right & (place <= line.at))
            def _(slab=slab):
                self.copy(j, slab, 0).wait_send()

            @pl.when(line.has_left & (place >= line.at))
            def _(slab=slab):
                self.copy(j, slab, 1).wait_send()


class Square:
    def __init__(self):
        me = lax.axis_index("tensor")
        self.me = me
        self.half = lax.rem(me, 2)
        self.mate = {"tensor": me + 1 - 2 * self.half}
        self.across = {"tensor": lax.rem(me + 2, 4)}

    def others(self):
        return [{"tensor": lax.rem(self.me + k, 4)} for k in (1, 2, 3)]


class Total:
    def __init__(self, square, part, got, far, other, send, recv):
        self.square, self.part, self.got, self.far, self.other = square, part, got, far, other
        self.send, self.recv = send, recv

    def first(self, c):
        sq = self.square
        return remote(
            self.part.at[2 * c + 1 - sq.half], self.got.at[c], self.send.at[0, c], self.recv.at[0, c], sq.mate
        )

    def second(self, c):
        sq = self.square
        return remote(self.part.at[2 * c + sq.half], self.far.at[c], self.send.at[1, c], self.recv.at[1, c], sq.across)

    def third(self, c):
        sq = self.square
        return remote(self.part.at[2 * c + sq.half], self.other.at[c], self.send.at[2, c], self.recv.at[2, c], sq.mate)

    def step(self, kind, c):
        slot = 2 * c + self.square.half
        if kind == 0:
            self.first(c).start()
        elif kind == 1:
            self.first(c).wait_recv()
            self.part[slot] = (self.part[slot].astype(F32) + self.got[c].astype(F32)).astype(BF16)
            self.second(c).start()
        elif kind == 2:
            self.second(c).wait()
            self.part[slot] = (self.part[slot].astype(F32) + self.far[c].astype(F32)).astype(BF16)
            self.third(c).start()
        else:
            self.third(c).wait_recv()
            self.first(c).wait_send()
            self.third(c).wait_send()
            self.part[2 * c + 1 - self.square.half] = self.other[c]


class Scatter:
    def __init__(self, line, part, out, near, far, send, recv):
        self.line, self.part, self.out, self.near, self.far = line, part, out, near, far
        self.send, self.recv = send, recv

    def order(self):
        n = self.line.n
        seq = []
        for i in range((n + 1) // 2):
            seq.append(i)
            if n - 1 - i != i:
                seq.append(n - 1 - i)
        return seq

    def cross(self, j, i):
        line = self.line
        return remote(
            self.part.at[j, 2 * i + 1 - line.side], self.near.at[j, i], self.send.at[0, j, i], self.recv.at[0, j, i], line.pair
        )

    def straight(self, j, i, source):
        line = self.line
        return remote(
            self.part.at[j, 2 * i + line.side], self.far.at[j, source], self.send.at[1, j, i], self.recv.at[1, j, source],
            {"dp": 2 * i + line.side},
        )

    def lead(self, j, m):
        self.cross(j, self.order()[m]).start()

    def start(self, j):
        for m in range(self.line.n):
            self.lead(j, m)

    def emit(self, j, turned, right, now=None):
        rows = self.part.shape[2]
        for m, i in enumerate(self.order()):
            value = mm(turned[2 * i * rows : 2 * (i + 1) * rows, :], right[...]).astype(BF16)
            self.part[j, 2 * i] = value[:rows]
            self.part[j, 2 * i + 1] = value[rows:]
            if now is None or m < now:
                self.lead(j, m)

    def fold(self, j, m):
        line = self.line
        i = self.order()[m]
        self.cross(j, i).wait_recv()
        slot = 2 * i + line.side
        self.part[j, slot] = (self.part[j, slot].astype(F32) + self.near[j, i].astype(F32)).astype(BF16)

        @pl.when(i != line.at)
        def _():
            self.straight(j, i, line.at).start()

    def finish(self, j):
        line = self.line
        out = self.out(j)
        out[...] = self.part[j, line.me].astype(out.dtype)
        for i in range(line.n):
            @pl.when(i != line.at)
            def _(i=i):
                self.straight(j, i, i).wait_recv()
                out[...] += self.far[j, i].astype(out.dtype)

    def drain(self, j):
        for i in range(self.line.n):
            self.cross(j, i).wait_send()

            @pl.when(i != self.line.at)
            def _(i=i):
                self.straight(j, i, self.line.at).wait_send()


def mm(left, right, dims=NN, precision=None):
    return lax.dot_general(left, right, dims, precision=precision, preferred_element_type=F32)


def sigmoid(v):
    return 0.5 * jnp.tanh(0.5 * v) + 0.5


def softplus(v):
    return jnp.maximum(v, 0.0) + jnp.log1p(jnp.exp(-jnp.abs(v)))


def split16(v):
    top = v.astype(BF16)
    return top, (v - top.astype(F32)).astype(BF16)


def expand(v, ind):
    top, rest = split16(v)
    return mm(top, ind) + mm(rest, ind)


def headsum(v, ind):
    return mm(v.astype(BF16), ind, NT)


def rowsum(v):
    return mm(jnp.ones((8, v.shape[1]), BF16), v.astype(BF16), NT)[0:1, :]


def iotas(n):
    return (
        lax.broadcasted_iota(jnp.int32, (n, n), 0),
        lax.broadcasted_iota(jnp.int32, (n, n), 1),
    )


def colsum(v):
    return jnp.sum(v, axis=0, keepdims=True)


def conv_pre(ext, par, n):
    total = par[4:5, :] + par[0:1, :] * ext[5 : 5 + n, :]
    for tap in range(1, 4):
        total = total + par[tap : tap + 1, :] * ext[5 + tap : 5 + tap + n, :]
    return total


def scan_prep(small, hp, ind, n):
    rows, cols = iotas(n)
    raw = small[:, 2 * STATE :] + hp[0:1, :]
    step = softplus(raw)
    rate = -jnp.exp(hp[1:2, :])
    lower = jnp.where(rows >= cols, 1.0, 0.0).astype(F32)
    cs = mm(lower, step * rate, precision=HIGH)
    tail = jnp.exp(cs[n - 1 : n, :] - cs)
    wide = mm(jnp.concatenate([step, jnp.exp(cs), tail], axis=0).astype(BF16), ind)
    return raw, step, rate, cs, wide[0:n], wide[n : 2 * n], wide[2 * n : 3 * n]


def block_of(slabs, at, rows):
    step = math.gcd(LANES, rows)
    pieces = []
    for k in range(LANES // step):
        row = at * LANES + k * step
        slab = row // rows
        pieces.append(slabs[slab, pl.ds(pl.multiple_of(row - slab * rows, step), step), :])
    return pieces[0] if len(pieces) == 1 else jnp.concatenate(pieces, axis=0)


def put_params(cp, sp, hp, ind, layer, params):
    conv, bias, norm, convs, biass, head = params
    width = cp.shape[1]
    row = lax.broadcasted_iota(jnp.int32, (LANES, width), 0)
    lane = lax.broadcasted_iota(jnp.int32, (LANES, width), 1)
    ind[...] = jnp.where(lane // HEAD == row, 1.0, 0.0).astype(BF16)
    hp[...] = head[layer]
    cp[0:4, :] = conv[layer]
    cp[4:5, :] = bias[layer : layer + 1, :]
    cp[5:6, :] = norm[layer : layer + 1, :]
    cp[6:8, :] = expand(hp[...], ind[...])[2:4, :]
    sp[0:4, :] = convs[layer]
    sp[4:5, :] = biass[layer : layer + 1, :]


def place_rows(dst, at, value):
    r = dst.shape[1]
    for g in range(0, value.shape[0], 16):
        dst[(at + g) // r, (at + g) % r : (at + g) % r + 16, :] = value[g : g + 16].astype(dst.dtype)


def pack_rows(size):
    return -(-PACK // (16 * size)) * 16


def put_pack(dst, me, turned, steps_low, sdel, dcp, dsp, dhp, dgain):
    model = turned.shape[0]
    quarter = model // 4
    w = sdel.shape[1]

    def empty(n):
        return jnp.zeros((n, w), F32)

    place_rows(dst, 0, mm(turned[pl.ds(pl.multiple_of(me * quarter, quarter), quarter), :], sdel[...]))
    place_rows(dst, quarter, jnp.concatenate([dsp, empty(8)], axis=0))
    grown = mm(turned[...], steps_low[...]).T[:16]
    at = quarter + 16
    for b in range(model // w):
        place_rows(dst, at, grown[:, b * w : (b + 1) * w])
        at += 16
    place_rows(dst, at, jnp.concatenate([dcp[:, :w], dcp[:, w : 2 * w]], axis=0))
    place_rows(dst, at + 16, jnp.concatenate([dcp[:, 2 * w :], jnp.concatenate([dhp, dhp], axis=1)], axis=0))
    rows = [dgain[:, b * w : (b + 1) * w] for b in range(model // w)]
    place_rows(dst, at + 32, jnp.concatenate(rows + [empty(16 - len(rows))], axis=0))
    assert at + 48 == PACK


class Smalls:
    def __init__(self, line, square, pack, near, away, own, full, wide, sems):
        send, recv, keep, gsend, grecv, self.xsend, self.xrecv = sems
        self.square, self.full, self.wide = square, full, wide
        self.layers = range(pack.shape[0])
        self.sum = Scatter(line, pack, lambda j: own.at[j], near, away, send, recv)
        self.spread = Gather(line, lambda j: own.at[j], full, keep, gsend, grecv)

    def swap(self, k):
        sq = self.square
        slot = (sq.me, sq.me, lax.rem(sq.me + 2, 4))[k]
        who = (sq.across, sq.mate, sq.mate)[k]
        return remote(self.wide.at[slot], self.wide.at[slot], self.xsend.at[k], self.xrecv.at[k], who)

    def start(self):
        for j in self.layers:
            self.sum.start(j)

    def fold(self):
        for j in self.layers:
            for m in range(self.sum.line.n):
                self.sum.fold(j, m)

    def turn(self):
        for j in self.layers:
            self.sum.finish(j)
            self.spread.start(j)

    def relay(self, k):
        for j in self.layers:
            self.spread.relay(j, k)

    def cross(self):
        for j in self.layers:
            self.spread.arrive(j)
            flat = self.full[j].reshape(-1, self.full.shape[3])
            self.wide[self.square.me, j] = flat[: self.wide.shape[2]]
        self.swap(0).start()
        self.swap(1).start()

    def cross_on(self):
        self.swap(0).wait_recv()
        self.swap(2).start()

    def end(self):
        self.swap(1).wait_recv()
        self.swap(2).wait_recv()
        for k in range(3):
            self.swap(k).wait_send()
        for j in self.layers:
            self.sum.drain(j)
            self.spread.drain(j)


def smalls_scratch(size, w, layers):
    r, n = pack_rows(size), size // 2
    buffers = [
        pltpu.VMEM((layers, size, r, w), BF16),
        pltpu.VMEM((layers, n, r, w), BF16),
        pltpu.VMEM((layers, n, r, w), BF16),
        pltpu.VMEM((layers, r, w), BF16),
        pltpu.VMEM((layers, size, r, w), BF16),
        pltpu.VMEM((4, layers, SPAN, w), BF16),
    ]
    sems = [
        pltpu.SemaphoreType.DMA((2, layers, n)),
        pltpu.SemaphoreType.DMA((2, layers, n)),
        pltpu.SemaphoreType.DMA((layers,)),
        pltpu.SemaphoreType.DMA((layers, 3, size)),
        pltpu.SemaphoreType.DMA((layers, size)),
        pltpu.SemaphoreType.DMA((3,)),
        pltpu.SemaphoreType.DMA((3,)),
    ]
    return buffers + sems


def forward_body(*refs, size, heads, per, steps, layer):
    refs = list(refs)

    def take(n):
        got = refs[:n]
        del refs[:n]
        return got

    mid = layer > 0
    (res_hbm,) = take(1)
    if mid:
        scaled_hbm, wout_hbm, sq_ref = take(3)
    state_hbm, step_hbm, in_hbm, out_hbm, gain_ref = take(5)
    params = take(6)
    if mid:
        new_hbm, sums_ref = take(2)
    normed_hbm, rnorm_ref, small_hbm, inner_hbm, gate_hbm, wt_hbm, full_hbm, ssd_ref, scaled_ref, sqs_ref, st_ref = take(11)
    if mid:
        scaled_in, wout, part, got, far, other, rows_got, facs, fresh, sends, recvs, rsend, rrecv = take(13)
    res, wstate, wt, slabs, normed, turned, small, inner, gate, ext, exts, state = take(12)
    cp_ref, sp_ref, hp_ref, ind_ref, keep, gsend, grecv, load, sems = take(9)
    assert not refs

    n = CHUNK
    tokens_n, model = res.shape
    width = inner.shape[1]
    top = 2 * width + 2 * STATE
    i = pl.program_id(0)
    line = Line(size)
    square = Square()
    job = Gather(line, lambda j: out_hbm.at[layer] if j == 2 else in_hbm.at[layer, 1 - j], slabs, keep, gsend, grecv)
    outgoing = [(turned, normed_hbm), (small, small_hbm), (inner, inner_hbm), (gate, gate_hbm)]
    outgoing += [(wt, wt_hbm), (slabs.at[2], full_hbm)]
    if mid:
        outgoing.append((fresh, new_hbm))

    def flush(k):
        return pltpu.make_async_copy(*outgoing[k], sems.at[k])


    @pl.when(i == 0)
    def _():
        pairs = [(res_hbm, res), (state_hbm.at[layer], wstate), (step_hbm.at[layer], wt.at[pl.ds(top, LANES), :])]
        if mid:
            pairs = [(scaled_hbm, scaled_in), (wout_hbm, wout)] + pairs
        loads = [pltpu.make_async_copy(src, dst, load.at[k]) for k, (src, dst) in enumerate(pairs)]
        for copy in loads:
            copy.start()
        line.greet(pltpu.get_barrier_semaphore(), square.others() if mid else ())
        job.start(0)
        put_params(cp_ref, sp_ref, hp_ref, ind_ref, layer, params)
        ticks = [functools.partial(job.relay, 0, k) for k in range(1, line.n)]
        ticks.append(functools.partial(job.start, 1))
        ticks += [functools.partial(job.relay, 1, k) for k in range(1, line.n)]
        ticks.append(functools.partial(job.start, 2))

        if mid:
            chunks = model // SLICE
            half = tokens_n // 2
            sums = Total(square, part, got, far, other, sends, recvs)
            copies = [
                remote(sq_ref, rows_got.at[square.me], rsend.at[k], rrecv.at[k], who)
                for k, who in enumerate(square.others())
            ]
            for copy in copies:
                copy.start()
            loads[0].wait()
            loads[1].wait()
            for c in range(chunks):
                value = mm(scaled_in[...], wout[c * SLICE : (c + 1) * SLICE, :], NT).astype(BF16)
                part[2 * c] = value[:half]
                part[2 * c + 1] = value[half:]
                sums.step(0, c)
                if c:
                    sums.step(1, c - 1)
            sums.step(1, chunks - 1)
            rows_got[square.me] = sq_ref[...]
            for copy in copies:
                copy.wait()
            total = (rows_got[0] + rows_got[1]) + (rows_got[2] + rows_got[3])
            sums_ref[...] = total
            factor = lax.rsqrt(total / INNER + EPS)
            for t in range(tokens_n // LANES):
                facs[t * LANES : (t + 1) * LANES, :] = jnp.broadcast_to(factor[t], (LANES, LANES)).T
            loads[2].wait()

            def use(c):
                for h in range(2):
                    where = slice(h * half, (h + 1) * half)
                    for s in range(SLICE // LANES):
                        lanes = slice(c * SLICE + s * LANES, c * SLICE + (s + 1) * LANES)
                        value = part[2 * c + h, :, s * LANES : (s + 1) * LANES].astype(F32)
                        fresh[where, lanes] = res[where, lanes].astype(F32) + facs[where, :] * value

            spread = max(1, -(-len(ticks) // chunks))
            for c in range(chunks):
                for tick in ticks[:spread]:
                    tick()
                ticks = ticks[spread:]
                sums.step(2, c)
                if c:
                    sums.step(3, c - 1)
                    use(c - 1)
            sums.step(3, chunks - 1)
            use(chunks - 1)
            flush(6).start()
        else:
            loads[0].wait()
        loads[-2].wait()
        loads[-1].wait()
        for b in range(2 * STATE // LANES):
            rows = slice(2 * width + b * LANES, 2 * width + (b + 1) * LANES)
            wt[rows, :] = wstate[:, b * LANES : (b + 1) * LANES].T

        def norm(t, _):
            rows = pl.ds(pl.multiple_of(t * TILE, TILE), TILE)
            value = (fresh if mid else res)[rows, :].astype(F32)
            scale = lax.rsqrt(jnp.sum(value * value, axis=1, keepdims=True) / model + EPS)
            low = (value * scale * gain_ref[layer : layer + 1, :]).astype(BF16)
            rnorm_ref[rows, :] = scale
            normed[rows, :] = low
            turned[:, rows] = low.T
            small[rows, : 2 * STATE] = mm(low, wstate[...])
            small[rows, 2 * STATE :] = mm(low, wt[top:, :], NT)
            return 0

        lax.fori_loop(0, tokens_n // TILE, norm, 0)
        flush(0).start()
        flush(1).start()
        for tick in ticks:
            tick()

        def project(j, dst):
            weight = slabs[j].reshape(model, width)

            def tile(t, _):
                rows = pl.ds(pl.multiple_of(t * TILE, TILE), TILE)
                dst[rows, :] = mm(normed[rows, :], weight)
                return 0

            lax.fori_loop(0, tokens_n // TILE, tile, 0)

        for j, dst in ((0, inner), (1, gate)):
            job.arrive(j)
            project(j, dst)
            flush(2 + j).start()

    for k in range(1, line.n):
        @pl.when(i == 1 + (k - 1) * steps // line.n)
        def _(k=k):
            job.relay(2, k)

    @pl.when(i > 0)
    def _():
        at = i - 1
        where = pl.ds(pl.multiple_of(at * n, n), n)

        @pl.when(lax.rem(at, per) == 0)
        def _():
            ext[0:8, :] = jnp.zeros((8, width), F32)
            exts[0:8, :] = jnp.zeros((8, 2 * STATE), F32)
            state[...] = jnp.zeros_like(state)

        rows, cols = iotas(n)
        ind = ind_ref[...]
        ext[8 : 8 + n, :] = inner[where, :]
        pre = conv_pre(ext, cp_ref, n)
        x = pre * sigmoid(pre)
        ext[0:8, :] = ext[n : n + 8, :]
        mini = small[where, :]
        exts[8 : 8 + n, :] = mini[:, : 2 * STATE]
        pres = conv_pre(exts, sp_ref, n)
        bc = (pres * sigmoid(pres)).astype(BF16)
        exts[0:8, :] = exts[n : n + 8, :]
        key, query = bc[:, :STATE], bc[:, STATE:]

        _, step, rate, cs, wide_step, wide_cs, wide_tail = scan_prep(mini, hp_ref, ind, n)
        cs2 = cs * LOG2E
        cs2t = cs2.T
        xs = x * wide_step
        lane = lax.broadcasted_iota(jnp.int32, (1, width), 1)
        half = jnp.where(lax.rem(lane, 2 * HEAD) < HEAD, 1.0, 0.0).astype(BF16)
        xsb = xs.astype(BF16)
        xs0 = xsb * half
        xs1 = xsb - xs0
        before = state[...]
        low = before.astype(BF16)
        st_ref[0] = low
        carried = mm(query, low) * wide_cs
        xw = (xs * wide_tail).astype(BF16)
        state[...] = before * wide_cs[n - 1 : n, :] + mm(key, xw, TN)
        scores = jnp.where(rows >= cols, mm(query, key, NT), 0.0)
        for pair in range(heads // 2):
            lanes = slice(pair * 2 * HEAD, (pair + 1) * 2 * HEAD)
            mats = []
            for h in (2 * pair, 2 * pair + 1):
                dec = jnp.exp2(jnp.minimum(cs2[:, h : h + 1] - cs2t[h : h + 1, :], 0.0))
                mats.append((scores * dec).astype(BF16))
            local = mm(
                jnp.concatenate(mats, axis=1),
                jnp.concatenate([xs0[:, lanes], xs1[:, lanes]], axis=0),
            )
            ssd_ref[:, lanes] = local + carried[:, lanes] + cp_ref[6:7, lanes] * x[:, lanes]
        gates = gate[where, :]
        gated = ssd_ref[...] * (gates * sigmoid(gates))
        sqs_ref[0] = rowsum(gated * gated)
        scaled_ref[...] = (gated * cp_ref[5:6, :]).astype(BF16)

        span = model // LANES
        share = -(-2 * span // steps)
        for k in range(share):
            b = at * share + k

            @pl.when(b < 2 * span)
            def _(b=b):
                j, col = b // span, lax.rem(b, span)
                slab_rows = slabs.shape[2]
                weight = slabs.at[j]
                piece = block_of(weight, col, slab_rows)
                wt[pl.ds(pl.multiple_of(j * width, width), width), pl.ds(pl.multiple_of(col * LANES, LANES), LANES)] = piece.T

    @pl.when(i == steps)
    def _():
        flush(4).start()
        job.arrive(2)
        flush(5).start()
        for j in range(3):
            job.drain(j)
        for k in range(len(outgoing)):
            flush(k).wait()


def forward(res, stateproj, steps_w, inproj, outt, gain, params, heads, size, layer, out=None):
    tokens_n, model = res.shape
    _, _, rows, width = inproj.shape
    top = 2 * width + 2 * STATE + LANES
    steps = tokens_n // CHUNK
    mid = out is not None
    hbm = pl.BlockSpec(memory_space=pl.ANY)
    chunks = model // SLICE

    def whole(a):
        return pl.BlockSpec(a.shape, lambda i: (0,) * len(a.shape))

    def row(w):
        return pl.BlockSpec((CHUNK, w), lambda i: (jnp.maximum(i - 1, 0), 0))

    args, in_specs, out_specs, out_shape, scratch = [res], [hbm], [], [], []
    if mid:
        args += list(out)
        in_specs += [hbm, hbm, whole(out[2])]
        out_specs += [hbm, whole(out[2])]
        out_shape += [jax.ShapeDtypeStruct(res.shape, F32), jax.ShapeDtypeStruct(out[2].shape, F32)]
        chunk = pltpu.VMEM((chunks, tokens_n // 2, SLICE), BF16)
        scratch += [
            pltpu.VMEM(out[0].shape, BF16),
            pltpu.VMEM(out[1].shape, BF16),
            pltpu.VMEM((2 * chunks, tokens_n // 2, SLICE), BF16),
            chunk, chunk, chunk,
            pltpu.VMEM((4,) + out[2].shape, F32),
            pltpu.VMEM((tokens_n, LANES), F32),
            pltpu.VMEM(res.shape, F32),
            pltpu.SemaphoreType.DMA((3, chunks)),
            pltpu.SemaphoreType.DMA((3, chunks)),
            pltpu.SemaphoreType.DMA((3,)),
            pltpu.SemaphoreType.DMA((3,)),
        ]
    args += [stateproj, steps_w, inproj, outt, gain, *params]
    in_specs += [hbm, hbm, hbm, hbm, whole(gain)] + [whole(v) for v in params]
    out_specs += [
        hbm, pl.BlockSpec((tokens_n, 1), lambda i: (0, 0)), hbm, hbm, hbm, hbm, hbm,
        row(width), row(width),
        pl.BlockSpec((1, 1, CHUNK), lambda i: (jnp.maximum(i - 1, 0), 0, 0)),
        pl.BlockSpec((1, STATE, width), lambda i: (jnp.maximum(i - 1, 0), 0, 0)),
    ]
    out_shape += [
        jax.ShapeDtypeStruct((model, tokens_n), BF16),
        jax.ShapeDtypeStruct((tokens_n, 1), F32),
        jax.ShapeDtypeStruct((tokens_n, 2 * STATE + LANES), F32),
        jax.ShapeDtypeStruct((tokens_n, width), F32),
        jax.ShapeDtypeStruct((tokens_n, width), F32),
        jax.ShapeDtypeStruct((top, model), BF16),
        jax.ShapeDtypeStruct((size, rows, width), BF16),
        jax.ShapeDtypeStruct((tokens_n, width), F32),
        jax.ShapeDtypeStruct((tokens_n, width), BF16),
        jax.ShapeDtypeStruct((steps, 1, CHUNK), F32),
        jax.ShapeDtypeStruct((steps, STATE, width), BF16),
    ]
    scratch += [
        pltpu.VMEM(res.shape, res.dtype),
        pltpu.VMEM((model, 2 * STATE), BF16),
        pltpu.VMEM((top, model), BF16),
        pltpu.VMEM((3, size, rows, width), BF16),
        pltpu.VMEM((tokens_n, model), BF16),
        pltpu.VMEM((model, tokens_n), BF16),
        pltpu.VMEM((tokens_n, 2 * STATE + LANES), F32),
        pltpu.VMEM((tokens_n, width), F32),
        pltpu.VMEM((tokens_n, width), F32),
        pltpu.VMEM((CHUNK + 8, width), F32),
        pltpu.VMEM((CHUNK + 8, 2 * STATE), F32),
        pltpu.VMEM((STATE, width), F32),
        pltpu.VMEM((8, width), F32),
        pltpu.VMEM((8, 2 * STATE), F32),
        pltpu.VMEM((8, LANES), F32),
        pltpu.VMEM((LANES, width), BF16),
        pltpu.SemaphoreType.DMA((3,)),
        pltpu.SemaphoreType.DMA((3, 3, size)),
        pltpu.SemaphoreType.DMA((3, size)),
        pltpu.SemaphoreType.DMA((5,)),
        pltpu.SemaphoreType.DMA((7,)),
    ]
    return pl.pallas_call(
        functools.partial(forward_body, size=size, heads=heads, per=LEN // CHUNK, steps=steps, layer=layer),
        grid=(steps + 1,),
        in_specs=in_specs,
        out_specs=out_specs,
        out_shape=out_shape,
        scratch_shapes=scratch,
        compiler_params=pltpu.CompilerParams(
            collective_id=min(layer, 1), has_side_effects=True, vmem_limit_bytes=VMEM_LIMIT
        ),
        name="forward",
    )(*args)


def back_body(*refs, heads, per, size, steps, layer, last):
    refs = list(refs)

    def take(n):
        got = refs[:n]
        del refs[:n]
        return got

    up_ref, sq_ref, gate_ref, ssd_ref, inner_ref, iprev_ref, small_ref, sprev_ref, st_ref, res_ref, rn_ref = take(11)
    gain_ref = take(1)[0]
    params = take(6)
    wout_hbm, scaled_hbm, wt_hbm, normed_hbm = take(4)
    if not last:
        next_normed, next_steps, next_sdel, next_dcp, next_dsp, next_dhp, next_dgain = take(7)
    new_ref, grad_hbm = take(2)
    if last:
        sdsum_ref, steplow_ref, dcp_ref, dsp_ref, dhp_ref, dgain_ref, mixed_ref = take(7)
    else:
        full_hbm, wide_hbm = take(2)
    ext, exts, cde, cdes, dstate, rq, cp_ref, sp_ref, hp_ref, ind_ref = take(10)
    wout, scaled, wt, turned, dy, glow, ilow, frow, srow, sgot = take(10)
    part, near, away, tpart, got, far, other = take(7)
    load, rsend, rrecv, ssend, srecv, sends, recvs, gsem = take(8)
    if last:
        fgot, opart, ogot, ofar, oother, fsend, frecv, osends, orecvs = take(9)
    else:
        dcp_ref, dsp_ref, dhp_ref, dgain_ref, step_all, sd_all = take(6)
        buffers = take(6)
        sems = take(7)
    assert not refs

    n = CHUNK
    model = up_ref.shape[1]
    i = pl.program_id(0)
    begin_gate = steps
    begin_scan = begin_gate + steps
    begin_norm = begin_scan + steps
    end = begin_norm + steps - 1
    line = Line(size)
    square = Square()
    rows_own = part.shape[2]
    count = part.shape[0]
    job = Scatter(line, part, lambda j: dy.at[pl.ds(j * rows_own, rows_own), :], near, away, ssend, srecv)
    sums = Total(square, tpart, got, far, other, sends, recvs)
    if last:
        outs = Total(square, opart, ogot, ofar, oother, osends, orecvs)
        half = steps * n // 2
        slices = model // SLICE
    else:
        minis = Smalls(line, square, *buffers, sems)
    moves = [(wout_hbm, wout), (scaled_hbm, scaled), (wt_hbm, wt), (normed_hbm, turned)]
    if not last:
        tokens_n = steps * n
        spots = (wt.at[pl.ds(0, model), pl.ds(0, tokens_n)],)
        spots += tuple(
            wt.at[pl.ds(0, tokens_n), pl.ds(tokens_n + at, w)] for at, w in ((0, LANES), (LANES, 2 * STATE))
        )
        moves += [(next_normed, spots[0]), (next_steps, spots[1]), (next_sdel, spots[2])]

    def move(k):
        return pltpu.make_async_copy(*moves[k], load.at[k])

    places = line.n

    def spaced(begin, stop, m):
        return begin + m * (stop - begin) // places

    middle = begin_scan + steps // 2
    folds = [(spaced(begin_scan, middle, m), 0, m) for m in range(places)]
    folds += [(spaced(middle, begin_norm, m) + 1, 1, m) for m in range(places)]

    def column(row):
        return jnp.broadcast_to(row, (n, n)).T[:, 0:1]

    @pl.when(i == 0)
    def _():
        for k in range(3):
            move(k).start()
        put_params(cp_ref, sp_ref, hp_ref, ind_ref, layer, params)
        rq[...] = jnp.zeros_like(rq)
        line.greet_all(pltpu.get_barrier_semaphore(), square.others())
        if last:
            rows = [
                remote(sq_ref, fgot.at[square.me], fsend.at[k], frecv.at[k], who)
                for k, who in enumerate(square.others())
            ]
            for copy in rows:
                copy.start()
            fgot[square.me] = sq_ref[...]
            move(0).wait()
            move(1).wait()
            for c in range(slices):
                value = mm(scaled[...], wout[c * SLICE : (c + 1) * SLICE, :], NT).astype(BF16)
                opart[2 * c] = value[:half]
                opart[2 * c + 1] = value[half:]
                outs.step(0, c)
            outs.step(1, 0)
            for copy in rows:
                copy.wait()
            total = (fgot[0] + fgot[1]) + (fgot[2] + fgot[3])
        else:
            total = sq_ref[...]
            move(0).wait()
            move(1).wait()
        dcp_ref[...] = jnp.zeros_like(dcp_ref)
        dsp_ref[...] = jnp.zeros_like(dsp_ref)
        dhp_ref[...] = jnp.zeros_like(dhp_ref)
        dgain_ref[...] = jnp.zeros_like(dgain_ref)
        frow[...] = lax.rsqrt(total / INNER + EPS)

    ind = ind_ref[...]
    for at, j, m in folds:
        @pl.when(i == at)
        def _(j=j, m=m):
            job.fold(j, m)

    @pl.when(i < begin_gate)
    def _():
        rows = pl.ds(pl.multiple_of(i * n, n), n)
        low = (column(frow[i]) * up_ref[...].astype(F32)).astype(BF16)
        turned[:, rows] = low.T
        sd = mm(low, wout[...])
        dy[rows, :] = sd
        piece = scaled[rows, :]
        srow[i] = rowsum(piece.astype(F32) * sd)

    @pl.when(i == begin_gate - 1)
    def _():
        copies = [
            remote(srow, sgot.at[square.me], rsend.at[k], rrecv.at[k], who) for k, who in enumerate(square.others())
        ]
        for copy in copies:
            copy.start()
        job.emit(0, turned, scaled)
        move(3).start()
        sgot[square.me] = srow[...]
        for copy in copies:
            copy.wait()
        srow[...] = (sgot[0] + sgot[1]) + (sgot[2] + sgot[3])

    if last:
        @pl.when(i == steps // 2)
        def _():
            outs.step(1, 1)

        @pl.when((i >= begin_gate) & (i < begin_gate + slices - 2))
        def _():
            outs.step(1, i - begin_gate + 2)

    @pl.when((i >= begin_gate) & (i < begin_scan))
    def _():
        c = i - begin_gate
        rows = pl.ds(pl.multiple_of(c * n, n), n)
        coef = column(frow[c] * frow[c] * srow[c]) / INNER
        gate = gate_ref[...]
        gsig = sigmoid(gate)
        gact = gate * gsig
        ssd = ssd_ref[...]
        sd = dy[rows, :]
        gated = ssd * gact
        gd = cp_ref[5:6, :] * sd - coef * gated
        dcp_ref[5:6, :] += colsum(gated * sd)
        dy[rows, :] = gd * gact
        glow[rows, :] = (gd * ssd * (gsig + gact * (1.0 - gsig))).astype(BF16)

    @pl.when(i == begin_scan - 1)
    def _():
        move(3).wait()
        job.emit(1, turned, glow)
        move(2).wait()

    @pl.when((i >= begin_scan) & (i < begin_norm))
    def _():
        q = i - begin_scan
        chunk = steps - 1 - q
        where = pl.ds(pl.multiple_of(chunk * n, n), n)

        @pl.when(lax.rem(chunk, per) == per - 1)
        def _():
            cde[n : n + 8, :] = jnp.zeros((8, cde.shape[1]), F32)
            cdes[n : n + 8, :] = jnp.zeros((8, cdes.shape[1]), F32)
            dstate[...] = jnp.zeros_like(dstate)

        keep = jnp.where(lax.rem(chunk, per) == 0, 0.0, 1.0).astype(F32)
        rows, cols = iotas(n)
        ext[0:8, :] = iprev_ref[...] * keep
        ext[8 : 8 + n, :] = inner_ref[...]
        exts[0:8, :] = sprev_ref[:, : 2 * STATE] * keep
        exts[8 : 8 + n, :] = small_ref[:, : 2 * STATE]
        pre = conv_pre(ext, cp_ref, n)
        sig = sigmoid(pre)
        x = pre * sig
        slope = sig + x * (1.0 - sig)
        pres = conv_pre(exts, sp_ref, n)
        sigs = sigmoid(pres)
        acts = pres * sigs
        slopes = sigs + acts * (1.0 - sigs)
        bc = acts.astype(BF16)
        key, query = bc[:, :STATE], bc[:, STATE:]
        dyc = dy[where, :]

        raw, step, rate, cs, wide_step, wide_cs, wide_tail = scan_prep(small_ref, hp_ref, ind, n)
        cs2 = cs * LOG2E
        cs2t = cs2.T
        xs = x * wide_step
        xsb = xs.astype(BF16)
        dyb = dyc.astype(BF16)
        lane = lax.broadcasted_iota(jnp.int32, (1, xs.shape[1]), 1)
        half = jnp.where(lax.rem(lane, 2 * HEAD) < HEAD, 1.0, 0.0).astype(BF16)
        dy0 = dyb * half
        dy1 = dyb - dy0
        low = st_ref[0]
        dst = dstate[...]
        dlow = dst.astype(BF16)
        dye = dyc * wide_cs
        dyeb = dye.astype(BF16)
        up = headsum(dye * mm(query, low), ind)
        dxs_state = wide_tail * mm(key, dlow)
        down = headsum(xs * dxs_state, ind)
        qdel = mm(dyeb, low, NT)
        kdel = mm((xs * wide_tail).astype(BF16), dlow, NT)
        through = headsum(jnp.broadcast_to(colsum(low.astype(F32) * dst), (8, dst.shape[1])), ind)[0:1, :]
        through = through * jnp.exp(cs[n - 1 : n, :])
        dstate[...] = dst * wide_cs[n - 1 : n, :] + mm(query, dyeb, TN)

        scores = jnp.where(rows <= cols, mm(key, query, NT), 0.0)
        dscores = jnp.zeros((n, n), F32)
        colq = jnp.zeros((n, LANES), F32)
        lane = lax.broadcasted_iota(jnp.int32, (n, LANES), 1)
        dxs = []
        for pair in range(heads // 2):
            lanes = slice(pair * 2 * HEAD, (pair + 1) * 2 * HEAD)
            stacked = jnp.concatenate([dy0[:, lanes], dy1[:, lanes]], axis=0)
            both = mm(xsb[:, lanes], stacked, NT)
            mats = []
            for which, h in enumerate((2 * pair, 2 * pair + 1)):
                dec = jnp.exp2(jnp.minimum(cs2t[h : h + 1, :] - cs2[:, h : h + 1], 0.0))
                mats.append((scores * dec).astype(BF16))
                term = dec * both[:, which * n : (which + 1) * n]
                dscores = dscores + term
                quad = scores * term
                rq[h : h + 1, :] = colsum(quad)
                colq = jnp.where(lane == h, jnp.sum(quad, axis=1, keepdims=True), colq)
            dxs.append(mm(jnp.concatenate(mats, axis=1), stacked))
        dxs = jnp.concatenate(dxs, axis=1) + dxs_state
        dscores = jnp.where(rows <= cols, dscores, 0.0).astype(BF16)
        kdel = kdel + mm(dscores, query)
        qdel = qdel + mm(dscores, key, TN)

        upper = jnp.where(rows <= cols, 1.0, 0.0).astype(F32)
        strict = jnp.where(rows > cols, 1.0, 0.0).astype(F32)
        da = mm(upper, rq[...].T - colq + up, precision=HIGH) + mm(strict, down, precision=HIGH) + through
        grown = headsum(x * dxs, ind) + rate * da
        step_pre = grown * sigmoid(raw)
        steplow = step_pre.astype(BF16)
        if last:
            steplow_ref[...] = steplow
        else:
            step_all[where, :] = steplow
        dhp_ref[0:1, :] += colsum(step_pre)
        dhp_ref[1:2, :] += rate * colsum(step * da)
        dcp_ref[6:7, :] += colsum(dyc * x)

        cd = (dxs * wide_step + cp_ref[6:7, :] * dyc) * slope
        cde[0:n, :] = cd
        center = ext[8 : 8 + n, :]
        total = cp_ref[3:4, :] * cd
        dcp_ref[3:4, :] += colsum(cd * center)
        for tap in range(3):
            shifted = cde[3 - tap : 3 - tap + n, :]
            total = total + cp_ref[tap : tap + 1, :] * shifted
            dcp_ref[tap : tap + 1, :] += colsum(shifted * center)
        inner_low = total.astype(BF16)
        ilow[where, :] = inner_low
        dcp_ref[4:5, :] += colsum(cd)
        cde[n : n + 8, :] = cde[0:8, :]

        cds = jnp.concatenate([kdel, qdel], axis=1) * slopes
        cdes[0:n, :] = cds
        center = exts[8 : 8 + n, :]
        total = sp_ref[3:4, :] * cds
        dsp_ref[3:4, :] += colsum(cds * center)
        for tap in range(3):
            shifted = cdes[3 - tap : 3 - tap + n, :]
            total = total + sp_ref[tap : tap + 1, :] * shifted
            dsp_ref[tap : tap + 1, :] += colsum(shifted * center)
        sdel = total.astype(BF16)
        dsp_ref[4:5, :] += colsum(cds)
        cdes[n : n + 8, :] = cdes[0:8, :]

        lows = jnp.concatenate([inner_low, glow[where, :], sdel, steplow], axis=1)
        value = mm(lows, wt[...]).astype(BF16)
        tpart[2 * q, :, :model] = value[: n // 2]
        tpart[2 * q + 1, :, :model] = value[n // 2 :]
        tpart[2 * q, :, model:] = sdel[: n // 2]
        tpart[2 * q + 1, :, model:] = sdel[n // 2 :]
        sums.step(0, q)

    @pl.when((i > begin_scan) & (i <= begin_norm))
    def _():
        sums.step(1, i - begin_scan - 1)

    @pl.when((i >= begin_scan + 3) & (i < begin_norm + 3))
    def _():
        sums.step(2, i - begin_scan - 3)

    @pl.when((i >= begin_scan + 4) & (i < begin_norm + 4))
    def _():
        sums.step(3, i - begin_scan - 4)

    if last:
        @pl.when((i > begin_scan) & (i <= begin_scan + slices))
        def _():
            outs.step(2, i - begin_scan - 1)

        @pl.when((i > begin_scan + 1) & (i <= begin_scan + slices + 1))
        def _():
            outs.step(3, i - begin_scan - 2)

    @pl.when(i == begin_norm - 1)
    def _():
        dhp_ref[2:3, :] = headsum(jnp.broadcast_to(dcp_ref[6:7, :], (8, dcp_ref.shape[1])), ind)[0:1, :]
        job.emit(2, turned, ilow, None if last else places // 2)
        if not last:
            for k in (4, 5, 6):
                move(k).start()

    if not last:
        @pl.when(i == begin_norm + 1)
        def _():
            for k in (4, 5, 6):
                move(k).wait()
            put_pack(
                buffers[0].at[1], square.me, *spots, next_dcp[...], next_dsp[...], next_dhp[...], next_dgain[...]
            )
            minis.sum.start(1)

    @pl.when(i >= begin_norm)
    def _():
        r = i - begin_norm
        chunk = steps - 1 - r
        if last:
            fac = column(frow[chunk])
            side = chunk // (steps // 2)
            base = (chunk - side * (steps // 2)) * n
        for h in range(2):
            rows = slice(h * (n // 2), (h + 1) * (n // 2))
            back = tpart[2 * r + h, :, :model].astype(F32)
            sdel = tpart[2 * r + h, :, model:]
            if last:
                sdsum_ref[rows, :] = sdel
            else:
                sd_all[pl.ds(pl.multiple_of(chunk * n + h * (n // 2), n // 2), n // 2), :] = sdel
            res = res_ref[rows, :].astype(F32)
            rn = rn_ref[rows, :]
            dgain_ref[...] += colsum(back * res * rn)
            gained = back * gain_ref[layer : layer + 1, :]
            mean = jnp.sum(gained * res, axis=1, keepdims=True) / model
            new_ref[rows, :] = up_ref[rows, :].astype(F32) + rn * gained - (rn * rn * rn * mean) * res
            if last:
                where = pl.ds(pl.multiple_of(base + h * (n // 2), n // 2), n // 2)
                for c in range(slices):
                    span = slice(c * SLICE, (c + 1) * SLICE)
                    summed = opart[2 * c + side, where, :].astype(F32)
                    mixed_ref[rows, span] = (res[:, span] + fac[rows, :] * summed).astype(BF16)

    @pl.when(i == end)
    def _():
        def finish(j):
            job.finish(j)
            pltpu.make_async_copy(dy.at[pl.ds(j * rows_own, rows_own), :], grad_hbm.at[j], gsem.at[j]).start()

        early = places if last else places // 2
        if not last:
            put_pack(
                buffers[0].at[0], square.me, turned, step_all, sd_all, dcp_ref[...], dsp_ref[...], dhp_ref[...], dgain_ref[...]
            )
            minis.sum.start(0)
            for m in range(places // 2, places):
                job.lead(2, m)
        for m in range(early):
            job.fold(2, m)
        finish(0)
        finish(1)
        if not last:
            minis.fold()
            minis.turn()
            for k in range(1, line.n):
                minis.relay(k)
            for m in range(places // 2, places):
                job.fold(2, m)
            minis.cross()
        finish(2)
        if not last:
            minis.cross_on()
            minis.end()
            tails = [
                pltpu.make_async_copy(src, dst, load.at[k])
                for k, (src, dst) in enumerate(((minis.full, full_hbm), (minis.wide, wide_hbm)))
            ]
            for copy in tails:
                copy.start()
        for j in range(count):
            job.drain(j)
            pltpu.make_async_copy(dy.at[pl.ds(j * rows_own, rows_own), :], grad_hbm.at[j], gsem.at[j]).wait()
        if not last:
            for copy in tails:
                copy.wait()


def back(up, sq, gate_pre, ssd, inner_raw, small, states, res, rnorm, gain, params,
         wout, scaled, wt, normed, heads, size, layer, after=None):
    tokens_n, width = inner_raw.shape
    model = up.shape[1]
    last = after is None
    steps = tokens_n // CHUNK
    begin_scan = 2 * steps
    begin_norm = begin_scan + steps
    rows = model // size
    n = size // 2
    hbm = pl.BlockSpec(memory_space=pl.ANY)
    top = steps - 1

    def norm_at(i):
        return jnp.where(i < begin_norm, top, top - (i - begin_norm))

    def scan_at(i):
        return jnp.clip(top - (i - begin_scan), 0, top)

    def first(w):
        return pl.BlockSpec((CHUNK, w), lambda i: (jnp.where(i < steps, i, norm_at(i)), 0))

    def second(w):
        return pl.BlockSpec((CHUNK, w), lambda i: (jnp.clip(i - steps, 0, top), 0))

    def scan(w):
        return pl.BlockSpec((CHUNK, w), lambda i: (scan_at(i), 0))

    def prev(w):
        return pl.BlockSpec((8, w), lambda i: (jnp.maximum(scan_at(i) * (CHUNK // 8) - 1, 0), 0))

    def norm(w):
        return pl.BlockSpec((CHUNK, w), lambda i: (norm_at(i), 0))

    def whole(a):
        return pl.BlockSpec(a.shape, lambda i: (0,) * len(a.shape))

    extra = model + 2 * STATE
    quarter = pltpu.VMEM((steps, CHUNK // 2, extra), BF16)
    pieces = pltpu.VMEM((3, n, rows, width), BF16)
    args = [up, sq, gate_pre, ssd, inner_raw, inner_raw, small, small, states, res, rnorm, gain, *params,
            wout, scaled, wt, normed]
    in_specs = [
        first(model), whole(sq), second(width), second(width),
        scan(width), prev(width), scan(small.shape[1]), prev(small.shape[1]),
        pl.BlockSpec((1, STATE, width), lambda i: (scan_at(i), 0, 0)),
        norm(model), norm(1), whole(gain),
    ] + [whole(a) for a in params] + [hbm] * 4
    out_specs = [norm(model), hbm]
    out_shape = [jax.ShapeDtypeStruct((tokens_n, model), F32), jax.ShapeDtypeStruct((3, rows, width), F32)]
    totals = [(8, width), (8, 2 * STATE), (8, LANES), (1, model)]
    scratch = [
        pltpu.VMEM((CHUNK + 8, width), F32),
        pltpu.VMEM((CHUNK + 8, 2 * STATE), F32),
        pltpu.VMEM((CHUNK + 8, width), F32),
        pltpu.VMEM((CHUNK + 8, 2 * STATE), F32),
        pltpu.VMEM((STATE, width), F32),
        pltpu.VMEM((LANES, CHUNK), F32),
        pltpu.VMEM((8, width), F32),
        pltpu.VMEM((8, 2 * STATE), F32),
        pltpu.VMEM((8, LANES), F32),
        pltpu.VMEM((LANES, width), BF16),
        pltpu.VMEM(wout.shape, BF16),
        pltpu.VMEM(scaled.shape, BF16),
        pltpu.VMEM(wt.shape, BF16),
        pltpu.VMEM(normed.shape, BF16),
        pltpu.VMEM((tokens_n, width), F32),
        pltpu.VMEM((tokens_n, width), BF16),
        pltpu.VMEM((tokens_n, width), BF16),
        pltpu.VMEM((steps, 1, CHUNK), F32),
        pltpu.VMEM((steps, 1, CHUNK), F32),
        pltpu.VMEM((4, steps, 1, CHUNK), F32),
        pltpu.VMEM((3, size, rows, width), BF16), pieces, pieces,
        pltpu.VMEM((2 * steps, CHUNK // 2, extra), BF16), quarter, quarter, quarter,
        pltpu.SemaphoreType.DMA((7,)),
        pltpu.SemaphoreType.DMA((3,)),
        pltpu.SemaphoreType.DMA((3,)),
        pltpu.SemaphoreType.DMA((2, 3, n)),
        pltpu.SemaphoreType.DMA((2, 3, n)),
        pltpu.SemaphoreType.DMA((3, steps)),
        pltpu.SemaphoreType.DMA((3, steps)),
        pltpu.SemaphoreType.DMA((3,)),
    ]
    if last:
        out_specs += [norm(2 * STATE), scan(LANES)]
        out_specs += [pl.BlockSpec(v, lambda i: (0, 0)) for v in totals] + [norm(model)]
        out_shape += [
            jax.ShapeDtypeStruct((tokens_n, 2 * STATE), BF16),
            jax.ShapeDtypeStruct((tokens_n, LANES), BF16),
        ]
        out_shape += [jax.ShapeDtypeStruct(v, F32) for v in totals]
        out_shape.append(jax.ShapeDtypeStruct((tokens_n, model), BF16))
        slices = model // SLICE
        chunk = pltpu.VMEM((slices, tokens_n // 2, SLICE), BF16)
        scratch += [
            pltpu.VMEM((4, steps, 1, CHUNK), F32),
            pltpu.VMEM((2 * slices, tokens_n // 2, SLICE), BF16), chunk, chunk, chunk,
            pltpu.SemaphoreType.DMA((3,)),
            pltpu.SemaphoreType.DMA((3,)),
            pltpu.SemaphoreType.DMA((3, slices)),
            pltpu.SemaphoreType.DMA((3, slices)),
        ]
    else:
        w = 2 * STATE
        r = pack_rows(size)
        args += list(after)
        in_specs += [hbm] * 3 + [whole(v) for v in after[3:]]
        out_specs += [hbm, hbm]
        out_shape += [
            jax.ShapeDtypeStruct((2, size, r, w), BF16),
            jax.ShapeDtypeStruct((4, 2, SPAN, w), BF16),
        ]
        scratch += [pltpu.VMEM(v, F32) for v in totals]
        scratch += [pltpu.VMEM((tokens_n, LANES), BF16), pltpu.VMEM((tokens_n, w), BF16)]
        scratch += smalls_scratch(size, w, 2)
    return pl.pallas_call(
        functools.partial(
            back_body, heads=heads, per=LEN // CHUNK, size=size, steps=steps, layer=layer, last=last
        ),
        grid=(begin_norm + steps,),
        in_specs=in_specs,
        out_specs=out_specs,
        out_shape=out_shape,
        scratch_shapes=scratch,
        compiler_params=pltpu.CompilerParams(
            collective_id=2 if last else 3, has_side_effects=True, vmem_limit_bytes=VMEM_LIMIT
        ),
        name="back",
    )(*args)


def unpack_body(full_ref, wide_ref, *refs, layers, heads):
    step_ref, state_ref, conv_ref, bias_ref, convs_ref, biass_ref = refs[:6]
    stepbias_ref, decay_ref, skip_ref, norm_ref, gain_ref = refs[6:]
    model = state_ref.shape[1]
    quarter = model // 4
    w = state_ref.shape[2]
    width = conv_ref.shape[2]
    for layer in range(layers):
        for t in range(4):
            state_ref[layer, t * quarter : (t + 1) * quarter, :] = wide_ref[t, layer, :quarter, :].astype(F32)
        taps = [wide_ref[t, layer, quarter : quarter + 16, :].astype(F32) for t in range(4)]
        taps = (taps[0] + taps[1]) + (taps[2] + taps[3])
        convs_ref[layer] = taps[0:4]
        biass_ref[layer : layer + 1, :] = taps[4:5]
        flat = full_ref[layer].reshape(-1, w)[:PACK].astype(F32)
        at = quarter + 16
        for b in range(model // w):
            step_ref[layer, :, b * w : (b + 1) * w] = flat[at : at + 16]
            at += 16
        for b in range(width // w):
            lanes = slice(b * w, (b + 1) * w)
            rows = flat[at + 8 * b : at + 8 * b + 8]
            conv_ref[layer, :, lanes] = rows[0:4]
            bias_ref[layer : layer + 1, lanes] = rows[4:5]
            norm_ref[layer : layer + 1, lanes] = rows[5:6]
        at += 8 * (width // w)
        for k, ref in enumerate((stepbias_ref, decay_ref, skip_ref)):
            ref[layer : layer + 1, :] = flat[at + k : at + k + 1, :heads]
        at += 8
        for b in range(model // w):
            gain_ref[layer : layer + 1, b * w : (b + 1) * w] = flat[at + b : at + b + 1]


def unpack(full, wide, model, width, heads):
    layers, w = full.shape[0], full.shape[3]
    vm = pl.BlockSpec(memory_space=pltpu.VMEM)
    shapes = [
        (layers, 16, model), (layers, model, w), (layers, 4, width), (layers, width), (layers, 4, w), (layers, w),
        (layers, heads), (layers, heads), (layers, heads), (layers, width), (layers, model),
    ]
    return pl.pallas_call(
        functools.partial(unpack_body, layers=layers, heads=heads),
        in_specs=[vm, vm],
        out_specs=[vm] * len(shapes),
        out_shape=[jax.ShapeDtypeStruct(v, F32) for v in shapes],
        compiler_params=pltpu.CompilerParams(vmem_limit_bytes=VMEM_LIMIT),
        name="unpack",
    )(full, wide)


def shards(
    tokens, inproj, stepproj, stateproj, outproj, convinner, biasinner, convstate, biasstate,
    stepbias, decaylog, skipgain, normgain, inputgain, cotangent,
):
    layers = inproj.shape[0]
    width = inproj.shape[3]
    heads = stepproj.shape[2]
    model = tokens.shape[1]
    pad = LANES - heads
    size = lax.axis_size("dp")
    steps_w = jnp.pad(jnp.swapaxes(stepproj, 1, 2), ((0, 0), (0, pad), (0, 0)))
    head = jnp.pad(jnp.stack([stepbias, decaylog, skipgain], axis=1), ((0, 0), (0, 5), (0, pad)))
    outt = jnp.swapaxes(outproj, 1, 2)
    params = (convinner, biasinner, normgain, convstate, biasstate, head)

    residual = tokens
    kept = []
    out = None
    for at in range(layers):
        results = forward(residual, stateproj, steps_w, inproj, outt, inputgain, params, heads, size, at, out=out)
        if at:
            residual, kept[-1][-1] = results[:2]
            results = results[2:]
        normed, rnorm, small, inner_raw, gate_pre, wt, w_out, ssd, scaled, sq, states = results
        w_out = w_out.reshape(model, width)
        kept.append([residual, normed, rnorm, small, inner_raw, gate_pre, wt, w_out, ssd, scaled, states, sq])
        out = (scaled, w_out, sq)

    assert layers == 2
    before, normed, rnorm, small, inner_raw, gate_pre, wt, w_out, ssd, scaled, states, sq = kept[1]
    upstream, second, sdel, steplow, *totals, mixed = back(
        cotangent, sq, gate_pre, ssd, inner_raw, small, states, before, rnorm, inputgain, params,
        w_out, scaled, wt, normed, heads, size, 1,
    )
    after = (normed, steplow, sdel, *totals)
    before, normed, rnorm, small, inner_raw, gate_pre, wt, w_out, ssd, scaled, states, sq = kept[0]
    upstream, first, full, wide = back(
        upstream, sq, gate_pre, ssd, inner_raw, small, states, before, rnorm, inputgain, params,
        w_out, scaled, wt, normed, heads, size, 0, after=after,
    )
    pieces = [first, second]
    (
        step_grad, state_grad, conv_grad, bias_grad, convs_grad, biass_grad,
        stepbias_grad, decay_grad, skip_grad, norm_grad, gain_grad,
    ) = unpack(full, wide, model, width, heads)
    return (
        mixed,
        upstream,
        jnp.stack([v[1:] for v in pieces]),
        jnp.swapaxes(step_grad[:, :heads], 1, 2),
        state_grad,
        jnp.swapaxes(jnp.stack([v[0] for v in pieces]), 1, 2),
        conv_grad,
        bias_grad,
        convs_grad,
        biass_grad,
        stepbias_grad,
        decay_grad,
        skip_grad,
        norm_grad,
        gain_grad,
    )


def solution(mesh):
    in_specs = (
        P("dp", None),
        P(None, None, "dp", "tensor"),
        P(None, None, "tensor"),
        P(),
        P(None, "tensor", "dp"),
        P(None, None, "tensor"),
        P(None, "tensor"),
        P(),
        P(),
        P(None, "tensor"),
        P(None, "tensor"),
        P(None, "tensor"),
        P(None, "tensor"),
        P(),
        P("dp", None),
    )
    out_specs = (
        P("dp", None),
        P("dp", None),
        P(None, None, "dp", "tensor"),
        P(None, None, "tensor"),
        P(),
        P(None, "tensor", "dp"),
        P(None, None, "tensor"),
        P(None, "tensor"),
        P(),
        P(),
        P(None, "tensor"),
        P(None, "tensor"),
        P(None, "tensor"),
        P(None, "tensor"),
        P(),
    )
    return jax.shard_map(shards, mesh=mesh, in_specs=in_specs, out_specs=out_specs, check_vma=False)
```

```python
import functools
import math

import jax
import jax.numpy as jnp
from jax import lax
from jax.experimental import pallas as pl
from jax.experimental.pallas import tpu as pltpu
from jax.sharding import PartitionSpec as P

STATE = 128
LEN = 1024
INNER = 3072
HEAD = 64
CHUNK = 128
SLICE = 256
TILE = 256
PACK = 544
SPAN = 400
VMEM_LIMIT = 65000 * 1024
LANES = 128
EPS = 1e-05
LOG2E = 1.4426950408889634

HIGH = lax.Precision.HIGHEST
NN = (((1,), (0,)), ((), ()))
NT = (((1,), (1,)), ((), ()))
TN = (((0,), (0,)), ((), ()))
F32 = jnp.float32
BF16 = jnp.bfloat16
MESH = pl.DeviceIdType.MESH


def remote(src, dst, send, recv, where):
    return pltpu.make_async_remote_copy(
        src_ref=src, dst_ref=dst, send_sem=send, recv_sem=recv, device_id=where, device_id_type=MESH
    )


class Line:
    def __init__(self, size):
        self.n = size // 2
        me = lax.axis_index("dp")
        self.me = me
        self.at = me // 2
        self.side = lax.rem(me, 2)
        self.pair = {"dp": me + 1 - 2 * self.side}
        self.right = {"dp": jnp.minimum(me + 2, size - 1)}
        self.left = {"dp": jnp.maximum(me - 2, 0)}
        odd = lax.rem(self.at, 2)
        self.odd = odd == 1
        self.near = {"dp": me + 2 - 4 * odd}
        self.has_left = self.at > 0
        self.has_right = self.at < self.n - 1

    def greet(self, barrier, more=()):
        for who in more:
            pl.semaphore_signal(barrier, inc=1, device_id=who, device_id_type=MESH)
        pl.semaphore_signal(barrier, inc=1, device_id=self.pair, device_id_type=MESH)

        @pl.when(self.has_left)
        def _():
            pl.semaphore_signal(barrier, inc=1, device_id=self.left, device_id_type=MESH)

        @pl.when(self.has_right)
        def _():
            pl.semaphore_signal(barrier, inc=1, device_id=self.right, device_id_type=MESH)

        peers = 1 + len(more) + self.has_left.astype(jnp.int32) + self.has_right.astype(jnp.int32)
        pl.semaphore_wait(barrier, peers)

    def greet_all(self, barrier, more=()):
        for who in list(more) + [self.pair]:
            pl.semaphore_signal(barrier, inc=1, device_id=who, device_id_type=MESH)
        for i in range(self.n):
            @pl.when(i != self.at)
            def _(i=i):
                pl.semaphore_signal(barrier, inc=1, device_id={"dp": 2 * i + self.side}, device_id_type=MESH)
        pl.semaphore_wait(barrier, self.n + len(more))


def upper(rows):
    return max(16, rows // 32 * 16)


class Gather:
    def __init__(self, line, own, full, keep, send, recv):
        self.line, self.own, self.full, self.keep, self.send, self.recv = line, own, full, keep, send, recv
        self.rows = full.shape[2]
        self.cut = upper(self.rows)

    def copy(self, j, slab, way, src=None, rest=False):
        where = (self.line.right, self.line.left, self.line.pair)[way]
        dst = self.full.at[j, slab]
        if rest:
            dst = self.full.at[j, slab, pl.ds(self.cut, self.rows - self.cut)]
        return remote(dst if src is None else src, dst, self.send.at[j, way, slab], self.recv.at[j, slab], where)

    def shared(self, j, slab, owner):
        part = self.full.at[j, slab, pl.ds(0, self.cut)]
        return remote(part, part, self.send.at[j, 0, slab], self.recv.at[j, owner], self.line.near)

    def start(self, j):
        line = self.line
        pltpu.make_async_copy(self.own(j), self.full.at[j, line.me], self.keep.at[j]).start()

        @pl.when(line.has_right)
        def _():
            self.copy(j, line.me, 0, self.own(j)).start()

        @pl.when(line.has_left)
        def _():
            self.copy(j, line.me, 1, self.own(j)).start()

        self.copy(j, line.me, 2, self.own(j)).start()

    def relay(self, j, k):
        line = self.line

        def forward(slab, way, go_on, near):
            self.copy(j, slab, way).wait_recv()

            @pl.when(go_on)
            def _():
                self.copy(j, slab, way).start()

            if k > 1:
                self.copy(j, slab, 2).start()
            else:
                @pl.when(near)
                def _():
                    self.copy(j, slab, 2, rest=True).start()

                @pl.when(jnp.logical_not(near))
                def _():
                    self.copy(j, slab, 2).start()

        @pl.when(line.at >= k)
        def _():
            forward(line.me - 2 * k, 0, line.has_right, line.odd)

        @pl.when(line.at + k < line.n)
        def _():
            forward(line.me + 2 * k, 1, line.has_left, jnp.logical_not(line.odd))

        if k == 1:
            slab = line.me + 1 - 2 * line.side
            self.copy(j, slab, 2).wait_recv()
            self.shared(j, slab, line.near["dp"]).start()

    def near_slab(self):
        line = self.line
        return line.near["dp"] + 1 - 2 * line.side

    def arrive(self, j):
        line = self.line
        pltpu.make_async_copy(self.own(j), self.full.at[j, line.me], self.keep.at[j]).wait()
        self.copy(j, self.near_slab(), 2, rest=True).wait_recv()
        self.shared(j, self.near_slab(), line.me).wait_recv()
        for place in range(line.n):
            slab = 2 * place + 1 - line.side

            @pl.when((slab != self.near_slab()) & (place != line.at))
            def _(slab=slab):
                self.copy(j, slab, 2).wait_recv()

    def drain(self, j):
        line = self.line
        self.shared(j, line.me + 1 - 2 * line.side, line.near["dp"]).wait_send()
        for place in range(line.n):
            slab = 2 * place + line.side
            near = slab == line.near["dp"]

            @pl.when(near)
            def _(slab=slab):
                self.copy(j, slab, 2, rest=True).wait_send()

            @pl.when(jnp.logical_not(near))
            def _(slab=slab):
                self.copy(j, slab, 2).wait_send()

            @pl.when(line.has_right & (place <= line.at))
            def _(slab=slab):
                self.copy(j, slab, 0).wait_send()

            @pl.when(line.has_left & (place >= line.at))
            def _(slab=slab):
                self.copy(j, slab, 1).wait_send()


class Square:
    def __init__(self):
        me = lax.axis_index("tensor")
        self.me = me
        self.half = lax.rem(me, 2)
        self.mate = {"tensor": me + 1 - 2 * self.half}
        self.across = {"tensor": lax.rem(me + 2, 4)}

    def others(self):
        return [{"tensor": lax.rem(self.me + k, 4)} for k in (1, 2, 3)]


class Total:
    def __init__(self, square, part, got, far, other, send, recv):
        self.square, self.part, self.got, self.far, self.other = square, part, got, far, other
        self.send, self.recv = send, recv

    def first(self, c):
        sq = self.square
        return remote(
            self.part.at[2 * c + 1 - sq.half], self.got.at[c], self.send.at[0, c], self.recv.at[0, c], sq.mate
        )

    def second(self, c):
        sq = self.square
        return remote(self.part.at[2 * c + sq.half], self.far.at[c], self.send.at[1, c], self.recv.at[1, c], sq.across)

    def third(self, c):
        sq = self.square
        return remote(self.part.at[2 * c + sq.half], self.other.at[c], self.send.at[2, c], self.recv.at[2, c], sq.mate)

    def step(self, kind, c):
        slot = 2 * c + self.square.half
        if kind == 0:
            self.first(c).start()
        elif kind == 1:
            self.first(c).wait_recv()
            self.part[slot] = (self.part[slot].astype(F32) + self.got[c].astype(F32)).astype(BF16)
            self.second(c).start()
        elif kind == 2:
            self.second(c).wait()
            self.part[slot] = (self.part[slot].astype(F32) + self.far[c].astype(F32)).astype(BF16)
            self.third(c).start()
        else:
            self.third(c).wait_recv()
            self.first(c).wait_send()
            self.third(c).wait_send()
            self.part[2 * c + 1 - self.square.half] = self.other[c]


class Scatter:
    def __init__(self, line, part, out, near, far, send, recv):
        self.line, self.part, self.out, self.near, self.far = line, part, out, near, far
        self.send, self.recv = send, recv

    def order(self):
        n = self.line.n
        seq = []
        for i in range((n + 1) // 2):
            seq.append(i)
            if n - 1 - i != i:
                seq.append(n - 1 - i)
        return seq

    def cross(self, j, i):
        line = self.line
        return remote(
            self.part.at[j, 2 * i + 1 - line.side], self.near.at[j, i], self.send.at[0, j, i], self.recv.at[0, j, i], line.pair
        )

    def straight(self, j, i, source):
        line = self.line
        return remote(
            self.part.at[j, 2 * i + line.side], self.far.at[j, source], self.send.at[1, j, i], self.recv.at[1, j, source],
            {"dp": 2 * i + line.side},
        )

    def lead(self, j, m):
        self.cross(j, self.order()[m]).start()

    def start(self, j):
        for m in range(self.line.n):
            self.lead(j, m)

    def emit(self, j, turned, right, now=None):
        rows = self.part.shape[2]
        for m, i in enumerate(self.order()):
            value = mm(turned[2 * i * rows : 2 * (i + 1) * rows, :], right[...]).astype(BF16)
            self.part[j, 2 * i] = value[:rows]
            self.part[j, 2 * i + 1] = value[rows:]
            if now is None or m < now:
                self.lead(j, m)

    def fold(self, j, m):
        line = self.line
        i = self.order()[m]
        self.cross(j, i).wait_recv()
        slot = 2 * i + line.side
        self.part[j, slot] = (self.part[j, slot].astype(F32) + self.near[j, i].astype(F32)).astype(BF16)

        @pl.when(i != line.at)
        def _():
            self.straight(j, i, line.at).start()

    def finish(self, j):
        line = self.line
        out = self.out(j)
        out[...] = self.part[j, line.me].astype(out.dtype)
        for i in range(line.n):
            @pl.when(i != line.at)
            def _(i=i):
                self.straight(j, i, i).wait_recv()
                out[...] += self.far[j, i].astype(out.dtype)

    def drain(self, j):
        for i in range(self.line.n):
            self.cross(j, i).wait_send()

            @pl.when(i != self.line.at)
            def _(i=i):
                self.straight(j, i, self.line.at).wait_send()


def mm(left, right, dims=NN, precision=None):
    return lax.dot_general(left, right, dims, precision=precision, preferred_element_type=F32)


def sigmoid(v):
    return 0.5 * jnp.tanh(0.5 * v) + 0.5


def softplus(v):
    return jnp.maximum(v, 0.0) + jnp.log1p(jnp.exp(-jnp.abs(v)))


def split16(v):
    top = v.astype(BF16)
    return top, (v - top.astype(F32)).astype(BF16)


def expand(v, ind):
    top, rest = split16(v)
    return mm(top, ind) + mm(rest, ind)


def headsum(v, ind):
    return mm(v.astype(BF16), ind, NT)


def rowsum(v):
    return mm(jnp.ones((8, v.shape[1]), BF16), v.astype(BF16), NT)[0:1, :]


def iotas(n):
    return (
        lax.broadcasted_iota(jnp.int32, (n, n), 0),
        lax.broadcasted_iota(jnp.int32, (n, n), 1),
    )


def colsum(v):
    return jnp.sum(v, axis=0, keepdims=True)


def conv_pre(ext, par, n):
    total = par[4:5, :] + par[0:1, :] * ext[5 : 5 + n, :]
    for tap in range(1, 4):
        total = total + par[tap : tap + 1, :] * ext[5 + tap : 5 + tap + n, :]
    return total


def scan_prep(small, hp, ind, n):
    rows, cols = iotas(n)
    raw = small[:, 2 * STATE :] + hp[0:1, :]
    step = softplus(raw)
    rate = -jnp.exp(hp[1:2, :])
    lower = jnp.where(rows >= cols, 1.0, 0.0).astype(F32)
    cs = mm(lower, step * rate, precision=HIGH)
    tail = jnp.exp(cs[n - 1 : n, :] - cs)
    wide = mm(jnp.concatenate([step, jnp.exp(cs), tail], axis=0).astype(BF16), ind)
    return raw, step, rate, cs, wide[0:n], wide[n : 2 * n], wide[2 * n : 3 * n]


def block_of(slabs, at, rows):
    step = math.gcd(LANES, rows)
    pieces = []
    for k in range(LANES // step):
        row = at * LANES + k * step
        slab = row // rows
        pieces.append(slabs[slab, pl.ds(pl.multiple_of(row - slab * rows, step), step), :])
    return pieces[0] if len(pieces) == 1 else jnp.concatenate(pieces, axis=0)


def put_params(cp, sp, hp, ind, layer, params):
    conv, bias, norm, convs, biass, head = params
    width = cp.shape[1]
    row = lax.broadcasted_iota(jnp.int32, (LANES, width), 0)
    lane = lax.broadcasted_iota(jnp.int32, (LANES, width), 1)
    ind[...] = jnp.where(lane // HEAD == row, 1.0, 0.0).astype(BF16)
    hp[...] = head[layer]
    cp[0:4, :] = conv[layer]
    cp[4:5, :] = bias[layer : layer + 1, :]
    cp[5:6, :] = norm[layer : layer + 1, :]
    cp[6:8, :] = expand(hp[...], ind[...])[2:4, :]
    sp[0:4, :] = convs[layer]
    sp[4:5, :] = biass[layer : layer + 1, :]


def place_rows(dst, at, value):
    r = dst.shape[1]
    for g in range(0, value.shape[0], 16):
        dst[(at + g) // r, (at + g) % r : (at + g) % r + 16, :] = value[g : g + 16].astype(dst.dtype)


def pack_rows(size):
    return -(-PACK // (16 * size)) * 16


def put_pack(dst, me, turned, steps_low, sdel, dcp, dsp, dhp, dgain):
    model = turned.shape[0]
    quarter = model // 4
    w = sdel.shape[1]

    def empty(n):
        return jnp.zeros((n, w), F32)

    place_rows(dst, 0, mm(turned[pl.ds(pl.multiple_of(me * quarter, quarter), quarter), :], sdel[...]))
    place_rows(dst, quarter, jnp.concatenate([dsp, empty(8)], axis=0))
    grown = mm(turned[...], steps_low[...]).T[:16]
    at = quarter + 16
    for b in range(model // w):
        place_rows(dst, at, grown[:, b * w : (b + 1) * w])
        at += 16
    place_rows(dst, at, jnp.concatenate([dcp[:, :w], dcp[:, w : 2 * w]], axis=0))
    place_rows(dst, at + 16, jnp.concatenate([dcp[:, 2 * w :], jnp.concatenate([dhp, dhp], axis=1)], axis=0))
    rows = [dgain[:, b * w : (b + 1) * w] for b in range(model // w)]
    place_rows(dst, at + 32, jnp.concatenate(rows + [empty(16 - len(rows))], axis=0))
    assert at + 48 == PACK


class Smalls:
    def __init__(self, line, square, pack, near, away, own, full, wide, sems):
        send, recv, keep, gsend, grecv, self.xsend, self.xrecv = sems
        self.square, self.full, self.wide = square, full, wide
        self.layers = range(pack.shape[0])
        self.sum = Scatter(line, pack, lambda j: own.at[j], near, away, send, recv)
        self.spread = Gather(line, lambda j: own.at[j], full, keep, gsend, grecv)

    def swap(self, k):
        sq = self.square
        slot = (sq.me, sq.me, lax.rem(sq.me + 2, 4))[k]
        who = (sq.across, sq.mate, sq.mate)[k]
        return remote(self.wide.at[slot], self.wide.at[slot], self.xsend.at[k], self.xrecv.at[k], who)

    def start(self):
        for j in self.layers:
            self.sum.start(j)

    def fold(self):
        for j in self.layers:
            for m in range(self.sum.line.n):
                self.sum.fold(j, m)

    def turn(self):
        for j in self.layers:
            self.sum.finish(j)
            self.spread.start(j)

    def relay(self, k):
        for j in self.layers:
            self.spread.relay(j, k)

    def cross(self):
        for j in self.layers:
            self.spread.arrive(j)
            flat = self.full[j].reshape(-1, self.full.shape[3])
            self.wide[self.square.me, j] = flat[: self.wide.shape[2]]
        self.swap(0).start()
        self.swap(1).start()

    def cross_on(self):
        self.swap(0).wait_recv()
        self.swap(2).start()

    def end(self):
        self.swap(1).wait_recv()
        self.swap(2).wait_recv()
        for k in range(3):
            self.swap(k).wait_send()
        for j in self.layers:
            self.sum.drain(j)
            self.spread.drain(j)


def smalls_scratch(size, w, layers):
    r, n = pack_rows(size), size // 2
    buffers = [
        pltpu.VMEM((layers, size, r, w), BF16),
        pltpu.VMEM((layers, n, r, w), BF16),
        pltpu.VMEM((layers, n, r, w), BF16),
        pltpu.VMEM((layers, r, w), BF16),
        pltpu.VMEM((layers, size, r, w), BF16),
        pltpu.VMEM((4, layers, SPAN, w), BF16),
    ]
    sems = [
        pltpu.SemaphoreType.DMA((2, layers, n)),
        pltpu.SemaphoreType.DMA((2, layers, n)),
        pltpu.SemaphoreType.DMA((layers,)),
        pltpu.SemaphoreType.DMA((layers, 3, size)),
        pltpu.SemaphoreType.DMA((layers, size)),
        pltpu.SemaphoreType.DMA((3,)),
        pltpu.SemaphoreType.DMA((3,)),
    ]
    return buffers + sems


def forward_body(*refs, size, heads, per, steps, layer):
    refs = list(refs)

    def take(n):
        got = refs[:n]
        del refs[:n]
        return got

    mid = layer > 0
    (res_hbm,) = take(1)
    if mid:
        scaled_hbm, wout_hbm, sq_ref = take(3)
    state_hbm, step_hbm, in_hbm, out_hbm, gain_ref = take(5)
    params = take(6)
    if mid:
        new_hbm, sums_ref = take(2)
    normed_hbm, rnorm_ref, small_hbm, inner_hbm, gate_hbm, wt_hbm, full_hbm, ssd_ref, scaled_ref, sqs_ref, st_ref = take(11)
    if mid:
        scaled_in, wout, part, got, far, other, rows_got, facs, fresh, sends, recvs, rsend, rrecv = take(13)
    res, wstate, wt, slabs, normed, turned, small, inner, gate, ext, exts, state = take(12)
    cp_ref, sp_ref, hp_ref, ind_ref, keep, gsend, grecv, load, sems = take(9)
    assert not refs

    n = CHUNK
    tokens_n, model = res.shape
    width = inner.shape[1]
    top = 2 * width + 2 * STATE
    i = pl.program_id(0)
    line = Line(size)
    square = Square()
    job = Gather(line, lambda j: out_hbm.at[layer] if j == 2 else in_hbm.at[layer, 1 - j], slabs, keep, gsend, grecv)
    outgoing = [(turned, normed_hbm), (small, small_hbm), (inner, inner_hbm), (gate, gate_hbm)]
    outgoing += [(wt, wt_hbm), (slabs.at[2], full_hbm)]
    if mid:
        outgoing.append((fresh, new_hbm))

    def flush(k):
        return pltpu.make_async_copy(*outgoing[k], sems.at[k])


    @pl.when(i == 0)
    def _():
        pairs = [(res_hbm, res), (state_hbm.at[layer], wstate), (step_hbm.at[layer], wt.at[pl.ds(top, LANES), :])]
        if mid:
            pairs = [(scaled_hbm, scaled_in), (wout_hbm, wout)] + pairs
        loads = [pltpu.make_async_copy(src, dst, load.at[k]) for k, (src, dst) in enumerate(pairs)]
        for copy in loads:
            copy.start()
        line.greet(pltpu.get_barrier_semaphore(), square.others() if mid else ())
        job.start(0)
        put_params(cp_ref, sp_ref, hp_ref, ind_ref, layer, params)
        ticks = [functools.partial(job.relay, 0, k) for k in range(1, line.n)]
        ticks.append(functools.partial(job.start, 1))
        ticks += [functools.partial(job.relay, 1, k) for k in range(1, line.n)]
        ticks.append(functools.partial(job.start, 2))

        if mid:
            chunks = model // SLICE
            half = tokens_n // 2
            sums = Total(square, part, got, far, other, sends, recvs)
            copies = [
                remote(sq_ref, rows_got.at[square.me], rsend.at[k], rrecv.at[k], who)
                for k, who in enumerate(square.others())
            ]
            for copy in copies:
                copy.start()
            loads[0].wait()
            loads[1].wait()
            for c in range(chunks):
                value = mm(scaled_in[...], wout[c * SLICE : (c + 1) * SLICE, :], NT).astype(BF16)
                part[2 * c] = value[:half]
                part[2 * c + 1] = value[half:]
                sums.step(0, c)
                if c:
                    sums.step(1, c - 1)
            sums.step(1, chunks - 1)
            rows_got[square.me] = sq_ref[...]
            for copy in copies:
                copy.wait()
            total = (rows_got[0] + rows_got[1]) + (rows_got[2] + rows_got[3])
            sums_ref[...] = total
            factor = lax.rsqrt(total / INNER + EPS)
            for t in range(tokens_n // LANES):
                facs[t * LANES : (t + 1) * LANES, :] = jnp.broadcast_to(factor[t], (LANES, LANES)).T
            loads[2].wait()

            def use(c):
                for h in range(2):
                    where = slice(h * half, (h + 1) * half)
                    for s in range(SLICE // LANES):
                        lanes = slice(c * SLICE + s * LANES, c * SLICE + (s + 1) * LANES)
                        value = part[2 * c + h, :, s * LANES : (s + 1) * LANES].astype(F32)
                        fresh[where, lanes] = res[where, lanes].astype(F32) + facs[where, :] * value

            spread = max(1, -(-len(ticks) // chunks))
            for c in range(chunks):
                for tick in ticks[:spread]:
                    tick()
                ticks = ticks[spread:]
                sums.step(2, c)
                if c:
                    sums.step(3, c - 1)
                    use(c - 1)
            sums.step(3, chunks - 1)
            use(chunks - 1)
            flush(6).start()
        else:
            loads[0].wait()
        loads[-2].wait()
        loads[-1].wait()
        for b in range(2 * STATE // LANES):
            rows = slice(2 * width + b * LANES, 2 * width + (b + 1) * LANES)
            wt[rows, :] = wstate[:, b * LANES : (b + 1) * LANES].T

        def norm(t, _):
            rows = pl.ds(pl.multiple_of(t * TILE, TILE), TILE)
            value = (fresh if mid else res)[rows, :].astype(F32)
            scale = lax.rsqrt(jnp.sum(value * value, axis=1, keepdims=True) / model + EPS)
            low = (value * scale * gain_ref[layer : layer + 1, :]).astype(BF16)
            rnorm_ref[rows, :] = scale
            normed[rows, :] = low
            turned[:, rows] = low.T
            small[rows, : 2 * STATE] = mm(low, wstate[...])
            small[rows, 2 * STATE :] = mm(low, wt[top:, :], NT)
            return 0

        lax.fori_loop(0, tokens_n // TILE, norm, 0)
        flush(0).start()
        flush(1).start()
        for tick in ticks:
            tick()

        def project(j, dst):
            weight = slabs[j].reshape(model, width)

            def tile(t, _):
                rows = pl.ds(pl.multiple_of(t * TILE, TILE), TILE)
                dst[rows, :] = mm(normed[rows, :], weight)
                return 0

            lax.fori_loop(0, tokens_n // TILE, tile, 0)

        for j, dst in ((0, inner), (1, gate)):
            job.arrive(j)
            project(j, dst)
            flush(2 + j).start()

    for k in range(1, line.n):
        @pl.when(i == 1 + (k - 1) * steps // line.n)
        def _(k=k):
            job.relay(2, k)

    @pl.when(i > 0)
    def _():
        at = i - 1
        where = pl.ds(pl.multiple_of(at * n, n), n)

        @pl.when(lax.rem(at, per) == 0)
        def _():
            ext[0:8, :] = jnp.zeros((8, width), F32)
            exts[0:8, :] = jnp.zeros((8, 2 * STATE), F32)
            state[...] = jnp.zeros_like(state)

        rows, cols = iotas(n)
        ind = ind_ref[...]
        ext[8 : 8 + n, :] = inner[where, :]
        pre = conv_pre(ext, cp_ref, n)
        x = pre * sigmoid(pre)
        ext[0:8, :] = ext[n : n + 8, :]
        mini = small[where, :]
        exts[8 : 8 + n, :] = mini[:, : 2 * STATE]
        pres = conv_pre(exts, sp_ref, n)
        bc = (pres * sigmoid(pres)).astype(BF16)
        exts[0:8, :] = exts[n : n + 8, :]
        key, query = bc[:, :STATE], bc[:, STATE:]

        _, step, rate, cs, wide_step, wide_cs, wide_tail = scan_prep(mini, hp_ref, ind, n)
        cs2 = cs * LOG2E
        cs2t = cs2.T
        xs = x * wide_step
        lane = lax.broadcasted_iota(jnp.int32, (1, width), 1)
        half = jnp.where(lax.rem(lane, 2 * HEAD) < HEAD, 1.0, 0.0).astype(BF16)
        xsb = xs.astype(BF16)
        xs0 = xsb * half
        xs1 = xsb - xs0
        before = state[...]
        low = before.astype(BF16)
        st_ref[0] = low
        carried = mm(query, low) * wide_cs
        xw = (xs * wide_tail).astype(BF16)
        state[...] = before * wide_cs[n - 1 : n, :] + mm(key, xw, TN)
        scores = jnp.where(rows >= cols, mm(query, key, NT), 0.0)
        for pair in range(heads // 2):
            lanes = slice(pair * 2 * HEAD, (pair + 1) * 2 * HEAD)
            mats = []
            for h in (2 * pair, 2 * pair + 1):
                dec = jnp.exp2(jnp.minimum(cs2[:, h : h + 1] - cs2t[h : h + 1, :], 0.0))
                mats.append((scores * dec).astype(BF16))
            local = mm(
                jnp.concatenate(mats, axis=1),
                jnp.concatenate([xs0[:, lanes], xs1[:, lanes]], axis=0),
            )
            ssd_ref[:, lanes] = local + carried[:, lanes] + cp_ref[6:7, lanes] * x[:, lanes]
        gates = gate[where, :]
        gated = ssd_ref[...] * (gates * sigmoid(gates))
        sqs_ref[0] = rowsum(gated * gated)
        scaled_ref[...] = (gated * cp_ref[5:6, :]).astype(BF16)

        span = model // LANES
        share = -(-2 * span // steps)
        for k in range(share):
            b = at * share + k

            @pl.when(b < 2 * span)
            def _(b=b):
                j, col = b // span, lax.rem(b, span)
                slab_rows = slabs.shape[2]
                weight = slabs.at[j]
                piece = block_of(weight, col, slab_rows)
                wt[pl.ds(pl.multiple_of(j * width, width), width), pl.ds(pl.multiple_of(col * LANES, LANES), LANES)] = piece.T

    @pl.when(i == steps)
    def _():
        flush(4).start()
        job.arrive(2)
        flush(5).start()
        for j in range(3):
            job.drain(j)
        for k in range(len(outgoing)):
            flush(k).wait()


def forward(res, stateproj, steps_w, inproj, outt, gain, params, heads, size, layer, out=None):
    tokens_n, model = res.shape
    _, _, rows, width = inproj.shape
    top = 2 * width + 2 * STATE + LANES
    steps = tokens_n // CHUNK
    mid = out is not None
    hbm = pl.BlockSpec(memory_space=pl.ANY)
    chunks = model // SLICE

    def whole(a):
        return pl.BlockSpec(a.shape, lambda i: (0,) * len(a.shape))

    def row(w):
        return pl.BlockSpec((CHUNK, w), lambda i: (jnp.maximum(i - 1, 0), 0))

    args, in_specs, out_specs, out_shape, scratch = [res], [hbm], [], [], []
    if mid:
        args += list(out)
        in_specs += [hbm, hbm, whole(out[2])]
        out_specs += [hbm, whole(out[2])]
        out_shape += [jax.ShapeDtypeStruct(res.shape, F32), jax.ShapeDtypeStruct(out[2].shape, F32)]
        chunk = pltpu.VMEM((chunks, tokens_n // 2, SLICE), BF16)
        scratch += [
            pltpu.VMEM(out[0].shape, BF16),
            pltpu.VMEM(out[1].shape, BF16),
            pltpu.VMEM((2 * chunks, tokens_n // 2, SLICE), BF16),
            chunk, chunk, chunk,
            pltpu.VMEM((4,) + out[2].shape, F32),
            pltpu.VMEM((tokens_n, LANES), F32),
            pltpu.VMEM(res.shape, F32),
            pltpu.SemaphoreType.DMA((3, chunks)),
            pltpu.SemaphoreType.DMA((3, chunks)),
            pltpu.SemaphoreType.DMA((3,)),
            pltpu.SemaphoreType.DMA((3,)),
        ]
    args += [stateproj, steps_w, inproj, outt, gain, *params]
    in_specs += [hbm, hbm, hbm, hbm, whole(gain)] + [whole(v) for v in params]
    out_specs += [
        hbm, pl.BlockSpec((tokens_n, 1), lambda i: (0, 0)), hbm, hbm, hbm, hbm, hbm,
        row(width), row(width),
        pl.BlockSpec((1, 1, CHUNK), lambda i: (jnp.maximum(i - 1, 0), 0, 0)),
        pl.BlockSpec((1, STATE, width), lambda i: (jnp.maximum(i - 1, 0), 0, 0)),
    ]
    out_shape += [
        jax.ShapeDtypeStruct((model, tokens_n), BF16),
        jax.ShapeDtypeStruct((tokens_n, 1), F32),
        jax.ShapeDtypeStruct((tokens_n, 2 * STATE + LANES), F32),
        jax.ShapeDtypeStruct((tokens_n, width), F32),
        jax.ShapeDtypeStruct((tokens_n, width), F32),
        jax.ShapeDtypeStruct((top, model), BF16),
        jax.ShapeDtypeStruct((size, rows, width), BF16),
        jax.ShapeDtypeStruct((tokens_n, width), F32),
        jax.ShapeDtypeStruct((tokens_n, width), BF16),
        jax.ShapeDtypeStruct((steps, 1, CHUNK), F32),
        jax.ShapeDtypeStruct((steps, STATE, width), BF16),
    ]
    scratch += [
        pltpu.VMEM(res.shape, res.dtype),
        pltpu.VMEM((model, 2 * STATE), BF16),
        pltpu.VMEM((top, model), BF16),
        pltpu.VMEM((3, size, rows, width), BF16),
        pltpu.VMEM((tokens_n, model), BF16),
        pltpu.VMEM((model, tokens_n), BF16),
        pltpu.VMEM((tokens_n, 2 * STATE + LANES), F32),
        pltpu.VMEM((tokens_n, width), F32),
        pltpu.VMEM((tokens_n, width), F32),
        pltpu.VMEM((CHUNK + 8, width), F32),
        pltpu.VMEM((CHUNK + 8, 2 * STATE), F32),
        pltpu.VMEM((STATE, width), F32),
        pltpu.VMEM((8, width), F32),
        pltpu.VMEM((8, 2 * STATE), F32),
        pltpu.VMEM((8, LANES), F32),
        pltpu.VMEM((LANES, width), BF16),
        pltpu.SemaphoreType.DMA((3,)),
        pltpu.SemaphoreType.DMA((3, 3, size)),
        pltpu.SemaphoreType.DMA((3, size)),
        pltpu.SemaphoreType.DMA((5,)),
        pltpu.SemaphoreType.DMA((7,)),
    ]
    return pl.pallas_call(
        functools.partial(forward_body, size=size, heads=heads, per=LEN // CHUNK, steps=steps, layer=layer),
        grid=(steps + 1,),
        in_specs=in_specs,
        out_specs=out_specs,
        out_shape=out_shape,
        scratch_shapes=scratch,
        compiler_params=pltpu.CompilerParams(
            collective_id=min(layer, 1), has_side_effects=True, vmem_limit_bytes=VMEM_LIMIT
        ),
        name="forward",
    )(*args)


def back_body(*refs, heads, per, size, steps, layer, last):
    refs = list(refs)

    def take(n):
        got = refs[:n]
        del refs[:n]
        return got

    up_ref, sq_ref, gate_ref, ssd_ref, inner_ref, iprev_ref, small_ref, sprev_ref, st_ref, res_ref, rn_ref = take(11)
    gain_ref = take(1)[0]
    params = take(6)
    wout_hbm, scaled_hbm, wt_hbm, normed_hbm = take(4)
    if not last:
        next_normed, next_steps, next_sdel, next_dcp, next_dsp, next_dhp, next_dgain = take(7)
    new_ref, grad_hbm = take(2)
    if last:
        sdsum_ref, steplow_ref, dcp_ref, dsp_ref, dhp_ref, dgain_ref, mixed_ref = take(7)
    else:
        full_hbm, wide_hbm = take(2)
    ext, exts, cde, cdes, dstate, rq, cp_ref, sp_ref, hp_ref, ind_ref = take(10)
    wout, scaled, wt, turned, dy, glow, ilow, frow, srow, sgot = take(10)
    part, near, away, tpart, got, far, other = take(7)
    load, rsend, rrecv, ssend, srecv, sends, recvs, gsem = take(8)
    if last:
        fgot, opart, ogot, ofar, oother, fsend, frecv, osends, orecvs = take(9)
    else:
        dcp_ref, dsp_ref, dhp_ref, dgain_ref, step_all, sd_all = take(6)
        buffers = take(6)
        sems = take(7)
    assert not refs

    n = CHUNK
    model = up_ref.shape[1]
    i = pl.program_id(0)
    begin_gate = steps
    begin_scan = begin_gate + steps
    begin_norm = begin_scan + steps
    end = begin_norm + steps - 1
    line = Line(size)
    square = Square()
    rows_own = part.shape[2]
    count = part.shape[0]
    job = Scatter(line, part, lambda j: dy.at[pl.ds(j * rows_own, rows_own), :], near, away, ssend, srecv)
    sums = Total(square, tpart, got, far, other, sends, recvs)
    if last:
        outs = Total(square, opart, ogot, ofar, oother, osends, orecvs)
        half = steps * n // 2
        slices = model // SLICE
    else:
        minis = Smalls(line, square, *buffers, sems)
    moves = [(wout_hbm, wout), (scaled_hbm, scaled), (wt_hbm, wt), (normed_hbm, turned)]
    if not last:
        tokens_n = steps * n
        spots = (wt.at[pl.ds(0, model), pl.ds(0, tokens_n)],)
        spots += tuple(
            wt.at[pl.ds(0, tokens_n), pl.ds(tokens_n + at, w)] for at, w in ((0, LANES), (LANES, 2 * STATE))
        )
        moves += [(next_normed, spots[0]), (next_steps, spots[1]), (next_sdel, spots[2])]

    def move(k):
        return pltpu.make_async_copy(*moves[k], load.at[k])

    places = line.n

    def spaced(begin, stop, m):
        return begin + m * (stop - begin) // places

    middle = begin_scan + steps // 2
    folds = [(spaced(begin_scan, middle, m), 0, m) for m in range(places)]
    folds += [(spaced(middle, begin_norm, m) + 1, 1, m) for m in range(places)]

    def column(row):
        return jnp.broadcast_to(row, (n, n)).T[:, 0:1]

    @pl.when(i == 0)
    def _():
        for k in range(3):
            move(k).start()
        put_params(cp_ref, sp_ref, hp_ref, ind_ref, layer, params)
        rq[...] = jnp.zeros_like(rq)
        line.greet_all(pltpu.get_barrier_semaphore(), square.others())
        if last:
            rows = [
                remote(sq_ref, fgot.at[square.me], fsend.at[k], frecv.at[k], who)
                for k, who in enumerate(square.others())
            ]
            for copy in rows:
                copy.start()
            fgot[square.me] = sq_ref[...]
            move(0).wait()
            move(1).wait()
            for c in range(slices):
                value = mm(scaled[...], wout[c * SLICE : (c + 1) * SLICE, :], NT).astype(BF16)
                opart[2 * c] = value[:half]
                opart[2 * c + 1] = value[half:]
                outs.step(0, c)
            outs.step(1, 0)
            for copy in rows:
                copy.wait()
            total = (fgot[0] + fgot[1]) + (fgot[2] + fgot[3])
        else:
            total = sq_ref[...]
            move(0).wait()
            move(1).wait()
        dcp_ref[...] = jnp.zeros_like(dcp_ref)
        dsp_ref[...] = jnp.zeros_like(dsp_ref)
        dhp_ref[...] = jnp.zeros_like(dhp_ref)
        dgain_ref[...] = jnp.zeros_like(dgain_ref)
        frow[...] = lax.rsqrt(total / INNER + EPS)

    ind = ind_ref[...]
    for at, j, m in folds:
        @pl.when(i == at)
        def _(j=j, m=m):
            job.fold(j, m)

    @pl.when(i < begin_gate)
    def _():
        rows = pl.ds(pl.multiple_of(i * n, n), n)
        low = (column(frow[i]) * up_ref[...].astype(F32)).astype(BF16)
        turned[:, rows] = low.T
        sd = mm(low, wout[...])
        dy[rows, :] = sd
        piece = scaled[rows, :]
        srow[i] = rowsum(piece.astype(F32) * sd)

    @pl.when(i == begin_gate - 1)
    def _():
        copies = [
            remote(srow, sgot.at[square.me], rsend.at[k], rrecv.at[k], who) for k, who in enumerate(square.others())
        ]
        for copy in copies:
            copy.start()
        job.emit(0, turned, scaled)
        move(3).start()
        sgot[square.me] = srow[...]
        for copy in copies:
            copy.wait()
        srow[...] = (sgot[0] + sgot[1]) + (sgot[2] + sgot[3])

    if last:
        @pl.when(i == steps // 2)
        def _():
            outs.step(1, 1)

        @pl.when((i >= begin_gate) & (i < begin_gate + slices - 2))
        def _():
            outs.step(1, i - begin_gate + 2)

    @pl.when((i >= begin_gate) & (i < begin_scan))
    def _():
        c = i - begin_gate
        rows = pl.ds(pl.multiple_of(c * n, n), n)
        coef = column(frow[c] * frow[c] * srow[c]) / INNER
        gate = gate_ref[...]
        gsig = sigmoid(gate)
        gact = gate * gsig
        ssd = ssd_ref[...]
        sd = dy[rows, :]
        gated = ssd * gact
        gd = cp_ref[5:6, :] * sd - coef * gated
        dcp_ref[5:6, :] += colsum(gated * sd)
        dy[rows, :] = gd * gact
        glow[rows, :] = (gd * ssd * (gsig + gact * (1.0 - gsig))).astype(BF16)

    @pl.when(i == begin_scan - 1)
    def _():
        move(3).wait()
        job.emit(1, turned, glow)
        move(2).wait()

    @pl.when((i >= begin_scan) & (i < begin_norm))
    def _():
        q = i - begin_scan
        chunk = steps - 1 - q
        where = pl.ds(pl.multiple_of(chunk * n, n), n)

        @pl.when(lax.rem(chunk, per) == per - 1)
        def _():
            cde[n : n + 8, :] = jnp.zeros((8, cde.shape[1]), F32)
            cdes[n : n + 8, :] = jnp.zeros((8, cdes.shape[1]), F32)
            dstate[...] = jnp.zeros_like(dstate)

        keep = jnp.where(lax.rem(chunk, per) == 0, 0.0, 1.0).astype(F32)
        rows, cols = iotas(n)
        ext[0:8, :] = iprev_ref[...] * keep
        ext[8 : 8 + n, :] = inner_ref[...]
        exts[0:8, :] = sprev_ref[:, : 2 * STATE] * keep
        exts[8 : 8 + n, :] = small_ref[:, : 2 * STATE]
        pre = conv_pre(ext, cp_ref, n)
        sig = sigmoid(pre)
        x = pre * sig
        slope = sig + x * (1.0 - sig)
        pres = conv_pre(exts, sp_ref, n)
        sigs = sigmoid(pres)
        acts = pres * sigs
        slopes = sigs + acts * (1.0 - sigs)
        bc = acts.astype(BF16)
        key, query = bc[:, :STATE], bc[:, STATE:]
        dyc = dy[where, :]

        raw, step, rate, cs, wide_step, wide_cs, wide_tail = scan_prep(small_ref, hp_ref, ind, n)
        cs2 = cs * LOG2E
        cs2t = cs2.T
        xs = x * wide_step
        xsb = xs.astype(BF16)
        dyb = dyc.astype(BF16)
        lane = lax.broadcasted_iota(jnp.int32, (1, xs.shape[1]), 1)
        half = jnp.where(lax.rem(lane, 2 * HEAD) < HEAD, 1.0, 0.0).astype(BF16)
        dy0 = dyb * half
        dy1 = dyb - dy0
        low = st_ref[0]
        dst = dstate[...]
        dlow = dst.astype(BF16)
        dye = dyc * wide_cs
        dyeb = dye.astype(BF16)
        up = headsum(dye * mm(query, low), ind)
        dxs_state = wide_tail * mm(key, dlow)
        down = headsum(xs * dxs_state, ind)
        qdel = mm(dyeb, low, NT)
        kdel = mm((xs * wide_tail).astype(BF16), dlow, NT)
        through = headsum(jnp.broadcast_to(colsum(low.astype(F32) * dst), (8, dst.shape[1])), ind)[0:1, :]
        through = through * jnp.exp(cs[n - 1 : n, :])
        dstate[...] = dst * wide_cs[n - 1 : n, :] + mm(query, dyeb, TN)

        scores = jnp.where(rows <= cols, mm(key, query, NT), 0.0)
        dscores = jnp.zeros((n, n), F32)
        colq = jnp.zeros((n, LANES), F32)
        lane = lax.broadcasted_iota(jnp.int32, (n, LANES), 1)
        dxs = []
        for pair in range(heads // 2):
            lanes = slice(pair * 2 * HEAD, (pair + 1) * 2 * HEAD)
            stacked = jnp.concatenate([dy0[:, lanes], dy1[:, lanes]], axis=0)
            both = mm(xsb[:, lanes], stacked, NT)
            mats = []
            for which, h in enumerate((2 * pair, 2 * pair + 1)):
                dec = jnp.exp2(jnp.minimum(cs2t[h : h + 1, :] - cs2[:, h : h + 1], 0.0))
                mats.append((scores * dec).astype(BF16))
                term = dec * both[:, which * n : (which + 1) * n]
                dscores = dscores + term
                quad = scores * term
                rq[h : h + 1, :] = colsum(quad)
                colq = jnp.where(lane == h, jnp.sum(quad, axis=1, keepdims=True), colq)
            dxs.append(mm(jnp.concatenate(mats, axis=1), stacked))
        dxs = jnp.concatenate(dxs, axis=1) + dxs_state
        dscores = jnp.where(rows <= cols, dscores, 0.0).astype(BF16)
        kdel = kdel + mm(dscores, query)
        qdel = qdel + mm(dscores, key, TN)

        upper = jnp.where(rows <= cols, 1.0, 0.0).astype(F32)
        strict = jnp.where(rows > cols, 1.0, 0.0).astype(F32)
        da = mm(upper, rq[...].T - colq + up, precision=HIGH) + mm(strict, down, precision=HIGH) + through
        grown = headsum(x * dxs, ind) + rate * da
        step_pre = grown * sigmoid(raw)
        steplow = step_pre.astype(BF16)
        if last:
            steplow_ref[...] = steplow
        else:
            step_all[where, :] = steplow
        dhp_ref[0:1, :] += colsum(step_pre)
        dhp_ref[1:2, :] += rate * colsum(step * da)
        dcp_ref[6:7, :] += colsum(dyc * x)

        cd = (dxs * wide_step + cp_ref[6:7, :] * dyc) * slope
        cde[0:n, :] = cd
        center = ext[8 : 8 + n, :]
        total = cp_ref[3:4, :] * cd
        dcp_ref[3:4, :] += colsum(cd * center)
        for tap in range(3):
            shifted = cde[3 - tap : 3 - tap + n, :]
            total = total + cp_ref[tap : tap + 1, :] * shifted
            dcp_ref[tap : tap + 1, :] += colsum(shifted * center)
        inner_low = total.astype(BF16)
        ilow[where, :] = inner_low
        dcp_ref[4:5, :] += colsum(cd)
        cde[n : n + 8, :] = cde[0:8, :]

        cds = jnp.concatenate([kdel, qdel], axis=1) * slopes
        cdes[0:n, :] = cds
        center = exts[8 : 8 + n, :]
        total = sp_ref[3:4, :] * cds
        dsp_ref[3:4, :] += colsum(cds * center)
        for tap in range(3):
            shifted = cdes[3 - tap : 3 - tap + n, :]
            total = total + sp_ref[tap : tap + 1, :] * shifted
            dsp_ref[tap : tap + 1, :] += colsum(shifted * center)
        sdel = total.astype(BF16)
        dsp_ref[4:5, :] += colsum(cds)
        cdes[n : n + 8, :] = cdes[0:8, :]

        lows = jnp.concatenate([inner_low, glow[where, :], sdel, steplow], axis=1)
        value = mm(lows, wt[...]).astype(BF16)
        tpart[2 * q, :, :model] = value[: n // 2]
        tpart[2 * q + 1, :, :model] = value[n // 2 :]
        tpart[2 * q, :, model:] = sdel[: n // 2]
        tpart[2 * q + 1, :, model:] = sdel[n // 2 :]
        sums.step(0, q)

    @pl.when((i > begin_scan) & (i <= begin_norm))
    def _():
        sums.step(1, i - begin_scan - 1)

    @pl.when((i >= begin_scan + 5) & (i < begin_norm + 5))
    def _():
        sums.step(2, i - begin_scan - 5)

    @pl.when((i >= begin_scan + 6) & (i < begin_norm + 6))
    def _():
        sums.step(3, i - begin_scan - 6)

    if last:
        @pl.when((i > begin_scan) & (i <= begin_scan + slices))
        def _():
            outs.step(2, i - begin_scan - 1)

        @pl.when((i > begin_scan + 1) & (i <= begin_scan + slices + 1))
        def _():
            outs.step(3, i - begin_scan - 2)

    @pl.when(i == begin_norm - 1)
    def _():
        dhp_ref[2:3, :] = headsum(jnp.broadcast_to(dcp_ref[6:7, :], (8, dcp_ref.shape[1])), ind)[0:1, :]
        job.emit(2, turned, ilow, None if last else places // 2)
        if not last:
            for k in (4, 5, 6):
                move(k).start()

    if not last:
        @pl.when(i == begin_norm + 1)
        def _():
            for k in (4, 5, 6):
                move(k).wait()
            put_pack(
                buffers[0].at[1], square.me, *spots, next_dcp[...], next_dsp[...], next_dhp[...], next_dgain[...]
            )
            minis.sum.start(1)

    @pl.when(i >= begin_norm)
    def _():
        r = i - begin_norm
        chunk = steps - 1 - r
        if last:
            fac = column(frow[chunk])
            side = chunk // (steps // 2)
            base = (chunk - side * (steps // 2)) * n
        for h in range(2):
            rows = slice(h * (n // 2), (h + 1) * (n // 2))
            back = tpart[2 * r + h, :, :model].astype(F32)
            sdel = tpart[2 * r + h, :, model:]
            if last:
                sdsum_ref[rows, :] = sdel
            else:
                sd_all[pl.ds(pl.multiple_of(chunk * n + h * (n // 2), n // 2), n // 2), :] = sdel
            res = res_ref[rows, :].astype(F32)
            rn = rn_ref[rows, :]
            dgain_ref[...] += colsum(back * res * rn)
            gained = back * gain_ref[layer : layer + 1, :]
            mean = jnp.sum(gained * res, axis=1, keepdims=True) / model
            new_ref[rows, :] = up_ref[rows, :].astype(F32) + rn * gained - (rn * rn * rn * mean) * res
            if last:
                where = pl.ds(pl.multiple_of(base + h * (n // 2), n // 2), n // 2)
                for c in range(slices):
                    span = slice(c * SLICE, (c + 1) * SLICE)
                    summed = opart[2 * c + side, where, :].astype(F32)
                    mixed_ref[rows, span] = (res[:, span] + fac[rows, :] * summed).astype(BF16)

    @pl.when(i == end)
    def _():
        def finish(j):
            job.finish(j)
            pltpu.make_async_copy(dy.at[pl.ds(j * rows_own, rows_own), :], grad_hbm.at[j], gsem.at[j]).start()

        early = places if last else places // 2
        if not last:
            put_pack(
                buffers[0].at[0], square.me, turned, step_all, sd_all, dcp_ref[...], dsp_ref[...], dhp_ref[...], dgain_ref[...]
            )
            minis.sum.start(0)
            for m in range(places // 2, places):
                job.lead(2, m)
        for m in range(early):
            job.fold(2, m)
        finish(0)
        finish(1)
        if not last:
            minis.fold()
            minis.turn()
            for k in range(1, line.n):
                minis.relay(k)
            for m in range(places // 2, places):
                job.fold(2, m)
            minis.cross()
        finish(2)
        if not last:
            minis.cross_on()
            minis.end()
            tails = [
                pltpu.make_async_copy(src, dst, load.at[k])
                for k, (src, dst) in enumerate(((minis.full, full_hbm), (minis.wide, wide_hbm)))
            ]
            for copy in tails:
                copy.start()
        for j in range(count):
            job.drain(j)
            pltpu.make_async_copy(dy.at[pl.ds(j * rows_own, rows_own), :], grad_hbm.at[j], gsem.at[j]).wait()
        if not last:
            for copy in tails:
                copy.wait()


def back(up, sq, gate_pre, ssd, inner_raw, small, states, res, rnorm, gain, params,
         wout, scaled, wt, normed, heads, size, layer, after=None):
    tokens_n, width = inner_raw.shape
    model = up.shape[1]
    last = after is None
    steps = tokens_n // CHUNK
    begin_scan = 2 * steps
    begin_norm = begin_scan + steps
    rows = model // size
    n = size // 2
    hbm = pl.BlockSpec(memory_space=pl.ANY)
    top = steps - 1

    def norm_at(i):
        return jnp.where(i < begin_norm, top, top - (i - begin_norm))

    def scan_at(i):
        return jnp.clip(top - (i - begin_scan), 0, top)

    def first(w):
        return pl.BlockSpec((CHUNK, w), lambda i: (jnp.where(i < steps, i, norm_at(i)), 0))

    def second(w):
        return pl.BlockSpec((CHUNK, w), lambda i: (jnp.clip(i - steps, 0, top), 0))

    def scan(w):
        return pl.BlockSpec((CHUNK, w), lambda i: (scan_at(i), 0))

    def prev(w):
        return pl.BlockSpec((8, w), lambda i: (jnp.maximum(scan_at(i) * (CHUNK // 8) - 1, 0), 0))

    def norm(w):
        return pl.BlockSpec((CHUNK, w), lambda i: (norm_at(i), 0))

    def whole(a):
        return pl.BlockSpec(a.shape, lambda i: (0,) * len(a.shape))

    extra = model + 2 * STATE
    quarter = pltpu.VMEM((steps, CHUNK // 2, extra), BF16)
    pieces = pltpu.VMEM((3, n, rows, width), BF16)
    args = [up, sq, gate_pre, ssd, inner_raw, inner_raw, small, small, states, res, rnorm, gain, *params,
            wout, scaled, wt, normed]
    in_specs = [
        first(model), whole(sq), second(width), second(width),
        scan(width), prev(width), scan(small.shape[1]), prev(small.shape[1]),
        pl.BlockSpec((1, STATE, width), lambda i: (scan_at(i), 0, 0)),
        norm(model), norm(1), whole(gain),
    ] + [whole(a) for a in params] + [hbm] * 4
    out_specs = [norm(model), hbm]
    out_shape = [jax.ShapeDtypeStruct((tokens_n, model), F32), jax.ShapeDtypeStruct((3, rows, width), F32)]
    totals = [(8, width), (8, 2 * STATE), (8, LANES), (1, model)]
    scratch = [
        pltpu.VMEM((CHUNK + 8, width), F32),
        pltpu.VMEM((CHUNK + 8, 2 * STATE), F32),
        pltpu.VMEM((CHUNK + 8, width), F32),
        pltpu.VMEM((CHUNK + 8, 2 * STATE), F32),
        pltpu.VMEM((STATE, width), F32),
        pltpu.VMEM((LANES, CHUNK), F32),
        pltpu.VMEM((8, width), F32),
        pltpu.VMEM((8, 2 * STATE), F32),
        pltpu.VMEM((8, LANES), F32),
        pltpu.VMEM((LANES, width), BF16),
        pltpu.VMEM(wout.shape, BF16),
        pltpu.VMEM(scaled.shape, BF16),
        pltpu.VMEM(wt.shape, BF16),
        pltpu.VMEM(normed.shape, BF16),
        pltpu.VMEM((tokens_n, width), F32),
        pltpu.VMEM((tokens_n, width), BF16),
        pltpu.VMEM((tokens_n, width), BF16),
        pltpu.VMEM((steps, 1, CHUNK), F32),
        pltpu.VMEM((steps, 1, CHUNK), F32),
        pltpu.VMEM((4, steps, 1, CHUNK), F32),
        pltpu.VMEM((3, size, rows, width), BF16), pieces, pieces,
        pltpu.VMEM((2 * steps, CHUNK // 2, extra), BF16), quarter, quarter, quarter,
        pltpu.SemaphoreType.DMA((7,)),
        pltpu.SemaphoreType.DMA((3,)),
        pltpu.SemaphoreType.DMA((3,)),
        pltpu.SemaphoreType.DMA((2, 3, n)),
        pltpu.SemaphoreType.DMA((2, 3, n)),
        pltpu.SemaphoreType.DMA((3, steps)),
        pltpu.SemaphoreType.DMA((3, steps)),
        pltpu.SemaphoreType.DMA((3,)),
    ]
    if last:
        out_specs += [norm(2 * STATE), scan(LANES)]
        out_specs += [pl.BlockSpec(v, lambda i: (0, 0)) for v in totals] + [norm(model)]
        out_shape += [
            jax.ShapeDtypeStruct((tokens_n, 2 * STATE), BF16),
            jax.ShapeDtypeStruct((tokens_n, LANES), BF16),
        ]
        out_shape += [jax.ShapeDtypeStruct(v, F32) for v in totals]
        out_shape.append(jax.ShapeDtypeStruct((tokens_n, model), BF16))
        slices = model // SLICE
        chunk = pltpu.VMEM((slices, tokens_n // 2, SLICE), BF16)
        scratch += [
            pltpu.VMEM((4, steps, 1, CHUNK), F32),
            pltpu.VMEM((2 * slices, tokens_n // 2, SLICE), BF16), chunk, chunk, chunk,
            pltpu.SemaphoreType.DMA((3,)),
            pltpu.SemaphoreType.DMA((3,)),
            pltpu.SemaphoreType.DMA((3, slices)),
            pltpu.SemaphoreType.DMA((3, slices)),
        ]
    else:
        w = 2 * STATE
        r = pack_rows(size)
        args += list(after)
        in_specs += [hbm] * 3 + [whole(v) for v in after[3:]]
        out_specs += [hbm, hbm]
        out_shape += [
            jax.ShapeDtypeStruct((2, size, r, w), BF16),
            jax.ShapeDtypeStruct((4, 2, SPAN, w), BF16),
        ]
        scratch += [pltpu.VMEM(v, F32) for v in totals]
        scratch += [pltpu.VMEM((tokens_n, LANES), BF16), pltpu.VMEM((tokens_n, w), BF16)]
        scratch += smalls_scratch(size, w, 2)
    return pl.pallas_call(
        functools.partial(
            back_body, heads=heads, per=LEN // CHUNK, size=size, steps=steps, layer=layer, last=last
        ),
        grid=(begin_norm + steps,),
        in_specs=in_specs,
        out_specs=out_specs,
        out_shape=out_shape,
        scratch_shapes=scratch,
        compiler_params=pltpu.CompilerParams(
            collective_id=2 if last else 3, has_side_effects=True, vmem_limit_bytes=VMEM_LIMIT
        ),
        name="back",
    )(*args)


def unpack_body(full_ref, wide_ref, *refs, layers, heads):
    step_ref, state_ref, conv_ref, bias_ref, convs_ref, biass_ref = refs[:6]
    stepbias_ref, decay_ref, skip_ref, norm_ref, gain_ref = refs[6:]
    model = state_ref.shape[1]
    quarter = model // 4
    w = state_ref.shape[2]
    width = conv_ref.shape[2]
    for layer in range(layers):
        for t in range(4):
            state_ref[layer, t * quarter : (t + 1) * quarter, :] = wide_ref[t, layer, :quarter, :].astype(F32)
        taps = [wide_ref[t, layer, quarter : quarter + 16, :].astype(F32) for t in range(4)]
        taps = (taps[0] + taps[1]) + (taps[2] + taps[3])
        convs_ref[layer] = taps[0:4]
        biass_ref[layer : layer + 1, :] = taps[4:5]
        flat = full_ref[layer].reshape(-1, w)[:PACK].astype(F32)
        at = quarter + 16
        for b in range(model // w):
            step_ref[layer, :, b * w : (b + 1) * w] = flat[at : at + 16]
            at += 16
        for b in range(width // w):
            lanes = slice(b * w, (b + 1) * w)
            rows = flat[at + 8 * b : at + 8 * b + 8]
            conv_ref[layer, :, lanes] = rows[0:4]
            bias_ref[layer : layer + 1, lanes] = rows[4:5]
            norm_ref[layer : layer + 1, lanes] = rows[5:6]
        at += 8 * (width // w)
        for k, ref in enumerate((stepbias_ref, decay_ref, skip_ref)):
            ref[layer : layer + 1, :] = flat[at + k : at + k + 1, :heads]
        at += 8
        for b in range(model // w):
            gain_ref[layer : layer + 1, b * w : (b + 1) * w] = flat[at + b : at + b + 1]


def unpack(full, wide, model, width, heads):
    layers, w = full.shape[0], full.shape[3]
    vm = pl.BlockSpec(memory_space=pltpu.VMEM)
    shapes = [
        (layers, 16, model), (layers, model, w), (layers, 4, width), (layers, width), (layers, 4, w), (layers, w),
        (layers, heads), (layers, heads), (layers, heads), (layers, width), (layers, model),
    ]
    return pl.pallas_call(
        functools.partial(unpack_body, layers=layers, heads=heads),
        in_specs=[vm, vm],
        out_specs=[vm] * len(shapes),
        out_shape=[jax.ShapeDtypeStruct(v, F32) for v in shapes],
        compiler_params=pltpu.CompilerParams(vmem_limit_bytes=VMEM_LIMIT),
        name="unpack",
    )(full, wide)


def shards(
    tokens, inproj, stepproj, stateproj, outproj, convinner, biasinner, convstate, biasstate,
    stepbias, decaylog, skipgain, normgain, inputgain, cotangent,
):
    layers = inproj.shape[0]
    width = inproj.shape[3]
    heads = stepproj.shape[2]
    model = tokens.shape[1]
    pad = LANES - heads
    size = lax.axis_size("dp")
    steps_w = jnp.pad(jnp.swapaxes(stepproj, 1, 2), ((0, 0), (0, pad), (0, 0)))
    head = jnp.pad(jnp.stack([stepbias, decaylog, skipgain], axis=1), ((0, 0), (0, 5), (0, pad)))
    outt = jnp.swapaxes(outproj, 1, 2)
    params = (convinner, biasinner, normgain, convstate, biasstate, head)

    residual = tokens
    kept = []
    out = None
    for at in range(layers):
        results = forward(residual, stateproj, steps_w, inproj, outt, inputgain, params, heads, size, at, out=out)
        if at:
            residual, kept[-1][-1] = results[:2]
            results = results[2:]
        normed, rnorm, small, inner_raw, gate_pre, wt, w_out, ssd, scaled, sq, states = results
        w_out = w_out.reshape(model, width)
        kept.append([residual, normed, rnorm, small, inner_raw, gate_pre, wt, w_out, ssd, scaled, states, sq])
        out = (scaled, w_out, sq)

    assert layers == 2
    before, normed, rnorm, small, inner_raw, gate_pre, wt, w_out, ssd, scaled, states, sq = kept[1]
    upstream, second, sdel, steplow, *totals, mixed = back(
        cotangent, sq, gate_pre, ssd, inner_raw, small, states, before, rnorm, inputgain, params,
        w_out, scaled, wt, normed, heads, size, 1,
    )
    after = (normed, steplow, sdel, *totals)
    before, normed, rnorm, small, inner_raw, gate_pre, wt, w_out, ssd, scaled, states, sq = kept[0]
    upstream, first, full, wide = back(
        upstream, sq, gate_pre, ssd, inner_raw, small, states, before, rnorm, inputgain, params,
        w_out, scaled, wt, normed, heads, size, 0, after=after,
    )
    pieces = [first, second]
    (
        step_grad, state_grad, conv_grad, bias_grad, convs_grad, biass_grad,
        stepbias_grad, decay_grad, skip_grad, norm_grad, gain_grad,
    ) = unpack(full, wide, model, width, heads)
    return (
        mixed,
        upstream,
        jnp.stack([v[1:] for v in pieces]),
        jnp.swapaxes(step_grad[:, :heads], 1, 2),
        state_grad,
        jnp.swapaxes(jnp.stack([v[0] for v in pieces]), 1, 2),
        conv_grad,
        bias_grad,
        convs_grad,
        biass_grad,
        stepbias_grad,
        decay_grad,
        skip_grad,
        norm_grad,
        gain_grad,
    )


def solution(mesh):
    in_specs = (
        P("dp", None),
        P(None, None, "dp", "tensor"),
        P(None, None, "tensor"),
        P(),
        P(None, "tensor", "dp"),
        P(None, None, "tensor"),
        P(None, "tensor"),
        P(),
        P(),
        P(None, "tensor"),
        P(None, "tensor"),
        P(None, "tensor"),
        P(None, "tensor"),
        P(),
        P("dp", None),
    )
    out_specs = (
        P("dp", None),
        P("dp", None),
        P(None, None, "dp", "tensor"),
        P(None, None, "tensor"),
        P(),
        P(None, "tensor", "dp"),
        P(None, None, "tensor"),
        P(None, "tensor"),
        P(),
        P(),
        P(None, "tensor"),
        P(None, "tensor"),
        P(None, "tensor"),
        P(None, "tensor"),
        P(),
    )
    return jax.shard_map(shards, mesh=mesh, in_specs=in_specs, out_specs=out_specs, check_vma=False)
```

```python
import functools
import math

import jax
import jax.numpy as jnp
from jax import lax
from jax.experimental import pallas as pl
from jax.experimental.pallas import tpu as pltpu
from jax.sharding import PartitionSpec as P

STATE = 128
LEN = 1024
INNER = 3072
HEAD = 64
CHUNK = 128
SLICE = 256
TILE = 256
PACK = 544
SPAN = 400
VMEM_LIMIT = 65000 * 1024
LANES = 128
EPS = 1e-05
LOG2E = 1.4426950408889634

HIGH = lax.Precision.HIGHEST
NN = (((1,), (0,)), ((), ()))
NT = (((1,), (1,)), ((), ()))
TN = (((0,), (0,)), ((), ()))
F32 = jnp.float32
BF16 = jnp.bfloat16
MESH = pl.DeviceIdType.MESH


def remote(src, dst, send, recv, where):
    return pltpu.make_async_remote_copy(
        src_ref=src, dst_ref=dst, send_sem=send, recv_sem=recv, device_id=where, device_id_type=MESH
    )


class Line:
    def __init__(self, size):
        self.n = size // 2
        me = lax.axis_index("dp")
        self.me = me
        self.at = me // 2
        self.side = lax.rem(me, 2)
        self.pair = {"dp": me + 1 - 2 * self.side}
        self.right = {"dp": jnp.minimum(me + 2, size - 1)}
        self.left = {"dp": jnp.maximum(me - 2, 0)}
        odd = lax.rem(self.at, 2)
        self.odd = odd == 1
        self.near = {"dp": me + 2 - 4 * odd}
        self.has_left = self.at > 0
        self.has_right = self.at < self.n - 1

    def greet(self, barrier, more=()):
        for who in more:
            pl.semaphore_signal(barrier, inc=1, device_id=who, device_id_type=MESH)
        pl.semaphore_signal(barrier, inc=1, device_id=self.pair, device_id_type=MESH)

        @pl.when(self.has_left)
        def _():
            pl.semaphore_signal(barrier, inc=1, device_id=self.left, device_id_type=MESH)

        @pl.when(self.has_right)
        def _():
            pl.semaphore_signal(barrier, inc=1, device_id=self.right, device_id_type=MESH)

        peers = 1 + len(more) + self.has_left.astype(jnp.int32) + self.has_right.astype(jnp.int32)
        pl.semaphore_wait(barrier, peers)

    def greet_all(self, barrier, more=()):
        for who in list(more) + [self.pair]:
            pl.semaphore_signal(barrier, inc=1, device_id=who, device_id_type=MESH)
        for i in range(self.n):
            @pl.when(i != self.at)
            def _(i=i):
                pl.semaphore_signal(barrier, inc=1, device_id={"dp": 2 * i + self.side}, device_id_type=MESH)
        pl.semaphore_wait(barrier, self.n + len(more))


def upper(rows):
    return max(16, rows // 32 * 16)


class Gather:
    def __init__(self, line, own, full, keep, send, recv):
        self.line, self.own, self.full, self.keep, self.send, self.recv = line, own, full, keep, send, recv
        self.rows = full.shape[2]
        self.cut = upper(self.rows)

    def copy(self, j, slab, way, src=None, rest=False):
        where = (self.line.right, self.line.left, self.line.pair)[way]
        dst = self.full.at[j, slab]
        if rest:
            dst = self.full.at[j, slab, pl.ds(self.cut, self.rows - self.cut)]
        return remote(dst if src is None else src, dst, self.send.at[j, way, slab], self.recv.at[j, slab], where)

    def shared(self, j, slab, owner):
        part = self.full.at[j, slab, pl.ds(0, self.cut)]
        return remote(part, part, self.send.at[j, 0, slab], self.recv.at[j, owner], self.line.near)

    def start(self, j):
        line = self.line
        pltpu.make_async_copy(self.own(j), self.full.at[j, line.me], self.keep.at[j]).start()

        @pl.when(line.has_right)
        def _():
            self.copy(j, line.me, 0, self.own(j)).start()

        @pl.when(line.has_left)
        def _():
            self.copy(j, line.me, 1, self.own(j)).start()

        self.copy(j, line.me, 2, self.own(j)).start()

    def relay(self, j, k):
        line = self.line

        def forward(slab, way, go_on, near):
            self.copy(j, slab, way).wait_recv()

            @pl.when(go_on)
            def _():
                self.copy(j, slab, way).start()

            if k > 1:
                self.copy(j, slab, 2).start()
            else:
                @pl.when(near)
                def _():
                    self.copy(j, slab, 2, rest=True).start()

                @pl.when(jnp.logical_not(near))
                def _():
                    self.copy(j, slab, 2).start()

        @pl.when(line.at >= k)
        def _():
            forward(line.me - 2 * k, 0, line.has_right, line.odd)

        @pl.when(line.at + k < line.n)
        def _():
            forward(line.me + 2 * k, 1, line.has_left, jnp.logical_not(line.odd))

        if k == 1:
            slab = line.me + 1 - 2 * line.side
            self.copy(j, slab, 2).wait_recv()
            self.shared(j, slab, line.near["dp"]).start()

    def near_slab(self):
        line = self.line
        return line.near["dp"] + 1 - 2 * line.side

    def arrive(self, j):
        line = self.line
        pltpu.make_async_copy(self.own(j), self.full.at[j, line.me], self.keep.at[j]).wait()
        self.copy(j, self.near_slab(), 2, rest=True).wait_recv()
        self.shared(j, self.near_slab(), line.me).wait_recv()
        for place in range(line.n):
            slab = 2 * place + 1 - line.side

            @pl.when((slab != self.near_slab()) & (place != line.at))
            def _(slab=slab):
                self.copy(j, slab, 2).wait_recv()

    def drain(self, j):
        line = self.line
        self.shared(j, line.me + 1 - 2 * line.side, line.near["dp"]).wait_send()
        for place in range(line.n):
            slab = 2 * place + line.side
            near = slab == line.near["dp"]

            @pl.when(near)
            def _(slab=slab):
                self.copy(j, slab, 2, rest=True).wait_send()

            @pl.when(jnp.logical_not(near))
            def _(slab=slab):
                self.copy(j, slab, 2).wait_send()

            @pl.when(line.has_right & (place <= line.at))
            def _(slab=slab):
                self.copy(j, slab, 0).wait_send()

            @pl.when(line.has_left & (place >= line.at))
            def _(slab=slab):
                self.copy(j, slab, 1).wait_send()


class Square:
    def __init__(self):
        me = lax.axis_index("tensor")
        self.me = me
        self.half = lax.rem(me, 2)
        self.mate = {"tensor": me + 1 - 2 * self.half}
        self.across = {"tensor": lax.rem(me + 2, 4)}

    def others(self):
        return [{"tensor": lax.rem(self.me + k, 4)} for k in (1, 2, 3)]


class Total:
    def __init__(self, square, part, got, far, other, send, recv):
        self.square, self.part, self.got, self.far, self.other = square, part, got, far, other
        self.send, self.recv = send, recv

    def first(self, c):
        sq = self.square
        return remote(
            self.part.at[2 * c + 1 - sq.half], self.got.at[c], self.send.at[0, c], self.recv.at[0, c], sq.mate
        )

    def second(self, c):
        sq = self.square
        return remote(self.part.at[2 * c + sq.half], self.far.at[c], self.send.at[1, c], self.recv.at[1, c], sq.across)

    def third(self, c):
        sq = self.square
        return remote(self.part.at[2 * c + sq.half], self.other.at[c], self.send.at[2, c], self.recv.at[2, c], sq.mate)

    def step(self, kind, c):
        slot = 2 * c + self.square.half
        if kind == 0:
            self.first(c).start()
        elif kind == 1:
            self.first(c).wait_recv()
            self.part[slot] = (self.part[slot].astype(F32) + self.got[c].astype(F32)).astype(BF16)
            self.second(c).start()
        elif kind == 2:
            self.second(c).wait()
            self.part[slot] = (self.part[slot].astype(F32) + self.far[c].astype(F32)).astype(BF16)
            self.third(c).start()
        else:
            self.third(c).wait_recv()
            self.first(c).wait_send()
            self.third(c).wait_send()
            self.part[2 * c + 1 - self.square.half] = self.other[c]


class Scatter:
    def __init__(self, line, part, out, near, far, send, recv):
        self.line, self.part, self.out, self.near, self.far = line, part, out, near, far
        self.send, self.recv = send, recv

    def order(self):
        n = self.line.n
        seq = []
        for i in range((n + 1) // 2):
            seq.append(i)
            if n - 1 - i != i:
                seq.append(n - 1 - i)
        return seq

    def cross(self, j, i):
        line = self.line
        return remote(
            self.part.at[j, 2 * i + 1 - line.side], self.near.at[j, i], self.send.at[0, j, i], self.recv.at[0, j, i], line.pair
        )

    def straight(self, j, i, source):
        line = self.line
        return remote(
            self.part.at[j, 2 * i + line.side], self.far.at[j, source], self.send.at[1, j, i], self.recv.at[1, j, source],
            {"dp": 2 * i + line.side},
        )

    def lead(self, j, m):
        self.cross(j, self.order()[m]).start()

    def start(self, j):
        for m in range(self.line.n):
            self.lead(j, m)

    def emit(self, j, turned, right, now=None):
        rows = self.part.shape[2]
        for m, i in enumerate(self.order()):
            value = mm(turned[2 * i * rows : 2 * (i + 1) * rows, :], right[...]).astype(BF16)
            self.part[j, 2 * i] = value[:rows]
            self.part[j, 2 * i + 1] = value[rows:]
            if now is None or m < now:
                self.lead(j, m)

    def product(self, dst, turned, right):
        rows = dst.shape[1]
        for i in range(self.line.n):
            value = mm(turned[2 * i * rows : 2 * (i + 1) * rows, :], right[...]).astype(BF16)
            dst[2 * i] = value[:rows]
            dst[2 * i + 1] = value[rows:]

    def fold(self, j, m):
        line = self.line
        i = self.order()[m]
        self.cross(j, i).wait_recv()
        slot = 2 * i + line.side
        self.part[j, slot] = (self.part[j, slot].astype(F32) + self.near[j, i].astype(F32)).astype(BF16)

        @pl.when(i != line.at)
        def _():
            self.straight(j, i, line.at).start()

    def finish(self, j):
        line = self.line
        out = self.out(j)
        out[...] = self.part[j, line.me].astype(out.dtype)
        for i in range(line.n):
            @pl.when(i != line.at)
            def _(i=i):
                self.straight(j, i, i).wait_recv()
                out[...] += self.far[j, i].astype(out.dtype)

    def drain(self, j):
        for i in range(self.line.n):
            self.cross(j, i).wait_send()

            @pl.when(i != self.line.at)
            def _(i=i):
                self.straight(j, i, self.line.at).wait_send()


def mm(left, right, dims=NN, precision=None):
    return lax.dot_general(left, right, dims, precision=precision, preferred_element_type=F32)


def sigmoid(v):
    return 0.5 * jnp.tanh(0.5 * v) + 0.5


def softplus(v):
    return jnp.maximum(v, 0.0) + jnp.log1p(jnp.exp(-jnp.abs(v)))


def split16(v):
    top = v.astype(BF16)
    return top, (v - top.astype(F32)).astype(BF16)


def expand(v, ind):
    top, rest = split16(v)
    return mm(top, ind) + mm(rest, ind)


def headsum(v, ind):
    return mm(v.astype(BF16), ind, NT)


def rowsum(v):
    return mm(jnp.ones((8, v.shape[1]), BF16), v.astype(BF16), NT)[0:1, :]


def iotas(n):
    return (
        lax.broadcasted_iota(jnp.int32, (n, n), 0),
        lax.broadcasted_iota(jnp.int32, (n, n), 1),
    )


def colsum(v):
    return jnp.sum(v, axis=0, keepdims=True)


def conv_pre(ext, par, n):
    total = par[4:5, :] + par[0:1, :] * ext[5 : 5 + n, :]
    for tap in range(1, 4):
        total = total + par[tap : tap + 1, :] * ext[5 + tap : 5 + tap + n, :]
    return total


def scan_prep(small, hp, ind, n):
    rows, cols = iotas(n)
    raw = small[:, 2 * STATE :] + hp[0:1, :]
    step = softplus(raw)
    rate = -jnp.exp(hp[1:2, :])
    lower = jnp.where(rows >= cols, 1.0, 0.0).astype(F32)
    cs = mm(lower, step * rate, precision=HIGH)
    tail = jnp.exp(cs[n - 1 : n, :] - cs)
    wide = mm(jnp.concatenate([step, jnp.exp(cs), tail], axis=0).astype(BF16), ind)
    return raw, step, rate, cs, wide[0:n], wide[n : 2 * n], wide[2 * n : 3 * n]


def block_of(slabs, at, rows):
    step = math.gcd(LANES, rows)
    pieces = []
    for k in range(LANES // step):
        row = at * LANES + k * step
        slab = row // rows
        pieces.append(slabs[slab, pl.ds(pl.multiple_of(row - slab * rows, step), step), :])
    return pieces[0] if len(pieces) == 1 else jnp.concatenate(pieces, axis=0)


def put_params(cp, sp, hp, ind, layer, params):
    conv, bias, norm, convs, biass, head = params
    width = cp.shape[1]
    row = lax.broadcasted_iota(jnp.int32, (LANES, width), 0)
    lane = lax.broadcasted_iota(jnp.int32, (LANES, width), 1)
    ind[...] = jnp.where(lane // HEAD == row, 1.0, 0.0).astype(BF16)
    hp[...] = head[layer]
    cp[0:4, :] = conv[layer]
    cp[4:5, :] = bias[layer : layer + 1, :]
    cp[5:6, :] = norm[layer : layer + 1, :]
    cp[6:8, :] = expand(hp[...], ind[...])[2:4, :]
    sp[0:4, :] = convs[layer]
    sp[4:5, :] = biass[layer : layer + 1, :]


def place_rows(dst, at, value):
    r = dst.shape[1]
    for g in range(0, value.shape[0], 16):
        dst[(at + g) // r, (at + g) % r : (at + g) % r + 16, :] = value[g : g + 16].astype(dst.dtype)


def pack_rows(size):
    return -(-PACK // (16 * size)) * 16


def put_pack(dst, me, turned, steps_low, sdel, dcp, dsp, dhp, dgain):
    model = turned.shape[0]
    quarter = model // 4
    w = sdel.shape[1]

    def empty(n):
        return jnp.zeros((n, w), F32)

    place_rows(dst, 0, mm(turned[pl.ds(pl.multiple_of(me * quarter, quarter), quarter), :], sdel[...]))
    place_rows(dst, quarter, jnp.concatenate([dsp, empty(8)], axis=0))
    grown = mm(turned[...], steps_low[...]).T[:16]
    at = quarter + 16
    for b in range(model // w):
        place_rows(dst, at, grown[:, b * w : (b + 1) * w])
        at += 16
    place_rows(dst, at, jnp.concatenate([dcp[:, :w], dcp[:, w : 2 * w]], axis=0))
    place_rows(dst, at + 16, jnp.concatenate([dcp[:, 2 * w :], jnp.concatenate([dhp, dhp], axis=1)], axis=0))
    rows = [dgain[:, b * w : (b + 1) * w] for b in range(model // w)]
    place_rows(dst, at + 32, jnp.concatenate(rows + [empty(16 - len(rows))], axis=0))
    assert at + 48 == PACK


class Smalls:
    def __init__(self, line, square, pack, near, away, own, full, wide, sems):
        send, recv, keep, gsend, grecv, self.xsend, self.xrecv = sems
        self.square, self.full, self.wide = square, full, wide
        self.layers = range(pack.shape[0])
        self.sum = Scatter(line, pack, lambda j: own.at[j], near, away, send, recv)
        self.spread = Gather(line, lambda j: own.at[j], full, keep, gsend, grecv)

    def swap(self, k):
        sq = self.square
        slot = (sq.me, sq.me, lax.rem(sq.me + 2, 4))[k]
        who = (sq.across, sq.mate, sq.mate)[k]
        return remote(self.wide.at[slot], self.wide.at[slot], self.xsend.at[k], self.xrecv.at[k], who)

    def start(self):
        for j in self.layers:
            self.sum.start(j)

    def fold(self):
        for j in self.layers:
            for m in range(self.sum.line.n):
                self.sum.fold(j, m)

    def turn(self):
        for j in self.layers:
            self.sum.finish(j)
            self.spread.start(j)

    def relay(self, k):
        for j in self.layers:
            self.spread.relay(j, k)

    def cross(self):
        for j in self.layers:
            self.spread.arrive(j)
            flat = self.full[j].reshape(-1, self.full.shape[3])
            self.wide[self.square.me, j] = flat[: self.wide.shape[2]]
        self.swap(0).start()
        self.swap(1).start()

    def cross_on(self):
        self.swap(0).wait_recv()
        self.swap(2).start()

    def end(self):
        self.swap(1).wait_recv()
        self.swap(2).wait_recv()
        for k in range(3):
            self.swap(k).wait_send()
        for j in self.layers:
            self.sum.drain(j)
            self.spread.drain(j)


def smalls_scratch(size, w, layers):
    r, n = pack_rows(size), size // 2
    buffers = [
        pltpu.VMEM((layers, size, r, w), BF16),
        pltpu.VMEM((layers, n, r, w), BF16),
        pltpu.VMEM((layers, n, r, w), BF16),
        pltpu.VMEM((layers, r, w), BF16),
        pltpu.VMEM((layers, size, r, w), BF16),
        pltpu.VMEM((4, layers, SPAN, w), BF16),
    ]
    sems = [
        pltpu.SemaphoreType.DMA((2, layers, n)),
        pltpu.SemaphoreType.DMA((2, layers, n)),
        pltpu.SemaphoreType.DMA((layers,)),
        pltpu.SemaphoreType.DMA((layers, 3, size)),
        pltpu.SemaphoreType.DMA((layers, size)),
        pltpu.SemaphoreType.DMA((3,)),
        pltpu.SemaphoreType.DMA((3,)),
    ]
    return buffers + sems


def forward_body(*refs, size, heads, per, steps, layer):
    refs = list(refs)

    def take(n):
        got = refs[:n]
        del refs[:n]
        return got

    mid = layer > 0
    (res_hbm,) = take(1)
    if mid:
        scaled_hbm, wout_hbm, sq_ref = take(3)
    state_hbm, step_hbm, in_hbm, out_hbm, gain_ref = take(5)
    params = take(6)
    if mid:
        new_hbm, sums_ref = take(2)
    normed_hbm, rnorm_ref, small_hbm, inner_hbm, gate_hbm, wt_hbm, full_hbm, ssd_ref, scaled_ref, sqs_ref, st_ref = take(11)
    if mid:
        scaled_in, wout, part, got, far, other, rows_got, facs, fresh, sends, recvs, rsend, rrecv = take(13)
    res, wstate, wt, slabs, normed, turned, small, inner, gate, ext, exts, state = take(12)
    cp_ref, sp_ref, hp_ref, ind_ref, keep, gsend, grecv, load, sems = take(9)
    assert not refs

    n = CHUNK
    tokens_n, model = res.shape
    width = inner.shape[1]
    top = 2 * width + 2 * STATE
    i = pl.program_id(0)
    line = Line(size)
    square = Square()
    job = Gather(line, lambda j: out_hbm.at[layer] if j == 2 else in_hbm.at[layer, 1 - j], slabs, keep, gsend, grecv)
    outgoing = [(turned, normed_hbm), (small, small_hbm), (inner, inner_hbm), (gate, gate_hbm)]
    outgoing += [(wt, wt_hbm), (slabs.at[2], full_hbm)]
    if mid:
        outgoing.append((fresh, new_hbm))

    def flush(k):
        return pltpu.make_async_copy(*outgoing[k], sems.at[k])


    @pl.when(i == 0)
    def _():
        pairs = [(res_hbm, res), (state_hbm.at[layer], wstate), (step_hbm.at[layer], wt.at[pl.ds(top, LANES), :])]
        if mid:
            pairs = [(scaled_hbm, scaled_in), (wout_hbm, wout)] + pairs
        loads = [pltpu.make_async_copy(src, dst, load.at[k]) for k, (src, dst) in enumerate(pairs)]
        for copy in loads:
            copy.start()
        line.greet(pltpu.get_barrier_semaphore(), square.others() if mid else ())
        job.start(0)
        put_params(cp_ref, sp_ref, hp_ref, ind_ref, layer, params)
        ticks = [functools.partial(job.relay, 0, k) for k in range(1, line.n)]
        ticks.append(functools.partial(job.start, 1))
        ticks += [functools.partial(job.relay, 1, k) for k in range(1, line.n)]
        ticks.append(functools.partial(job.start, 2))

        if mid:
            chunks = model // SLICE
            half = tokens_n // 2
            sums = Total(square, part, got, far, other, sends, recvs)
            copies = [
                remote(sq_ref, rows_got.at[square.me], rsend.at[k], rrecv.at[k], who)
                for k, who in enumerate(square.others())
            ]
            for copy in copies:
                copy.start()
            loads[0].wait()
            loads[1].wait()
            for c in range(chunks):
                value = mm(scaled_in[...], wout[c * SLICE : (c + 1) * SLICE, :], NT).astype(BF16)
                part[2 * c] = value[:half]
                part[2 * c + 1] = value[half:]
                sums.step(0, c)
                if c:
                    sums.step(1, c - 1)
            sums.step(1, chunks - 1)
            rows_got[square.me] = sq_ref[...]
            for copy in copies:
                copy.wait()
            total = (rows_got[0] + rows_got[1]) + (rows_got[2] + rows_got[3])
            sums_ref[...] = total
            factor = lax.rsqrt(total / INNER + EPS)
            for t in range(tokens_n // LANES):
                facs[t * LANES : (t + 1) * LANES, :] = jnp.broadcast_to(factor[t], (LANES, LANES)).T
            loads[2].wait()

            def use(c):
                for h in range(2):
                    where = slice(h * half, (h + 1) * half)
                    for s in range(SLICE // LANES):
                        lanes = slice(c * SLICE + s * LANES, c * SLICE + (s + 1) * LANES)
                        value = part[2 * c + h, :, s * LANES : (s + 1) * LANES].astype(F32)
                        fresh[where, lanes] = res[where, lanes].astype(F32) + facs[where, :] * value

            spread = max(1, -(-len(ticks) // chunks))
            for c in range(chunks):
                for tick in ticks[:spread]:
                    tick()
                ticks = ticks[spread:]
                sums.step(2, c)
                if c:
                    sums.step(3, c - 1)
                    use(c - 1)
            sums.step(3, chunks - 1)
            use(chunks - 1)
            flush(6).start()
        else:
            loads[0].wait()
        loads[-2].wait()
        loads[-1].wait()
        for b in range(2 * STATE // LANES):
            rows = slice(2 * width + b * LANES, 2 * width + (b + 1) * LANES)
            wt[rows, :] = wstate[:, b * LANES : (b + 1) * LANES].T

        def norm(t, _):
            rows = pl.ds(pl.multiple_of(t * TILE, TILE), TILE)
            value = (fresh if mid else res)[rows, :].astype(F32)
            scale = lax.rsqrt(jnp.sum(value * value, axis=1, keepdims=True) / model + EPS)
            low = (value * scale * gain_ref[layer : layer + 1, :]).astype(BF16)
            rnorm_ref[rows, :] = scale
            normed[rows, :] = low
            turned[:, rows] = low.T
            small[rows, : 2 * STATE] = mm(low, wstate[...])
            small[rows, 2 * STATE :] = mm(low, wt[top:, :], NT)
            return 0

        lax.fori_loop(0, tokens_n // TILE, norm, 0)
        flush(0).start()
        flush(1).start()
        for tick in ticks:
            tick()

        def project(j, dst):
            weight = slabs[j].reshape(model, width)

            def tile(t, _):
                rows = pl.ds(pl.multiple_of(t * TILE, TILE), TILE)
                dst[rows, :] = mm(normed[rows, :], weight)
                return 0

            lax.fori_loop(0, tokens_n // TILE, tile, 0)

        for j, dst in ((0, inner), (1, gate)):
            job.arrive(j)
            project(j, dst)
            flush(2 + j).start()

    for k in range(1, line.n):
        @pl.when(i == 1 + (k - 1) * steps // line.n)
        def _(k=k):
            job.relay(2, k)

    @pl.when(i > 0)
    def _():
        at = i - 1
        where = pl.ds(pl.multiple_of(at * n, n), n)

        @pl.when(lax.rem(at, per) == 0)
        def _():
            ext[0:8, :] = jnp.zeros((8, width), F32)
            exts[0:8, :] = jnp.zeros((8, 2 * STATE), F32)
            state[...] = jnp.zeros_like(state)

        rows, cols = iotas(n)
        ind = ind_ref[...]
        ext[8 : 8 + n, :] = inner[where, :]
        pre = conv_pre(ext, cp_ref, n)
        x = pre * sigmoid(pre)
        ext[0:8, :] = ext[n : n + 8, :]
        mini = small[where, :]
        exts[8 : 8 + n, :] = mini[:, : 2 * STATE]
        pres = conv_pre(exts, sp_ref, n)
        bc = (pres * sigmoid(pres)).astype(BF16)
        exts[0:8, :] = exts[n : n + 8, :]
        key, query = bc[:, :STATE], bc[:, STATE:]

        _, step, rate, cs, wide_step, wide_cs, wide_tail = scan_prep(mini, hp_ref, ind, n)
        cs2 = cs * LOG2E
        cs2t = cs2.T
        xs = x * wide_step
        lane = lax.broadcasted_iota(jnp.int32, (1, width), 1)
        half = jnp.where(lax.rem(lane, 2 * HEAD) < HEAD, 1.0, 0.0).astype(BF16)
        xsb = xs.astype(BF16)
        xs0 = xsb * half
        xs1 = xsb - xs0
        before = state[...]
        low = before.astype(BF16)
        st_ref[0] = low
        carried = mm(query, low) * wide_cs
        xw = (xs * wide_tail).astype(BF16)
        state[...] = before * wide_cs[n - 1 : n, :] + mm(key, xw, TN)
        scores = jnp.where(rows >= cols, mm(query, key, NT), 0.0)
        for pair in range(heads // 2):
            lanes = slice(pair * 2 * HEAD, (pair + 1) * 2 * HEAD)
            mats = []
            for h in (2 * pair, 2 * pair + 1):
                dec = jnp.exp2(jnp.minimum(cs2[:, h : h + 1] - cs2t[h : h + 1, :], 0.0))
                mats.append((scores * dec).astype(BF16))
            local = mm(
                jnp.concatenate(mats, axis=1),
                jnp.concatenate([xs0[:, lanes], xs1[:, lanes]], axis=0),
            )
            ssd_ref[:, lanes] = local + carried[:, lanes] + cp_ref[6:7, lanes] * x[:, lanes]
        gates = gate[where, :]
        gated = ssd_ref[...] * (gates * sigmoid(gates))
        sqs_ref[0] = rowsum(gated * gated)
        scaled_ref[...] = (gated * cp_ref[5:6, :]).astype(BF16)

        span = model // LANES
        share = -(-2 * span // steps)
        for k in range(share):
            b = at * share + k

            @pl.when(b < 2 * span)
            def _(b=b):
                j, col = b // span, lax.rem(b, span)
                slab_rows = slabs.shape[2]
                weight = slabs.at[j]
                piece = block_of(weight, col, slab_rows)
                wt[pl.ds(pl.multiple_of(j * width, width), width), pl.ds(pl.multiple_of(col * LANES, LANES), LANES)] = piece.T

    @pl.when(i == steps)
    def _():
        flush(4).start()
        job.arrive(2)
        flush(5).start()
        for j in range(3):
            job.drain(j)
        for k in range(len(outgoing)):
            flush(k).wait()


def forward(res, stateproj, steps_w, inproj, outt, gain, params, heads, size, layer, out=None):
    tokens_n, model = res.shape
    _, _, rows, width = inproj.shape
    top = 2 * width + 2 * STATE + LANES
    steps = tokens_n // CHUNK
    mid = out is not None
    hbm = pl.BlockSpec(memory_space=pl.ANY)
    chunks = model // SLICE

    def whole(a):
        return pl.BlockSpec(a.shape, lambda i: (0,) * len(a.shape))

    def row(w):
        return pl.BlockSpec((CHUNK, w), lambda i: (jnp.maximum(i - 1, 0), 0))

    args, in_specs, out_specs, out_shape, scratch = [res], [hbm], [], [], []
    if mid:
        args += list(out)
        in_specs += [hbm, hbm, whole(out[2])]
        out_specs += [hbm, whole(out[2])]
        out_shape += [jax.ShapeDtypeStruct(res.shape, F32), jax.ShapeDtypeStruct(out[2].shape, F32)]
        chunk = pltpu.VMEM((chunks, tokens_n // 2, SLICE), BF16)
        scratch += [
            pltpu.VMEM(out[0].shape, BF16),
            pltpu.VMEM(out[1].shape, BF16),
            pltpu.VMEM((2 * chunks, tokens_n // 2, SLICE), BF16),
            chunk, chunk, chunk,
            pltpu.VMEM((4,) + out[2].shape, F32),
            pltpu.VMEM((tokens_n, LANES), F32),
            pltpu.VMEM(res.shape, F32),
            pltpu.SemaphoreType.DMA((3, chunks)),
            pltpu.SemaphoreType.DMA((3, chunks)),
            pltpu.SemaphoreType.DMA((3,)),
            pltpu.SemaphoreType.DMA((3,)),
        ]
    args += [stateproj, steps_w, inproj, outt, gain, *params]
    in_specs += [hbm, hbm, hbm, hbm, whole(gain)] + [whole(v) for v in params]
    out_specs += [
        hbm, pl.BlockSpec((tokens_n, 1), lambda i: (0, 0)), hbm, hbm, hbm, hbm, hbm,
        row(width), row(width),
        pl.BlockSpec((1, 1, CHUNK), lambda i: (jnp.maximum(i - 1, 0), 0, 0)),
        pl.BlockSpec((1, STATE, width), lambda i: (jnp.maximum(i - 1, 0), 0, 0)),
    ]
    out_shape += [
        jax.ShapeDtypeStruct((model, tokens_n), BF16),
        jax.ShapeDtypeStruct((tokens_n, 1), F32),
        jax.ShapeDtypeStruct((tokens_n, 2 * STATE + LANES), F32),
        jax.ShapeDtypeStruct((tokens_n, width), F32),
        jax.ShapeDtypeStruct((tokens_n, width), F32),
        jax.ShapeDtypeStruct((top, model), BF16),
        jax.ShapeDtypeStruct((size, rows, width), BF16),
        jax.ShapeDtypeStruct((tokens_n, width), F32),
        jax.ShapeDtypeStruct((tokens_n, width), BF16),
        jax.ShapeDtypeStruct((steps, 1, CHUNK), F32),
        jax.ShapeDtypeStruct((steps, STATE, width), BF16),
    ]
    scratch += [
        pltpu.VMEM(res.shape, res.dtype),
        pltpu.VMEM((model, 2 * STATE), BF16),
        pltpu.VMEM((top, model), BF16),
        pltpu.VMEM((3, size, rows, width), BF16),
        pltpu.VMEM((tokens_n, model), BF16),
        pltpu.VMEM((model, tokens_n), BF16),
        pltpu.VMEM((tokens_n, 2 * STATE + LANES), F32),
        pltpu.VMEM((tokens_n, width), F32),
        pltpu.VMEM((tokens_n, width), F32),
        pltpu.VMEM((CHUNK + 8, width), F32),
        pltpu.VMEM((CHUNK + 8, 2 * STATE), F32),
        pltpu.VMEM((STATE, width), F32),
        pltpu.VMEM((8, width), F32),
        pltpu.VMEM((8, 2 * STATE), F32),
        pltpu.VMEM((8, LANES), F32),
        pltpu.VMEM((LANES, width), BF16),
        pltpu.SemaphoreType.DMA((3,)),
        pltpu.SemaphoreType.DMA((3, 3, size)),
        pltpu.SemaphoreType.DMA((3, size)),
        pltpu.SemaphoreType.DMA((5,)),
        pltpu.SemaphoreType.DMA((7,)),
    ]
    return pl.pallas_call(
        functools.partial(forward_body, size=size, heads=heads, per=LEN // CHUNK, steps=steps, layer=layer),
        grid=(steps + 1,),
        in_specs=in_specs,
        out_specs=out_specs,
        out_shape=out_shape,
        scratch_shapes=scratch,
        compiler_params=pltpu.CompilerParams(
            collective_id=min(layer, 1), has_side_effects=True, vmem_limit_bytes=VMEM_LIMIT
        ),
        name="forward",
    )(*args)


def back_body(*refs, heads, per, size, steps, layer, last):
    refs = list(refs)

    def take(n):
        got = refs[:n]
        del refs[:n]
        return got

    up_ref, sq_ref, gate_ref, ssd_ref, inner_ref, iprev_ref, small_ref, sprev_ref, st_ref, res_ref, rn_ref = take(11)
    gain_ref = take(1)[0]
    params = take(6)
    wout_hbm, scaled_hbm, wt_hbm, normed_hbm = take(4)
    if not last:
        next_normed, next_steps, next_sdel, next_inner, next_dcp, next_dsp, next_dhp, next_dgain = take(8)
    new_ref, grad_hbm = take(2)
    if last:
        held_hbm, sdsum_ref, steplow_ref, dcp_ref, dsp_ref, dhp_ref, dgain_ref, mixed_ref = take(8)
    else:
        full_hbm, wide_hbm = take(2)
    ext, exts, cde, cdes, dstate, rq, cp_ref, sp_ref, hp_ref, ind_ref = take(10)
    wout, scaled, wt, turned, dy, glow, ilow, frow, srow, sgot = take(10)
    part, near, away, tpart, got, far, other = take(7)
    load, rsend, rrecv, ssend, srecv, sends, recvs, gsem = take(8)
    if last:
        held, fgot, opart, ogot, ofar, oother, fsend, frecv, osends, orecvs = take(10)
    else:
        dcp_ref, dsp_ref, dhp_ref, dgain_ref = take(4)
        sd_all = scaled.at[:, pl.ds(0, 2 * STATE)]
        step_all = scaled.at[:, pl.ds(2 * STATE, LANES)]
        buffers = take(6)
        sems = take(7)
    assert not refs

    n = CHUNK
    model = up_ref.shape[1]
    i = pl.program_id(0)
    begin_gate = steps
    begin_scan = begin_gate + steps
    begin_norm = begin_scan + steps
    end = begin_norm + steps - 1
    line = Line(size)
    square = Square()
    rows_own = part.shape[2]
    count = part.shape[0]
    job = Scatter(line, part, lambda j: dy.at[pl.ds(j * rows_own, rows_own), :], near, away, ssend, srecv)
    sums = Total(square, tpart, got, far, other, sends, recvs)
    if last:
        outs = Total(square, opart, ogot, ofar, oother, osends, orecvs)
        half = steps * n // 2
        slices = model // SLICE
    else:
        minis = Smalls(line, square, *buffers, sems)
    moves = [(wout_hbm, wout), (scaled_hbm, scaled), (wt_hbm, wt), (normed_hbm, turned)]
    if last:
        moves.append((held, held_hbm))
    else:
        tokens_n = steps * n
        spots = (wt.at[pl.ds(0, model), pl.ds(0, tokens_n)],)
        spots += tuple(
            wt.at[pl.ds(0, tokens_n), pl.ds(tokens_n + at, w)] for at, w in ((0, LANES), (LANES, 2 * STATE))
        )
        moves += [(next_normed, spots[0]), (next_steps, spots[1]), (next_sdel, spots[2]), (next_inner, part.at[3])]

    def move(k):
        return pltpu.make_async_copy(*moves[k], load.at[k])

    places = line.n

    def spaced(begin, stop, m):
        return begin + m * (stop - begin) // places

    middle = begin_scan + steps // 2
    if last:
        folds = [(spaced(begin_scan, middle, m), 0, m) for m in range(places)]
        folds += [(spaced(middle, begin_norm, m) + 1, 1, m) for m in range(places)]
    else:
        folds = [(spaced(begin_gate - 1, begin_scan + 3, m), 3, m) for m in range(places)]
        folds += [(spaced(begin_scan + 2, middle + 3, m), 0, m) for m in range(places)]
        folds += [(spaced(begin_norm - 1, end - 1, m), 1, m) for m in range(places)]

    def column(row):
        return jnp.broadcast_to(row, (n, n)).T[:, 0:1]

    @pl.when(i == 0)
    def _():
        for k in range(3):
            move(k).start()
        if not last:
            move(7).start()
        put_params(cp_ref, sp_ref, hp_ref, ind_ref, layer, params)
        rq[...] = jnp.zeros_like(rq)
        line.greet_all(pltpu.get_barrier_semaphore(), square.others())
        if last:
            rows = [
                remote(sq_ref, fgot.at[square.me], fsend.at[k], frecv.at[k], who)
                for k, who in enumerate(square.others())
            ]
            for copy in rows:
                copy.start()
            fgot[square.me] = sq_ref[...]
            move(0).wait()
            move(1).wait()
            for c in range(slices):
                value = mm(scaled[...], wout[c * SLICE : (c + 1) * SLICE, :], NT).astype(BF16)
                opart[2 * c] = value[:half]
                opart[2 * c + 1] = value[half:]
                outs.step(0, c)
            outs.step(1, 0)
            for copy in rows:
                copy.wait()
            total = (fgot[0] + fgot[1]) + (fgot[2] + fgot[3])
        else:
            move(7).wait()
            job.start(3)
            total = sq_ref[...]
            move(0).wait()
            move(1).wait()
        dcp_ref[...] = jnp.zeros_like(dcp_ref)
        dsp_ref[...] = jnp.zeros_like(dsp_ref)
        dhp_ref[...] = jnp.zeros_like(dhp_ref)
        dgain_ref[...] = jnp.zeros_like(dgain_ref)
        frow[...] = lax.rsqrt(total / INNER + EPS)

    ind = ind_ref[...]
    for at, j, m in folds:
        @pl.when(i == at)
        def _(j=j, m=m):
            job.fold(j, m)

    @pl.when(i < begin_gate)
    def _():
        rows = pl.ds(pl.multiple_of(i * n, n), n)
        low = (column(frow[i]) * up_ref[...].astype(F32)).astype(BF16)
        turned[:, rows] = low.T
        sd = mm(low, wout[...])
        dy[rows, :] = sd
        piece = scaled[rows, :]
        srow[i] = rowsum(piece.astype(F32) * sd)

    @pl.when(i == begin_gate - 1)
    def _():
        copies = [
            remote(srow, sgot.at[square.me], rsend.at[k], rrecv.at[k], who) for k, who in enumerate(square.others())
        ]
        for copy in copies:
            copy.start()
        job.emit(0, turned, scaled)
        move(3).start()
        sgot[square.me] = srow[...]
        for copy in copies:
            copy.wait()
        srow[...] = (sgot[0] + sgot[1]) + (sgot[2] + sgot[3])

    if last:
        @pl.when(i == steps // 2)
        def _():
            outs.step(1, 1)

        @pl.when((i >= begin_gate) & (i < begin_gate + slices - 2))
        def _():
            outs.step(1, i - begin_gate + 2)

    @pl.when((i >= begin_gate) & (i < begin_scan))
    def _():
        c = i - begin_gate
        rows = pl.ds(pl.multiple_of(c * n, n), n)
        coef = column(frow[c] * frow[c] * srow[c]) / INNER
        gate = gate_ref[...]
        gsig = sigmoid(gate)
        gact = gate * gsig
        ssd = ssd_ref[...]
        sd = dy[rows, :]
        gated = ssd * gact
        gd = cp_ref[5:6, :] * sd - coef * gated
        dcp_ref[5:6, :] += colsum(gated * sd)
        dy[rows, :] = gd * gact
        glow[rows, :] = (gd * ssd * (gsig + gact * (1.0 - gsig))).astype(BF16)

    @pl.when(i == begin_scan - 1)
    def _():
        move(3).wait()
        job.emit(1, turned, glow)
        move(2).wait()

    @pl.when((i >= begin_scan) & (i < begin_norm))
    def _():
        q = i - begin_scan
        chunk = steps - 1 - q
        where = pl.ds(pl.multiple_of(chunk * n, n), n)

        @pl.when(lax.rem(chunk, per) == per - 1)
        def _():
            cde[n : n + 8, :] = jnp.zeros((8, cde.shape[1]), F32)
            cdes[n : n + 8, :] = jnp.zeros((8, cdes.shape[1]), F32)
            dstate[...] = jnp.zeros_like(dstate)

        keep = jnp.where(lax.rem(chunk, per) == 0, 0.0, 1.0).astype(F32)
        rows, cols = iotas(n)
        ext[0:8, :] = iprev_ref[...] * keep
        ext[8 : 8 + n, :] = inner_ref[...]
        exts[0:8, :] = sprev_ref[:, : 2 * STATE] * keep
        exts[8 : 8 + n, :] = small_ref[:, : 2 * STATE]
        pre = conv_pre(ext, cp_ref, n)
        sig = sigmoid(pre)
        x = pre * sig
        slope = sig + x * (1.0 - sig)
        pres = conv_pre(exts, sp_ref, n)
        sigs = sigmoid(pres)
        acts = pres * sigs
        slopes = sigs + acts * (1.0 - sigs)
        bc = acts.astype(BF16)
        key, query = bc[:, :STATE], bc[:, STATE:]
        dyc = dy[where, :]

        raw, step, rate, cs, wide_step, wide_cs, wide_tail = scan_prep(small_ref, hp_ref, ind, n)
        cs2 = cs * LOG2E
        cs2t = cs2.T
        xs = x * wide_step
        xsb = xs.astype(BF16)
        dyb = dyc.astype(BF16)
        lane = lax.broadcasted_iota(jnp.int32, (1, xs.shape[1]), 1)
        half = jnp.where(lax.rem(lane, 2 * HEAD) < HEAD, 1.0, 0.0).astype(BF16)
        dy0 = dyb * half
        dy1 = dyb - dy0
        low = st_ref[0]
        dst = dstate[...]
        dlow = dst.astype(BF16)
        dye = dyc * wide_cs
        dyeb = dye.astype(BF16)
        up = headsum(dye * mm(query, low), ind)
        dxs_state = wide_tail * mm(key, dlow)
        down = headsum(xs * dxs_state, ind)
        qdel = mm(dyeb, low, NT)
        kdel = mm((xs * wide_tail).astype(BF16), dlow, NT)
        through = headsum(jnp.broadcast_to(colsum(low.astype(F32) * dst), (8, dst.shape[1])), ind)[0:1, :]
        through = through * jnp.exp(cs[n - 1 : n, :])
        dstate[...] = dst * wide_cs[n - 1 : n, :] + mm(query, dyeb, TN)

        scores = jnp.where(rows <= cols, mm(key, query, NT), 0.0)
        dscores = jnp.zeros((n, n), F32)
        colq = jnp.zeros((n, LANES), F32)
        lane = lax.broadcasted_iota(jnp.int32, (n, LANES), 1)
        dxs = []
        for pair in range(heads // 2):
            lanes = slice(pair * 2 * HEAD, (pair + 1) * 2 * HEAD)
            stacked = jnp.concatenate([dy0[:, lanes], dy1[:, lanes]], axis=0)
            both = mm(xsb[:, lanes], stacked, NT)
            mats = []
            for which, h in enumerate((2 * pair, 2 * pair + 1)):
                dec = jnp.exp2(jnp.minimum(cs2t[h : h + 1, :] - cs2[:, h : h + 1], 0.0))
                mats.append((scores * dec).astype(BF16))
                term = dec * both[:, which * n : (which + 1) * n]
                dscores = dscores + term
                quad = scores * term
                rq[h : h + 1, :] = colsum(quad)
                colq = jnp.where(lane == h, jnp.sum(quad, axis=1, keepdims=True), colq)
            dxs.append(mm(jnp.concatenate(mats, axis=1), stacked))
        dxs = jnp.concatenate(dxs, axis=1) + dxs_state
        dscores = jnp.where(rows <= cols, dscores, 0.0).astype(BF16)
        kdel = kdel + mm(dscores, query)
        qdel = qdel + mm(dscores, key, TN)

        upper = jnp.where(rows <= cols, 1.0, 0.0).astype(F32)
        strict = jnp.where(rows > cols, 1.0, 0.0).astype(F32)
        da = mm(upper, rq[...].T - colq + up, precision=HIGH) + mm(strict, down, precision=HIGH) + through
        grown = headsum(x * dxs, ind) + rate * da
        step_pre = grown * sigmoid(raw)
        steplow = step_pre.astype(BF16)
        if last:
            steplow_ref[...] = steplow
        else:
            step_all[where, :] = steplow
        dhp_ref[0:1, :] += colsum(step_pre)
        dhp_ref[1:2, :] += rate * colsum(step * da)
        dcp_ref[6:7, :] += colsum(dyc * x)

        cd = (dxs * wide_step + cp_ref[6:7, :] * dyc) * slope
        cde[0:n, :] = cd
        center = ext[8 : 8 + n, :]
        total = cp_ref[3:4, :] * cd
        dcp_ref[3:4, :] += colsum(cd * center)
        for tap in range(3):
            shifted = cde[3 - tap : 3 - tap + n, :]
            total = total + cp_ref[tap : tap + 1, :] * shifted
            dcp_ref[tap : tap + 1, :] += colsum(shifted * center)
        inner_low = total.astype(BF16)
        ilow[where, :] = inner_low
        dcp_ref[4:5, :] += colsum(cd)
        cde[n : n + 8, :] = cde[0:8, :]

        cds = jnp.concatenate([kdel, qdel], axis=1) * slopes
        cdes[0:n, :] = cds
        center = exts[8 : 8 + n, :]
        total = sp_ref[3:4, :] * cds
        dsp_ref[3:4, :] += colsum(cds * center)
        for tap in range(3):
            shifted = cdes[3 - tap : 3 - tap + n, :]
            total = total + sp_ref[tap : tap + 1, :] * shifted
            dsp_ref[tap : tap + 1, :] += colsum(shifted * center)
        sdel = total.astype(BF16)
        dsp_ref[4:5, :] += colsum(cds)
        cdes[n : n + 8, :] = cdes[0:8, :]

        lows = jnp.concatenate([inner_low, glow[where, :], sdel, steplow], axis=1)
        value = mm(lows, wt[...]).astype(BF16)
        tpart[2 * q, :, :model] = value[: n // 2]
        tpart[2 * q + 1, :, :model] = value[n // 2 :]
        tpart[2 * q, :, model:] = sdel[: n // 2]
        tpart[2 * q + 1, :, model:] = sdel[n // 2 :]
        sums.step(0, q)

    @pl.when((i > begin_scan) & (i <= begin_norm))
    def _():
        sums.step(1, i - begin_scan - 1)

    @pl.when((i >= begin_scan + 5) & (i < begin_norm + 5))
    def _():
        sums.step(2, i - begin_scan - 5)

    @pl.when((i >= begin_scan + 6) & (i < begin_norm + 6))
    def _():
        sums.step(3, i - begin_scan - 6)

    if last:
        @pl.when((i > begin_scan) & (i <= begin_scan + slices))
        def _():
            outs.step(2, i - begin_scan - 1)

        @pl.when((i > begin_scan + 1) & (i <= begin_scan + slices + 1))
        def _():
            outs.step(3, i - begin_scan - 2)

    @pl.when(i == begin_norm - 1)
    def _():
        dhp_ref[2:3, :] = headsum(jnp.broadcast_to(dcp_ref[6:7, :], (8, dcp_ref.shape[1])), ind)[0:1, :]
        if last:
            job.product(held, turned, ilow)
            move(4).start()
        else:
            job.emit(2, turned, ilow, places // 2)
            for k in (4, 5, 6):
                move(k).start()

    if not last:
        @pl.when(i == begin_norm + 1)
        def _():
            for k in (4, 5, 6):
                move(k).wait()
            put_pack(
                buffers[0].at[1], square.me, *spots, next_dcp[...], next_dsp[...], next_dhp[...], next_dgain[...]
            )
            minis.sum.start(1)

    @pl.when(i >= begin_norm)
    def _():
        r = i - begin_norm
        chunk = steps - 1 - r
        if last:
            fac = column(frow[chunk])
            side = chunk // (steps // 2)
            base = (chunk - side * (steps // 2)) * n
        for h in range(2):
            rows = slice(h * (n // 2), (h + 1) * (n // 2))
            back = tpart[2 * r + h, :, :model].astype(F32)
            sdel = tpart[2 * r + h, :, model:]
            if last:
                sdsum_ref[rows, :] = sdel
            else:
                sd_all[pl.ds(pl.multiple_of(chunk * n + h * (n // 2), n // 2), n // 2), :] = sdel
            res = res_ref[rows, :].astype(F32)
            rn = rn_ref[rows, :]
            dgain_ref[...] += colsum(back * res * rn)
            gained = back * gain_ref[layer : layer + 1, :]
            mean = jnp.sum(gained * res, axis=1, keepdims=True) / model
            new_ref[rows, :] = up_ref[rows, :].astype(F32) + rn * gained - (rn * rn * rn * mean) * res
            if last:
                where = pl.ds(pl.multiple_of(base + h * (n // 2), n // 2), n // 2)
                for c in range(slices):
                    span = slice(c * SLICE, (c + 1) * SLICE)
                    summed = opart[2 * c + side, where, :].astype(F32)
                    mixed_ref[rows, span] = (res[:, span] + fac[rows, :] * summed).astype(BF16)

    @pl.when(i == end)
    def _():
        def finish(j):
            job.finish(j)
            pltpu.make_async_copy(dy.at[pl.ds(j * rows_own, rows_own), :], grad_hbm.at[j], gsem.at[j]).start()

        if not last:
            put_pack(
                buffers[0].at[0], square.me, turned, step_all, sd_all, dcp_ref[...], dsp_ref[...], dhp_ref[...], dgain_ref[...]
            )
            minis.sum.start(0)
            for m in range(places // 2, places):
                job.lead(2, m)
            for m in range(places // 2):
                job.fold(2, m)
            finish(3)
        finish(0)
        finish(1)
        if not last:
            minis.fold()
            minis.turn()
            for k in range(1, line.n):
                minis.relay(k)
            for m in range(places // 2, places):
                job.fold(2, m)
            minis.cross()
            finish(2)
            minis.cross_on()
            minis.end()
            tails = [
                pltpu.make_async_copy(src, dst, load.at[k])
                for k, (src, dst) in enumerate(((minis.full, full_hbm), (minis.wide, wide_hbm)))
            ]
            for copy in tails:
                copy.start()
        for j in range(count):
            job.drain(j)
            pltpu.make_async_copy(dy.at[pl.ds(j * rows_own, rows_own), :], grad_hbm.at[j], gsem.at[j]).wait()
        if last:
            move(4).wait()
        else:
            for copy in tails:
                copy.wait()


def back(up, sq, gate_pre, ssd, inner_raw, small, states, res, rnorm, gain, params,
         wout, scaled, wt, normed, heads, size, layer, after=None):
    tokens_n, width = inner_raw.shape
    model = up.shape[1]
    last = after is None
    steps = tokens_n // CHUNK
    begin_scan = 2 * steps
    begin_norm = begin_scan + steps
    rows = model // size
    n = size // 2
    hbm = pl.BlockSpec(memory_space=pl.ANY)
    top = steps - 1

    def norm_at(i):
        return jnp.where(i < begin_norm, top, top - (i - begin_norm))

    def scan_at(i):
        return jnp.clip(top - (i - begin_scan), 0, top)

    def first(w):
        return pl.BlockSpec((CHUNK, w), lambda i: (jnp.where(i < steps, i, norm_at(i)), 0))

    def second(w):
        return pl.BlockSpec((CHUNK, w), lambda i: (jnp.clip(i - steps, 0, top), 0))

    def scan(w):
        return pl.BlockSpec((CHUNK, w), lambda i: (scan_at(i), 0))

    def prev(w):
        return pl.BlockSpec((8, w), lambda i: (jnp.maximum(scan_at(i) * (CHUNK // 8) - 1, 0), 0))

    def norm(w):
        return pl.BlockSpec((CHUNK, w), lambda i: (norm_at(i), 0))

    def whole(a):
        return pl.BlockSpec(a.shape, lambda i: (0,) * len(a.shape))

    extra = model + 2 * STATE
    quarter = pltpu.VMEM((steps, CHUNK // 2, extra), BF16)
    count = 2 if last else 4
    pieces = pltpu.VMEM((count, n, rows, width), BF16)
    args = [up, sq, gate_pre, ssd, inner_raw, inner_raw, small, small, states, res, rnorm, gain, *params,
            wout, scaled, wt, normed]
    in_specs = [
        first(model), whole(sq), second(width), second(width),
        scan(width), prev(width), scan(small.shape[1]), prev(small.shape[1]),
        pl.BlockSpec((1, STATE, width), lambda i: (scan_at(i), 0, 0)),
        norm(model), norm(1), whole(gain),
    ] + [whole(a) for a in params] + [hbm] * 4
    out_specs = [norm(model), hbm]
    out_shape = [jax.ShapeDtypeStruct((tokens_n, model), F32), jax.ShapeDtypeStruct((count, rows, width), F32)]
    totals = [(8, width), (8, 2 * STATE), (8, LANES), (1, model)]
    scratch = [
        pltpu.VMEM((CHUNK + 8, width), F32),
        pltpu.VMEM((CHUNK + 8, 2 * STATE), F32),
        pltpu.VMEM((CHUNK + 8, width), F32),
        pltpu.VMEM((CHUNK + 8, 2 * STATE), F32),
        pltpu.VMEM((STATE, width), F32),
        pltpu.VMEM((LANES, CHUNK), F32),
        pltpu.VMEM((8, width), F32),
        pltpu.VMEM((8, 2 * STATE), F32),
        pltpu.VMEM((8, LANES), F32),
        pltpu.VMEM((LANES, width), BF16),
        pltpu.VMEM(wout.shape, BF16),
        pltpu.VMEM(scaled.shape, BF16),
        pltpu.VMEM(wt.shape, BF16),
        pltpu.VMEM(normed.shape, BF16),
        pltpu.VMEM((tokens_n, width), F32),
        pltpu.VMEM((tokens_n, width), BF16),
        pltpu.VMEM((tokens_n, width), BF16),
        pltpu.VMEM((steps, 1, CHUNK), F32),
        pltpu.VMEM((steps, 1, CHUNK), F32),
        pltpu.VMEM((4, steps, 1, CHUNK), F32),
        pltpu.VMEM((count, size, rows, width), BF16), pieces, pieces,
        pltpu.VMEM((2 * steps, CHUNK // 2, extra), BF16), quarter, quarter, quarter,
        pltpu.SemaphoreType.DMA((8,)),
        pltpu.SemaphoreType.DMA((3,)),
        pltpu.SemaphoreType.DMA((3,)),
        pltpu.SemaphoreType.DMA((2, count, n)),
        pltpu.SemaphoreType.DMA((2, count, n)),
        pltpu.SemaphoreType.DMA((3, steps)),
        pltpu.SemaphoreType.DMA((3, steps)),
        pltpu.SemaphoreType.DMA((count,)),
    ]
    if last:
        out_specs += [hbm, norm(2 * STATE), scan(LANES)]
        out_specs += [pl.BlockSpec(v, lambda i: (0, 0)) for v in totals] + [norm(model)]
        out_shape += [
            jax.ShapeDtypeStruct((size, rows, width), BF16),
            jax.ShapeDtypeStruct((tokens_n, 2 * STATE), BF16),
            jax.ShapeDtypeStruct((tokens_n, LANES), BF16),
        ]
        out_shape += [jax.ShapeDtypeStruct(v, F32) for v in totals]
        out_shape.append(jax.ShapeDtypeStruct((tokens_n, model), BF16))
        slices = model // SLICE
        chunk = pltpu.VMEM((slices, tokens_n // 2, SLICE), BF16)
        scratch += [
            pltpu.VMEM((size, rows, width), BF16),
            pltpu.VMEM((4, steps, 1, CHUNK), F32),
            pltpu.VMEM((2 * slices, tokens_n // 2, SLICE), BF16), chunk, chunk, chunk,
            pltpu.SemaphoreType.DMA((3,)),
            pltpu.SemaphoreType.DMA((3,)),
            pltpu.SemaphoreType.DMA((3, slices)),
            pltpu.SemaphoreType.DMA((3, slices)),
        ]
    else:
        w = 2 * STATE
        r = pack_rows(size)
        args += list(after)
        in_specs += [hbm] * 4 + [whole(v) for v in after[4:]]
        out_specs += [hbm, hbm]
        out_shape += [
            jax.ShapeDtypeStruct((2, size, r, w), BF16),
            jax.ShapeDtypeStruct((4, 2, SPAN, w), BF16),
        ]
        scratch += [pltpu.VMEM(v, F32) for v in totals]
        scratch += smalls_scratch(size, w, 2)
    return pl.pallas_call(
        functools.partial(
            back_body, heads=heads, per=LEN // CHUNK, size=size, steps=steps, layer=layer, last=last
        ),
        grid=(begin_norm + steps,),
        in_specs=in_specs,
        out_specs=out_specs,
        out_shape=out_shape,
        scratch_shapes=scratch,
        compiler_params=pltpu.CompilerParams(
            collective_id=2 if last else 3, has_side_effects=True, vmem_limit_bytes=VMEM_LIMIT
        ),
        name="back",
    )(*args)


def unpack_body(full_ref, wide_ref, *refs, layers, heads):
    step_ref, state_ref, conv_ref, bias_ref, convs_ref, biass_ref = refs[:6]
    stepbias_ref, decay_ref, skip_ref, norm_ref, gain_ref = refs[6:]
    model = state_ref.shape[1]
    quarter = model // 4
    w = state_ref.shape[2]
    width = conv_ref.shape[2]
    for layer in range(layers):
        for t in range(4):
            state_ref[layer, t * quarter : (t + 1) * quarter, :] = wide_ref[t, layer, :quarter, :].astype(F32)
        taps = [wide_ref[t, layer, quarter : quarter + 16, :].astype(F32) for t in range(4)]
        taps = (taps[0] + taps[1]) + (taps[2] + taps[3])
        convs_ref[layer] = taps[0:4]
        biass_ref[layer : layer + 1, :] = taps[4:5]
        flat = full_ref[layer].reshape(-1, w)[:PACK].astype(F32)
        at = quarter + 16
        for b in range(model // w):
            step_ref[layer, :, b * w : (b + 1) * w] = flat[at : at + 16]
            at += 16
        for b in range(width // w):
            lanes = slice(b * w, (b + 1) * w)
            rows = flat[at + 8 * b : at + 8 * b + 8]
            conv_ref[layer, :, lanes] = rows[0:4]
            bias_ref[layer : layer + 1, lanes] = rows[4:5]
            norm_ref[layer : layer + 1, lanes] = rows[5:6]
        at += 8 * (width // w)
        for k, ref in enumerate((stepbias_ref, decay_ref, skip_ref)):
            ref[layer : layer + 1, :] = flat[at + k : at + k + 1, :heads]
        at += 8
        for b in range(model // w):
            gain_ref[layer : layer + 1, b * w : (b + 1) * w] = flat[at + b : at + b + 1]


def unpack(full, wide, model, width, heads):
    layers, w = full.shape[0], full.shape[3]
    vm = pl.BlockSpec(memory_space=pltpu.VMEM)
    shapes = [
        (layers, 16, model), (layers, model, w), (layers, 4, width), (layers, width), (layers, 4, w), (layers, w),
        (layers, heads), (layers, heads), (layers, heads), (layers, width), (layers, model),
    ]
    return pl.pallas_call(
        functools.partial(unpack_body, layers=layers, heads=heads),
        in_specs=[vm, vm],
        out_specs=[vm] * len(shapes),
        out_shape=[jax.ShapeDtypeStruct(v, F32) for v in shapes],
        compiler_params=pltpu.CompilerParams(vmem_limit_bytes=VMEM_LIMIT),
        name="unpack",
    )(full, wide)


def shards(
    tokens, inproj, stepproj, stateproj, outproj, convinner, biasinner, convstate, biasstate,
    stepbias, decaylog, skipgain, normgain, inputgain, cotangent,
):
    layers = inproj.shape[0]
    width = inproj.shape[3]
    heads = stepproj.shape[2]
    model = tokens.shape[1]
    pad = LANES - heads
    size = lax.axis_size("dp")
    steps_w = jnp.pad(jnp.swapaxes(stepproj, 1, 2), ((0, 0), (0, pad), (0, 0)))
    head = jnp.pad(jnp.stack([stepbias, decaylog, skipgain], axis=1), ((0, 0), (0, 5), (0, pad)))
    outt = jnp.swapaxes(outproj, 1, 2)
    params = (convinner, biasinner, normgain, convstate, biasstate, head)

    residual = tokens
    kept = []
    out = None
    for at in range(layers):
        results = forward(residual, stateproj, steps_w, inproj, outt, inputgain, params, heads, size, at, out=out)
        if at:
            residual, kept[-1][-1] = results[:2]
            results = results[2:]
        normed, rnorm, small, inner_raw, gate_pre, wt, w_out, ssd, scaled, sq, states = results
        w_out = w_out.reshape(model, width)
        kept.append([residual, normed, rnorm, small, inner_raw, gate_pre, wt, w_out, ssd, scaled, states, sq])
        out = (scaled, w_out, sq)

    assert layers == 2
    before, normed, rnorm, small, inner_raw, gate_pre, wt, w_out, ssd, scaled, states, sq = kept[1]
    upstream, second, held, sdel, steplow, *totals, mixed = back(
        cotangent, sq, gate_pre, ssd, inner_raw, small, states, before, rnorm, inputgain, params,
        w_out, scaled, wt, normed, heads, size, 1,
    )
    after = (normed, steplow, sdel, held, *totals)
    before, normed, rnorm, small, inner_raw, gate_pre, wt, w_out, ssd, scaled, states, sq = kept[0]
    upstream, first, full, wide = back(
        upstream, sq, gate_pre, ssd, inner_raw, small, states, before, rnorm, inputgain, params,
        w_out, scaled, wt, normed, heads, size, 0, after=after,
    )
    pairs = [first[1:3], jnp.stack([second[1], first[3]])]
    (
        step_grad, state_grad, conv_grad, bias_grad, convs_grad, biass_grad,
        stepbias_grad, decay_grad, skip_grad, norm_grad, gain_grad,
    ) = unpack(full, wide, model, width, heads)
    return (
        mixed,
        upstream,
        jnp.stack(pairs),
        jnp.swapaxes(step_grad[:, :heads], 1, 2),
        state_grad,
        jnp.swapaxes(jnp.stack([first[0], second[0]]), 1, 2),
        conv_grad,
        bias_grad,
        convs_grad,
        biass_grad,
        stepbias_grad,
        decay_grad,
        skip_grad,
        norm_grad,
        gain_grad,
    )


def solution(mesh):
    in_specs = (
        P("dp", None),
        P(None, None, "dp", "tensor"),
        P(None, None, "tensor"),
        P(),
        P(None, "tensor", "dp"),
        P(None, None, "tensor"),
        P(None, "tensor"),
        P(),
        P(),
        P(None, "tensor"),
        P(None, "tensor"),
        P(None, "tensor"),
        P(None, "tensor"),
        P(),
        P("dp", None),
    )
    out_specs = (
        P("dp", None),
        P("dp", None),
        P(None, None, "dp", "tensor"),
        P(None, None, "tensor"),
        P(),
        P(None, "tensor", "dp"),
        P(None, None, "tensor"),
        P(None, "tensor"),
        P(),
        P(),
        P(None, "tensor"),
        P(None, "tensor"),
        P(None, "tensor"),
        P(None, "tensor"),
        P(),
    )
    return jax.shard_map(shards, mesh=mesh, in_specs=in_specs, out_specs=out_specs, check_vma=False)
```

```python
import functools
import math

import jax
import jax.numpy as jnp
from jax import lax
from jax.experimental import pallas as pl
from jax.experimental.pallas import tpu as pltpu
from jax.sharding import PartitionSpec as P

STATE = 128
LEN = 1024
INNER = 3072
HEAD = 64
CHUNK = 128
SLICE = 256
TILE = 256
PACK = 544
SPAN = 400
VMEM_LIMIT = 65000 * 1024
LANES = 128
EPS = 1e-05
LOG2E = 1.4426950408889634

HIGH = lax.Precision.HIGHEST
NN = (((1,), (0,)), ((), ()))
NT = (((1,), (1,)), ((), ()))
TN = (((0,), (0,)), ((), ()))
F32 = jnp.float32
BF16 = jnp.bfloat16
MESH = pl.DeviceIdType.MESH


def remote(src, dst, send, recv, where):
    return pltpu.make_async_remote_copy(
        src_ref=src, dst_ref=dst, send_sem=send, recv_sem=recv, device_id=where, device_id_type=MESH
    )


class Line:
    def __init__(self, size):
        self.n = size // 2
        me = lax.axis_index("dp")
        self.me = me
        self.at = me // 2
        self.side = lax.rem(me, 2)
        self.pair = {"dp": me + 1 - 2 * self.side}
        self.right = {"dp": jnp.minimum(me + 2, size - 1)}
        self.left = {"dp": jnp.maximum(me - 2, 0)}
        odd = lax.rem(self.at, 2)
        self.odd = odd == 1
        self.near = {"dp": me + 2 - 4 * odd}
        self.has_left = self.at > 0
        self.has_right = self.at < self.n - 1

    def greet(self, barrier, more=()):
        for who in more:
            pl.semaphore_signal(barrier, inc=1, device_id=who, device_id_type=MESH)
        pl.semaphore_signal(barrier, inc=1, device_id=self.pair, device_id_type=MESH)

        @pl.when(self.has_left)
        def _():
            pl.semaphore_signal(barrier, inc=1, device_id=self.left, device_id_type=MESH)

        @pl.when(self.has_right)
        def _():
            pl.semaphore_signal(barrier, inc=1, device_id=self.right, device_id_type=MESH)

        peers = 1 + len(more) + self.has_left.astype(jnp.int32) + self.has_right.astype(jnp.int32)
        pl.semaphore_wait(barrier, peers)

    def greet_all(self, barrier, more=()):
        for who in list(more) + [self.pair]:
            pl.semaphore_signal(barrier, inc=1, device_id=who, device_id_type=MESH)
        for i in range(self.n):
            @pl.when(i != self.at)
            def _(i=i):
                pl.semaphore_signal(barrier, inc=1, device_id={"dp": 2 * i + self.side}, device_id_type=MESH)
        pl.semaphore_wait(barrier, self.n + len(more))


def upper(rows):
    return max(16, rows // 32 * 16)


class Gather:
    def __init__(self, line, own, full, keep, send, recv):
        self.line, self.own, self.full, self.keep, self.send, self.recv = line, own, full, keep, send, recv
        self.rows = full.shape[2]
        self.cut = upper(self.rows)

    def copy(self, j, slab, way, src=None, rest=False):
        where = (self.line.right, self.line.left, self.line.pair)[way]
        dst = self.full.at[j, slab]
        if rest:
            dst = self.full.at[j, slab, pl.ds(self.cut, self.rows - self.cut)]
        return remote(dst if src is None else src, dst, self.send.at[j, way, slab], self.recv.at[j, slab], where)

    def shared(self, j, slab, owner):
        part = self.full.at[j, slab, pl.ds(0, self.cut)]
        return remote(part, part, self.send.at[j, 0, slab], self.recv.at[j, owner], self.line.near)

    def start(self, j):
        line = self.line
        pltpu.make_async_copy(self.own(j), self.full.at[j, line.me], self.keep.at[j]).start()

        @pl.when(line.has_right)
        def _():
            self.copy(j, line.me, 0, self.own(j)).start()

        @pl.when(line.has_left)
        def _():
            self.copy(j, line.me, 1, self.own(j)).start()

        self.copy(j, line.me, 2, self.own(j)).start()

    def relay(self, j, k):
        line = self.line

        def forward(slab, way, go_on, near):
            self.copy(j, slab, way).wait_recv()

            @pl.when(go_on)
            def _():
                self.copy(j, slab, way).start()

            if k > 1:
                self.copy(j, slab, 2).start()
            else:
                @pl.when(near)
                def _():
                    self.copy(j, slab, 2, rest=True).start()

                @pl.when(jnp.logical_not(near))
                def _():
                    self.copy(j, slab, 2).start()

        @pl.when(line.at >= k)
        def _():
            forward(line.me - 2 * k, 0, line.has_right, line.odd)

        @pl.when(line.at + k < line.n)
        def _():
            forward(line.me + 2 * k, 1, line.has_left, jnp.logical_not(line.odd))

        if k == 1:
            slab = line.me + 1 - 2 * line.side
            self.copy(j, slab, 2).wait_recv()
            self.shared(j, slab, line.near["dp"]).start()

    def near_slab(self):
        line = self.line
        return line.near["dp"] + 1 - 2 * line.side

    def arrive(self, j):
        line = self.line
        pltpu.make_async_copy(self.own(j), self.full.at[j, line.me], self.keep.at[j]).wait()
        self.copy(j, self.near_slab(), 2, rest=True).wait_recv()
        self.shared(j, self.near_slab(), line.me).wait_recv()
        for place in range(line.n):
            slab = 2 * place + 1 - line.side

            @pl.when((slab != self.near_slab()) & (place != line.at))
            def _(slab=slab):
                self.copy(j, slab, 2).wait_recv()

    def drain(self, j):
        line = self.line
        self.shared(j, line.me + 1 - 2 * line.side, line.near["dp"]).wait_send()
        for place in range(line.n):
            slab = 2 * place + line.side
            near = slab == line.near["dp"]

            @pl.when(near)
            def _(slab=slab):
                self.copy(j, slab, 2, rest=True).wait_send()

            @pl.when(jnp.logical_not(near))
            def _(slab=slab):
                self.copy(j, slab, 2).wait_send()

            @pl.when(line.has_right & (place <= line.at))
            def _(slab=slab):
                self.copy(j, slab, 0).wait_send()

            @pl.when(line.has_left & (place >= line.at))
            def _(slab=slab):
                self.copy(j, slab, 1).wait_send()


class Square:
    def __init__(self):
        me = lax.axis_index("tensor")
        self.me = me
        self.half = lax.rem(me, 2)
        self.mate = {"tensor": me + 1 - 2 * self.half}
        self.across = {"tensor": lax.rem(me + 2, 4)}

    def others(self):
        return [{"tensor": lax.rem(self.me + k, 4)} for k in (1, 2, 3)]


class Total:
    def __init__(self, square, part, got, far, other, send, recv):
        self.square, self.part, self.got, self.far, self.other = square, part, got, far, other
        self.send, self.recv = send, recv

    def first(self, c):
        sq = self.square
        return remote(
            self.part.at[2 * c + 1 - sq.half], self.got.at[c], self.send.at[0, c], self.recv.at[0, c], sq.mate
        )

    def second(self, c):
        sq = self.square
        return remote(self.part.at[2 * c + sq.half], self.far.at[c], self.send.at[1, c], self.recv.at[1, c], sq.across)

    def third(self, c):
        sq = self.square
        return remote(self.part.at[2 * c + sq.half], self.other.at[c], self.send.at[2, c], self.recv.at[2, c], sq.mate)

    def step(self, kind, c):
        slot = 2 * c + self.square.half
        if kind == 0:
            self.first(c).start()
        elif kind == 1:
            self.first(c).wait_recv()
            self.part[slot] = (self.part[slot].astype(F32) + self.got[c].astype(F32)).astype(BF16)
            self.second(c).start()
        elif kind == 2:
            self.second(c).wait()
            self.part[slot] = (self.part[slot].astype(F32) + self.far[c].astype(F32)).astype(BF16)
            self.third(c).start()
        else:
            self.third(c).wait_recv()
            self.first(c).wait_send()
            self.third(c).wait_send()
            self.part[2 * c + 1 - self.square.half] = self.other[c]


class Scatter:
    def __init__(self, line, part, out, near, far, send, recv):
        self.line, self.part, self.out, self.near, self.far = line, part, out, near, far
        self.send, self.recv = send, recv

    def order(self):
        n = self.line.n
        seq = []
        for i in range((n + 1) // 2):
            seq.append(i)
            if n - 1 - i != i:
                seq.append(n - 1 - i)
        return seq

    def cross(self, j, i):
        line = self.line
        return remote(
            self.part.at[j, 2 * i + 1 - line.side], self.near.at[j, i], self.send.at[0, j, i], self.recv.at[0, j, i], line.pair
        )

    def straight(self, j, i, source):
        line = self.line
        return remote(
            self.part.at[j, 2 * i + line.side], self.far.at[j, source], self.send.at[1, j, i], self.recv.at[1, j, source],
            {"dp": 2 * i + line.side},
        )

    def lead(self, j, m):
        self.cross(j, self.order()[m]).start()

    def start(self, j):
        for m in range(self.line.n):
            self.lead(j, m)

    def emit(self, j, turned, right, now=None):
        rows = self.part.shape[2]
        for m, i in enumerate(self.order()):
            value = mm(turned[2 * i * rows : 2 * (i + 1) * rows, :], right[...]).astype(BF16)
            self.part[j, 2 * i] = value[:rows]
            self.part[j, 2 * i + 1] = value[rows:]
            if now is None or m < now:
                self.lead(j, m)

    def product(self, dst, turned, right):
        rows = dst.shape[1]
        for i in range(self.line.n):
            value = mm(turned[2 * i * rows : 2 * (i + 1) * rows, :], right[...]).astype(BF16)
            dst[2 * i] = value[:rows]
            dst[2 * i + 1] = value[rows:]

    def fold(self, j, m):
        line = self.line
        i = self.order()[m]
        self.cross(j, i).wait_recv()
        slot = 2 * i + line.side
        self.part[j, slot] = (self.part[j, slot].astype(F32) + self.near[j, i].astype(F32)).astype(BF16)

        @pl.when(i != line.at)
        def _():
            self.straight(j, i, line.at).start()

    def finish(self, j):
        line = self.line
        out = self.out(j)
        out[...] = self.part[j, line.me].astype(out.dtype)
        for i in range(line.n):
            @pl.when(i != line.at)
            def _(i=i):
                self.straight(j, i, i).wait_recv()
                out[...] += self.far[j, i].astype(out.dtype)

    def drain(self, j):
        for i in range(self.line.n):
            self.cross(j, i).wait_send()

            @pl.when(i != self.line.at)
            def _(i=i):
                self.straight(j, i, self.line.at).wait_send()


def mm(left, right, dims=NN, precision=None):
    return lax.dot_general(left, right, dims, precision=precision, preferred_element_type=F32)


def sigmoid(v):
    return 0.5 * jnp.tanh(0.5 * v) + 0.5


def softplus(v):
    return jnp.maximum(v, 0.0) + jnp.log1p(jnp.exp(-jnp.abs(v)))


def split16(v):
    top = v.astype(BF16)
    return top, (v - top.astype(F32)).astype(BF16)


def expand(v, ind):
    top, rest = split16(v)
    return mm(top, ind) + mm(rest, ind)


def headsum(v, ind):
    return mm(v.astype(BF16), ind, NT)


def rowsum(v):
    return mm(jnp.ones((8, v.shape[1]), BF16), v.astype(BF16), NT)[0:1, :]


def iotas(n):
    return (
        lax.broadcasted_iota(jnp.int32, (n, n), 0),
        lax.broadcasted_iota(jnp.int32, (n, n), 1),
    )


def colsum(v):
    return jnp.sum(v, axis=0, keepdims=True)


def conv_pre(ext, par, n):
    total = par[4:5, :] + par[0:1, :] * ext[5 : 5 + n, :]
    for tap in range(1, 4):
        total = total + par[tap : tap + 1, :] * ext[5 + tap : 5 + tap + n, :]
    return total


def scan_prep(small, hp, ind, n):
    rows, cols = iotas(n)
    raw = small[:, 2 * STATE :] + hp[0:1, :]
    step = softplus(raw)
    rate = -jnp.exp(hp[1:2, :])
    lower = jnp.where(rows >= cols, 1.0, 0.0).astype(F32)
    cs = mm(lower, step * rate, precision=HIGH)
    tail = jnp.exp(cs[n - 1 : n, :] - cs)
    wide = mm(jnp.concatenate([step, jnp.exp(cs), tail], axis=0).astype(BF16), ind)
    return raw, step, rate, cs, wide[0:n], wide[n : 2 * n], wide[2 * n : 3 * n]


def block_of(slabs, at, rows):
    step = math.gcd(LANES, rows)
    pieces = []
    for k in range(LANES // step):
        row = at * LANES + k * step
        slab = row // rows
        pieces.append(slabs[slab, pl.ds(pl.multiple_of(row - slab * rows, step), step), :])
    return pieces[0] if len(pieces) == 1 else jnp.concatenate(pieces, axis=0)


def put_params(cp, sp, hp, ind, layer, params):
    conv, bias, norm, convs, biass, head = params
    width = cp.shape[1]
    row = lax.broadcasted_iota(jnp.int32, (LANES, width), 0)
    lane = lax.broadcasted_iota(jnp.int32, (LANES, width), 1)
    ind[...] = jnp.where(lane // HEAD == row, 1.0, 0.0).astype(BF16)
    hp[...] = head[layer]
    cp[0:4, :] = conv[layer]
    cp[4:5, :] = bias[layer : layer + 1, :]
    cp[5:6, :] = norm[layer : layer + 1, :]
    cp[6:8, :] = expand(hp[...], ind[...])[2:4, :]
    sp[0:4, :] = convs[layer]
    sp[4:5, :] = biass[layer : layer + 1, :]


def place_rows(dst, at, value):
    r = dst.shape[1]
    for g in range(0, value.shape[0], 16):
        dst[(at + g) // r, (at + g) % r : (at + g) % r + 16, :] = value[g : g + 16].astype(dst.dtype)


def pack_rows(size):
    return -(-PACK // (16 * size)) * 16


def put_pack(dst, me, turned, steps_low, sdel, dcp, dsp, dhp, dgain):
    model = turned.shape[0]
    quarter = model // 4
    w = sdel.shape[1]

    def empty(n):
        return jnp.zeros((n, w), F32)

    place_rows(dst, 0, mm(turned[pl.ds(pl.multiple_of(me * quarter, quarter), quarter), :], sdel[...]))
    place_rows(dst, quarter, jnp.concatenate([dsp, empty(8)], axis=0))
    grown = mm(turned[...], steps_low[...]).T[:16]
    at = quarter + 16
    for b in range(model // w):
        place_rows(dst, at, grown[:, b * w : (b + 1) * w])
        at += 16
    place_rows(dst, at, jnp.concatenate([dcp[:, :w], dcp[:, w : 2 * w]], axis=0))
    place_rows(dst, at + 16, jnp.concatenate([dcp[:, 2 * w :], jnp.concatenate([dhp, dhp], axis=1)], axis=0))
    rows = [dgain[:, b * w : (b + 1) * w] for b in range(model // w)]
    place_rows(dst, at + 32, jnp.concatenate(rows + [empty(16 - len(rows))], axis=0))
    assert at + 48 == PACK


class Smalls:
    def __init__(self, line, square, pack, near, away, own, full, wide, sems):
        send, recv, keep, gsend, grecv, self.xsend, self.xrecv = sems
        self.square, self.full, self.wide = square, full, wide
        self.sum = Scatter(line, pack, lambda j: own.at[j], near, away, send, recv)
        self.spread = Gather(line, lambda j: own.at[j], full, keep, gsend, grecv)

    def swap(self, j, k):
        sq = self.square
        slot = (sq.me, sq.me, lax.rem(sq.me + 2, 4))[k]
        who = (sq.across, sq.mate, sq.mate)[k]
        return remote(self.wide.at[j, slot], self.wide.at[j, slot], self.xsend.at[j, k], self.xrecv.at[j, k], who)

    def fold(self, j):
        for m in range(self.sum.line.n):
            self.sum.fold(j, m)

    def turn(self, j):
        self.sum.finish(j)
        self.spread.start(j)

    def cross(self, j):
        self.spread.arrive(j)
        flat = self.full[j].reshape(-1, self.full.shape[3])
        self.wide[j, self.square.me] = flat[: self.wide.shape[2]]
        self.swap(j, 0).start()
        self.swap(j, 1).start()

    def cross_on(self, j):
        self.swap(j, 0).wait_recv()
        self.swap(j, 2).start()

    def end(self, j):
        self.swap(j, 1).wait_recv()
        self.swap(j, 2).wait_recv()
        for k in range(3):
            self.swap(j, k).wait_send()
        self.sum.drain(j)
        self.spread.drain(j)


def smalls_scratch(size, w, layers):
    r, n = pack_rows(size), size // 2
    buffers = [
        pltpu.VMEM((layers, size, r, w), BF16),
        pltpu.VMEM((layers, n, r, w), BF16),
        pltpu.VMEM((layers, n, r, w), BF16),
        pltpu.VMEM((layers, r, w), BF16),
        pltpu.VMEM((layers, size, r, w), BF16),
        pltpu.VMEM((layers, 4, SPAN, w), BF16),
    ]
    sems = [
        pltpu.SemaphoreType.DMA((2, layers, n)),
        pltpu.SemaphoreType.DMA((2, layers, n)),
        pltpu.SemaphoreType.DMA((layers,)),
        pltpu.SemaphoreType.DMA((layers, 3, size)),
        pltpu.SemaphoreType.DMA((layers, size)),
        pltpu.SemaphoreType.DMA((layers, 3)),
        pltpu.SemaphoreType.DMA((layers, 3)),
    ]
    return buffers + sems


def forward_body(*refs, size, heads, per, steps, layer):
    refs = list(refs)

    def take(n):
        got = refs[:n]
        del refs[:n]
        return got

    mid = layer > 0
    (res_hbm,) = take(1)
    if mid:
        scaled_hbm, wout_hbm, sq_ref = take(3)
    state_hbm, step_hbm, in_hbm, out_hbm, gain_ref = take(5)
    params = take(6)
    if mid:
        new_hbm, sums_ref = take(2)
    normed_hbm, rnorm_ref, small_hbm, inner_hbm, gate_hbm, wt_hbm, full_hbm, ssd_ref, scaled_ref, sqs_ref, st_ref = take(11)
    if mid:
        scaled_in, wout, part, got, far, other, rows_got, facs, fresh, sends, recvs, rsend, rrecv = take(13)
    res, wstate, wt, slabs, normed, turned, small, inner, gate, ext, exts, state = take(12)
    cp_ref, sp_ref, hp_ref, ind_ref, keep, gsend, grecv, load, sems = take(9)
    assert not refs

    n = CHUNK
    tokens_n, model = res.shape
    width = inner.shape[1]
    top = 2 * width + 2 * STATE
    i = pl.program_id(0)
    line = Line(size)
    square = Square()
    job = Gather(line, lambda j: out_hbm.at[layer] if j == 2 else in_hbm.at[layer, 1 - j], slabs, keep, gsend, grecv)
    outgoing = [(turned, normed_hbm), (small, small_hbm), (inner, inner_hbm), (gate, gate_hbm)]
    outgoing += [(wt, wt_hbm), (slabs.at[2], full_hbm)]
    if mid:
        outgoing.append((fresh, new_hbm))

    def flush(k):
        return pltpu.make_async_copy(*outgoing[k], sems.at[k])


    @pl.when(i == 0)
    def _():
        pairs = [(res_hbm, res), (state_hbm.at[layer], wstate), (step_hbm.at[layer], wt.at[pl.ds(top, LANES), :])]
        if mid:
            pairs = [(scaled_hbm, scaled_in), (wout_hbm, wout)] + pairs
        loads = [pltpu.make_async_copy(src, dst, load.at[k]) for k, (src, dst) in enumerate(pairs)]
        for copy in loads:
            copy.start()
        line.greet(pltpu.get_barrier_semaphore(), square.others() if mid else ())
        job.start(0)
        put_params(cp_ref, sp_ref, hp_ref, ind_ref, layer, params)
        ticks = [functools.partial(job.relay, 0, k) for k in range(1, line.n)]
        ticks.append(functools.partial(job.start, 1))
        ticks += [functools.partial(job.relay, 1, k) for k in range(1, line.n)]
        ticks.append(functools.partial(job.start, 2))

        if mid:
            chunks = model // SLICE
            half = tokens_n // 2
            sums = Total(square, part, got, far, other, sends, recvs)
            copies = [
                remote(sq_ref, rows_got.at[square.me], rsend.at[k], rrecv.at[k], who)
                for k, who in enumerate(square.others())
            ]
            for copy in copies:
                copy.start()
            loads[0].wait()
            loads[1].wait()
            for c in range(chunks):
                value = mm(scaled_in[...], wout[c * SLICE : (c + 1) * SLICE, :], NT).astype(BF16)
                part[2 * c] = value[:half]
                part[2 * c + 1] = value[half:]
                sums.step(0, c)
                if c:
                    sums.step(1, c - 1)
            sums.step(1, chunks - 1)
            rows_got[square.me] = sq_ref[...]
            for copy in copies:
                copy.wait()
            total = (rows_got[0] + rows_got[1]) + (rows_got[2] + rows_got[3])
            sums_ref[...] = total
            factor = lax.rsqrt(total / INNER + EPS)
            for t in range(tokens_n // LANES):
                facs[t * LANES : (t + 1) * LANES, :] = jnp.broadcast_to(factor[t], (LANES, LANES)).T
            loads[2].wait()

            def use(c):
                for h in range(2):
                    where = slice(h * half, (h + 1) * half)
                    for s in range(SLICE // LANES):
                        lanes = slice(c * SLICE + s * LANES, c * SLICE + (s + 1) * LANES)
                        value = part[2 * c + h, :, s * LANES : (s + 1) * LANES].astype(F32)
                        fresh[where, lanes] = res[where, lanes].astype(F32) + facs[where, :] * value

            spread = max(1, -(-len(ticks) // chunks))
            for c in range(chunks):
                for tick in ticks[:spread]:
                    tick()
                ticks = ticks[spread:]
                sums.step(2, c)
                if c:
                    sums.step(3, c - 1)
                    use(c - 1)
            sums.step(3, chunks - 1)
            use(chunks - 1)
            flush(6).start()
        else:
            loads[0].wait()
        loads[-2].wait()
        loads[-1].wait()
        for b in range(2 * STATE // LANES):
            rows = slice(2 * width + b * LANES, 2 * width + (b + 1) * LANES)
            wt[rows, :] = wstate[:, b * LANES : (b + 1) * LANES].T

        def norm(t, _):
            rows = pl.ds(pl.multiple_of(t * TILE, TILE), TILE)
            value = (fresh if mid else res)[rows, :].astype(F32)
            scale = lax.rsqrt(jnp.sum(value * value, axis=1, keepdims=True) / model + EPS)
            low = (value * scale * gain_ref[layer : layer + 1, :]).astype(BF16)
            rnorm_ref[rows, :] = scale
            normed[rows, :] = low
            turned[:, rows] = low.T
            small[rows, : 2 * STATE] = mm(low, wstate[...])
            small[rows, 2 * STATE :] = mm(low, wt[top:, :], NT)
            return 0

        lax.fori_loop(0, tokens_n // TILE, norm, 0)
        flush(0).start()
        flush(1).start()
        for tick in ticks:
            tick()

        def project(j, dst):
            weight = slabs[j].reshape(model, width)

            def tile(t, _):
                rows = pl.ds(pl.multiple_of(t * TILE, TILE), TILE)
                dst[rows, :] = mm(normed[rows, :], weight)
                return 0

            lax.fori_loop(0, tokens_n // TILE, tile, 0)

        for j, dst in ((0, inner), (1, gate)):
            job.arrive(j)
            project(j, dst)
            flush(2 + j).start()

    for k in range(1, line.n):
        @pl.when(i == 1 + (k - 1) * steps // line.n)
        def _(k=k):
            job.relay(2, k)

    @pl.when(i > 0)
    def _():
        at = i - 1
        where = pl.ds(pl.multiple_of(at * n, n), n)

        @pl.when(lax.rem(at, per) == 0)
        def _():
            ext[0:8, :] = jnp.zeros((8, width), F32)
            exts[0:8, :] = jnp.zeros((8, 2 * STATE), F32)
            state[...] = jnp.zeros_like(state)

        rows, cols = iotas(n)
        ind = ind_ref[...]
        ext[8 : 8 + n, :] = inner[where, :]
        pre = conv_pre(ext, cp_ref, n)
        x = pre * sigmoid(pre)
        ext[0:8, :] = ext[n : n + 8, :]
        mini = small[where, :]
        exts[8 : 8 + n, :] = mini[:, : 2 * STATE]
        pres = conv_pre(exts, sp_ref, n)
        bc = (pres * sigmoid(pres)).astype(BF16)
        exts[0:8, :] = exts[n : n + 8, :]
        key, query = bc[:, :STATE], bc[:, STATE:]

        _, step, rate, cs, wide_step, wide_cs, wide_tail = scan_prep(mini, hp_ref, ind, n)
        cs2 = cs * LOG2E
        cs2t = cs2.T
        xs = x * wide_step
        lane = lax.broadcasted_iota(jnp.int32, (1, width), 1)
        half = jnp.where(lax.rem(lane, 2 * HEAD) < HEAD, 1.0, 0.0).astype(BF16)
        xsb = xs.astype(BF16)
        xs0 = xsb * half
        xs1 = xsb - xs0
        before = state[...]
        low = before.astype(BF16)
        st_ref[0] = low
        carried = mm(query, low) * wide_cs
        xw = (xs * wide_tail).astype(BF16)
        state[...] = before * wide_cs[n - 1 : n, :] + mm(key, xw, TN)
        scores = jnp.where(rows >= cols, mm(query, key, NT), 0.0)
        for pair in range(heads // 2):
            lanes = slice(pair * 2 * HEAD, (pair + 1) * 2 * HEAD)
            mats = []
            for h in (2 * pair, 2 * pair + 1):
                dec = jnp.exp2(jnp.minimum(cs2[:, h : h + 1] - cs2t[h : h + 1, :], 0.0))
                mats.append((scores * dec).astype(BF16))
            local = mm(
                jnp.concatenate(mats, axis=1),
                jnp.concatenate([xs0[:, lanes], xs1[:, lanes]], axis=0),
            )
            ssd_ref[:, lanes] = local + carried[:, lanes] + cp_ref[6:7, lanes] * x[:, lanes]
        gates = gate[where, :]
        gated = ssd_ref[...] * (gates * sigmoid(gates))
        sqs_ref[0] = rowsum(gated * gated)
        scaled_ref[...] = (gated * cp_ref[5:6, :]).astype(BF16)

        span = model // LANES
        share = -(-2 * span // steps)
        for k in range(share):
            b = at * share + k

            @pl.when(b < 2 * span)
            def _(b=b):
                j, col = b // span, lax.rem(b, span)
                slab_rows = slabs.shape[2]
                weight = slabs.at[j]
                piece = block_of(weight, col, slab_rows)
                wt[pl.ds(pl.multiple_of(j * width, width), width), pl.ds(pl.multiple_of(col * LANES, LANES), LANES)] = piece.T

    @pl.when(i == steps)
    def _():
        flush(4).start()
        job.arrive(2)
        flush(5).start()
        for j in range(3):
            job.drain(j)
        for k in range(len(outgoing)):
            flush(k).wait()


def forward(res, stateproj, steps_w, inproj, outt, gain, params, heads, size, layer, out=None):
    tokens_n, model = res.shape
    _, _, rows, width = inproj.shape
    top = 2 * width + 2 * STATE + LANES
    steps = tokens_n // CHUNK
    mid = out is not None
    hbm = pl.BlockSpec(memory_space=pl.ANY)
    chunks = model // SLICE

    def whole(a):
        return pl.BlockSpec(a.shape, lambda i: (0,) * len(a.shape))

    def row(w):
        return pl.BlockSpec((CHUNK, w), lambda i: (jnp.maximum(i - 1, 0), 0))

    args, in_specs, out_specs, out_shape, scratch = [res], [hbm], [], [], []
    if mid:
        args += list(out)
        in_specs += [hbm, hbm, whole(out[2])]
        out_specs += [hbm, whole(out[2])]
        out_shape += [jax.ShapeDtypeStruct(res.shape, F32), jax.ShapeDtypeStruct(out[2].shape, F32)]
        chunk = pltpu.VMEM((chunks, tokens_n // 2, SLICE), BF16)
        scratch += [
            pltpu.VMEM(out[0].shape, BF16),
            pltpu.VMEM(out[1].shape, BF16),
            pltpu.VMEM((2 * chunks, tokens_n // 2, SLICE), BF16),
            chunk, chunk, chunk,
            pltpu.VMEM((4,) + out[2].shape, F32),
            pltpu.VMEM((tokens_n, LANES), F32),
            pltpu.VMEM(res.shape, F32),
            pltpu.SemaphoreType.DMA((3, chunks)),
            pltpu.SemaphoreType.DMA((3, chunks)),
            pltpu.SemaphoreType.DMA((3,)),
            pltpu.SemaphoreType.DMA((3,)),
        ]
    args += [stateproj, steps_w, inproj, outt, gain, *params]
    in_specs += [hbm, hbm, hbm, hbm, whole(gain)] + [whole(v) for v in params]
    out_specs += [
        hbm, pl.BlockSpec((tokens_n, 1), lambda i: (0, 0)), hbm, hbm, hbm, hbm, hbm,
        row(width), row(width),
        pl.BlockSpec((1, 1, CHUNK), lambda i: (jnp.maximum(i - 1, 0), 0, 0)),
        pl.BlockSpec((1, STATE, width), lambda i: (jnp.maximum(i - 1, 0), 0, 0)),
    ]
    out_shape += [
        jax.ShapeDtypeStruct((model, tokens_n), BF16),
        jax.ShapeDtypeStruct((tokens_n, 1), F32),
        jax.ShapeDtypeStruct((tokens_n, 2 * STATE + LANES), F32),
        jax.ShapeDtypeStruct((tokens_n, width), F32),
        jax.ShapeDtypeStruct((tokens_n, width), F32),
        jax.ShapeDtypeStruct((top, model), BF16),
        jax.ShapeDtypeStruct((size, rows, width), BF16),
        jax.ShapeDtypeStruct((tokens_n, width), F32),
        jax.ShapeDtypeStruct((tokens_n, width), BF16),
        jax.ShapeDtypeStruct((steps, 1, CHUNK), F32),
        jax.ShapeDtypeStruct((steps, STATE, width), BF16),
    ]
    scratch += [
        pltpu.VMEM(res.shape, res.dtype),
        pltpu.VMEM((model, 2 * STATE), BF16),
        pltpu.VMEM((top, model), BF16),
        pltpu.VMEM((3, size, rows, width), BF16),
        pltpu.VMEM((tokens_n, model), BF16),
        pltpu.VMEM((model, tokens_n), BF16),
        pltpu.VMEM((tokens_n, 2 * STATE + LANES), F32),
        pltpu.VMEM((tokens_n, width), F32),
        pltpu.VMEM((tokens_n, width), F32),
        pltpu.VMEM((CHUNK + 8, width), F32),
        pltpu.VMEM((CHUNK + 8, 2 * STATE), F32),
        pltpu.VMEM((STATE, width), F32),
        pltpu.VMEM((8, width), F32),
        pltpu.VMEM((8, 2 * STATE), F32),
        pltpu.VMEM((8, LANES), F32),
        pltpu.VMEM((LANES, width), BF16),
        pltpu.SemaphoreType.DMA((3,)),
        pltpu.SemaphoreType.DMA((3, 3, size)),
        pltpu.SemaphoreType.DMA((3, size)),
        pltpu.SemaphoreType.DMA((5,)),
        pltpu.SemaphoreType.DMA((7,)),
    ]
    return pl.pallas_call(
        functools.partial(forward_body, size=size, heads=heads, per=LEN // CHUNK, steps=steps, layer=layer),
        grid=(steps + 1,),
        in_specs=in_specs,
        out_specs=out_specs,
        out_shape=out_shape,
        scratch_shapes=scratch,
        compiler_params=pltpu.CompilerParams(
            collective_id=min(layer, 1), has_side_effects=True, vmem_limit_bytes=VMEM_LIMIT
        ),
        name="forward",
    )(*args)


def back_body(*refs, heads, per, size, steps, layer, last):
    refs = list(refs)

    def take(n):
        got = refs[:n]
        del refs[:n]
        return got

    up_ref, sq_ref, gate_ref, ssd_ref, inner_ref, iprev_ref, small_ref, sprev_ref, st_ref, res_ref, rn_ref = take(11)
    gain_ref = take(1)[0]
    params = take(6)
    wout_hbm, scaled_hbm, wt_hbm, normed_hbm = take(4)
    if not last:
        next_normed, next_steps, next_sdel, next_inner, next_dcp, next_dsp, next_dhp, next_dgain = take(8)
    new_ref, grad_hbm = take(2)
    if last:
        held_hbm, sdsum_ref, steplow_ref, dcp_ref, dsp_ref, dhp_ref, dgain_ref, mixed_ref = take(8)
    else:
        full_hbm, wide_hbm = take(2)
    ext, exts, cde, cdes, dstate, rq, cp_ref, sp_ref, hp_ref, ind_ref = take(10)
    wout, scaled, wt, turned, dy, glow, ilow, frow, srow, sgot = take(10)
    part, near, away, tpart, got, far, other = take(7)
    load, rsend, rrecv, ssend, srecv, sends, recvs, gsem = take(8)
    if last:
        held, fgot, opart, ogot, ofar, oother, fsend, frecv, osends, orecvs = take(10)
    else:
        dcp_ref, dsp_ref, dhp_ref, dgain_ref = take(4)
        sd_all = scaled.at[:, pl.ds(0, 2 * STATE)]
        step_all = scaled.at[:, pl.ds(2 * STATE, LANES)]
        buffers = take(6)
        sems = take(7)
    assert not refs

    n = CHUNK
    model = up_ref.shape[1]
    i = pl.program_id(0)
    begin_gate = steps
    begin_scan = begin_gate + steps
    begin_norm = begin_scan + steps
    end = begin_norm + steps - 1
    line = Line(size)
    square = Square()
    rows_own = part.shape[2]
    count = part.shape[0]
    job = Scatter(line, part, lambda j: dy.at[pl.ds(j * rows_own, rows_own), :], near, away, ssend, srecv)
    sums = Total(square, tpart, got, far, other, sends, recvs)
    if last:
        outs = Total(square, opart, ogot, ofar, oother, osends, orecvs)
        half = steps * n // 2
        slices = model // SLICE
    else:
        minis = Smalls(line, square, *buffers, sems)
    moves = [(wout_hbm, wout), (scaled_hbm, scaled), (wt_hbm, wt), (normed_hbm, turned)]
    if last:
        moves.append((held, held_hbm))
    else:
        tokens_n = steps * n
        spots = (wt.at[pl.ds(0, model), pl.ds(0, tokens_n)],)
        spots += tuple(
            wt.at[pl.ds(0, tokens_n), pl.ds(tokens_n + at, w)] for at, w in ((0, LANES), (LANES, 2 * STATE))
        )
        moves += [(next_normed, spots[0]), (next_steps, spots[1]), (next_sdel, spots[2]), (next_inner, part.at[3])]

    def move(k):
        return pltpu.make_async_copy(*moves[k], load.at[k])

    places = line.n

    def spaced(begin, stop, m):
        return begin + m * (stop - begin) // places

    middle = begin_scan + steps // 2
    if last:
        folds = [(spaced(begin_scan, middle, m), 0, m) for m in range(places)]
        folds += [(spaced(middle, begin_norm, m) + 1, 1, m) for m in range(places)]
    else:
        folds = [(spaced(begin_gate - 1, begin_scan + 3, m), 3, m) for m in range(places)]
        folds += [(spaced(begin_scan + 2, middle + 3, m), 0, m) for m in range(places)]
        folds += [(spaced(begin_norm - 1, end - 1, m), 1, m) for m in range(places)]

    def column(row):
        return jnp.broadcast_to(row, (n, n)).T[:, 0:1]

    @pl.when(i == 0)
    def _():
        for k in range(3) if last else (7, 4, 5, 6, 0, 1):
            move(k).start()
        put_params(cp_ref, sp_ref, hp_ref, ind_ref, layer, params)
        rq[...] = jnp.zeros_like(rq)
        line.greet_all(pltpu.get_barrier_semaphore(), square.others())
        if last:
            rows = [
                remote(sq_ref, fgot.at[square.me], fsend.at[k], frecv.at[k], who)
                for k, who in enumerate(square.others())
            ]
            for copy in rows:
                copy.start()
            fgot[square.me] = sq_ref[...]
            move(0).wait()
            move(1).wait()
            for c in range(slices):
                value = mm(scaled[...], wout[c * SLICE : (c + 1) * SLICE, :], NT).astype(BF16)
                opart[2 * c] = value[:half]
                opart[2 * c + 1] = value[half:]
                outs.step(0, c)
            outs.step(1, 0)
            for copy in rows:
                copy.wait()
            total = (fgot[0] + fgot[1]) + (fgot[2] + fgot[3])
        else:
            move(7).wait()
            for m in range(places // 2):
                job.lead(3, m)
            for k in (4, 5, 6):
                move(k).wait()
            put_pack(
                buffers[0].at[1], square.me, *spots, next_dcp[...], next_dsp[...], next_dhp[...], next_dgain[...]
            )
            minis.sum.start(1)
            move(2).start()
            for m in range(places // 2, places):
                job.lead(3, m)
            total = sq_ref[...]
            move(0).wait()
            move(1).wait()
        dcp_ref[...] = jnp.zeros_like(dcp_ref)
        dsp_ref[...] = jnp.zeros_like(dsp_ref)
        dhp_ref[...] = jnp.zeros_like(dhp_ref)
        dgain_ref[...] = jnp.zeros_like(dgain_ref)
        frow[...] = lax.rsqrt(total / INNER + EPS)

    ind = ind_ref[...]
    for at, j, m in folds:
        @pl.when(i == at)
        def _(j=j, m=m):
            job.fold(j, m)

    @pl.when(i < begin_gate)
    def _():
        rows = pl.ds(pl.multiple_of(i * n, n), n)
        low = (column(frow[i]) * up_ref[...].astype(F32)).astype(BF16)
        turned[:, rows] = low.T
        sd = mm(low, wout[...])
        dy[rows, :] = sd
        piece = scaled[rows, :]
        srow[i] = rowsum(piece.astype(F32) * sd)

    @pl.when(i == begin_gate - 1)
    def _():
        copies = [
            remote(srow, sgot.at[square.me], rsend.at[k], rrecv.at[k], who) for k, who in enumerate(square.others())
        ]
        for copy in copies:
            copy.start()
        job.emit(0, turned, scaled)
        move(3).start()
        sgot[square.me] = srow[...]
        for copy in copies:
            copy.wait()
        srow[...] = (sgot[0] + sgot[1]) + (sgot[2] + sgot[3])

    if last:
        @pl.when(i == steps // 2)
        def _():
            outs.step(1, 1)

        @pl.when((i >= begin_gate) & (i < begin_gate + slices - 2))
        def _():
            outs.step(1, i - begin_gate + 2)

    @pl.when((i >= begin_gate) & (i < begin_scan))
    def _():
        c = i - begin_gate
        rows = pl.ds(pl.multiple_of(c * n, n), n)
        coef = column(frow[c] * frow[c] * srow[c]) / INNER
        gate = gate_ref[...]
        gsig = sigmoid(gate)
        gact = gate * gsig
        ssd = ssd_ref[...]
        sd = dy[rows, :]
        gated = ssd * gact
        gd = cp_ref[5:6, :] * sd - coef * gated
        dcp_ref[5:6, :] += colsum(gated * sd)
        dy[rows, :] = gd * gact
        glow[rows, :] = (gd * ssd * (gsig + gact * (1.0 - gsig))).astype(BF16)

    @pl.when(i == begin_scan - 1)
    def _():
        move(3).wait()
        job.emit(1, turned, glow)
        move(2).wait()

    @pl.when((i >= begin_scan) & (i < begin_norm))
    def _():
        q = i - begin_scan
        chunk = steps - 1 - q
        where = pl.ds(pl.multiple_of(chunk * n, n), n)

        @pl.when(lax.rem(chunk, per) == per - 1)
        def _():
            cde[n : n + 8, :] = jnp.zeros((8, cde.shape[1]), F32)
            cdes[n : n + 8, :] = jnp.zeros((8, cdes.shape[1]), F32)
            dstate[...] = jnp.zeros_like(dstate)

        keep = jnp.where(lax.rem(chunk, per) == 0, 0.0, 1.0).astype(F32)
        rows, cols = iotas(n)
        ext[0:8, :] = iprev_ref[...] * keep
        ext[8 : 8 + n, :] = inner_ref[...]
        exts[0:8, :] = sprev_ref[:, : 2 * STATE] * keep
        exts[8 : 8 + n, :] = small_ref[:, : 2 * STATE]
        pre = conv_pre(ext, cp_ref, n)
        sig = sigmoid(pre)
        x = pre * sig
        slope = sig + x * (1.0 - sig)
        pres = conv_pre(exts, sp_ref, n)
        sigs = sigmoid(pres)
        acts = pres * sigs
        slopes = sigs + acts * (1.0 - sigs)
        bc = acts.astype(BF16)
        key, query = bc[:, :STATE], bc[:, STATE:]
        dyc = dy[where, :]

        raw, step, rate, cs, wide_step, wide_cs, wide_tail = scan_prep(small_ref, hp_ref, ind, n)
        cs2 = cs * LOG2E
        cs2t = cs2.T
        xs = x * wide_step
        xsb = xs.astype(BF16)
        dyb = dyc.astype(BF16)
        lane = lax.broadcasted_iota(jnp.int32, (1, xs.shape[1]), 1)
        half = jnp.where(lax.rem(lane, 2 * HEAD) < HEAD, 1.0, 0.0).astype(BF16)
        dy0 = dyb * half
        dy1 = dyb - dy0
        low = st_ref[0]
        dst = dstate[...]
        dlow = dst.astype(BF16)
        dye = dyc * wide_cs
        dyeb = dye.astype(BF16)
        up = headsum(dye * mm(query, low), ind)
        dxs_state = wide_tail * mm(key, dlow)
        down = headsum(xs * dxs_state, ind)
        qdel = mm(dyeb, low, NT)
        kdel = mm((xs * wide_tail).astype(BF16), dlow, NT)
        through = headsum(jnp.broadcast_to(colsum(low.astype(F32) * dst), (8, dst.shape[1])), ind)[0:1, :]
        through = through * jnp.exp(cs[n - 1 : n, :])
        dstate[...] = dst * wide_cs[n - 1 : n, :] + mm(query, dyeb, TN)

        scores = jnp.where(rows <= cols, mm(key, query, NT), 0.0)
        dscores = jnp.zeros((n, n), F32)
        colq = jnp.zeros((n, LANES), F32)
        lane = lax.broadcasted_iota(jnp.int32, (n, LANES), 1)
        dxs = []
        for pair in range(heads // 2):
            lanes = slice(pair * 2 * HEAD, (pair + 1) * 2 * HEAD)
            stacked = jnp.concatenate([dy0[:, lanes], dy1[:, lanes]], axis=0)
            both = mm(xsb[:, lanes], stacked, NT)
            mats = []
            for which, h in enumerate((2 * pair, 2 * pair + 1)):
                dec = jnp.exp2(jnp.minimum(cs2t[h : h + 1, :] - cs2[:, h : h + 1], 0.0))
                mats.append((scores * dec).astype(BF16))
                term = dec * both[:, which * n : (which + 1) * n]
                dscores = dscores + term
                quad = scores * term
                rq[h : h + 1, :] = colsum(quad)
                colq = jnp.where(lane == h, jnp.sum(quad, axis=1, keepdims=True), colq)
            dxs.append(mm(jnp.concatenate(mats, axis=1), stacked))
        dxs = jnp.concatenate(dxs, axis=1) + dxs_state
        dscores = jnp.where(rows <= cols, dscores, 0.0).astype(BF16)
        kdel = kdel + mm(dscores, query)
        qdel = qdel + mm(dscores, key, TN)

        upper = jnp.where(rows <= cols, 1.0, 0.0).astype(F32)
        strict = jnp.where(rows > cols, 1.0, 0.0).astype(F32)
        da = mm(upper, rq[...].T - colq + up, precision=HIGH) + mm(strict, down, precision=HIGH) + through
        grown = headsum(x * dxs, ind) + rate * da
        step_pre = grown * sigmoid(raw)
        steplow = step_pre.astype(BF16)
        if last:
            steplow_ref[...] = steplow
        else:
            step_all[where, :] = steplow
        dhp_ref[0:1, :] += colsum(step_pre)
        dhp_ref[1:2, :] += rate * colsum(step * da)
        dcp_ref[6:7, :] += colsum(dyc * x)

        cd = (dxs * wide_step + cp_ref[6:7, :] * dyc) * slope
        cde[0:n, :] = cd
        center = ext[8 : 8 + n, :]
        total = cp_ref[3:4, :] * cd
        dcp_ref[3:4, :] += colsum(cd * center)
        for tap in range(3):
            shifted = cde[3 - tap : 3 - tap + n, :]
            total = total + cp_ref[tap : tap + 1, :] * shifted
            dcp_ref[tap : tap + 1, :] += colsum(shifted * center)
        inner_low = total.astype(BF16)
        ilow[where, :] = inner_low
        dcp_ref[4:5, :] += colsum(cd)
        cde[n : n + 8, :] = cde[0:8, :]

        cds = jnp.concatenate([kdel, qdel], axis=1) * slopes
        cdes[0:n, :] = cds
        center = exts[8 : 8 + n, :]
        total = sp_ref[3:4, :] * cds
        dsp_ref[3:4, :] += colsum(cds * center)
        for tap in range(3):
            shifted = cdes[3 - tap : 3 - tap + n, :]
            total = total + sp_ref[tap : tap + 1, :] * shifted
            dsp_ref[tap : tap + 1, :] += colsum(shifted * center)
        sdel = total.astype(BF16)
        dsp_ref[4:5, :] += colsum(cds)
        cdes[n : n + 8, :] = cdes[0:8, :]

        lows = jnp.concatenate([inner_low, glow[where, :], sdel, steplow], axis=1)
        value = mm(lows, wt[...]).astype(BF16)
        tpart[2 * q, :, :model] = value[: n // 2]
        tpart[2 * q + 1, :, :model] = value[n // 2 :]
        tpart[2 * q, :, model:] = sdel[: n // 2]
        tpart[2 * q + 1, :, model:] = sdel[n // 2 :]
        sums.step(0, q)

    @pl.when((i > begin_scan) & (i <= begin_norm))
    def _():
        sums.step(1, i - begin_scan - 1)

    @pl.when((i >= begin_scan + 5) & (i < begin_norm + 5))
    def _():
        sums.step(2, i - begin_scan - 5)

    @pl.when((i >= begin_scan + 6) & (i < begin_norm + 6))
    def _():
        sums.step(3, i - begin_scan - 6)

    if last:
        @pl.when((i > begin_scan) & (i <= begin_scan + slices))
        def _():
            outs.step(2, i - begin_scan - 1)

        @pl.when((i > begin_scan + 1) & (i <= begin_scan + slices + 1))
        def _():
            outs.step(3, i - begin_scan - 2)

    @pl.when(i == begin_norm - 1)
    def _():
        dhp_ref[2:3, :] = headsum(jnp.broadcast_to(dcp_ref[6:7, :], (8, dcp_ref.shape[1])), ind)[0:1, :]
        if last:
            job.product(held, turned, ilow)
            move(4).start()
        else:
            job.emit(2, turned, ilow, places // 2)

    if not last:
        @pl.when(i == begin_gate + 4)
        def _():
            minis.fold(1)

        @pl.when(i == begin_gate + 6)
        def _():
            minis.turn(1)

        for k in range(1, line.n):
            @pl.when(i == begin_scan + (k - 1) * 6 // line.n)
            def _(k=k):
                minis.spread.relay(1, k)

        @pl.when(i == begin_norm)
        def _():
            minis.cross(1)

        @pl.when(i == begin_norm + 4)
        def _():
            minis.cross_on(1)

    @pl.when(i >= begin_norm)
    def _():
        r = i - begin_norm
        chunk = steps - 1 - r
        if last:
            fac = column(frow[chunk])
            side = chunk // (steps // 2)
            base = (chunk - side * (steps // 2)) * n
        for h in range(2):
            rows = slice(h * (n // 2), (h + 1) * (n // 2))
            back = tpart[2 * r + h, :, :model].astype(F32)
            sdel = tpart[2 * r + h, :, model:]
            if last:
                sdsum_ref[rows, :] = sdel
            else:
                sd_all[pl.ds(pl.multiple_of(chunk * n + h * (n // 2), n // 2), n // 2), :] = sdel
            res = res_ref[rows, :].astype(F32)
            rn = rn_ref[rows, :]
            dgain_ref[...] += colsum(back * res * rn)
            gained = back * gain_ref[layer : layer + 1, :]
            mean = jnp.sum(gained * res, axis=1, keepdims=True) / model
            new_ref[rows, :] = up_ref[rows, :].astype(F32) + rn * gained - (rn * rn * rn * mean) * res
            if last:
                where = pl.ds(pl.multiple_of(base + h * (n // 2), n // 2), n // 2)
                for c in range(slices):
                    span = slice(c * SLICE, (c + 1) * SLICE)
                    summed = opart[2 * c + side, where, :].astype(F32)
                    mixed_ref[rows, span] = (res[:, span] + fac[rows, :] * summed).astype(BF16)

    @pl.when(i == end)
    def _():
        def finish(j):
            job.finish(j)
            pltpu.make_async_copy(dy.at[pl.ds(j * rows_own, rows_own), :], grad_hbm.at[j], gsem.at[j]).start()

        if not last:
            put_pack(
                buffers[0].at[0], square.me, turned, step_all, sd_all, dcp_ref[...], dsp_ref[...], dhp_ref[...], dgain_ref[...]
            )
            minis.sum.start(0)
            for m in range(places // 2, places):
                job.lead(2, m)
            for m in range(places // 2):
                job.fold(2, m)
            finish(3)
        finish(0)
        finish(1)
        if not last:
            minis.fold(0)
            minis.turn(0)
            for k in range(1, line.n):
                minis.spread.relay(0, k)
            for m in range(places // 2, places):
                job.fold(2, m)
            minis.cross(0)
            finish(2)
            minis.cross_on(0)
            minis.end(1)
            minis.end(0)
            tails = [
                pltpu.make_async_copy(src, dst, load.at[k])
                for k, (src, dst) in enumerate(((minis.full, full_hbm), (minis.wide, wide_hbm)))
            ]
            for copy in tails:
                copy.start()
        for j in range(count):
            job.drain(j)
            pltpu.make_async_copy(dy.at[pl.ds(j * rows_own, rows_own), :], grad_hbm.at[j], gsem.at[j]).wait()
        if last:
            move(4).wait()
        else:
            for copy in tails:
                copy.wait()


def back(up, sq, gate_pre, ssd, inner_raw, small, states, res, rnorm, gain, params,
         wout, scaled, wt, normed, heads, size, layer, after=None):
    tokens_n, width = inner_raw.shape
    model = up.shape[1]
    last = after is None
    steps = tokens_n // CHUNK
    begin_scan = 2 * steps
    begin_norm = begin_scan + steps
    rows = model // size
    n = size // 2
    hbm = pl.BlockSpec(memory_space=pl.ANY)
    top = steps - 1

    def norm_at(i):
        return jnp.where(i < begin_norm, top, top - (i - begin_norm))

    def scan_at(i):
        return jnp.clip(top - (i - begin_scan), 0, top)

    def first(w):
        return pl.BlockSpec((CHUNK, w), lambda i: (jnp.where(i < steps, i, norm_at(i)), 0))

    def second(w):
        return pl.BlockSpec((CHUNK, w), lambda i: (jnp.clip(i - steps, 0, top), 0))

    def scan(w):
        return pl.BlockSpec((CHUNK, w), lambda i: (scan_at(i), 0))

    def prev(w):
        return pl.BlockSpec((8, w), lambda i: (jnp.maximum(scan_at(i) * (CHUNK // 8) - 1, 0), 0))

    def norm(w):
        return pl.BlockSpec((CHUNK, w), lambda i: (norm_at(i), 0))

    def whole(a):
        return pl.BlockSpec(a.shape, lambda i: (0,) * len(a.shape))

    extra = model + 2 * STATE
    quarter = pltpu.VMEM((steps, CHUNK // 2, extra), BF16)
    count = 2 if last else 4
    pieces = pltpu.VMEM((count, n, rows, width), BF16)
    args = [up, sq, gate_pre, ssd, inner_raw, inner_raw, small, small, states, res, rnorm, gain, *params,
            wout, scaled, wt, normed]
    in_specs = [
        first(model), whole(sq), second(width), second(width),
        scan(width), prev(width), scan(small.shape[1]), prev(small.shape[1]),
        pl.BlockSpec((1, STATE, width), lambda i: (scan_at(i), 0, 0)),
        norm(model), norm(1), whole(gain),
    ] + [whole(a) for a in params] + [hbm] * 4
    out_specs = [norm(model), hbm]
    out_shape = [jax.ShapeDtypeStruct((tokens_n, model), F32), jax.ShapeDtypeStruct((count, rows, width), F32)]
    totals = [(8, width), (8, 2 * STATE), (8, LANES), (1, model)]
    scratch = [
        pltpu.VMEM((CHUNK + 8, width), F32),
        pltpu.VMEM((CHUNK + 8, 2 * STATE), F32),
        pltpu.VMEM((CHUNK + 8, width), F32),
        pltpu.VMEM((CHUNK + 8, 2 * STATE), F32),
        pltpu.VMEM((STATE, width), F32),
        pltpu.VMEM((LANES, CHUNK), F32),
        pltpu.VMEM((8, width), F32),
        pltpu.VMEM((8, 2 * STATE), F32),
        pltpu.VMEM((8, LANES), F32),
        pltpu.VMEM((LANES, width), BF16),
        pltpu.VMEM(wout.shape, BF16),
        pltpu.VMEM(scaled.shape, BF16),
        pltpu.VMEM(wt.shape, BF16),
        pltpu.VMEM(normed.shape, BF16),
        pltpu.VMEM((tokens_n, width), F32),
        pltpu.VMEM((tokens_n, width), BF16),
        pltpu.VMEM((tokens_n, width), BF16),
        pltpu.VMEM((steps, 1, CHUNK), F32),
        pltpu.VMEM((steps, 1, CHUNK), F32),
        pltpu.VMEM((4, steps, 1, CHUNK), F32),
        pltpu.VMEM((count, size, rows, width), BF16), pieces, pieces,
        pltpu.VMEM((2 * steps, CHUNK // 2, extra), BF16), quarter, quarter, quarter,
        pltpu.SemaphoreType.DMA((8,)),
        pltpu.SemaphoreType.DMA((3,)),
        pltpu.SemaphoreType.DMA((3,)),
        pltpu.SemaphoreType.DMA((2, count, n)),
        pltpu.SemaphoreType.DMA((2, count, n)),
        pltpu.SemaphoreType.DMA((3, steps)),
        pltpu.SemaphoreType.DMA((3, steps)),
        pltpu.SemaphoreType.DMA((count,)),
    ]
    if last:
        out_specs += [hbm, norm(2 * STATE), scan(LANES)]
        out_specs += [pl.BlockSpec(v, lambda i: (0, 0)) for v in totals] + [norm(model)]
        out_shape += [
            jax.ShapeDtypeStruct((size, rows, width), BF16),
            jax.ShapeDtypeStruct((tokens_n, 2 * STATE), BF16),
            jax.ShapeDtypeStruct((tokens_n, LANES), BF16),
        ]
        out_shape += [jax.ShapeDtypeStruct(v, F32) for v in totals]
        out_shape.append(jax.ShapeDtypeStruct((tokens_n, model), BF16))
        slices = model // SLICE
        chunk = pltpu.VMEM((slices, tokens_n // 2, SLICE), BF16)
        scratch += [
            pltpu.VMEM((size, rows, width), BF16),
            pltpu.VMEM((4, steps, 1, CHUNK), F32),
            pltpu.VMEM((2 * slices, tokens_n // 2, SLICE), BF16), chunk, chunk, chunk,
            pltpu.SemaphoreType.DMA((3,)),
            pltpu.SemaphoreType.DMA((3,)),
            pltpu.SemaphoreType.DMA((3, slices)),
            pltpu.SemaphoreType.DMA((3, slices)),
        ]
    else:
        w = 2 * STATE
        r = pack_rows(size)
        args += list(after)
        in_specs += [hbm] * 4 + [whole(v) for v in after[4:]]
        out_specs += [hbm, hbm]
        out_shape += [
            jax.ShapeDtypeStruct((2, size, r, w), BF16),
            jax.ShapeDtypeStruct((2, 4, SPAN, w), BF16),
        ]
        scratch += [pltpu.VMEM(v, F32) for v in totals]
        scratch += smalls_scratch(size, w, 2)
    return pl.pallas_call(
        functools.partial(
            back_body, heads=heads, per=LEN // CHUNK, size=size, steps=steps, layer=layer, last=last
        ),
        grid=(begin_norm + steps,),
        in_specs=in_specs,
        out_specs=out_specs,
        out_shape=out_shape,
        scratch_shapes=scratch,
        compiler_params=pltpu.CompilerParams(
            collective_id=2 if last else 3, has_side_effects=True, vmem_limit_bytes=VMEM_LIMIT
        ),
        name="back",
    )(*args)


def unpack_body(full_ref, wide_ref, *refs, layers, heads):
    step_ref, state_ref, conv_ref, bias_ref, convs_ref, biass_ref = refs[:6]
    stepbias_ref, decay_ref, skip_ref, norm_ref, gain_ref = refs[6:]
    model = state_ref.shape[1]
    quarter = model // 4
    w = state_ref.shape[2]
    width = conv_ref.shape[2]
    for layer in range(layers):
        for t in range(4):
            state_ref[layer, t * quarter : (t + 1) * quarter, :] = wide_ref[layer, t, :quarter, :].astype(F32)
        taps = [wide_ref[layer, t, quarter : quarter + 16, :].astype(F32) for t in range(4)]
        taps = (taps[0] + taps[1]) + (taps[2] + taps[3])
        convs_ref[layer] = taps[0:4]
        biass_ref[layer : layer + 1, :] = taps[4:5]
        flat = full_ref[layer].reshape(-1, w)[:PACK].astype(F32)
        at = quarter + 16
        for b in range(model // w):
            step_ref[layer, :, b * w : (b + 1) * w] = flat[at : at + 16]
            at += 16
        for b in range(width // w):
            lanes = slice(b * w, (b + 1) * w)
            rows = flat[at + 8 * b : at + 8 * b + 8]
            conv_ref[layer, :, lanes] = rows[0:4]
            bias_ref[layer : layer + 1, lanes] = rows[4:5]
            norm_ref[layer : layer + 1, lanes] = rows[5:6]
        at += 8 * (width // w)
        for k, ref in enumerate((stepbias_ref, decay_ref, skip_ref)):
            ref[layer : layer + 1, :] = flat[at + k : at + k + 1, :heads]
        at += 8
        for b in range(model // w):
            gain_ref[layer : layer + 1, b * w : (b + 1) * w] = flat[at + b : at + b + 1]


def unpack(full, wide, model, width, heads):
    layers, w = full.shape[0], full.shape[3]
    vm = pl.BlockSpec(memory_space=pltpu.VMEM)
    shapes = [
        (layers, 16, model), (layers, model, w), (layers, 4, width), (layers, width), (layers, 4, w), (layers, w),
        (layers, heads), (layers, heads), (layers, heads), (layers, width), (layers, model),
    ]
    return pl.pallas_call(
        functools.partial(unpack_body, layers=layers, heads=heads),
        in_specs=[vm, vm],
        out_specs=[vm] * len(shapes),
        out_shape=[jax.ShapeDtypeStruct(v, F32) for v in shapes],
        compiler_params=pltpu.CompilerParams(vmem_limit_bytes=VMEM_LIMIT),
        name="unpack",
    )(full, wide)


def shards(
    tokens, inproj, stepproj, stateproj, outproj, convinner, biasinner, convstate, biasstate,
    stepbias, decaylog, skipgain, normgain, inputgain, cotangent,
):
    layers = inproj.shape[0]
    width = inproj.shape[3]
    heads = stepproj.shape[2]
    model = tokens.shape[1]
    pad = LANES - heads
    size = lax.axis_size("dp")
    steps_w = jnp.pad(jnp.swapaxes(stepproj, 1, 2), ((0, 0), (0, pad), (0, 0)))
    head = jnp.pad(jnp.stack([stepbias, decaylog, skipgain], axis=1), ((0, 0), (0, 5), (0, pad)))
    outt = jnp.swapaxes(outproj, 1, 2)
    params = (convinner, biasinner, normgain, convstate, biasstate, head)

    residual = tokens
    kept = []
    out = None
    for at in range(layers):
        results = forward(residual, stateproj, steps_w, inproj, outt, inputgain, params, heads, size, at, out=out)
        if at:
            residual, kept[-1][-1] = results[:2]
            results = results[2:]
        normed, rnorm, small, inner_raw, gate_pre, wt, w_out, ssd, scaled, sq, states = results
        w_out = w_out.reshape(model, width)
        kept.append([residual, normed, rnorm, small, inner_raw, gate_pre, wt, w_out, ssd, scaled, states, sq])
        out = (scaled, w_out, sq)

    assert layers == 2
    before, normed, rnorm, small, inner_raw, gate_pre, wt, w_out, ssd, scaled, states, sq = kept[1]
    upstream, second, held, sdel, steplow, *totals, mixed = back(
        cotangent, sq, gate_pre, ssd, inner_raw, small, states, before, rnorm, inputgain, params,
        w_out, scaled, wt, normed, heads, size, 1,
    )
    after = (normed, steplow, sdel, held, *totals)
    before, normed, rnorm, small, inner_raw, gate_pre, wt, w_out, ssd, scaled, states, sq = kept[0]
    upstream, first, full, wide = back(
        upstream, sq, gate_pre, ssd, inner_raw, small, states, before, rnorm, inputgain, params,
        w_out, scaled, wt, normed, heads, size, 0, after=after,
    )
    pairs = [first[1:3], jnp.stack([second[1], first[3]])]
    (
        step_grad, state_grad, conv_grad, bias_grad, convs_grad, biass_grad,
        stepbias_grad, decay_grad, skip_grad, norm_grad, gain_grad,
    ) = unpack(full, wide, model, width, heads)
    return (
        mixed,
        upstream,
        jnp.stack(pairs),
        jnp.swapaxes(step_grad[:, :heads], 1, 2),
        state_grad,
        jnp.swapaxes(jnp.stack([first[0], second[0]]), 1, 2),
        conv_grad,
        bias_grad,
        convs_grad,
        biass_grad,
        stepbias_grad,
        decay_grad,
        skip_grad,
        norm_grad,
        gain_grad,
    )


def solution(mesh):
    in_specs = (
        P("dp", None),
        P(None, None, "dp", "tensor"),
        P(None, None, "tensor"),
        P(),
        P(None, "tensor", "dp"),
        P(None, None, "tensor"),
        P(None, "tensor"),
        P(),
        P(),
        P(None, "tensor"),
        P(None, "tensor"),
        P(None, "tensor"),
        P(None, "tensor"),
        P(),
        P("dp", None),
    )
    out_specs = (
        P("dp", None),
        P("dp", None),
        P(None, None, "dp", "tensor"),
        P(None, None, "tensor"),
        P(),
        P(None, "tensor", "dp"),
        P(None, None, "tensor"),
        P(None, "tensor"),
        P(),
        P(),
        P(None, "tensor"),
        P(None, "tensor"),
        P(None, "tensor"),
        P(None, "tensor"),
        P(),
    )
    return jax.shard_map(shards, mesh=mesh, in_specs=in_specs, out_specs=out_specs, check_vma=False)
```

```python
import functools
import math

import jax
import jax.numpy as jnp
from jax import lax
from jax.experimental import pallas as pl
from jax.experimental.pallas import tpu as pltpu
from jax.sharding import PartitionSpec as P

STATE = 128
LEN = 1024
INNER = 3072
HEAD = 64
CHUNK = 128
SLICE = 256
TILE = 256
PACK = 544
SPAN = 400
VMEM_LIMIT = 65000 * 1024
LANES = 128
EPS = 1e-05
LOG2E = 1.4426950408889634

HIGH = lax.Precision.HIGHEST
NN = (((1,), (0,)), ((), ()))
NT = (((1,), (1,)), ((), ()))
TN = (((0,), (0,)), ((), ()))
F32 = jnp.float32
BF16 = jnp.bfloat16
MESH = pl.DeviceIdType.MESH


def remote(src, dst, send, recv, where):
    return pltpu.make_async_remote_copy(
        src_ref=src, dst_ref=dst, send_sem=send, recv_sem=recv, device_id=where, device_id_type=MESH
    )


class Line:
    def __init__(self, size):
        self.n = size // 2
        me = lax.axis_index("dp")
        self.me = me
        self.at = me // 2
        self.side = lax.rem(me, 2)
        self.pair = {"dp": me + 1 - 2 * self.side}
        self.right = {"dp": jnp.minimum(me + 2, size - 1)}
        self.left = {"dp": jnp.maximum(me - 2, 0)}
        odd = lax.rem(self.at, 2)
        self.odd = odd == 1
        self.near = {"dp": me + 2 - 4 * odd}
        self.has_left = self.at > 0
        self.has_right = self.at < self.n - 1

    def greet(self, barrier, more=()):
        for who in more:
            pl.semaphore_signal(barrier, inc=1, device_id=who, device_id_type=MESH)
        pl.semaphore_signal(barrier, inc=1, device_id=self.pair, device_id_type=MESH)

        @pl.when(self.has_left)
        def _():
            pl.semaphore_signal(barrier, inc=1, device_id=self.left, device_id_type=MESH)

        @pl.when(self.has_right)
        def _():
            pl.semaphore_signal(barrier, inc=1, device_id=self.right, device_id_type=MESH)

        peers = 1 + len(more) + self.has_left.astype(jnp.int32) + self.has_right.astype(jnp.int32)
        pl.semaphore_wait(barrier, peers)

    def greet_all(self, barrier, more=()):
        for who in list(more) + [self.pair]:
            pl.semaphore_signal(barrier, inc=1, device_id=who, device_id_type=MESH)
        for i in range(self.n):
            @pl.when(i != self.at)
            def _(i=i):
                pl.semaphore_signal(barrier, inc=1, device_id={"dp": 2 * i + self.side}, device_id_type=MESH)
        pl.semaphore_wait(barrier, self.n + len(more))


def upper(rows):
    return max(16, rows // 32 * 16)


class Gather:
    def __init__(self, line, own, full, keep, send, recv):
        self.line, self.own, self.full, self.keep, self.send, self.recv = line, own, full, keep, send, recv
        self.rows = full.shape[2]
        self.cut = upper(self.rows)

    def copy(self, j, slab, way, src=None, rest=False):
        where = (self.line.right, self.line.left, self.line.pair)[way]
        dst = self.full.at[j, slab]
        if rest:
            dst = self.full.at[j, slab, pl.ds(self.cut, self.rows - self.cut)]
        return remote(dst if src is None else src, dst, self.send.at[j, way, slab], self.recv.at[j, slab], where)

    def shared(self, j, slab, owner):
        part = self.full.at[j, slab, pl.ds(0, self.cut)]
        return remote(part, part, self.send.at[j, 0, slab], self.recv.at[j, owner], self.line.near)

    def start(self, j):
        line = self.line
        pltpu.make_async_copy(self.own(j), self.full.at[j, line.me], self.keep.at[j]).start()

        @pl.when(line.has_right)
        def _():
            self.copy(j, line.me, 0, self.own(j)).start()

        @pl.when(line.has_left)
        def _():
            self.copy(j, line.me, 1, self.own(j)).start()

        self.copy(j, line.me, 2, self.own(j)).start()

    def relay(self, j, k):
        line = self.line

        def forward(slab, way, go_on, near):
            self.copy(j, slab, way).wait_recv()

            @pl.when(go_on)
            def _():
                self.copy(j, slab, way).start()

            if k > 1:
                self.copy(j, slab, 2).start()
            else:
                @pl.when(near)
                def _():
                    self.copy(j, slab, 2, rest=True).start()

                @pl.when(jnp.logical_not(near))
                def _():
                    self.copy(j, slab, 2).start()

        @pl.when(line.at >= k)
        def _():
            forward(line.me - 2 * k, 0, line.has_right, line.odd)

        @pl.when(line.at + k < line.n)
        def _():
            forward(line.me + 2 * k, 1, line.has_left, jnp.logical_not(line.odd))

        if k == 1:
            slab = line.me + 1 - 2 * line.side
            self.copy(j, slab, 2).wait_recv()
            self.shared(j, slab, line.near["dp"]).start()

    def near_slab(self):
        line = self.line
        return line.near["dp"] + 1 - 2 * line.side

    def arrive(self, j):
        line = self.line
        pltpu.make_async_copy(self.own(j), self.full.at[j, line.me], self.keep.at[j]).wait()
        self.copy(j, self.near_slab(), 2, rest=True).wait_recv()
        self.shared(j, self.near_slab(), line.me).wait_recv()
        for place in range(line.n):
            slab = 2 * place + 1 - line.side

            @pl.when((slab != self.near_slab()) & (place != line.at))
            def _(slab=slab):
                self.copy(j, slab, 2).wait_recv()

    def drain(self, j):
        line = self.line
        self.shared(j, line.me + 1 - 2 * line.side, line.near["dp"]).wait_send()
        for place in range(line.n):
            slab = 2 * place + line.side
            near = slab == line.near["dp"]

            @pl.when(near)
            def _(slab=slab):
                self.copy(j, slab, 2, rest=True).wait_send()

            @pl.when(jnp.logical_not(near))
            def _(slab=slab):
                self.copy(j, slab, 2).wait_send()

            @pl.when(line.has_right & (place <= line.at))
            def _(slab=slab):
                self.copy(j, slab, 0).wait_send()

            @pl.when(line.has_left & (place >= line.at))
            def _(slab=slab):
                self.copy(j, slab, 1).wait_send()


class Square:
    def __init__(self):
        me = lax.axis_index("tensor")
        self.me = me
        self.half = lax.rem(me, 2)
        self.mate = {"tensor": me + 1 - 2 * self.half}
        self.across = {"tensor": lax.rem(me + 2, 4)}

    def others(self):
        return [{"tensor": lax.rem(self.me + k, 4)} for k in (1, 2, 3)]


class Total:
    def __init__(self, square, part, got, far, other, send, recv):
        self.square, self.part, self.got, self.far, self.other = square, part, got, far, other
        self.send, self.recv = send, recv

    def first(self, c):
        sq = self.square
        return remote(
            self.part.at[2 * c + 1 - sq.half], self.got.at[c], self.send.at[0, c], self.recv.at[0, c], sq.mate
        )

    def second(self, c):
        sq = self.square
        return remote(self.part.at[2 * c + sq.half], self.far.at[c], self.send.at[1, c], self.recv.at[1, c], sq.across)

    def third(self, c):
        sq = self.square
        return remote(self.part.at[2 * c + sq.half], self.other.at[c], self.send.at[2, c], self.recv.at[2, c], sq.mate)

    def step(self, kind, c):
        slot = 2 * c + self.square.half
        if kind == 0:
            self.first(c).start()
        elif kind == 1:
            self.first(c).wait_recv()
            self.part[slot] = (self.part[slot].astype(F32) + self.got[c].astype(F32)).astype(BF16)
            self.second(c).start()
        elif kind == 2:
            self.second(c).wait()
            self.part[slot] = (self.part[slot].astype(F32) + self.far[c].astype(F32)).astype(BF16)
            self.third(c).start()
        else:
            self.third(c).wait_recv()
            self.first(c).wait_send()
            self.third(c).wait_send()
            self.part[2 * c + 1 - self.square.half] = self.other[c]


class Scatter:
    def __init__(self, line, part, out, near, far, send, recv):
        self.line, self.part, self.out, self.near, self.far = line, part, out, near, far
        self.send, self.recv = send, recv

    def order(self):
        n = self.line.n
        seq = []
        for i in range((n + 1) // 2):
            seq.append(i)
            if n - 1 - i != i:
                seq.append(n - 1 - i)
        return seq

    def cross(self, j, i):
        line = self.line
        return remote(
            self.part.at[j, 2 * i + 1 - line.side], self.near.at[j, i], self.send.at[0, j, i], self.recv.at[0, j, i], line.pair
        )

    def straight(self, j, i, source):
        line = self.line
        return remote(
            self.part.at[j, 2 * i + line.side], self.far.at[j, source], self.send.at[1, j, i], self.recv.at[1, j, source],
            {"dp": 2 * i + line.side},
        )

    def lead(self, j, m):
        self.cross(j, self.order()[m]).start()

    def start(self, j):
        for m in range(self.line.n):
            self.lead(j, m)

    def emit(self, j, turned, right, now=None):
        rows = self.part.shape[2]
        for m, i in enumerate(self.order()):
            value = mm(turned[2 * i * rows : 2 * (i + 1) * rows, :], right[...]).astype(BF16)
            self.part[j, 2 * i] = value[:rows]
            self.part[j, 2 * i + 1] = value[rows:]
            if now is None or m < now:
                self.lead(j, m)

    def product(self, dst, turned, right):
        rows = dst.shape[1]
        for i in range(self.line.n):
            value = mm(turned[2 * i * rows : 2 * (i + 1) * rows, :], right[...]).astype(BF16)
            dst[2 * i] = value[:rows]
            dst[2 * i + 1] = value[rows:]

    def fold(self, j, m):
        line = self.line
        i = self.order()[m]
        self.cross(j, i).wait_recv()
        slot = 2 * i + line.side
        self.part[j, slot] = (self.part[j, slot].astype(F32) + self.near[j, i].astype(F32)).astype(BF16)

        @pl.when(i != line.at)
        def _():
            self.straight(j, i, line.at).start()

    def finish(self, j):
        line = self.line
        out = self.out(j)
        out[...] = self.part[j, line.me].astype(out.dtype)
        for i in range(line.n):
            @pl.when(i != line.at)
            def _(i=i):
                self.straight(j, i, i).wait_recv()
                out[...] += self.far[j, i].astype(out.dtype)

    def drain(self, j):
        for i in range(self.line.n):
            self.cross(j, i).wait_send()

            @pl.when(i != self.line.at)
            def _(i=i):
                self.straight(j, i, self.line.at).wait_send()


def mm(left, right, dims=NN, precision=None):
    return lax.dot_general(left, right, dims, precision=precision, preferred_element_type=F32)


def sigmoid(v):
    return 0.5 * jnp.tanh(0.5 * v) + 0.5


def softplus(v):
    return jnp.maximum(v, 0.0) + jnp.log1p(jnp.exp(-jnp.abs(v)))


def split16(v):
    top = v.astype(BF16)
    return top, (v - top.astype(F32)).astype(BF16)


def expand(v, ind):
    top, rest = split16(v)
    return mm(top, ind) + mm(rest, ind)


def headsum(v, ind):
    return mm(v.astype(BF16), ind, NT)


def rowsum(v):
    return mm(jnp.ones((8, v.shape[1]), BF16), v.astype(BF16), NT)[0:1, :]


def iotas(n):
    return (
        lax.broadcasted_iota(jnp.int32, (n, n), 0),
        lax.broadcasted_iota(jnp.int32, (n, n), 1),
    )


def colsum(v):
    return jnp.sum(v, axis=0, keepdims=True)


def conv_pre(ext, par, n):
    total = par[4:5, :] + par[0:1, :] * ext[5 : 5 + n, :]
    for tap in range(1, 4):
        total = total + par[tap : tap + 1, :] * ext[5 + tap : 5 + tap + n, :]
    return total


def scan_prep(small, hp, ind, n):
    rows, cols = iotas(n)
    raw = small[:, 2 * STATE :] + hp[0:1, :]
    step = softplus(raw)
    rate = -jnp.exp(hp[1:2, :])
    lower = jnp.where(rows >= cols, 1.0, 0.0).astype(F32)
    cs = mm(lower, step * rate, precision=HIGH)
    tail = jnp.exp(cs[n - 1 : n, :] - cs)
    wide = mm(jnp.concatenate([step, jnp.exp(cs), tail], axis=0).astype(BF16), ind)
    return raw, step, rate, cs, wide[0:n], wide[n : 2 * n], wide[2 * n : 3 * n]


def block_of(slabs, at, rows):
    step = math.gcd(LANES, rows)
    pieces = []
    for k in range(LANES // step):
        row = at * LANES + k * step
        slab = row // rows
        pieces.append(slabs[slab, pl.ds(pl.multiple_of(row - slab * rows, step), step), :])
    return pieces[0] if len(pieces) == 1 else jnp.concatenate(pieces, axis=0)


def put_params(cp, sp, hp, ind, layer, params):
    conv, bias, norm, convs, biass, head = params
    width = cp.shape[1]
    row = lax.broadcasted_iota(jnp.int32, (LANES, width), 0)
    lane = lax.broadcasted_iota(jnp.int32, (LANES, width), 1)
    ind[...] = jnp.where(lane // HEAD == row, 1.0, 0.0).astype(BF16)
    hp[...] = head[layer]
    cp[0:4, :] = conv[layer]
    cp[4:5, :] = bias[layer : layer + 1, :]
    cp[5:6, :] = norm[layer : layer + 1, :]
    cp[6:8, :] = expand(hp[...], ind[...])[2:4, :]
    sp[0:4, :] = convs[layer]
    sp[4:5, :] = biass[layer : layer + 1, :]


def place_rows(dst, at, value):
    r = dst.shape[1]
    for g in range(0, value.shape[0], 16):
        dst[(at + g) // r, (at + g) % r : (at + g) % r + 16, :] = value[g : g + 16].astype(dst.dtype)


def pack_rows(size):
    return -(-PACK // (16 * size)) * 16


def put_pack(dst, me, turned, steps_low, sdel, dcp, dsp, dhp, dgain):
    model = turned.shape[0]
    quarter = model // 4
    w = sdel.shape[1]

    def empty(n):
        return jnp.zeros((n, w), F32)

    place_rows(dst, 0, mm(turned[pl.ds(pl.multiple_of(me * quarter, quarter), quarter), :], sdel[...]))
    place_rows(dst, quarter, jnp.concatenate([dsp, empty(8)], axis=0))
    grown = mm(turned[...], steps_low[...]).T[:16]
    at = quarter + 16
    for b in range(model // w):
        place_rows(dst, at, grown[:, b * w : (b + 1) * w])
        at += 16
    place_rows(dst, at, jnp.concatenate([dcp[:, :w], dcp[:, w : 2 * w]], axis=0))
    place_rows(dst, at + 16, jnp.concatenate([dcp[:, 2 * w :], jnp.concatenate([dhp, dhp], axis=1)], axis=0))
    rows = [dgain[:, b * w : (b + 1) * w] for b in range(model // w)]
    place_rows(dst, at + 32, jnp.concatenate(rows + [empty(16 - len(rows))], axis=0))
    assert at + 48 == PACK


class Smalls:
    def __init__(self, line, square, pack, near, away, own, full, wide, sems):
        send, recv, keep, gsend, grecv, self.xsend, self.xrecv = sems
        self.square, self.full, self.wide = square, full, wide
        self.layers = range(pack.shape[0])
        self.sum = Scatter(line, pack, lambda j: own.at[j], near, away, send, recv)
        self.spread = Gather(line, lambda j: own.at[j], full, keep, gsend, grecv)

    def swap(self, k):
        sq = self.square
        slot = (sq.me, sq.me, lax.rem(sq.me + 2, 4))[k]
        who = (sq.across, sq.mate, sq.mate)[k]
        return remote(self.wide.at[slot], self.wide.at[slot], self.xsend.at[k], self.xrecv.at[k], who)

    def start(self):
        for j in self.layers:
            self.sum.start(j)

    def fold(self):
        for j in self.layers:
            for m in range(self.sum.line.n):
                self.sum.fold(j, m)

    def turn(self):
        for j in self.layers:
            self.sum.finish(j)
            self.spread.start(j)

    def relay(self, k):
        for j in self.layers:
            self.spread.relay(j, k)

    def cross(self):
        for j in self.layers:
            self.spread.arrive(j)
            flat = self.full[j].reshape(-1, self.full.shape[3])
            self.wide[self.square.me, j] = flat[: self.wide.shape[2]]
        self.swap(0).start()
        self.swap(1).start()

    def cross_on(self):
        self.swap(0).wait_recv()
        self.swap(2).start()

    def end(self):
        self.swap(1).wait_recv()
        self.swap(2).wait_recv()
        for k in range(3):
            self.swap(k).wait_send()
        for j in self.layers:
            self.sum.drain(j)
            self.spread.drain(j)


def smalls_scratch(size, w, layers):
    r, n = pack_rows(size), size // 2
    buffers = [
        pltpu.VMEM((layers, size, r, w), BF16),
        pltpu.VMEM((layers, n, r, w), BF16),
        pltpu.VMEM((layers, n, r, w), BF16),
        pltpu.VMEM((layers, r, w), BF16),
        pltpu.VMEM((layers, size, r, w), BF16),
        pltpu.VMEM((4, layers, SPAN, w), BF16),
    ]
    sems = [
        pltpu.SemaphoreType.DMA((2, layers, n)),
        pltpu.SemaphoreType.DMA((2, layers, n)),
        pltpu.SemaphoreType.DMA((layers,)),
        pltpu.SemaphoreType.DMA((layers, 3, size)),
        pltpu.SemaphoreType.DMA((layers, size)),
        pltpu.SemaphoreType.DMA((3,)),
        pltpu.SemaphoreType.DMA((3,)),
    ]
    return buffers + sems


def forward_body(*refs, size, heads, per, steps, layer):
    refs = list(refs)

    def take(n):
        got = refs[:n]
        del refs[:n]
        return got

    mid = layer > 0
    (res_hbm,) = take(1)
    if mid:
        scaled_hbm, wout_hbm, sq_ref = take(3)
    state_hbm, step_hbm, in_hbm, out_hbm, gain_ref = take(5)
    params = take(6)
    if mid:
        new_hbm, sums_ref = take(2)
    normed_hbm, rnorm_ref, small_hbm, inner_hbm, gate_hbm, wt_hbm, full_hbm, ssd_ref, scaled_ref, sqs_ref, st_ref = take(11)
    if mid:
        scaled_in, wout, part, got, far, other, rows_got, facs, fresh, sends, recvs, rsend, rrecv = take(13)
    res, wstate, wt, slabs, normed, turned, small, inner, gate, ext, exts, state = take(12)
    cp_ref, sp_ref, hp_ref, ind_ref, keep, gsend, grecv, load, sems = take(9)
    assert not refs

    n = CHUNK
    tokens_n, model = res.shape
    width = inner.shape[1]
    top = 2 * width + 2 * STATE
    i = pl.program_id(0)
    line = Line(size)
    square = Square()
    job = Gather(line, lambda j: out_hbm.at[layer] if j == 2 else in_hbm.at[layer, 1 - j], slabs, keep, gsend, grecv)
    outgoing = [(turned, normed_hbm), (small, small_hbm), (inner, inner_hbm), (gate, gate_hbm)]
    outgoing += [(wt, wt_hbm), (slabs.at[2], full_hbm)]
    if mid:
        outgoing.append((fresh, new_hbm))

    def flush(k):
        return pltpu.make_async_copy(*outgoing[k], sems.at[k])


    @pl.when(i == 0)
    def _():
        pairs = [(res_hbm, res), (state_hbm.at[layer], wstate), (step_hbm.at[layer], wt.at[pl.ds(top, LANES), :])]
        if mid:
            pairs = [(scaled_hbm, scaled_in), (wout_hbm, wout)] + pairs
        loads = [pltpu.make_async_copy(src, dst, load.at[k]) for k, (src, dst) in enumerate(pairs)]
        for copy in loads:
            copy.start()
        line.greet(pltpu.get_barrier_semaphore(), square.others() if mid else ())
        job.start(0)
        put_params(cp_ref, sp_ref, hp_ref, ind_ref, layer, params)
        ticks = [functools.partial(job.relay, 0, k) for k in range(1, line.n)]
        ticks.append(functools.partial(job.start, 1))
        span = model // LANES

        def project(j, dst):
            weight = slabs[j].reshape(model, width)

            def tile(t, _):
                rows = pl.ds(pl.multiple_of(t * TILE, TILE), TILE)
                dst[rows, :] = mm(normed[rows, :], weight)
                return 0

            lax.fori_loop(0, tokens_n // TILE, tile, 0)

        def turn_inner(b, _):
            wt[:width, pl.ds(pl.multiple_of(b * LANES, LANES), LANES)] = block_of(slabs.at[0], b, slabs.shape[2]).T
            return 0

        def settle():
            job.arrive(0)
            if not mid:
                project(0, inner)
                flush(2).start()
            lax.fori_loop(0, span, turn_inner, 0)

        ticks.append(functools.partial(job.relay, 1, 1))
        ticks.append(settle)
        ticks += [functools.partial(job.relay, 1, k) for k in range(2, line.n)]
        ticks.append(functools.partial(job.start, 2))

        if mid:
            chunks = model // SLICE
            half = tokens_n // 2
            sums = Total(square, part, got, far, other, sends, recvs)
            copies = [
                remote(sq_ref, rows_got.at[square.me], rsend.at[k], rrecv.at[k], who)
                for k, who in enumerate(square.others())
            ]
            for copy in copies:
                copy.start()
            loads[0].wait()
            loads[1].wait()
            for c in range(chunks):
                value = mm(scaled_in[...], wout[c * SLICE : (c + 1) * SLICE, :], NT).astype(BF16)
                part[2 * c] = value[:half]
                part[2 * c + 1] = value[half:]
                sums.step(0, c)
                if c:
                    sums.step(1, c - 1)
            sums.step(1, chunks - 1)
            rows_got[square.me] = sq_ref[...]
            for copy in copies:
                copy.wait()
            total = (rows_got[0] + rows_got[1]) + (rows_got[2] + rows_got[3])
            sums_ref[...] = total
            factor = lax.rsqrt(total / INNER + EPS)
            for t in range(tokens_n // LANES):
                facs[t * LANES : (t + 1) * LANES, :] = jnp.broadcast_to(factor[t], (LANES, LANES)).T
            loads[2].wait()

            def use(c):
                for h in range(2):
                    where = slice(h * half, (h + 1) * half)
                    for s in range(SLICE // LANES):
                        lanes = slice(c * SLICE + s * LANES, c * SLICE + (s + 1) * LANES)
                        value = part[2 * c + h, :, s * LANES : (s + 1) * LANES].astype(F32)
                        fresh[where, lanes] = res[where, lanes].astype(F32) + facs[where, :] * value

            spread = max(1, -(-len(ticks) // chunks))
            for c in range(chunks):
                for tick in ticks[:spread]:
                    tick()
                ticks = ticks[spread:]
                sums.step(2, c)
                if c:
                    sums.step(3, c - 1)
                    use(c - 1)
            sums.step(3, chunks - 1)
            use(chunks - 1)
            flush(6).start()
        else:
            loads[0].wait()
        loads[-2].wait()
        loads[-1].wait()
        for b in range(2 * STATE // LANES):
            rows = slice(2 * width + b * LANES, 2 * width + (b + 1) * LANES)
            wt[rows, :] = wstate[:, b * LANES : (b + 1) * LANES].T

        def norm(t, _):
            rows = pl.ds(pl.multiple_of(t * TILE, TILE), TILE)
            value = (fresh if mid else res)[rows, :].astype(F32)
            scale = lax.rsqrt(jnp.sum(value * value, axis=1, keepdims=True) / model + EPS)
            low = (value * scale * gain_ref[layer : layer + 1, :]).astype(BF16)
            rnorm_ref[rows, :] = scale
            normed[rows, :] = low
            turned[:, rows] = low.T
            small[rows, : 2 * STATE] = mm(low, wstate[...])
            small[rows, 2 * STATE :] = mm(low, wt[top:, :], NT)
            return 0

        lax.fori_loop(0, tokens_n // TILE, norm, 0)
        flush(0).start()
        flush(1).start()
        for tick in ticks:
            tick()

        if mid:
            project(0, inner)
            flush(2).start()
        job.arrive(1)
        project(1, gate)
        flush(3).start()

    for k in range(1, line.n):
        @pl.when(i == 1 + (k - 1) * steps // line.n)
        def _(k=k):
            job.relay(2, k)

    @pl.when(i > 0)
    def _():
        at = i - 1
        where = pl.ds(pl.multiple_of(at * n, n), n)

        @pl.when(lax.rem(at, per) == 0)
        def _():
            ext[0:8, :] = jnp.zeros((8, width), F32)
            exts[0:8, :] = jnp.zeros((8, 2 * STATE), F32)
            state[...] = jnp.zeros_like(state)

        rows, cols = iotas(n)
        ind = ind_ref[...]
        ext[8 : 8 + n, :] = inner[where, :]
        pre = conv_pre(ext, cp_ref, n)
        x = pre * sigmoid(pre)
        ext[0:8, :] = ext[n : n + 8, :]
        mini = small[where, :]
        exts[8 : 8 + n, :] = mini[:, : 2 * STATE]
        pres = conv_pre(exts, sp_ref, n)
        bc = (pres * sigmoid(pres)).astype(BF16)
        exts[0:8, :] = exts[n : n + 8, :]
        key, query = bc[:, :STATE], bc[:, STATE:]

        _, step, rate, cs, wide_step, wide_cs, wide_tail = scan_prep(mini, hp_ref, ind, n)
        cs2 = cs * LOG2E
        cs2t = cs2.T
        xs = x * wide_step
        lane = lax.broadcasted_iota(jnp.int32, (1, width), 1)
        half = jnp.where(lax.rem(lane, 2 * HEAD) < HEAD, 1.0, 0.0).astype(BF16)
        xsb = xs.astype(BF16)
        xs0 = xsb * half
        xs1 = xsb - xs0
        before = state[...]
        low = before.astype(BF16)
        st_ref[0] = low
        carried = mm(query, low) * wide_cs
        xw = (xs * wide_tail).astype(BF16)
        state[...] = before * wide_cs[n - 1 : n, :] + mm(key, xw, TN)
        scores = jnp.where(rows >= cols, mm(query, key, NT), 0.0)
        for pair in range(heads // 2):
            lanes = slice(pair * 2 * HEAD, (pair + 1) * 2 * HEAD)
            mats = []
            for h in (2 * pair, 2 * pair + 1):
                dec = jnp.exp2(jnp.minimum(cs2[:, h : h + 1] - cs2t[h : h + 1, :], 0.0))
                mats.append((scores * dec).astype(BF16))
            local = mm(
                jnp.concatenate(mats, axis=1),
                jnp.concatenate([xs0[:, lanes], xs1[:, lanes]], axis=0),
            )
            ssd_ref[:, lanes] = local + carried[:, lanes] + cp_ref[6:7, lanes] * x[:, lanes]
        gates = gate[where, :]
        gated = ssd_ref[...] * (gates * sigmoid(gates))
        sqs_ref[0] = rowsum(gated * gated)
        scaled_ref[...] = (gated * cp_ref[5:6, :]).astype(BF16)

        span = model // LANES
        share = -(-span // steps)
        for k in range(share):
            b = at * share + k

            @pl.when(b < span)
            def _(b=b):
                piece = block_of(slabs.at[1], b, slabs.shape[2]).T
                wt[width : 2 * width, pl.ds(pl.multiple_of(b * LANES, LANES), LANES)] = piece

    @pl.when(i == steps)
    def _():
        flush(4).start()
        job.arrive(2)
        flush(5).start()
        for j in range(3):
            job.drain(j)
        for k in range(len(outgoing)):
            flush(k).wait()


def forward(res, stateproj, steps_w, inproj, outt, gain, params, heads, size, layer, out=None):
    tokens_n, model = res.shape
    _, _, rows, width = inproj.shape
    top = 2 * width + 2 * STATE + LANES
    steps = tokens_n // CHUNK
    mid = out is not None
    hbm = pl.BlockSpec(memory_space=pl.ANY)
    chunks = model // SLICE

    def whole(a):
        return pl.BlockSpec(a.shape, lambda i: (0,) * len(a.shape))

    def row(w):
        return pl.BlockSpec((CHUNK, w), lambda i: (jnp.maximum(i - 1, 0), 0))

    args, in_specs, out_specs, out_shape, scratch = [res], [hbm], [], [], []
    if mid:
        args += list(out)
        in_specs += [hbm, hbm, whole(out[2])]
        out_specs += [hbm, whole(out[2])]
        out_shape += [jax.ShapeDtypeStruct(res.shape, F32), jax.ShapeDtypeStruct(out[2].shape, F32)]
        chunk = pltpu.VMEM((chunks, tokens_n // 2, SLICE), BF16)
        scratch += [
            pltpu.VMEM(out[0].shape, BF16),
            pltpu.VMEM(out[1].shape, BF16),
            pltpu.VMEM((2 * chunks, tokens_n // 2, SLICE), BF16),
            chunk, chunk, chunk,
            pltpu.VMEM((4,) + out[2].shape, F32),
            pltpu.VMEM((tokens_n, LANES), F32),
            pltpu.VMEM(res.shape, F32),
            pltpu.SemaphoreType.DMA((3, chunks)),
            pltpu.SemaphoreType.DMA((3, chunks)),
            pltpu.SemaphoreType.DMA((3,)),
            pltpu.SemaphoreType.DMA((3,)),
        ]
    args += [stateproj, steps_w, inproj, outt, gain, *params]
    in_specs += [hbm, hbm, hbm, hbm, whole(gain)] + [whole(v) for v in params]
    out_specs += [
        hbm, pl.BlockSpec((tokens_n, 1), lambda i: (0, 0)), hbm, hbm, hbm, hbm, hbm,
        row(width), row(width),
        pl.BlockSpec((1, 1, CHUNK), lambda i: (jnp.maximum(i - 1, 0), 0, 0)),
        pl.BlockSpec((1, STATE, width), lambda i: (jnp.maximum(i - 1, 0), 0, 0)),
    ]
    out_shape += [
        jax.ShapeDtypeStruct((model, tokens_n), BF16),
        jax.ShapeDtypeStruct((tokens_n, 1), F32),
        jax.ShapeDtypeStruct((tokens_n, 2 * STATE + LANES), F32),
        jax.ShapeDtypeStruct((tokens_n, width), F32),
        jax.ShapeDtypeStruct((tokens_n, width), F32),
        jax.ShapeDtypeStruct((top, model), BF16),
        jax.ShapeDtypeStruct((size, rows, width), BF16),
        jax.ShapeDtypeStruct((tokens_n, width), F32),
        jax.ShapeDtypeStruct((tokens_n, width), BF16),
        jax.ShapeDtypeStruct((steps, 1, CHUNK), F32),
        jax.ShapeDtypeStruct((steps, STATE, width), BF16),
    ]
    scratch += [
        pltpu.VMEM(res.shape, res.dtype),
        pltpu.VMEM((model, 2 * STATE), BF16),
        pltpu.VMEM((top, model), BF16),
        pltpu.VMEM((3, size, rows, width), BF16),
        pltpu.VMEM((tokens_n, model), BF16),
        pltpu.VMEM((model, tokens_n), BF16),
        pltpu.VMEM((tokens_n, 2 * STATE + LANES), F32),
        pltpu.VMEM((tokens_n, width), F32),
        pltpu.VMEM((tokens_n, width), F32),
        pltpu.VMEM((CHUNK + 8, width), F32),
        pltpu.VMEM((CHUNK + 8, 2 * STATE), F32),
        pltpu.VMEM((STATE, width), F32),
        pltpu.VMEM((8, width), F32),
        pltpu.VMEM((8, 2 * STATE), F32),
        pltpu.VMEM((8, LANES), F32),
        pltpu.VMEM((LANES, width), BF16),
        pltpu.SemaphoreType.DMA((3,)),
        pltpu.SemaphoreType.DMA((3, 3, size)),
        pltpu.SemaphoreType.DMA((3, size)),
        pltpu.SemaphoreType.DMA((5,)),
        pltpu.SemaphoreType.DMA((7,)),
    ]
    return pl.pallas_call(
        functools.partial(forward_body, size=size, heads=heads, per=LEN // CHUNK, steps=steps, layer=layer),
        grid=(steps + 1,),
        in_specs=in_specs,
        out_specs=out_specs,
        out_shape=out_shape,
        scratch_shapes=scratch,
        compiler_params=pltpu.CompilerParams(
            collective_id=min(layer, 1), has_side_effects=True, vmem_limit_bytes=VMEM_LIMIT
        ),
        name="forward",
    )(*args)


def back_body(*refs, heads, per, size, steps, layer, last):
    refs = list(refs)

    def take(n):
        got = refs[:n]
        del refs[:n]
        return got

    up_ref, sq_ref, gate_ref, ssd_ref, inner_ref, iprev_ref, small_ref, sprev_ref, st_ref, res_ref, rn_ref = take(11)
    gain_ref = take(1)[0]
    params = take(6)
    wout_hbm, scaled_hbm, wt_hbm, normed_hbm = take(4)
    if not last:
        next_normed, next_steps, next_sdel, next_inner, next_dcp, next_dsp, next_dhp, next_dgain = take(8)
    new_ref, grad_hbm = take(2)
    if last:
        held_hbm, sdsum_ref, steplow_ref, dcp_ref, dsp_ref, dhp_ref, dgain_ref, mixed_ref = take(8)
    else:
        full_hbm, wide_hbm = take(2)
    ext, exts, cde, cdes, dstate, rq, cp_ref, sp_ref, hp_ref, ind_ref = take(10)
    wout, scaled, wt, turned, dy, glow, ilow, frow, srow, sgot = take(10)
    part, near, away, tpart, got, far, other = take(7)
    load, rsend, rrecv, ssend, srecv, sends, recvs, gsem = take(8)
    if last:
        held, fgot, opart, ogot, ofar, oother, fsend, frecv, osends, orecvs = take(10)
    else:
        dcp_ref, dsp_ref, dhp_ref, dgain_ref = take(4)
        sd_all = scaled.at[:, pl.ds(0, 2 * STATE)]
        step_all = scaled.at[:, pl.ds(2 * STATE, LANES)]
        buffers = take(6)
        sems = take(7)
    assert not refs

    n = CHUNK
    model = up_ref.shape[1]
    i = pl.program_id(0)
    begin_gate = steps
    begin_scan = begin_gate + steps
    begin_norm = begin_scan + steps
    end = begin_norm + steps - 1
    line = Line(size)
    square = Square()
    rows_own = part.shape[2]
    count = part.shape[0]
    job = Scatter(line, part, lambda j: dy.at[pl.ds(j * rows_own, rows_own), :], near, away, ssend, srecv)
    sums = Total(square, tpart, got, far, other, sends, recvs)
    if last:
        outs = Total(square, opart, ogot, ofar, oother, osends, orecvs)
        half = steps * n // 2
        slices = model // SLICE
    else:
        minis = Smalls(line, square, *buffers, sems)
    moves = [(wout_hbm, wout), (scaled_hbm, scaled), (wt_hbm, wt), (normed_hbm, turned)]
    if last:
        moves.append((held, held_hbm))
    else:
        tokens_n = steps * n
        spots = (wt.at[pl.ds(0, model), pl.ds(0, tokens_n)],)
        spots += tuple(
            wt.at[pl.ds(0, tokens_n), pl.ds(tokens_n + at, w)] for at, w in ((0, LANES), (LANES, 2 * STATE))
        )
        moves += [(next_normed, spots[0]), (next_steps, spots[1]), (next_sdel, spots[2]), (next_inner, part.at[3])]

    def move(k):
        return pltpu.make_async_copy(*moves[k], load.at[k])

    places = line.n

    def spaced(begin, stop, m):
        return begin + m * (stop - begin) // places

    middle = begin_scan + steps // 2
    if last:
        folds = [(spaced(begin_scan, middle, m), 0, m) for m in range(places)]
        folds += [(spaced(middle, begin_norm, m) + 1, 1, m) for m in range(places)]
    else:
        folds = [(spaced(begin_gate - 1, begin_scan + 3, m), 3, m) for m in range(places)]
        folds += [(spaced(begin_scan + 2, middle + 3, m), 0, m) for m in range(places)]
        folds += [(spaced(begin_norm - 1, end - 1, m), 1, m) for m in range(places)]

    def column(row):
        return jnp.broadcast_to(row, (n, n)).T[:, 0:1]

    @pl.when(i == 0)
    def _():
        for k in range(3):
            move(k).start()
        if not last:
            move(7).start()
        put_params(cp_ref, sp_ref, hp_ref, ind_ref, layer, params)
        rq[...] = jnp.zeros_like(rq)
        line.greet_all(pltpu.get_barrier_semaphore(), square.others())
        if last:
            rows = [
                remote(sq_ref, fgot.at[square.me], fsend.at[k], frecv.at[k], who)
                for k, who in enumerate(square.others())
            ]
            for copy in rows:
                copy.start()
            fgot[square.me] = sq_ref[...]
            move(0).wait()
            move(1).wait()
            for c in range(slices):
                value = mm(scaled[...], wout[c * SLICE : (c + 1) * SLICE, :], NT).astype(BF16)
                opart[2 * c] = value[:half]
                opart[2 * c + 1] = value[half:]
                outs.step(0, c)
            outs.step(1, 0)
            for copy in rows:
                copy.wait()
            total = (fgot[0] + fgot[1]) + (fgot[2] + fgot[3])
        else:
            move(7).wait()
            job.start(3)
            total = sq_ref[...]
            move(0).wait()
            move(1).wait()
        dcp_ref[...] = jnp.zeros_like(dcp_ref)
        dsp_ref[...] = jnp.zeros_like(dsp_ref)
        dhp_ref[...] = jnp.zeros_like(dhp_ref)
        dgain_ref[...] = jnp.zeros_like(dgain_ref)
        frow[...] = lax.rsqrt(total / INNER + EPS)

    ind = ind_ref[...]
    for at, j, m in folds:
        @pl.when(i == at)
        def _(j=j, m=m):
            job.fold(j, m)

    @pl.when(i < begin_gate)
    def _():
        rows = pl.ds(pl.multiple_of(i * n, n), n)
        low = (column(frow[i]) * up_ref[...].astype(F32)).astype(BF16)
        turned[:, rows] = low.T
        sd = mm(low, wout[...])
        dy[rows, :] = sd
        piece = scaled[rows, :]
        srow[i] = rowsum(piece.astype(F32) * sd)

    @pl.when(i == begin_gate - 1)
    def _():
        copies = [
            remote(srow, sgot.at[square.me], rsend.at[k], rrecv.at[k], who) for k, who in enumerate(square.others())
        ]
        for copy in copies:
            copy.start()
        job.emit(0, turned, scaled)
        move(3).start()
        sgot[square.me] = srow[...]
        for copy in copies:
            copy.wait()
        srow[...] = (sgot[0] + sgot[1]) + (sgot[2] + sgot[3])

    if last:
        @pl.when(i == steps // 2)
        def _():
            outs.step(1, 1)

        @pl.when((i >= begin_gate) & (i < begin_gate + slices - 2))
        def _():
            outs.step(1, i - begin_gate + 2)

    @pl.when((i >= begin_gate) & (i < begin_scan))
    def _():
        c = i - begin_gate
        rows = pl.ds(pl.multiple_of(c * n, n), n)
        coef = column(frow[c] * frow[c] * srow[c]) / INNER
        gate = gate_ref[...]
        gsig = sigmoid(gate)
        gact = gate * gsig
        ssd = ssd_ref[...]
        sd = dy[rows, :]
        gated = ssd * gact
        gd = cp_ref[5:6, :] * sd - coef * gated
        dcp_ref[5:6, :] += colsum(gated * sd)
        dy[rows, :] = gd * gact
        glow[rows, :] = (gd * ssd * (gsig + gact * (1.0 - gsig))).astype(BF16)

    @pl.when(i == begin_scan - 1)
    def _():
        move(3).wait()
        job.emit(1, turned, glow)
        move(2).wait()

    @pl.when((i >= begin_scan) & (i < begin_norm))
    def _():
        q = i - begin_scan
        chunk = steps - 1 - q
        where = pl.ds(pl.multiple_of(chunk * n, n), n)

        @pl.when(lax.rem(chunk, per) == per - 1)
        def _():
            cde[n : n + 8, :] = jnp.zeros((8, cde.shape[1]), F32)
            cdes[n : n + 8, :] = jnp.zeros((8, cdes.shape[1]), F32)
            dstate[...] = jnp.zeros_like(dstate)

        keep = jnp.where(lax.rem(chunk, per) == 0, 0.0, 1.0).astype(F32)
        rows, cols = iotas(n)
        ext[0:8, :] = iprev_ref[...] * keep
        ext[8 : 8 + n, :] = inner_ref[...]
        exts[0:8, :] = sprev_ref[:, : 2 * STATE] * keep
        exts[8 : 8 + n, :] = small_ref[:, : 2 * STATE]
        pre = conv_pre(ext, cp_ref, n)
        sig = sigmoid(pre)
        x = pre * sig
        slope = sig + x * (1.0 - sig)
        pres = conv_pre(exts, sp_ref, n)
        sigs = sigmoid(pres)
        acts = pres * sigs
        slopes = sigs + acts * (1.0 - sigs)
        bc = acts.astype(BF16)
        key, query = bc[:, :STATE], bc[:, STATE:]
        dyc = dy[where, :]

        raw, step, rate, cs, wide_step, wide_cs, wide_tail = scan_prep(small_ref, hp_ref, ind, n)
        cs2 = cs * LOG2E
        cs2t = cs2.T
        xs = x * wide_step
        xsb = xs.astype(BF16)
        dyb = dyc.astype(BF16)
        lane = lax.broadcasted_iota(jnp.int32, (1, xs.shape[1]), 1)
        half = jnp.where(lax.rem(lane, 2 * HEAD) < HEAD, 1.0, 0.0).astype(BF16)
        dy0 = dyb * half
        dy1 = dyb - dy0
        low = st_ref[0]
        dst = dstate[...]
        dlow = dst.astype(BF16)
        dye = dyc * wide_cs
        dyeb = dye.astype(BF16)
        up = headsum(dye * mm(query, low), ind)
        dxs_state = wide_tail * mm(key, dlow)
        down = headsum(xs * dxs_state, ind)
        qdel = mm(dyeb, low, NT)
        kdel = mm((xs * wide_tail).astype(BF16), dlow, NT)
        through = headsum(jnp.broadcast_to(colsum(low.astype(F32) * dst), (8, dst.shape[1])), ind)[0:1, :]
        through = through * jnp.exp(cs[n - 1 : n, :])
        dstate[...] = dst * wide_cs[n - 1 : n, :] + mm(query, dyeb, TN)

        scores = jnp.where(rows <= cols, mm(key, query, NT), 0.0)
        dscores = jnp.zeros((n, n), F32)
        colq = jnp.zeros((n, LANES), F32)
        lane = lax.broadcasted_iota(jnp.int32, (n, LANES), 1)
        dxs = []
        for pair in range(heads // 2):
            lanes = slice(pair * 2 * HEAD, (pair + 1) * 2 * HEAD)
            stacked = jnp.concatenate([dy0[:, lanes], dy1[:, lanes]], axis=0)
            both = mm(xsb[:, lanes], stacked, NT)
            mats = []
            for which, h in enumerate((2 * pair, 2 * pair + 1)):
                dec = jnp.exp2(jnp.minimum(cs2t[h : h + 1, :] - cs2[:, h : h + 1], 0.0))
                mats.append((scores * dec).astype(BF16))
                term = dec * both[:, which * n : (which + 1) * n]
                dscores = dscores + term
                quad = scores * term
                rq[h : h + 1, :] = colsum(quad)
                colq = jnp.where(lane == h, jnp.sum(quad, axis=1, keepdims=True), colq)
            dxs.append(mm(jnp.concatenate(mats, axis=1), stacked))
        dxs = jnp.concatenate(dxs, axis=1) + dxs_state
        dscores = jnp.where(rows <= cols, dscores, 0.0).astype(BF16)
        kdel = kdel + mm(dscores, query)
        qdel = qdel + mm(dscores, key, TN)

        upper = jnp.where(rows <= cols, 1.0, 0.0).astype(F32)
        strict = jnp.where(rows > cols, 1.0, 0.0).astype(F32)
        da = mm(upper, rq[...].T - colq + up, precision=HIGH) + mm(strict, down, precision=HIGH) + through
        grown = headsum(x * dxs, ind) + rate * da
        step_pre = grown * sigmoid(raw)
        steplow = step_pre.astype(BF16)
        if last:
            steplow_ref[...] = steplow
        else:
            step_all[where, :] = steplow
        dhp_ref[0:1, :] += colsum(step_pre)
        dhp_ref[1:2, :] += rate * colsum(step * da)
        dcp_ref[6:7, :] += colsum(dyc * x)

        cd = (dxs * wide_step + cp_ref[6:7, :] * dyc) * slope
        cde[0:n, :] = cd
        center = ext[8 : 8 + n, :]
        total = cp_ref[3:4, :] * cd
        dcp_ref[3:4, :] += colsum(cd * center)
        for tap in range(3):
            shifted = cde[3 - tap : 3 - tap + n, :]
            total = total + cp_ref[tap : tap + 1, :] * shifted
            dcp_ref[tap : tap + 1, :] += colsum(shifted * center)
        inner_low = total.astype(BF16)
        ilow[where, :] = inner_low
        dcp_ref[4:5, :] += colsum(cd)
        cde[n : n + 8, :] = cde[0:8, :]

        cds = jnp.concatenate([kdel, qdel], axis=1) * slopes
        cdes[0:n, :] = cds
        center = exts[8 : 8 + n, :]
        total = sp_ref[3:4, :] * cds
        dsp_ref[3:4, :] += colsum(cds * center)
        for tap in range(3):
            shifted = cdes[3 - tap : 3 - tap + n, :]
            total = total + sp_ref[tap : tap + 1, :] * shifted
            dsp_ref[tap : tap + 1, :] += colsum(shifted * center)
        sdel = total.astype(BF16)
        dsp_ref[4:5, :] += colsum(cds)
        cdes[n : n + 8, :] = cdes[0:8, :]

        lows = jnp.concatenate([inner_low, glow[where, :], sdel, steplow], axis=1)
        value = mm(lows, wt[...]).astype(BF16)
        tpart[2 * q, :, :model] = value[: n // 2]
        tpart[2 * q + 1, :, :model] = value[n // 2 :]
        tpart[2 * q, :, model:] = sdel[: n // 2]
        tpart[2 * q + 1, :, model:] = sdel[n // 2 :]
        sums.step(0, q)

    @pl.when((i > begin_scan) & (i <= begin_norm))
    def _():
        sums.step(1, i - begin_scan - 1)

    @pl.when((i >= begin_scan + 5) & (i < begin_norm + 5))
    def _():
        sums.step(2, i - begin_scan - 5)

    @pl.when((i >= begin_scan + 6) & (i < begin_norm + 6))
    def _():
        sums.step(3, i - begin_scan - 6)

    if last:
        @pl.when((i > begin_scan) & (i <= begin_scan + slices))
        def _():
            outs.step(2, i - begin_scan - 1)

        @pl.when((i > begin_scan + 1) & (i <= begin_scan + slices + 1))
        def _():
            outs.step(3, i - begin_scan - 2)

    @pl.when(i == begin_norm - 1)
    def _():
        dhp_ref[2:3, :] = headsum(jnp.broadcast_to(dcp_ref[6:7, :], (8, dcp_ref.shape[1])), ind)[0:1, :]
        if last:
            job.product(held, turned, ilow)
            move(4).start()
        else:
            job.emit(2, turned, ilow, places // 2)
            for k in (4, 5, 6):
                move(k).start()

    if not last:
        @pl.when(i == begin_norm + 1)
        def _():
            for k in (4, 5, 6):
                move(k).wait()
            put_pack(
                buffers[0].at[1], square.me, *spots, next_dcp[...], next_dsp[...], next_dhp[...], next_dgain[...]
            )
            minis.sum.start(1)

    @pl.when(i >= begin_norm)
    def _():
        r = i - begin_norm
        chunk = steps - 1 - r
        if last:
            fac = column(frow[chunk])
            side = chunk // (steps // 2)
            base = (chunk - side * (steps // 2)) * n
        for h in range(2):
            rows = slice(h * (n // 2), (h + 1) * (n // 2))
            back = tpart[2 * r + h, :, :model].astype(F32)
            sdel = tpart[2 * r + h, :, model:]
            if last:
                sdsum_ref[rows, :] = sdel
            else:
                sd_all[pl.ds(pl.multiple_of(chunk * n + h * (n // 2), n // 2), n // 2), :] = sdel
            res = res_ref[rows, :].astype(F32)
            rn = rn_ref[rows, :]
            dgain_ref[...] += colsum(back * res * rn)
            gained = back * gain_ref[layer : layer + 1, :]
            mean = jnp.sum(gained * res, axis=1, keepdims=True) / model
            new_ref[rows, :] = up_ref[rows, :].astype(F32) + rn * gained - (rn * rn * rn * mean) * res
            if last:
                where = pl.ds(pl.multiple_of(base + h * (n // 2), n // 2), n // 2)
                for c in range(slices):
                    span = slice(c * SLICE, (c + 1) * SLICE)
                    summed = opart[2 * c + side, where, :].astype(F32)
                    mixed_ref[rows, span] = (res[:, span] + fac[rows, :] * summed).astype(BF16)

    @pl.when(i == end)
    def _():
        def finish(j):
            job.finish(j)
            pltpu.make_async_copy(dy.at[pl.ds(j * rows_own, rows_own), :], grad_hbm.at[j], gsem.at[j]).start()

        if not last:
            put_pack(
                buffers[0].at[0], square.me, turned, step_all, sd_all, dcp_ref[...], dsp_ref[...], dhp_ref[...], dgain_ref[...]
            )
            minis.sum.start(0)
            for m in range(places // 2, places - 1):
                job.lead(2, m)
            for m in range(places // 2):
                job.fold(2, m)
            finish(3)
        finish(0)
        finish(1)
        if not last:
            minis.fold()
            minis.turn()
            for k in range(1, line.n):
                minis.relay(k)
            job.lead(2, places - 1)
            for m in range(places // 2, places):
                job.fold(2, m)
            minis.cross()
            finish(2)
            minis.cross_on()
            minis.end()
            tails = [
                pltpu.make_async_copy(src, dst, load.at[k])
                for k, (src, dst) in enumerate(((minis.full, full_hbm), (minis.wide, wide_hbm)))
            ]
            for copy in tails:
                copy.start()
        for j in range(count):
            job.drain(j)
            pltpu.make_async_copy(dy.at[pl.ds(j * rows_own, rows_own), :], grad_hbm.at[j], gsem.at[j]).wait()
        if last:
            move(4).wait()
        else:
            for copy in tails:
                copy.wait()


def back(up, sq, gate_pre, ssd, inner_raw, small, states, res, rnorm, gain, params,
         wout, scaled, wt, normed, heads, size, layer, after=None):
    tokens_n, width = inner_raw.shape
    model = up.shape[1]
    last = after is None
    steps = tokens_n // CHUNK
    begin_scan = 2 * steps
    begin_norm = begin_scan + steps
    rows = model // size
    n = size // 2
    hbm = pl.BlockSpec(memory_space=pl.ANY)
    top = steps - 1

    def norm_at(i):
        return jnp.where(i < begin_norm, top, top - (i - begin_norm))

    def scan_at(i):
        return jnp.clip(top - (i - begin_scan), 0, top)

    def first(w):
        return pl.BlockSpec((CHUNK, w), lambda i: (jnp.where(i < steps, i, norm_at(i)), 0))

    def second(w):
        return pl.BlockSpec((CHUNK, w), lambda i: (jnp.clip(i - steps, 0, top), 0))

    def scan(w):
        return pl.BlockSpec((CHUNK, w), lambda i: (scan_at(i), 0))

    def prev(w):
        return pl.BlockSpec((8, w), lambda i: (jnp.maximum(scan_at(i) * (CHUNK // 8) - 1, 0), 0))

    def norm(w):
        return pl.BlockSpec((CHUNK, w), lambda i: (norm_at(i), 0))

    def whole(a):
        return pl.BlockSpec(a.shape, lambda i: (0,) * len(a.shape))

    extra = model + 2 * STATE
    quarter = pltpu.VMEM((steps, CHUNK // 2, extra), BF16)
    count = 2 if last else 4
    pieces = pltpu.VMEM((count, n, rows, width), BF16)
    args = [up, sq, gate_pre, ssd, inner_raw, inner_raw, small, small, states, res, rnorm, gain, *params,
            wout, scaled, wt, normed]
    in_specs = [
        first(model), whole(sq), second(width), second(width),
        scan(width), prev(width), scan(small.shape[1]), prev(small.shape[1]),
        pl.BlockSpec((1, STATE, width), lambda i: (scan_at(i), 0, 0)),
        norm(model), norm(1), whole(gain),
    ] + [whole(a) for a in params] + [hbm] * 4
    out_specs = [norm(model), hbm]
    out_shape = [jax.ShapeDtypeStruct((tokens_n, model), F32), jax.ShapeDtypeStruct((count, rows, width), F32)]
    totals = [(8, width), (8, 2 * STATE), (8, LANES), (1, model)]
    scratch = [
        pltpu.VMEM((CHUNK + 8, width), F32),
        pltpu.VMEM((CHUNK + 8, 2 * STATE), F32),
        pltpu.VMEM((CHUNK + 8, width), F32),
        pltpu.VMEM((CHUNK + 8, 2 * STATE), F32),
        pltpu.VMEM((STATE, width), F32),
        pltpu.VMEM((LANES, CHUNK), F32),
        pltpu.VMEM((8, width), F32),
        pltpu.VMEM((8, 2 * STATE), F32),
        pltpu.VMEM((8, LANES), F32),
        pltpu.VMEM((LANES, width), BF16),
        pltpu.VMEM(wout.shape, BF16),
        pltpu.VMEM(scaled.shape, BF16),
        pltpu.VMEM(wt.shape, BF16),
        pltpu.VMEM(normed.shape, BF16),
        pltpu.VMEM((tokens_n, width), F32),
        pltpu.VMEM((tokens_n, width), BF16),
        pltpu.VMEM((tokens_n, width), BF16),
        pltpu.VMEM((steps, 1, CHUNK), F32),
        pltpu.VMEM((steps, 1, CHUNK), F32),
        pltpu.VMEM((4, steps, 1, CHUNK), F32),
        pltpu.VMEM((count, size, rows, width), BF16), pieces, pieces,
        pltpu.VMEM((2 * steps, CHUNK // 2, extra), BF16), quarter, quarter, quarter,
        pltpu.SemaphoreType.DMA((8,)),
        pltpu.SemaphoreType.DMA((3,)),
        pltpu.SemaphoreType.DMA((3,)),
        pltpu.SemaphoreType.DMA((2, count, n)),
        pltpu.SemaphoreType.DMA((2, count, n)),
        pltpu.SemaphoreType.DMA((3, steps)),
        pltpu.SemaphoreType.DMA((3, steps)),
        pltpu.SemaphoreType.DMA((count,)),
    ]
    if last:
        out_specs += [hbm, norm(2 * STATE), scan(LANES)]
        out_specs += [pl.BlockSpec(v, lambda i: (0, 0)) for v in totals] + [norm(model)]
        out_shape += [
            jax.ShapeDtypeStruct((size, rows, width), BF16),
            jax.ShapeDtypeStruct((tokens_n, 2 * STATE), BF16),
            jax.ShapeDtypeStruct((tokens_n, LANES), BF16),
        ]
        out_shape += [jax.ShapeDtypeStruct(v, F32) for v in totals]
        out_shape.append(jax.ShapeDtypeStruct((tokens_n, model), BF16))
        slices = model // SLICE
        chunk = pltpu.VMEM((slices, tokens_n // 2, SLICE), BF16)
        scratch += [
            pltpu.VMEM((size, rows, width), BF16),
            pltpu.VMEM((4, steps, 1, CHUNK), F32),
            pltpu.VMEM((2 * slices, tokens_n // 2, SLICE), BF16), chunk, chunk, chunk,
            pltpu.SemaphoreType.DMA((3,)),
            pltpu.SemaphoreType.DMA((3,)),
            pltpu.SemaphoreType.DMA((3, slices)),
            pltpu.SemaphoreType.DMA((3, slices)),
        ]
    else:
        w = 2 * STATE
        r = pack_rows(size)
        args += list(after)
        in_specs += [hbm] * 4 + [whole(v) for v in after[4:]]
        out_specs += [hbm, hbm]
        out_shape += [
            jax.ShapeDtypeStruct((2, size, r, w), BF16),
            jax.ShapeDtypeStruct((4, 2, SPAN, w), BF16),
        ]
        scratch += [pltpu.VMEM(v, F32) for v in totals]
        scratch += smalls_scratch(size, w, 2)
    return pl.pallas_call(
        functools.partial(
            back_body, heads=heads, per=LEN // CHUNK, size=size, steps=steps, layer=layer, last=last
        ),
        grid=(begin_norm + steps,),
        in_specs=in_specs,
        out_specs=out_specs,
        out_shape=out_shape,
        scratch_shapes=scratch,
        compiler_params=pltpu.CompilerParams(
            collective_id=2 if last else 3, has_side_effects=True, vmem_limit_bytes=VMEM_LIMIT
        ),
        name="back",
    )(*args)


def results_body(full_ref, wide_ref, first_hbm, second_hbm, mixed_hbm, up_hbm, *refs, layers, heads):
    pair_out, out_out, mixed_out, up_out = refs[11:15]
    first, second, mixed, up, load, store = refs[15:]
    refs = refs[:11]
    loads = [
        pltpu.make_async_copy(src, dst, load.at[k])
        for k, (src, dst) in enumerate(((up_hbm, up), (mixed_hbm, mixed), (first_hbm, first), (second_hbm, second)))
    ]
    for copy in loads:
        copy.start()
    step_ref, state_ref, conv_ref, bias_ref, convs_ref, biass_ref = refs[:6]
    stepbias_ref, decay_ref, skip_ref, norm_ref, gain_ref = refs[6:]
    model = state_ref.shape[1]
    quarter = model // 4
    w = state_ref.shape[2]
    width = conv_ref.shape[2]
    for layer in range(layers):
        for t in range(4):
            state_ref[layer, t * quarter : (t + 1) * quarter, :] = wide_ref[t, layer, :quarter, :].astype(F32)
        taps = [wide_ref[t, layer, quarter : quarter + 16, :].astype(F32) for t in range(4)]
        taps = (taps[0] + taps[1]) + (taps[2] + taps[3])
        convs_ref[layer] = taps[0:4]
        biass_ref[layer : layer + 1, :] = taps[4:5]
        flat = full_ref[layer].reshape(-1, w)[:PACK].astype(F32)
        at = quarter + 16
        for b in range(model // w):
            step_ref[layer, :, b * w : (b + 1) * w] = flat[at : at + 16]
            at += 16
        for b in range(width // w):
            lanes = slice(b * w, (b + 1) * w)
            rows = flat[at + 8 * b : at + 8 * b + 8]
            conv_ref[layer, :, lanes] = rows[0:4]
            bias_ref[layer : layer + 1, lanes] = rows[4:5]
            norm_ref[layer : layer + 1, lanes] = rows[5:6]
        at += 8 * (width // w)
        for k, ref in enumerate((stepbias_ref, decay_ref, skip_ref)):
            ref[layer : layer + 1, :] = flat[at + k : at + k + 1, :heads]
        at += 8
        for b in range(model // w):
            gain_ref[layer : layer + 1, b * w : (b + 1) * w] = flat[at + b : at + b + 1]
    for copy in loads:
        copy.wait()
    moves = [
        (up, up_out), (mixed, mixed_out), (first.at[pl.ds(1, 2)], pair_out.at[0]), (second.at[1], pair_out.at[1, 0]),
        (first.at[3], pair_out.at[1, 1]), (first.at[0], out_out.at[0]), (second.at[0], out_out.at[1]),
    ]
    stores = [pltpu.make_async_copy(src, dst, store.at[k]) for k, (src, dst) in enumerate(moves)]
    for copy in stores:
        copy.start()
    for copy in stores:
        copy.wait()


def write_results(full, wide, first, second, mixed, up, heads):
    layers, w = full.shape[0], full.shape[3]
    _, rows, width = first.shape
    model = up.shape[1]
    vm = pl.BlockSpec(memory_space=pltpu.VMEM)
    hbm = pl.BlockSpec(memory_space=pl.ANY)
    shapes = [
        (layers, 16, model), (layers, model, w), (layers, 4, width), (layers, width), (layers, 4, w), (layers, w),
        (layers, heads), (layers, heads), (layers, heads), (layers, width), (layers, model),
    ]
    return pl.pallas_call(
        functools.partial(results_body, layers=layers, heads=heads),
        in_specs=[vm, vm] + [hbm] * 4,
        out_specs=[vm] * len(shapes) + [hbm] * 4,
        out_shape=[jax.ShapeDtypeStruct(v, F32) for v in shapes] + [
            jax.ShapeDtypeStruct((layers, 2, rows, width), F32),
            jax.ShapeDtypeStruct((layers, rows, width), F32),
            jax.ShapeDtypeStruct(mixed.shape, mixed.dtype),
            jax.ShapeDtypeStruct(up.shape, up.dtype),
        ],
        scratch_shapes=[
            pltpu.VMEM(first.shape, F32),
            pltpu.VMEM(second.shape, F32),
            pltpu.VMEM(mixed.shape, mixed.dtype),
            pltpu.VMEM(up.shape, up.dtype),
            pltpu.SemaphoreType.DMA((4,)),
            pltpu.SemaphoreType.DMA((7,)),
        ],
        compiler_params=pltpu.CompilerParams(vmem_limit_bytes=VMEM_LIMIT),
        name="results",
    )(full, wide, first, second, mixed, up)


def shards(
    tokens, inproj, stepproj, stateproj, outproj, convinner, biasinner, convstate, biasstate,
    stepbias, decaylog, skipgain, normgain, inputgain, cotangent,
):
    layers = inproj.shape[0]
    width = inproj.shape[3]
    heads = stepproj.shape[2]
    model = tokens.shape[1]
    pad = LANES - heads
    size = lax.axis_size("dp")
    steps_w = jnp.pad(jnp.swapaxes(stepproj, 1, 2), ((0, 0), (0, pad), (0, 0)))
    head = jnp.pad(jnp.stack([stepbias, decaylog, skipgain], axis=1), ((0, 0), (0, 5), (0, pad)))
    outt = jnp.swapaxes(outproj, 1, 2)
    params = (convinner, biasinner, normgain, convstate, biasstate, head)

    residual = tokens
    kept = []
    out = None
    for at in range(layers):
        results = forward(residual, stateproj, steps_w, inproj, outt, inputgain, params, heads, size, at, out=out)
        if at:
            residual, kept[-1][-1] = results[:2]
            results = results[2:]
        normed, rnorm, small, inner_raw, gate_pre, wt, w_out, ssd, scaled, sq, states = results
        w_out = w_out.reshape(model, width)
        kept.append([residual, normed, rnorm, small, inner_raw, gate_pre, wt, w_out, ssd, scaled, states, sq])
        out = (scaled, w_out, sq)

    assert layers == 2
    before, normed, rnorm, small, inner_raw, gate_pre, wt, w_out, ssd, scaled, states, sq = kept[1]
    upstream, second, held, sdel, steplow, *totals, mixed = back(
        cotangent, sq, gate_pre, ssd, inner_raw, small, states, before, rnorm, inputgain, params,
        w_out, scaled, wt, normed, heads, size, 1,
    )
    after = (normed, steplow, sdel, held, *totals)
    before, normed, rnorm, small, inner_raw, gate_pre, wt, w_out, ssd, scaled, states, sq = kept[0]
    upstream, first, full, wide = back(
        upstream, sq, gate_pre, ssd, inner_raw, small, states, before, rnorm, inputgain, params,
        w_out, scaled, wt, normed, heads, size, 0, after=after,
    )
    (
        step_grad, state_grad, conv_grad, bias_grad, convs_grad, biass_grad,
        stepbias_grad, decay_grad, skip_grad, norm_grad, gain_grad, pair_grad, out_grad, mixed, upstream,
    ) = write_results(full, wide, first, second, mixed, upstream, heads)
    return (
        mixed,
        upstream,
        pair_grad,
        jnp.swapaxes(step_grad[:, :heads], 1, 2),
        state_grad,
        jnp.swapaxes(out_grad, 1, 2),
        conv_grad,
        bias_grad,
        convs_grad,
        biass_grad,
        stepbias_grad,
        decay_grad,
        skip_grad,
        norm_grad,
        gain_grad,
    )


def solution(mesh):
    in_specs = (
        P("dp", None),
        P(None, None, "dp", "tensor"),
        P(None, None, "tensor"),
        P(),
        P(None, "tensor", "dp"),
        P(None, None, "tensor"),
        P(None, "tensor"),
        P(),
        P(),
        P(None, "tensor"),
        P(None, "tensor"),
        P(None, "tensor"),
        P(None, "tensor"),
        P(),
        P("dp", None),
    )
    out_specs = (
        P("dp", None),
        P("dp", None),
        P(None, None, "dp", "tensor"),
        P(None, None, "tensor"),
        P(),
        P(None, "tensor", "dp"),
        P(None, None, "tensor"),
        P(None, "tensor"),
        P(),
        P(),
        P(None, "tensor"),
        P(None, "tensor"),
        P(None, "tensor"),
        P(None, "tensor"),
        P(),
    )
    return jax.shard_map(shards, mesh=mesh, in_specs=in_specs, out_specs=out_specs, check_vma=False)
```

```python
import functools
import math

import jax
import jax.numpy as jnp
from jax import lax
from jax.experimental import pallas as pl
from jax.experimental.pallas import tpu as pltpu
from jax.sharding import PartitionSpec as P

STATE = 128
LEN = 1024
INNER = 3072
HEAD = 64
CHUNK = 128
SLICE = 256
TILE = 256
PACK = 544
SPAN = 400
VMEM_LIMIT = 65000 * 1024
LANES = 128
EPS = 1e-05
LOG2E = 1.4426950408889634

HIGH = lax.Precision.HIGHEST
NN = (((1,), (0,)), ((), ()))
NT = (((1,), (1,)), ((), ()))
TN = (((0,), (0,)), ((), ()))
F32 = jnp.float32
BF16 = jnp.bfloat16
MESH = pl.DeviceIdType.MESH


def remote(src, dst, send, recv, where):
    return pltpu.make_async_remote_copy(
        src_ref=src, dst_ref=dst, send_sem=send, recv_sem=recv, device_id=where, device_id_type=MESH
    )


class Line:
    def __init__(self, size):
        self.n = size // 2
        me = lax.axis_index("dp")
        self.me = me
        self.at = me // 2
        self.side = lax.rem(me, 2)
        self.pair = {"dp": me + 1 - 2 * self.side}
        self.right = {"dp": jnp.minimum(me + 2, size - 1)}
        self.left = {"dp": jnp.maximum(me - 2, 0)}
        odd = lax.rem(self.at, 2)
        self.odd = odd == 1
        self.near = {"dp": me + 2 - 4 * odd}
        self.has_left = self.at > 0
        self.has_right = self.at < self.n - 1

    def greet(self, barrier, more=()):
        for who in more:
            pl.semaphore_signal(barrier, inc=1, device_id=who, device_id_type=MESH)
        pl.semaphore_signal(barrier, inc=1, device_id=self.pair, device_id_type=MESH)

        @pl.when(self.has_left)
        def _():
            pl.semaphore_signal(barrier, inc=1, device_id=self.left, device_id_type=MESH)

        @pl.when(self.has_right)
        def _():
            pl.semaphore_signal(barrier, inc=1, device_id=self.right, device_id_type=MESH)

        peers = 1 + len(more) + self.has_left.astype(jnp.int32) + self.has_right.astype(jnp.int32)
        pl.semaphore_wait(barrier, peers)

    def greet_all(self, barrier, more=()):
        for who in list(more) + [self.pair]:
            pl.semaphore_signal(barrier, inc=1, device_id=who, device_id_type=MESH)
        for i in range(self.n):
            @pl.when(i != self.at)
            def _(i=i):
                pl.semaphore_signal(barrier, inc=1, device_id={"dp": 2 * i + self.side}, device_id_type=MESH)
        pl.semaphore_wait(barrier, self.n + len(more))


def upper(rows):
    return max(16, rows // 32 * 16)


class Gather:
    def __init__(self, line, own, full, keep, send, recv):
        self.line, self.own, self.full, self.keep, self.send, self.recv = line, own, full, keep, send, recv
        self.rows = full.shape[2]
        self.cut = upper(self.rows)

    def copy(self, j, slab, way, src=None, rest=False):
        where = (self.line.right, self.line.left, self.line.pair)[way]
        dst = self.full.at[j, slab]
        if rest:
            dst = self.full.at[j, slab, pl.ds(self.cut, self.rows - self.cut)]
        return remote(dst if src is None else src, dst, self.send.at[j, way, slab], self.recv.at[j, slab], where)

    def shared(self, j, slab, owner):
        part = self.full.at[j, slab, pl.ds(0, self.cut)]
        return remote(part, part, self.send.at[j, 0, slab], self.recv.at[j, owner], self.line.near)

    def start(self, j):
        line = self.line
        pltpu.make_async_copy(self.own(j), self.full.at[j, line.me], self.keep.at[j]).start()

        @pl.when(line.has_right)
        def _():
            self.copy(j, line.me, 0, self.own(j)).start()

        @pl.when(line.has_left)
        def _():
            self.copy(j, line.me, 1, self.own(j)).start()

        self.copy(j, line.me, 2, self.own(j)).start()

    def relay(self, j, k):
        line = self.line

        def forward(slab, way, go_on, near):
            self.copy(j, slab, way).wait_recv()

            @pl.when(go_on)
            def _():
                self.copy(j, slab, way).start()

            if k > 1:
                self.copy(j, slab, 2).start()
            else:
                @pl.when(near)
                def _():
                    self.copy(j, slab, 2, rest=True).start()

                @pl.when(jnp.logical_not(near))
                def _():
                    self.copy(j, slab, 2).start()

        @pl.when(line.at >= k)
        def _():
            forward(line.me - 2 * k, 0, line.has_right, line.odd)

        @pl.when(line.at + k < line.n)
        def _():
            forward(line.me + 2 * k, 1, line.has_left, jnp.logical_not(line.odd))

        if k == 1:
            slab = line.me + 1 - 2 * line.side
            self.copy(j, slab, 2).wait_recv()
            self.shared(j, slab, line.near["dp"]).start()

    def near_slab(self):
        line = self.line
        return line.near["dp"] + 1 - 2 * line.side

    def arrive(self, j):
        line = self.line
        pltpu.make_async_copy(self.own(j), self.full.at[j, line.me], self.keep.at[j]).wait()
        self.copy(j, self.near_slab(), 2, rest=True).wait_recv()
        self.shared(j, self.near_slab(), line.me).wait_recv()
        for place in range(line.n):
            slab = 2 * place + 1 - line.side

            @pl.when((slab != self.near_slab()) & (place != line.at))
            def _(slab=slab):
                self.copy(j, slab, 2).wait_recv()

    def drain(self, j):
        line = self.line
        self.shared(j, line.me + 1 - 2 * line.side, line.near["dp"]).wait_send()
        for place in range(line.n):
            slab = 2 * place + line.side
            near = slab == line.near["dp"]

            @pl.when(near)
            def _(slab=slab):
                self.copy(j, slab, 2, rest=True).wait_send()

            @pl.when(jnp.logical_not(near))
            def _(slab=slab):
                self.copy(j, slab, 2).wait_send()

            @pl.when(line.has_right & (place <= line.at))
            def _(slab=slab):
                self.copy(j, slab, 0).wait_send()

            @pl.when(line.has_left & (place >= line.at))
            def _(slab=slab):
                self.copy(j, slab, 1).wait_send()


class Square:
    def __init__(self):
        me = lax.axis_index("tensor")
        self.me = me
        self.half = lax.rem(me, 2)
        self.mate = {"tensor": me + 1 - 2 * self.half}
        self.across = {"tensor": lax.rem(me + 2, 4)}

    def others(self):
        return [{"tensor": lax.rem(self.me + k, 4)} for k in (1, 2, 3)]


class Total:
    def __init__(self, square, part, got, far, other, send, recv):
        self.square, self.part, self.got, self.far, self.other = square, part, got, far, other
        self.send, self.recv = send, recv

    def first(self, c):
        sq = self.square
        return remote(
            self.part.at[2 * c + 1 - sq.half], self.got.at[c], self.send.at[0, c], self.recv.at[0, c], sq.mate
        )

    def second(self, c):
        sq = self.square
        return remote(self.part.at[2 * c + sq.half], self.far.at[c], self.send.at[1, c], self.recv.at[1, c], sq.across)

    def third(self, c):
        sq = self.square
        return remote(self.part.at[2 * c + sq.half], self.other.at[c], self.send.at[2, c], self.recv.at[2, c], sq.mate)

    def step(self, kind, c):
        slot = 2 * c + self.square.half
        if kind == 0:
            self.first(c).start()
        elif kind == 1:
            self.first(c).wait_recv()
            self.part[slot] = (self.part[slot].astype(F32) + self.got[c].astype(F32)).astype(BF16)
            self.second(c).start()
        elif kind == 2:
            self.second(c).wait()
            self.part[slot] = (self.part[slot].astype(F32) + self.far[c].astype(F32)).astype(BF16)
            self.third(c).start()
        else:
            self.third(c).wait_recv()
            self.first(c).wait_send()
            self.third(c).wait_send()
            self.part[2 * c + 1 - self.square.half] = self.other[c]


class Scatter:
    def __init__(self, line, part, out, near, far, send, recv):
        self.line, self.part, self.out, self.near, self.far = line, part, out, near, far
        self.send, self.recv = send, recv

    def order(self):
        n = self.line.n
        seq = []
        for i in range((n + 1) // 2):
            seq.append(i)
            if n - 1 - i != i:
                seq.append(n - 1 - i)
        return seq

    def cross(self, j, i):
        line = self.line
        return remote(
            self.part.at[j, 2 * i + 1 - line.side], self.near.at[j, i], self.send.at[0, j, i], self.recv.at[0, j, i], line.pair
        )

    def straight(self, j, i, source):
        line = self.line
        return remote(
            self.part.at[j, 2 * i + line.side], self.far.at[j, source], self.send.at[1, j, i], self.recv.at[1, j, source],
            {"dp": 2 * i + line.side},
        )

    def lead(self, j, m):
        self.cross(j, self.order()[m]).start()

    def start(self, j):
        for m in range(self.line.n):
            self.lead(j, m)

    def emit(self, j, turned, right, now=None):
        rows = self.part.shape[2]
        for m, i in enumerate(self.order()):
            value = mm(turned[2 * i * rows : 2 * (i + 1) * rows, :], right[...]).astype(BF16)
            self.part[j, 2 * i] = value[:rows]
            self.part[j, 2 * i + 1] = value[rows:]
            if now is None or m < now:
                self.lead(j, m)

    def product(self, dst, turned, right):
        rows = dst.shape[1]
        for i in range(self.line.n):
            value = mm(turned[2 * i * rows : 2 * (i + 1) * rows, :], right[...]).astype(BF16)
            dst[2 * i] = value[:rows]
            dst[2 * i + 1] = value[rows:]

    def fold(self, j, m):
        line = self.line
        i = self.order()[m]
        self.cross(j, i).wait_recv()
        slot = 2 * i + line.side
        self.part[j, slot] = (self.part[j, slot].astype(F32) + self.near[j, i].astype(F32)).astype(BF16)

        @pl.when(i != line.at)
        def _():
            self.straight(j, i, line.at).start()

    def finish(self, j):
        line = self.line
        out = self.out(j)
        out[...] = self.part[j, line.me].astype(out.dtype)
        for i in range(line.n):
            @pl.when(i != line.at)
            def _(i=i):
                self.straight(j, i, i).wait_recv()
                out[...] += self.far[j, i].astype(out.dtype)

    def drain(self, j):
        for i in range(self.line.n):
            self.cross(j, i).wait_send()

            @pl.when(i != self.line.at)
            def _(i=i):
                self.straight(j, i, self.line.at).wait_send()


def mm(left, right, dims=NN, precision=None):
    return lax.dot_general(left, right, dims, precision=precision, preferred_element_type=F32)


def sigmoid(v):
    return 0.5 * jnp.tanh(0.5 * v) + 0.5


def softplus(v):
    return jnp.maximum(v, 0.0) + jnp.log1p(jnp.exp(-jnp.abs(v)))


def split16(v):
    top = v.astype(BF16)
    return top, (v - top.astype(F32)).astype(BF16)


def expand(v, ind):
    top, rest = split16(v)
    return mm(top, ind) + mm(rest, ind)


def headsum(v, ind):
    return mm(v.astype(BF16), ind, NT)


def rowsum(v):
    return mm(jnp.ones((8, v.shape[1]), BF16), v.astype(BF16), NT)[0:1, :]


def iotas(n):
    return (
        lax.broadcasted_iota(jnp.int32, (n, n), 0),
        lax.broadcasted_iota(jnp.int32, (n, n), 1),
    )


def colsum(v):
    return jnp.sum(v, axis=0, keepdims=True)


def conv_pre(ext, par, n):
    total = par[4:5, :] + par[0:1, :] * ext[5 : 5 + n, :]
    for tap in range(1, 4):
        total = total + par[tap : tap + 1, :] * ext[5 + tap : 5 + tap + n, :]
    return total


def scan_prep(small, hp, ind, n):
    rows, cols = iotas(n)
    raw = small[:, 2 * STATE :] + hp[0:1, :]
    step = softplus(raw)
    rate = -jnp.exp(hp[1:2, :])
    lower = jnp.where(rows >= cols, 1.0, 0.0).astype(F32)
    cs = mm(lower, step * rate, precision=HIGH)
    tail = jnp.exp(cs[n - 1 : n, :] - cs)
    wide = mm(jnp.concatenate([step, jnp.exp(cs), tail], axis=0).astype(BF16), ind)
    return raw, step, rate, cs, wide[0:n], wide[n : 2 * n], wide[2 * n : 3 * n]


def block_of(slabs, at, rows):
    step = math.gcd(LANES, rows)
    pieces = []
    for k in range(LANES // step):
        row = at * LANES + k * step
        slab = row // rows
        pieces.append(slabs[slab, pl.ds(pl.multiple_of(row - slab * rows, step), step), :])
    return pieces[0] if len(pieces) == 1 else jnp.concatenate(pieces, axis=0)


def put_params(cp, sp, hp, ind, layer, params):
    conv, bias, norm, convs, biass, head = params
    width = cp.shape[1]
    row = lax.broadcasted_iota(jnp.int32, (LANES, width), 0)
    lane = lax.broadcasted_iota(jnp.int32, (LANES, width), 1)
    ind[...] = jnp.where(lane // HEAD == row, 1.0, 0.0).astype(BF16)
    hp[...] = head[layer]
    cp[0:4, :] = conv[layer]
    cp[4:5, :] = bias[layer : layer + 1, :]
    cp[5:6, :] = norm[layer : layer + 1, :]
    cp[6:8, :] = expand(hp[...], ind[...])[2:4, :]
    sp[0:4, :] = convs[layer]
    sp[4:5, :] = biass[layer : layer + 1, :]


def place_rows(dst, at, value):
    r = dst.shape[1]
    for g in range(0, value.shape[0], 16):
        dst[(at + g) // r, (at + g) % r : (at + g) % r + 16, :] = value[g : g + 16].astype(dst.dtype)


def pack_rows(size):
    return -(-PACK // (16 * size)) * 16


def put_pack(dst, me, turned, steps_low, sdel, dcp, dsp, dhp, dgain):
    model = turned.shape[0]
    quarter = model // 4
    w = sdel.shape[1]

    def empty(n):
        return jnp.zeros((n, w), F32)

    place_rows(dst, 0, mm(turned[pl.ds(pl.multiple_of(me * quarter, quarter), quarter), :], sdel[...]))
    place_rows(dst, quarter, jnp.concatenate([dsp, empty(8)], axis=0))
    grown = mm(turned[...], steps_low[...]).T[:16]
    at = quarter + 16
    for b in range(model // w):
        place_rows(dst, at, grown[:, b * w : (b + 1) * w])
        at += 16
    place_rows(dst, at, jnp.concatenate([dcp[:, :w], dcp[:, w : 2 * w]], axis=0))
    place_rows(dst, at + 16, jnp.concatenate([dcp[:, 2 * w :], jnp.concatenate([dhp, dhp], axis=1)], axis=0))
    rows = [dgain[:, b * w : (b + 1) * w] for b in range(model // w)]
    place_rows(dst, at + 32, jnp.concatenate(rows + [empty(16 - len(rows))], axis=0))
    assert at + 48 == PACK


class Smalls:
    def __init__(self, line, square, pack, near, away, own, full, wide, sems):
        send, recv, keep, gsend, grecv, self.xsend, self.xrecv = sems
        self.square, self.full, self.wide = square, full, wide
        self.layers = range(pack.shape[0])
        self.sum = Scatter(line, pack, lambda j: own.at[j], near, away, send, recv)
        self.spread = Gather(line, lambda j: own.at[j], full, keep, gsend, grecv)

    def swap(self, k):
        sq = self.square
        slot = (sq.me, sq.me, lax.rem(sq.me + 2, 4))[k]
        who = (sq.across, sq.mate, sq.mate)[k]
        return remote(self.wide.at[slot], self.wide.at[slot], self.xsend.at[k], self.xrecv.at[k], who)

    def start(self):
        for j in self.layers:
            self.sum.start(j)

    def fold(self):
        for j in self.layers:
            for m in range(self.sum.line.n):
                self.sum.fold(j, m)

    def turn(self):
        for j in self.layers:
            self.sum.finish(j)
            self.spread.start(j)

    def relay(self, k):
        for j in self.layers:
            self.spread.relay(j, k)

    def cross(self):
        for j in self.layers:
            self.spread.arrive(j)
            flat = self.full[j].reshape(-1, self.full.shape[3])
            self.wide[self.square.me, j] = flat[: self.wide.shape[2]]
        self.swap(0).start()
        self.swap(1).start()

    def cross_on(self):
        self.swap(0).wait_recv()
        self.swap(2).start()

    def end(self):
        self.swap(1).wait_recv()
        self.swap(2).wait_recv()
        for k in range(3):
            self.swap(k).wait_send()
        for j in self.layers:
            self.sum.drain(j)
            self.spread.drain(j)


def smalls_scratch(size, w, layers):
    r, n = pack_rows(size), size // 2
    buffers = [
        pltpu.VMEM((layers, size, r, w), BF16),
        pltpu.VMEM((layers, n, r, w), BF16),
        pltpu.VMEM((layers, n, r, w), BF16),
        pltpu.VMEM((layers, r, w), BF16),
        pltpu.VMEM((layers, size, r, w), BF16),
        pltpu.VMEM((4, layers, SPAN, w), BF16),
    ]
    sems = [
        pltpu.SemaphoreType.DMA((2, layers, n)),
        pltpu.SemaphoreType.DMA((2, layers, n)),
        pltpu.SemaphoreType.DMA((layers,)),
        pltpu.SemaphoreType.DMA((layers, 3, size)),
        pltpu.SemaphoreType.DMA((layers, size)),
        pltpu.SemaphoreType.DMA((3,)),
        pltpu.SemaphoreType.DMA((3,)),
    ]
    return buffers + sems


def forward_body(*refs, size, heads, per, steps, layer):
    refs = list(refs)

    def take(n):
        got = refs[:n]
        del refs[:n]
        return got

    mid = layer > 0
    (res_hbm,) = take(1)
    if mid:
        scaled_hbm, wout_hbm, sq_ref = take(3)
    state_hbm, step_hbm, in_hbm, out_hbm, gain_ref = take(5)
    params = take(6)
    if mid:
        new_hbm, sums_ref = take(2)
    normed_hbm, rnorm_ref, small_hbm, inner_hbm, gate_hbm, wt_hbm, full_hbm, ssd_ref, scaled_ref, sqs_ref, st_ref = take(11)
    if mid:
        scaled_in, wout, part, got, far, other, rows_got, facs, fresh, sends, recvs, rsend, rrecv = take(13)
    res, wstate, wt, slabs, normed, turned, small, inner, gate, ext, exts, state = take(12)
    cp_ref, sp_ref, hp_ref, ind_ref, keep, gsend, grecv, load, sems = take(9)
    assert not refs

    n = CHUNK
    tokens_n, model = res.shape
    width = inner.shape[1]
    top = 2 * width + 2 * STATE
    i = pl.program_id(0)
    line = Line(size)
    square = Square()
    job = Gather(line, lambda j: out_hbm.at[layer] if j == 2 else in_hbm.at[layer, 1 - j], slabs, keep, gsend, grecv)
    outgoing = [(turned, normed_hbm), (small, small_hbm), (inner, inner_hbm), (gate, gate_hbm)]
    outgoing += [(wt, wt_hbm), (slabs.at[2], full_hbm)]
    if mid:
        outgoing.append((fresh, new_hbm))

    def flush(k):
        return pltpu.make_async_copy(*outgoing[k], sems.at[k])


    @pl.when(i == 0)
    def _():
        pairs = [(res_hbm, res), (state_hbm.at[layer], wstate), (step_hbm.at[layer], wt.at[pl.ds(top, LANES), :])]
        if mid:
            pairs = [(scaled_hbm, scaled_in), (wout_hbm, wout)] + pairs
        loads = [pltpu.make_async_copy(src, dst, load.at[k]) for k, (src, dst) in enumerate(pairs)]
        for copy in loads:
            copy.start()
        line.greet(pltpu.get_barrier_semaphore(), square.others() if mid else ())
        job.start(0)
        put_params(cp_ref, sp_ref, hp_ref, ind_ref, layer, params)
        ticks = [functools.partial(job.relay, 0, k) for k in range(1, line.n)]
        ticks.append(functools.partial(job.start, 1))
        span = model // LANES

        def project(j, dst):
            weight = slabs[j].reshape(model, width)

            def tile(t, _):
                rows = pl.ds(pl.multiple_of(t * TILE, TILE), TILE)
                dst[rows, :] = mm(normed[rows, :], weight)
                return 0

            lax.fori_loop(0, tokens_n // TILE, tile, 0)

        def turn_inner(b, _):
            wt[:width, pl.ds(pl.multiple_of(b * LANES, LANES), LANES)] = block_of(slabs.at[0], b, slabs.shape[2]).T
            return 0

        def settle():
            job.arrive(0)
            if not mid:
                project(0, inner)
                flush(2).start()
            lax.fori_loop(0, span, turn_inner, 0)

        ticks.append(functools.partial(job.relay, 1, 1))
        ticks.append(settle)
        ticks += [functools.partial(job.relay, 1, k) for k in range(2, line.n)]
        ticks.append(functools.partial(job.start, 2))

        if mid:
            chunks = model // SLICE
            half = tokens_n // 2
            sums = Total(square, part, got, far, other, sends, recvs)
            copies = [
                remote(sq_ref, rows_got.at[square.me], rsend.at[k], rrecv.at[k], who)
                for k, who in enumerate(square.others())
            ]
            for copy in copies:
                copy.start()
            loads[0].wait()
            loads[1].wait()
            for c in range(chunks):
                value = mm(scaled_in[...], wout[c * SLICE : (c + 1) * SLICE, :], NT).astype(BF16)
                part[2 * c] = value[:half]
                part[2 * c + 1] = value[half:]
                sums.step(0, c)
                if c:
                    sums.step(1, c - 1)
            sums.step(1, chunks - 1)
            rows_got[square.me] = sq_ref[...]
            for copy in copies:
                copy.wait()
            total = (rows_got[0] + rows_got[1]) + (rows_got[2] + rows_got[3])
            sums_ref[...] = total
            factor = lax.rsqrt(total / INNER + EPS)
            for t in range(tokens_n // LANES):
                facs[t * LANES : (t + 1) * LANES, :] = jnp.broadcast_to(factor[t], (LANES, LANES)).T
            loads[2].wait()

            def use(c):
                for h in range(2):
                    where = slice(h * half, (h + 1) * half)
                    for s in range(SLICE // LANES):
                        lanes = slice(c * SLICE + s * LANES, c * SLICE + (s + 1) * LANES)
                        value = part[2 * c + h, :, s * LANES : (s + 1) * LANES].astype(F32)
                        fresh[where, lanes] = res[where, lanes].astype(F32) + facs[where, :] * value

            spread = max(1, -(-len(ticks) // chunks))
            for c in range(chunks):
                for tick in ticks[:spread]:
                    tick()
                ticks = ticks[spread:]
                sums.step(2, c)
                if c:
                    sums.step(3, c - 1)
                    use(c - 1)
            sums.step(3, chunks - 1)
            use(chunks - 1)
            flush(6).start()
        else:
            loads[0].wait()
        loads[-2].wait()
        loads[-1].wait()
        for b in range(2 * STATE // LANES):
            rows = slice(2 * width + b * LANES, 2 * width + (b + 1) * LANES)
            wt[rows, :] = wstate[:, b * LANES : (b + 1) * LANES].T

        def norm(t, _):
            rows = pl.ds(pl.multiple_of(t * TILE, TILE), TILE)
            value = (fresh if mid else res)[rows, :].astype(F32)
            scale = lax.rsqrt(jnp.sum(value * value, axis=1, keepdims=True) / model + EPS)
            low = (value * scale * gain_ref[layer : layer + 1, :]).astype(BF16)
            rnorm_ref[rows, :] = scale
            normed[rows, :] = low
            turned[:, rows] = low.T
            small[rows, : 2 * STATE] = mm(low, wstate[...])
            small[rows, 2 * STATE :] = mm(low, wt[top:, :], NT)
            return 0

        lax.fori_loop(0, tokens_n // TILE, norm, 0)
        flush(0).start()
        flush(1).start()
        for tick in ticks:
            tick()

        if mid:
            job.relay(2, 1)
            project(0, inner)
            flush(2).start()
            job.relay(2, 2)
        job.arrive(1)
        project(1, gate)
        flush(3).start()
        if not mid:
            job.relay(2, 1)

    passed = 2 if mid else 1
    for k in range(passed + 1, line.n):
        @pl.when(i == 1 + (k - passed - 1) * steps // line.n)
        def _(k=k):
            job.relay(2, k)

    @pl.when(i > 0)
    def _():
        at = i - 1
        where = pl.ds(pl.multiple_of(at * n, n), n)

        @pl.when(lax.rem(at, per) == 0)
        def _():
            ext[0:8, :] = jnp.zeros((8, width), F32)
            exts[0:8, :] = jnp.zeros((8, 2 * STATE), F32)
            state[...] = jnp.zeros_like(state)

        rows, cols = iotas(n)
        ind = ind_ref[...]
        ext[8 : 8 + n, :] = inner[where, :]
        pre = conv_pre(ext, cp_ref, n)
        x = pre * sigmoid(pre)
        ext[0:8, :] = ext[n : n + 8, :]
        mini = small[where, :]
        exts[8 : 8 + n, :] = mini[:, : 2 * STATE]
        pres = conv_pre(exts, sp_ref, n)
        bc = (pres * sigmoid(pres)).astype(BF16)
        exts[0:8, :] = exts[n : n + 8, :]
        key, query = bc[:, :STATE], bc[:, STATE:]

        _, step, rate, cs, wide_step, wide_cs, wide_tail = scan_prep(mini, hp_ref, ind, n)
        cs2 = cs * LOG2E
        cs2t = cs2.T
        xs = x * wide_step
        lane = lax.broadcasted_iota(jnp.int32, (1, width), 1)
        half = jnp.where(lax.rem(lane, 2 * HEAD) < HEAD, 1.0, 0.0).astype(BF16)
        xsb = xs.astype(BF16)
        xs0 = xsb * half
        xs1 = xsb - xs0
        before = state[...]
        low = before.astype(BF16)
        st_ref[0] = low
        carried = mm(query, low) * wide_cs
        xw = (xs * wide_tail).astype(BF16)
        state[...] = before * wide_cs[n - 1 : n, :] + mm(key, xw, TN)
        scores = jnp.where(rows >= cols, mm(query, key, NT), 0.0)
        for pair in range(heads // 2):
            lanes = slice(pair * 2 * HEAD, (pair + 1) * 2 * HEAD)
            mats = []
            for h in (2 * pair, 2 * pair + 1):
                dec = jnp.exp2(jnp.minimum(cs2[:, h : h + 1] - cs2t[h : h + 1, :], 0.0))
                mats.append((scores * dec).astype(BF16))
            local = mm(
                jnp.concatenate(mats, axis=1),
                jnp.concatenate([xs0[:, lanes], xs1[:, lanes]], axis=0),
            )
            ssd_ref[:, lanes] = local + carried[:, lanes] + cp_ref[6:7, lanes] * x[:, lanes]
        gates = gate[where, :]
        gated = ssd_ref[...] * (gates * sigmoid(gates))
        sqs_ref[0] = rowsum(gated * gated)
        scaled_ref[...] = (gated * cp_ref[5:6, :]).astype(BF16)

        span = model // LANES
        share = -(-span // steps)
        for k in range(share):
            b = at * share + k

            @pl.when(b < span)
            def _(b=b):
                piece = block_of(slabs.at[1], b, slabs.shape[2]).T
                wt[width : 2 * width, pl.ds(pl.multiple_of(b * LANES, LANES), LANES)] = piece

    @pl.when(i == steps)
    def _():
        flush(4).start()
        job.arrive(2)
        flush(5).start()
        for j in range(3):
            job.drain(j)
        for k in range(len(outgoing)):
            flush(k).wait()


def forward(res, stateproj, steps_w, inproj, outt, gain, params, heads, size, layer, out=None):
    tokens_n, model = res.shape
    _, _, rows, width = inproj.shape
    top = 2 * width + 2 * STATE + LANES
    steps = tokens_n // CHUNK
    mid = out is not None
    hbm = pl.BlockSpec(memory_space=pl.ANY)
    chunks = model // SLICE

    def whole(a):
        return pl.BlockSpec(a.shape, lambda i: (0,) * len(a.shape))

    def row(w):
        return pl.BlockSpec((CHUNK, w), lambda i: (jnp.maximum(i - 1, 0), 0))

    args, in_specs, out_specs, out_shape, scratch = [res], [hbm], [], [], []
    if mid:
        args += list(out)
        in_specs += [hbm, hbm, whole(out[2])]
        out_specs += [hbm, whole(out[2])]
        out_shape += [jax.ShapeDtypeStruct(res.shape, F32), jax.ShapeDtypeStruct(out[2].shape, F32)]
        chunk = pltpu.VMEM((chunks, tokens_n // 2, SLICE), BF16)
        scratch += [
            pltpu.VMEM(out[0].shape, BF16),
            pltpu.VMEM(out[1].shape, BF16),
            pltpu.VMEM((2 * chunks, tokens_n // 2, SLICE), BF16),
            chunk, chunk, chunk,
            pltpu.VMEM((4,) + out[2].shape, F32),
            pltpu.VMEM((tokens_n, LANES), F32),
            pltpu.VMEM(res.shape, F32),
            pltpu.SemaphoreType.DMA((3, chunks)),
            pltpu.SemaphoreType.DMA((3, chunks)),
            pltpu.SemaphoreType.DMA((3,)),
            pltpu.SemaphoreType.DMA((3,)),
        ]
    args += [stateproj, steps_w, inproj, outt, gain, *params]
    in_specs += [hbm, hbm, hbm, hbm, whole(gain)] + [whole(v) for v in params]
    out_specs += [
        hbm, pl.BlockSpec((tokens_n, 1), lambda i: (0, 0)), hbm, hbm, hbm, hbm, hbm,
        row(width), row(width),
        pl.BlockSpec((1, 1, CHUNK), lambda i: (jnp.maximum(i - 1, 0), 0, 0)),
        pl.BlockSpec((1, STATE, width), lambda i: (jnp.maximum(i - 1, 0), 0, 0)),
    ]
    out_shape += [
        jax.ShapeDtypeStruct((model, tokens_n), BF16),
        jax.ShapeDtypeStruct((tokens_n, 1), F32),
        jax.ShapeDtypeStruct((tokens_n, 2 * STATE + LANES), F32),
        jax.ShapeDtypeStruct((tokens_n, width), F32),
        jax.ShapeDtypeStruct((tokens_n, width), F32),
        jax.ShapeDtypeStruct((top, model), BF16),
        jax.ShapeDtypeStruct((size, rows, width), BF16),
        jax.ShapeDtypeStruct((tokens_n, width), F32),
        jax.ShapeDtypeStruct((tokens_n, width), BF16),
        jax.ShapeDtypeStruct((steps, 1, CHUNK), F32),
        jax.ShapeDtypeStruct((steps, STATE, width), BF16),
    ]
    scratch += [
        pltpu.VMEM(res.shape, res.dtype),
        pltpu.VMEM((model, 2 * STATE), BF16),
        pltpu.VMEM((top, model), BF16),
        pltpu.VMEM((3, size, rows, width), BF16),
        pltpu.VMEM((tokens_n, model), BF16),
        pltpu.VMEM((model, tokens_n), BF16),
        pltpu.VMEM((tokens_n, 2 * STATE + LANES), F32),
        pltpu.VMEM((tokens_n, width), F32),
        pltpu.VMEM((tokens_n, width), F32),
        pltpu.VMEM((CHUNK + 8, width), F32),
        pltpu.VMEM((CHUNK + 8, 2 * STATE), F32),
        pltpu.VMEM((STATE, width), F32),
        pltpu.VMEM((8, width), F32),
        pltpu.VMEM((8, 2 * STATE), F32),
        pltpu.VMEM((8, LANES), F32),
        pltpu.VMEM((LANES, width), BF16),
        pltpu.SemaphoreType.DMA((3,)),
        pltpu.SemaphoreType.DMA((3, 3, size)),
        pltpu.SemaphoreType.DMA((3, size)),
        pltpu.SemaphoreType.DMA((5,)),
        pltpu.SemaphoreType.DMA((7,)),
    ]
    return pl.pallas_call(
        functools.partial(forward_body, size=size, heads=heads, per=LEN // CHUNK, steps=steps, layer=layer),
        grid=(steps + 1,),
        in_specs=in_specs,
        out_specs=out_specs,
        out_shape=out_shape,
        scratch_shapes=scratch,
        compiler_params=pltpu.CompilerParams(
            collective_id=min(layer, 1), has_side_effects=True, vmem_limit_bytes=VMEM_LIMIT
        ),
        name="forward",
    )(*args)


def back_body(*refs, heads, per, size, steps, layer, last):
    refs = list(refs)

    def take(n):
        got = refs[:n]
        del refs[:n]
        return got

    up_ref, sq_ref, gate_ref, ssd_ref, inner_ref, iprev_ref, small_ref, sprev_ref, st_ref, res_ref, rn_ref = take(11)
    gain_ref = take(1)[0]
    params = take(6)
    wout_hbm, scaled_hbm, wt_hbm, normed_hbm = take(4)
    if not last:
        next_normed, next_steps, next_sdel, next_inner, next_dcp, next_dsp, next_dhp, next_dgain = take(8)
    new_ref, grad_hbm = take(2)
    if last:
        held_hbm, sdsum_ref, steplow_ref, dcp_ref, dsp_ref, dhp_ref, dgain_ref, mixed_ref = take(8)
    else:
        full_hbm, wide_hbm = take(2)
    ext, exts, cde, cdes, dstate, rq, cp_ref, sp_ref, hp_ref, ind_ref = take(10)
    wout, scaled, wt, turned, dy, glow, ilow, frow, srow, sgot = take(10)
    part, near, away, tpart, got, far, other = take(7)
    load, rsend, rrecv, ssend, srecv, sends, recvs, gsem = take(8)
    if last:
        held, fgot, opart, ogot, ofar, oother, fsend, frecv, osends, orecvs = take(10)
    else:
        dcp_ref, dsp_ref, dhp_ref, dgain_ref = take(4)
        sd_all = scaled.at[:, pl.ds(0, 2 * STATE)]
        step_all = scaled.at[:, pl.ds(2 * STATE, LANES)]
        buffers = take(6)
        sems = take(7)
    assert not refs

    n = CHUNK
    model = up_ref.shape[1]
    i = pl.program_id(0)
    begin_gate = steps
    begin_scan = begin_gate + steps
    begin_norm = begin_scan + steps
    end = begin_norm + steps - 1
    line = Line(size)
    square = Square()
    rows_own = part.shape[2]
    count = part.shape[0]
    job = Scatter(line, part, lambda j: dy.at[pl.ds(j * rows_own, rows_own), :], near, away, ssend, srecv)
    sums = Total(square, tpart, got, far, other, sends, recvs)
    if last:
        outs = Total(square, opart, ogot, ofar, oother, osends, orecvs)
        half = steps * n // 2
        slices = model // SLICE
    else:
        minis = Smalls(line, square, *buffers, sems)
    moves = [(wout_hbm, wout), (scaled_hbm, scaled), (wt_hbm, wt), (normed_hbm, turned)]
    if last:
        moves.append((held, held_hbm))
    else:
        tokens_n = steps * n
        spots = (wt.at[pl.ds(0, model), pl.ds(0, tokens_n)],)
        spots += tuple(
            wt.at[pl.ds(0, tokens_n), pl.ds(tokens_n + at, w)] for at, w in ((0, LANES), (LANES, 2 * STATE))
        )
        moves += [(next_normed, spots[0]), (next_steps, spots[1]), (next_sdel, spots[2]), (next_inner, part.at[3])]

    def move(k):
        return pltpu.make_async_copy(*moves[k], load.at[k])

    places = line.n

    def spaced(begin, stop, m):
        return begin + m * (stop - begin) // places

    middle = begin_scan + steps // 2
    if last:
        folds = [(spaced(begin_scan, middle, m), 0, m) for m in range(places)]
        folds += [(spaced(middle, begin_norm, m) + 1, 1, m) for m in range(places)]
    else:
        folds = [(spaced(begin_gate - 1, begin_scan + 3, m), 3, m) for m in range(places)]
        folds += [(spaced(begin_scan + 2, middle + 3, m), 0, m) for m in range(places)]
        folds += [(spaced(begin_norm - 1, end - 1, m), 1, m) for m in range(places)]

    def column(row):
        return jnp.broadcast_to(row, (n, n)).T[:, 0:1]

    @pl.when(i == 0)
    def _():
        for k in range(3):
            move(k).start()
        if not last:
            move(7).start()
        put_params(cp_ref, sp_ref, hp_ref, ind_ref, layer, params)
        rq[...] = jnp.zeros_like(rq)
        line.greet_all(pltpu.get_barrier_semaphore(), square.others())
        if last:
            rows = [
                remote(sq_ref, fgot.at[square.me], fsend.at[k], frecv.at[k], who)
                for k, who in enumerate(square.others())
            ]
            for copy in rows:
                copy.start()
            fgot[square.me] = sq_ref[...]
            move(0).wait()
            move(1).wait()
            for c in range(slices):
                value = mm(scaled[...], wout[c * SLICE : (c + 1) * SLICE, :], NT).astype(BF16)
                opart[2 * c] = value[:half]
                opart[2 * c + 1] = value[half:]
                outs.step(0, c)
            outs.step(1, 0)
            for copy in rows:
                copy.wait()
            total = (fgot[0] + fgot[1]) + (fgot[2] + fgot[3])
        else:
            move(7).wait()
            job.start(3)
            total = sq_ref[...]
            move(0).wait()
            move(1).wait()
        dcp_ref[...] = jnp.zeros_like(dcp_ref)
        dsp_ref[...] = jnp.zeros_like(dsp_ref)
        dhp_ref[...] = jnp.zeros_like(dhp_ref)
        dgain_ref[...] = jnp.zeros_like(dgain_ref)
        frow[...] = lax.rsqrt(total / INNER + EPS)

    ind = ind_ref[...]
    for at, j, m in folds:
        @pl.when(i == at)
        def _(j=j, m=m):
            job.fold(j, m)

    @pl.when(i < begin_gate)
    def _():
        rows = pl.ds(pl.multiple_of(i * n, n), n)
        low = (column(frow[i]) * up_ref[...].astype(F32)).astype(BF16)
        turned[:, rows] = low.T
        sd = mm(low, wout[...])
        dy[rows, :] = sd
        piece = scaled[rows, :]
        srow[i] = rowsum(piece.astype(F32) * sd)

    @pl.when(i == begin_gate - 1)
    def _():
        copies = [
            remote(srow, sgot.at[square.me], rsend.at[k], rrecv.at[k], who) for k, who in enumerate(square.others())
        ]
        for copy in copies:
            copy.start()
        job.emit(0, turned, scaled)
        move(3).start()
        sgot[square.me] = srow[...]
        for copy in copies:
            copy.wait()
        srow[...] = (sgot[0] + sgot[1]) + (sgot[2] + sgot[3])

    if last:
        @pl.when(i == steps // 2)
        def _():
            outs.step(1, 1)

        @pl.when((i >= begin_gate) & (i < begin_gate + slices - 2))
        def _():
            outs.step(1, i - begin_gate + 2)

    @pl.when((i >= begin_gate) & (i < begin_scan))
    def _():
        c = i - begin_gate
        rows = pl.ds(pl.multiple_of(c * n, n), n)
        coef = column(frow[c] * frow[c] * srow[c]) / INNER
        gate = gate_ref[...]
        gsig = sigmoid(gate)
        gact = gate * gsig
        ssd = ssd_ref[...]
        sd = dy[rows, :]
        gated = ssd * gact
        gd = cp_ref[5:6, :] * sd - coef * gated
        dcp_ref[5:6, :] += colsum(gated * sd)
        dy[rows, :] = gd * gact
        glow[rows, :] = (gd * ssd * (gsig + gact * (1.0 - gsig))).astype(BF16)

    @pl.when(i == begin_scan - 1)
    def _():
        move(3).wait()
        job.emit(1, turned, glow)
        move(2).wait()

    @pl.when((i >= begin_scan) & (i < begin_norm))
    def _():
        q = i - begin_scan
        chunk = steps - 1 - q
        where = pl.ds(pl.multiple_of(chunk * n, n), n)

        @pl.when(lax.rem(chunk, per) == per - 1)
        def _():
            cde[n : n + 8, :] = jnp.zeros((8, cde.shape[1]), F32)
            cdes[n : n + 8, :] = jnp.zeros((8, cdes.shape[1]), F32)
            dstate[...] = jnp.zeros_like(dstate)

        keep = jnp.where(lax.rem(chunk, per) == 0, 0.0, 1.0).astype(F32)
        rows, cols = iotas(n)
        ext[0:8, :] = iprev_ref[...] * keep
        ext[8 : 8 + n, :] = inner_ref[...]
        exts[0:8, :] = sprev_ref[:, : 2 * STATE] * keep
        exts[8 : 8 + n, :] = small_ref[:, : 2 * STATE]
        pre = conv_pre(ext, cp_ref, n)
        sig = sigmoid(pre)
        x = pre * sig
        slope = sig + x * (1.0 - sig)
        pres = conv_pre(exts, sp_ref, n)
        sigs = sigmoid(pres)
        acts = pres * sigs
        slopes = sigs + acts * (1.0 - sigs)
        bc = acts.astype(BF16)
        key, query = bc[:, :STATE], bc[:, STATE:]
        dyc = dy[where, :]

        raw, step, rate, cs, wide_step, wide_cs, wide_tail = scan_prep(small_ref, hp_ref, ind, n)
        cs2 = cs * LOG2E
        cs2t = cs2.T
        xs = x * wide_step
        xsb = xs.astype(BF16)
        dyb = dyc.astype(BF16)
        lane = lax.broadcasted_iota(jnp.int32, (1, xs.shape[1]), 1)
        half = jnp.where(lax.rem(lane, 2 * HEAD) < HEAD, 1.0, 0.0).astype(BF16)
        dy0 = dyb * half
        dy1 = dyb - dy0
        low = st_ref[0]
        dst = dstate[...]
        dlow = dst.astype(BF16)
        dye = dyc * wide_cs
        dyeb = dye.astype(BF16)
        up = headsum(dye * mm(query, low), ind)
        dxs_state = wide_tail * mm(key, dlow)
        down = headsum(xs * dxs_state, ind)
        qdel = mm(dyeb, low, NT)
        kdel = mm((xs * wide_tail).astype(BF16), dlow, NT)
        through = headsum(jnp.broadcast_to(colsum(low.astype(F32) * dst), (8, dst.shape[1])), ind)[0:1, :]
        through = through * jnp.exp(cs[n - 1 : n, :])
        dstate[...] = dst * wide_cs[n - 1 : n, :] + mm(query, dyeb, TN)

        scores = jnp.where(rows <= cols, mm(key, query, NT), 0.0)
        dscores = jnp.zeros((n, n), F32)
        colq = jnp.zeros((n, LANES), F32)
        lane = lax.broadcasted_iota(jnp.int32, (n, LANES), 1)
        dxs = []
        for pair in range(heads // 2):
            lanes = slice(pair * 2 * HEAD, (pair + 1) * 2 * HEAD)
            stacked = jnp.concatenate([dy0[:, lanes], dy1[:, lanes]], axis=0)
            both = mm(xsb[:, lanes], stacked, NT)
            mats = []
            for which, h in enumerate((2 * pair, 2 * pair + 1)):
                dec = jnp.exp2(jnp.minimum(cs2t[h : h + 1, :] - cs2[:, h : h + 1], 0.0))
                mats.append((scores * dec).astype(BF16))
                term = dec * both[:, which * n : (which + 1) * n]
                dscores = dscores + term
                quad = scores * term
                rq[h : h + 1, :] = colsum(quad)
                colq = jnp.where(lane == h, jnp.sum(quad, axis=1, keepdims=True), colq)
            dxs.append(mm(jnp.concatenate(mats, axis=1), stacked))
        dxs = jnp.concatenate(dxs, axis=1) + dxs_state
        dscores = jnp.where(rows <= cols, dscores, 0.0).astype(BF16)
        kdel = kdel + mm(dscores, query)
        qdel = qdel + mm(dscores, key, TN)

        upper = jnp.where(rows <= cols, 1.0, 0.0).astype(F32)
        strict = jnp.where(rows > cols, 1.0, 0.0).astype(F32)
        da = mm(upper, rq[...].T - colq + up, precision=HIGH) + mm(strict, down, precision=HIGH) + through
        grown = headsum(x * dxs, ind) + rate * da
        step_pre = grown * sigmoid(raw)
        steplow = step_pre.astype(BF16)
        if last:
            steplow_ref[...] = steplow
        else:
            step_all[where, :] = steplow
        dhp_ref[0:1, :] += colsum(step_pre)
        dhp_ref[1:2, :] += rate * colsum(step * da)
        dcp_ref[6:7, :] += colsum(dyc * x)

        cd = (dxs * wide_step + cp_ref[6:7, :] * dyc) * slope
        cde[0:n, :] = cd
        center = ext[8 : 8 + n, :]
        total = cp_ref[3:4, :] * cd
        dcp_ref[3:4, :] += colsum(cd * center)
        for tap in range(3):
            shifted = cde[3 - tap : 3 - tap + n, :]
            total = total + cp_ref[tap : tap + 1, :] * shifted
            dcp_ref[tap : tap + 1, :] += colsum(shifted * center)
        inner_low = total.astype(BF16)
        ilow[where, :] = inner_low
        dcp_ref[4:5, :] += colsum(cd)
        cde[n : n + 8, :] = cde[0:8, :]

        cds = jnp.concatenate([kdel, qdel], axis=1) * slopes
        cdes[0:n, :] = cds
        center = exts[8 : 8 + n, :]
        total = sp_ref[3:4, :] * cds
        dsp_ref[3:4, :] += colsum(cds * center)
        for tap in range(3):
            shifted = cdes[3 - tap : 3 - tap + n, :]
            total = total + sp_ref[tap : tap + 1, :] * shifted
            dsp_ref[tap : tap + 1, :] += colsum(shifted * center)
        sdel = total.astype(BF16)
        dsp_ref[4:5, :] += colsum(cds)
        cdes[n : n + 8, :] = cdes[0:8, :]

        lows = jnp.concatenate([inner_low, glow[where, :], sdel, steplow], axis=1)
        value = mm(lows, wt[...]).astype(BF16)
        tpart[2 * q, :, :model] = value[: n // 2]
        tpart[2 * q + 1, :, :model] = value[n // 2 :]
        tpart[2 * q, :, model:] = sdel[: n // 2]
        tpart[2 * q + 1, :, model:] = sdel[n // 2 :]
        sums.step(0, q)

    @pl.when((i > begin_scan) & (i <= begin_norm))
    def _():
        sums.step(1, i - begin_scan - 1)

    @pl.when((i >= begin_scan + 5) & (i < begin_norm + 5))
    def _():
        sums.step(2, i - begin_scan - 5)

    @pl.when((i >= begin_scan + 6) & (i < begin_norm + 6))
    def _():
        sums.step(3, i - begin_scan - 6)

    if last:
        @pl.when((i > begin_scan) & (i <= begin_scan + slices))
        def _():
            outs.step(2, i - begin_scan - 1)

        @pl.when((i > begin_scan + 1) & (i <= begin_scan + slices + 1))
        def _():
            outs.step(3, i - begin_scan - 2)

    @pl.when(i == begin_norm - 1)
    def _():
        dhp_ref[2:3, :] = headsum(jnp.broadcast_to(dcp_ref[6:7, :], (8, dcp_ref.shape[1])), ind)[0:1, :]
        if last:
            job.product(held, turned, ilow)
            move(4).start()
        else:
            job.emit(2, turned, ilow, places - 1)
            for k in (4, 5, 6):
                move(k).start()

    if not last:
        @pl.when(i == begin_norm + 1)
        def _():
            for k in (4, 5, 6):
                move(k).wait()
            put_pack(
                buffers[0].at[1], square.me, *spots, next_dcp[...], next_dsp[...], next_dhp[...], next_dgain[...]
            )
            minis.sum.start(1)

    @pl.when(i >= begin_norm)
    def _():
        r = i - begin_norm
        chunk = steps - 1 - r
        if last:
            fac = column(frow[chunk])
            side = chunk // (steps // 2)
            base = (chunk - side * (steps // 2)) * n
        for h in range(2):
            rows = slice(h * (n // 2), (h + 1) * (n // 2))
            back = tpart[2 * r + h, :, :model].astype(F32)
            sdel = tpart[2 * r + h, :, model:]
            if last:
                sdsum_ref[rows, :] = sdel
            else:
                sd_all[pl.ds(pl.multiple_of(chunk * n + h * (n // 2), n // 2), n // 2), :] = sdel
            res = res_ref[rows, :].astype(F32)
            rn = rn_ref[rows, :]
            dgain_ref[...] += colsum(back * res * rn)
            gained = back * gain_ref[layer : layer + 1, :]
            mean = jnp.sum(gained * res, axis=1, keepdims=True) / model
            new_ref[rows, :] = up_ref[rows, :].astype(F32) + rn * gained - (rn * rn * rn * mean) * res
            if last:
                where = pl.ds(pl.multiple_of(base + h * (n // 2), n // 2), n // 2)
                for c in range(slices):
                    span = slice(c * SLICE, (c + 1) * SLICE)
                    summed = opart[2 * c + side, where, :].astype(F32)
                    mixed_ref[rows, span] = (res[:, span] + fac[rows, :] * summed).astype(BF16)

    @pl.when(i == end)
    def _():
        def finish(j):
            job.finish(j)
            pltpu.make_async_copy(dy.at[pl.ds(j * rows_own, rows_own), :], grad_hbm.at[j], gsem.at[j]).start()

        if not last:
            put_pack(
                buffers[0].at[0], square.me, turned, step_all, sd_all, dcp_ref[...], dsp_ref[...], dhp_ref[...], dgain_ref[...]
            )
            minis.sum.start(0)
            for m in range(places // 2):
                job.fold(2, m)
            finish(3)
        finish(0)
        finish(1)
        if not last:
            minis.fold()
            minis.turn()
            for k in range(1, line.n):
                minis.relay(k)
            job.lead(2, places - 1)
            for m in range(places // 2, places):
                job.fold(2, m)
            minis.cross()
            finish(2)
            minis.cross_on()
            minis.end()
            tails = [
                pltpu.make_async_copy(src, dst, load.at[k])
                for k, (src, dst) in enumerate(((minis.full, full_hbm), (minis.wide, wide_hbm)))
            ]
            for copy in tails:
                copy.start()
        for j in range(count):
            job.drain(j)
            pltpu.make_async_copy(dy.at[pl.ds(j * rows_own, rows_own), :], grad_hbm.at[j], gsem.at[j]).wait()
        if last:
            move(4).wait()
        else:
            for copy in tails:
                copy.wait()


def back(up, sq, gate_pre, ssd, inner_raw, small, states, res, rnorm, gain, params,
         wout, scaled, wt, normed, heads, size, layer, after=None):
    tokens_n, width = inner_raw.shape
    model = up.shape[1]
    last = after is None
    steps = tokens_n // CHUNK
    begin_scan = 2 * steps
    begin_norm = begin_scan + steps
    rows = model // size
    n = size // 2
    hbm = pl.BlockSpec(memory_space=pl.ANY)
    top = steps - 1

    def norm_at(i):
        return jnp.where(i < begin_norm, top, top - (i - begin_norm))

    def scan_at(i):
        return jnp.clip(top - (i - begin_scan), 0, top)

    def first(w):
        return pl.BlockSpec((CHUNK, w), lambda i: (jnp.where(i < steps, i, norm_at(i)), 0))

    def second(w):
        return pl.BlockSpec((CHUNK, w), lambda i: (jnp.clip(i - steps, 0, top), 0))

    def scan(w):
        return pl.BlockSpec((CHUNK, w), lambda i: (scan_at(i), 0))

    def prev(w):
        return pl.BlockSpec((8, w), lambda i: (jnp.maximum(scan_at(i) * (CHUNK // 8) - 1, 0), 0))

    def norm(w):
        return pl.BlockSpec((CHUNK, w), lambda i: (norm_at(i), 0))

    def whole(a):
        return pl.BlockSpec(a.shape, lambda i: (0,) * len(a.shape))

    extra = model + 2 * STATE
    quarter = pltpu.VMEM((steps, CHUNK // 2, extra), BF16)
    count = 2 if last else 4
    pieces = pltpu.VMEM((count, n, rows, width), BF16)
    args = [up, sq, gate_pre, ssd, inner_raw, inner_raw, small, small, states, res, rnorm, gain, *params,
            wout, scaled, wt, normed]
    in_specs = [
        first(model), whole(sq), second(width), second(width),
        scan(width), prev(width), scan(small.shape[1]), prev(small.shape[1]),
        pl.BlockSpec((1, STATE, width), lambda i: (scan_at(i), 0, 0)),
        norm(model), norm(1), whole(gain),
    ] + [whole(a) for a in params] + [hbm] * 4
    out_specs = [norm(model), hbm]
    out_shape = [jax.ShapeDtypeStruct((tokens_n, model), F32), jax.ShapeDtypeStruct((count, rows, width), F32)]
    totals = [(8, width), (8, 2 * STATE), (8, LANES), (1, model)]
    scratch = [
        pltpu.VMEM((CHUNK + 8, width), F32),
        pltpu.VMEM((CHUNK + 8, 2 * STATE), F32),
        pltpu.VMEM((CHUNK + 8, width), F32),
        pltpu.VMEM((CHUNK + 8, 2 * STATE), F32),
        pltpu.VMEM((STATE, width), F32),
        pltpu.VMEM((LANES, CHUNK), F32),
        pltpu.VMEM((8, width), F32),
        pltpu.VMEM((8, 2 * STATE), F32),
        pltpu.VMEM((8, LANES), F32),
        pltpu.VMEM((LANES, width), BF16),
        pltpu.VMEM(wout.shape, BF16),
        pltpu.VMEM(scaled.shape, BF16),
        pltpu.VMEM(wt.shape, BF16),
        pltpu.VMEM(normed.shape, BF16),
        pltpu.VMEM((tokens_n, width), F32),
        pltpu.VMEM((tokens_n, width), BF16),
        pltpu.VMEM((tokens_n, width), BF16),
        pltpu.VMEM((steps, 1, CHUNK), F32),
        pltpu.VMEM((steps, 1, CHUNK), F32),
        pltpu.VMEM((4, steps, 1, CHUNK), F32),
        pltpu.VMEM((count, size, rows, width), BF16), pieces, pieces,
        pltpu.VMEM((2 * steps, CHUNK // 2, extra), BF16), quarter, quarter, quarter,
        pltpu.SemaphoreType.DMA((8,)),
        pltpu.SemaphoreType.DMA((3,)),
        pltpu.SemaphoreType.DMA((3,)),
        pltpu.SemaphoreType.DMA((2, count, n)),
        pltpu.SemaphoreType.DMA((2, count, n)),
        pltpu.SemaphoreType.DMA((3, steps)),
        pltpu.SemaphoreType.DMA((3, steps)),
        pltpu.SemaphoreType.DMA((count,)),
    ]
    if last:
        out_specs += [hbm, norm(2 * STATE), scan(LANES)]
        out_specs += [pl.BlockSpec(v, lambda i: (0, 0)) for v in totals] + [norm(model)]
        out_shape += [
            jax.ShapeDtypeStruct((size, rows, width), BF16),
            jax.ShapeDtypeStruct((tokens_n, 2 * STATE), BF16),
            jax.ShapeDtypeStruct((tokens_n, LANES), BF16),
        ]
        out_shape += [jax.ShapeDtypeStruct(v, F32) for v in totals]
        out_shape.append(jax.ShapeDtypeStruct((tokens_n, model), BF16))
        slices = model // SLICE
        chunk = pltpu.VMEM((slices, tokens_n // 2, SLICE), BF16)
        scratch += [
            pltpu.VMEM((size, rows, width), BF16),
            pltpu.VMEM((4, steps, 1, CHUNK), F32),
            pltpu.VMEM((2 * slices, tokens_n // 2, SLICE), BF16), chunk, chunk, chunk,
            pltpu.SemaphoreType.DMA((3,)),
            pltpu.SemaphoreType.DMA((3,)),
            pltpu.SemaphoreType.DMA((3, slices)),
            pltpu.SemaphoreType.DMA((3, slices)),
        ]
    else:
        w = 2 * STATE
        r = pack_rows(size)
        args += list(after)
        in_specs += [hbm] * 4 + [whole(v) for v in after[4:]]
        out_specs += [hbm, hbm]
        out_shape += [
            jax.ShapeDtypeStruct((2, size, r, w), BF16),
            jax.ShapeDtypeStruct((4, 2, SPAN, w), BF16),
        ]
        scratch += [pltpu.VMEM(v, F32) for v in totals]
        scratch += smalls_scratch(size, w, 2)
    return pl.pallas_call(
        functools.partial(
            back_body, heads=heads, per=LEN // CHUNK, size=size, steps=steps, layer=layer, last=last
        ),
        grid=(begin_norm + steps,),
        in_specs=in_specs,
        out_specs=out_specs,
        out_shape=out_shape,
        scratch_shapes=scratch,
        compiler_params=pltpu.CompilerParams(
            collective_id=2 if last else 3, has_side_effects=True, vmem_limit_bytes=VMEM_LIMIT
        ),
        name="back",
    )(*args)


def results_body(full_ref, wide_ref, first_hbm, second_hbm, mixed_hbm, up_hbm, *refs, layers, heads):
    pair_out, out_out, mixed_out, up_out = refs[11:15]
    first, second, mixed, up, load, store = refs[15:]
    refs = refs[:11]
    loads = [
        pltpu.make_async_copy(src, dst, load.at[k])
        for k, (src, dst) in enumerate(((up_hbm, up), (mixed_hbm, mixed), (first_hbm, first), (second_hbm, second)))
    ]
    for copy in loads:
        copy.start()
    moves = [
        (up, up_out), (mixed, mixed_out), (first.at[pl.ds(1, 2)], pair_out.at[0]), (second.at[1], pair_out.at[1, 0]),
        (first.at[3], pair_out.at[1, 1]), (first.at[0], out_out.at[0]), (second.at[0], out_out.at[1]),
    ]
    stores = [pltpu.make_async_copy(src, dst, store.at[k]) for k, (src, dst) in enumerate(moves)]
    for k, copy in enumerate(stores):
        if k < 3:
            loads[k].wait()
        if k == 3:
            loads[3].wait()
        copy.start()
    step_ref, state_ref, conv_ref, bias_ref, convs_ref, biass_ref = refs[:6]
    stepbias_ref, decay_ref, skip_ref, norm_ref, gain_ref = refs[6:]
    model = state_ref.shape[1]
    quarter = model // 4
    w = state_ref.shape[2]
    width = conv_ref.shape[2]
    for layer in range(layers):
        for t in range(4):
            state_ref[layer, t * quarter : (t + 1) * quarter, :] = wide_ref[t, layer, :quarter, :].astype(F32)
        taps = [wide_ref[t, layer, quarter : quarter + 16, :].astype(F32) for t in range(4)]
        taps = (taps[0] + taps[1]) + (taps[2] + taps[3])
        convs_ref[layer] = taps[0:4]
        biass_ref[layer : layer + 1, :] = taps[4:5]
        flat = full_ref[layer].reshape(-1, w)[:PACK].astype(F32)
        at = quarter + 16
        for b in range(model // w):
            step_ref[layer, :, b * w : (b + 1) * w] = flat[at : at + 16]
            at += 16
        for b in range(width // w):
            lanes = slice(b * w, (b + 1) * w)
            rows = flat[at + 8 * b : at + 8 * b + 8]
            conv_ref[layer, :, lanes] = rows[0:4]
            bias_ref[layer : layer + 1, lanes] = rows[4:5]
            norm_ref[layer : layer + 1, lanes] = rows[5:6]
        at += 8 * (width // w)
        for k, ref in enumerate((stepbias_ref, decay_ref, skip_ref)):
            ref[layer : layer + 1, :] = flat[at + k : at + k + 1, :heads]
        at += 8
        for b in range(model // w):
            gain_ref[layer : layer + 1, b * w : (b + 1) * w] = flat[at + b : at + b + 1]
    for copy in stores:
        copy.wait()


def write_results(full, wide, first, second, mixed, up, heads):
    layers, w = full.shape[0], full.shape[3]
    _, rows, width = first.shape
    model = up.shape[1]
    vm = pl.BlockSpec(memory_space=pltpu.VMEM)
    hbm = pl.BlockSpec(memory_space=pl.ANY)
    shapes = [
        (layers, 16, model), (layers, model, w), (layers, 4, width), (layers, width), (layers, 4, w), (layers, w),
        (layers, heads), (layers, heads), (layers, heads), (layers, width), (layers, model),
    ]
    return pl.pallas_call(
        functools.partial(results_body, layers=layers, heads=heads),
        in_specs=[vm, vm] + [hbm] * 4,
        out_specs=[vm] * len(shapes) + [hbm] * 4,
        out_shape=[jax.ShapeDtypeStruct(v, F32) for v in shapes] + [
            jax.ShapeDtypeStruct((layers, 2, rows, width), F32),
            jax.ShapeDtypeStruct((layers, rows, width), F32),
            jax.ShapeDtypeStruct(mixed.shape, mixed.dtype),
            jax.ShapeDtypeStruct(up.shape, up.dtype),
        ],
        scratch_shapes=[
            pltpu.VMEM(first.shape, F32),
            pltpu.VMEM(second.shape, F32),
            pltpu.VMEM(mixed.shape, mixed.dtype),
            pltpu.VMEM(up.shape, up.dtype),
            pltpu.SemaphoreType.DMA((4,)),
            pltpu.SemaphoreType.DMA((7,)),
        ],
        compiler_params=pltpu.CompilerParams(vmem_limit_bytes=VMEM_LIMIT),
        name="results",
    )(full, wide, first, second, mixed, up)


def shards(
    tokens, inproj, stepproj, stateproj, outproj, convinner, biasinner, convstate, biasstate,
    stepbias, decaylog, skipgain, normgain, inputgain, cotangent,
):
    layers = inproj.shape[0]
    width = inproj.shape[3]
    heads = stepproj.shape[2]
    model = tokens.shape[1]
    pad = LANES - heads
    size = lax.axis_size("dp")
    steps_w = jnp.pad(jnp.swapaxes(stepproj, 1, 2), ((0, 0), (0, pad), (0, 0)))
    head = jnp.pad(jnp.stack([stepbias, decaylog, skipgain], axis=1), ((0, 0), (0, 5), (0, pad)))
    outt = jnp.swapaxes(outproj, 1, 2)
    params = (convinner, biasinner, normgain, convstate, biasstate, head)

    residual = tokens
    kept = []
    out = None
    for at in range(layers):
        results = forward(residual, stateproj, steps_w, inproj, outt, inputgain, params, heads, size, at, out=out)
        if at:
            residual, kept[-1][-1] = results[:2]
            results = results[2:]
        normed, rnorm, small, inner_raw, gate_pre, wt, w_out, ssd, scaled, sq, states = results
        w_out = w_out.reshape(model, width)
        kept.append([residual, normed, rnorm, small, inner_raw, gate_pre, wt, w_out, ssd, scaled, states, sq])
        out = (scaled, w_out, sq)

    assert layers == 2
    before, normed, rnorm, small, inner_raw, gate_pre, wt, w_out, ssd, scaled, states, sq = kept[1]
    upstream, second, held, sdel, steplow, *totals, mixed = back(
        cotangent, sq, gate_pre, ssd, inner_raw, small, states, before, rnorm, inputgain, params,
        w_out, scaled, wt, normed, heads, size, 1,
    )
    after = (normed, steplow, sdel, held, *totals)
    before, normed, rnorm, small, inner_raw, gate_pre, wt, w_out, ssd, scaled, states, sq = kept[0]
    upstream, first, full, wide = back(
        upstream, sq, gate_pre, ssd, inner_raw, small, states, before, rnorm, inputgain, params,
        w_out, scaled, wt, normed, heads, size, 0, after=after,
    )
    (
        step_grad, state_grad, conv_grad, bias_grad, convs_grad, biass_grad,
        stepbias_grad, decay_grad, skip_grad, norm_grad, gain_grad, pair_grad, out_grad, mixed, upstream,
    ) = write_results(full, wide, first, second, mixed, upstream, heads)
    return (
        mixed,
        upstream,
        pair_grad,
        jnp.swapaxes(step_grad[:, :heads], 1, 2),
        state_grad,
        jnp.swapaxes(out_grad, 1, 2),
        conv_grad,
        bias_grad,
        convs_grad,
        biass_grad,
        stepbias_grad,
        decay_grad,
        skip_grad,
        norm_grad,
        gain_grad,
    )


def solution(mesh):
    in_specs = (
        P("dp", None),
        P(None, None, "dp", "tensor"),
        P(None, None, "tensor"),
        P(),
        P(None, "tensor", "dp"),
        P(None, None, "tensor"),
        P(None, "tensor"),
        P(),
        P(),
        P(None, "tensor"),
        P(None, "tensor"),
        P(None, "tensor"),
        P(None, "tensor"),
        P(),
        P("dp", None),
    )
    out_specs = (
        P("dp", None),
        P("dp", None),
        P(None, None, "dp", "tensor"),
        P(None, None, "tensor"),
        P(),
        P(None, "tensor", "dp"),
        P(None, None, "tensor"),
        P(None, "tensor"),
        P(),
        P(),
        P(None, "tensor"),
        P(None, "tensor"),
        P(None, "tensor"),
        P(None, "tensor"),
        P(),
    )
    return jax.shard_map(shards, mesh=mesh, in_specs=in_specs, out_specs=out_specs, check_vma=False)
```

```python
import functools
import math

import jax
import jax.numpy as jnp
from jax import lax
from jax.experimental import pallas as pl
from jax.experimental.pallas import tpu as pltpu
from jax.sharding import PartitionSpec as P

STATE = 128
LEN = 1024
INNER = 3072
HEAD = 64
CHUNK = 128
SLICE = 256
TILE = 256
PACK = 544
SPAN = 400
VMEM_LIMIT = 65000 * 1024
LANES = 128
EPS = 1e-05
LOG2E = 1.4426950408889634

HIGH = lax.Precision.HIGHEST
NN = (((1,), (0,)), ((), ()))
NT = (((1,), (1,)), ((), ()))
TN = (((0,), (0,)), ((), ()))
F32 = jnp.float32
BF16 = jnp.bfloat16
MESH = pl.DeviceIdType.MESH


def remote(src, dst, send, recv, where):
    return pltpu.make_async_remote_copy(
        src_ref=src, dst_ref=dst, send_sem=send, recv_sem=recv, device_id=where, device_id_type=MESH
    )


class Line:
    def __init__(self, size):
        self.n = size // 2
        me = lax.axis_index("dp")
        self.me = me
        self.at = me // 2
        self.side = lax.rem(me, 2)
        self.pair = {"dp": me + 1 - 2 * self.side}
        self.right = {"dp": jnp.minimum(me + 2, size - 1)}
        self.left = {"dp": jnp.maximum(me - 2, 0)}
        odd = lax.rem(self.at, 2)
        self.odd = odd == 1
        self.near = {"dp": me + 2 - 4 * odd}
        self.has_left = self.at > 0
        self.has_right = self.at < self.n - 1

    def greet(self, barrier, more=()):
        for who in more:
            pl.semaphore_signal(barrier, inc=1, device_id=who, device_id_type=MESH)
        pl.semaphore_signal(barrier, inc=1, device_id=self.pair, device_id_type=MESH)

        @pl.when(self.has_left)
        def _():
            pl.semaphore_signal(barrier, inc=1, device_id=self.left, device_id_type=MESH)

        @pl.when(self.has_right)
        def _():
            pl.semaphore_signal(barrier, inc=1, device_id=self.right, device_id_type=MESH)

        peers = 1 + len(more) + self.has_left.astype(jnp.int32) + self.has_right.astype(jnp.int32)
        pl.semaphore_wait(barrier, peers)

    def greet_all(self, barrier, more=()):
        for who in list(more) + [self.pair]:
            pl.semaphore_signal(barrier, inc=1, device_id=who, device_id_type=MESH)
        for i in range(self.n):
            @pl.when(i != self.at)
            def _(i=i):
                pl.semaphore_signal(barrier, inc=1, device_id={"dp": 2 * i + self.side}, device_id_type=MESH)
        pl.semaphore_wait(barrier, self.n + len(more))


def upper(rows):
    return max(16, rows // 32 * 16)


class Gather:
    def __init__(self, line, own, full, keep, send, recv):
        self.line, self.own, self.full, self.keep, self.send, self.recv = line, own, full, keep, send, recv
        self.rows = full.shape[2]
        self.cut = upper(self.rows)

    def copy(self, j, slab, way, src=None, rest=False):
        where = (self.line.right, self.line.left, self.line.pair)[way]
        dst = self.full.at[j, slab]
        if rest:
            dst = self.full.at[j, slab, pl.ds(self.cut, self.rows - self.cut)]
        return remote(dst if src is None else src, dst, self.send.at[j, way, slab], self.recv.at[j, slab], where)

    def shared(self, j, slab, owner):
        part = self.full.at[j, slab, pl.ds(0, self.cut)]
        return remote(part, part, self.send.at[j, 0, slab], self.recv.at[j, owner], self.line.near)

    def start(self, j):
        line = self.line
        pltpu.make_async_copy(self.own(j), self.full.at[j, line.me], self.keep.at[j]).start()

        @pl.when(line.has_right)
        def _():
            self.copy(j, line.me, 0, self.own(j)).start()

        @pl.when(line.has_left)
        def _():
            self.copy(j, line.me, 1, self.own(j)).start()

        self.copy(j, line.me, 2, self.own(j)).start()

    def relay(self, j, k):
        line = self.line

        def forward(slab, way, go_on, near):
            self.copy(j, slab, way).wait_recv()

            @pl.when(go_on)
            def _():
                self.copy(j, slab, way).start()

            if k > 1:
                self.copy(j, slab, 2).start()
            else:
                @pl.when(near)
                def _():
                    self.copy(j, slab, 2, rest=True).start()

                @pl.when(jnp.logical_not(near))
                def _():
                    self.copy(j, slab, 2).start()

        @pl.when(line.at >= k)
        def _():
            forward(line.me - 2 * k, 0, line.has_right, line.odd)

        @pl.when(line.at + k < line.n)
        def _():
            forward(line.me + 2 * k, 1, line.has_left, jnp.logical_not(line.odd))

        if k == 1:
            slab = line.me + 1 - 2 * line.side
            self.copy(j, slab, 2).wait_recv()
            self.shared(j, slab, line.near["dp"]).start()

    def near_slab(self):
        line = self.line
        return line.near["dp"] + 1 - 2 * line.side

    def arrive(self, j):
        line = self.line
        pltpu.make_async_copy(self.own(j), self.full.at[j, line.me], self.keep.at[j]).wait()
        self.copy(j, self.near_slab(), 2, rest=True).wait_recv()
        self.shared(j, self.near_slab(), line.me).wait_recv()
        for place in range(line.n):
            slab = 2 * place + 1 - line.side

            @pl.when((slab != self.near_slab()) & (place != line.at))
            def _(slab=slab):
                self.copy(j, slab, 2).wait_recv()

    def drain(self, j):
        line = self.line
        self.shared(j, line.me + 1 - 2 * line.side, line.near["dp"]).wait_send()
        for place in range(line.n):
            slab = 2 * place + line.side
            near = slab == line.near["dp"]

            @pl.when(near)
            def _(slab=slab):
                self.copy(j, slab, 2, rest=True).wait_send()

            @pl.when(jnp.logical_not(near))
            def _(slab=slab):
                self.copy(j, slab, 2).wait_send()

            @pl.when(line.has_right & (place <= line.at))
            def _(slab=slab):
                self.copy(j, slab, 0).wait_send()

            @pl.when(line.has_left & (place >= line.at))
            def _(slab=slab):
                self.copy(j, slab, 1).wait_send()


class Square:
    def __init__(self):
        me = lax.axis_index("tensor")
        self.me = me
        self.half = lax.rem(me, 2)
        self.mate = {"tensor": me + 1 - 2 * self.half}
        self.across = {"tensor": lax.rem(me + 2, 4)}

    def others(self):
        return [{"tensor": lax.rem(self.me + k, 4)} for k in (1, 2, 3)]


class Total:
    def __init__(self, square, part, got, far, other, send, recv):
        self.square, self.part, self.got, self.far, self.other = square, part, got, far, other
        self.send, self.recv = send, recv

    def first(self, c):
        sq = self.square
        return remote(
            self.part.at[2 * c + 1 - sq.half], self.got.at[c], self.send.at[0, c], self.recv.at[0, c], sq.mate
        )

    def second(self, c):
        sq = self.square
        return remote(self.part.at[2 * c + sq.half], self.far.at[c], self.send.at[1, c], self.recv.at[1, c], sq.across)

    def third(self, c):
        sq = self.square
        return remote(self.part.at[2 * c + sq.half], self.other.at[c], self.send.at[2, c], self.recv.at[2, c], sq.mate)

    def step(self, kind, c):
        slot = 2 * c + self.square.half
        if kind == 0:
            self.first(c).start()
        elif kind == 1:
            self.first(c).wait_recv()
            self.part[slot] = (self.part[slot].astype(F32) + self.got[c].astype(F32)).astype(BF16)
            self.second(c).start()
        elif kind == 2:
            self.second(c).wait()
            self.part[slot] = (self.part[slot].astype(F32) + self.far[c].astype(F32)).astype(BF16)
            self.third(c).start()
        else:
            self.third(c).wait_recv()
            self.first(c).wait_send()
            self.third(c).wait_send()
            self.part[2 * c + 1 - self.square.half] = self.other[c]


class Scatter:
    def __init__(self, line, part, out, near, far, send, recv):
        self.line, self.part, self.out, self.near, self.far = line, part, out, near, far
        self.send, self.recv = send, recv

    def order(self):
        n = self.line.n
        seq = []
        for i in range((n + 1) // 2):
            seq.append(i)
            if n - 1 - i != i:
                seq.append(n - 1 - i)
        return seq

    def cross(self, j, i):
        line = self.line
        return remote(
            self.part.at[j, 2 * i + 1 - line.side], self.near.at[j, i], self.send.at[0, j, i], self.recv.at[0, j, i], line.pair
        )

    def straight(self, j, i, source):
        line = self.line
        return remote(
            self.part.at[j, 2 * i + line.side], self.far.at[j, source], self.send.at[1, j, i], self.recv.at[1, j, source],
            {"dp": 2 * i + line.side},
        )

    def lead(self, j, m):
        self.cross(j, self.order()[m]).start()

    def start(self, j):
        for m in range(self.line.n):
            self.lead(j, m)

    def emit(self, j, turned, right, now=None):
        rows = self.part.shape[2]
        for m, i in enumerate(self.order()):
            value = mm(turned[2 * i * rows : 2 * (i + 1) * rows, :], right[...]).astype(BF16)
            self.part[j, 2 * i] = value[:rows]
            self.part[j, 2 * i + 1] = value[rows:]
            if now is None or m < now:
                self.lead(j, m)

    def product(self, dst, turned, right):
        rows = dst.shape[1]
        for i in range(self.line.n):
            value = mm(turned[2 * i * rows : 2 * (i + 1) * rows, :], right[...]).astype(BF16)
            dst[2 * i] = value[:rows]
            dst[2 * i + 1] = value[rows:]

    def fold(self, j, m):
        line = self.line
        i = self.order()[m]
        self.cross(j, i).wait_recv()
        slot = 2 * i + line.side
        self.part[j, slot] = (self.part[j, slot].astype(F32) + self.near[j, i].astype(F32)).astype(BF16)

        @pl.when(i != line.at)
        def _():
            self.straight(j, i, line.at).start()

    def finish(self, j):
        line = self.line
        out = self.out(j)
        out[...] = self.part[j, line.me].astype(out.dtype)
        for i in range(line.n):
            @pl.when(i != line.at)
            def _(i=i):
                self.straight(j, i, i).wait_recv()
                out[...] += self.far[j, i].astype(out.dtype)

    def drain(self, j):
        for i in range(self.line.n):
            self.cross(j, i).wait_send()

            @pl.when(i != self.line.at)
            def _(i=i):
                self.straight(j, i, self.line.at).wait_send()


class EvenScatter:
    def __init__(self, line, part, out, near, far, send, recv):
        self.line, self.part, self.out, self.near, self.far = line, part, out, near, far
        self.send, self.recv = send, recv
        self.rows = part.shape[2]
        self.cut = upper(self.rows)
        n = line.n
        self.masks = [1] + list(range(n - 1, 1, -1)) + [0]
        self.an_end = (line.at == 0) | (line.at == n - 1)
        self.by_end = (line.at == 1) | (line.at == n - 2)

    def place(self, mask):
        at = self.line.at
        bit, result = 1, at
        while bit <= mask:
            if mask & bit:
                result = result + bit - 2 * bit * lax.rem(at // bit, 2)
            bit *= 2
        return result

    def cross(self, j, m):
        line = self.line
        slab = 2 * self.place(self.masks[m]) + 1 - line.side
        src, dst = self.part.at[j, slab], self.near.at[j, m]
        if self.masks[m] == 1:
            rest = pl.ds(self.cut, self.rows - self.cut)
            src, dst = self.part.at[j, slab, rest], self.near.at[j, m, rest]
        return remote(src, dst, self.send.at[0, j, m], self.recv.at[0, j, m], line.pair)

    def shared(self, j):
        line = self.line
        slab = line.near["dp"] + 1 - 2 * line.side
        some = pl.ds(0, self.cut)
        return remote(
            self.part.at[j, slab, some], self.near.at[j, 0, some], self.send.at[2, j, 0], self.recv.at[2, j, 0], line.near
        )

    def straight(self, j, mask):
        line = self.line
        slab = 2 * self.place(mask) + line.side
        return remote(
            self.part.at[j, slab], self.far.at[j, mask - 1], self.send.at[1, j, mask - 1], self.recv.at[1, j, mask - 1],
            {"dp": slab},
        )

    def through(self, j):
        line = self.line
        n = line.n
        slab = 2 * self.place(n - 1) + line.side
        return remote(
            self.part.at[j, slab], self.far.at[j, n - 1], self.send.at[1, j, n - 2], self.recv.at[1, j, n - 1], line.near
        )

    def lead(self, j, m):
        line = self.line
        if self.masks[m] == 1:
            self.shared(j).start()
        if self.masks[m] == 0:
            self.shared(j).wait_recv()
            slab = line.me + 1 - 2 * line.side
            both = self.part[j, slab, : self.cut].astype(F32) + self.near[j, 0, : self.cut].astype(F32)
            self.part[j, slab, : self.cut] = both.astype(BF16)
        self.cross(j, m).start()

    def emit(self, j, turned, right, now):
        rows = self.rows
        for m, mask in enumerate(self.masks):
            i = self.place(mask)
            left = turned[pl.ds(pl.multiple_of(2 * i * rows, 2 * rows), 2 * rows), :]
            value = mm(left, right[...]).astype(BF16)
            self.part[j, 2 * i] = value[:rows]
            self.part[j, 2 * i + 1] = value[rows:]
            if m < now:
                self.lead(j, m)

    def fold(self, j, m):
        line = self.line
        n = line.n
        mask = self.masks[m]
        self.cross(j, m).wait_recv()
        slot = 2 * self.place(mask) + line.side
        if mask == 1:
            both = self.part[j, slot, self.cut :].astype(F32) + self.near[j, m, self.cut :].astype(F32)
            self.part[j, slot, self.cut :] = both.astype(BF16)
        else:
            self.part[j, slot] = (self.part[j, slot].astype(F32) + self.near[j, m].astype(F32)).astype(BF16)
        if mask == n - 1:
            @pl.when(self.an_end)
            def _():
                self.through(j).start()

            @pl.when(jnp.logical_not(self.an_end))
            def _():
                self.straight(j, mask).start()
        elif mask:
            if mask == n - 2:
                @pl.when(self.by_end)
                def _():
                    self.through(j).wait_recv()
                    self.part[j, slot] = (self.part[j, slot].astype(F32) + self.far[j, n - 1].astype(F32)).astype(BF16)

            self.straight(j, mask).start()

    def finish(self, j):
        line = self.line
        n = line.n
        out = self.out(j)
        value = self.part[j, line.me].astype(out.dtype)
        for mask in range(1, n - 1):
            self.straight(j, mask).wait_recv()
            value = value + self.far[j, mask - 1].astype(out.dtype)
        out[...] = value

        @pl.when(jnp.logical_not(self.an_end))
        def _():
            self.straight(j, n - 1).wait_recv()
            out[...] += self.far[j, n - 2].astype(out.dtype)

    def drain(self, j):
        n = self.line.n
        self.shared(j).wait_send()
        for m in range(n):
            self.cross(j, m).wait_send()
        for mask in range(1, n):
            self.straight(j, mask).wait_send()


def mm(left, right, dims=NN, precision=None):
    return lax.dot_general(left, right, dims, precision=precision, preferred_element_type=F32)


def sigmoid(v):
    return 0.5 * jnp.tanh(0.5 * v) + 0.5


def softplus(v):
    return jnp.maximum(v, 0.0) + jnp.log1p(jnp.exp(-jnp.abs(v)))


def split16(v):
    top = v.astype(BF16)
    return top, (v - top.astype(F32)).astype(BF16)


def expand(v, ind):
    top, rest = split16(v)
    return mm(top, ind) + mm(rest, ind)


def headsum(v, ind):
    return mm(v.astype(BF16), ind, NT)


def rowsum(v):
    return mm(jnp.ones((8, v.shape[1]), BF16), v.astype(BF16), NT)[0:1, :]


def iotas(n):
    return (
        lax.broadcasted_iota(jnp.int32, (n, n), 0),
        lax.broadcasted_iota(jnp.int32, (n, n), 1),
    )


def colsum(v):
    return jnp.sum(v, axis=0, keepdims=True)


def conv_pre(ext, par, n):
    total = par[4:5, :] + par[0:1, :] * ext[5 : 5 + n, :]
    for tap in range(1, 4):
        total = total + par[tap : tap + 1, :] * ext[5 + tap : 5 + tap + n, :]
    return total


def scan_prep(small, hp, ind, n):
    rows, cols = iotas(n)
    raw = small[:, 2 * STATE :] + hp[0:1, :]
    step = softplus(raw)
    rate = -jnp.exp(hp[1:2, :])
    lower = jnp.where(rows >= cols, 1.0, 0.0).astype(F32)
    cs = mm(lower, step * rate, precision=HIGH)
    tail = jnp.exp(cs[n - 1 : n, :] - cs)
    wide = mm(jnp.concatenate([step, jnp.exp(cs), tail], axis=0).astype(BF16), ind)
    return raw, step, rate, cs, wide[0:n], wide[n : 2 * n], wide[2 * n : 3 * n]


def block_of(slabs, at, rows):
    step = math.gcd(LANES, rows)
    pieces = []
    for k in range(LANES // step):
        row = at * LANES + k * step
        slab = row // rows
        pieces.append(slabs[slab, pl.ds(pl.multiple_of(row - slab * rows, step), step), :])
    return pieces[0] if len(pieces) == 1 else jnp.concatenate(pieces, axis=0)


def put_params(cp, sp, hp, ind, layer, params):
    conv, bias, norm, convs, biass, head = params
    width = cp.shape[1]
    row = lax.broadcasted_iota(jnp.int32, (LANES, width), 0)
    lane = lax.broadcasted_iota(jnp.int32, (LANES, width), 1)
    ind[...] = jnp.where(lane // HEAD == row, 1.0, 0.0).astype(BF16)
    hp[...] = head[layer]
    cp[0:4, :] = conv[layer]
    cp[4:5, :] = bias[layer : layer + 1, :]
    cp[5:6, :] = norm[layer : layer + 1, :]
    cp[6:8, :] = expand(hp[...], ind[...])[2:4, :]
    sp[0:4, :] = convs[layer]
    sp[4:5, :] = biass[layer : layer + 1, :]


def place_rows(dst, at, value):
    r = dst.shape[1]
    for g in range(0, value.shape[0], 16):
        dst[(at + g) // r, (at + g) % r : (at + g) % r + 16, :] = value[g : g + 16].astype(dst.dtype)


def pack_rows(size):
    return -(-PACK // (16 * size)) * 16


def put_pack(dst, me, turned, steps_low, sdel, dcp, dsp, dhp, dgain):
    model = turned.shape[0]
    quarter = model // 4
    w = sdel.shape[1]

    def empty(n):
        return jnp.zeros((n, w), F32)

    place_rows(dst, 0, mm(turned[pl.ds(pl.multiple_of(me * quarter, quarter), quarter), :], sdel[...]))
    place_rows(dst, quarter, jnp.concatenate([dsp, empty(8)], axis=0))
    grown = mm(turned[...], steps_low[...]).T[:16]
    at = quarter + 16
    for b in range(model // w):
        place_rows(dst, at, grown[:, b * w : (b + 1) * w])
        at += 16
    place_rows(dst, at, jnp.concatenate([dcp[:, :w], dcp[:, w : 2 * w]], axis=0))
    place_rows(dst, at + 16, jnp.concatenate([dcp[:, 2 * w :], jnp.concatenate([dhp, dhp], axis=1)], axis=0))
    rows = [dgain[:, b * w : (b + 1) * w] for b in range(model // w)]
    place_rows(dst, at + 32, jnp.concatenate(rows + [empty(16 - len(rows))], axis=0))
    assert at + 48 == PACK


class Smalls:
    def __init__(self, line, square, pack, near, away, own, full, wide, sems):
        send, recv, keep, gsend, grecv, self.xsend, self.xrecv = sems
        self.square, self.full, self.wide = square, full, wide
        self.layers = range(pack.shape[0])
        self.sum = Scatter(line, pack, lambda j: own.at[j], near, away, send, recv)
        self.spread = Gather(line, lambda j: own.at[j], full, keep, gsend, grecv)

    def swap(self, k):
        sq = self.square
        slot = (sq.me, sq.me, lax.rem(sq.me + 2, 4))[k]
        who = (sq.across, sq.mate, sq.mate)[k]
        return remote(self.wide.at[slot], self.wide.at[slot], self.xsend.at[k], self.xrecv.at[k], who)

    def start(self):
        for j in self.layers:
            self.sum.start(j)

    def fold(self):
        for j in self.layers:
            for m in range(self.sum.line.n):
                self.sum.fold(j, m)

    def turn(self):
        for j in self.layers:
            self.sum.finish(j)
            self.spread.start(j)

    def relay(self, k):
        for j in self.layers:
            self.spread.relay(j, k)

    def cross(self):
        for j in self.layers:
            self.spread.arrive(j)
            flat = self.full[j].reshape(-1, self.full.shape[3])
            self.wide[self.square.me, j] = flat[: self.wide.shape[2]]
        self.swap(0).start()
        self.swap(1).start()

    def cross_on(self):
        self.swap(0).wait_recv()
        self.swap(2).start()

    def end(self):
        self.swap(1).wait_recv()
        self.swap(2).wait_recv()
        for k in range(3):
            self.swap(k).wait_send()
        for j in self.layers:
            self.sum.drain(j)
            self.spread.drain(j)


def smalls_scratch(size, w, layers):
    r, n = pack_rows(size), size // 2
    buffers = [
        pltpu.VMEM((layers, size, r, w), BF16),
        pltpu.VMEM((layers, n, r, w), BF16),
        pltpu.VMEM((layers, n, r, w), BF16),
        pltpu.VMEM((layers, r, w), BF16),
        pltpu.VMEM((layers, size, r, w), BF16),
        pltpu.VMEM((4, layers, SPAN, w), BF16),
    ]
    sems = [
        pltpu.SemaphoreType.DMA((2, layers, n)),
        pltpu.SemaphoreType.DMA((2, layers, n)),
        pltpu.SemaphoreType.DMA((layers,)),
        pltpu.SemaphoreType.DMA((layers, 3, size)),
        pltpu.SemaphoreType.DMA((layers, size)),
        pltpu.SemaphoreType.DMA((3,)),
        pltpu.SemaphoreType.DMA((3,)),
    ]
    return buffers + sems


def forward_body(*refs, size, heads, per, steps, layer):
    refs = list(refs)

    def take(n):
        got = refs[:n]
        del refs[:n]
        return got

    mid = layer > 0
    (res_hbm,) = take(1)
    if mid:
        scaled_hbm, wout_hbm, sq_ref = take(3)
    state_hbm, step_hbm, in_hbm, out_hbm, gain_ref = take(5)
    params = take(6)
    if mid:
        new_hbm, sums_ref = take(2)
    normed_hbm, rnorm_ref, small_hbm, inner_hbm, gate_hbm, wt_hbm, full_hbm, ssd_ref, scaled_ref, sqs_ref, st_ref = take(11)
    if mid:
        scaled_in, wout, part, got, far, other, rows_got, facs, fresh, sends, recvs, rsend, rrecv = take(13)
    res, wstate, wt, slabs, normed, turned, small, inner, gate, ext, exts, state = take(12)
    cp_ref, sp_ref, hp_ref, ind_ref, keep, gsend, grecv, load, sems = take(9)
    assert not refs

    n = CHUNK
    tokens_n, model = res.shape
    width = inner.shape[1]
    top = 2 * width + 2 * STATE
    i = pl.program_id(0)
    line = Line(size)
    square = Square()
    job = Gather(line, lambda j: out_hbm.at[layer] if j == 2 else in_hbm.at[layer, 1 - j], slabs, keep, gsend, grecv)
    outgoing = [(turned, normed_hbm), (small, small_hbm), (inner, inner_hbm), (gate, gate_hbm)]
    outgoing += [(wt, wt_hbm), (slabs.at[2], full_hbm)]
    if mid:
        outgoing.append((fresh, new_hbm))

    def flush(k):
        return pltpu.make_async_copy(*outgoing[k], sems.at[k])


    @pl.when(i == 0)
    def _():
        pairs = [(res_hbm, res), (state_hbm.at[layer], wstate), (step_hbm.at[layer], wt.at[pl.ds(top, LANES), :])]
        if mid:
            pairs = [(scaled_hbm, scaled_in), (wout_hbm, wout)] + pairs
        loads = [pltpu.make_async_copy(src, dst, load.at[k]) for k, (src, dst) in enumerate(pairs)]
        for copy in loads:
            copy.start()
        line.greet(pltpu.get_barrier_semaphore(), square.others() if mid else ())
        job.start(0)
        put_params(cp_ref, sp_ref, hp_ref, ind_ref, layer, params)
        ticks = [functools.partial(job.relay, 0, k) for k in range(1, line.n)]
        ticks.append(functools.partial(job.start, 1))
        span = model // LANES

        def project(j, dst):
            weight = slabs[j].reshape(model, width)

            def tile(t, _):
                rows = pl.ds(pl.multiple_of(t * TILE, TILE), TILE)
                dst[rows, :] = mm(normed[rows, :], weight)
                return 0

            lax.fori_loop(0, tokens_n // TILE, tile, 0)

        def turn_inner(b, _):
            wt[:width, pl.ds(pl.multiple_of(b * LANES, LANES), LANES)] = block_of(slabs.at[0], b, slabs.shape[2]).T
            return 0

        def settle():
            job.arrive(0)
            if not mid:
                project(0, inner)
                flush(2).start()
            lax.fori_loop(0, span, turn_inner, 0)

        ticks.append(functools.partial(job.relay, 1, 1))
        ticks.append(settle)
        ticks += [functools.partial(job.relay, 1, k) for k in range(2, line.n)]
        ticks.append(functools.partial(job.start, 2))

        if mid:
            chunks = model // SLICE
            half = tokens_n // 2
            sums = Total(square, part, got, far, other, sends, recvs)
            copies = [
                remote(sq_ref, rows_got.at[square.me], rsend.at[k], rrecv.at[k], who)
                for k, who in enumerate(square.others())
            ]
            for copy in copies:
                copy.start()
            loads[0].wait()
            loads[1].wait()
            for c in range(chunks):
                value = mm(scaled_in[...], wout[c * SLICE : (c + 1) * SLICE, :], NT).astype(BF16)
                part[2 * c] = value[:half]
                part[2 * c + 1] = value[half:]
                sums.step(0, c)
                if c:
                    sums.step(1, c - 1)
            sums.step(1, chunks - 1)
            rows_got[square.me] = sq_ref[...]
            for copy in copies:
                copy.wait()
            total = (rows_got[0] + rows_got[1]) + (rows_got[2] + rows_got[3])
            sums_ref[...] = total
            factor = lax.rsqrt(total / INNER + EPS)
            for t in range(tokens_n // LANES):
                facs[t * LANES : (t + 1) * LANES, :] = jnp.broadcast_to(factor[t], (LANES, LANES)).T
            loads[2].wait()

            def use(c):
                for h in range(2):
                    where = slice(h * half, (h + 1) * half)
                    for s in range(SLICE // LANES):
                        lanes = slice(c * SLICE + s * LANES, c * SLICE + (s + 1) * LANES)
                        value = part[2 * c + h, :, s * LANES : (s + 1) * LANES].astype(F32)
                        fresh[where, lanes] = res[where, lanes].astype(F32) + facs[where, :] * value

            spread = max(1, -(-len(ticks) // chunks))
            for c in range(chunks):
                for tick in ticks[:spread]:
                    tick()
                ticks = ticks[spread:]
                sums.step(2, c)
                if c:
                    sums.step(3, c - 1)
                    use(c - 1)
            sums.step(3, chunks - 1)
            use(chunks - 1)
            flush(6).start()
        else:
            loads[0].wait()
        loads[-2].wait()
        loads[-1].wait()
        for b in range(2 * STATE // LANES):
            rows = slice(2 * width + b * LANES, 2 * width + (b + 1) * LANES)
            wt[rows, :] = wstate[:, b * LANES : (b + 1) * LANES].T

        def norm(t, _):
            rows = pl.ds(pl.multiple_of(t * TILE, TILE), TILE)
            value = (fresh if mid else res)[rows, :].astype(F32)
            scale = lax.rsqrt(jnp.sum(value * value, axis=1, keepdims=True) / model + EPS)
            low = (value * scale * gain_ref[layer : layer + 1, :]).astype(BF16)
            rnorm_ref[rows, :] = scale
            normed[rows, :] = low
            turned[:, rows] = low.T
            small[rows, : 2 * STATE] = mm(low, wstate[...])
            small[rows, 2 * STATE :] = mm(low, wt[top:, :], NT)
            return 0

        lax.fori_loop(0, tokens_n // TILE, norm, 0)
        flush(0).start()
        flush(1).start()
        for tick in ticks:
            tick()

        if mid:
            project(0, inner)
            flush(2).start()
        job.arrive(1)
        project(1, gate)
        flush(3).start()

    for k in range(1, line.n):
        @pl.when(i == 1 + (k - 1) * steps // line.n)
        def _(k=k):
            job.relay(2, k)

    @pl.when(i > 0)
    def _():
        at = i - 1
        where = pl.ds(pl.multiple_of(at * n, n), n)

        @pl.when(lax.rem(at, per) == 0)
        def _():
            ext[0:8, :] = jnp.zeros((8, width), F32)
            exts[0:8, :] = jnp.zeros((8, 2 * STATE), F32)
            state[...] = jnp.zeros_like(state)

        rows, cols = iotas(n)
        ind = ind_ref[...]
        ext[8 : 8 + n, :] = inner[where, :]
        pre = conv_pre(ext, cp_ref, n)
        x = pre * sigmoid(pre)
        ext[0:8, :] = ext[n : n + 8, :]
        mini = small[where, :]
        exts[8 : 8 + n, :] = mini[:, : 2 * STATE]
        pres = conv_pre(exts, sp_ref, n)
        bc = (pres * sigmoid(pres)).astype(BF16)
        exts[0:8, :] = exts[n : n + 8, :]
        key, query = bc[:, :STATE], bc[:, STATE:]

        _, step, rate, cs, wide_step, wide_cs, wide_tail = scan_prep(mini, hp_ref, ind, n)
        cs2 = cs * LOG2E
        cs2t = cs2.T
        xs = x * wide_step
        lane = lax.broadcasted_iota(jnp.int32, (1, width), 1)
        half = jnp.where(lax.rem(lane, 2 * HEAD) < HEAD, 1.0, 0.0).astype(BF16)
        xsb = xs.astype(BF16)
        xs0 = xsb * half
        xs1 = xsb - xs0
        before = state[...]
        low = before.astype(BF16)
        st_ref[0] = low
        carried = mm(query, low) * wide_cs
        xw = (xs * wide_tail).astype(BF16)
        state[...] = before * wide_cs[n - 1 : n, :] + mm(key, xw, TN)
        scores = jnp.where(rows >= cols, mm(query, key, NT), 0.0)
        for pair in range(heads // 2):
            lanes = slice(pair * 2 * HEAD, (pair + 1) * 2 * HEAD)
            mats = []
            for h in (2 * pair, 2 * pair + 1):
                dec = jnp.exp2(jnp.minimum(cs2[:, h : h + 1] - cs2t[h : h + 1, :], 0.0))
                mats.append((scores * dec).astype(BF16))
            local = mm(
                jnp.concatenate(mats, axis=1),
                jnp.concatenate([xs0[:, lanes], xs1[:, lanes]], axis=0),
            )
            ssd_ref[:, lanes] = local + carried[:, lanes] + cp_ref[6:7, lanes] * x[:, lanes]
        gates = gate[where, :]
        gated = ssd_ref[...] * (gates * sigmoid(gates))
        sqs_ref[0] = rowsum(gated * gated)
        scaled_ref[...] = (gated * cp_ref[5:6, :]).astype(BF16)

        span = model // LANES
        share = -(-span // steps)
        for k in range(share):
            b = at * share + k

            @pl.when(b < span)
            def _(b=b):
                piece = block_of(slabs.at[1], b, slabs.shape[2]).T
                wt[width : 2 * width, pl.ds(pl.multiple_of(b * LANES, LANES), LANES)] = piece

    @pl.when(i == steps)
    def _():
        flush(4).start()
        job.arrive(2)
        flush(5).start()
        for j in range(3):
            job.drain(j)
        for k in range(len(outgoing)):
            flush(k).wait()


def forward(res, stateproj, steps_w, inproj, outt, gain, params, heads, size, layer, out=None):
    tokens_n, model = res.shape
    _, _, rows, width = inproj.shape
    top = 2 * width + 2 * STATE + LANES
    steps = tokens_n // CHUNK
    mid = out is not None
    hbm = pl.BlockSpec(memory_space=pl.ANY)
    chunks = model // SLICE

    def whole(a):
        return pl.BlockSpec(a.shape, lambda i: (0,) * len(a.shape))

    def row(w):
        return pl.BlockSpec((CHUNK, w), lambda i: (jnp.maximum(i - 1, 0), 0))

    args, in_specs, out_specs, out_shape, scratch = [res], [hbm], [], [], []
    if mid:
        args += list(out)
        in_specs += [hbm, hbm, whole(out[2])]
        out_specs += [hbm, whole(out[2])]
        out_shape += [jax.ShapeDtypeStruct(res.shape, F32), jax.ShapeDtypeStruct(out[2].shape, F32)]
        chunk = pltpu.VMEM((chunks, tokens_n // 2, SLICE), BF16)
        scratch += [
            pltpu.VMEM(out[0].shape, BF16),
            pltpu.VMEM(out[1].shape, BF16),
            pltpu.VMEM((2 * chunks, tokens_n // 2, SLICE), BF16),
            chunk, chunk, chunk,
            pltpu.VMEM((4,) + out[2].shape, F32),
            pltpu.VMEM((tokens_n, LANES), F32),
            pltpu.VMEM(res.shape, F32),
            pltpu.SemaphoreType.DMA((3, chunks)),
            pltpu.SemaphoreType.DMA((3, chunks)),
            pltpu.SemaphoreType.DMA((3,)),
            pltpu.SemaphoreType.DMA((3,)),
        ]
    args += [stateproj, steps_w, inproj, outt, gain, *params]
    in_specs += [hbm, hbm, hbm, hbm, whole(gain)] + [whole(v) for v in params]
    out_specs += [
        hbm, pl.BlockSpec((tokens_n, 1), lambda i: (0, 0)), hbm, hbm, hbm, hbm, hbm,
        row(width), row(width),
        pl.BlockSpec((1, 1, CHUNK), lambda i: (jnp.maximum(i - 1, 0), 0, 0)),
        pl.BlockSpec((1, STATE, width), lambda i: (jnp.maximum(i - 1, 0), 0, 0)),
    ]
    out_shape += [
        jax.ShapeDtypeStruct((model, tokens_n), BF16),
        jax.ShapeDtypeStruct((tokens_n, 1), F32),
        jax.ShapeDtypeStruct((tokens_n, 2 * STATE + LANES), F32),
        jax.ShapeDtypeStruct((tokens_n, width), F32),
        jax.ShapeDtypeStruct((tokens_n, width), F32),
        jax.ShapeDtypeStruct((top, model), BF16),
        jax.ShapeDtypeStruct((size, rows, width), BF16),
        jax.ShapeDtypeStruct((tokens_n, width), F32),
        jax.ShapeDtypeStruct((tokens_n, width), BF16),
        jax.ShapeDtypeStruct((steps, 1, CHUNK), F32),
        jax.ShapeDtypeStruct((steps, STATE, width), BF16),
    ]
    scratch += [
        pltpu.VMEM(res.shape, res.dtype),
        pltpu.VMEM((model, 2 * STATE), BF16),
        pltpu.VMEM((top, model), BF16),
        pltpu.VMEM((3, size, rows, width), BF16),
        pltpu.VMEM((tokens_n, model), BF16),
        pltpu.VMEM((model, tokens_n), BF16),
        pltpu.VMEM((tokens_n, 2 * STATE + LANES), F32),
        pltpu.VMEM((tokens_n, width), F32),
        pltpu.VMEM((tokens_n, width), F32),
        pltpu.VMEM((CHUNK + 8, width), F32),
        pltpu.VMEM((CHUNK + 8, 2 * STATE), F32),
        pltpu.VMEM((STATE, width), F32),
        pltpu.VMEM((8, width), F32),
        pltpu.VMEM((8, 2 * STATE), F32),
        pltpu.VMEM((8, LANES), F32),
        pltpu.VMEM((LANES, width), BF16),
        pltpu.SemaphoreType.DMA((3,)),
        pltpu.SemaphoreType.DMA((3, 3, size)),
        pltpu.SemaphoreType.DMA((3, size)),
        pltpu.SemaphoreType.DMA((5,)),
        pltpu.SemaphoreType.DMA((7,)),
    ]
    return pl.pallas_call(
        functools.partial(forward_body, size=size, heads=heads, per=LEN // CHUNK, steps=steps, layer=layer),
        grid=(steps + 1,),
        in_specs=in_specs,
        out_specs=out_specs,
        out_shape=out_shape,
        scratch_shapes=scratch,
        compiler_params=pltpu.CompilerParams(
            collective_id=min(layer, 1), has_side_effects=True, vmem_limit_bytes=VMEM_LIMIT
        ),
        name="forward",
    )(*args)


def back_body(*refs, heads, per, size, steps, layer, last):
    refs = list(refs)

    def take(n):
        got = refs[:n]
        del refs[:n]
        return got

    up_ref, sq_ref, gate_ref, ssd_ref, inner_ref, iprev_ref, small_ref, sprev_ref, st_ref, res_ref, rn_ref = take(11)
    gain_ref = take(1)[0]
    params = take(6)
    wout_hbm, scaled_hbm, wt_hbm, normed_hbm = take(4)
    if not last:
        next_normed, next_steps, next_sdel, next_inner, next_dcp, next_dsp, next_dhp, next_dgain = take(8)
    new_ref, grad_hbm = take(2)
    if last:
        held_hbm, sdsum_ref, steplow_ref, dcp_ref, dsp_ref, dhp_ref, dgain_ref, mixed_ref = take(8)
    else:
        full_hbm, wide_hbm = take(2)
    ext, exts, cde, cdes, dstate, rq, cp_ref, sp_ref, hp_ref, ind_ref = take(10)
    wout, scaled, wt, turned, dy, glow, ilow, frow, srow, sgot = take(10)
    part, near, away, tpart, got, far, other = take(7)
    load, rsend, rrecv, ssend, srecv, sends, recvs, gsem = take(8)
    if last:
        held, fgot, opart, ogot, ofar, oother, fsend, frecv, osends, orecvs = take(10)
    else:
        dcp_ref, dsp_ref, dhp_ref, dgain_ref = take(4)
        sd_all = scaled.at[:, pl.ds(0, 2 * STATE)]
        step_all = scaled.at[:, pl.ds(2 * STATE, LANES)]
        buffers = take(6)
        sems = take(7)
    assert not refs

    n = CHUNK
    model = up_ref.shape[1]
    i = pl.program_id(0)
    begin_gate = steps
    begin_scan = begin_gate + steps
    begin_norm = begin_scan + steps
    end = begin_norm + steps - 1
    line = Line(size)
    square = Square()
    rows_own = part.shape[2]
    count = part.shape[0]
    kind = Scatter if last else EvenScatter
    job = kind(line, part, lambda j: dy.at[pl.ds(j * rows_own, rows_own), :], near, away, ssend, srecv)
    sums = Total(square, tpart, got, far, other, sends, recvs)
    if last:
        outs = Total(square, opart, ogot, ofar, oother, osends, orecvs)
        half = steps * n // 2
        slices = model // SLICE
    else:
        minis = Smalls(line, square, *buffers, sems)
    moves = [(wout_hbm, wout), (scaled_hbm, scaled), (wt_hbm, wt), (normed_hbm, turned)]
    if last:
        moves.append((held, held_hbm))
    else:
        tokens_n = steps * n
        spots = (wt.at[pl.ds(0, model), pl.ds(0, tokens_n)],)
        spots += tuple(
            wt.at[pl.ds(0, tokens_n), pl.ds(tokens_n + at, w)] for at, w in ((0, LANES), (LANES, 2 * STATE))
        )
        moves += [(next_normed, spots[0]), (next_steps, spots[1]), (next_sdel, spots[2]), (next_inner, part.at[3])]

    def move(k):
        return pltpu.make_async_copy(*moves[k], load.at[k])

    places = line.n

    def spaced(begin, stop, m):
        return begin + m * (stop - begin) // places

    middle = begin_scan + steps // 2
    if last:
        folds = [(spaced(begin_scan, middle, m), 0, m) for m in range(places)]
        folds += [(spaced(middle, begin_norm, m) + 1, 1, m) for m in range(places)]
    else:
        folds = [(spaced(begin_gate - 3, begin_scan + 3, m), 3, m) for m in range(places)]
        folds += [(spaced(begin_scan + 1, begin_norm - 1, m), 0, m) for m in range(places)]
        folds += [(spaced(begin_norm - 2, begin_norm + 5, m), 1, m) for m in range(places)]
        behind = [(2, 3), (begin_gate + 2, 0), (begin_scan + 1, 1)]

    def column(row):
        return jnp.broadcast_to(row, (n, n)).T[:, 0:1]

    @pl.when(i == 0)
    def _():
        for k in range(3):
            move(k).start()
        if not last:
            move(7).start()
        put_params(cp_ref, sp_ref, hp_ref, ind_ref, layer, params)
        rq[...] = jnp.zeros_like(rq)
        line.greet_all(pltpu.get_barrier_semaphore(), square.others())
        if last:
            rows = [
                remote(sq_ref, fgot.at[square.me], fsend.at[k], frecv.at[k], who)
                for k, who in enumerate(square.others())
            ]
            for copy in rows:
                copy.start()
            fgot[square.me] = sq_ref[...]
            move(0).wait()
            move(1).wait()
            for c in range(slices):
                value = mm(scaled[...], wout[c * SLICE : (c + 1) * SLICE, :], NT).astype(BF16)
                opart[2 * c] = value[:half]
                opart[2 * c + 1] = value[half:]
                outs.step(0, c)
            outs.step(1, 0)
            for copy in rows:
                copy.wait()
            total = (fgot[0] + fgot[1]) + (fgot[2] + fgot[3])
        else:
            move(7).wait()
            for m in range(places - 1):
                job.lead(3, m)
            total = sq_ref[...]
            move(0).wait()
            move(1).wait()
        dcp_ref[...] = jnp.zeros_like(dcp_ref)
        dsp_ref[...] = jnp.zeros_like(dsp_ref)
        dhp_ref[...] = jnp.zeros_like(dhp_ref)
        dgain_ref[...] = jnp.zeros_like(dgain_ref)
        frow[...] = lax.rsqrt(total / INNER + EPS)

    ind = ind_ref[...]
    for at, j, m in folds:
        @pl.when(i == at)
        def _(j=j, m=m):
            job.fold(j, m)

    if not last:
        for at, j in behind:
            @pl.when(i == at)
            def _(j=j):
                job.lead(j, places - 1)

    @pl.when(i < begin_gate)
    def _():
        rows = pl.ds(pl.multiple_of(i * n, n), n)
        low = (column(frow[i]) * up_ref[...].astype(F32)).astype(BF16)
        turned[:, rows] = low.T
        sd = mm(low, wout[...])
        dy[rows, :] = sd
        piece = scaled[rows, :]
        srow[i] = rowsum(piece.astype(F32) * sd)

    @pl.when(i == begin_gate - 1)
    def _():
        copies = [
            remote(srow, sgot.at[square.me], rsend.at[k], rrecv.at[k], who) for k, who in enumerate(square.others())
        ]
        for copy in copies:
            copy.start()
        job.emit(0, turned, scaled, places if last else places - 1)
        move(3).start()
        sgot[square.me] = srow[...]
        for copy in copies:
            copy.wait()
        srow[...] = (sgot[0] + sgot[1]) + (sgot[2] + sgot[3])

    if last:
        @pl.when(i == steps // 2)
        def _():
            outs.step(1, 1)

        @pl.when((i >= begin_gate) & (i < begin_gate + slices - 2))
        def _():
            outs.step(1, i - begin_gate + 2)

    @pl.when((i >= begin_gate) & (i < begin_scan))
    def _():
        c = i - begin_gate
        rows = pl.ds(pl.multiple_of(c * n, n), n)
        coef = column(frow[c] * frow[c] * srow[c]) / INNER
        gate = gate_ref[...]
        gsig = sigmoid(gate)
        gact = gate * gsig
        ssd = ssd_ref[...]
        sd = dy[rows, :]
        gated = ssd * gact
        gd = cp_ref[5:6, :] * sd - coef * gated
        dcp_ref[5:6, :] += colsum(gated * sd)
        dy[rows, :] = gd * gact
        glow[rows, :] = (gd * ssd * (gsig + gact * (1.0 - gsig))).astype(BF16)

    @pl.when(i == begin_scan - 1)
    def _():
        move(3).wait()
        job.emit(1, turned, glow, places if last else places - 1)
        move(2).wait()

    @pl.when((i >= begin_scan) & (i < begin_norm))
    def _():
        q = i - begin_scan
        chunk = steps - 1 - q
        where = pl.ds(pl.multiple_of(chunk * n, n), n)

        @pl.when(lax.rem(chunk, per) == per - 1)
        def _():
            cde[n : n + 8, :] = jnp.zeros((8, cde.shape[1]), F32)
            cdes[n : n + 8, :] = jnp.zeros((8, cdes.shape[1]), F32)
            dstate[...] = jnp.zeros_like(dstate)

        keep = jnp.where(lax.rem(chunk, per) == 0, 0.0, 1.0).astype(F32)
        rows, cols = iotas(n)
        ext[0:8, :] = iprev_ref[...] * keep
        ext[8 : 8 + n, :] = inner_ref[...]
        exts[0:8, :] = sprev_ref[:, : 2 * STATE] * keep
        exts[8 : 8 + n, :] = small_ref[:, : 2 * STATE]
        pre = conv_pre(ext, cp_ref, n)
        sig = sigmoid(pre)
        x = pre * sig
        slope = sig + x * (1.0 - sig)
        pres = conv_pre(exts, sp_ref, n)
        sigs = sigmoid(pres)
        acts = pres * sigs
        slopes = sigs + acts * (1.0 - sigs)
        bc = acts.astype(BF16)
        key, query = bc[:, :STATE], bc[:, STATE:]
        dyc = dy[where, :]

        raw, step, rate, cs, wide_step, wide_cs, wide_tail = scan_prep(small_ref, hp_ref, ind, n)
        cs2 = cs * LOG2E
        cs2t = cs2.T
        xs = x * wide_step
        xsb = xs.astype(BF16)
        dyb = dyc.astype(BF16)
        lane = lax.broadcasted_iota(jnp.int32, (1, xs.shape[1]), 1)
        half = jnp.where(lax.rem(lane, 2 * HEAD) < HEAD, 1.0, 0.0).astype(BF16)
        dy0 = dyb * half
        dy1 = dyb - dy0
        low = st_ref[0]
        dst = dstate[...]
        dlow = dst.astype(BF16)
        dye = dyc * wide_cs
        dyeb = dye.astype(BF16)
        up = headsum(dye * mm(query, low), ind)
        dxs_state = wide_tail * mm(key, dlow)
        down = headsum(xs * dxs_state, ind)
        qdel = mm(dyeb, low, NT)
        kdel = mm((xs * wide_tail).astype(BF16), dlow, NT)
        through = headsum(jnp.broadcast_to(colsum(low.astype(F32) * dst), (8, dst.shape[1])), ind)[0:1, :]
        through = through * jnp.exp(cs[n - 1 : n, :])
        dstate[...] = dst * wide_cs[n - 1 : n, :] + mm(query, dyeb, TN)

        scores = jnp.where(rows <= cols, mm(key, query, NT), 0.0)
        dscores = jnp.zeros((n, n), F32)
        colq = jnp.zeros((n, LANES), F32)
        lane = lax.broadcasted_iota(jnp.int32, (n, LANES), 1)
        dxs = []
        for pair in range(heads // 2):
            lanes = slice(pair * 2 * HEAD, (pair + 1) * 2 * HEAD)
            stacked = jnp.concatenate([dy0[:, lanes], dy1[:, lanes]], axis=0)
            both = mm(xsb[:, lanes], stacked, NT)
            mats = []
            for which, h in enumerate((2 * pair, 2 * pair + 1)):
                dec = jnp.exp2(jnp.minimum(cs2t[h : h + 1, :] - cs2[:, h : h + 1], 0.0))
                mats.append((scores * dec).astype(BF16))
                term = dec * both[:, which * n : (which + 1) * n]
                dscores = dscores + term
                quad = scores * term
                rq[h : h + 1, :] = colsum(quad)
                colq = jnp.where(lane == h, jnp.sum(quad, axis=1, keepdims=True), colq)
            dxs.append(mm(jnp.concatenate(mats, axis=1), stacked))
        dxs = jnp.concatenate(dxs, axis=1) + dxs_state
        dscores = jnp.where(rows <= cols, dscores, 0.0).astype(BF16)
        kdel = kdel + mm(dscores, query)
        qdel = qdel + mm(dscores, key, TN)

        upper = jnp.where(rows <= cols, 1.0, 0.0).astype(F32)
        strict = jnp.where(rows > cols, 1.0, 0.0).astype(F32)
        da = mm(upper, rq[...].T - colq + up, precision=HIGH) + mm(strict, down, precision=HIGH) + through
        grown = headsum(x * dxs, ind) + rate * da
        step_pre = grown * sigmoid(raw)
        steplow = step_pre.astype(BF16)
        if last:
            steplow_ref[...] = steplow
        else:
            step_all[where, :] = steplow
        dhp_ref[0:1, :] += colsum(step_pre)
        dhp_ref[1:2, :] += rate * colsum(step * da)
        dcp_ref[6:7, :] += colsum(dyc * x)

        cd = (dxs * wide_step + cp_ref[6:7, :] * dyc) * slope
        cde[0:n, :] = cd
        center = ext[8 : 8 + n, :]
        total = cp_ref[3:4, :] * cd
        dcp_ref[3:4, :] += colsum(cd * center)
        for tap in range(3):
            shifted = cde[3 - tap : 3 - tap + n, :]
            total = total + cp_ref[tap : tap + 1, :] * shifted
            dcp_ref[tap : tap + 1, :] += colsum(shifted * center)
        inner_low = total.astype(BF16)
        ilow[where, :] = inner_low
        dcp_ref[4:5, :] += colsum(cd)
        cde[n : n + 8, :] = cde[0:8, :]

        cds = jnp.concatenate([kdel, qdel], axis=1) * slopes
        cdes[0:n, :] = cds
        center = exts[8 : 8 + n, :]
        total = sp_ref[3:4, :] * cds
        dsp_ref[3:4, :] += colsum(cds * center)
        for tap in range(3):
            shifted = cdes[3 - tap : 3 - tap + n, :]
            total = total + sp_ref[tap : tap + 1, :] * shifted
            dsp_ref[tap : tap + 1, :] += colsum(shifted * center)
        sdel = total.astype(BF16)
        dsp_ref[4:5, :] += colsum(cds)
        cdes[n : n + 8, :] = cdes[0:8, :]

        lows = jnp.concatenate([inner_low, glow[where, :], sdel, steplow], axis=1)
        value = mm(lows, wt[...]).astype(BF16)
        tpart[2 * q, :, :model] = value[: n // 2]
        tpart[2 * q + 1, :, :model] = value[n // 2 :]
        tpart[2 * q, :, model:] = sdel[: n // 2]
        tpart[2 * q + 1, :, model:] = sdel[n // 2 :]
        sums.step(0, q)

    @pl.when((i > begin_scan) & (i <= begin_norm))
    def _():
        sums.step(1, i - begin_scan - 1)

    @pl.when((i >= begin_scan + 5) & (i < begin_norm + 5))
    def _():
        sums.step(2, i - begin_scan - 5)

    @pl.when((i >= begin_scan + 6) & (i < begin_norm + 6))
    def _():
        sums.step(3, i - begin_scan - 6)

    if last:
        @pl.when((i > begin_scan) & (i <= begin_scan + slices))
        def _():
            outs.step(2, i - begin_scan - 1)

        @pl.when((i > begin_scan + 1) & (i <= begin_scan + slices + 1))
        def _():
            outs.step(3, i - begin_scan - 2)

    @pl.when(i == begin_norm - 1)
    def _():
        dhp_ref[2:3, :] = headsum(jnp.broadcast_to(dcp_ref[6:7, :], (8, dcp_ref.shape[1])), ind)[0:1, :]
        if last:
            job.product(held, turned, ilow)
            move(4).start()
        else:
            job.emit(2, turned, ilow, places - 1)
            for k in (4, 5, 6):
                move(k).start()

    if not last:
        @pl.when(i == begin_norm + 1)
        def _():
            for k in (4, 5, 6):
                move(k).wait()
            put_pack(
                buffers[0].at[1], square.me, *spots, next_dcp[...], next_dsp[...], next_dhp[...], next_dgain[...]
            )
            minis.sum.start(1)

    @pl.when(i >= begin_norm)
    def _():
        r = i - begin_norm
        chunk = steps - 1 - r
        if last:
            fac = column(frow[chunk])
            side = chunk // (steps // 2)
            base = (chunk - side * (steps // 2)) * n
        for h in range(2):
            rows = slice(h * (n // 2), (h + 1) * (n // 2))
            back = tpart[2 * r + h, :, :model].astype(F32)
            sdel = tpart[2 * r + h, :, model:]
            if last:
                sdsum_ref[rows, :] = sdel
            else:
                sd_all[pl.ds(pl.multiple_of(chunk * n + h * (n // 2), n // 2), n // 2), :] = sdel
            res = res_ref[rows, :].astype(F32)
            rn = rn_ref[rows, :]
            dgain_ref[...] += colsum(back * res * rn)
            gained = back * gain_ref[layer : layer + 1, :]
            mean = jnp.sum(gained * res, axis=1, keepdims=True) / model
            new_ref[rows, :] = up_ref[rows, :].astype(F32) + rn * gained - (rn * rn * rn * mean) * res
            if last:
                where = pl.ds(pl.multiple_of(base + h * (n // 2), n // 2), n // 2)
                for c in range(slices):
                    span = slice(c * SLICE, (c + 1) * SLICE)
                    summed = opart[2 * c + side, where, :].astype(F32)
                    mixed_ref[rows, span] = (res[:, span] + fac[rows, :] * summed).astype(BF16)

    @pl.when(i == end)
    def _():
        def finish(j):
            job.finish(j)
            pltpu.make_async_copy(dy.at[pl.ds(j * rows_own, rows_own), :], grad_hbm.at[j], gsem.at[j]).start()

        if not last:
            put_pack(
                buffers[0].at[0], square.me, turned, step_all, sd_all, dcp_ref[...], dsp_ref[...], dhp_ref[...], dgain_ref[...]
            )
            minis.sum.start(0)
            for m in range(places // 2):
                job.fold(2, m)
            finish(3)
        finish(0)
        finish(1)
        if not last:
            minis.fold()
            minis.turn()
            for k in range(1, line.n):
                minis.relay(k)
            job.lead(2, places - 1)
            for m in range(places // 2, places):
                job.fold(2, m)
            minis.cross()
            finish(2)
            minis.cross_on()
            minis.end()
            tails = [
                pltpu.make_async_copy(src, dst, load.at[k])
                for k, (src, dst) in enumerate(((minis.full, full_hbm), (minis.wide, wide_hbm)))
            ]
            for copy in tails:
                copy.start()
        for j in range(count):
            job.drain(j)
            pltpu.make_async_copy(dy.at[pl.ds(j * rows_own, rows_own), :], grad_hbm.at[j], gsem.at[j]).wait()
        if last:
            move(4).wait()
        else:
            for copy in tails:
                copy.wait()


def back(up, sq, gate_pre, ssd, inner_raw, small, states, res, rnorm, gain, params,
         wout, scaled, wt, normed, heads, size, layer, after=None):
    tokens_n, width = inner_raw.shape
    model = up.shape[1]
    last = after is None
    steps = tokens_n // CHUNK
    begin_scan = 2 * steps
    begin_norm = begin_scan + steps
    rows = model // size
    n = size // 2
    hbm = pl.BlockSpec(memory_space=pl.ANY)
    top = steps - 1

    def norm_at(i):
        return jnp.where(i < begin_norm, top, top - (i - begin_norm))

    def scan_at(i):
        return jnp.clip(top - (i - begin_scan), 0, top)

    def first(w):
        return pl.BlockSpec((CHUNK, w), lambda i: (jnp.where(i < steps, i, norm_at(i)), 0))

    def second(w):
        return pl.BlockSpec((CHUNK, w), lambda i: (jnp.clip(i - steps, 0, top), 0))

    def scan(w):
        return pl.BlockSpec((CHUNK, w), lambda i: (scan_at(i), 0))

    def prev(w):
        return pl.BlockSpec((8, w), lambda i: (jnp.maximum(scan_at(i) * (CHUNK // 8) - 1, 0), 0))

    def norm(w):
        return pl.BlockSpec((CHUNK, w), lambda i: (norm_at(i), 0))

    def whole(a):
        return pl.BlockSpec(a.shape, lambda i: (0,) * len(a.shape))

    extra = model + 2 * STATE
    quarter = pltpu.VMEM((steps, CHUNK // 2, extra), BF16)
    count = 2 if last else 4
    pieces = pltpu.VMEM((count, n, rows, width), BF16)
    args = [up, sq, gate_pre, ssd, inner_raw, inner_raw, small, small, states, res, rnorm, gain, *params,
            wout, scaled, wt, normed]
    in_specs = [
        first(model), whole(sq), second(width), second(width),
        scan(width), prev(width), scan(small.shape[1]), prev(small.shape[1]),
        pl.BlockSpec((1, STATE, width), lambda i: (scan_at(i), 0, 0)),
        norm(model), norm(1), whole(gain),
    ] + [whole(a) for a in params] + [hbm] * 4
    out_specs = [norm(model), hbm]
    out_shape = [jax.ShapeDtypeStruct((tokens_n, model), F32), jax.ShapeDtypeStruct((count, rows, width), F32)]
    totals = [(8, width), (8, 2 * STATE), (8, LANES), (1, model)]
    scratch = [
        pltpu.VMEM((CHUNK + 8, width), F32),
        pltpu.VMEM((CHUNK + 8, 2 * STATE), F32),
        pltpu.VMEM((CHUNK + 8, width), F32),
        pltpu.VMEM((CHUNK + 8, 2 * STATE), F32),
        pltpu.VMEM((STATE, width), F32),
        pltpu.VMEM((LANES, CHUNK), F32),
        pltpu.VMEM((8, width), F32),
        pltpu.VMEM((8, 2 * STATE), F32),
        pltpu.VMEM((8, LANES), F32),
        pltpu.VMEM((LANES, width), BF16),
        pltpu.VMEM(wout.shape, BF16),
        pltpu.VMEM(scaled.shape, BF16),
        pltpu.VMEM(wt.shape, BF16),
        pltpu.VMEM(normed.shape, BF16),
        pltpu.VMEM((tokens_n, width), F32),
        pltpu.VMEM((tokens_n, width), BF16),
        pltpu.VMEM((tokens_n, width), BF16),
        pltpu.VMEM((steps, 1, CHUNK), F32),
        pltpu.VMEM((steps, 1, CHUNK), F32),
        pltpu.VMEM((4, steps, 1, CHUNK), F32),
        pltpu.VMEM((count, size, rows, width), BF16), pieces, pieces,
        pltpu.VMEM((2 * steps, CHUNK // 2, extra), BF16), quarter, quarter, quarter,
        pltpu.SemaphoreType.DMA((8,)),
        pltpu.SemaphoreType.DMA((3,)),
        pltpu.SemaphoreType.DMA((3,)),
        pltpu.SemaphoreType.DMA((3, count, n)),
        pltpu.SemaphoreType.DMA((3, count, n)),
        pltpu.SemaphoreType.DMA((3, steps)),
        pltpu.SemaphoreType.DMA((3, steps)),
        pltpu.SemaphoreType.DMA((count,)),
    ]
    if last:
        out_specs += [hbm, norm(2 * STATE), scan(LANES)]
        out_specs += [pl.BlockSpec(v, lambda i: (0, 0)) for v in totals] + [norm(model)]
        out_shape += [
            jax.ShapeDtypeStruct((size, rows, width), BF16),
            jax.ShapeDtypeStruct((tokens_n, 2 * STATE), BF16),
            jax.ShapeDtypeStruct((tokens_n, LANES), BF16),
        ]
        out_shape += [jax.ShapeDtypeStruct(v, F32) for v in totals]
        out_shape.append(jax.ShapeDtypeStruct((tokens_n, model), BF16))
        slices = model // SLICE
        chunk = pltpu.VMEM((slices, tokens_n // 2, SLICE), BF16)
        scratch += [
            pltpu.VMEM((size, rows, width), BF16),
            pltpu.VMEM((4, steps, 1, CHUNK), F32),
            pltpu.VMEM((2 * slices, tokens_n // 2, SLICE), BF16), chunk, chunk, chunk,
            pltpu.SemaphoreType.DMA((3,)),
            pltpu.SemaphoreType.DMA((3,)),
            pltpu.SemaphoreType.DMA((3, slices)),
            pltpu.SemaphoreType.DMA((3, slices)),
        ]
    else:
        w = 2 * STATE
        r = pack_rows(size)
        args += list(after)
        in_specs += [hbm] * 4 + [whole(v) for v in after[4:]]
        out_specs += [hbm, hbm]
        out_shape += [
            jax.ShapeDtypeStruct((2, size, r, w), BF16),
            jax.ShapeDtypeStruct((4, 2, SPAN, w), BF16),
        ]
        scratch += [pltpu.VMEM(v, F32) for v in totals]
        scratch += smalls_scratch(size, w, 2)
    return pl.pallas_call(
        functools.partial(
            back_body, heads=heads, per=LEN // CHUNK, size=size, steps=steps, layer=layer, last=last
        ),
        grid=(begin_norm + steps,),
        in_specs=in_specs,
        out_specs=out_specs,
        out_shape=out_shape,
        scratch_shapes=scratch,
        compiler_params=pltpu.CompilerParams(
            collective_id=2 if last else 3, has_side_effects=True, vmem_limit_bytes=VMEM_LIMIT
        ),
        name="back",
    )(*args)


def results_body(full_ref, wide_ref, first_hbm, second_hbm, mixed_hbm, up_hbm, *refs, layers, heads):
    pair_out, out_out, mixed_out, up_out = refs[11:15]
    first, second, mixed, up, load, store = refs[15:]
    refs = refs[:11]
    loads = [
        pltpu.make_async_copy(src, dst, load.at[k])
        for k, (src, dst) in enumerate(((up_hbm, up), (mixed_hbm, mixed), (first_hbm, first), (second_hbm, second)))
    ]
    for copy in loads:
        copy.start()
    moves = [
        (up, up_out), (mixed, mixed_out), (first.at[pl.ds(1, 2)], pair_out.at[0]), (second.at[1], pair_out.at[1, 0]),
        (first.at[3], pair_out.at[1, 1]), (first.at[0], out_out.at[0]), (second.at[0], out_out.at[1]),
    ]
    stores = [pltpu.make_async_copy(src, dst, store.at[k]) for k, (src, dst) in enumerate(moves)]
    for k, copy in enumerate(stores):
        if k < 3:
            loads[k].wait()
        if k == 3:
            loads[3].wait()
        copy.start()
    step_ref, state_ref, conv_ref, bias_ref, convs_ref, biass_ref = refs[:6]
    stepbias_ref, decay_ref, skip_ref, norm_ref, gain_ref = refs[6:]
    model = state_ref.shape[1]
    quarter = model // 4
    w = state_ref.shape[2]
    width = conv_ref.shape[2]
    for layer in range(layers):
        for t in range(4):
            state_ref[layer, t * quarter : (t + 1) * quarter, :] = wide_ref[t, layer, :quarter, :].astype(F32)
        taps = [wide_ref[t, layer, quarter : quarter + 16, :].astype(F32) for t in range(4)]
        taps = (taps[0] + taps[1]) + (taps[2] + taps[3])
        convs_ref[layer] = taps[0:4]
        biass_ref[layer : layer + 1, :] = taps[4:5]
        flat = full_ref[layer].reshape(-1, w)[:PACK].astype(F32)
        at = quarter + 16
        for b in range(model // w):
            step_ref[layer, :, b * w : (b + 1) * w] = flat[at : at + 16]
            at += 16
        for b in range(width // w):
            lanes = slice(b * w, (b + 1) * w)
            rows = flat[at + 8 * b : at + 8 * b + 8]
            conv_ref[layer, :, lanes] = rows[0:4]
            bias_ref[layer : layer + 1, lanes] = rows[4:5]
            norm_ref[layer : layer + 1, lanes] = rows[5:6]
        at += 8 * (width // w)
        for k, ref in enumerate((stepbias_ref, decay_ref, skip_ref)):
            ref[layer : layer + 1, :] = flat[at + k : at + k + 1, :heads]
        at += 8
        for b in range(model // w):
            gain_ref[layer : layer + 1, b * w : (b + 1) * w] = flat[at + b : at + b + 1]
    for copy in stores:
        copy.wait()


def write_results(full, wide, first, second, mixed, up, heads):
    layers, w = full.shape[0], full.shape[3]
    _, rows, width = first.shape
    model = up.shape[1]
    vm = pl.BlockSpec(memory_space=pltpu.VMEM)
    hbm = pl.BlockSpec(memory_space=pl.ANY)
    shapes = [
        (layers, 16, model), (layers, model, w), (layers, 4, width), (layers, width), (layers, 4, w), (layers, w),
        (layers, heads), (layers, heads), (layers, heads), (layers, width), (layers, model),
    ]
    return pl.pallas_call(
        functools.partial(results_body, layers=layers, heads=heads),
        in_specs=[vm, vm] + [hbm] * 4,
        out_specs=[vm] * len(shapes) + [hbm] * 4,
        out_shape=[jax.ShapeDtypeStruct(v, F32) for v in shapes] + [
            jax.ShapeDtypeStruct((layers, 2, rows, width), F32),
            jax.ShapeDtypeStruct((layers, rows, width), F32),
            jax.ShapeDtypeStruct(mixed.shape, mixed.dtype),
            jax.ShapeDtypeStruct(up.shape, up.dtype),
        ],
        scratch_shapes=[
            pltpu.VMEM(first.shape, F32),
            pltpu.VMEM(second.shape, F32),
            pltpu.VMEM(mixed.shape, mixed.dtype),
            pltpu.VMEM(up.shape, up.dtype),
            pltpu.SemaphoreType.DMA((4,)),
            pltpu.SemaphoreType.DMA((7,)),
        ],
        compiler_params=pltpu.CompilerParams(vmem_limit_bytes=VMEM_LIMIT),
        name="results",
    )(full, wide, first, second, mixed, up)


def shards(
    tokens, inproj, stepproj, stateproj, outproj, convinner, biasinner, convstate, biasstate,
    stepbias, decaylog, skipgain, normgain, inputgain, cotangent,
):
    layers = inproj.shape[0]
    width = inproj.shape[3]
    heads = stepproj.shape[2]
    model = tokens.shape[1]
    pad = LANES - heads
    size = lax.axis_size("dp")
    steps_w = jnp.pad(jnp.swapaxes(stepproj, 1, 2), ((0, 0), (0, pad), (0, 0)))
    head = jnp.pad(jnp.stack([stepbias, decaylog, skipgain], axis=1), ((0, 0), (0, 5), (0, pad)))
    outt = jnp.swapaxes(outproj, 1, 2)
    params = (convinner, biasinner, normgain, convstate, biasstate, head)

    residual = tokens
    kept = []
    out = None
    for at in range(layers):
        results = forward(residual, stateproj, steps_w, inproj, outt, inputgain, params, heads, size, at, out=out)
        if at:
            residual, kept[-1][-1] = results[:2]
            results = results[2:]
        normed, rnorm, small, inner_raw, gate_pre, wt, w_out, ssd, scaled, sq, states = results
        w_out = w_out.reshape(model, width)
        kept.append([residual, normed, rnorm, small, inner_raw, gate_pre, wt, w_out, ssd, scaled, states, sq])
        out = (scaled, w_out, sq)

    assert layers == 2
    before, normed, rnorm, small, inner_raw, gate_pre, wt, w_out, ssd, scaled, states, sq = kept[1]
    upstream, second, held, sdel, steplow, *totals, mixed = back(
        cotangent, sq, gate_pre, ssd, inner_raw, small, states, before, rnorm, inputgain, params,
        w_out, scaled, wt, normed, heads, size, 1,
    )
    after = (normed, steplow, sdel, held, *totals)
    before, normed, rnorm, small, inner_raw, gate_pre, wt, w_out, ssd, scaled, states, sq = kept[0]
    upstream, first, full, wide = back(
        upstream, sq, gate_pre, ssd, inner_raw, small, states, before, rnorm, inputgain, params,
        w_out, scaled, wt, normed, heads, size, 0, after=after,
    )
    (
        step_grad, state_grad, conv_grad, bias_grad, convs_grad, biass_grad,
        stepbias_grad, decay_grad, skip_grad, norm_grad, gain_grad, pair_grad, out_grad, mixed, upstream,
    ) = write_results(full, wide, first, second, mixed, upstream, heads)
    return (
        mixed,
        upstream,
        pair_grad,
        jnp.swapaxes(step_grad[:, :heads], 1, 2),
        state_grad,
        jnp.swapaxes(out_grad, 1, 2),
        conv_grad,
        bias_grad,
        convs_grad,
        biass_grad,
        stepbias_grad,
        decay_grad,
        skip_grad,
        norm_grad,
        gain_grad,
    )


def solution(mesh):
    in_specs = (
        P("dp", None),
        P(None, None, "dp", "tensor"),
        P(None, None, "tensor"),
        P(),
        P(None, "tensor", "dp"),
        P(None, None, "tensor"),
        P(None, "tensor"),
        P(),
        P(),
        P(None, "tensor"),
        P(None, "tensor"),
        P(None, "tensor"),
        P(None, "tensor"),
        P(),
        P("dp", None),
    )
    out_specs = (
        P("dp", None),
        P("dp", None),
        P(None, None, "dp", "tensor"),
        P(None, None, "tensor"),
        P(),
        P(None, "tensor", "dp"),
        P(None, None, "tensor"),
        P(None, "tensor"),
        P(),
        P(),
        P(None, "tensor"),
        P(None, "tensor"),
        P(None, "tensor"),
        P(None, "tensor"),
        P(),
    )
    return jax.shard_map(shards, mesh=mesh, in_specs=in_specs, out_specs=out_specs, check_vma=False)
```

```python
import functools
import math

import jax
import jax.numpy as jnp
from jax import lax
from jax.experimental import pallas as pl
from jax.experimental.pallas import tpu as pltpu
from jax.sharding import PartitionSpec as P

STATE = 128
LEN = 1024
INNER = 3072
HEAD = 64
CHUNK = 128
SLICE = 256
TILE = 256
PACK = 544
SPAN = 400
VMEM_LIMIT = 65000 * 1024
LANES = 128
EPS = 1e-05
LOG2E = 1.4426950408889634

HIGH = lax.Precision.HIGHEST
NN = (((1,), (0,)), ((), ()))
NT = (((1,), (1,)), ((), ()))
TN = (((0,), (0,)), ((), ()))
F32 = jnp.float32
BF16 = jnp.bfloat16
MESH = pl.DeviceIdType.MESH


def remote(src, dst, send, recv, where):
    return pltpu.make_async_remote_copy(
        src_ref=src, dst_ref=dst, send_sem=send, recv_sem=recv, device_id=where, device_id_type=MESH
    )


class Line:
    def __init__(self, size):
        self.n = size // 2
        me = lax.axis_index("dp")
        self.me = me
        self.at = me // 2
        self.side = lax.rem(me, 2)
        self.pair = {"dp": me + 1 - 2 * self.side}
        self.right = {"dp": jnp.minimum(me + 2, size - 1)}
        self.left = {"dp": jnp.maximum(me - 2, 0)}
        odd = lax.rem(self.at, 2)
        self.odd = odd == 1
        self.near = {"dp": me + 2 - 4 * odd}
        self.has_left = self.at > 0
        self.has_right = self.at < self.n - 1

    def greet(self, barrier, more=()):
        for who in more:
            pl.semaphore_signal(barrier, inc=1, device_id=who, device_id_type=MESH)
        pl.semaphore_signal(barrier, inc=1, device_id=self.pair, device_id_type=MESH)

        @pl.when(self.has_left)
        def _():
            pl.semaphore_signal(barrier, inc=1, device_id=self.left, device_id_type=MESH)

        @pl.when(self.has_right)
        def _():
            pl.semaphore_signal(barrier, inc=1, device_id=self.right, device_id_type=MESH)

        peers = 1 + len(more) + self.has_left.astype(jnp.int32) + self.has_right.astype(jnp.int32)
        pl.semaphore_wait(barrier, peers)

    def greet_all(self, barrier, more=()):
        for who in list(more) + [self.pair]:
            pl.semaphore_signal(barrier, inc=1, device_id=who, device_id_type=MESH)
        for i in range(self.n):
            @pl.when(i != self.at)
            def _(i=i):
                pl.semaphore_signal(barrier, inc=1, device_id={"dp": 2 * i + self.side}, device_id_type=MESH)
        pl.semaphore_wait(barrier, self.n + len(more))


def upper(rows):
    return max(16, rows // 32 * 16)


class Gather:
    def __init__(self, line, own, full, keep, send, recv):
        self.line, self.own, self.full, self.keep, self.send, self.recv = line, own, full, keep, send, recv
        self.rows = full.shape[2]
        self.cut = upper(self.rows)

    def copy(self, j, slab, way, src=None, rest=False):
        where = (self.line.right, self.line.left, self.line.pair)[way]
        dst = self.full.at[j, slab]
        if rest:
            dst = self.full.at[j, slab, pl.ds(self.cut, self.rows - self.cut)]
        return remote(dst if src is None else src, dst, self.send.at[j, way, slab], self.recv.at[j, slab], where)

    def shared(self, j, slab, owner):
        part = self.full.at[j, slab, pl.ds(0, self.cut)]
        return remote(part, part, self.send.at[j, 0, slab], self.recv.at[j, owner], self.line.near)

    def start(self, j):
        line = self.line
        pltpu.make_async_copy(self.own(j), self.full.at[j, line.me], self.keep.at[j]).start()

        @pl.when(line.has_right)
        def _():
            self.copy(j, line.me, 0, self.own(j)).start()

        @pl.when(line.has_left)
        def _():
            self.copy(j, line.me, 1, self.own(j)).start()

        self.copy(j, line.me, 2, self.own(j)).start()

    def relay(self, j, k):
        line = self.line

        def forward(slab, way, go_on, near):
            self.copy(j, slab, way).wait_recv()

            @pl.when(go_on)
            def _():
                self.copy(j, slab, way).start()

            if k > 1:
                self.copy(j, slab, 2).start()
            else:
                @pl.when(near)
                def _():
                    self.copy(j, slab, 2, rest=True).start()

                @pl.when(jnp.logical_not(near))
                def _():
                    self.copy(j, slab, 2).start()

        @pl.when(line.at >= k)
        def _():
            forward(line.me - 2 * k, 0, line.has_right, line.odd)

        @pl.when(line.at + k < line.n)
        def _():
            forward(line.me + 2 * k, 1, line.has_left, jnp.logical_not(line.odd))

        if k == 1:
            slab = line.me + 1 - 2 * line.side
            self.copy(j, slab, 2).wait_recv()
            self.shared(j, slab, line.near["dp"]).start()

    def near_slab(self):
        line = self.line
        return line.near["dp"] + 1 - 2 * line.side

    def arrive(self, j):
        line = self.line
        pltpu.make_async_copy(self.own(j), self.full.at[j, line.me], self.keep.at[j]).wait()
        self.copy(j, self.near_slab(), 2, rest=True).wait_recv()
        self.shared(j, self.near_slab(), line.me).wait_recv()
        for place in range(line.n):
            slab = 2 * place + 1 - line.side

            @pl.when((slab != self.near_slab()) & (place != line.at))
            def _(slab=slab):
                self.copy(j, slab, 2).wait_recv()

    def drain(self, j):
        line = self.line
        self.shared(j, line.me + 1 - 2 * line.side, line.near["dp"]).wait_send()
        for place in range(line.n):
            slab = 2 * place + line.side
            near = slab == line.near["dp"]

            @pl.when(near)
            def _(slab=slab):
                self.copy(j, slab, 2, rest=True).wait_send()

            @pl.when(jnp.logical_not(near))
            def _(slab=slab):
                self.copy(j, slab, 2).wait_send()

            @pl.when(line.has_right & (place <= line.at))
            def _(slab=slab):
                self.copy(j, slab, 0).wait_send()

            @pl.when(line.has_left & (place >= line.at))
            def _(slab=slab):
                self.copy(j, slab, 1).wait_send()


class Square:
    def __init__(self):
        me = lax.axis_index("tensor")
        self.me = me
        self.half = lax.rem(me, 2)
        self.mate = {"tensor": me + 1 - 2 * self.half}
        self.across = {"tensor": lax.rem(me + 2, 4)}

    def others(self):
        return [{"tensor": lax.rem(self.me + k, 4)} for k in (1, 2, 3)]


class Total:
    def __init__(self, square, part, got, far, other, send, recv):
        self.square, self.part, self.got, self.far, self.other = square, part, got, far, other
        self.send, self.recv = send, recv

    def first(self, c):
        sq = self.square
        return remote(
            self.part.at[2 * c + 1 - sq.half], self.got.at[c], self.send.at[0, c], self.recv.at[0, c], sq.mate
        )

    def second(self, c):
        sq = self.square
        return remote(self.part.at[2 * c + sq.half], self.far.at[c], self.send.at[1, c], self.recv.at[1, c], sq.across)

    def third(self, c):
        sq = self.square
        return remote(self.part.at[2 * c + sq.half], self.other.at[c], self.send.at[2, c], self.recv.at[2, c], sq.mate)

    def step(self, kind, c):
        slot = 2 * c + self.square.half
        if kind == 0:
            self.first(c).start()
        elif kind == 1:
            self.first(c).wait_recv()
            self.part[slot] = (self.part[slot].astype(F32) + self.got[c].astype(F32)).astype(BF16)
            self.second(c).start()
        elif kind == 2:
            self.second(c).wait()
            self.part[slot] = (self.part[slot].astype(F32) + self.far[c].astype(F32)).astype(BF16)
            self.third(c).start()
        else:
            self.third(c).wait_recv()
            self.first(c).wait_send()
            self.third(c).wait_send()
            self.part[2 * c + 1 - self.square.half] = self.other[c]


class Scatter:
    def __init__(self, line, part, out, near, far, send, recv):
        self.line, self.part, self.out, self.near, self.far = line, part, out, near, far
        self.send, self.recv = send, recv

    def order(self):
        n = self.line.n
        seq = []
        for i in range((n + 1) // 2):
            seq.append(i)
            if n - 1 - i != i:
                seq.append(n - 1 - i)
        return seq

    def cross(self, j, i):
        line = self.line
        return remote(
            self.part.at[j, 2 * i + 1 - line.side], self.near.at[j, i], self.send.at[0, j, i], self.recv.at[0, j, i], line.pair
        )

    def straight(self, j, i, source):
        line = self.line
        return remote(
            self.part.at[j, 2 * i + line.side], self.far.at[j, source], self.send.at[1, j, i], self.recv.at[1, j, source],
            {"dp": 2 * i + line.side},
        )

    def lead(self, j, m):
        self.cross(j, self.order()[m]).start()

    def start(self, j):
        for m in range(self.line.n):
            self.lead(j, m)

    def emit(self, j, turned, right, now=None):
        rows = self.part.shape[2]
        for m, i in enumerate(self.order()):
            value = mm(turned[2 * i * rows : 2 * (i + 1) * rows, :], right[...]).astype(BF16)
            self.part[j, 2 * i] = value[:rows]
            self.part[j, 2 * i + 1] = value[rows:]
            if now is None or m < now:
                self.lead(j, m)

    def product(self, dst, turned, right):
        rows = dst.shape[1]
        for i in range(self.line.n):
            value = mm(turned[2 * i * rows : 2 * (i + 1) * rows, :], right[...]).astype(BF16)
            dst[2 * i] = value[:rows]
            dst[2 * i + 1] = value[rows:]

    def fold(self, j, m):
        line = self.line
        i = self.order()[m]
        self.cross(j, i).wait_recv()
        slot = 2 * i + line.side
        self.part[j, slot] = (self.part[j, slot].astype(F32) + self.near[j, i].astype(F32)).astype(BF16)

        @pl.when(i != line.at)
        def _():
            self.straight(j, i, line.at).start()

    def finish(self, j):
        line = self.line
        out = self.out(j)
        out[...] = self.part[j, line.me].astype(out.dtype)
        for i in range(line.n):
            @pl.when(i != line.at)
            def _(i=i):
                self.straight(j, i, i).wait_recv()
                out[...] += self.far[j, i].astype(out.dtype)

    def drain(self, j):
        for i in range(self.line.n):
            self.cross(j, i).wait_send()

            @pl.when(i != self.line.at)
            def _(i=i):
                self.straight(j, i, self.line.at).wait_send()


def mm(left, right, dims=NN, precision=None):
    return lax.dot_general(left, right, dims, precision=precision, preferred_element_type=F32)


def sigmoid(v):
    return 0.5 * jnp.tanh(0.5 * v) + 0.5


def softplus(v):
    return jnp.maximum(v, 0.0) + jnp.log1p(jnp.exp(-jnp.abs(v)))


def split16(v):
    top = v.astype(BF16)
    return top, (v - top.astype(F32)).astype(BF16)


def expand(v, ind):
    top, rest = split16(v)
    return mm(top, ind) + mm(rest, ind)


def headsum(v, ind):
    return mm(v.astype(BF16), ind, NT)


def rowsum(v):
    return mm(jnp.ones((8, v.shape[1]), BF16), v.astype(BF16), NT)[0:1, :]


def iotas(n):
    return (
        lax.broadcasted_iota(jnp.int32, (n, n), 0),
        lax.broadcasted_iota(jnp.int32, (n, n), 1),
    )


def colsum(v):
    return jnp.sum(v, axis=0, keepdims=True)


def conv_pre(ext, par, n):
    total = par[4:5, :] + par[0:1, :] * ext[5 : 5 + n, :]
    for tap in range(1, 4):
        total = total + par[tap : tap + 1, :] * ext[5 + tap : 5 + tap + n, :]
    return total


def scan_prep(small, hp, ind, n):
    rows, cols = iotas(n)
    raw = small[:, 2 * STATE :] + hp[0:1, :]
    step = softplus(raw)
    rate = -jnp.exp(hp[1:2, :])
    lower = jnp.where(rows >= cols, 1.0, 0.0).astype(F32)
    cs = mm(lower, step * rate, precision=HIGH)
    tail = jnp.exp(cs[n - 1 : n, :] - cs)
    wide = mm(jnp.concatenate([step, jnp.exp(cs), tail], axis=0).astype(BF16), ind)
    return raw, step, rate, cs, wide[0:n], wide[n : 2 * n], wide[2 * n : 3 * n]


def block_of(slabs, at, rows):
    step = math.gcd(LANES, rows)
    pieces = []
    for k in range(LANES // step):
        row = at * LANES + k * step
        slab = row // rows
        pieces.append(slabs[slab, pl.ds(pl.multiple_of(row - slab * rows, step), step), :])
    return pieces[0] if len(pieces) == 1 else jnp.concatenate(pieces, axis=0)


def put_params(cp, sp, hp, ind, layer, params):
    conv, bias, norm, convs, biass, head = params
    width = cp.shape[1]
    row = lax.broadcasted_iota(jnp.int32, (LANES, width), 0)
    lane = lax.broadcasted_iota(jnp.int32, (LANES, width), 1)
    ind[...] = jnp.where(lane // HEAD == row, 1.0, 0.0).astype(BF16)
    hp[...] = head[layer]
    cp[0:4, :] = conv[layer]
    cp[4:5, :] = bias[layer : layer + 1, :]
    cp[5:6, :] = norm[layer : layer + 1, :]
    cp[6:8, :] = expand(hp[...], ind[...])[2:4, :]
    sp[0:4, :] = convs[layer]
    sp[4:5, :] = biass[layer : layer + 1, :]


def place_rows(dst, at, value):
    r = dst.shape[1]
    for g in range(0, value.shape[0], 16):
        dst[(at + g) // r, (at + g) % r : (at + g) % r + 16, :] = value[g : g + 16].astype(dst.dtype)


def pack_rows(size):
    return -(-PACK // (16 * size)) * 16


def put_pack(dst, me, turned, steps_low, sdel, dcp, dsp, dhp, dgain):
    model = turned.shape[0]
    quarter = model // 4
    w = sdel.shape[1]

    def empty(n):
        return jnp.zeros((n, w), F32)

    place_rows(dst, 0, mm(turned[pl.ds(pl.multiple_of(me * quarter, quarter), quarter), :], sdel[...]))
    place_rows(dst, quarter, jnp.concatenate([dsp, empty(8)], axis=0))
    grown = mm(turned[...], steps_low[...]).T[:16]
    at = quarter + 16
    for b in range(model // w):
        place_rows(dst, at, grown[:, b * w : (b + 1) * w])
        at += 16
    place_rows(dst, at, jnp.concatenate([dcp[:, :w], dcp[:, w : 2 * w]], axis=0))
    place_rows(dst, at + 16, jnp.concatenate([dcp[:, 2 * w :], jnp.concatenate([dhp, dhp], axis=1)], axis=0))
    rows = [dgain[:, b * w : (b + 1) * w] for b in range(model // w)]
    place_rows(dst, at + 32, jnp.concatenate(rows + [empty(16 - len(rows))], axis=0))
    assert at + 48 == PACK


class Smalls:
    def __init__(self, line, square, pack, near, away, own, full, wide, sems):
        send, recv, keep, gsend, grecv, self.xsend, self.xrecv = sems
        self.square, self.full, self.wide = square, full, wide
        self.layers = range(pack.shape[0])
        self.sum = Scatter(line, pack, lambda j: own.at[j], near, away, send, recv)
        self.spread = Gather(line, lambda j: own.at[j], full, keep, gsend, grecv)

    def swap(self, k):
        sq = self.square
        slot = (sq.me, sq.me, lax.rem(sq.me + 2, 4))[k]
        who = (sq.across, sq.mate, sq.mate)[k]
        return remote(self.wide.at[slot], self.wide.at[slot], self.xsend.at[k], self.xrecv.at[k], who)

    def start(self):
        for j in self.layers:
            self.sum.start(j)

    def fold(self):
        for j in self.layers:
            for m in range(self.sum.line.n):
                self.sum.fold(j, m)

    def turn(self):
        for j in self.layers:
            self.sum.finish(j)
            self.spread.start(j)

    def relay(self, k):
        for j in self.layers:
            self.spread.relay(j, k)

    def cross(self):
        for j in self.layers:
            self.spread.arrive(j)
            flat = self.full[j].reshape(-1, self.full.shape[3])
            self.wide[self.square.me, j] = flat[: self.wide.shape[2]]
        self.swap(0).start()
        self.swap(1).start()

    def cross_on(self):
        self.swap(0).wait_recv()
        self.swap(2).start()

    def end(self):
        self.swap(1).wait_recv()
        self.swap(2).wait_recv()
        for k in range(3):
            self.swap(k).wait_send()
        for j in self.layers:
            self.sum.drain(j)
            self.spread.drain(j)


def smalls_scratch(size, w, layers):
    r, n = pack_rows(size), size // 2
    buffers = [
        pltpu.VMEM((layers, size, r, w), BF16),
        pltpu.VMEM((layers, n, r, w), BF16),
        pltpu.VMEM((layers, n, r, w), BF16),
        pltpu.VMEM((layers, r, w), BF16),
        pltpu.VMEM((layers, size, r, w), BF16),
        pltpu.VMEM((4, layers, SPAN, w), BF16),
    ]
    sems = [
        pltpu.SemaphoreType.DMA((2, layers, n)),
        pltpu.SemaphoreType.DMA((2, layers, n)),
        pltpu.SemaphoreType.DMA((layers,)),
        pltpu.SemaphoreType.DMA((layers, 3, size)),
        pltpu.SemaphoreType.DMA((layers, size)),
        pltpu.SemaphoreType.DMA((3,)),
        pltpu.SemaphoreType.DMA((3,)),
    ]
    return buffers + sems


def forward_body(*refs, size, heads, per, steps, layer):
    refs = list(refs)

    def take(n):
        got = refs[:n]
        del refs[:n]
        return got

    mid = layer > 0
    (res_hbm,) = take(1)
    if mid:
        scaled_hbm, wout_hbm, sq_ref = take(3)
    state_hbm, step_hbm, in_hbm, out_hbm, gain_ref = take(5)
    params = take(6)
    if mid:
        new_hbm, sums_ref = take(2)
    normed_hbm, rnorm_ref, small_hbm, inner_hbm, gate_hbm, wt_hbm, full_hbm, ssd_ref, scaled_ref, sqs_ref, st_ref = take(11)
    if mid:
        scaled_in, wout, part, got, far, other, rows_got, facs, fresh, sends, recvs, rsend, rrecv = take(13)
    res, wstate, wt, slabs, normed, turned, small, inner, gate, ext, exts, state = take(12)
    cp_ref, sp_ref, hp_ref, ind_ref, keep, gsend, grecv, load, sems = take(9)
    assert not refs

    n = CHUNK
    tokens_n, model = res.shape
    width = inner.shape[1]
    top = 2 * width + 2 * STATE
    i = pl.program_id(0)
    line = Line(size)
    square = Square()
    job = Gather(line, lambda j: out_hbm.at[layer] if j == 2 else in_hbm.at[layer, 1 - j], slabs, keep, gsend, grecv)
    outgoing = [(turned, normed_hbm), (small, small_hbm), (inner, inner_hbm), (gate, gate_hbm)]
    outgoing += [(wt, wt_hbm), (slabs.at[2], full_hbm)]
    if mid:
        outgoing.append((fresh, new_hbm))

    def flush(k):
        return pltpu.make_async_copy(*outgoing[k], sems.at[k])


    @pl.when(i == 0)
    def _():
        pairs = [(res_hbm, res), (state_hbm.at[layer], wstate), (step_hbm.at[layer], wt.at[pl.ds(top, LANES), :])]
        if mid:
            pairs = [(scaled_hbm, scaled_in), (wout_hbm, wout)] + pairs
        loads = [pltpu.make_async_copy(src, dst, load.at[k]) for k, (src, dst) in enumerate(pairs)]
        for copy in loads:
            copy.start()
        line.greet(pltpu.get_barrier_semaphore(), square.others() if mid else ())
        job.start(0)
        put_params(cp_ref, sp_ref, hp_ref, ind_ref, layer, params)
        ticks = [functools.partial(job.relay, 0, k) for k in range(1, line.n)]
        ticks.append(functools.partial(job.start, 1))
        span = model // LANES

        def project(j, dst):
            weight = slabs[j].reshape(model, width)

            def tile(t, _):
                rows = pl.ds(pl.multiple_of(t * TILE, TILE), TILE)
                dst[rows, :] = mm(normed[rows, :], weight)
                return 0

            lax.fori_loop(0, tokens_n // TILE, tile, 0)

        def turn_inner(b, _):
            wt[:width, pl.ds(pl.multiple_of(b * LANES, LANES), LANES)] = block_of(slabs.at[0], b, slabs.shape[2]).T
            return 0

        def settle():
            job.arrive(0)
            if not mid:
                project(0, inner)
                flush(2).start()
            lax.fori_loop(0, span, turn_inner, 0)

        ticks.append(functools.partial(job.relay, 1, 1))
        ticks.append(settle)
        ticks += [functools.partial(job.relay, 1, k) for k in range(2, line.n)]
        ticks.append(functools.partial(job.start, 2))

        if mid:
            chunks = model // SLICE
            half = tokens_n // 2
            sums = Total(square, part, got, far, other, sends, recvs)
            copies = [
                remote(sq_ref, rows_got.at[square.me], rsend.at[k], rrecv.at[k], who)
                for k, who in enumerate(square.others())
            ]
            for copy in copies:
                copy.start()
            loads[0].wait()
            loads[1].wait()
            for c in range(chunks):
                value = mm(scaled_in[...], wout[c * SLICE : (c + 1) * SLICE, :], NT).astype(BF16)
                part[2 * c] = value[:half]
                part[2 * c + 1] = value[half:]
                sums.step(0, c)
                if c:
                    sums.step(1, c - 1)
            sums.step(1, chunks - 1)
            rows_got[square.me] = sq_ref[...]
            for copy in copies:
                copy.wait()
            total = (rows_got[0] + rows_got[1]) + (rows_got[2] + rows_got[3])
            sums_ref[...] = total
            factor = lax.rsqrt(total / INNER + EPS)
            for t in range(tokens_n // LANES):
                facs[t * LANES : (t + 1) * LANES, :] = jnp.broadcast_to(factor[t], (LANES, LANES)).T
            loads[2].wait()

            def use(c):
                for h in range(2):
                    where = slice(h * half, (h + 1) * half)
                    for s in range(SLICE // LANES):
                        lanes = slice(c * SLICE + s * LANES, c * SLICE + (s + 1) * LANES)
                        value = part[2 * c + h, :, s * LANES : (s + 1) * LANES].astype(F32)
                        fresh[where, lanes] = res[where, lanes].astype(F32) + facs[where, :] * value

            spread = max(1, -(-len(ticks) // chunks))
            for c in range(chunks):
                for tick in ticks[:spread]:
                    tick()
                ticks = ticks[spread:]
                sums.step(2, c)
                if c:
                    sums.step(3, c - 1)
                    use(c - 1)
            sums.step(3, chunks - 1)
            use(chunks - 1)
            flush(6).start()
        else:
            loads[0].wait()
        loads[-2].wait()
        loads[-1].wait()
        for b in range(2 * STATE // LANES):
            rows = slice(2 * width + b * LANES, 2 * width + (b + 1) * LANES)
            wt[rows, :] = wstate[:, b * LANES : (b + 1) * LANES].T

        def norm(t, _):
            rows = pl.ds(pl.multiple_of(t * TILE, TILE), TILE)
            value = (fresh if mid else res)[rows, :].astype(F32)
            scale = lax.rsqrt(jnp.sum(value * value, axis=1, keepdims=True) / model + EPS)
            low = (value * scale * gain_ref[layer : layer + 1, :]).astype(BF16)
            rnorm_ref[rows, :] = scale
            normed[rows, :] = low
            turned[:, rows] = low.T
            small[rows, : 2 * STATE] = mm(low, wstate[...])
            small[rows, 2 * STATE :] = mm(low, wt[top:, :], NT)
            return 0

        lax.fori_loop(0, tokens_n // TILE, norm, 0)
        flush(0).start()
        flush(1).start()
        for tick in ticks:
            tick()

        if mid:
            project(0, inner)
            flush(2).start()
        job.arrive(1)
        project(1, gate)
        flush(3).start()

    for k in range(1, line.n):
        @pl.when(i == 1 + k * steps // (line.n + 1))
        def _(k=k):
            job.relay(2, k)

    @pl.when(i > 0)
    def _():
        at = i - 1
        where = pl.ds(pl.multiple_of(at * n, n), n)

        @pl.when(lax.rem(at, per) == 0)
        def _():
            ext[0:8, :] = jnp.zeros((8, width), F32)
            exts[0:8, :] = jnp.zeros((8, 2 * STATE), F32)
            state[...] = jnp.zeros_like(state)

        rows, cols = iotas(n)
        ind = ind_ref[...]
        ext[8 : 8 + n, :] = inner[where, :]
        pre = conv_pre(ext, cp_ref, n)
        x = pre * sigmoid(pre)
        ext[0:8, :] = ext[n : n + 8, :]
        mini = small[where, :]
        exts[8 : 8 + n, :] = mini[:, : 2 * STATE]
        pres = conv_pre(exts, sp_ref, n)
        bc = (pres * sigmoid(pres)).astype(BF16)
        exts[0:8, :] = exts[n : n + 8, :]
        key, query = bc[:, :STATE], bc[:, STATE:]

        _, step, rate, cs, wide_step, wide_cs, wide_tail = scan_prep(mini, hp_ref, ind, n)
        cs2 = cs * LOG2E
        cs2t = cs2.T
        xs = x * wide_step
        lane = lax.broadcasted_iota(jnp.int32, (1, width), 1)
        half = jnp.where(lax.rem(lane, 2 * HEAD) < HEAD, 1.0, 0.0).astype(BF16)
        xsb = xs.astype(BF16)
        xs0 = xsb * half
        xs1 = xsb - xs0
        before = state[...]
        low = before.astype(BF16)
        st_ref[0] = low
        carried = mm(query, low) * wide_cs
        xw = (xs * wide_tail).astype(BF16)
        state[...] = before * wide_cs[n - 1 : n, :] + mm(key, xw, TN)
        scores = jnp.where(rows >= cols, mm(query, key, NT), 0.0)
        for pair in range(heads // 2):
            lanes = slice(pair * 2 * HEAD, (pair + 1) * 2 * HEAD)
            mats = []
            for h in (2 * pair, 2 * pair + 1):
                dec = jnp.exp2(jnp.minimum(cs2[:, h : h + 1] - cs2t[h : h + 1, :], 0.0))
                mats.append((scores * dec).astype(BF16))
            local = mm(
                jnp.concatenate(mats, axis=1),
                jnp.concatenate([xs0[:, lanes], xs1[:, lanes]], axis=0),
            )
            ssd_ref[:, lanes] = local + carried[:, lanes] + cp_ref[6:7, lanes] * x[:, lanes]
        gates = gate[where, :]
        gated = ssd_ref[...] * (gates * sigmoid(gates))
        sqs_ref[0] = rowsum(gated * gated)
        scaled_ref[...] = (gated * cp_ref[5:6, :]).astype(BF16)

        span = model // LANES
        share = -(-span // steps)
        for k in range(share):
            b = at * share + k

            @pl.when(b < span)
            def _(b=b):
                piece = block_of(slabs.at[1], b, slabs.shape[2]).T
                wt[width : 2 * width, pl.ds(pl.multiple_of(b * LANES, LANES), LANES)] = piece

    @pl.when(i == steps)
    def _():
        flush(4).start()
        job.arrive(2)
        flush(5).start()
        for j in range(3):
            job.drain(j)
        for k in range(len(outgoing)):
            flush(k).wait()


def forward(res, stateproj, steps_w, inproj, outt, gain, params, heads, size, layer, out=None):
    tokens_n, model = res.shape
    _, _, rows, width = inproj.shape
    top = 2 * width + 2 * STATE + LANES
    steps = tokens_n // CHUNK
    mid = out is not None
    hbm = pl.BlockSpec(memory_space=pl.ANY)
    chunks = model // SLICE

    def whole(a):
        return pl.BlockSpec(a.shape, lambda i: (0,) * len(a.shape))

    def row(w):
        return pl.BlockSpec((CHUNK, w), lambda i: (jnp.maximum(i - 1, 0), 0))

    args, in_specs, out_specs, out_shape, scratch = [res], [hbm], [], [], []
    if mid:
        args += list(out)
        in_specs += [hbm, hbm, whole(out[2])]
        out_specs += [hbm, whole(out[2])]
        out_shape += [jax.ShapeDtypeStruct(res.shape, F32), jax.ShapeDtypeStruct(out[2].shape, F32)]
        chunk = pltpu.VMEM((chunks, tokens_n // 2, SLICE), BF16)
        scratch += [
            pltpu.VMEM(out[0].shape, BF16),
            pltpu.VMEM(out[1].shape, BF16),
            pltpu.VMEM((2 * chunks, tokens_n // 2, SLICE), BF16),
            chunk, chunk, chunk,
            pltpu.VMEM((4,) + out[2].shape, F32),
            pltpu.VMEM((tokens_n, LANES), F32),
            pltpu.VMEM(res.shape, F32),
            pltpu.SemaphoreType.DMA((3, chunks)),
            pltpu.SemaphoreType.DMA((3, chunks)),
            pltpu.SemaphoreType.DMA((3,)),
            pltpu.SemaphoreType.DMA((3,)),
        ]
    args += [stateproj, steps_w, inproj, outt, gain, *params]
    in_specs += [hbm, hbm, hbm, hbm, whole(gain)] + [whole(v) for v in params]
    out_specs += [
        hbm, pl.BlockSpec((tokens_n, 1), lambda i: (0, 0)), hbm, hbm, hbm, hbm, hbm,
        row(width), row(width),
        pl.BlockSpec((1, 1, CHUNK), lambda i: (jnp.maximum(i - 1, 0), 0, 0)),
        pl.BlockSpec((1, STATE, width), lambda i: (jnp.maximum(i - 1, 0), 0, 0)),
    ]
    out_shape += [
        jax.ShapeDtypeStruct((model, tokens_n), BF16),
        jax.ShapeDtypeStruct((tokens_n, 1), F32),
        jax.ShapeDtypeStruct((tokens_n, 2 * STATE + LANES), F32),
        jax.ShapeDtypeStruct((tokens_n, width), F32),
        jax.ShapeDtypeStruct((tokens_n, width), F32),
        jax.ShapeDtypeStruct((top, model), BF16),
        jax.ShapeDtypeStruct((size, rows, width), BF16),
        jax.ShapeDtypeStruct((tokens_n, width), F32),
        jax.ShapeDtypeStruct((tokens_n, width), BF16),
        jax.ShapeDtypeStruct((steps, 1, CHUNK), F32),
        jax.ShapeDtypeStruct((steps, STATE, width), BF16),
    ]
    scratch += [
        pltpu.VMEM(res.shape, res.dtype),
        pltpu.VMEM((model, 2 * STATE), BF16),
        pltpu.VMEM((top, model), BF16),
        pltpu.VMEM((3, size, rows, width), BF16),
        pltpu.VMEM((tokens_n, model), BF16),
        pltpu.VMEM((model, tokens_n), BF16),
        pltpu.VMEM((tokens_n, 2 * STATE + LANES), F32),
        pltpu.VMEM((tokens_n, width), F32),
        pltpu.VMEM((tokens_n, width), F32),
        pltpu.VMEM((CHUNK + 8, width), F32),
        pltpu.VMEM((CHUNK + 8, 2 * STATE), F32),
        pltpu.VMEM((STATE, width), F32),
        pltpu.VMEM((8, width), F32),
        pltpu.VMEM((8, 2 * STATE), F32),
        pltpu.VMEM((8, LANES), F32),
        pltpu.VMEM((LANES, width), BF16),
        pltpu.SemaphoreType.DMA((3,)),
        pltpu.SemaphoreType.DMA((3, 3, size)),
        pltpu.SemaphoreType.DMA((3, size)),
        pltpu.SemaphoreType.DMA((5,)),
        pltpu.SemaphoreType.DMA((7,)),
    ]
    return pl.pallas_call(
        functools.partial(forward_body, size=size, heads=heads, per=LEN // CHUNK, steps=steps, layer=layer),
        grid=(steps + 1,),
        in_specs=in_specs,
        out_specs=out_specs,
        out_shape=out_shape,
        scratch_shapes=scratch,
        compiler_params=pltpu.CompilerParams(
            collective_id=min(layer, 1), has_side_effects=True, vmem_limit_bytes=VMEM_LIMIT
        ),
        name="forward",
    )(*args)


def back_body(*refs, heads, per, size, steps, layer, last):
    refs = list(refs)

    def take(n):
        got = refs[:n]
        del refs[:n]
        return got

    up_ref, sq_ref, gate_ref, ssd_ref, inner_ref, iprev_ref, small_ref, sprev_ref, st_ref, res_ref, rn_ref = take(11)
    gain_ref = take(1)[0]
    params = take(6)
    wout_hbm, scaled_hbm, wt_hbm, normed_hbm = take(4)
    if not last:
        next_normed, next_steps, next_sdel, next_inner, next_dcp, next_dsp, next_dhp, next_dgain = take(8)
    new_ref, grad_hbm = take(2)
    if last:
        held_hbm, sdsum_ref, steplow_ref, dcp_ref, dsp_ref, dhp_ref, dgain_ref, mixed_ref = take(8)
    else:
        full_hbm, wide_hbm = take(2)
    ext, exts, cde, cdes, dstate, rq, cp_ref, sp_ref, hp_ref, ind_ref = take(10)
    wout, scaled, wt, turned, dy, glow, ilow, frow, srow, sgot = take(10)
    part, near, away, tpart, got, far, other = take(7)
    load, rsend, rrecv, ssend, srecv, sends, recvs, gsem = take(8)
    if last:
        held, fgot, opart, ogot, ofar, oother, fsend, frecv, osends, orecvs = take(10)
    else:
        dcp_ref, dsp_ref, dhp_ref, dgain_ref = take(4)
        sd_all = scaled.at[:, pl.ds(0, 2 * STATE)]
        step_all = scaled.at[:, pl.ds(2 * STATE, LANES)]
        buffers = take(6)
        sems = take(7)
    assert not refs

    n = CHUNK
    model = up_ref.shape[1]
    i = pl.program_id(0)
    begin_gate = steps
    begin_scan = begin_gate + steps
    begin_norm = begin_scan + steps
    end = begin_norm + steps - 1
    line = Line(size)
    square = Square()
    rows_own = part.shape[2]
    count = part.shape[0]
    job = Scatter(line, part, lambda j: dy.at[pl.ds(j * rows_own, rows_own), :], near, away, ssend, srecv)
    sums = Total(square, tpart, got, far, other, sends, recvs)
    if last:
        outs = Total(square, opart, ogot, ofar, oother, osends, orecvs)
        half = steps * n // 2
        slices = model // SLICE
    else:
        minis = Smalls(line, square, *buffers, sems)
    moves = [(wout_hbm, wout), (scaled_hbm, scaled), (wt_hbm, wt), (normed_hbm, turned)]
    if last:
        moves.append((held, held_hbm))
    else:
        tokens_n = steps * n
        spots = (wt.at[pl.ds(0, model), pl.ds(0, tokens_n)],)
        spots += tuple(
            wt.at[pl.ds(0, tokens_n), pl.ds(tokens_n + at, w)] for at, w in ((0, LANES), (LANES, 2 * STATE))
        )
        moves += [(next_normed, spots[0]), (next_steps, spots[1]), (next_sdel, spots[2]), (next_inner, part.at[3])]

    def move(k):
        return pltpu.make_async_copy(*moves[k], load.at[k])

    places = line.n

    def spaced(begin, stop, m):
        return begin + m * (stop - begin) // places

    middle = begin_scan + steps // 2
    if last:
        folds = [(spaced(begin_scan, middle, m) + 1, 0, m) for m in range(places)]
        folds += [(spaced(middle, begin_norm, m) + 2, 1, m) for m in range(places)]
    else:
        folds = [(spaced(begin_gate, begin_scan + 4, m), 3, m) for m in range(places)]
        folds += [(spaced(begin_scan + 3, begin_norm + 1, m), 0, m) for m in range(places)]
        folds += [(spaced(begin_norm, end, m), 1, m) for m in range(places)]

    def column(row):
        return jnp.broadcast_to(row, (n, n)).T[:, 0:1]

    @pl.when(i == 0)
    def _():
        for k in range(3):
            move(k).start()
        if not last:
            move(7).start()
        put_params(cp_ref, sp_ref, hp_ref, ind_ref, layer, params)
        rq[...] = jnp.zeros_like(rq)
        line.greet_all(pltpu.get_barrier_semaphore(), square.others())
        if last:
            rows = [
                remote(sq_ref, fgot.at[square.me], fsend.at[k], frecv.at[k], who)
                for k, who in enumerate(square.others())
            ]
            for copy in rows:
                copy.start()
            fgot[square.me] = sq_ref[...]
            move(0).wait()
            move(1).wait()
            for c in range(slices):
                value = mm(scaled[...], wout[c * SLICE : (c + 1) * SLICE, :], NT).astype(BF16)
                opart[2 * c] = value[:half]
                opart[2 * c + 1] = value[half:]
                outs.step(0, c)
            outs.step(1, 0)
            for copy in rows:
                copy.wait()
            total = (fgot[0] + fgot[1]) + (fgot[2] + fgot[3])
        else:
            move(7).wait()
            job.start(3)
            total = sq_ref[...]
            move(0).wait()
            move(1).wait()
        dcp_ref[...] = jnp.zeros_like(dcp_ref)
        dsp_ref[...] = jnp.zeros_like(dsp_ref)
        dhp_ref[...] = jnp.zeros_like(dhp_ref)
        dgain_ref[...] = jnp.zeros_like(dgain_ref)
        frow[...] = lax.rsqrt(total / INNER + EPS)

    ind = ind_ref[...]
    for at, j, m in folds:
        @pl.when(i == at)
        def _(j=j, m=m):
            job.fold(j, m)

    @pl.when(i < begin_gate)
    def _():
        rows = pl.ds(pl.multiple_of(i * n, n), n)
        low = (column(frow[i]) * up_ref[...].astype(F32)).astype(BF16)
        turned[:, rows] = low.T
        sd = mm(low, wout[...])
        dy[rows, :] = sd
        piece = scaled[rows, :]
        srow[i] = rowsum(piece.astype(F32) * sd)

    @pl.when(i == begin_gate - 1)
    def _():
        copies = [
            remote(srow, sgot.at[square.me], rsend.at[k], rrecv.at[k], who) for k, who in enumerate(square.others())
        ]
        for copy in copies:
            copy.start()
        job.emit(0, turned, scaled)
        move(3).start()
        sgot[square.me] = srow[...]
        for copy in copies:
            copy.wait()
        srow[...] = (sgot[0] + sgot[1]) + (sgot[2] + sgot[3])

    if last:
        @pl.when(i == steps // 2)
        def _():
            outs.step(1, 1)

        @pl.when((i >= begin_gate) & (i < begin_gate + slices - 2))
        def _():
            outs.step(1, i - begin_gate + 2)

    @pl.when((i >= begin_gate) & (i < begin_scan))
    def _():
        c = i - begin_gate
        rows = pl.ds(pl.multiple_of(c * n, n), n)
        coef = column(frow[c] * frow[c] * srow[c]) / INNER
        gate = gate_ref[...]
        gsig = sigmoid(gate)
        gact = gate * gsig
        ssd = ssd_ref[...]
        sd = dy[rows, :]
        gated = ssd * gact
        gd = cp_ref[5:6, :] * sd - coef * gated
        dcp_ref[5:6, :] += colsum(gated * sd)
        dy[rows, :] = gd * gact
        glow[rows, :] = (gd * ssd * (gsig + gact * (1.0 - gsig))).astype(BF16)

    @pl.when(i == begin_scan - 1)
    def _():
        move(3).wait()
        job.emit(1, turned, glow)
        move(2).wait()

    @pl.when((i >= begin_scan) & (i < begin_norm))
    def _():
        q = i - begin_scan
        chunk = steps - 1 - q
        where = pl.ds(pl.multiple_of(chunk * n, n), n)

        @pl.when(lax.rem(chunk, per) == per - 1)
        def _():
            cde[n : n + 8, :] = jnp.zeros((8, cde.shape[1]), F32)
            cdes[n : n + 8, :] = jnp.zeros((8, cdes.shape[1]), F32)
            dstate[...] = jnp.zeros_like(dstate)

        keep = jnp.where(lax.rem(chunk, per) == 0, 0.0, 1.0).astype(F32)
        rows, cols = iotas(n)
        ext[0:8, :] = iprev_ref[...] * keep
        ext[8 : 8 + n, :] = inner_ref[...]
        exts[0:8, :] = sprev_ref[:, : 2 * STATE] * keep
        exts[8 : 8 + n, :] = small_ref[:, : 2 * STATE]
        pre = conv_pre(ext, cp_ref, n)
        sig = sigmoid(pre)
        x = pre * sig
        slope = sig + x * (1.0 - sig)
        pres = conv_pre(exts, sp_ref, n)
        sigs = sigmoid(pres)
        acts = pres * sigs
        slopes = sigs + acts * (1.0 - sigs)
        bc = acts.astype(BF16)
        key, query = bc[:, :STATE], bc[:, STATE:]
        dyc = dy[where, :]

        raw, step, rate, cs, wide_step, wide_cs, wide_tail = scan_prep(small_ref, hp_ref, ind, n)
        cs2 = cs * LOG2E
        cs2t = cs2.T
        xs = x * wide_step
        xsb = xs.astype(BF16)
        dyb = dyc.astype(BF16)
        lane = lax.broadcasted_iota(jnp.int32, (1, xs.shape[1]), 1)
        half = jnp.where(lax.rem(lane, 2 * HEAD) < HEAD, 1.0, 0.0).astype(BF16)
        dy0 = dyb * half
        dy1 = dyb - dy0
        low = st_ref[0]
        dst = dstate[...]
        dlow = dst.astype(BF16)
        dye = dyc * wide_cs
        dyeb = dye.astype(BF16)
        up = headsum(dye * mm(query, low), ind)
        dxs_state = wide_tail * mm(key, dlow)
        down = headsum(xs * dxs_state, ind)
        qdel = mm(dyeb, low, NT)
        kdel = mm((xs * wide_tail).astype(BF16), dlow, NT)
        through = headsum(jnp.broadcast_to(colsum(low.astype(F32) * dst), (8, dst.shape[1])), ind)[0:1, :]
        through = through * jnp.exp(cs[n - 1 : n, :])
        dstate[...] = dst * wide_cs[n - 1 : n, :] + mm(query, dyeb, TN)

        scores = jnp.where(rows <= cols, mm(key, query, NT), 0.0)
        dscores = jnp.zeros((n, n), F32)
        colq = jnp.zeros((n, LANES), F32)
        lane = lax.broadcasted_iota(jnp.int32, (n, LANES), 1)
        dxs = []
        for pair in range(heads // 2):
            lanes = slice(pair * 2 * HEAD, (pair + 1) * 2 * HEAD)
            stacked = jnp.concatenate([dy0[:, lanes], dy1[:, lanes]], axis=0)
            both = mm(xsb[:, lanes], stacked, NT)
            mats = []
            for which, h in enumerate((2 * pair, 2 * pair + 1)):
                dec = jnp.exp2(jnp.minimum(cs2t[h : h + 1, :] - cs2[:, h : h + 1], 0.0))
                mats.append((scores * dec).astype(BF16))
                term = dec * both[:, which * n : (which + 1) * n]
                dscores = dscores + term
                quad = scores * term
                rq[h : h + 1, :] = colsum(quad)
                colq = jnp.where(lane == h, jnp.sum(quad, axis=1, keepdims=True), colq)
            dxs.append(mm(jnp.concatenate(mats, axis=1), stacked))
        dxs = jnp.concatenate(dxs, axis=1) + dxs_state
        dscores = jnp.where(rows <= cols, dscores, 0.0).astype(BF16)
        kdel = kdel + mm(dscores, query)
        qdel = qdel + mm(dscores, key, TN)

        upper = jnp.where(rows <= cols, 1.0, 0.0).astype(F32)
        strict = jnp.where(rows > cols, 1.0, 0.0).astype(F32)
        da = mm(upper, rq[...].T - colq + up, precision=HIGH) + mm(strict, down, precision=HIGH) + through
        grown = headsum(x * dxs, ind) + rate * da
        step_pre = grown * sigmoid(raw)
        steplow = step_pre.astype(BF16)
        if last:
            steplow_ref[...] = steplow
        else:
            step_all[where, :] = steplow
        dhp_ref[0:1, :] += colsum(step_pre)
        dhp_ref[1:2, :] += rate * colsum(step * da)
        dcp_ref[6:7, :] += colsum(dyc * x)

        cd = (dxs * wide_step + cp_ref[6:7, :] * dyc) * slope
        cde[0:n, :] = cd
        center = ext[8 : 8 + n, :]
        total = cp_ref[3:4, :] * cd
        dcp_ref[3:4, :] += colsum(cd * center)
        for tap in range(3):
            shifted = cde[3 - tap : 3 - tap + n, :]
            total = total + cp_ref[tap : tap + 1, :] * shifted
            dcp_ref[tap : tap + 1, :] += colsum(shifted * center)
        inner_low = total.astype(BF16)
        ilow[where, :] = inner_low
        dcp_ref[4:5, :] += colsum(cd)
        cde[n : n + 8, :] = cde[0:8, :]

        cds = jnp.concatenate([kdel, qdel], axis=1) * slopes
        cdes[0:n, :] = cds
        center = exts[8 : 8 + n, :]
        total = sp_ref[3:4, :] * cds
        dsp_ref[3:4, :] += colsum(cds * center)
        for tap in range(3):
            shifted = cdes[3 - tap : 3 - tap + n, :]
            total = total + sp_ref[tap : tap + 1, :] * shifted
            dsp_ref[tap : tap + 1, :] += colsum(shifted * center)
        sdel = total.astype(BF16)
        dsp_ref[4:5, :] += colsum(cds)
        cdes[n : n + 8, :] = cdes[0:8, :]

        lows = jnp.concatenate([inner_low, glow[where, :], sdel, steplow], axis=1)
        value = mm(lows, wt[...]).astype(BF16)
        tpart[2 * q, :, :model] = value[: n // 2]
        tpart[2 * q + 1, :, :model] = value[n // 2 :]
        tpart[2 * q, :, model:] = sdel[: n // 2]
        tpart[2 * q + 1, :, model:] = sdel[n // 2 :]
        sums.step(0, q)

    @pl.when((i > begin_scan) & (i <= begin_norm))
    def _():
        sums.step(1, i - begin_scan - 1)

    @pl.when((i >= begin_scan + 5) & (i < begin_norm + 5))
    def _():
        sums.step(2, i - begin_scan - 5)

    @pl.when((i >= begin_scan + 6) & (i < begin_norm + 6))
    def _():
        sums.step(3, i - begin_scan - 6)

    if last:
        @pl.when((i > begin_scan) & (i <= begin_scan + slices))
        def _():
            outs.step(2, i - begin_scan - 1)

        @pl.when((i > begin_scan + 1) & (i <= begin_scan + slices + 1))
        def _():
            outs.step(3, i - begin_scan - 2)

    @pl.when(i == begin_norm - 1)
    def _():
        dhp_ref[2:3, :] = headsum(jnp.broadcast_to(dcp_ref[6:7, :], (8, dcp_ref.shape[1])), ind)[0:1, :]
        if last:
            job.product(held, turned, ilow)
            move(4).start()
        else:
            job.emit(2, turned, ilow, places // 2)
            for k in (4, 5, 6):
                move(k).start()

    if not last:
        @pl.when(i == begin_norm + 1)
        def _():
            for k in (4, 5, 6):
                move(k).wait()
            put_pack(
                buffers[0].at[1], square.me, *spots, next_dcp[...], next_dsp[...], next_dhp[...], next_dgain[...]
            )
            minis.sum.start(1)

    @pl.when(i >= begin_norm)
    def _():
        r = i - begin_norm
        chunk = steps - 1 - r
        if last:
            fac = column(frow[chunk])
            side = chunk // (steps // 2)
            base = (chunk - side * (steps // 2)) * n
        for h in range(2):
            rows = slice(h * (n // 2), (h + 1) * (n // 2))
            back = tpart[2 * r + h, :, :model].astype(F32)
            sdel = tpart[2 * r + h, :, model:]
            if last:
                sdsum_ref[rows, :] = sdel
            else:
                sd_all[pl.ds(pl.multiple_of(chunk * n + h * (n // 2), n // 2), n // 2), :] = sdel
            res = res_ref[rows, :].astype(F32)
            rn = rn_ref[rows, :]
            dgain_ref[...] += colsum(back * res * rn)
            gained = back * gain_ref[layer : layer + 1, :]
            mean = jnp.sum(gained * res, axis=1, keepdims=True) / model
            new_ref[rows, :] = up_ref[rows, :].astype(F32) + rn * gained - (rn * rn * rn * mean) * res
            if last:
                where = pl.ds(pl.multiple_of(base + h * (n // 2), n // 2), n // 2)
                for c in range(slices):
                    span = slice(c * SLICE, (c + 1) * SLICE)
                    summed = opart[2 * c + side, where, :].astype(F32)
                    mixed_ref[rows, span] = (res[:, span] + fac[rows, :] * summed).astype(BF16)

    @pl.when(i == end)
    def _():
        def finish(j):
            job.finish(j)
            pltpu.make_async_copy(dy.at[pl.ds(j * rows_own, rows_own), :], grad_hbm.at[j], gsem.at[j]).start()

        if not last:
            put_pack(
                buffers[0].at[0], square.me, turned, step_all, sd_all, dcp_ref[...], dsp_ref[...], dhp_ref[...], dgain_ref[...]
            )
            minis.sum.start(0)
            for m in range(places // 2, places - 1):
                job.lead(2, m)
            for m in range(places // 2):
                job.fold(2, m)
            finish(3)
        finish(0)
        finish(1)
        if not last:
            minis.fold()
            minis.turn()
            for k in range(1, line.n):
                minis.relay(k)
            job.lead(2, places - 1)
            for m in range(places // 2, places):
                job.fold(2, m)
            minis.cross()
            finish(2)
            minis.cross_on()
            minis.end()
            tails = [
                pltpu.make_async_copy(src, dst, load.at[k])
                for k, (src, dst) in enumerate(((minis.full, full_hbm), (minis.wide, wide_hbm)))
            ]
            for copy in tails:
                copy.start()
        for j in range(count):
            job.drain(j)
            pltpu.make_async_copy(dy.at[pl.ds(j * rows_own, rows_own), :], grad_hbm.at[j], gsem.at[j]).wait()
        if last:
            move(4).wait()
        else:
            for copy in tails:
                copy.wait()


def back(up, sq, gate_pre, ssd, inner_raw, small, states, res, rnorm, gain, params,
         wout, scaled, wt, normed, heads, size, layer, after=None):
    tokens_n, width = inner_raw.shape
    model = up.shape[1]
    last = after is None
    steps = tokens_n // CHUNK
    begin_scan = 2 * steps
    begin_norm = begin_scan + steps
    rows = model // size
    n = size // 2
    hbm = pl.BlockSpec(memory_space=pl.ANY)
    top = steps - 1

    def norm_at(i):
        return jnp.where(i < begin_norm, top, top - (i - begin_norm))

    def scan_at(i):
        return jnp.clip(top - (i - begin_scan), 0, top)

    def first(w):
        return pl.BlockSpec((CHUNK, w), lambda i: (jnp.where(i < steps, i, norm_at(i)), 0))

    def second(w):
        return pl.BlockSpec((CHUNK, w), lambda i: (jnp.clip(i - steps, 0, top), 0))

    def scan(w):
        return pl.BlockSpec((CHUNK, w), lambda i: (scan_at(i), 0))

    def prev(w):
        return pl.BlockSpec((8, w), lambda i: (jnp.maximum(scan_at(i) * (CHUNK // 8) - 1, 0), 0))

    def norm(w):
        return pl.BlockSpec((CHUNK, w), lambda i: (norm_at(i), 0))

    def whole(a):
        return pl.BlockSpec(a.shape, lambda i: (0,) * len(a.shape))

    extra = model + 2 * STATE
    quarter = pltpu.VMEM((steps, CHUNK // 2, extra), BF16)
    count = 2 if last else 4
    pieces = pltpu.VMEM((count, n, rows, width), BF16)
    args = [up, sq, gate_pre, ssd, inner_raw, inner_raw, small, small, states, res, rnorm, gain, *params,
            wout, scaled, wt, normed]
    in_specs = [
        first(model), whole(sq), second(width), second(width),
        scan(width), prev(width), scan(small.shape[1]), prev(small.shape[1]),
        pl.BlockSpec((1, STATE, width), lambda i: (scan_at(i), 0, 0)),
        norm(model), norm(1), whole(gain),
    ] + [whole(a) for a in params] + [hbm] * 4
    out_specs = [norm(model), hbm]
    out_shape = [jax.ShapeDtypeStruct((tokens_n, model), F32), jax.ShapeDtypeStruct((count, rows, width), F32)]
    totals = [(8, width), (8, 2 * STATE), (8, LANES), (1, model)]
    scratch = [
        pltpu.VMEM((CHUNK + 8, width), F32),
        pltpu.VMEM((CHUNK + 8, 2 * STATE), F32),
        pltpu.VMEM((CHUNK + 8, width), F32),
        pltpu.VMEM((CHUNK + 8, 2 * STATE), F32),
        pltpu.VMEM((STATE, width), F32),
        pltpu.VMEM((LANES, CHUNK), F32),
        pltpu.VMEM((8, width), F32),
        pltpu.VMEM((8, 2 * STATE), F32),
        pltpu.VMEM((8, LANES), F32),
        pltpu.VMEM((LANES, width), BF16),
        pltpu.VMEM(wout.shape, BF16),
        pltpu.VMEM(scaled.shape, BF16),
        pltpu.VMEM(wt.shape, BF16),
        pltpu.VMEM(normed.shape, BF16),
        pltpu.VMEM((tokens_n, width), F32),
        pltpu.VMEM((tokens_n, width), BF16),
        pltpu.VMEM((tokens_n, width), BF16),
        pltpu.VMEM((steps, 1, CHUNK), F32),
        pltpu.VMEM((steps, 1, CHUNK), F32),
        pltpu.VMEM((4, steps, 1, CHUNK), F32),
        pltpu.VMEM((count, size, rows, width), BF16), pieces, pieces,
        pltpu.VMEM((2 * steps, CHUNK // 2, extra), BF16), quarter, quarter, quarter,
        pltpu.SemaphoreType.DMA((8,)),
        pltpu.SemaphoreType.DMA((3,)),
        pltpu.SemaphoreType.DMA((3,)),
        pltpu.SemaphoreType.DMA((2, count, n)),
        pltpu.SemaphoreType.DMA((2, count, n)),
        pltpu.SemaphoreType.DMA((3, steps)),
        pltpu.SemaphoreType.DMA((3, steps)),
        pltpu.SemaphoreType.DMA((count,)),
    ]
    if last:
        out_specs += [hbm, norm(2 * STATE), scan(LANES)]
        out_specs += [pl.BlockSpec(v, lambda i: (0, 0)) for v in totals] + [norm(model)]
        out_shape += [
            jax.ShapeDtypeStruct((size, rows, width), BF16),
            jax.ShapeDtypeStruct((tokens_n, 2 * STATE), BF16),
            jax.ShapeDtypeStruct((tokens_n, LANES), BF16),
        ]
        out_shape += [jax.ShapeDtypeStruct(v, F32) for v in totals]
        out_shape.append(jax.ShapeDtypeStruct((tokens_n, model), BF16))
        slices = model // SLICE
        chunk = pltpu.VMEM((slices, tokens_n // 2, SLICE), BF16)
        scratch += [
            pltpu.VMEM((size, rows, width), BF16),
            pltpu.VMEM((4, steps, 1, CHUNK), F32),
            pltpu.VMEM((2 * slices, tokens_n // 2, SLICE), BF16), chunk, chunk, chunk,
            pltpu.SemaphoreType.DMA((3,)),
            pltpu.SemaphoreType.DMA((3,)),
            pltpu.SemaphoreType.DMA((3, slices)),
            pltpu.SemaphoreType.DMA((3, slices)),
        ]
    else:
        w = 2 * STATE
        r = pack_rows(size)
        args += list(after)
        in_specs += [hbm] * 4 + [whole(v) for v in after[4:]]
        out_specs += [hbm, hbm]
        out_shape += [
            jax.ShapeDtypeStruct((2, size, r, w), BF16),
            jax.ShapeDtypeStruct((4, 2, SPAN, w), BF16),
        ]
        scratch += [pltpu.VMEM(v, F32) for v in totals]
        scratch += smalls_scratch(size, w, 2)
    return pl.pallas_call(
        functools.partial(
            back_body, heads=heads, per=LEN // CHUNK, size=size, steps=steps, layer=layer, last=last
        ),
        grid=(begin_norm + steps,),
        in_specs=in_specs,
        out_specs=out_specs,
        out_shape=out_shape,
        scratch_shapes=scratch,
        compiler_params=pltpu.CompilerParams(
            collective_id=2 if last else 3, has_side_effects=True, vmem_limit_bytes=VMEM_LIMIT
        ),
        name="back",
    )(*args)


def results_body(full_ref, wide_ref, first_hbm, second_hbm, mixed_hbm, up_hbm, *refs, layers, heads):
    pair_out, out_out, mixed_out, up_out = refs[11:15]
    first, second, mixed, up, load, store = refs[15:]
    refs = refs[:11]
    loads = [
        pltpu.make_async_copy(src, dst, load.at[k])
        for k, (src, dst) in enumerate(((up_hbm, up), (mixed_hbm, mixed), (first_hbm, first), (second_hbm, second)))
    ]
    for copy in loads:
        copy.start()
    moves = [
        (up, up_out), (mixed, mixed_out), (first.at[pl.ds(1, 2)], pair_out.at[0]), (second.at[1], pair_out.at[1, 0]),
        (first.at[3], pair_out.at[1, 1]), (first.at[0], out_out.at[0]), (second.at[0], out_out.at[1]),
    ]
    stores = [pltpu.make_async_copy(src, dst, store.at[k]) for k, (src, dst) in enumerate(moves)]
    for k, copy in enumerate(stores):
        if k < 3:
            loads[k].wait()
        if k == 3:
            loads[3].wait()
        copy.start()
    step_ref, state_ref, conv_ref, bias_ref, convs_ref, biass_ref = refs[:6]
    stepbias_ref, decay_ref, skip_ref, norm_ref, gain_ref = refs[6:]
    model = state_ref.shape[1]
    quarter = model // 4
    w = state_ref.shape[2]
    width = conv_ref.shape[2]
    for layer in range(layers):
        for t in range(4):
            state_ref[layer, t * quarter : (t + 1) * quarter, :] = wide_ref[t, layer, :quarter, :].astype(F32)
        taps = [wide_ref[t, layer, quarter : quarter + 16, :].astype(F32) for t in range(4)]
        taps = (taps[0] + taps[1]) + (taps[2] + taps[3])
        convs_ref[layer] = taps[0:4]
        biass_ref[layer : layer + 1, :] = taps[4:5]
        flat = full_ref[layer].reshape(-1, w)[:PACK].astype(F32)
        at = quarter + 16
        for b in range(model // w):
            step_ref[layer, :, b * w : (b + 1) * w] = flat[at : at + 16]
            at += 16
        for b in range(width // w):
            lanes = slice(b * w, (b + 1) * w)
            rows = flat[at + 8 * b : at + 8 * b + 8]
            conv_ref[layer, :, lanes] = rows[0:4]
            bias_ref[layer : layer + 1, lanes] = rows[4:5]
            norm_ref[layer : layer + 1, lanes] = rows[5:6]
        at += 8 * (width // w)
        for k, ref in enumerate((stepbias_ref, decay_ref, skip_ref)):
            ref[layer : layer + 1, :] = flat[at + k : at + k + 1, :heads]
        at += 8
        for b in range(model // w):
            gain_ref[layer : layer + 1, b * w : (b + 1) * w] = flat[at + b : at + b + 1]
    for copy in stores:
        copy.wait()


def write_results(full, wide, first, second, mixed, up, heads):
    layers, w = full.shape[0], full.shape[3]
    _, rows, width = first.shape
    model = up.shape[1]
    vm = pl.BlockSpec(memory_space=pltpu.VMEM)
    hbm = pl.BlockSpec(memory_space=pl.ANY)
    shapes = [
        (layers, 16, model), (layers, model, w), (layers, 4, width), (layers, width), (layers, 4, w), (layers, w),
        (layers, heads), (layers, heads), (layers, heads), (layers, width), (layers, model),
    ]
    return pl.pallas_call(
        functools.partial(results_body, layers=layers, heads=heads),
        in_specs=[vm, vm] + [hbm] * 4,
        out_specs=[vm] * len(shapes) + [hbm] * 4,
        out_shape=[jax.ShapeDtypeStruct(v, F32) for v in shapes] + [
            jax.ShapeDtypeStruct((layers, 2, rows, width), F32),
            jax.ShapeDtypeStruct((layers, rows, width), F32),
            jax.ShapeDtypeStruct(mixed.shape, mixed.dtype),
            jax.ShapeDtypeStruct(up.shape, up.dtype),
        ],
        scratch_shapes=[
            pltpu.VMEM(first.shape, F32),
            pltpu.VMEM(second.shape, F32),
            pltpu.VMEM(mixed.shape, mixed.dtype),
            pltpu.VMEM(up.shape, up.dtype),
            pltpu.SemaphoreType.DMA((4,)),
            pltpu.SemaphoreType.DMA((7,)),
        ],
        compiler_params=pltpu.CompilerParams(vmem_limit_bytes=VMEM_LIMIT),
        name="results",
    )(full, wide, first, second, mixed, up)


def shards(
    tokens, inproj, stepproj, stateproj, outproj, convinner, biasinner, convstate, biasstate,
    stepbias, decaylog, skipgain, normgain, inputgain, cotangent,
):
    layers = inproj.shape[0]
    width = inproj.shape[3]
    heads = stepproj.shape[2]
    model = tokens.shape[1]
    pad = LANES - heads
    size = lax.axis_size("dp")
    steps_w = jnp.pad(jnp.swapaxes(stepproj, 1, 2), ((0, 0), (0, pad), (0, 0)))
    head = jnp.pad(jnp.stack([stepbias, decaylog, skipgain], axis=1), ((0, 0), (0, 5), (0, pad)))
    outt = jnp.swapaxes(outproj, 1, 2)
    params = (convinner, biasinner, normgain, convstate, biasstate, head)

    residual = tokens
    kept = []
    out = None
    for at in range(layers):
        results = forward(residual, stateproj, steps_w, inproj, outt, inputgain, params, heads, size, at, out=out)
        if at:
            residual, kept[-1][-1] = results[:2]
            results = results[2:]
        normed, rnorm, small, inner_raw, gate_pre, wt, w_out, ssd, scaled, sq, states = results
        w_out = w_out.reshape(model, width)
        kept.append([residual, normed, rnorm, small, inner_raw, gate_pre, wt, w_out, ssd, scaled, states, sq])
        out = (scaled, w_out, sq)

    assert layers == 2
    before, normed, rnorm, small, inner_raw, gate_pre, wt, w_out, ssd, scaled, states, sq = kept[1]
    upstream, second, held, sdel, steplow, *totals, mixed = back(
        cotangent, sq, gate_pre, ssd, inner_raw, small, states, before, rnorm, inputgain, params,
        w_out, scaled, wt, normed, heads, size, 1,
    )
    after = (normed, steplow, sdel, held, *totals)
    before, normed, rnorm, small, inner_raw, gate_pre, wt, w_out, ssd, scaled, states, sq = kept[0]
    upstream, first, full, wide = back(
        upstream, sq, gate_pre, ssd, inner_raw, small, states, before, rnorm, inputgain, params,
        w_out, scaled, wt, normed, heads, size, 0, after=after,
    )
    (
        step_grad, state_grad, conv_grad, bias_grad, convs_grad, biass_grad,
        stepbias_grad, decay_grad, skip_grad, norm_grad, gain_grad, pair_grad, out_grad, mixed, upstream,
    ) = write_results(full, wide, first, second, mixed, upstream, heads)
    return (
        mixed,
        upstream,
        pair_grad,
        jnp.swapaxes(step_grad[:, :heads], 1, 2),
        state_grad,
        jnp.swapaxes(out_grad, 1, 2),
        conv_grad,
        bias_grad,
        convs_grad,
        biass_grad,
        stepbias_grad,
        decay_grad,
        skip_grad,
        norm_grad,
        gain_grad,
    )


def solution(mesh):
    in_specs = (
        P("dp", None),
        P(None, None, "dp", "tensor"),
        P(None, None, "tensor"),
        P(),
        P(None, "tensor", "dp"),
        P(None, None, "tensor"),
        P(None, "tensor"),
        P(),
        P(),
        P(None, "tensor"),
        P(None, "tensor"),
        P(None, "tensor"),
        P(None, "tensor"),
        P(),
        P("dp", None),
    )
    out_specs = (
        P("dp", None),
        P("dp", None),
        P(None, None, "dp", "tensor"),
        P(None, None, "tensor"),
        P(),
        P(None, "tensor", "dp"),
        P(None, None, "tensor"),
        P(None, "tensor"),
        P(),
        P(),
        P(None, "tensor"),
        P(None, "tensor"),
        P(None, "tensor"),
        P(None, "tensor"),
        P(),
    )
    return jax.shard_map(shards, mesh=mesh, in_specs=in_specs, out_specs=out_specs, check_vma=False)
```
